32 devices in a mesh: dp: 16 (over z, y, x), tensor: 2 (over core).
Axes of the slice: x: 2, y: 2, z: 4, core: 2. Of those that a mesh axis runs over, the one named last changes fastest.
Arguments:
- hidden_in: bfloat16 [16384, 1536], P('dp'), may hold values from -6 to 6
- out_grad: bfloat16 [16384, 1536], P('dp'), may hold values from -6 to 6
- routes: int32 [16384, 8], P('dp'), may hold values from 0 to 15, all different within a row; in each aligned block of 1024 rows (0 to 1023, 1024 to 2047, ...) at most 768 rows name the same one
- segments: int32 [16384], P('dp'), may hold values from 0 to 60, never falling along the last dimension, each value on 1 to 800 neighbouring positions
- norm_gains: float32 [2, 1536], P(None, 'dp'), may hold values from 0.5 to 1.5
- gains_mean: float32 [2, 1536], P(None, 'dp'), may hold values from -256 to 256
- gains_square: float32 [2, 1536], P(None, 'dp'), may hold values from 3883.008 to 62095.36
- w_query: float32 [1536, 1536], P('dp', 'tensor'), may hold values from -0.5 to 0.5
- query_mean: float32 [1536, 1536], P('dp', 'tensor'), may hold values from -80 to 80
- query_square: float32 [1536, 1536], P('dp', 'tensor'), may hold values from 430.8992 to 6897.664
- key_value_weight: float32 [2, 1536, 512], P(None, 'dp', 'tensor'), may hold values from -0.5 to 0.5
- key_value_first_moment: float32 [2, 1536, 512], P(None, 'dp', 'tensor'), may hold values from -80 to 80
- key_value_second_moment: float32 [2, 1536, 512], P(None, 'dp', 'tensor'), may hold values from 430.8992 to 6897.664
- w_out: float32 [1536, 1536], P('tensor', 'dp'), may hold values from -1.5 to 1.5
- out_mean: float32 [1536, 1536], P('tensor', 'dp'), may hold values from -16 to 16
- out_square: float32 [1536, 1536], P('tensor', 'dp'), may hold values from 13.9264 to 222.8224
- w_router: float32 [1536, 16], P('dp'), may hold values from -0.078125 to 0.078125
- router_mean: float32 [1536, 16], P('dp'), may hold values from -896 to 896
- router_square: float32 [1536, 16], P('dp'), may hold values from 43089.92 to 689766.4
- w_gateup: float32 [16, 2, 1536, 512], P(None, None, 'dp', 'tensor'), may hold values from -0.15625 to 0.15625
- gateup_mean: float32 [16, 2, 1536, 512], P(None, None, 'dp', 'tensor'), may hold values from -32 to 32
- gateup_square: float32 [16, 2, 1536, 512], P(None, None, 'dp', 'tensor'), may hold values from 52.4288 to 851.968
- w_down: float32 [16, 512, 1536], P(None, 'tensor', 'dp'), may hold values from -4 to 4
- down_mean: float32 [16, 512, 1536], P(None, 'tensor', 'dp'), may hold values from -1 to 1
- down_square: float32 [16, 512, 1536], P(None, 'tensor', 'dp'), may hold values from 0.0589824 to 0.950272
Outputs:
- block_out: bfloat16 [16384, 1536], P('dp')
- input_grad: float32 [16384, 1536], P('dp')
- gains_mean_new: float32 [2, 1536], P(None, 'dp')
- gains_square_new: float32 [2, 1536], P(None, 'dp')
- gains_new: float32 [2, 1536], P(None, 'dp')
- query_mean_new: float32 [1536, 1536], P('dp', 'tensor')
- query_square_new: float32 [1536, 1536], P('dp', 'tensor')
- query_new: float32 [1536, 1536], P('dp', 'tensor')
- keyval_mean_new: float32 [2, 1536, 512], P(None, 'dp', 'tensor')
- keyval_square_new: float32 [2, 1536, 512], P(None, 'dp', 'tensor')
- keyval_new: float32 [2, 1536, 512], P(None, 'dp', 'tensor')
- out_mean_new: float32 [1536, 1536], P('tensor', 'dp')
- out_square_new: float32 [1536, 1536], P('tensor', 'dp')
- out_new: float32 [1536, 1536], P('tensor', 'dp')
- router_mean_new: float32 [1536, 16], P('dp')
- router_square_new: float32 [1536, 16], P('dp')
- router_new: float32 [1536, 16], P('dp')
- gateup_mean_new: float32 [16, 2, 1536, 512], P(None, None, 'dp', 'tensor')
- gateup_square_new: float32 [16, 2, 1536, 512], P(None, None, 'dp', 'tensor')
- gateup_new: float32 [16, 2, 1536, 512], P(None, None, 'dp', 'tensor')
- down_mean_new: float32 [16, 512, 1536], P(None, 'tensor', 'dp')
- down_square_new: float32 [16, 512, 1536], P(None, 'tensor', 'dp')
- down_new: float32 [16, 512, 1536], P(None, 'tensor', 'dp')
The draws below stay inside these ranges and needn't reach their ends.
Inputs may be any that keep to these rules, and one draw needn't show every extreme that they name: `routes`: each row names 8 different experts. Among the rows of one device (each aligned block of 1024 rows) no expert is named by more than 768 rows, a bound that some block reaches. `segments`: ids never fall along the array; each id covers 1 to 800 positions, and one covers exactly 800.
All inputs are finite; a program needn't handle non-finite values.
Results may differ from the reference program's by a relative error of at most 0.018.
The reference program's roundings to bfloat16 on the way count: a program that leaves them out, or rounds other values in their place, can miss the bound.
Values may be sent and summed in bfloat16 or wider, within the bound.
A program may use at most 384 MiB of HBM per device.

```python
import math
import jax
import jax.numpy as jnp
import numpy as np
from jax import lax

MODEL_DIM = 1536
QUERY_HEADS = 24
KEY_VALUE_HEADS = 8
HEAD_DIM = 64
F = 512
TOPK = 8
E = 16
SEQUENCE_LENGTH = 1024
DOC_MOST = 800
STEP = 10
TOK_DEV = 1024
TOKEN_TOTAL = 16384
CAP = 768
DOCS = 61


def levels(rng, extent, split, least, top_value):
    def one(axis_at, parts):
        steps = jax.random.uniform(jax.random.fold_in(jax.random.fold_in(rng, 6), axis_at), (parts,), jnp.float32, least / len(split), top_value / len(split))
        return jnp.repeat(jnp.exp(steps), extent[axis_at] // parts).reshape((-1,) + (1,) * (len(extent) - axis_at - 1))

    level = one(*split[0])
    for cut in split[1:]:
        level = level * one(*cut)
    return level


def profile(number_of, total, reach, lean):
    portions = [(1 << 20) // math.isqrt(rank ** lean) + 1 for rank in range(2, number_of + 1)]
    spare, given = total - reach - (number_of - 1), [1] * (number_of - 1)
    while spare > 0:
        candidates = [i for i in range(number_of - 1) if given[i] < reach]
        mass, budget = sum([portions[i] for i in candidates]), spare
        for i in candidates:
            more = min(reach - given[i], max(1, budget * portions[i] // mass), spare)
            given[i] = given[i] + more
            spare = spare - more
    return np.array([reach] + given)


def uneven_parts(own_key, number_of, total, reach, lean):
    if number_of == 2:
        one = jax.random.randint(own_key, (), max(1, total - reach), min(reach, total - 1) + 1)
        return jnp.stack([one, total - one])
    lengths = jnp.asarray(profile(number_of, total, reach, lean), jnp.int32)
    couples = (number_of - 1) // 2
    donor, receiver = lengths[1:1 + 2 * couples:2], lengths[2:2 + 2 * couples:2]
    slack = jnp.minimum(donor - 1, reach - receiver)
    moved = jax.random.randint(jax.random.fold_in(own_key, 1), (couples,), 0, 1 << 20) % (slack + 1)
    lengths = lengths.at[1:1 + 2 * couples:2].set(donor - moved).at[2:2 + 2 * couples:2].set(receiver + moved)
    return lengths[jax.random.permutation(jax.random.fold_in(own_key, 2), number_of)]


def assign_block(key, own, number, rows, amount, top, bound, slope):
    ranking = jax.random.permutation(key, amount)
    heavy_load, common = portions_of(amount, rows * top, bound, slope, True), portions_of(amount, rows * top, bound, slope, False)
    places = jnp.arange(amount)

    def named(sizes, turn):
        used = int((sizes > 0).sum())
        fixed = max(1, used // 4)
        shifted = fixed + (places - fixed + turn * (used - fixed)) % max(1, amount - fixed)
        return jnp.zeros((amount,), jnp.int32).at[ranking[jnp.where(places < fixed, places, shifted)]].set(jnp.asarray(sizes, jnp.int32))

    sizes = jnp.where(number % 4 == 0, named(heavy_load, number // 4), named(common, number - number // 4 - 1))
    mixed = jax.random.permutation(jax.random.fold_in(own, 3), amount)
    donor, receiver = mixed[0:amount // 2 * 2:2], mixed[1:amount // 2 * 2:2]
    margin = jnp.minimum(sizes[donor] - 1, bound - sizes[receiver]) // 2
    margin = jnp.where((donor == ranking[0]) | (receiver == ranking[0]) | (sizes[receiver] == 0), 0, jnp.maximum(margin, 0))
    shifted = jax.random.randint(jax.random.fold_in(own, 4), (amount // 2,), 0, 1 << 20) % (margin + 1)
    sizes = sizes.at[donor].add(-shifted).at[receiver].add(shifted)
    items = jnp.searchsorted(jnp.cumsum(sizes), jnp.arange(rows * top), side="right").astype(jnp.int32)
    grid = items.reshape(top, rows).T
    grid = grid[jax.random.permutation(jax.random.fold_in(own, 1), rows)]
    turn = jax.random.randint(jax.random.fold_in(own, 2), (rows, 1), 0, top)
    return jnp.take_along_axis(grid, (jnp.arange(top)[None, :] + turn) % top, axis=1)


def portions_of(count, total, most, lean, full):
    weights = [(1 << 20) // math.isqrt(rank ** lean) + 1 for rank in range(1, count + 1)]
    largest = most if full else min(most, max(-(-total // count), total * weights[0] // sum(weights)))
    least = 1 if total - largest >= count - 1 else 0
    counts, spare = [largest] + [least] * (count - 1), total - largest - least * (count - 1)
    while spare > 0:
        candidates = [i for i in range(1, count) if counts[i] < largest] or [i for i in range(1, count) if counts[i] < most]
        whole, budget = sum([weights[i] for i in candidates]), spare
        for i in candidates:
            addition = min(most - counts[i], max(1, budget * weights[i] // whole), spare)
            counts[i] = counts[i] + addition
            spare = spare - addition
    return np.array(counts)


def scatter_about(rng, dims, spread, reach, split=(), kind=jnp.bfloat16):
    loudness = levels(rng, dims, split, -0.22, 0.18) if split else 1.0
    entries = jax.random.normal(rng, dims, jnp.float32) * spread * loudness
    return jnp.minimum(jnp.maximum(entries, -reach), reach).astype(kind)


def setup_inputs(seed: int = 0) -> dict:
    seeds = jax.random.split(jax.random.key(seed), 26)
    hidden_in = scatter_about(seeds[0], (TOKEN_TOTAL, MODEL_DIM), 1.0, 6.0, ((0, 16),))
    out_grad = scatter_about(seeds[1], (TOKEN_TOTAL, MODEL_DIM), 1.0, 6.0, ((0, 16),))
    routes_keys = jax.random.split(jax.random.fold_in(seeds[2], 1), TOKEN_TOTAL // TOK_DEV)
    routes_turns = jax.random.permutation(jax.random.fold_in(seeds[2], 3), TOKEN_TOTAL // TOK_DEV)
    routes = jax.vmap(lambda own, number: assign_block(jax.random.fold_in(seeds[2], 2), own, number, TOK_DEV, E, TOPK, CAP, 1))(routes_keys, routes_turns).reshape((TOKEN_TOTAL, TOPK))
    segments = jnp.searchsorted(jnp.cumsum(uneven_parts(seeds[3], DOCS, TOKEN_TOTAL, DOC_MOST, 1)), jnp.arange(TOKEN_TOTAL), side="right").astype(jnp.int32)
    norm_gains = jnp.clip(1.0 + 0.1 * jax.random.normal(seeds[4], (2, MODEL_DIM), jnp.float32), 0.5, 1.5)
    gains_mean = scatter_about(seeds[5], (2, MODEL_DIM), (0.333 * TOKEN_TOTAL ** 0.5), 256.0, ((1, 16),), jnp.float32)
    gains_square = jnp.clip(jnp.exp(math.log(62095.36) - 2.772061 * jax.random.uniform(seeds[6], (2, MODEL_DIM), jnp.float32) ** levels(seeds[6], (2, MODEL_DIM), ((1, 16),), -0.2, 0.2)), 3883.008, 62095.36)
    w_query = scatter_about(seeds[7], (MODEL_DIM, QUERY_HEADS * HEAD_DIM), (MODEL_DIM // 12) ** -0.5, 0.5, ((0, 16), (1, 2)), jnp.float32)
    query_mean = scatter_about(seeds[8], (MODEL_DIM, QUERY_HEADS * HEAD_DIM), (0.111 * TOKEN_TOTAL ** 0.5), 80.0, ((0, 16), (1, 2)), jnp.float32)
    query_square = jnp.clip(jnp.exp(math.log(6897.664) - 2.773064 * jax.random.uniform(seeds[9], (MODEL_DIM, QUERY_HEADS * HEAD_DIM), jnp.float32) ** levels(seeds[9], (MODEL_DIM, QUERY_HEADS * HEAD_DIM), ((0, 16), (1, 2)), -0.2, 0.2)), 430.8992, 6897.664)
    key_value_weight = scatter_about(seeds[10], (2, MODEL_DIM, KEY_VALUE_HEADS * HEAD_DIM), (MODEL_DIM // 12) ** -0.5, 0.5, ((1, 16), (2, 2)), jnp.float32)
    key_value_first_moment = scatter_about(seeds[11], (2, MODEL_DIM, KEY_VALUE_HEADS * HEAD_DIM), (0.111 * TOKEN_TOTAL ** 0.5), 80.0, ((1, 16), (2, 2)), jnp.float32)
    key_value_second_moment = jnp.clip(jnp.exp(math.log(6897.664) - 2.773064 * jax.random.uniform(seeds[12], (2, MODEL_DIM, KEY_VALUE_HEADS * HEAD_DIM), jnp.float32) ** levels(seeds[12], (2, MODEL_DIM, KEY_VALUE_HEADS * HEAD_DIM), ((1, 16), (2, 2)), -0.2, 0.2)), 430.8992, 6897.664)
    w_out = scatter_about(seeds[13], (QUERY_HEADS * HEAD_DIM, MODEL_DIM), (max(1, QUERY_HEADS * HEAD_DIM // 96)) ** -0.5, 1.5, ((0, 2), (1, 16)), jnp.float32)
    out_mean = scatter_about(seeds[14], (QUERY_HEADS * HEAD_DIM, MODEL_DIM), (0.02 * TOKEN_TOTAL ** 0.5), 16.0, ((0, 2), (1, 16)), jnp.float32)
    out_square = jnp.clip(jnp.exp(math.log(222.8224) - 2.7725887 * jax.random.uniform(seeds[15], (QUERY_HEADS * HEAD_DIM, MODEL_DIM), jnp.float32) ** levels(seeds[15], (QUERY_HEADS * HEAD_DIM, MODEL_DIM), ((0, 2), (1, 16)), -0.2, 0.2)), 13.9264, 222.8224)
    w_router = scatter_about(seeds[16], (MODEL_DIM, E), (4 * MODEL_DIM) ** -0.5, 0.078125, ((0, 16),), jnp.float32)
    router_mean = scatter_about(seeds[17], (MODEL_DIM, E), (1.11 * TOKEN_TOTAL ** 0.5), 896.0, ((0, 16),), jnp.float32)
    router_square = jnp.clip(jnp.exp(math.log(689766.4) - 2.773064 * jax.random.uniform(seeds[18], (MODEL_DIM, E), jnp.float32) ** levels(seeds[18], (MODEL_DIM, E), ((0, 16),), -0.2, 0.2)), 43089.92, 689766.4)
    w_gateup = scatter_about(seeds[19], (E, 2, MODEL_DIM, F), MODEL_DIM ** -0.5, 0.15625, ((2, 16), (3, 2)), jnp.float32)
    gateup_mean = scatter_about(seeds[20], (E, 2, MODEL_DIM, F), (0.039 * TOKEN_TOTAL ** 0.5), 32.0, ((2, 16), (3, 2)), jnp.float32)
    gateup_square = jnp.clip(jnp.exp(math.log(851.968) - 2.78809295 * jax.random.uniform(seeds[21], (E, 2, MODEL_DIM, F), jnp.float32) ** levels(seeds[21], (E, 2, MODEL_DIM, F), ((2, 16), (3, 2)), -0.2, 0.2)), 52.4288, 851.968)
    w_down = scatter_about(seeds[22], (E, F, MODEL_DIM), (max(1, F // 256)) ** -0.5, 4.0, ((1, 2), (2, 16)), jnp.float32)
    down_mean = scatter_about(seeds[23], (E, F, MODEL_DIM), (0.0013 * TOKEN_TOTAL ** 0.5), 1.0, ((1, 2), (2, 16)), jnp.float32)
    down_square = jnp.clip(jnp.exp(math.log(0.950272) - 2.7795092 * jax.random.uniform(seeds[24], (E, F, MODEL_DIM), jnp.float32) ** levels(seeds[24], (E, F, MODEL_DIM), ((1, 2), (2, 16)), -0.2, 0.2)), 0.0589824, 0.950272)
    return {"hidden_in": hidden_in, "out_grad": out_grad, "routes": routes, "segments": segments, "norm_gains": norm_gains, "gains_mean": gains_mean, "gains_square": gains_square, "w_query": w_query, "query_mean": query_mean, "query_square": query_square, "key_value_weight": key_value_weight, "key_value_first_moment": key_value_first_moment, "key_value_second_moment": key_value_second_moment, "w_out": w_out, "out_mean": out_mean, "out_square": out_square, "w_router": w_router, "router_mean": router_mean, "router_square": router_square, "w_gateup": w_gateup, "gateup_mean": gateup_mean, "gateup_square": gateup_square, "w_down": w_down, "down_mean": down_mean, "down_square": down_square}


NORM_EPSILON = 1e-06
SCORE_SCALE = 0.015625
RESIDUAL_SCALE = 0.22
ROPE_BASE = 10000.0
FIRST_DECAY = 0.9
SECOND_DECAY = 0.95
ADAM_EPSILON = 1e-08
WEIGHT_DECAY = 0.1
GAIN_RATE = 0.6
MASK_VALUE = -1e+30
HIGHEST_PRECISION = lax.Precision.HIGHEST

@jax.custom_vjp
def reduced_forward(v):
    return lax.optimization_barrier(v.astype(jnp.bfloat16)).astype(jnp.float32)

@jax.custom_vjp
def reduced_backward(v):
    return v

def low_keep(v):
    return (reduced_forward(v), None)

def low_pass(kept, grad):
    return (grad,)

def back_keep(v):
    return (v, None)

def back_low(kept, grad):
    return (reduced_forward(grad),)
reduced_forward.defvjp(low_keep, low_pass)
reduced_backward.defvjp(back_keep, back_low)

def seq_positions(segment_row):
    counter = jnp.arange(segment_row.shape[0], dtype=jnp.int32)
    earlier = jnp.concatenate([segment_row[:1] - 1, segment_row[:-1]])
    starts = lax.cummax(jnp.where(segment_row != earlier, counter, 0), axis=0)
    return (counter - starts).astype(jnp.int32)

def rope_tables(positions):
    half_width = HEAD_DIM // 2
    frequency = ROPE_BASE ** (-2.0 * jnp.arange(half_width, dtype=jnp.float32) / HEAD_DIM)
    angles = positions.astype(jnp.float32)[:, None] * frequency[None, :]
    return (jnp.cos(angles), jnp.sin(angles))

def rotary_apply(values, cosine_lookup, sine_lookup):
    half_width = values.shape[-1] // 2
    first_half = values[..., :half_width]
    second = values[..., half_width:]
    cosine_rows = cosine_lookup[:, None, :]
    sine_rows = sine_lookup[:, None, :]
    return jnp.concatenate([first_half * cosine_rows - second * sine_rows, second * cosine_rows + first_half * sine_rows], axis=-1)

def rms_norm(values, gain_row):
    return values * lax.rsqrt(lax.optimization_barrier(jnp.mean(values * values, axis=-1, keepdims=True)) + NORM_EPSILON) * gain_row

def attend(query_matrix, key_matrix, value_matrix, segment_row):
    sequence_span = query_matrix.shape[0]
    query_group_width = QUERY_HEADS // KEY_VALUE_HEADS
    grouped_queries = query_matrix.reshape(sequence_span, KEY_VALUE_HEADS, query_group_width, HEAD_DIM)
    scores = jnp.einsum('qkgd,skd->kgqs', grouped_queries, key_matrix, precision=HIGHEST_PRECISION) * SCORE_SCALE
    scores = reduced_backward(scores)
    counter = jnp.arange(sequence_span, dtype=jnp.int32)
    allowed = (counter[:, None] >= counter[None, :]) & (segment_row[:, None] == segment_row[None, :])
    scores = jnp.where(allowed, scores, MASK_VALUE)
    highest = lax.optimization_barrier(jnp.max(scores, axis=-1, keepdims=True))
    weights = jnp.exp(scores - highest)
    probability = reduced_forward(weights / lax.optimization_barrier(jnp.sum(weights, axis=-1, keepdims=True)))
    attention_output = jnp.einsum('kgqs,skd->qkgd', probability, value_matrix, precision=HIGHEST_PRECISION)
    return attention_output.reshape(sequence_span, QUERY_HEADS * HEAD_DIM)

def sequence_attention(operands):
    return jax.checkpoint(attend)(*operands)

def block_forward(block_in, params, block_routes, block_segments):
    norm_gains, w_query, key_value_weight, w_out, w_router, w_gateup, w_down = params
    token_inputs = block_in.shape[0]
    sequence_list = token_inputs // SEQUENCE_LENGTH
    normed_low = reduced_forward(rms_norm(block_in, norm_gains[0]))
    query_lin = jnp.dot(normed_low, reduced_forward(w_query), precision=HIGHEST_PRECISION)
    key_value_linear = jnp.einsum('td,kdc->ktc', normed_low, reduced_forward(key_value_weight), precision=HIGHEST_PRECISION)
    document_ids = block_segments.reshape(sequence_list, SEQUENCE_LENGTH)
    positions = jax.vmap(seq_positions)(document_ids).reshape(token_inputs)
    cosine_lookup, sine_lookup = rope_tables(positions)
    query_matrix = reduced_forward(rotary_apply(reduced_backward(query_lin.reshape(token_inputs, QUERY_HEADS, HEAD_DIM)), cosine_lookup, sine_lookup))
    key_matrix = reduced_forward(rotary_apply(reduced_backward(key_value_linear[0].reshape(token_inputs, KEY_VALUE_HEADS, HEAD_DIM)), cosine_lookup, sine_lookup))
    value_matrix = reduced_forward(reduced_backward(key_value_linear[1].reshape(token_inputs, KEY_VALUE_HEADS, HEAD_DIM)))
    attention_output = lax.map(sequence_attention, (query_matrix.reshape(sequence_list, SEQUENCE_LENGTH, QUERY_HEADS, HEAD_DIM), key_matrix.reshape(sequence_list, SEQUENCE_LENGTH, KEY_VALUE_HEADS, HEAD_DIM), value_matrix.reshape(sequence_list, SEQUENCE_LENGTH, KEY_VALUE_HEADS, HEAD_DIM), document_ids))
    attention_output = reduced_forward(reduced_backward(attention_output.reshape(token_inputs, QUERY_HEADS * HEAD_DIM)))
    attention = reduced_backward(jnp.dot(attention_output, reduced_forward(w_out), precision=HIGHEST_PRECISION))
    middle = block_in + RESIDUAL_SCALE * attention
    normed_two = rms_norm(middle, norm_gains[1])
    logits = jnp.dot(normed_two, w_router, precision=HIGHEST_PRECISION)
    chosen = jnp.take_along_axis(logits, block_routes, axis=1)
    gate_values = jax.nn.softmax(chosen, axis=-1)
    one_hot = (block_routes[:, :, None] == jnp.arange(E, dtype=jnp.int32)[None, None, :]).astype(jnp.float32)
    combine = jnp.einsum('tk,tke->te', gate_values, one_hot, precision=HIGHEST_PRECISION)
    normed_two_low = reduced_forward(normed_two)

    def expert_term(running, operands):
        gateup_weight, down_weight, expert_column = operands
        gate_up = reduced_backward(jnp.einsum('td,kdf->ktf', normed_two_low, reduced_forward(gateup_weight), precision=HIGHEST_PRECISION))
        inner_value = reduced_forward(jax.nn.silu(gate_up[0]) * gate_up[1])
        output = reduced_backward(jnp.dot(inner_value, reduced_forward(down_weight), precision=HIGHEST_PRECISION))
        return (running + expert_column[:, None] * output, None)
    expert_mix, unused = lax.scan(jax.checkpoint(expert_term), jnp.zeros_like(block_in), (w_gateup, w_down, combine.T))
    return middle + RESIDUAL_SCALE * expert_mix

def adam_update(value, gradient, mean_old, square_old, rate, decay):
    mean_new = FIRST_DECAY * mean_old + (1.0 - FIRST_DECAY) * gradient
    square_new = SECOND_DECAY * square_old + (1.0 - SECOND_DECAY) * gradient * gradient
    mean_hat = mean_new / (1.0 - FIRST_DECAY ** STEP)
    square_hat = square_new / (1.0 - SECOND_DECAY ** STEP)
    updated = value - rate * (mean_hat / (jnp.sqrt(square_hat) + ADAM_EPSILON) + decay * value)
    return (mean_new, square_new, updated)

def reference(hidden_in, out_grad, routes, segments, norm_gains, gains_mean, gains_square, w_query, query_mean, query_square, key_value_weight, key_value_first_moment, key_value_second_moment, w_out, out_mean, out_square, w_router, router_mean, router_square, w_gateup, gateup_mean, gateup_square, w_down, down_mean, down_square):
    params = (norm_gains, w_query, key_value_weight, w_out, w_router, w_gateup, w_down)
    group_tokens = min(TOKEN_TOTAL, 4 * SEQUENCE_LENGTH)
    group_count = TOKEN_TOTAL // group_tokens

    def one_group(running, operands):
        block_in, block_back, block_routes, block_segments = operands

        def forward(values, weights):
            return block_forward(values, weights, block_routes, block_segments)
        result, pullback = jax.vjp(forward, block_in, params)
        grad_in, weight_grads = pullback(block_back)
        running = jax.tree.map(jnp.add, running, weight_grads)
        return (running, (result.astype(jnp.bfloat16), grad_in))
    inputs = hidden_in.astype(jnp.float32).reshape(group_count, group_tokens, MODEL_DIM)
    cotangent = out_grad.astype(jnp.float32).reshape(group_count, group_tokens, MODEL_DIM)
    route_groups = routes.reshape(group_count, group_tokens, TOPK)
    segment_groups = segments.reshape(group_count, group_tokens)
    grads, (block_out, input_grad) = lax.scan(one_group, jax.tree.map(jnp.zeros_like, params), (inputs, cotangent, route_groups, segment_groups))
    block_out = block_out.reshape(TOKEN_TOTAL, MODEL_DIM)
    input_grad = input_grad.reshape(TOKEN_TOTAL, MODEL_DIM)
    gains_grad, query_grad, keyval_grad, out_weight_grad, router_grad, gateup_grad, down_grad = grads
    gains_result = adam_update(norm_gains, gains_grad, gains_mean, gains_square, GAIN_RATE, 0.0)
    query_result = adam_update(w_query, query_grad, query_mean, query_square, (MODEL_DIM // 12) ** (-0.5), WEIGHT_DECAY)
    keyval_result = adam_update(key_value_weight, keyval_grad, key_value_first_moment, key_value_second_moment, (MODEL_DIM // 12) ** (-0.5), WEIGHT_DECAY)
    out_result = adam_update(w_out, out_weight_grad, out_mean, out_square, max(1, QUERY_HEADS * HEAD_DIM // 96) ** (-0.5), WEIGHT_DECAY)
    router_result = adam_update(w_router, router_grad, router_mean, router_square, (4 * MODEL_DIM) ** (-0.5), WEIGHT_DECAY)
    gateup_result = adam_update(w_gateup, gateup_grad, gateup_mean, gateup_square, MODEL_DIM ** (-0.5), WEIGHT_DECAY)
    down_result = adam_update(w_down, down_grad, down_mean, down_square, max(1, F // 256) ** (-0.5), WEIGHT_DECAY)
    return (block_out, input_grad, gains_result[0], gains_result[1], gains_result[2], query_result[0], query_result[1], query_result[2], keyval_result[0], keyval_result[1], keyval_result[2], out_result[0], out_result[1], out_result[2], router_result[0], router_result[1], router_result[2], gateup_result[0], gateup_result[1], gateup_result[2], down_result[0], down_result[1], down_result[2])
```

```python
import functools

import jax
import jax.numpy as jnp
from jax import lax
from jax.experimental import pallas as pl
from jax.experimental.pallas import tpu as pltpu
from jax.sharding import PartitionSpec as P

MODEL_DIM = 1536
QUERY_HEADS = 24
HEAD_DIM = 64
F = 512
SEQUENCE_LENGTH = 1024
STEP = 10

NORM_EPSILON = 1e-06
SCORE_SCALE = 0.015625
RESIDUAL_SCALE = 0.22
ROPE_BASE = 10000.0
FIRST_DECAY = 0.9
SECOND_DECAY = 0.95
ADAM_EPSILON = 1e-08
WEIGHT_DECAY = 0.1
GAIN_RATE = 0.6
MASK_VALUE = -1e30
HIGHEST_PRECISION = lax.Precision.HIGHEST

BF16 = jnp.bfloat16
F32 = jnp.float32
LANES = 128
ROWS = 256
VMEM_BYTES = 58 * 1024 * 1024

NN = (((1,), (0,)), ((), ()))
NT = (((1,), (1,)), ((), ()))
TN = (((0,), (0,)), ((), ()))


def dot(a, b, dims=NN):
    return lax.dot_general(a, b, dims, preferred_element_type=F32)


def seq_positions(segment_row):
    counter = jnp.arange(segment_row.shape[0], dtype=jnp.int32)
    earlier = jnp.concatenate([segment_row[:1] - 1, segment_row[:-1]])
    starts = lax.cummax(jnp.where(segment_row != earlier, counter, 0), axis=0)
    return counter - starts


def rope_tables(positions):
    half_width = HEAD_DIM // 2
    frequency = ROPE_BASE ** (-2.0 * jnp.arange(half_width, dtype=F32) / HEAD_DIM)
    angles = positions.astype(F32)[:, None] * frequency[None, :]
    cosine, sine = jnp.cos(angles), jnp.sin(angles)
    return (
        jnp.concatenate([cosine] * 4, axis=1),
        jnp.concatenate([-sine, sine] * 2, axis=1),
    )


def rotate_halves(slab):
    lane = lax.broadcasted_iota(jnp.int32, slab.shape, 1)
    ahead = pltpu.roll(slab, LANES - HEAD_DIM // 2, 1)
    behind = pltpu.roll(slab, HEAD_DIM // 2, 1)
    return jnp.where(lane % HEAD_DIM < HEAD_DIM // 2, ahead, behind)


def half_mask(rows, upper):
    lane = lax.broadcasted_iota(jnp.int32, (rows, LANES), 1)
    return (lane >= HEAD_DIM) if upper else (lane < HEAD_DIM)


def spread_heads(slab, lower_out, upper_out, index):
    rows = slab.shape[0]
    moved = pltpu.roll(slab.astype(F32), HEAD_DIM, 1).astype(BF16)
    zero = jnp.zeros_like(slab)
    low, high = half_mask(rows, False), half_mask(rows, True)
    lower_out[index] = jnp.where(low, slab, zero)
    upper_out[index] = jnp.where(high, moved, zero)
    lower_out[index + 1] = jnp.where(low, moved, zero)
    upper_out[index + 1] = jnp.where(high, slab, zero)


def fill_bias(bias, seg_col, seg_row):
    span = bias.shape[0]
    for at in range(0, span, ROWS):
        rows_at = at + lax.broadcasted_iota(jnp.int32, (ROWS, span), 0)
        cols_at = lax.broadcasted_iota(jnp.int32, (ROWS, span), 1)
        allowed = (rows_at >= cols_at) & (seg_col[at : at + ROWS, :] == seg_row[...])
        bias[at : at + ROWS, :] = jnp.where(allowed, 0.0, MASK_VALUE).astype(F32)


def attention_forward_kernel(
    lin_ref, kv_ref, cos_ref, sin_ref, seg_col, seg_row,
    out_ref, q_ref, k_ref, v_ref, lse_ref,
    bias, k_low, k_high, v_low, v_high,
):
    slab_at = pl.program_id(0)
    span = lin_ref.shape[0]
    kv_slabs = kv_ref.shape[1] // (2 * LANES)

    @pl.when(slab_at == 0)
    def _():
        fill_bias(bias, seg_col, seg_row)
        for j in range(kv_slabs):
            lanes = slice(j * LANES, (j + 1) * LANES)
            lin = kv_ref[:, lanes]
            keys = (lin * cos_ref[...] + rotate_halves(lin) * sin_ref[...]).astype(BF16)
            k_ref[:, lanes] = keys
            spread_heads(keys, k_low, k_high, 2 * j)
            lanes = slice((kv_slabs + j) * LANES, (kv_slabs + j + 1) * LANES)
            values = kv_ref[:, lanes].astype(BF16)
            v_ref[:, slice(j * LANES, (j + 1) * LANES)] = values
            spread_heads(values, v_low, v_high, 2 * j)

    lin = lin_ref[...]
    q_ref[...] = (lin * cos_ref[...] + rotate_halves(lin) * sin_ref[...]).astype(BF16)
    kv_even, kv_odd = (2 * slab_at) // 3, (2 * slab_at + 1) // 3
    for at in range(0, span, ROWS):
        rows = slice(at, at + ROWS)
        queries = q_ref[rows, :]
        total = None
        stats = []
        for keys, values, kv_at in ((k_low, v_low, kv_even), (k_high, v_high, kv_odd)):
            upto = at + ROWS
            scores = dot(queries, keys[kv_at, :upto, :], NT) * SCORE_SCALE + bias[rows, :upto]
            highest = jnp.max(scores, axis=1, keepdims=True)
            weights = jnp.exp(scores - highest)
            summed = jnp.sum(weights, axis=1, keepdims=True)
            probability = (weights * (1.0 / summed)).astype(BF16)
            part = dot(probability, values[kv_at, :upto, :])
            total = part if total is None else total + part
            stats.append(highest + jnp.log(summed))
        out_ref[rows, :] = total.astype(BF16)
        spread = jnp.where(half_mask(ROWS, False), stats[0], stats[1])
        turned = spread.T
        lse_ref[0, 0:1, rows] = turned[0:1, :]
        lse_ref[0, 1:2, rows] = turned[HEAD_DIM : HEAD_DIM + 1, :]


def attention_forward(qkv_lin, cosine, sine, segment_row):
    span = qkv_lin.shape[0]
    q_width = MODEL_DIM // 2
    kv_width = (qkv_lin.shape[1] - q_width) // 2
    slabs, kv_heads = q_width // LANES, kv_width // HEAD_DIM
    whole = lambda shape: pl.BlockSpec(shape, lambda g: (0,) * len(shape))
    slab = pl.BlockSpec((span, LANES), lambda g: (0, g))
    q_lin, kv_lin = qkv_lin[:, :q_width], qkv_lin[:, q_width:]
    return pl.pallas_call(
        attention_forward_kernel,
        grid=(slabs,),
        in_specs=[
            slab, whole((span, 2 * kv_width)), whole((span, LANES)), whole((span, LANES)),
            whole((span, 1)), whole((1, span)),
        ],
        out_specs=[
            slab, slab, whole((span, kv_width)), whole((span, kv_width)),
            pl.BlockSpec((1, 8, span), lambda g: (g, 0, 0)),
        ],
        out_shape=[
            jax.ShapeDtypeStruct((span, q_width), BF16),
            jax.ShapeDtypeStruct((span, q_width), BF16),
            jax.ShapeDtypeStruct((span, kv_width), BF16),
            jax.ShapeDtypeStruct((span, kv_width), BF16),
            jax.ShapeDtypeStruct((slabs, 8, span), F32),
        ],
        scratch_shapes=[pltpu.VMEM((span, span), F32)]
        + [pltpu.VMEM((kv_heads, span, LANES), BF16)] * 4,
        compiler_params=pltpu.CompilerParams(vmem_limit_bytes=VMEM_BYTES),
        cost_estimate=pl.CostEstimate(
            flops=4 * slabs * span * span * LANES, bytes_accessed=16 * span * q_width,
            transcendentals=slabs * span * span,
        ),
        name="attention_forward",
    )(q_lin, kv_lin, cosine, sine, segment_row[:, None], segment_row[None, :])


def attention_backward_kernel(
    q_ref, k_ref, v_ref, out_ref, grad_ref, cos_ref, sin_ref, seg_col, seg_row, lse_ref,
    dq_ref, dkv_ref,
    bias, k_low, k_high, v_low, v_high, dk_low, dk_high, dv_low, dv_high, dq_sum,
):
    slab_at = pl.program_id(0)
    span = q_ref.shape[0]
    kv_slabs = k_ref.shape[1] // LANES

    @pl.when(slab_at == 0)
    def _():
        for at in range(0, span, ROWS):
            keys_at = at + lax.broadcasted_iota(jnp.int32, (ROWS, span), 0)
            rows_at = lax.broadcasted_iota(jnp.int32, (ROWS, span), 1)
            allowed = (rows_at >= keys_at) & (seg_col[at : at + ROWS, :] == seg_row[...])
            bias[at : at + ROWS, :] = jnp.where(allowed, 0.0, MASK_VALUE).astype(F32)
        for j in range(kv_slabs):
            lanes = slice(j * LANES, (j + 1) * LANES)
            spread_heads(k_ref[:, lanes], k_low, k_high, 2 * j)
            spread_heads(v_ref[:, lanes], v_low, v_high, 2 * j)
        for sums in (dk_low, dk_high, dv_low, dv_high):
            sums[...] = jnp.zeros_like(sums)

    kv_even, kv_odd = (2 * slab_at) // 3, (2 * slab_at + 1) // 3
    for at in range(0, span, ROWS):
        rows = slice(at, at + ROWS)
        upto = at + ROWS
        queries, grads = q_ref[rows, :], grad_ref[rows, :]
        turned = (grads.astype(F32) * out_ref[rows, :].astype(F32)).T
        zero = jnp.zeros_like(queries)
        dq_part = None
        for upper, keys, values, dk_sum, dv_sum, kv_at in (
            (False, k_low, v_low, dk_low, dv_low, kv_even),
            (True, k_high, v_high, dk_high, dv_high, kv_odd),
        ):
            first = HEAD_DIM if upper else 0
            delta = jnp.sum(turned[first : first + HEAD_DIM, :], axis=0, keepdims=True)
            head = 1 if upper else 0
            total = lse_ref[0, head : head + 1, rows]
            keys_here = keys[kv_at, :upto, :]
            scores = dot(keys_here, queries, NT) * SCORE_SCALE + bias[:upto, rows]
            probability = jnp.exp(scores - total)
            prob_grad = dot(values[kv_at, :upto, :], grads, NT)
            score_grad = (probability * (prob_grad - delta)).astype(BF16)
            mask = half_mask(ROWS, upper)
            dv_sum[kv_at, :upto, :] += dot(
                probability.astype(BF16), jnp.where(mask, grads, zero)
            )
            dk_sum[kv_at, :upto, :] += dot(score_grad, jnp.where(mask, queries, zero))
            part = dot(score_grad, keys_here, TN)
            dq_part = part if dq_part is None else dq_part + part
        dq_sum[rows, :] = dq_part * SCORE_SCALE
    slab = dq_sum[...]
    dq_ref[...] = (slab * cos_ref[...] - rotate_halves(slab) * sin_ref[...]).astype(BF16)

    @pl.when(slab_at == pl.num_programs(0) - 1)
    def _():
        low = half_mask(span, False)

        def joined(sums_low, sums_high, j):
            one = sums_low[2 * j] + pltpu.roll(sums_high[2 * j], HEAD_DIM, 1)
            two = pltpu.roll(sums_low[2 * j + 1], HEAD_DIM, 1) + sums_high[2 * j + 1]
            return jnp.where(low, one, two)

        for j in range(kv_slabs):
            slab = joined(dk_low, dk_high, j) * SCORE_SCALE
            dkv_ref[:, j * LANES : (j + 1) * LANES] = (
                slab * cos_ref[...] - rotate_halves(slab) * sin_ref[...]
            ).astype(BF16)
            at = (kv_slabs + j) * LANES
            dkv_ref[:, at : at + LANES] = joined(dv_low, dv_high, j).astype(BF16)


def attention_backward(queries, keys, values, attended, grad, cosine, sine, segment_row, lse):
    span, q_width = queries.shape
    kv_width = keys.shape[1]
    slabs, kv_heads = q_width // LANES, kv_width // HEAD_DIM
    whole = lambda shape: pl.BlockSpec(shape, lambda g: (0,) * len(shape))
    slab = pl.BlockSpec((span, LANES), lambda g: (0, g))
    return pl.pallas_call(
        attention_backward_kernel,
        grid=(slabs,),
        in_specs=[
            slab, whole((span, kv_width)), whole((span, kv_width)), slab, slab,
            whole((span, LANES)), whole((span, LANES)), whole((span, 1)), whole((1, span)),
            pl.BlockSpec((1, 8, span), lambda g: (g, 0, 0)),
        ],
        out_specs=[slab, whole((span, 2 * kv_width))],
        out_shape=[
            jax.ShapeDtypeStruct((span, q_width), BF16),
            jax.ShapeDtypeStruct((span, 2 * kv_width), BF16),
        ],
        scratch_shapes=[pltpu.VMEM((span, span), F32)]
        + [pltpu.VMEM((kv_heads, span, LANES), BF16)] * 4
        + [pltpu.VMEM((kv_heads, span, LANES), F32)] * 4
        + [pltpu.VMEM((span, LANES), F32)],
        compiler_params=pltpu.CompilerParams(vmem_limit_bytes=VMEM_BYTES),
        cost_estimate=pl.CostEstimate(
            flops=10 * slabs * span * span * LANES, bytes_accessed=16 * span * q_width,
            transcendentals=slabs * span * span,
        ),
        name="attention_backward",
    )(
        queries, keys, values, attended, grad, cosine, sine,
        segment_row[:, None], segment_row[None, :], lse,
    )


def experts_kernel(
    x_ref, xt_ref, og_ref, ogt_ref, combine_ref, w_ref,
    grad_ref, mix_ref, dx_ref, gate_ref,
    held,
):
    expert = pl.program_id(0)
    tokens, width = x_ref.shape
    hidden = held.shape[1] // 3
    tile = 512

    @pl.when(expert == 0)
    def _():
        mix_ref[...] = jnp.zeros_like(mix_ref)
        dx_ref[...] = jnp.zeros_like(dx_ref)
        gate_ref[...] = jnp.zeros_like(gate_ref)

    def forward_rows(step, carry):
        rows = pl.ds(pl.multiple_of(step * ROWS, ROWS), ROWS)
        gate_up = dot(x_ref[rows, :], w_ref[:, : 2 * hidden])
        raw = dot(og_ref[rows, :], w_ref[:, 2 * hidden :]) * RESIDUAL_SCALE
        gate, up = gate_up[:, :hidden], gate_up[:, hidden:]
        lane = lax.broadcasted_iota(jnp.int32, (ROWS, combine_ref.shape[1]), 1)
        column = jnp.sum(
            jnp.where(lane == expert, combine_ref[rows, :], 0.0), axis=1, keepdims=True
        )
        sigmoid = 1.0 / (1.0 + jnp.exp(-gate))
        active = gate * sigmoid
        inner = (active * up).astype(BF16).astype(F32)
        chosen = (inner * column).astype(BF16)
        held[rows, 2 * hidden :] = chosen
        gate_grad = jnp.sum(inner * raw, axis=1, keepdims=True)
        gate_ref[rows, :] = jnp.where(lane == expert, gate_grad, gate_ref[rows, :])
        inner_grad = raw * column
        held[rows, :hidden] = (
            inner_grad * up * sigmoid * (1.0 + gate * (1.0 - sigmoid))
        ).astype(BF16)
        held[rows, hidden : 2 * hidden] = (inner_grad * active).astype(BF16)
        for at in range(0, width, tile):
            cols = slice(at, at + tile)
            mix_ref[rows, cols] += dot(chosen, w_ref[cols, 2 * hidden :], NT)
            dx_ref[rows, cols] += dot(held[rows, : 2 * hidden], w_ref[cols, : 2 * hidden], NT)
        return carry

    lax.fori_loop(0, tokens // ROWS, forward_rows, 0)

    def grad_rows(step, carry):
        rows = pl.ds(pl.multiple_of(step * ROWS, ROWS), ROWS)
        grad_ref[rows, : 2 * hidden] = dot(xt_ref[rows, :], held[:, : 2 * hidden]).astype(BF16)
        grad_ref[rows, 2 * hidden :] = (
            dot(ogt_ref[rows, :], held[:, 2 * hidden :]) * RESIDUAL_SCALE
        ).astype(BF16)
        return carry

    lax.fori_loop(0, width // ROWS, grad_rows, 0)


def experts_pass(x, out_grad, combine, weights):
    tokens, width = x.shape
    experts = combine.shape[1]
    block = weights.shape[1] // experts
    whole = lambda shape: pl.BlockSpec(
        shape, lambda e: (0,) * len(shape), pipeline_mode=pl.Buffered(1)
    )
    return pl.pallas_call(
        experts_kernel,
        grid=(experts,),
        in_specs=[
            whole((tokens, width)), whole((width, tokens)),
            whole((tokens, width)), whole((width, tokens)),
            whole((tokens, experts)),
            pl.BlockSpec((width, block), lambda e: (0, e)),
        ],
        out_specs=[
            pl.BlockSpec((width, block), lambda e: (0, e)),
            whole((tokens, width)), whole((tokens, width)), whole((tokens, experts)),
        ],
        out_shape=[
            jax.ShapeDtypeStruct(weights.shape, BF16),
            jax.ShapeDtypeStruct((tokens, width), F32),
            jax.ShapeDtypeStruct((tokens, width), F32),
            jax.ShapeDtypeStruct((tokens, experts), F32),
        ],
        scratch_shapes=[pltpu.VMEM((tokens, block), BF16)],
        compiler_params=pltpu.CompilerParams(vmem_limit_bytes=VMEM_BYTES),
        cost_estimate=pl.CostEstimate(
            flops=6 * tokens * width * weights.shape[1],
            bytes_accessed=4 * weights.size + 20 * tokens * width, transcendentals=0,
        ),
        name="experts_pass",
    )(x, x.T, out_grad, out_grad.T, combine, weights)


def split_three(values):
    high = values.astype(BF16)
    rest = values - high.astype(F32)
    middle = rest.astype(BF16)
    low = (rest - middle.astype(F32)).astype(BF16)
    return [high, middle, low]


def pair_sum(part):
    other = lax.ppermute(part, "tensor", [(0, 1), (1, 0)])
    return part.astype(F32) + other.astype(F32)


def norm_backward(values, inverse, gain_row, upstream):
    scaled = values * inverse
    weighted = upstream * gain_row
    mean_term = jnp.mean(weighted * scaled, axis=-1, keepdims=True)
    return (inverse * (weighted - scaled * mean_term), jnp.sum(upstream * scaled, axis=0))


def adam_update(value, gradient, mean_old, square_old, rate, decay):
    mean_new = FIRST_DECAY * mean_old + (1.0 - FIRST_DECAY) * gradient
    square_new = SECOND_DECAY * square_old + (1.0 - SECOND_DECAY) * gradient * gradient
    mean_hat = mean_new / (1.0 - FIRST_DECAY**STEP)
    square_hat = square_new / (1.0 - SECOND_DECAY**STEP)
    updated = value - rate * (mean_hat / (jnp.sqrt(square_hat) + ADAM_EPSILON) + decay * value)
    return (mean_new, square_new, updated)


def shards(
    hidden_in,
    out_grad,
    routes,
    segments,
    norm_gains,
    gains_mean,
    gains_square,
    w_query,
    query_mean,
    query_square,
    key_value_weight,
    key_value_first_moment,
    key_value_second_moment,
    w_out,
    out_mean,
    out_square,
    w_router,
    router_mean,
    router_square,
    w_gateup,
    gateup_mean,
    gateup_square,
    w_down,
    down_mean,
    down_square,
):
    tokens, width = hidden_in.shape
    own = w_query.shape[0]
    experts, hidden = w_down.shape[0], w_down.shape[1]
    q_width, kv_width = w_query.shape[1], key_value_weight.shape[2]
    qkv_width = q_width + 2 * kv_width
    small_width = 3 * (2 + experts)
    attention_width = qkv_width + q_width
    attention_shard = jnp.concatenate(
        [
            w_query.astype(BF16),
            key_value_weight[0].astype(BF16),
            key_value_weight[1].astype(BF16),
            w_out.T.astype(BF16),
        ]
        + split_three(jnp.concatenate([norm_gains.T, w_router], axis=1))
        + [jnp.zeros((own, LANES - small_width), BF16)],
        axis=1,
    )
    expert_shard = jnp.concatenate(
        [
            w_gateup[:, 0].astype(BF16),
            w_gateup[:, 1].astype(BF16),
            w_down.astype(BF16).transpose(0, 2, 1),
        ],
        axis=2,
    )
    expert_shard = expert_shard.transpose(1, 0, 2).reshape(own, experts * 3 * hidden)
    attention_full = lax.all_gather(attention_shard, "dp", axis=0, tiled=True)
    expert_full = lax.all_gather(expert_shard, "dp", axis=0, tiled=True)
    qkv_full = attention_full[:, :qkv_width]
    output_full = attention_full[:, qkv_width:attention_width]
    pieces = attention_full[:, attention_width : attention_width + small_width].astype(F32)
    each = 2 + experts
    small = pieces[:, :each] + pieces[:, each : 2 * each] + pieces[:, 2 * each :]
    gains_full, router_full = small[:, :2].T, small[:, 2:]

    inputs = hidden_in.astype(F32)
    inverse_one = lax.rsqrt(jnp.mean(inputs * inputs, axis=-1, keepdims=True) + NORM_EPSILON)
    normed_low = (inputs * inverse_one * gains_full[0]).astype(BF16)
    qkv_lin = jnp.dot(normed_low, qkv_full, preferred_element_type=F32)
    cosine, sine = rope_tables(seq_positions(segments))
    attended, queries, keys, values, lse = attention_forward(qkv_lin, cosine, sine, segments)
    attention_part = lax.dot_general(attended, output_full, NT, preferred_element_type=F32)
    attention = pair_sum(attention_part.astype(BF16))
    middle = inputs + RESIDUAL_SCALE * attention
    inverse_two = lax.rsqrt(jnp.mean(middle * middle, axis=-1, keepdims=True) + NORM_EPSILON)
    normed_two = middle * inverse_two * gains_full[1]
    normed_two_low = normed_two.astype(BF16)
    logits = jnp.dot(normed_two, router_full, precision=HIGHEST_PRECISION)
    expert_ids = jnp.arange(experts, dtype=jnp.int32)
    chosen = jnp.any(routes[:, :, None] == expert_ids[None, None, :], axis=1)
    combine = jax.nn.softmax(jnp.where(chosen, logits, -jnp.inf), axis=-1)

    expert_grads, mix_part, dx_part, gate_part = experts_pass(
        normed_two_low, out_grad, combine, expert_full
    )
    expert_share = lax.psum_scatter(expert_grads, "dp", scatter_dimension=0, tiled=True)
    normed_two_part = pair_sum(dx_part.astype(BF16))
    gate_grad = pair_sum(gate_part)
    expert_mix = pair_sum(mix_part.astype(BF16))
    block_out = (middle + RESIDUAL_SCALE * expert_mix).astype(BF16)

    logit_grad = combine * (gate_grad - jnp.sum(combine * gate_grad, axis=-1, keepdims=True))
    router_grad = jnp.dot(normed_two.T, logit_grad, precision=HIGHEST_PRECISION)
    normed_two_grad = normed_two_part + jnp.dot(
        logit_grad, router_full.T, precision=HIGHEST_PRECISION
    )
    middle_part, gain_two_grad = norm_backward(middle, inverse_two, gains_full[1], normed_two_grad)
    middle_grad = out_grad.astype(F32) + middle_part
    attention_back = (RESIDUAL_SCALE * middle_grad).astype(BF16)
    attended_grad = jnp.dot(attention_back, output_full, preferred_element_type=F32).astype(BF16)
    query_grad, keyval_grad = attention_backward(
        queries, keys, values, attended, attended_grad, cosine, sine, segments, lse
    )
    qkv_grad = jnp.concatenate([query_grad, keyval_grad], axis=1)
    normed_part = lax.dot_general(qkv_grad, qkv_full, NT, preferred_element_type=F32)
    normed_grad = pair_sum(normed_part.astype(BF16))
    qkv_weight_grad = lax.dot_general(normed_low, qkv_grad, TN, preferred_element_type=F32)
    output_weight_grad = lax.dot_general(attention_back, attended, TN, preferred_element_type=F32)
    input_part, gain_one_grad = norm_backward(inputs, inverse_one, gains_full[0], normed_grad)
    input_grad = middle_grad + input_part
    small_grads = jnp.concatenate(
        [gain_one_grad[:, None], gain_two_grad[:, None], router_grad], axis=1
    )
    attention_share = lax.psum_scatter(
        jnp.concatenate(
            [qkv_weight_grad.astype(BF16), output_weight_grad.astype(BF16)], axis=1
        ),
        "dp", scatter_dimension=0, tiled=True,
    ).astype(F32)
    small_share = lax.psum_scatter(small_grads, "dp", scatter_dimension=0, tiled=True)

    gains_share, router_share = small_share[:, :2].T, small_share[:, 2:]
    query_share = attention_share[:, :q_width]
    keyval_share = jnp.stack(
        [
            attention_share[:, q_width : q_width + kv_width],
            attention_share[:, q_width + kv_width : qkv_width],
        ]
    )
    output_share = attention_share[:, qkv_width:].T
    expert_share = expert_share.reshape(own, experts, 3, hidden)
    gateup_share = expert_share[:, :, :2].transpose(1, 2, 0, 3).astype(F32)
    down_share = expert_share[:, :, 2].transpose(1, 2, 0).astype(F32)

    gains_result = adam_update(norm_gains, gains_share, gains_mean, gains_square, GAIN_RATE, 0.0)
    query_result = adam_update(
        w_query, query_share, query_mean, query_square, (MODEL_DIM // 12) ** (-0.5), WEIGHT_DECAY
    )
    keyval_result = adam_update(
        key_value_weight,
        keyval_share,
        key_value_first_moment,
        key_value_second_moment,
        (MODEL_DIM // 12) ** (-0.5),
        WEIGHT_DECAY,
    )
    out_result = adam_update(
        w_out,
        output_share,
        out_mean,
        out_square,
        max(1, QUERY_HEADS * HEAD_DIM // 96) ** (-0.5),
        WEIGHT_DECAY,
    )
    router_result = adam_update(
        w_router, router_share, router_mean, router_square, (4 * MODEL_DIM) ** (-0.5), WEIGHT_DECAY
    )
    gateup_result = adam_update(
        w_gateup, gateup_share, gateup_mean, gateup_square, MODEL_DIM ** (-0.5), WEIGHT_DECAY
    )
    down_result = adam_update(
        w_down, down_share, down_mean, down_square, max(1, F // 256) ** (-0.5), WEIGHT_DECAY
    )
    return (
        (block_out, input_grad)
        + gains_result
        + query_result
        + keyval_result
        + out_result
        + router_result
        + gateup_result
        + down_result
    )


def solution(mesh):
    tokens, gains = P("dp", None), P(None, "dp")
    query, keyval, out = P("dp", "tensor"), P(None, "dp", "tensor"), P("tensor", "dp")
    router, gateup, down = P("dp", None), P(None, None, "dp", "tensor"), P(None, "tensor", "dp")
    states = tuple(
        spec for one in (gains, query, keyval, out, router, gateup, down) for spec in (one,) * 3
    )
    return jax.shard_map(
        shards,
        mesh=mesh,
        in_specs=(tokens, tokens, tokens, P("dp")) + states,
        out_specs=(tokens, tokens) + states,
        check_vma=False,
    )
```

```python
import functools

import jax
import jax.numpy as jnp
from jax import lax
from jax.experimental import pallas as pl
from jax.experimental.pallas import tpu as pltpu
from jax.sharding import PartitionSpec as P

MODEL_DIM = 1536
QUERY_HEADS = 24
HEAD_DIM = 64
F = 512
SEQUENCE_LENGTH = 1024
STEP = 10

NORM_EPSILON = 1e-06
SCORE_SCALE = 0.015625
RESIDUAL_SCALE = 0.22
ROPE_BASE = 10000.0
FIRST_DECAY = 0.9
SECOND_DECAY = 0.95
ADAM_EPSILON = 1e-08
WEIGHT_DECAY = 0.1
GAIN_RATE = 0.6
MASK_VALUE = -1e30
HIGHEST_PRECISION = lax.Precision.HIGHEST

BF16 = jnp.bfloat16
F32 = jnp.float32
LANES = 128
ROWS = 256
VMEM_BYTES = 58 * 1024 * 1024

NN = (((1,), (0,)), ((), ()))
NT = (((1,), (1,)), ((), ()))
TN = (((0,), (0,)), ((), ()))


def dot(a, b, dims=NN):
    return lax.dot_general(a, b, dims, preferred_element_type=F32)


def seq_positions(segment_row):
    counter = jnp.arange(segment_row.shape[0], dtype=jnp.int32)
    earlier = jnp.concatenate([segment_row[:1] - 1, segment_row[:-1]])
    starts = lax.cummax(jnp.where(segment_row != earlier, counter, 0), axis=0)
    return counter - starts


def rope_tables(positions):
    half_width = HEAD_DIM // 2
    frequency = ROPE_BASE ** (-2.0 * jnp.arange(half_width, dtype=F32) / HEAD_DIM)
    angles = positions.astype(F32)[:, None] * frequency[None, :]
    cosine, sine = jnp.cos(angles), jnp.sin(angles)
    return (
        jnp.concatenate([cosine] * 4, axis=1),
        jnp.concatenate([-sine, sine] * 2, axis=1),
    )


def rotate_halves(slab):
    lane = lax.broadcasted_iota(jnp.int32, slab.shape, 1)
    ahead = pltpu.roll(slab, LANES - HEAD_DIM // 2, 1)
    behind = pltpu.roll(slab, HEAD_DIM // 2, 1)
    return jnp.where(lane % HEAD_DIM < HEAD_DIM // 2, ahead, behind)


def half_mask(rows, upper):
    lane = lax.broadcasted_iota(jnp.int32, (rows, LANES), 1)
    return (lane >= HEAD_DIM) if upper else (lane < HEAD_DIM)


def spread_heads(slab, lower_out, upper_out, index):
    rows = slab.shape[0]
    moved = pltpu.roll(slab.astype(F32), HEAD_DIM, 1).astype(BF16)
    zero = jnp.zeros_like(slab)
    low, high = half_mask(rows, False), half_mask(rows, True)
    lower_out[index] = jnp.where(low, slab, zero)
    upper_out[index] = jnp.where(high, moved, zero)
    lower_out[index + 1] = jnp.where(low, moved, zero)
    upper_out[index + 1] = jnp.where(high, slab, zero)


def fill_bias(bias, seg_col, seg_row):
    span = bias.shape[0]
    for at in range(0, span, ROWS):
        rows_at = at + lax.broadcasted_iota(jnp.int32, (ROWS, span), 0)
        cols_at = lax.broadcasted_iota(jnp.int32, (ROWS, span), 1)
        allowed = (rows_at >= cols_at) & (seg_col[at : at + ROWS, :] == seg_row[...])
        bias[at : at + ROWS, :] = jnp.where(allowed, 0.0, MASK_VALUE).astype(F32)


def attention_forward_kernel(
    lin_ref, kv_ref, cos_ref, sin_ref, seg_col, seg_row,
    out_ref, q_ref, k_ref, v_ref, lse_ref,
    bias, k_low, k_high, v_low, v_high,
):
    slab_at = pl.program_id(0)
    span = lin_ref.shape[0]
    kv_slabs = kv_ref.shape[1] // (2 * LANES)

    @pl.when(slab_at == 0)
    def _():
        fill_bias(bias, seg_col, seg_row)
        for j in range(kv_slabs):
            lanes = slice(j * LANES, (j + 1) * LANES)
            lin = kv_ref[:, lanes]
            keys = (lin * cos_ref[...] + rotate_halves(lin) * sin_ref[...]).astype(BF16)
            k_ref[:, lanes] = keys
            spread_heads(keys, k_low, k_high, 2 * j)
            lanes = slice((kv_slabs + j) * LANES, (kv_slabs + j + 1) * LANES)
            values = kv_ref[:, lanes].astype(BF16)
            v_ref[:, slice(j * LANES, (j + 1) * LANES)] = values
            spread_heads(values, v_low, v_high, 2 * j)

    lin = lin_ref[...]
    q_ref[...] = (lin * cos_ref[...] + rotate_halves(lin) * sin_ref[...]).astype(BF16)
    kv_even, kv_odd = (2 * slab_at) // 3, (2 * slab_at + 1) // 3
    for at in range(0, span, ROWS):
        rows = slice(at, at + ROWS)
        queries = q_ref[rows, :]
        total = None
        stats = []
        for keys, values, kv_at in ((k_low, v_low, kv_even), (k_high, v_high, kv_odd)):
            upto = at + ROWS
            scores = dot(queries, keys[kv_at, :upto, :], NT) * SCORE_SCALE + bias[rows, :upto]
            highest = jnp.max(scores, axis=1, keepdims=True)
            weights = jnp.exp(scores - highest)
            summed = jnp.sum(weights, axis=1, keepdims=True)
            probability = (weights * (1.0 / summed)).astype(BF16)
            part = dot(probability, values[kv_at, :upto, :])
            total = part if total is None else total + part
            stats.append(highest + jnp.log(summed))
        out_ref[rows, :] = total.astype(BF16)
        spread = jnp.where(half_mask(ROWS, False), stats[0], stats[1])
        turned = spread.T
        lse_ref[0, 0:1, rows] = turned[0:1, :]
        lse_ref[0, 1:2, rows] = turned[HEAD_DIM : HEAD_DIM + 1, :]


def attention_forward(qkv_lin, cosine, sine, segment_row):
    span = qkv_lin.shape[0]
    q_width = MODEL_DIM // 2
    kv_width = (qkv_lin.shape[1] - q_width) // 2
    slabs, kv_heads = q_width // LANES, kv_width // HEAD_DIM
    whole = lambda shape: pl.BlockSpec(shape, lambda g: (0,) * len(shape))
    slab = pl.BlockSpec((span, LANES), lambda g: (0, g))
    q_lin, kv_lin = qkv_lin[:, :q_width], qkv_lin[:, q_width:]
    return pl.pallas_call(
        attention_forward_kernel,
        grid=(slabs,),
        in_specs=[
            slab, whole((span, 2 * kv_width)), whole((span, LANES)), whole((span, LANES)),
            whole((span, 1)), whole((1, span)),
        ],
        out_specs=[
            slab, slab, whole((span, kv_width)), whole((span, kv_width)),
            pl.BlockSpec((1, 8, span), lambda g: (g, 0, 0)),
        ],
        out_shape=[
            jax.ShapeDtypeStruct((span, q_width), BF16),
            jax.ShapeDtypeStruct((span, q_width), BF16),
            jax.ShapeDtypeStruct((span, kv_width), BF16),
            jax.ShapeDtypeStruct((span, kv_width), BF16),
            jax.ShapeDtypeStruct((slabs, 8, span), F32),
        ],
        scratch_shapes=[pltpu.VMEM((span, span), F32)]
        + [pltpu.VMEM((kv_heads, span, LANES), BF16)] * 4,
        compiler_params=pltpu.CompilerParams(vmem_limit_bytes=VMEM_BYTES),
        cost_estimate=pl.CostEstimate(
            flops=4 * slabs * span * span * LANES, bytes_accessed=16 * span * q_width,
            transcendentals=slabs * span * span,
        ),
        name="attention_forward",
    )(q_lin, kv_lin, cosine, sine, segment_row[:, None], segment_row[None, :])


def attention_backward_kernel(
    q_ref, k_ref, v_ref, out_ref, grad_ref, cos_ref, sin_ref, seg_col, seg_row, lse_ref,
    dq_ref, dkv_ref,
    bias, k_low, k_high, v_low, v_high, dk_low, dk_high, dv_low, dv_high, dq_sum,
):
    slab_at = pl.program_id(0)
    span = q_ref.shape[0]
    kv_slabs = k_ref.shape[1] // LANES

    @pl.when(slab_at == 0)
    def _():
        for at in range(0, span, ROWS):
            keys_at = at + lax.broadcasted_iota(jnp.int32, (ROWS, span), 0)
            rows_at = lax.broadcasted_iota(jnp.int32, (ROWS, span), 1)
            allowed = (rows_at >= keys_at) & (seg_col[at : at + ROWS, :] == seg_row[...])
            bias[at : at + ROWS, :] = jnp.where(allowed, 0.0, MASK_VALUE).astype(F32)
        for j in range(kv_slabs):
            lanes = slice(j * LANES, (j + 1) * LANES)
            spread_heads(k_ref[:, lanes], k_low, k_high, 2 * j)
            spread_heads(v_ref[:, lanes], v_low, v_high, 2 * j)
        for sums in (dk_low, dk_high, dv_low, dv_high):
            sums[...] = jnp.zeros_like(sums)

    kv_even, kv_odd = (2 * slab_at) // 3, (2 * slab_at + 1) // 3
    for at in range(0, span, ROWS):
        rows = slice(at, at + ROWS)
        upto = at + ROWS
        queries, grads = q_ref[rows, :], grad_ref[rows, :]
        turned = (grads.astype(F32) * out_ref[rows, :].astype(F32)).T
        zero = jnp.zeros_like(queries)
        dq_part = None
        for upper, keys, values, dk_sum, dv_sum, kv_at in (
            (False, k_low, v_low, dk_low, dv_low, kv_even),
            (True, k_high, v_high, dk_high, dv_high, kv_odd),
        ):
            first = HEAD_DIM if upper else 0
            delta = jnp.sum(turned[first : first + HEAD_DIM, :], axis=0, keepdims=True)
            head = 1 if upper else 0
            total = lse_ref[0, head : head + 1, rows]
            keys_here = keys[kv_at, :upto, :]
            scores = dot(keys_here, queries, NT) * SCORE_SCALE + bias[:upto, rows]
            probability = jnp.exp(scores - total)
            prob_grad = dot(values[kv_at, :upto, :], grads, NT)
            score_grad = (probability * (prob_grad - delta)).astype(BF16)
            mask = half_mask(ROWS, upper)
            dv_sum[kv_at, :upto, :] += dot(
                probability.astype(BF16), jnp.where(mask, grads, zero)
            )
            dk_sum[kv_at, :upto, :] += dot(score_grad, jnp.where(mask, queries, zero))
            part = dot(score_grad, keys_here, TN)
            dq_part = part if dq_part is None else dq_part + part
        dq_sum[rows, :] = dq_part * SCORE_SCALE
    slab = dq_sum[...]
    dq_ref[...] = (slab * cos_ref[...] - rotate_halves(slab) * sin_ref[...]).astype(BF16)

    @pl.when(slab_at == pl.num_programs(0) - 1)
    def _():
        low = half_mask(span, False)

        def joined(sums_low, sums_high, j):
            one = sums_low[2 * j] + pltpu.roll(sums_high[2 * j], HEAD_DIM, 1)
            two = pltpu.roll(sums_low[2 * j + 1], HEAD_DIM, 1) + sums_high[2 * j + 1]
            return jnp.where(low, one, two)

        for j in range(kv_slabs):
            slab = joined(dk_low, dk_high, j) * SCORE_SCALE
            dkv_ref[:, j * LANES : (j + 1) * LANES] = (
                slab * cos_ref[...] - rotate_halves(slab) * sin_ref[...]
            ).astype(BF16)
            at = (kv_slabs + j) * LANES
            dkv_ref[:, at : at + LANES] = joined(dv_low, dv_high, j).astype(BF16)


def attention_backward(queries, keys, values, attended, grad, cosine, sine, segment_row, lse):
    span, q_width = queries.shape
    kv_width = keys.shape[1]
    slabs, kv_heads = q_width // LANES, kv_width // HEAD_DIM
    whole = lambda shape: pl.BlockSpec(shape, lambda g: (0,) * len(shape))
    slab = pl.BlockSpec((span, LANES), lambda g: (0, g))
    return pl.pallas_call(
        attention_backward_kernel,
        grid=(slabs,),
        in_specs=[
            slab, whole((span, kv_width)), whole((span, kv_width)), slab, slab,
            whole((span, LANES)), whole((span, LANES)), whole((span, 1)), whole((1, span)),
            pl.BlockSpec((1, 8, span), lambda g: (g, 0, 0)),
        ],
        out_specs=[slab, whole((span, 2 * kv_width))],
        out_shape=[
            jax.ShapeDtypeStruct((span, q_width), BF16),
            jax.ShapeDtypeStruct((span, 2 * kv_width), BF16),
        ],
        scratch_shapes=[pltpu.VMEM((span, span), F32)]
        + [pltpu.VMEM((kv_heads, span, LANES), BF16)] * 4
        + [pltpu.VMEM((kv_heads, span, LANES), F32)] * 4
        + [pltpu.VMEM((span, LANES), F32)],
        compiler_params=pltpu.CompilerParams(vmem_limit_bytes=VMEM_BYTES),
        cost_estimate=pl.CostEstimate(
            flops=10 * slabs * span * span * LANES, bytes_accessed=16 * span * q_width,
            transcendentals=slabs * span * span,
        ),
        name="attention_backward",
    )(
        queries, keys, values, attended, grad, cosine, sine,
        segment_row[:, None], segment_row[None, :], lse,
    )


def experts_kernel(
    rows_at, first, x_ref, xt_ref, og_ref, ogt_ref, combine_ref, *refs
):
    pieces, refs = refs[:4], refs[4:]
    mix_in, dx_in, gate_in = refs[:3]
    grads, refs = refs[3:7], refs[7:]
    mix_ref, dx_ref, gate_ref, w_ref, grad_ref, held = refs
    expert = first[0] + pl.program_id(0)
    tokens, width = x_ref.shape
    hidden = held.shape[1] // 3
    slots, own = pieces[0].shape[0], pieces[0].shape[2]
    tile = 512

    @pl.when(pl.program_id(0) == 0)
    def _():
        mix_ref[...] = mix_in[...]
        dx_ref[...] = dx_in[...]
        gate_ref[...] = gate_in[...]

    for group, piece in enumerate(pieces):
        for slot in range(slots):
            at = pl.multiple_of(rows_at[group * slots + slot], own)
            w_ref[pl.ds(at, own), :] = piece[slot, 0]

    def forward_rows(step, carry):
        rows = pl.ds(pl.multiple_of(step * ROWS, ROWS), ROWS)
        gate_up = dot(x_ref[rows, :], w_ref[:, : 2 * hidden])
        raw = dot(og_ref[rows, :], w_ref[:, 2 * hidden :]) * RESIDUAL_SCALE
        gate, up = gate_up[:, :hidden], gate_up[:, hidden:]
        lane = lax.broadcasted_iota(jnp.int32, (ROWS, combine_ref.shape[1]), 1)
        column = jnp.sum(
            jnp.where(lane == expert, combine_ref[rows, :], 0.0), axis=1, keepdims=True
        )
        sigmoid = 1.0 / (1.0 + jnp.exp(-gate))
        active = gate * sigmoid
        inner = (active * up).astype(BF16).astype(F32)
        chosen = (inner * column).astype(BF16)
        held[rows, 2 * hidden :] = chosen
        gate_grad = jnp.sum(inner * raw, axis=1, keepdims=True)
        gate_ref[rows, :] = jnp.where(lane == expert, gate_grad, gate_ref[rows, :])
        inner_grad = raw * column
        held[rows, :hidden] = (
            inner_grad * up * sigmoid * (1.0 + gate * (1.0 - sigmoid))
        ).astype(BF16)
        held[rows, hidden : 2 * hidden] = (inner_grad * active).astype(BF16)
        for at in range(0, width, tile):
            cols = slice(at, at + tile)
            mix_ref[rows, cols] += dot(chosen, w_ref[cols, 2 * hidden :], NT)
            dx_ref[rows, cols] += dot(held[rows, : 2 * hidden], w_ref[cols, : 2 * hidden], NT)
        return carry

    lax.fori_loop(0, tokens // ROWS, forward_rows, 0)

    def grad_rows(step, carry):
        rows = pl.ds(pl.multiple_of(step * ROWS, ROWS), ROWS)
        grad_ref[rows, : 2 * hidden] = dot(xt_ref[rows, :], held[:, : 2 * hidden]).astype(BF16)
        grad_ref[rows, 2 * hidden :] = (
            dot(ogt_ref[rows, :], held[:, 2 * hidden :]) * RESIDUAL_SCALE
        ).astype(BF16)
        return carry

    lax.fori_loop(0, width // ROWS, grad_rows, 0)

    for group, grad in enumerate(grads):
        for slot in range(slots):
            at = pl.multiple_of(rows_at[group * slots + slot], own)
            grad[slot, 0] = grad_ref[pl.ds(at, own), :]


def experts_pass(rows_at, first, x, xt, out_grad, ogt, combine, pieces, sums):
    tokens, width = x.shape
    experts = combine.shape[1]
    slots, count, own, block = pieces[0].shape
    whole = lambda shape: pl.BlockSpec(
        shape, lambda e, *_: (0,) * len(shape), pipeline_mode=pl.Buffered(1)
    )
    piece = pl.BlockSpec((slots, 1, own, block), lambda e, *_: (0, e, 0, 0))
    state = [whole((tokens, width)), whole((tokens, width)), whole((tokens, experts))]
    outs = pl.pallas_call(
        experts_kernel,
        grid_spec=pltpu.PrefetchScalarGridSpec(
            num_scalar_prefetch=2,
            grid=(count,),
            in_specs=[
                whole((tokens, width)), whole((width, tokens)),
                whole((tokens, width)), whole((width, tokens)),
                whole((tokens, experts)),
            ]
            + [piece] * 4
            + state,
            out_specs=[piece] * 4 + state,
            scratch_shapes=[
                pltpu.VMEM((width, block), BF16),
                pltpu.VMEM((width, block), BF16),
                pltpu.VMEM((tokens, block), BF16),
            ],
        ),
        out_shape=[jax.ShapeDtypeStruct(pieces[0].shape, BF16)] * 4
        + [
            jax.ShapeDtypeStruct((tokens, width), F32),
            jax.ShapeDtypeStruct((tokens, width), F32),
            jax.ShapeDtypeStruct((tokens, experts), F32),
        ],
        input_output_aliases={11: 4, 12: 5, 13: 6},
        compiler_params=pltpu.CompilerParams(vmem_limit_bytes=VMEM_BYTES),
        cost_estimate=pl.CostEstimate(
            flops=6 * tokens * width * count * block,
            bytes_accessed=4 * count * width * block + 36 * tokens * width, transcendentals=0,
        ),
        name="experts_pass",
    )(rows_at, first, x, xt, out_grad, ogt, combine, *pieces, *sums)
    return outs[:4], outs[4:]


SLOTS = 4
Z_FROM = (0, -1, 1, 2)


def group_permute(array, dz, dy, dx, total):
    inner = total // 16
    pairs = []
    for at in range(16):
        z, y, x = at // 4, at // 2 % 2, at % 2
        to = ((z + dz) % 4) * 4 + (y ^ dy) * 2 + (x ^ dx)
        pairs += [(at * inner + i, to * inner + i) for i in range(inner)]
    return lax.ppermute(array, "dp", pairs)


def inner_groups(total):
    inner = total // 16
    return [[at * inner + i for i in range(inner)] for at in range(16)]


def slot_rows(total, rows):
    at = lax.axis_index("dp") // (total // 16)
    z, y, x = at // 4, at // 2 % 2, at % 2
    starts = []
    for dy, dx in ((0, 0), (1, 0), (0, 1), (1, 1)):
        for dz in Z_FROM:
            starts.append((((z + dz + 4) % 4) * 4 + (y ^ dy) * 2 + (x ^ dx)) * rows)
    return jnp.stack(starts).astype(jnp.int32)


def gather_pieces(shard, total, turn):
    move = functools.partial(group_permute, total=total)
    if total > 16:
        shard = lax.all_gather(
            shard, "dp", axis=1, tiled=True, axis_index_groups=inner_groups(total)
        )
    own = jnp.stack([shard] + [move(shard, -dz, 0, 0) for dz in Z_FROM[1:]])
    along_y = move(own, 0, 1, 0)
    along_x = move(own, 0, 0, 1)
    both = move(along_y, 0, 0, 1) if turn == 0 else move(along_x, 0, 1, 0)
    return own, along_y, along_x, both


def scatter_pieces(grads, total, turn):
    move = functools.partial(group_permute, total=total)
    own, along_y, along_x, both = grads
    if turn == 0:
        got, got_both = move(along_x, 0, 0, 1), move(both, 0, 0, 1)
        passed = (along_y.astype(F32) + got_both.astype(F32)).astype(BF16)
        last = move(passed, 0, 1, 0)
    else:
        got, got_both = move(along_y, 0, 1, 0), move(both, 0, 1, 0)
        passed = (along_x.astype(F32) + got_both.astype(F32)).astype(BF16)
        last = move(passed, 0, 0, 1)
    sums = [
        own[k].astype(F32) + got[k].astype(F32) + last[k].astype(F32) for k in range(SLOTS)
    ]
    result = sums[0]
    moved = [move(sums[k].astype(BF16), Z_FROM[k], 0, 0) for k in range(1, SLOTS)]
    for one in moved:
        result = result + one.astype(F32)
    if total > 16:
        result = lax.psum_scatter(
            result, "dp", scatter_dimension=1, tiled=True, axis_index_groups=inner_groups(total)
        )
    return result, got_both, last, moved[-1]


def split_three(values):
    high = values.astype(BF16)
    rest = values - high.astype(F32)
    middle = rest.astype(BF16)
    low = (rest - middle.astype(F32)).astype(BF16)
    return [high, middle, low]


def pair_sum(part):
    other = lax.ppermute(part, "tensor", [(0, 1), (1, 0)])
    return part.astype(F32) + other.astype(F32)


def norm_backward(values, inverse, gain_row, upstream):
    scaled = values * inverse
    weighted = upstream * gain_row
    mean_term = jnp.mean(weighted * scaled, axis=-1, keepdims=True)
    return (inverse * (weighted - scaled * mean_term), jnp.sum(upstream * scaled, axis=0))


def adam_update(value, gradient, mean_old, square_old, rate, decay):
    mean_new = FIRST_DECAY * mean_old + (1.0 - FIRST_DECAY) * gradient
    square_new = SECOND_DECAY * square_old + (1.0 - SECOND_DECAY) * gradient * gradient
    mean_hat = mean_new / (1.0 - FIRST_DECAY**STEP)
    square_hat = square_new / (1.0 - SECOND_DECAY**STEP)
    updated = value - rate * (mean_hat / (jnp.sqrt(square_hat) + ADAM_EPSILON) + decay * value)
    return (mean_new, square_new, updated)


def shards(
    hidden_in,
    out_grad,
    routes,
    segments,
    norm_gains,
    gains_mean,
    gains_square,
    w_query,
    query_mean,
    query_square,
    key_value_weight,
    key_value_first_moment,
    key_value_second_moment,
    w_out,
    out_mean,
    out_square,
    w_router,
    router_mean,
    router_square,
    w_gateup,
    gateup_mean,
    gateup_square,
    w_down,
    down_mean,
    down_square,
):
    tokens, width = hidden_in.shape
    own = w_query.shape[0]
    experts, hidden = w_down.shape[0], w_down.shape[1]
    q_width, kv_width = w_query.shape[1], key_value_weight.shape[2]
    qkv_width = q_width + 2 * kv_width
    small_width = 3 * (2 + experts)
    attention_width = qkv_width + q_width
    attention_shard = jnp.concatenate(
        [
            w_query.astype(BF16),
            key_value_weight[0].astype(BF16),
            key_value_weight[1].astype(BF16),
            w_out.T.astype(BF16),
        ]
        + split_three(jnp.concatenate([norm_gains.T, w_router], axis=1))
        + [jnp.zeros((own, LANES - small_width), BF16)],
        axis=1,
    )
    expert_shard = jnp.concatenate(
        [
            w_gateup[:, 0].astype(BF16),
            w_gateup[:, 1].astype(BF16),
            w_down.astype(BF16).transpose(0, 2, 1),
        ],
        axis=2,
    )
    total = lax.axis_size("dp")
    chunk = 2
    starts = range(0, experts, chunk)
    attention_full = lax.all_gather(attention_shard, "dp", axis=0, tiled=True)
    expert_pieces = [
        gather_pieces(expert_shard[at : at + chunk], total, at // chunk % 2) for at in starts
    ]
    qkv_full = attention_full[:, :qkv_width]
    output_full = attention_full[:, qkv_width:attention_width]
    pieces = attention_full[:, attention_width : attention_width + small_width].astype(F32)
    each = 2 + experts
    small = pieces[:, :each] + pieces[:, each : 2 * each] + pieces[:, 2 * each :]
    gains_full, router_full = small[:, :2].T, small[:, 2:]

    inputs = hidden_in.astype(F32)
    inverse_one = lax.rsqrt(jnp.mean(inputs * inputs, axis=-1, keepdims=True) + NORM_EPSILON)
    normed_low = (inputs * inverse_one * gains_full[0]).astype(BF16)
    qkv_lin = jnp.dot(normed_low, qkv_full, preferred_element_type=F32)
    cosine, sine = rope_tables(seq_positions(segments))
    attended, queries, keys, values, lse = attention_forward(qkv_lin, cosine, sine, segments)
    attention_part = lax.dot_general(attended, output_full, NT, preferred_element_type=F32)
    attention = pair_sum(attention_part.astype(BF16))
    middle = inputs + RESIDUAL_SCALE * attention
    inverse_two = lax.rsqrt(jnp.mean(middle * middle, axis=-1, keepdims=True) + NORM_EPSILON)
    normed_two = middle * inverse_two * gains_full[1]
    normed_two_low = normed_two.astype(BF16)
    logits = jnp.dot(normed_two, router_full, precision=HIGHEST_PRECISION)
    expert_ids = jnp.arange(experts, dtype=jnp.int32)
    chosen = jnp.any(routes[:, :, None] == expert_ids[None, None, :], axis=1)
    combine = jax.nn.softmax(jnp.where(chosen, logits, -jnp.inf), axis=-1)

    rows_at = slot_rows(total, width // 16)
    sums = (
        jnp.zeros((tokens, width), F32),
        jnp.zeros((tokens, width), F32),
        jnp.zeros((tokens, experts), F32),
    )
    x_turned, og_turned = normed_two_low.T, out_grad.T
    shares, first_moves, second_moves, third_moves = [], [], [], []
    for at, pieces in zip(starts, expert_pieces):
        where = jnp.full((1,), at, jnp.int32)
        step = at // chunk
        for moves, behind in ((first_moves, 2), (second_moves, 3), (third_moves, 5)):
            if step >= behind:
                where = lax.optimization_barrier((where, moves[step - behind]))[0]
        grads, sums = experts_pass(
            rows_at, where, normed_two_low, x_turned, out_grad, og_turned,
            combine, pieces, sums,
        )
        share, one, two, three = scatter_pieces(grads, total, step % 2)
        shares.append(share)
        first_moves.append(one)
        second_moves.append(two)
        third_moves.append(three)
    mix_part, dx_part, gate_part = sums
    expert_share = jnp.concatenate(shares)
    normed_two_part = pair_sum(dx_part.astype(BF16))
    gate_grad = pair_sum(gate_part)
    expert_mix = pair_sum(mix_part.astype(BF16))
    block_out = (middle + RESIDUAL_SCALE * expert_mix).astype(BF16)

    logit_grad = combine * (gate_grad - jnp.sum(combine * gate_grad, axis=-1, keepdims=True))
    router_grad = jnp.dot(normed_two.T, logit_grad, precision=HIGHEST_PRECISION)
    normed_two_grad = normed_two_part + jnp.dot(
        logit_grad, router_full.T, precision=HIGHEST_PRECISION
    )
    middle_part, gain_two_grad = norm_backward(middle, inverse_two, gains_full[1], normed_two_grad)
    middle_grad = out_grad.astype(F32) + middle_part
    attention_back = (RESIDUAL_SCALE * middle_grad).astype(BF16)
    attended_grad = jnp.dot(attention_back, output_full, preferred_element_type=F32).astype(BF16)
    query_grad, keyval_grad = attention_backward(
        queries, keys, values, attended, attended_grad, cosine, sine, segments, lse
    )
    qkv_grad = jnp.concatenate([query_grad, keyval_grad], axis=1)
    normed_part = lax.dot_general(qkv_grad, qkv_full, NT, preferred_element_type=F32)
    normed_grad = pair_sum(normed_part.astype(BF16))
    qkv_weight_grad = lax.dot_general(normed_low, qkv_grad, TN, preferred_element_type=F32)
    output_weight_grad = lax.dot_general(attention_back, attended, TN, preferred_element_type=F32)
    input_part, gain_one_grad = norm_backward(inputs, inverse_one, gains_full[0], normed_grad)
    input_grad = middle_grad + input_part
    small_grads = jnp.concatenate(
        [gain_one_grad[:, None], gain_two_grad[:, None], router_grad], axis=1
    )
    attention_share = lax.psum_scatter(
        jnp.concatenate(
            [qkv_weight_grad.astype(BF16), output_weight_grad.astype(BF16)], axis=1
        ),
        "dp", scatter_dimension=0, tiled=True,
    ).astype(F32)
    small_share = lax.psum_scatter(small_grads, "dp", scatter_dimension=0, tiled=True)

    gains_share, router_share = small_share[:, :2].T, small_share[:, 2:]
    query_share = attention_share[:, :q_width]
    keyval_share = jnp.stack(
        [
            attention_share[:, q_width : q_width + kv_width],
            attention_share[:, q_width + kv_width : qkv_width],
        ]
    )
    output_share = attention_share[:, qkv_width:].T
    expert_share = expert_share.reshape(experts, own, 3, hidden)
    gateup_share = expert_share[:, :, :2].transpose(0, 2, 1, 3)
    down_share = expert_share[:, :, 2].transpose(0, 2, 1)

    gains_result = adam_update(norm_gains, gains_share, gains_mean, gains_square, GAIN_RATE, 0.0)
    query_result = adam_update(
        w_query, query_share, query_mean, query_square, (MODEL_DIM // 12) ** (-0.5), WEIGHT_DECAY
    )
    keyval_result = adam_update(
        key_value_weight,
        keyval_share,
        key_value_first_moment,
        key_value_second_moment,
        (MODEL_DIM // 12) ** (-0.5),
        WEIGHT_DECAY,
    )
    out_result = adam_update(
        w_out,
        output_share,
        out_mean,
        out_square,
        max(1, QUERY_HEADS * HEAD_DIM // 96) ** (-0.5),
        WEIGHT_DECAY,
    )
    router_result = adam_update(
        w_router, router_share, router_mean, router_square, (4 * MODEL_DIM) ** (-0.5), WEIGHT_DECAY
    )
    gateup_result = adam_update(
        w_gateup, gateup_share, gateup_mean, gateup_square, MODEL_DIM ** (-0.5), WEIGHT_DECAY
    )
    down_result = adam_update(
        w_down, down_share, down_mean, down_square, max(1, F // 256) ** (-0.5), WEIGHT_DECAY
    )
    return (
        (block_out, input_grad)
        + gains_result
        + query_result
        + keyval_result
        + out_result
        + router_result
        + gateup_result
        + down_result
    )


def solution(mesh):
    tokens, gains = P("dp", None), P(None, "dp")
    query, keyval, out = P("dp", "tensor"), P(None, "dp", "tensor"), P("tensor", "dp")
    router, gateup, down = P("dp", None), P(None, None, "dp", "tensor"), P(None, "tensor", "dp")
    states = tuple(
        spec for one in (gains, query, keyval, out, router, gateup, down) for spec in (one,) * 3
    )
    return jax.shard_map(
        shards,
        mesh=mesh,
        in_specs=(tokens, tokens, tokens, P("dp")) + states,
        out_specs=(tokens, tokens) + states,
        check_vma=False,
    )
```

```python
import functools

import jax
import jax.numpy as jnp
from jax import lax
from jax.experimental import pallas as pl
from jax.experimental.pallas import tpu as pltpu
from jax.sharding import PartitionSpec as P

MODEL_DIM = 1536
QUERY_HEADS = 24
HEAD_DIM = 64
F = 512
SEQUENCE_LENGTH = 1024
STEP = 10

NORM_EPSILON = 1e-06
SCORE_SCALE = 0.015625
RESIDUAL_SCALE = 0.22
ROPE_BASE = 10000.0
FIRST_DECAY = 0.9
SECOND_DECAY = 0.95
ADAM_EPSILON = 1e-08
WEIGHT_DECAY = 0.1
GAIN_RATE = 0.6
MASK_VALUE = -1e30
HIGHEST_PRECISION = lax.Precision.HIGHEST

BF16 = jnp.bfloat16
F32 = jnp.float32
LANES = 128
ROWS = 256
VMEM_BYTES = 58 * 1024 * 1024

NN = (((1,), (0,)), ((), ()))
NT = (((1,), (1,)), ((), ()))
TN = (((0,), (0,)), ((), ()))


def dot(a, b, dims=NN):
    return lax.dot_general(a, b, dims, preferred_element_type=F32)


def seq_positions(segment_row):
    counter = jnp.arange(segment_row.shape[0], dtype=jnp.int32)
    earlier = jnp.concatenate([segment_row[:1] - 1, segment_row[:-1]])
    starts = lax.cummax(jnp.where(segment_row != earlier, counter, 0), axis=0)
    return counter - starts


def rope_tables(positions):
    half_width = HEAD_DIM // 2
    frequency = ROPE_BASE ** (-2.0 * jnp.arange(half_width, dtype=F32) / HEAD_DIM)
    angles = positions.astype(F32)[:, None] * frequency[None, :]
    cosine, sine = jnp.cos(angles), jnp.sin(angles)
    return (
        jnp.concatenate([cosine] * 4, axis=1),
        jnp.concatenate([-sine, sine] * 2, axis=1),
    )


def rotate_halves(slab):
    lane = lax.broadcasted_iota(jnp.int32, slab.shape, 1)
    ahead = pltpu.roll(slab, LANES - HEAD_DIM // 2, 1)
    behind = pltpu.roll(slab, HEAD_DIM // 2, 1)
    return jnp.where(lane % HEAD_DIM < HEAD_DIM // 2, ahead, behind)


def half_mask(rows, upper):
    lane = lax.broadcasted_iota(jnp.int32, (rows, LANES), 1)
    return (lane >= HEAD_DIM) if upper else (lane < HEAD_DIM)


def spread_heads(slab, lower_out, upper_out, index):
    rows = slab.shape[0]
    moved = pltpu.roll(slab.astype(F32), HEAD_DIM, 1).astype(BF16)
    zero = jnp.zeros_like(slab)
    low, high = half_mask(rows, False), half_mask(rows, True)
    lower_out[index] = jnp.where(low, slab, zero)
    upper_out[index] = jnp.where(high, moved, zero)
    lower_out[index + 1] = jnp.where(low, moved, zero)
    upper_out[index + 1] = jnp.where(high, slab, zero)


def fill_bias(bias, seg_col, seg_row):
    span = bias.shape[0]
    for at in range(0, span, ROWS):
        rows_at = at + lax.broadcasted_iota(jnp.int32, (ROWS, span), 0)
        cols_at = lax.broadcasted_iota(jnp.int32, (ROWS, span), 1)
        allowed = (rows_at >= cols_at) & (seg_col[at : at + ROWS, :] == seg_row[...])
        bias[at : at + ROWS, :] = jnp.where(allowed, 0.0, MASK_VALUE).astype(F32)


def with_earlier(kernel, inputs, count):
    def run(*refs):
        kernel(*refs[:inputs], *refs[inputs + count :])

    return run


def any_specs(arrays):
    return [pl.BlockSpec(memory_space=pl.ANY)] * len(arrays)


def attention_forward_kernel(
    lin_ref, kv_ref, cos_ref, sin_ref, seg_col, seg_row,
    out_ref, q_ref, k_ref, v_ref, lse_ref,
    bias, k_low, k_high, v_low, v_high,
):
    slab_at = pl.program_id(0)
    span = lin_ref.shape[0]
    kv_slabs = kv_ref.shape[1] // (2 * LANES)

    @pl.when(slab_at == 0)
    def _():
        fill_bias(bias, seg_col, seg_row)
        for j in range(kv_slabs):
            lanes = slice(j * LANES, (j + 1) * LANES)
            lin = kv_ref[:, lanes]
            keys = (lin * cos_ref[...] + rotate_halves(lin) * sin_ref[...]).astype(BF16)
            k_ref[:, lanes] = keys
            spread_heads(keys, k_low, k_high, 2 * j)
            lanes = slice((kv_slabs + j) * LANES, (kv_slabs + j + 1) * LANES)
            values = kv_ref[:, lanes].astype(BF16)
            v_ref[:, slice(j * LANES, (j + 1) * LANES)] = values
            spread_heads(values, v_low, v_high, 2 * j)

    lin = lin_ref[...]
    q_ref[...] = (lin * cos_ref[...] + rotate_halves(lin) * sin_ref[...]).astype(BF16)
    kv_even, kv_odd = (2 * slab_at) // 3, (2 * slab_at + 1) // 3
    for at in range(0, span, ROWS):
        rows = slice(at, at + ROWS)
        queries = q_ref[rows, :]
        total = None
        stats = []
        for keys, values, kv_at in ((k_low, v_low, kv_even), (k_high, v_high, kv_odd)):
            upto = at + ROWS
            scores = dot(queries, keys[kv_at, :upto, :], NT) * SCORE_SCALE + bias[rows, :upto]
            highest = jnp.max(scores, axis=1, keepdims=True)
            weights = jnp.exp(scores - highest)
            summed = jnp.sum(weights, axis=1, keepdims=True)
            probability = (weights * (1.0 / summed)).astype(BF16)
            part = dot(probability, values[kv_at, :upto, :])
            total = part if total is None else total + part
            stats.append(highest + jnp.log(summed))
        out_ref[rows, :] = total.astype(BF16)
        spread = jnp.where(half_mask(ROWS, False), stats[0], stats[1])
        turned = spread.T
        lse_ref[0, 0:1, rows] = turned[0:1, :]
        lse_ref[0, 1:2, rows] = turned[HEAD_DIM : HEAD_DIM + 1, :]


def attention_forward(qkv_lin, cosine, sine, segment_row, earlier=()):
    span = qkv_lin.shape[0]
    q_width = MODEL_DIM // 2
    kv_width = (qkv_lin.shape[1] - q_width) // 2
    slabs, kv_heads = q_width // LANES, kv_width // HEAD_DIM
    whole = lambda shape: pl.BlockSpec(shape, lambda g: (0,) * len(shape))
    slab = pl.BlockSpec((span, LANES), lambda g: (0, g))
    q_lin, kv_lin = qkv_lin[:, :q_width], qkv_lin[:, q_width:]
    return pl.pallas_call(
        with_earlier(attention_forward_kernel, 6, len(earlier)),
        grid=(slabs,),
        in_specs=[
            slab, whole((span, 2 * kv_width)), whole((span, LANES)), whole((span, LANES)),
            whole((span, 1)), whole((1, span)),
        ]
        + any_specs(earlier),
        out_specs=[
            slab, slab, whole((span, kv_width)), whole((span, kv_width)),
            pl.BlockSpec((1, 8, span), lambda g: (g, 0, 0)),
        ],
        out_shape=[
            jax.ShapeDtypeStruct((span, q_width), BF16),
            jax.ShapeDtypeStruct((span, q_width), BF16),
            jax.ShapeDtypeStruct((span, kv_width), BF16),
            jax.ShapeDtypeStruct((span, kv_width), BF16),
            jax.ShapeDtypeStruct((slabs, 8, span), F32),
        ],
        scratch_shapes=[pltpu.VMEM((span, span), F32)]
        + [pltpu.VMEM((kv_heads, span, LANES), BF16)] * 4,
        compiler_params=pltpu.CompilerParams(vmem_limit_bytes=VMEM_BYTES),
        cost_estimate=pl.CostEstimate(
            flops=32 * slabs * span * span * LANES, bytes_accessed=16 * span * q_width,
            transcendentals=slabs * span * span,
        ),
        name="attention_forward",
    )(q_lin, kv_lin, cosine, sine, segment_row[:, None], segment_row[None, :], *earlier)


def attention_backward_kernel(
    q_ref, k_ref, v_ref, out_ref, grad_ref, cos_ref, sin_ref, seg_col, seg_row, lse_ref,
    dq_ref, dkv_ref,
    bias, k_low, k_high, v_low, v_high, dk_low, dk_high, dv_low, dv_high, dq_sum,
):
    slab_at = pl.program_id(0)
    span = q_ref.shape[0]
    kv_slabs = k_ref.shape[1] // LANES

    @pl.when(slab_at == 0)
    def _():
        for at in range(0, span, ROWS):
            keys_at = at + lax.broadcasted_iota(jnp.int32, (ROWS, span), 0)
            rows_at = lax.broadcasted_iota(jnp.int32, (ROWS, span), 1)
            allowed = (rows_at >= keys_at) & (seg_col[at : at + ROWS, :] == seg_row[...])
            bias[at : at + ROWS, :] = jnp.where(allowed, 0.0, MASK_VALUE).astype(F32)
        for j in range(kv_slabs):
            lanes = slice(j * LANES, (j + 1) * LANES)
            spread_heads(k_ref[:, lanes], k_low, k_high, 2 * j)
            spread_heads(v_ref[:, lanes], v_low, v_high, 2 * j)
        for sums in (dk_low, dk_high, dv_low, dv_high):
            sums[...] = jnp.zeros_like(sums)

    kv_even, kv_odd = (2 * slab_at) // 3, (2 * slab_at + 1) // 3
    for at in range(0, span, ROWS):
        rows = slice(at, at + ROWS)
        upto = at + ROWS
        queries, grads = q_ref[rows, :], grad_ref[rows, :]
        turned = (grads.astype(F32) * out_ref[rows, :].astype(F32)).T
        zero = jnp.zeros_like(queries)
        dq_part = None
        for upper, keys, values, dk_sum, dv_sum, kv_at in (
            (False, k_low, v_low, dk_low, dv_low, kv_even),
            (True, k_high, v_high, dk_high, dv_high, kv_odd),
        ):
            first = HEAD_DIM if upper else 0
            delta = jnp.sum(turned[first : first + HEAD_DIM, :], axis=0, keepdims=True)
            head = 1 if upper else 0
            total = lse_ref[0, head : head + 1, rows]
            keys_here = keys[kv_at, :upto, :]
            scores = dot(keys_here, queries, NT) * SCORE_SCALE + bias[:upto, rows]
            probability = jnp.exp(scores - total)
            prob_grad = dot(values[kv_at, :upto, :], grads, NT)
            score_grad = (probability * (prob_grad - delta)).astype(BF16)
            mask = half_mask(ROWS, upper)
            dv_sum[kv_at, :upto, :] += dot(
                probability.astype(BF16), jnp.where(mask, grads, zero)
            )
            dk_sum[kv_at, :upto, :] += dot(score_grad, jnp.where(mask, queries, zero))
            part = dot(score_grad, keys_here, TN)
            dq_part = part if dq_part is None else dq_part + part
        dq_sum[rows, :] = dq_part * SCORE_SCALE
    slab = dq_sum[...]
    dq_ref[...] = (slab * cos_ref[...] - rotate_halves(slab) * sin_ref[...]).astype(BF16)

    @pl.when(slab_at == pl.num_programs(0) - 1)
    def _():
        low = half_mask(span, False)

        def joined(sums_low, sums_high, j):
            one = sums_low[2 * j] + pltpu.roll(sums_high[2 * j], HEAD_DIM, 1)
            two = pltpu.roll(sums_low[2 * j + 1], HEAD_DIM, 1) + sums_high[2 * j + 1]
            return jnp.where(low, one, two)

        for j in range(kv_slabs):
            slab = joined(dk_low, dk_high, j) * SCORE_SCALE
            dkv_ref[:, j * LANES : (j + 1) * LANES] = (
                slab * cos_ref[...] - rotate_halves(slab) * sin_ref[...]
            ).astype(BF16)
            at = (kv_slabs + j) * LANES
            dkv_ref[:, at : at + LANES] = joined(dv_low, dv_high, j).astype(BF16)


def attention_backward(
    queries, keys, values, attended, grad, cosine, sine, segment_row, lse, earlier=()
):
    span, q_width = queries.shape
    kv_width = keys.shape[1]
    slabs, kv_heads = q_width // LANES, kv_width // HEAD_DIM
    whole = lambda shape: pl.BlockSpec(shape, lambda g: (0,) * len(shape))
    slab = pl.BlockSpec((span, LANES), lambda g: (0, g))
    return pl.pallas_call(
        with_earlier(attention_backward_kernel, 10, len(earlier)),
        grid=(slabs,),
        in_specs=[
            slab, whole((span, kv_width)), whole((span, kv_width)), slab, slab,
            whole((span, LANES)), whole((span, LANES)), whole((span, 1)), whole((1, span)),
            pl.BlockSpec((1, 8, span), lambda g: (g, 0, 0)),
        ]
        + any_specs(earlier),
        out_specs=[slab, whole((span, 2 * kv_width))],
        out_shape=[
            jax.ShapeDtypeStruct((span, q_width), BF16),
            jax.ShapeDtypeStruct((span, 2 * kv_width), BF16),
        ],
        scratch_shapes=[pltpu.VMEM((span, span), F32)]
        + [pltpu.VMEM((kv_heads, span, LANES), BF16)] * 4
        + [pltpu.VMEM((kv_heads, span, LANES), F32)] * 4
        + [pltpu.VMEM((span, LANES), F32)],
        compiler_params=pltpu.CompilerParams(vmem_limit_bytes=VMEM_BYTES),
        cost_estimate=pl.CostEstimate(
            flops=40 * slabs * span * span * LANES, bytes_accessed=16 * span * q_width,
            transcendentals=slabs * span * span,
        ),
        name="attention_backward",
    )(
        queries, keys, values, attended, grad, cosine, sine,
        segment_row[:, None], segment_row[None, :], lse, *earlier,
    )


EXPERT_ROWS = 256
WIDTH_ROWS = 512


def experts_kernel(
    rows_at, x_ref, og_ref, xt_ref, ogt_ref, combine_ref, own_ref, other_ref, *refs,
    first, row_steps, has_sums,
):
    sums, refs = (refs[:2], refs[2:]) if has_sums else (None, refs)
    own_grad, other_grad, mix_ref, dx_ref, gate_ref = refs[:5]
    w_both, w_down, grad_both, grad_down, held_both, held_down = refs[5:]
    step = pl.program_id(0)
    slots, halves, count, own, block = own_ref.shape
    hidden = block // 3
    width = w_both.shape[0]
    tile = 512

    def each_block():
        for group in range(2):
            for slot in range(slots):
                for half in range(halves):
                    at = rows_at[(group * slots + slot) * halves + half]
                    yield group, slot, half, pl.ds(pl.multiple_of(at, own), own)

    @pl.when(step == 0)
    def _():
        for group, slot, half, rows in each_block():
            piece = (own_ref, other_ref)[group]
            for e in range(count):
                w_both[rows, 2 * hidden * e : 2 * hidden * (e + 1)] = piece[
                    slot, half, e, :, : 2 * hidden
                ]
                w_down[rows, hidden * e : hidden * (e + 1)] = piece[slot, half, e, :, 2 * hidden :]

    @pl.when(step < row_steps)
    def _():
        rows = pl.ds(pl.multiple_of(step * EXPERT_ROWS, EXPERT_ROWS), EXPERT_ROWS)
        for e in range(count):
            both = slice(2 * hidden * e, 2 * hidden * (e + 1))
            down = slice(hidden * e, hidden * (e + 1))
            gate_up = dot(x_ref[...], w_both[:, both])
            raw = dot(og_ref[...], w_down[:, down]) * RESIDUAL_SCALE
            gate, up = gate_up[:, :hidden], gate_up[:, hidden:]
            column = combine_ref[:, first + e : first + e + 1]
            sigmoid = 1.0 / (1.0 + jnp.exp(-gate))
            active = gate * sigmoid
            inner = (active * up).astype(BF16).astype(F32)
            held_down[rows, down] = (inner * column).astype(BF16)
            gate_ref[:, e : e + 1] = jnp.sum(inner * raw, axis=1, keepdims=True)
            inner_grad = raw * column
            middle = hidden * (2 * e + 1)
            held_both[rows, 2 * hidden * e : middle] = (
                inner_grad * up * sigmoid * (1.0 + gate * (1.0 - sigmoid))
            ).astype(BF16)
            held_both[rows, middle : middle + hidden] = (inner_grad * active).astype(BF16)
        for at in range(0, width, tile):
            cols = slice(at, at + tile)
            mix = dot(held_down[rows, :], w_down[cols, :], NT)
            dx = dot(held_both[rows, :], w_both[cols, :], NT)
            if has_sums:
                mix = mix + sums[0][:, cols]
                dx = dx + sums[1][:, cols]
            mix_ref[:, cols] = mix.astype(mix_ref.dtype)
            dx_ref[:, cols] = dx.astype(dx_ref.dtype)

    @pl.when(step >= row_steps)
    def _():
        at = pl.multiple_of((step - row_steps) * WIDTH_ROWS, WIDTH_ROWS)
        rows = pl.ds(at, WIDTH_ROWS)
        grad_both[rows, :] = dot(xt_ref[...], held_both[...]).astype(BF16)
        grad_down[rows, :] = (dot(ogt_ref[...], held_down[...]) * RESIDUAL_SCALE).astype(BF16)

    @pl.when(step == pl.num_programs(0) - 1)
    def _():
        for group, slot, half, rows in each_block():
            piece = (own_grad, other_grad)[group]
            for e in range(count):
                piece[slot, half, e, :, : 2 * hidden] = grad_both[
                    rows, 2 * hidden * e : 2 * hidden * (e + 1)
                ]
                piece[slot, half, e, :, 2 * hidden :] = grad_down[
                    rows, hidden * e : hidden * (e + 1)
                ]


def experts_pass(rows_at, x, og, xt, ogt, combine, pieces, sums, first, last, earlier):
    tokens, width = x.shape
    slots, halves, count, own, block = pieces[0].shape
    hidden = block // 3
    row_steps, width_steps = tokens // EXPERT_ROWS, width // WIDTH_ROWS
    row_at = lambda s, *_: (jnp.minimum(s, row_steps - 1), 0)
    width_at = lambda s, *_: (jnp.maximum(s - row_steps, 0), 0)
    row = pl.BlockSpec((EXPERT_ROWS, width), row_at)
    turned = pl.BlockSpec((WIDTH_ROWS, tokens), width_at)
    piece = pl.BlockSpec(
        pieces[0].shape, lambda s, *_: (0, 0, 0, 0, 0), pipeline_mode=pl.Buffered(1)
    )
    sum_type = BF16 if last else F32
    outs = pl.pallas_call(
        with_earlier(
            functools.partial(
                experts_kernel, first=first, row_steps=row_steps, has_sums=sums is not None
            ),
            8 + len(sums or ()), len(earlier),
        ),
        grid_spec=pltpu.PrefetchScalarGridSpec(
            num_scalar_prefetch=1,
            grid=(row_steps + width_steps,),
            in_specs=[
                row, row, turned, turned,
                pl.BlockSpec((EXPERT_ROWS, combine.shape[1]), row_at), piece, piece,
            ]
            + ([row, row] if sums is not None else [])
            + any_specs(earlier),
            out_specs=[piece, piece, row, row, pl.BlockSpec((EXPERT_ROWS, count), row_at)],
            scratch_shapes=[
                pltpu.VMEM((width, 2 * hidden * count), BF16),
                pltpu.VMEM((width, hidden * count), BF16),
                pltpu.VMEM((width, 2 * hidden * count), BF16),
                pltpu.VMEM((width, hidden * count), BF16),
                pltpu.VMEM((tokens, 2 * hidden * count), BF16),
                pltpu.VMEM((tokens, hidden * count), BF16),
            ],
        ),
        out_shape=[jax.ShapeDtypeStruct(pieces[0].shape, BF16)] * 2
        + [
            jax.ShapeDtypeStruct((tokens, width), sum_type),
            jax.ShapeDtypeStruct((tokens, width), sum_type),
            jax.ShapeDtypeStruct((tokens, count), F32),
        ],
        compiler_params=pltpu.CompilerParams(vmem_limit_bytes=VMEM_BYTES),
        cost_estimate=pl.CostEstimate(
            flops=6 * tokens * width * count * block,
            bytes_accessed=4 * count * width * block + 20 * tokens * width, transcendentals=0,
        ),
        name="experts_pass",
    )(rows_at, x, og, xt, ogt, combine, *pieces, *(sums or ()), *earlier)
    return outs[:2], outs[2:4], outs[4]


SLOTS = 4
Z_FROM = (0, -1, 1, 2)


def move(array, dz=0, dy=0, dx=0):
    total = lax.axis_size("dp")
    inner = total // 16
    pairs = []
    for at in range(16):
        z, y, x = at // 4, at // 2 % 2, at % 2
        to = ((z + dz) % 4) * 4 + (y ^ dy) * 2 + (x ^ dx)
        pairs += [(at * inner + i, to * inner + i) for i in range(inner)]
    return lax.ppermute(array, "dp", pairs)


def place():
    at = lax.axis_index("dp") // (lax.axis_size("dp") // 16)
    return at // 4, at // 2 % 2, at % 2


def inner_groups(total):
    inner = total // 16
    return [[at * inner + i for i in range(inner)] for at in range(16)]


def inner_gather(shard, axis):
    total = lax.axis_size("dp")
    if total == 16:
        return shard
    return lax.all_gather(
        shard, "dp", axis=axis, tiled=True, axis_index_groups=inner_groups(total)
    )


def inner_scatter(share, axis):
    total = lax.axis_size("dp")
    if total == 16:
        return share
    return lax.psum_scatter(
        share, "dp", scatter_dimension=axis, tiled=True, axis_index_groups=inner_groups(total)
    )


def block_rows(parts, rows):
    z, y, x = place()
    starts = []
    for dz, dy, dx in parts:
        starts.append((((z + dz + 4) % 4) * 4 + (y ^ dy) * 2 + (x ^ dx)) * rows)
    return jnp.stack(starts).astype(jnp.int32)


def gather_z(shard):
    return jnp.stack([shard] + [move(shard, dz=-dz) for dz in Z_FROM[1:]])


def send_z(parts):
    return [move(parts[k].astype(BF16), dz=Z_FROM[k]) for k in range(1, SLOTS)]


def scatter_z(parts, moved=None):
    result = parts[0]
    for one in moved or send_z(parts):
        result = result + one.astype(F32)
    return result


def gather_plane(own):
    half = own.shape[-1] // 2
    along_y, along_x = move(own, dy=1), move(own, dx=1)
    both = (move(along_y[..., :half], dx=1), move(along_x[..., half:], dy=1))
    return own, along_y, along_x, *both


def scatter_plane(pieces):
    own, along_y, along_x, both_one, both_two = pieces
    half = both_one.shape[-1]
    got_one, got_two = move(both_one, dx=1), move(both_two, dy=1)
    pass_y = jnp.concatenate(
        [(along_y[..., :half].astype(F32) + got_one.astype(F32)).astype(BF16), along_y[..., half:]],
        axis=-1,
    )
    pass_x = jnp.concatenate(
        [along_x[..., :half], (along_x[..., half:].astype(F32) + got_two.astype(F32)).astype(BF16)],
        axis=-1,
    )
    got_y, got_x = move(pass_y, dy=1), move(pass_x, dx=1)
    return scatter_z(
        [
            own[k].astype(F32) + got_y[k].astype(F32) + got_x[k].astype(F32)
            for k in range(SLOTS)
        ]
    )


PLANE = [(dz, dy, dx) for dy, dx in ((0, 0), (1, 0), (0, 1), (1, 1)) for dz in Z_FROM]


def join_kernel(rows_at, *refs):
    pieces, out = refs[:-1], refs[-1]
    slots, own, width = pieces[0].shape
    half = width // 2
    for at in range(4 * slots):
        rows = pl.ds(pl.multiple_of(rows_at[at], own), own)
        group, slot = at // slots, at % slots
        if group < 3:
            out[rows, :] = pieces[group][slot]
        else:
            out[rows, :half] = pieces[3][slot]
            out[rows, half:] = pieces[4][slot]


def part_kernel(rows_at, whole, *pieces):
    slots, own, width = pieces[0].shape
    half = width // 2
    for at in range(4 * slots):
        rows = pl.ds(pl.multiple_of(rows_at[at], own), own)
        group, slot = at // slots, at % slots
        if group < 3:
            pieces[group][slot] = whole[rows, :]
        else:
            pieces[3][slot] = whole[rows, :half]
            pieces[4][slot] = whole[rows, half:]


def smem_spec():
    return pl.BlockSpec(memory_space=pltpu.SMEM)


def vmem_spec():
    return pl.BlockSpec(memory_space=pltpu.VMEM)


def join_blocks(rows_at, pieces, earlier=()):
    slots, own, width = pieces[0].shape
    return pl.pallas_call(
        with_earlier(join_kernel, 6, len(earlier)),
        in_specs=[smem_spec()] + [vmem_spec()] * 5 + any_specs(earlier),
        out_specs=vmem_spec(),
        out_shape=jax.ShapeDtypeStruct((4 * slots * own, width), BF16),
        compiler_params=pltpu.CompilerParams(vmem_limit_bytes=VMEM_BYTES),
        name="join_blocks",
    )(rows_at, *pieces, *earlier)


def part_blocks(rows_at, whole, earlier=()):
    own, width = whole.shape[0] // (4 * SLOTS), whole.shape[1]
    full = jax.ShapeDtypeStruct((SLOTS, own, width), BF16)
    half = jax.ShapeDtypeStruct((SLOTS, own, width // 2), BF16)
    return pl.pallas_call(
        with_earlier(part_kernel, 2, len(earlier)),
        in_specs=[smem_spec(), vmem_spec()] + any_specs(earlier),
        out_specs=[vmem_spec()] * 5,
        out_shape=[full] * 3 + [half] * 2,
        compiler_params=pltpu.CompilerParams(vmem_limit_bytes=VMEM_BYTES),
        name="part_blocks",
    )(rows_at, whole, *earlier)


def after(value, *earlier):
    marks = []
    for one in earlier:
        slots = one.shape[0] if one.shape[0] == SLOTS else 1
        lead, rest = (slots > 1) * 1, one.ndim - 1
        marks.append(lax.slice(one, (lead,) + (0,) * rest, (slots,) + (1,) * rest))
    return lax.optimization_barrier((value, *marks))[0]


def split_three(values):
    high = values.astype(BF16)
    rest = values - high.astype(F32)
    middle = rest.astype(BF16)
    low = (rest - middle.astype(F32)).astype(BF16)
    return [high, middle, low]


def swap_cores(part):
    return lax.ppermute(part, "tensor", [(0, 1), (1, 0)])


def pair_sum(part):
    return part.astype(F32) + swap_cores(part).astype(F32)


def norm_backward(values, inverse, gain_row, upstream):
    scaled = values * inverse
    weighted = upstream * gain_row
    mean_term = jnp.mean(weighted * scaled, axis=-1, keepdims=True)
    return (inverse * (weighted - scaled * mean_term), jnp.sum(upstream * scaled, axis=0))


def adam_update(value, gradient, mean_old, square_old, rate, decay):
    mean_new = FIRST_DECAY * mean_old + (1.0 - FIRST_DECAY) * gradient
    square_new = SECOND_DECAY * square_old + (1.0 - SECOND_DECAY) * gradient * gradient
    mean_hat = mean_new / (1.0 - FIRST_DECAY**STEP)
    square_hat = square_new / (1.0 - SECOND_DECAY**STEP)
    updated = value - rate * (mean_hat / (jnp.sqrt(square_hat) + ADAM_EPSILON) + decay * value)
    return (mean_new, square_new, updated)


def shards(
    hidden_in,
    out_grad,
    routes,
    segments,
    norm_gains,
    gains_mean,
    gains_square,
    w_query,
    query_mean,
    query_square,
    key_value_weight,
    key_value_first_moment,
    key_value_second_moment,
    w_out,
    out_mean,
    out_square,
    w_router,
    router_mean,
    router_square,
    w_gateup,
    gateup_mean,
    gateup_square,
    w_down,
    down_mean,
    down_square,
):
    tokens, width = hidden_in.shape
    own = w_query.shape[0]
    experts, hidden = w_down.shape[0], w_down.shape[1]
    q_width, kv_width = w_query.shape[1], key_value_weight.shape[2]
    qkv_width = q_width + 2 * kv_width
    each = 2 + experts
    half_experts = experts // 2
    block = width // 16
    z_at, y_at, x_at = place()
    core = lax.axis_index("tensor")
    plane_rows = block_rows(PLANE, block)
    pair_rows = block_rows(
        [(dz, dy, dx) for dy in (0, 1) for dz in Z_FROM for dx in (0, 1)], block
    )

    qkv_shard = jnp.concatenate(
        [w_query.astype(BF16), key_value_weight[0].astype(BF16), key_value_weight[1].astype(BF16)]
        + split_three(jnp.concatenate([norm_gains.T, w_router], axis=1))
        + [jnp.zeros((own, 2 * LANES - 3 * each), BF16)],
        axis=1,
    )
    expert_shard = jnp.concatenate(
        [
            w_gateup[:, 0].astype(BF16),
            w_gateup[:, 1].astype(BF16),
            w_down.astype(BF16).transpose(0, 2, 1),
        ],
        axis=2,
    )
    expert_shard = inner_gather(expert_shard, 1)
    kept = lax.dynamic_slice_in_dim(expert_shard, half_experts * x_at, half_experts)
    given = lax.dynamic_slice_in_dim(expert_shard, half_experts * (1 - x_at), half_experts)
    chunk = 2
    chunks = range(half_experts // chunk)

    def half_of(array, other=False):
        half = array.shape[0] // 2
        return lax.dynamic_slice_in_dim(array, half * ((1 - core) if other else core), half)

    def join_halves(mine):
        other = swap_cores(mine)
        first = core == 0
        return jnp.concatenate([jnp.where(first, mine, other), jnp.where(first, other, mine)])

    og_got = move(half_of(out_grad), dx=1)
    taken = [move(given[:chunk], dx=1)]
    qkv_z = gather_z(inner_gather(qkv_shard, 0))
    out_z = gather_z(inner_gather(after(w_out.T.astype(BF16), qkv_z), 0))
    qkv_pieces = gather_plane(qkv_z)

    def pair_chunk(c, got):
        return jnp.stack([kept[chunk * c : chunk * (c + 1)], got])

    along_z = [gather_z(after(pair_chunk(0, taken[0]), out_z))]
    out_pieces = gather_plane(after(out_z, qkv_pieces[3]))
    rest = move(after(given[chunk:], out_pieces[1]), dx=1)
    taken += [rest[chunk * c : chunk * (c + 1)] for c in range(len(chunks) - 1)]
    for c in chunks[1:]:
        along_z.append(gather_z(after(pair_chunk(c, taken[c]), along_z[c - 1])))
    along_y = [move(along_z[0], dy=1)]

    qkv_small = join_blocks(plane_rows, qkv_pieces)
    qkv_full = qkv_small[:, :qkv_width]
    pieces = qkv_small[:, qkv_width : qkv_width + 3 * each].astype(F32)
    small = pieces[:, :each] + pieces[:, each : 2 * each] + pieces[:, 2 * each :]
    gains_full, router_full = small[:, :2].T, small[:, 2:]

    inputs = hidden_in.astype(F32)
    inverse_one = lax.rsqrt(jnp.mean(inputs * inputs, axis=-1, keepdims=True) + NORM_EPSILON)
    normed_low = (inputs * inverse_one * gains_full[0]).astype(BF16)
    qkv_lin = jnp.dot(normed_low, qkv_full, preferred_element_type=F32)
    cosine, sine = rope_tables(seq_positions(segments))
    attended, queries, keys, values, lse = attention_forward(
        qkv_lin, cosine, sine, segments, earlier=(out_pieces[1],)
    )
    output_full = join_blocks(plane_rows, out_pieces, earlier=(og_got, along_z[0], attended))
    attention_part = lax.dot_general(attended, output_full, NT, preferred_element_type=F32)
    attention_part = attention_part.astype(BF16)
    og_pair = jnp.concatenate([out_grad, join_halves(og_got)])
    attention = pair_sum(attention_part)
    middle = inputs + RESIDUAL_SCALE * attention
    inverse_two = lax.rsqrt(jnp.mean(middle * middle, axis=-1, keepdims=True) + NORM_EPSILON)
    normed_two = middle * inverse_two * gains_full[1]
    normed_two_low = normed_two.astype(BF16)
    logits = jnp.dot(normed_two, router_full, precision=HIGHEST_PRECISION)
    expert_ids = jnp.arange(experts, dtype=jnp.int32)
    chosen = jnp.any(routes[:, :, None] == expert_ids[None, None, :], axis=1)
    combine = jax.nn.softmax(jnp.where(chosen, logits, -jnp.inf), axis=-1)

    def halves_of(columns):
        one, two = columns[:, :half_experts], columns[:, half_experts:]
        first = x_at == 0
        return jnp.where(first, one, two), jnp.where(first, two, one)

    combine_kept, combine_given = halves_of(combine)
    combine_pair = jnp.concatenate([combine_kept, move(combine_given, dx=1)])
    x_pair = jnp.concatenate([normed_two_low, join_halves(move(half_of(normed_two_low), dx=1))])
    x_turned, og_turned = x_pair.T, og_pair.T

    def sum_along_y(c):
        return [grads[c][0][k].astype(F32) + got_y[c][k].astype(F32) for k in range(SLOTS)]

    sums, gates, grads, got_y, z_parts, z_got = None, [], [], [], [], []
    for c in chunks:
        if c + 1 < len(chunks):
            along_y.append(move(along_z[c + 1], dy=1))
        if c >= 2:
            z_parts.append(sum_along_y(c - 2))
            z_got.append(send_z(z_parts[-1]))
        earlier = {0: along_z[1:3], 1: along_z[3:], 2: got_y[:1], 3: got_y[1:2] + sum(z_got, [])}
        grad, sums, gate = experts_pass(
            pair_rows, x_pair, og_pair, x_turned, og_turned, combine_pair,
            (along_z[c], along_y[c]), sums, chunk * c, c + 1 == len(chunks),
            [] if c + 1 > len(earlier) else earlier[c],
        )
        gates.append(gate)
        grads.append(grad)
        got_y.append(move(grad[1], dy=1))
    mix_pair, dx_pair = sums
    gate_pair = jnp.concatenate(gates, axis=1)

    def to_neighbour(part):
        both = half_of(part).astype(F32) + swap_cores(half_of(part, other=True)).astype(F32)
        return join_halves(move(both.astype(BF16), dx=1))

    gate_got = move(gate_pair[tokens:], dx=1)
    first = x_at == 0
    gate_grad = pair_sum(
        jnp.concatenate(
            [
                jnp.where(first, gate_pair[:tokens], gate_got),
                jnp.where(first, gate_got, gate_pair[:tokens]),
            ],
            axis=1,
        )
    )
    normed_two_part = pair_sum(dx_pair[:tokens]) + to_neighbour(dx_pair[tokens:]).astype(F32)
    logit_grad = combine * (gate_grad - jnp.sum(combine * gate_grad, axis=-1, keepdims=True))
    router_grad = jnp.dot(normed_two.T, logit_grad, precision=HIGHEST_PRECISION)
    normed_two_grad = normed_two_part + jnp.dot(
        logit_grad, router_full.T, precision=HIGHEST_PRECISION
    )
    middle_part, gain_two_grad = norm_backward(middle, inverse_two, gains_full[1], normed_two_grad)
    middle_grad = out_grad.astype(F32) + middle_part
    attention_back = (RESIDUAL_SCALE * middle_grad).astype(BF16)
    attended_grad = jnp.dot(attention_back, output_full, preferred_element_type=F32).astype(BF16)
    output_weight_grad = lax.dot_general(attention_back, attended, TN, preferred_element_type=F32)
    z_parts.append(after(tuple(sum_along_y(2)), normed_two_part))
    z_got.append(send_z(z_parts[2]))
    output_share = scatter_plane(
        part_blocks(plane_rows, output_weight_grad.astype(BF16), earlier=z_got[1])
    )
    query_grad, keyval_grad = attention_backward(
        queries, keys, values, attended, attended_grad, cosine, sine, segments, lse,
        earlier=z_got[2],
    )
    z_parts.append(after(tuple(sum_along_y(3)), z_got[2][0]))
    z_got.append(send_z(z_parts[3]))
    expert_shares = [scatter_z(parts, got) for parts, got in zip(z_parts, z_got)]
    qkv_grad = jnp.concatenate([query_grad, keyval_grad], axis=1)
    qkv_weight_grad = lax.dot_general(normed_low, qkv_grad, TN, preferred_element_type=F32)
    qkv_share = scatter_plane(
        part_blocks(
            plane_rows,
            jnp.concatenate(
                [
                    qkv_weight_grad.astype(BF16),
                    gain_two_grad[:, None].astype(BF16),
                    router_grad.astype(BF16),
                    jnp.zeros((width, 2 * LANES - 1 - experts), BF16),
                ],
                axis=1,
            ),
            earlier=z_got[3],
        )
    )
    normed_part = lax.dot_general(qkv_grad, qkv_full, NT, preferred_element_type=F32)
    normed_grad = pair_sum(normed_part.astype(BF16))
    scaled = inputs * inverse_one
    weighted = normed_grad * gains_full[0]
    mean_term = jnp.mean(weighted * scaled, axis=-1, keepdims=True)
    input_grad = middle_grad + inverse_one * (weighted - scaled * mean_term)

    mix_part = after(mix_pair, qkv_grad)
    expert_mix = pair_sum(mix_part[:tokens]) + to_neighbour(mix_part[tokens:]).astype(F32)
    block_out = (middle + RESIDUAL_SCALE * expert_mix).astype(BF16)
    expert_pair = after(jnp.concatenate(expert_shares, axis=1), qkv_grad)
    expert_got = move(expert_pair[1].astype(BF16), dx=1).astype(F32)
    expert_kept = expert_pair[0]
    expert_share = inner_scatter(
        jnp.concatenate(
            [jnp.where(first, expert_kept, expert_got), jnp.where(first, expert_got, expert_kept)]
        ),
        1,
    ).reshape(experts, own, 3, hidden)
    gateup_share = expert_share[:, :, :2].transpose(0, 2, 1, 3)
    down_share = expert_share[:, :, 2].transpose(0, 2, 1)

    output_share = inner_scatter(output_share, 0).T
    qkv_share = inner_scatter(qkv_share, 0)
    query_share = qkv_share[:, :q_width]
    keyval_share = jnp.stack(
        [qkv_share[:, q_width : q_width + kv_width], qkv_share[:, q_width + kv_width : qkv_width]]
    )
    gain_one_part = jnp.sum(w_query.astype(BF16).astype(F32) * query_share, axis=1) + jnp.sum(
        key_value_weight.astype(BF16).astype(F32) * keyval_share, axis=(0, 2)
    )
    gain_one_share = pair_sum(gain_one_part[None, :]) / norm_gains[:1]
    gains_share = jnp.concatenate([gain_one_share, qkv_share[:, qkv_width][None, :]])
    router_share = qkv_share[:, qkv_width + 1 : qkv_width + 1 + experts]

    gains_result = adam_update(norm_gains, gains_share, gains_mean, gains_square, GAIN_RATE, 0.0)
    query_result = adam_update(
        w_query, query_share, query_mean, query_square, (MODEL_DIM // 12) ** (-0.5), WEIGHT_DECAY
    )
    keyval_result = adam_update(
        key_value_weight,
        keyval_share,
        key_value_first_moment,
        key_value_second_moment,
        (MODEL_DIM // 12) ** (-0.5),
        WEIGHT_DECAY,
    )
    out_result = adam_update(
        w_out,
        output_share,
        out_mean,
        out_square,
        max(1, QUERY_HEADS * HEAD_DIM // 96) ** (-0.5),
        WEIGHT_DECAY,
    )
    router_result = adam_update(
        w_router, router_share, router_mean, router_square, (4 * MODEL_DIM) ** (-0.5), WEIGHT_DECAY
    )
    gateup_result = adam_update(
        w_gateup, gateup_share, gateup_mean, gateup_square, MODEL_DIM ** (-0.5), WEIGHT_DECAY
    )
    down_result = adam_update(
        w_down, down_share, down_mean, down_square, max(1, F // 256) ** (-0.5), WEIGHT_DECAY
    )
    return (
        (block_out, input_grad)
        + gains_result
        + query_result
        + keyval_result
        + out_result
        + router_result
        + gateup_result
        + down_result
    )


def solution(mesh):
    tokens, gains = P("dp", None), P(None, "dp")
    query, keyval, out = P("dp", "tensor"), P(None, "dp", "tensor"), P("tensor", "dp")
    router, gateup, down = P("dp", None), P(None, None, "dp", "tensor"), P(None, "tensor", "dp")
    states = tuple(
        spec for one in (gains, query, keyval, out, router, gateup, down) for spec in (one,) * 3
    )
    return jax.shard_map(
        shards,
        mesh=mesh,
        in_specs=(tokens, tokens, tokens, P("dp")) + states,
        out_specs=(tokens, tokens) + states,
        check_vma=False,
    )
```

```python
import functools

import jax
import jax.numpy as jnp
from jax import lax
from jax.experimental import pallas as pl
from jax.experimental.pallas import tpu as pltpu
from jax.sharding import PartitionSpec as P

MODEL_DIM = 1536
QUERY_HEADS = 24
HEAD_DIM = 64
F = 512
SEQUENCE_LENGTH = 1024
STEP = 10

NORM_EPSILON = 1e-06
SCORE_SCALE = 0.015625
RESIDUAL_SCALE = 0.22
ROPE_BASE = 10000.0
FIRST_DECAY = 0.9
SECOND_DECAY = 0.95
ADAM_EPSILON = 1e-08
WEIGHT_DECAY = 0.1
GAIN_RATE = 0.6
MASK_VALUE = -1e30
HIGHEST_PRECISION = lax.Precision.HIGHEST

BF16 = jnp.bfloat16
F32 = jnp.float32
LANES = 128
ROWS = 256
VMEM_BYTES = 58 * 1024 * 1024

NN = (((1,), (0,)), ((), ()))
NT = (((1,), (1,)), ((), ()))
TN = (((0,), (0,)), ((), ()))


def dot(a, b, dims=NN):
    return lax.dot_general(a, b, dims, preferred_element_type=F32)


def seq_positions(segment_row):
    counter = jnp.arange(segment_row.shape[0], dtype=jnp.int32)
    earlier = jnp.concatenate([segment_row[:1] - 1, segment_row[:-1]])
    starts = lax.cummax(jnp.where(segment_row != earlier, counter, 0), axis=0)
    return counter - starts


def rope_tables(positions):
    half_width = HEAD_DIM // 2
    frequency = ROPE_BASE ** (-2.0 * jnp.arange(half_width, dtype=F32) / HEAD_DIM)
    angles = positions.astype(F32)[:, None] * frequency[None, :]
    cosine, sine = jnp.cos(angles), jnp.sin(angles)
    return (
        jnp.concatenate([cosine] * 4, axis=1),
        jnp.concatenate([-sine, sine] * 2, axis=1),
    )


def rotate_halves(slab):
    lane = lax.broadcasted_iota(jnp.int32, slab.shape, 1)
    ahead = pltpu.roll(slab, LANES - HEAD_DIM // 2, 1)
    behind = pltpu.roll(slab, HEAD_DIM // 2, 1)
    return jnp.where(lane % HEAD_DIM < HEAD_DIM // 2, ahead, behind)


def half_mask(rows, upper):
    lane = lax.broadcasted_iota(jnp.int32, (rows, LANES), 1)
    return (lane >= HEAD_DIM) if upper else (lane < HEAD_DIM)


def spread_heads(slab, lower_out, upper_out, index):
    rows = slab.shape[0]
    moved = pltpu.roll(slab.astype(F32), HEAD_DIM, 1).astype(BF16)
    zero = jnp.zeros_like(slab)
    low, high = half_mask(rows, False), half_mask(rows, True)
    lower_out[index] = jnp.where(low, slab, zero)
    upper_out[index] = jnp.where(high, moved, zero)
    lower_out[index + 1] = jnp.where(low, moved, zero)
    upper_out[index + 1] = jnp.where(high, slab, zero)


def fill_bias(bias, seg_col, seg_row):
    span = bias.shape[0]
    for at in range(0, span, ROWS):
        rows_at = at + lax.broadcasted_iota(jnp.int32, (ROWS, span), 0)
        cols_at = lax.broadcasted_iota(jnp.int32, (ROWS, span), 1)
        allowed = (rows_at >= cols_at) & (seg_col[at : at + ROWS, :] == seg_row[...])
        bias[at : at + ROWS, :] = jnp.where(allowed, 0.0, MASK_VALUE).astype(F32)


def with_earlier(kernel, inputs, count):
    def run(*refs):
        kernel(*refs[:inputs], *refs[inputs + count :])

    return run


def any_specs(arrays):
    return [pl.BlockSpec(memory_space=pl.ANY)] * len(arrays)


def attention_forward_kernel(
    lin_ref, kv_ref, cos_ref, sin_ref, seg_col, seg_row,
    out_ref, q_ref, k_ref, v_ref, lse_ref,
    bias, k_low, k_high, v_low, v_high,
):
    slab_at = pl.program_id(0)
    span = lin_ref.shape[0]
    kv_slabs = kv_ref.shape[1] // (2 * LANES)

    @pl.when(slab_at == 0)
    def _():
        fill_bias(bias, seg_col, seg_row)
        for j in range(kv_slabs):
            lanes = slice(j * LANES, (j + 1) * LANES)
            lin = kv_ref[:, lanes]
            keys = (lin * cos_ref[...] + rotate_halves(lin) * sin_ref[...]).astype(BF16)
            k_ref[:, lanes] = keys
            spread_heads(keys, k_low, k_high, 2 * j)
            lanes = slice((kv_slabs + j) * LANES, (kv_slabs + j + 1) * LANES)
            values = kv_ref[:, lanes].astype(BF16)
            v_ref[:, slice(j * LANES, (j + 1) * LANES)] = values
            spread_heads(values, v_low, v_high, 2 * j)

    lin = lin_ref[...]
    q_ref[...] = (lin * cos_ref[...] + rotate_halves(lin) * sin_ref[...]).astype(BF16)
    kv_even, kv_odd = (2 * slab_at) // 3, (2 * slab_at + 1) // 3
    for at in range(0, span, ROWS):
        rows = slice(at, at + ROWS)
        queries = q_ref[rows, :]
        total = None
        stats = []
        for keys, values, kv_at in ((k_low, v_low, kv_even), (k_high, v_high, kv_odd)):
            upto = at + ROWS
            scores = dot(queries, keys[kv_at, :upto, :], NT) * SCORE_SCALE + bias[rows, :upto]
            highest = jnp.max(scores, axis=1, keepdims=True)
            weights = jnp.exp(scores - highest)
            summed = jnp.sum(weights, axis=1, keepdims=True)
            probability = (weights * (1.0 / summed)).astype(BF16)
            part = dot(probability, values[kv_at, :upto, :])
            total = part if total is None else total + part
            stats.append(highest + jnp.log(summed))
        out_ref[rows, :] = total.astype(BF16)
        spread = jnp.where(half_mask(ROWS, False), stats[0], stats[1])
        turned = spread.T
        lse_ref[0, 0:1, rows] = turned[0:1, :]
        lse_ref[0, 1:2, rows] = turned[HEAD_DIM : HEAD_DIM + 1, :]


def attention_forward(qkv_lin, cosine, sine, segment_row, earlier=()):
    span = qkv_lin.shape[0]
    q_width = MODEL_DIM // 2
    kv_width = (qkv_lin.shape[1] - q_width) // 2
    slabs, kv_heads = q_width // LANES, kv_width // HEAD_DIM
    whole = lambda shape: pl.BlockSpec(shape, lambda g: (0,) * len(shape))
    slab = pl.BlockSpec((span, LANES), lambda g: (0, g))
    q_lin, kv_lin = qkv_lin[:, :q_width], qkv_lin[:, q_width:]
    return pl.pallas_call(
        with_earlier(attention_forward_kernel, 6, len(earlier)),
        grid=(slabs,),
        in_specs=[
            slab, whole((span, 2 * kv_width)), whole((span, LANES)), whole((span, LANES)),
            whole((span, 1)), whole((1, span)),
        ]
        + any_specs(earlier),
        out_specs=[
            slab, slab, whole((span, kv_width)), whole((span, kv_width)),
            pl.BlockSpec((1, 8, span), lambda g: (g, 0, 0)),
        ],
        out_shape=[
            jax.ShapeDtypeStruct((span, q_width), BF16),
            jax.ShapeDtypeStruct((span, q_width), BF16),
            jax.ShapeDtypeStruct((span, kv_width), BF16),
            jax.ShapeDtypeStruct((span, kv_width), BF16),
            jax.ShapeDtypeStruct((slabs, 8, span), F32),
        ],
        scratch_shapes=[pltpu.VMEM((span, span), F32)]
        + [pltpu.VMEM((kv_heads, span, LANES), BF16)] * 4,
        compiler_params=pltpu.CompilerParams(vmem_limit_bytes=VMEM_BYTES),
        cost_estimate=pl.CostEstimate(
            flops=32 * slabs * span * span * LANES, bytes_accessed=16 * span * q_width,
            transcendentals=slabs * span * span,
        ),
        name="attention_forward",
    )(q_lin, kv_lin, cosine, sine, segment_row[:, None], segment_row[None, :], *earlier)


def attention_backward_kernel(
    q_ref, k_ref, v_ref, out_ref, grad_ref, cos_ref, sin_ref, seg_col, seg_row, lse_ref,
    dq_ref, dkv_ref,
    bias, k_low, k_high, v_low, v_high, dk_low, dk_high, dv_low, dv_high, dq_sum,
):
    slab_at = pl.program_id(0)
    span = q_ref.shape[0]
    kv_slabs = k_ref.shape[1] // LANES

    @pl.when(slab_at == 0)
    def _():
        for at in range(0, span, ROWS):
            keys_at = at + lax.broadcasted_iota(jnp.int32, (ROWS, span), 0)
            rows_at = lax.broadcasted_iota(jnp.int32, (ROWS, span), 1)
            allowed = (rows_at >= keys_at) & (seg_col[at : at + ROWS, :] == seg_row[...])
            bias[at : at + ROWS, :] = jnp.where(allowed, 0.0, MASK_VALUE).astype(F32)
        for j in range(kv_slabs):
            lanes = slice(j * LANES, (j + 1) * LANES)
            spread_heads(k_ref[:, lanes], k_low, k_high, 2 * j)
            spread_heads(v_ref[:, lanes], v_low, v_high, 2 * j)
        for sums in (dk_low, dk_high, dv_low, dv_high):
            sums[...] = jnp.zeros_like(sums)

    kv_even, kv_odd = (2 * slab_at) // 3, (2 * slab_at + 1) // 3
    for at in range(0, span, ROWS):
        rows = slice(at, at + ROWS)
        upto = at + ROWS
        queries, grads = q_ref[rows, :], grad_ref[rows, :]
        turned = (grads.astype(F32) * out_ref[rows, :].astype(F32)).T
        zero = jnp.zeros_like(queries)
        dq_part = None
        for upper, keys, values, dk_sum, dv_sum, kv_at in (
            (False, k_low, v_low, dk_low, dv_low, kv_even),
            (True, k_high, v_high, dk_high, dv_high, kv_odd),
        ):
            first = HEAD_DIM if upper else 0
            delta = jnp.sum(turned[first : first + HEAD_DIM, :], axis=0, keepdims=True)
            head = 1 if upper else 0
            total = lse_ref[0, head : head + 1, rows]
            keys_here = keys[kv_at, :upto, :]
            scores = dot(keys_here, queries, NT) * SCORE_SCALE + bias[:upto, rows]
            probability = jnp.exp(scores - total)
            prob_grad = dot(values[kv_at, :upto, :], grads, NT)
            score_grad = (probability * (prob_grad - delta)).astype(BF16)
            mask = half_mask(ROWS, upper)
            dv_sum[kv_at, :upto, :] += dot(
                probability.astype(BF16), jnp.where(mask, grads, zero)
            )
            dk_sum[kv_at, :upto, :] += dot(score_grad, jnp.where(mask, queries, zero))
            part = dot(score_grad, keys_here, TN)
            dq_part = part if dq_part is None else dq_part + part
        dq_sum[rows, :] = dq_part * SCORE_SCALE
    slab = dq_sum[...]
    dq_ref[...] = (slab * cos_ref[...] - rotate_halves(slab) * sin_ref[...]).astype(BF16)

    @pl.when(slab_at == pl.num_programs(0) - 1)
    def _():
        low = half_mask(span, False)

        def joined(sums_low, sums_high, j):
            one = sums_low[2 * j] + pltpu.roll(sums_high[2 * j], HEAD_DIM, 1)
            two = pltpu.roll(sums_low[2 * j + 1], HEAD_DIM, 1) + sums_high[2 * j + 1]
            return jnp.where(low, one, two)

        for j in range(kv_slabs):
            slab = joined(dk_low, dk_high, j) * SCORE_SCALE
            dkv_ref[:, j * LANES : (j + 1) * LANES] = (
                slab * cos_ref[...] - rotate_halves(slab) * sin_ref[...]
            ).astype(BF16)
            at = (kv_slabs + j) * LANES
            dkv_ref[:, at : at + LANES] = joined(dv_low, dv_high, j).astype(BF16)


def attention_backward(
    queries, keys, values, attended, grad, cosine, sine, segment_row, lse, earlier=()
):
    span, q_width = queries.shape
    kv_width = keys.shape[1]
    slabs, kv_heads = q_width // LANES, kv_width // HEAD_DIM
    whole = lambda shape: pl.BlockSpec(shape, lambda g: (0,) * len(shape))
    slab = pl.BlockSpec((span, LANES), lambda g: (0, g))
    return pl.pallas_call(
        with_earlier(attention_backward_kernel, 10, len(earlier)),
        grid=(slabs,),
        in_specs=[
            slab, whole((span, kv_width)), whole((span, kv_width)), slab, slab,
            whole((span, LANES)), whole((span, LANES)), whole((span, 1)), whole((1, span)),
            pl.BlockSpec((1, 8, span), lambda g: (g, 0, 0)),
        ]
        + any_specs(earlier),
        out_specs=[slab, whole((span, 2 * kv_width))],
        out_shape=[
            jax.ShapeDtypeStruct((span, q_width), BF16),
            jax.ShapeDtypeStruct((span, 2 * kv_width), BF16),
        ],
        scratch_shapes=[pltpu.VMEM((span, span), F32)]
        + [pltpu.VMEM((kv_heads, span, LANES), BF16)] * 4
        + [pltpu.VMEM((kv_heads, span, LANES), F32)] * 4
        + [pltpu.VMEM((span, LANES), F32)],
        compiler_params=pltpu.CompilerParams(vmem_limit_bytes=VMEM_BYTES),
        cost_estimate=pl.CostEstimate(
            flops=40 * slabs * span * span * LANES, bytes_accessed=16 * span * q_width,
            transcendentals=slabs * span * span,
        ),
        name="attention_backward",
    )(
        queries, keys, values, attended, grad, cosine, sine,
        segment_row[:, None], segment_row[None, :], lse, *earlier,
    )


EXPERT_ROWS = 256
EXPERT_VMEM = 61 * 1024 * 1024
SLOTS = 4
Z_FROM = (0, -1, 1, 2)
CHUNK = 2
LATE = 2
SENT = 2
MESH_ID = pl.DeviceIdType.MESH


def experts_kernel(
    inner, chunks, row_steps, x_ref, og_ref, xt_ref, ogt_ref, combine_ref, *refs
):
    near_refs, refs = refs[: SLOTS * (chunks - 1)], refs[SLOTS * (chunks - 1) :]
    last_near, far_refs, refs = refs[0], refs[1 : 1 + LATE], refs[1 + LATE :]
    mix_ref, dx_ref, gate_ref, refs = *refs[:3], refs[3:]
    sum_refs, refs = refs[: SENT * SLOTS], refs[SENT * SLOTS :]
    near_outs, refs = refs[: chunks - SENT], refs[chunks - SENT :]
    far_outs, refs = refs[: chunks - SENT], refs[chunks - SENT :]
    weights, grads, arrived, held_both, held_down = refs[:5]
    near_sem, far_sem, z_send, z_recv, y_send, y_recv, sum_send, sum_recv, out_sem = refs[5:]
    step = pl.program_id(0)
    steps = row_steps + SLOTS
    chunk, turn = step // steps, step % steps
    side = chunk % 2
    block = x_ref.shape[1] // 16
    hidden = held_down.shape[1] // CHUNK
    both = 2 * hidden * CHUNK
    lane = lax.broadcasted_iota(jnp.int32, (EXPERT_ROWS, combine_ref.shape[1]), 1)

    me = lax.axis_index("dp")
    at = me // inner
    z, y = at // 4, at // 2 % 2
    spots = [(z + dz + 4) % 4 for dz in Z_FROM]
    across = me + (1 - 2 * y) * 2 * inner
    along = [me + (spot - z) * 4 * inner for spot in spots]

    def to(device):
        return {"dp": device}

    def near_copy(c, k):
        source = last_near if c == chunks - 1 else near_refs[SLOTS * c + k]
        return pltpu.make_async_copy(source, weights.at[c, spots[k], y], near_sem.at[c, k])

    def far_copy(c, k):
        return pltpu.make_async_copy(
            far_refs[c].at[k], weights.at[c, spots[k], 1 - y], far_sem.at[c, k]
        )

    def z_copy(k):
        here = weights.at[chunks - 1, z, y]
        return pltpu.make_async_remote_copy(
            last_near, here, z_send.at[k], z_recv.at[(0, 2, 1, 3)[k]],
            device_id=to(along[k]), device_id_type=MESH_ID,
        )

    def z_wait(k):
        place = weights.at[chunks - 1, spots[k], y]
        return pltpu.make_async_remote_copy(
            last_near, place, z_send.at[k], z_recv.at[k],
            device_id=to(along[k]), device_id_type=MESH_ID,
        )

    def y_copy(c, k):
        place = weights.at[c, spots[k], y]
        if c == chunks - 1:
            source = last_near if k == 0 else place
        else:
            source = near_refs[SLOTS * c + k]
        return pltpu.make_async_remote_copy(
            source, place, y_send.at[c - LATE, k], y_recv.at[c - LATE, k],
            device_id=to(across), device_id_type=MESH_ID,
        )

    def y_wait(c, k):
        place = weights.at[c, spots[k], 1 - y]
        return pltpu.make_async_remote_copy(
            place, place, y_send.at[c - LATE, k], y_recv.at[c - LATE, k],
            device_id=to(across), device_id_type=MESH_ID,
        )

    def sum_copy(c):
        return pltpu.make_async_remote_copy(
            grads.at[c % 2, :, 1 - y], arrived.at[c], sum_send.at[c], sum_recv.at[c],
            device_id=to(across), device_id_type=MESH_ID,
        )

    def sum_out(c, k):
        return pltpu.make_async_copy(
            grads.at[c % 2, spots[k], y], sum_refs[SLOTS * c + k], out_sem.at[c, k]
        )

    def near_out_copy(c, k):
        return pltpu.make_async_copy(
            grads.at[c % 2, spots[k], y], near_outs[c - SENT].at[k], out_sem.at[c, k]
        )

    def far_out_copy(c, k):
        return pltpu.make_async_copy(
            grads.at[c % 2, spots[k], 1 - y], far_outs[c - SENT].at[k], out_sem.at[c, SLOTS + k]
        )

    @pl.when(step == 0)
    def _():
        barrier = pltpu.get_barrier_semaphore()
        for device in [across] + along[1:]:
            pl.semaphore_signal(barrier, inc=1, device_id=to(device), device_id_type=MESH_ID)
        pl.semaphore_wait(barrier, SLOTS)
        for k in range(SLOTS):
            near_copy(0, k).start()
            far_copy(0, k).start()
        for c in range(LATE, chunks - 1):
            for k in range(SLOTS):
                y_copy(c, k).start()
        for k in range(1, SLOTS):
            z_copy(k).start()
        for c in range(1, chunks):
            for k in range(SLOTS):
                if c < chunks - 1 or k == 0:
                    near_copy(c, k).start()
                if c < LATE:
                    far_copy(c, k).start()

    for c in range(chunks):

        @pl.when(step == c * steps)
        def _():
            for k in range(SLOTS):
                if c < chunks - 1 or k == 0:
                    near_copy(c, k).wait()
                if c < LATE:
                    far_copy(c, k).wait()
                else:
                    y_wait(c, k).wait_recv()

    @pl.when(step == steps)
    def _():
        for k in range(SLOTS):
            if k > 0:
                z_wait(k).wait_recv()
            y_copy(chunks - 1, k).start()

    for c in range(SENT):

        @pl.when(step == (c + 2) * steps + row_steps - 2)
        def _():
            sum_copy(c).wait_recv()
            for k in range(SLOTS):
                own = grads.at[c % 2, spots[k], y]
                own[...] = (
                    own[...].astype(F32) + arrived[c, spots[k]].astype(F32)
                ).astype(BF16)
                sum_out(c, k).start()

        @pl.when(step == (c + 2) * steps + row_steps)
        def _():
            sum_copy(c).wait_send()
            for k in range(SLOTS):
                sum_out(c, k).wait()

    @pl.when(turn < row_steps)
    def _():
        rows = pl.ds(pl.multiple_of(turn * EXPERT_ROWS, EXPERT_ROWS), EXPERT_ROWS)
        width = x_ref.shape[1]
        for e in range(CHUNK):
            first = 2 * hidden * e
            w_both = weights[chunk, :, :, :, first : first + 2 * hidden].reshape(width, 2 * hidden)
            start = both + hidden * e
            w_down = weights[chunk, :, :, :, start : start + hidden].reshape(width, hidden)
            gate_up = dot(x_ref[...], w_both)
            raw = dot(og_ref[...], w_down) * RESIDUAL_SCALE
            gate, up = gate_up[:, :hidden], gate_up[:, hidden:]
            column = jnp.sum(
                jnp.where(lane == chunk * CHUNK + e, combine_ref[...], 0.0), axis=1, keepdims=True
            )
            sigmoid = 1.0 / (1.0 + jnp.exp(-gate))
            active = gate * sigmoid
            inner_value = (active * up).astype(BF16).astype(F32)
            held_down[rows, hidden * e : hidden * (e + 1)] = (inner_value * column).astype(BF16)
            gate_ref[0, :, e : e + 1] = jnp.sum(inner_value * raw, axis=1, keepdims=True)
            inner_grad = raw * column
            held_both[rows, first : first + hidden] = (
                inner_grad * up * sigmoid * (1.0 + gate * (1.0 - sigmoid))
            ).astype(BF16)
            held_both[rows, first + hidden : first + 2 * hidden] = (inner_grad * active).astype(BF16)
        for part in range(SLOTS):
            cols = slice(4 * block * part, 4 * block * (part + 1))
            w_both = weights[chunk, part, :, :, :both].reshape(4 * block, both)
            w_down = weights[chunk, part, :, :, both:].reshape(4 * block, hidden * CHUNK)
            mix_ref[0, :, cols] = dot(held_down[rows, :], w_down, NT).astype(BF16)
            dx_ref[0, :, cols] = dot(held_both[rows, :], w_both, NT).astype(BF16)

    @pl.when(turn >= row_steps)
    def _():
        part = turn - row_steps
        grads[side, part, :, :, :both] = (
            dot(xt_ref[...], held_both[...]).astype(BF16).reshape(2, 2 * block, both)
        )
        grads[side, part, :, :, both:] = (
            (dot(ogt_ref[...], held_down[...]) * RESIDUAL_SCALE)
            .astype(BF16)
            .reshape(2, 2 * block, hidden * CHUNK)
        )

    for c in range(chunks):

        @pl.when(step == (c + 1) * steps - 1)
        def _():
            if c < SENT:
                sum_copy(c).start()
            else:
                for k in range(SLOTS):
                    near_out_copy(c, k).start()
                    far_out_copy(c, k).start()

    @pl.when(step == chunks * steps - 1)
    def _():
        for c in range(SENT, chunks):
            for k in range(SLOTS):
                near_out_copy(c, k).wait()
                far_out_copy(c, k).wait()
        for c in range(LATE, chunks):
            for k in range(SLOTS):
                y_copy(c, k).wait_send()
        for k in range(1, SLOTS):
            z_copy(k).wait_send()


def experts_pass(x, og, xt, ogt, combine, near, last_near, far):
    tokens, width = x.shape
    chunks = len(near) + 1
    pair, columns = last_near.shape
    hidden = columns // (3 * CHUNK)
    row_steps = tokens // EXPERT_ROWS
    steps = row_steps + SLOTS
    inner = lax.axis_size("dp") // 16
    row_at = lambda s: (jnp.minimum(s % steps, row_steps - 1), 0)
    width_at = lambda s: (jnp.maximum(s % steps - row_steps, 0), 0)
    sum_at = lambda s: (s // steps, jnp.minimum(s % steps, row_steps - 1), 0)
    row = pl.BlockSpec((EXPERT_ROWS, width), row_at)
    turned = pl.BlockSpec((width // SLOTS, tokens), width_at)
    summed = pl.BlockSpec((1, EXPERT_ROWS, width), sum_at)
    anywhere = pl.BlockSpec(memory_space=pl.ANY)
    near = [one for pieces in near for one in pieces]
    outs = pl.pallas_call(
        functools.partial(experts_kernel, inner, chunks, row_steps),
        grid=(chunks * steps,),
        in_specs=[row, row, turned, turned, pl.BlockSpec((EXPERT_ROWS, combine.shape[1]), row_at)]
        + [anywhere] * (len(near) + 1 + len(far)),
        out_specs=[summed, summed, pl.BlockSpec((1, EXPERT_ROWS, CHUNK), sum_at)]
        + [anywhere] * (SENT * SLOTS + 2 * (chunks - SENT)),
        out_shape=[
            jax.ShapeDtypeStruct((chunks, tokens, width), BF16),
            jax.ShapeDtypeStruct((chunks, tokens, width), BF16),
            jax.ShapeDtypeStruct((chunks, tokens, CHUNK), F32),
        ]
        + [jax.ShapeDtypeStruct((pair, columns), BF16)] * (SENT * SLOTS)
        + [jax.ShapeDtypeStruct((SLOTS, pair, columns), BF16)] * (2 * (chunks - SENT)),
        scratch_shapes=[
            pltpu.VMEM((chunks, SLOTS, 2, pair, columns), BF16),
            pltpu.VMEM((2, SLOTS, 2, pair, columns), BF16),
            pltpu.VMEM((SENT, SLOTS, pair, columns), BF16),
            pltpu.VMEM((tokens, 2 * hidden * CHUNK), BF16),
            pltpu.VMEM((tokens, hidden * CHUNK), BF16),
            pltpu.SemaphoreType.DMA((chunks, SLOTS)),
            pltpu.SemaphoreType.DMA((LATE, SLOTS)),
            pltpu.SemaphoreType.DMA((SLOTS,)),
            pltpu.SemaphoreType.DMA((SLOTS,)),
            pltpu.SemaphoreType.DMA((chunks - LATE, SLOTS)),
            pltpu.SemaphoreType.DMA((chunks - LATE, SLOTS)),
            pltpu.SemaphoreType.DMA((SENT,)),
            pltpu.SemaphoreType.DMA((SENT,)),
            pltpu.SemaphoreType.DMA((chunks, 2 * SLOTS)),
        ],
        compiler_params=pltpu.CompilerParams(
            vmem_limit_bytes=EXPERT_VMEM, collective_id=0, has_side_effects=True
        ),
        cost_estimate=pl.CostEstimate(
            flops=8 * tokens * width * chunks * columns,
            bytes_accessed=2 * chunks * width * columns, transcendentals=0,
        ),
        name="experts_pass",
    )(x, og, xt, ogt, combine, *near, last_near, *far)
    outs, rest = outs[:3], outs[3:]
    sums = [rest[SLOTS * c : SLOTS * (c + 1)] for c in range(SENT)]
    rest = rest[SENT * SLOTS :]
    return *outs, sums, rest[: chunks - SENT], rest[chunks - SENT :]


def whole_call(kernel, values, outs, earlier=(), name=None):
    return pl.pallas_call(
        with_earlier(kernel, len(values), len(earlier)),
        in_specs=[vmem_spec()] * len(values) + any_specs(earlier),
        out_specs=[vmem_spec()] * len(outs),
        out_shape=[jax.ShapeDtypeStruct(shape, dtype) for shape, dtype in outs],
        compiler_params=pltpu.CompilerParams(vmem_limit_bytes=VMEM_BYTES),
        name=name,
    )(*values, *earlier)


def fence_kernel(*refs):
    count = len(refs) // 2
    for value, out in zip(refs[:count], refs[count:]):
        out[...] = value[...]


def fence_all(values, *earlier):
    return whole_call(fence_kernel, values, [(v.shape, v.dtype) for v in values], earlier, "fence")


def fence(value, *earlier):
    return fence_all([value], *earlier)[0]


def sum_y_kernel(near, got, *outs):
    for k, out in enumerate(outs):
        out[...] = (near[k].astype(F32) + got[k].astype(F32)).astype(BF16)


def sum_y(near, got, *earlier):
    outs = [(near.shape[1:], BF16)] * SLOTS
    return whole_call(sum_y_kernel, [near, got], outs, earlier, "sum_y")


def sum_z_kernel(x_at, *refs):
    kept, given = refs[-2:]
    half = kept.shape[1]
    for c in range(kept.shape[0]):
        parts = refs[SLOTS * c : SLOTS * (c + 1)]
        for rows, out in ((x_at[0], kept), (1 - x_at[0], given)):
            rows = pl.ds(pl.multiple_of(rows * half, half), half)
            total = parts[0][rows, :].astype(F32)
            for part in parts[1:]:
                total = total + part[rows, :].astype(F32)
            out[c] = total.astype(out.dtype)


def sum_z(x_at, chunks, *earlier):
    count = len(chunks)
    pair, columns = chunks[0][0].shape
    flat = [part for parts in chunks for part in parts]
    return pl.pallas_call(
        with_earlier(sum_z_kernel, 1 + len(flat), len(earlier)),
        in_specs=[smem_spec()] + [vmem_spec()] * len(flat) + any_specs(earlier),
        out_specs=[vmem_spec()] * 2,
        out_shape=[
            jax.ShapeDtypeStruct((count, pair // 2, columns), F32),
            jax.ShapeDtypeStruct((count, pair // 2, columns), BF16),
        ],
        compiler_params=pltpu.CompilerParams(vmem_limit_bytes=VMEM_BYTES),
        name="sum_z",
    )(x_at, *flat, *earlier)


def sum_parts_kernel(parts, out):
    total = parts[0].astype(F32)
    for c in range(1, parts.shape[0]):
        total = total + parts[c].astype(F32)
    out[...] = total.astype(BF16)


def sum_parts(parts, *earlier):
    chunks, tokens, width = parts.shape
    return pl.pallas_call(
        with_earlier(sum_parts_kernel, 1, len(earlier)),
        grid=(tokens // EXPERT_ROWS,),
        in_specs=[pl.BlockSpec((chunks, EXPERT_ROWS, width), lambda s: (0, s, 0))]
        + any_specs(earlier),
        out_specs=pl.BlockSpec((EXPERT_ROWS, width), lambda s: (s, 0)),
        out_shape=jax.ShapeDtypeStruct((tokens, width), BF16),
        compiler_params=pltpu.CompilerParams(vmem_limit_bytes=VMEM_BYTES),
        name="sum_parts",
    )(parts, *earlier)


def adam_experts_kernel(x_at, kept, got, *refs):
    states, outs = refs[:6], refs[6:]
    own = kept.shape[1]
    hidden = states[0].shape[3]
    mine = pl.program_id(0) // (pl.num_programs(0) // 2) == x_at[0]
    grad = jnp.where(mine, kept[0], got[0].astype(F32))
    for e in range(CHUNK):
        for part in range(2):
            first = hidden * (2 * e + part)
            results = adam_update(
                states[0][e, part], grad[:, first : first + hidden],
                states[1][e, part], states[2][e, part], MODEL_DIM ** (-0.5), WEIGHT_DECAY,
            )
            for out, result in zip(outs[:3], results):
                out[e, part] = result
        first = hidden * (2 * CHUNK + e)
        turned = grad[:, first : first + hidden].T
        results = adam_update(
            states[3][e], turned, states[4][e], states[5][e],
            max(1, F // 256) ** (-0.5), WEIGHT_DECAY,
        )
        for out, result in zip(outs[3:], results):
            out[e] = result


def adam_experts(x_at, kept, got, gateup, down):
    chunks, own, columns = kept.shape
    experts, hidden = down[0].shape[:2]
    share = pl.BlockSpec((1, own, columns), lambda j: (j % chunks, 0, 0))
    big = pl.BlockSpec((CHUNK, 2, own, hidden), lambda j: (j, 0, 0, 0))
    small = pl.BlockSpec((CHUNK, hidden, own), lambda j: (j, 0, 0))
    return pl.pallas_call(
        adam_experts_kernel,
        grid=(experts // CHUNK,),
        in_specs=[smem_spec(), share, share] + [big] * 3 + [small] * 3,
        out_specs=[big] * 3 + [small] * 3,
        out_shape=[jax.ShapeDtypeStruct(gateup[0].shape, F32)] * 3
        + [jax.ShapeDtypeStruct(down[0].shape, F32)] * 3,
        compiler_params=pltpu.CompilerParams(vmem_limit_bytes=VMEM_BYTES),
        name="adam_experts",
    )(x_at, kept, got, *gateup, *down)


def join_tokens_kernel(own, first, second, out, turned):
    half = own.shape[0] // 2
    for at, part in ((0, own[:half, :]), (half, own[half:, :]), (2 * half, first[...]), (3 * half, second[...])):
        out[at : at + half, :] = part
        turned[:, at : at + half] = part.T


def join_tokens(own, first, second, *earlier):
    tokens, width = own.shape
    return pl.pallas_call(
        with_earlier(join_tokens_kernel, 3, len(earlier)),
        in_specs=[vmem_spec()] * 3 + any_specs(earlier),
        out_specs=[vmem_spec()] * 2,
        out_shape=[
            jax.ShapeDtypeStruct((2 * tokens, width), own.dtype),
            jax.ShapeDtypeStruct((width, 2 * tokens), own.dtype),
        ],
        compiler_params=pltpu.CompilerParams(vmem_limit_bytes=VMEM_BYTES),
        name="join_tokens",
    )(own, first, second, *earlier)


def move(array, dz=0, dy=0, dx=0):
    total = lax.axis_size("dp")
    inner = total // 16
    pairs = []
    for at in range(16):
        z, y, x = at // 4, at // 2 % 2, at % 2
        to = ((z + dz) % 4) * 4 + (y ^ dy) * 2 + (x ^ dx)
        pairs += [(at * inner + i, to * inner + i) for i in range(inner)]
    return lax.ppermute(array, "dp", pairs)


def place():
    at = lax.axis_index("dp") // (lax.axis_size("dp") // 16)
    return at // 4, at // 2 % 2, at % 2


def inner_groups(total):
    inner = total // 16
    return [[at * inner + i for i in range(inner)] for at in range(16)]


def inner_gather(shard, axis):
    total = lax.axis_size("dp")
    if total == 16:
        return shard
    return lax.all_gather(
        shard, "dp", axis=axis, tiled=True, axis_index_groups=inner_groups(total)
    )


def inner_scatter(share, axis):
    total = lax.axis_size("dp")
    if total == 16:
        return share
    return lax.psum_scatter(
        share, "dp", scatter_dimension=axis, tiled=True, axis_index_groups=inner_groups(total)
    )


def block_rows(parts, rows):
    z, y, x = place()
    starts = []
    for dz, dy, dx in parts:
        starts.append((((z + dz + 4) % 4) * 4 + (y ^ dy) * 2 + (x ^ dx)) * rows)
    return jnp.stack(starts).astype(jnp.int32)


def gather_z(shard):
    return jnp.stack([shard] + [move(shard, dz=-dz) for dz in Z_FROM[1:]])


def gather_ring(shard):
    below, above = move(shard, dz=1), move(shard, dz=-1)
    return [shard, below, above, move(below, dz=1)]


def send_z(parts):
    return [move(parts[k].astype(BF16), dz=Z_FROM[k]) for k in range(1, SLOTS)]


def scatter_z(parts, moved=None):
    result = parts[0]
    for one in moved or send_z(parts):
        result = result + one.astype(F32)
    return result


def gather_plane(own):
    half = own.shape[-1] // 2
    along_y, along_x = move(own, dy=1), move(own, dx=1)
    both = (move(along_y[..., :half], dx=1), move(along_x[..., half:], dy=1))
    return own, along_y, along_x, *both


def scatter_plane(pieces):
    own, along_y, along_x, both_one, both_two = pieces
    half = both_one.shape[-1]
    got_one, got_two = move(both_one, dx=1), move(both_two, dy=1)
    pass_y = jnp.concatenate(
        [(along_y[..., :half].astype(F32) + got_one.astype(F32)).astype(BF16), along_y[..., half:]],
        axis=-1,
    )
    pass_x = jnp.concatenate(
        [along_x[..., :half], (along_x[..., half:].astype(F32) + got_two.astype(F32)).astype(BF16)],
        axis=-1,
    )
    got_y, got_x = move(pass_y, dy=1), move(pass_x, dx=1)
    return scatter_z(
        [
            own[k].astype(F32) + got_y[k].astype(F32) + got_x[k].astype(F32)
            for k in range(SLOTS)
        ]
    )


PLANE = [(dz, dy, dx) for dy, dx in ((0, 0), (1, 0), (0, 1), (1, 1)) for dz in Z_FROM]


def join_kernel(rows_at, *refs):
    pieces, out = refs[:-1], refs[-1]
    slots, own, width = pieces[0].shape
    half = width // 2
    for at in range(4 * slots):
        rows = pl.ds(pl.multiple_of(rows_at[at], own), own)
        group, slot = at // slots, at % slots
        if group < 3:
            out[rows, :] = pieces[group][slot]
        else:
            out[rows, :half] = pieces[3][slot]
            out[rows, half:] = pieces[4][slot]


def part_kernel(rows_at, whole, *pieces):
    slots, own, width = pieces[0].shape
    half = width // 2
    for at in range(4 * slots):
        rows = pl.ds(pl.multiple_of(rows_at[at], own), own)
        group, slot = at // slots, at % slots
        if group < 3:
            pieces[group][slot] = whole[rows, :]
        else:
            pieces[3][slot] = whole[rows, :half]
            pieces[4][slot] = whole[rows, half:]


def smem_spec():
    return pl.BlockSpec(memory_space=pltpu.SMEM)


def vmem_spec():
    return pl.BlockSpec(memory_space=pltpu.VMEM)


def join_blocks(rows_at, pieces, earlier=()):
    slots, own, width = pieces[0].shape
    return pl.pallas_call(
        with_earlier(join_kernel, 6, len(earlier)),
        in_specs=[smem_spec()] + [vmem_spec()] * 5 + any_specs(earlier),
        out_specs=vmem_spec(),
        out_shape=jax.ShapeDtypeStruct((4 * slots * own, width), BF16),
        compiler_params=pltpu.CompilerParams(vmem_limit_bytes=VMEM_BYTES),
        name="join_blocks",
    )(rows_at, *pieces, *earlier)


def part_blocks(rows_at, whole, earlier=()):
    own, width = whole.shape[0] // (4 * SLOTS), whole.shape[1]
    full = jax.ShapeDtypeStruct((SLOTS, own, width), BF16)
    half = jax.ShapeDtypeStruct((SLOTS, own, width // 2), BF16)
    return pl.pallas_call(
        with_earlier(part_kernel, 2, len(earlier)),
        in_specs=[smem_spec(), vmem_spec()] + any_specs(earlier),
        out_specs=[vmem_spec()] * 5,
        out_shape=[full] * 3 + [half] * 2,
        compiler_params=pltpu.CompilerParams(vmem_limit_bytes=VMEM_BYTES),
        name="part_blocks",
    )(rows_at, whole, *earlier)


def after(value, *earlier):
    marks = []
    for one in earlier:
        slots = one.shape[0] if one.shape[0] == SLOTS else 1
        lead, rest = (slots > 1) * 1, one.ndim - 1
        marks.append(lax.slice(one, (lead,) + (0,) * rest, (slots,) + (1,) * rest))
    return lax.optimization_barrier((value, *marks))[0]


def split_three(values):
    high = values.astype(BF16)
    rest = values - high.astype(F32)
    middle = rest.astype(BF16)
    low = (rest - middle.astype(F32)).astype(BF16)
    return [high, middle, low]


def swap_cores(part):
    return lax.ppermute(part, "tensor", [(0, 1), (1, 0)])


def pair_sum(part):
    return part.astype(F32) + swap_cores(part).astype(F32)


def norm_backward(values, inverse, gain_row, upstream):
    scaled = values * inverse
    weighted = upstream * gain_row
    mean_term = jnp.mean(weighted * scaled, axis=-1, keepdims=True)
    return (inverse * (weighted - scaled * mean_term), jnp.sum(upstream * scaled, axis=0))


def adam_update(value, gradient, mean_old, square_old, rate, decay):
    mean_new = FIRST_DECAY * mean_old + (1.0 - FIRST_DECAY) * gradient
    square_new = SECOND_DECAY * square_old + (1.0 - SECOND_DECAY) * gradient * gradient
    mean_hat = mean_new / (1.0 - FIRST_DECAY**STEP)
    square_hat = square_new / (1.0 - SECOND_DECAY**STEP)
    updated = value - rate * (mean_hat / (jnp.sqrt(square_hat) + ADAM_EPSILON) + decay * value)
    return (mean_new, square_new, updated)


def shards(
    hidden_in,
    out_grad,
    routes,
    segments,
    norm_gains,
    gains_mean,
    gains_square,
    w_query,
    query_mean,
    query_square,
    key_value_weight,
    key_value_first_moment,
    key_value_second_moment,
    w_out,
    out_mean,
    out_square,
    w_router,
    router_mean,
    router_square,
    w_gateup,
    gateup_mean,
    gateup_square,
    w_down,
    down_mean,
    down_square,
):
    tokens, width = hidden_in.shape
    own = w_query.shape[0]
    experts, hidden = w_down.shape[0], w_down.shape[1]
    q_width, kv_width = w_query.shape[1], key_value_weight.shape[2]
    qkv_width = q_width + 2 * kv_width
    each = 2 + experts
    half_experts = experts // 2
    block = width // 16
    z_at, y_at, x_at = place()
    core = lax.axis_index("tensor")
    plane_rows = block_rows(PLANE, block)
    qkv_shard = jnp.concatenate(
        [w_query.astype(BF16), key_value_weight[0].astype(BF16), key_value_weight[1].astype(BF16)]
        + split_three(jnp.concatenate([norm_gains.T, w_router], axis=1))
        + [jnp.zeros((own, 2 * LANES - 3 * each), BF16)],
        axis=1,
    )
    all_chunks = experts // CHUNK
    chunks = all_chunks // 2
    expert_shard = jnp.concatenate(
        [
            w_gateup.astype(BF16)
            .reshape(all_chunks, CHUNK, 2, own, hidden)
            .transpose(0, 3, 1, 2, 4)
            .reshape(all_chunks, own, 2 * CHUNK * hidden),
            w_down.astype(BF16)
            .reshape(all_chunks, CHUNK, hidden, own)
            .transpose(0, 3, 1, 2)
            .reshape(all_chunks, own, CHUNK * hidden),
        ],
        axis=2,
    )
    expert_shard = inner_gather(expert_shard, 1)
    kept = lax.dynamic_slice_in_dim(expert_shard, chunks * x_at, chunks)
    given = lax.dynamic_slice_in_dim(expert_shard, chunks * (1 - x_at), chunks)
    first = x_at == 0

    def half_of(array, other=False):
        half = array.shape[0] // 2
        return lax.dynamic_slice_in_dim(array, half * ((1 - core) if other else core), half)

    def both_halves(mine):
        other = swap_cores(mine)
        lower = core == 0
        return jnp.where(lower, mine, other), jnp.where(lower, other, mine)

    def pair_chunk(c, got):
        return jnp.concatenate([jnp.where(first, kept[c], got), jnp.where(first, got, kept[c])])

    qkv_z = gather_z(inner_gather(qkv_shard, 0))
    taken = [move(given[0], dx=1)]
    pair_now = fence(pair_chunk(0, taken[0]), qkv_z)
    qkv_pieces = gather_plane(qkv_z)
    along_z = [gather_ring(pair_now)]
    out_z = gather_z(inner_gather(fence(w_out.T.astype(BF16), qkv_pieces[1], qkv_pieces[2]), 0))
    rest = move(fence(given[1:], qkv_pieces[3], qkv_pieces[4]), dx=1)
    taken += [rest[c] for c in range(chunks - 1)]
    out_pieces = gather_plane(out_z)
    pairs = [pair_now] + [pair_chunk(c, taken[c]) for c in range(1, chunks)]
    for c in range(1, chunks - 1):
        along_z.append(gather_ring(fence(pairs[c], along_z[c - 1][3])))
    along_y = [move(jnp.stack(along_z[c]), dy=1) for c in range(LATE)]

    qkv_small = join_blocks(plane_rows, qkv_pieces)
    qkv_full = qkv_small[:, :qkv_width]
    pieces = qkv_small[:, qkv_width : qkv_width + 3 * each].astype(F32)
    small = pieces[:, :each] + pieces[:, each : 2 * each] + pieces[:, 2 * each :]
    gains_full, router_full = small[:, :2].T, small[:, 2:]

    inputs = hidden_in.astype(F32)
    inverse_one = lax.rsqrt(jnp.mean(inputs * inputs, axis=-1, keepdims=True) + NORM_EPSILON)
    normed_low = (inputs * inverse_one * gains_full[0]).astype(BF16)
    qkv_lin = jnp.dot(normed_low, qkv_full, preferred_element_type=F32)
    cosine, sine = rope_tables(seq_positions(segments))
    attended, queries, keys, values, lse = attention_forward(
        qkv_lin, cosine, sine, segments, earlier=(out_pieces[1], taken[0])
    )
    output_full = join_blocks(plane_rows, out_pieces, earlier=(attended, along_z[0][3]))
    attention_part = lax.dot_general(attended, output_full, NT, preferred_element_type=F32)
    attention_part = attention_part.astype(BF16)
    og_got = move(fence(half_of(out_grad), output_full), dx=1)
    attention = pair_sum(attention_part)
    middle = inputs + RESIDUAL_SCALE * attention
    inverse_two = lax.rsqrt(jnp.mean(middle * middle, axis=-1, keepdims=True) + NORM_EPSILON)
    normed_two = middle * inverse_two * gains_full[1]
    normed_two_low = normed_two.astype(BF16)
    logits = jnp.dot(normed_two, router_full, precision=HIGHEST_PRECISION)
    expert_ids = jnp.arange(experts, dtype=jnp.int32)
    chosen = jnp.any(routes[:, :, None] == expert_ids[None, None, :], axis=1)
    combine = jax.nn.softmax(jnp.where(chosen, logits, -jnp.inf), axis=-1)

    def halves_of(columns):
        one, two = columns[:, :half_experts], columns[:, half_experts:]
        first = x_at == 0
        return jnp.where(first, one, two), jnp.where(first, two, one)

    combine_kept, combine_given = halves_of(combine)
    combine_pair = jnp.concatenate([combine_kept, move(combine_given, dx=1)])
    x_got = move(half_of(normed_two_low), dx=1)
    og_pair, og_turned = join_tokens(out_grad, *both_halves(og_got), along_z[1][3])
    x_pair, x_turned = join_tokens(normed_two_low, *both_halves(x_got), along_z[2][3], along_y[0])

    mix_parts, dx_parts, gate_parts, z_parts, near_grads, far_grads = experts_pass(
        x_pair, og_pair, x_turned, og_turned, combine_pair, along_z, pairs[-1], along_y
    )
    gate_pair = jnp.concatenate([gate_parts[c] for c in range(chunks)], axis=1)

    def to_neighbour(part):
        both = half_of(part).astype(F32) + swap_cores(half_of(part, other=True)).astype(F32)
        return jnp.concatenate(both_halves(move(both.astype(BF16), dx=1)))

    gate_got = move(gate_pair[tokens:], dx=1)
    gate_grad = pair_sum(
        jnp.concatenate(
            [
                jnp.where(first, gate_pair[:tokens], gate_got),
                jnp.where(first, gate_got, gate_pair[:tokens]),
            ],
            axis=1,
        )
    )
    z_got = [send_z(z_parts[0])]
    got_y = [move(far_grads[0], dy=1)]
    dx_pair = sum_parts(dx_parts)
    normed_two_part = pair_sum(dx_pair[:tokens]) + to_neighbour(dx_pair[tokens:]).astype(F32)
    z_got.append(send_z([None, *fence_all(z_parts[1][1:], *z_got[0])]))
    got_y.append(move(fence(far_grads[1], got_y[0]), dy=1))

    logit_grad = combine * (gate_grad - jnp.sum(combine * gate_grad, axis=-1, keepdims=True))
    router_grad = jnp.dot(normed_two.T, logit_grad, precision=HIGHEST_PRECISION)
    normed_two_grad = normed_two_part + jnp.dot(
        logit_grad, router_full.T, precision=HIGHEST_PRECISION
    )
    middle_part, gain_two_grad = norm_backward(middle, inverse_two, gains_full[1], normed_two_grad)
    middle_grad = out_grad.astype(F32) + middle_part
    attention_back = (RESIDUAL_SCALE * middle_grad).astype(BF16)
    attended_grad = jnp.dot(attention_back, output_full, preferred_element_type=F32).astype(BF16)
    output_weight_grad = lax.dot_general(attention_back, attended, TN, preferred_element_type=F32)
    output_share = scatter_plane(
        part_blocks(plane_rows, output_weight_grad.astype(BF16), earlier=z_got[0])
    )
    query_grad, keyval_grad = attention_backward(
        queries, keys, values, attended, attended_grad, cosine, sine, segments, lse,
        earlier=got_y[:1],
    )
    for c in range(chunks - SENT):
        waits = (query_grad, *z_got[-1])
        z_parts.append(sum_y(near_grads[c], got_y[c], *waits))
        z_got.append(send_z(z_parts[-1]))
    qkv_grad = jnp.concatenate([query_grad, keyval_grad], axis=1)
    qkv_weight_grad = lax.dot_general(normed_low, qkv_grad, TN, preferred_element_type=F32)
    qkv_parts = part_blocks(
        plane_rows,
        jnp.concatenate(
            [
                qkv_weight_grad.astype(BF16),
                gain_two_grad[:, None].astype(BF16),
                router_grad.astype(BF16),
                jnp.zeros((width, 2 * LANES - 1 - experts), BF16),
            ],
            axis=1,
        ),
    )
    qkv_share = scatter_plane(qkv_parts)
    normed_part = lax.dot_general(qkv_grad, qkv_full, NT, preferred_element_type=F32)
    normed_grad = pair_sum(normed_part.astype(BF16))
    scaled = inputs * inverse_one
    weighted = normed_grad * gains_full[0]
    mean_term = jnp.mean(weighted * scaled, axis=-1, keepdims=True)
    input_grad = middle_grad + inverse_one * (weighted - scaled * mean_term)

    mix_pair = sum_parts(mix_parts, qkv_parts[0])
    expert_mix = pair_sum(mix_pair[:tokens]) + to_neighbour(mix_pair[tokens:]).astype(F32)
    block_out = (middle + RESIDUAL_SCALE * expert_mix).astype(BF16)
    kept_shares, got_shares = [], []
    x_here = x_at.astype(jnp.int32)[None]
    for low in range(0, chunks, 2):
        kept_share, given_share = sum_z(
            x_here,
            [[z_parts[c][0], *z_got[c]] for c in range(low, low + 2)],
            query_grad,
        )
        kept_shares.append(kept_share)
        got_shares.append(move(given_share, dx=1))
    kept_share = inner_scatter(jnp.concatenate(kept_shares), 1)
    got_share = inner_scatter(jnp.concatenate(got_shares), 1)

    output_share = inner_scatter(output_share, 0).T
    qkv_share = inner_scatter(qkv_share, 0)
    query_share = qkv_share[:, :q_width]
    keyval_share = jnp.stack(
        [qkv_share[:, q_width : q_width + kv_width], qkv_share[:, q_width + kv_width : qkv_width]]
    )
    gain_one_part = jnp.sum(w_query.astype(BF16).astype(F32) * query_share, axis=1) + jnp.sum(
        key_value_weight.astype(BF16).astype(F32) * keyval_share, axis=(0, 2)
    )
    gain_one_share = pair_sum(gain_one_part[None, :]) / norm_gains[:1]
    gains_share = jnp.concatenate([gain_one_share, qkv_share[:, qkv_width][None, :]])
    router_share = qkv_share[:, qkv_width + 1 : qkv_width + 1 + experts]

    gains_result = adam_update(norm_gains, gains_share, gains_mean, gains_square, GAIN_RATE, 0.0)
    query_result = adam_update(
        w_query, query_share, query_mean, query_square, (MODEL_DIM // 12) ** (-0.5), WEIGHT_DECAY
    )
    keyval_result = adam_update(
        key_value_weight,
        keyval_share,
        key_value_first_moment,
        key_value_second_moment,
        (MODEL_DIM // 12) ** (-0.5),
        WEIGHT_DECAY,
    )
    out_result = adam_update(
        w_out,
        output_share,
        out_mean,
        out_square,
        max(1, QUERY_HEADS * HEAD_DIM // 96) ** (-0.5),
        WEIGHT_DECAY,
    )
    router_result = adam_update(
        w_router, router_share, router_mean, router_square, (4 * MODEL_DIM) ** (-0.5), WEIGHT_DECAY
    )
    expert_results = adam_experts(
        x_here, kept_share, got_share,
        (w_gateup, gateup_mean, gateup_square), (w_down, down_mean, down_square),
    )
    return (
        (block_out, input_grad)
        + gains_result
        + query_result
        + keyval_result
        + out_result
        + router_result
        + tuple(expert_results)
    )


def solution(mesh):
    tokens, gains = P("dp", None), P(None, "dp")
    query, keyval, out = P("dp", "tensor"), P(None, "dp", "tensor"), P("tensor", "dp")
    router, gateup, down = P("dp", None), P(None, None, "dp", "tensor"), P(None, "tensor", "dp")
    states = tuple(
        spec for one in (gains, query, keyval, out, router, gateup, down) for spec in (one,) * 3
    )
    return jax.shard_map(
        shards,
        mesh=mesh,
        in_specs=(tokens, tokens, tokens, P("dp")) + states,
        out_specs=(tokens, tokens) + states,
        check_vma=False,
    )
```

```python
import functools

import jax
import jax.numpy as jnp
from jax import lax
from jax.experimental import pallas as pl
from jax.experimental.pallas import tpu as pltpu
from jax.sharding import PartitionSpec as P

MODEL_DIM = 1536
QUERY_HEADS = 24
HEAD_DIM = 64
F = 512
SEQUENCE_LENGTH = 1024
STEP = 10

NORM_EPSILON = 1e-06
SCORE_SCALE = 0.015625
RESIDUAL_SCALE = 0.22
ROPE_BASE = 10000.0
FIRST_DECAY = 0.9
SECOND_DECAY = 0.95
ADAM_EPSILON = 1e-08
WEIGHT_DECAY = 0.1
GAIN_RATE = 0.6
MASK_VALUE = -1e30
HIGHEST_PRECISION = lax.Precision.HIGHEST

BF16 = jnp.bfloat16
F32 = jnp.float32
LANES = 128
ROWS = 256
VMEM_BYTES = 58 * 1024 * 1024

NN = (((1,), (0,)), ((), ()))
NT = (((1,), (1,)), ((), ()))
TN = (((0,), (0,)), ((), ()))


def dot(a, b, dims=NN):
    return lax.dot_general(a, b, dims, preferred_element_type=F32)


def seq_positions(segment_row):
    counter = jnp.arange(segment_row.shape[0], dtype=jnp.int32)
    earlier = jnp.concatenate([segment_row[:1] - 1, segment_row[:-1]])
    starts = lax.cummax(jnp.where(segment_row != earlier, counter, 0), axis=0)
    return counter - starts


def rope_tables(positions):
    half_width = HEAD_DIM // 2
    frequency = ROPE_BASE ** (-2.0 * jnp.arange(half_width, dtype=F32) / HEAD_DIM)
    angles = positions.astype(F32)[:, None] * frequency[None, :]
    cosine, sine = jnp.cos(angles), jnp.sin(angles)
    return (
        jnp.concatenate([cosine] * 4, axis=1),
        jnp.concatenate([-sine, sine] * 2, axis=1),
    )


def rotate_halves(slab):
    lane = lax.broadcasted_iota(jnp.int32, slab.shape, 1)
    ahead = pltpu.roll(slab, LANES - HEAD_DIM // 2, 1)
    behind = pltpu.roll(slab, HEAD_DIM // 2, 1)
    return jnp.where(lane % HEAD_DIM < HEAD_DIM // 2, ahead, behind)


def half_mask(rows, upper):
    lane = lax.broadcasted_iota(jnp.int32, (rows, LANES), 1)
    return (lane >= HEAD_DIM) if upper else (lane < HEAD_DIM)


def spread_heads(slab, lower_out, upper_out, index):
    rows = slab.shape[0]
    moved = pltpu.roll(slab.astype(F32), HEAD_DIM, 1).astype(BF16)
    zero = jnp.zeros_like(slab)
    low, high = half_mask(rows, False), half_mask(rows, True)
    lower_out[index] = jnp.where(low, slab, zero)
    upper_out[index] = jnp.where(high, moved, zero)
    lower_out[index + 1] = jnp.where(low, moved, zero)
    upper_out[index + 1] = jnp.where(high, slab, zero)


def fill_bias(bias, seg_col, seg_row):
    span = bias.shape[0]
    for at in range(0, span, ROWS):
        rows_at = at + lax.broadcasted_iota(jnp.int32, (ROWS, span), 0)
        cols_at = lax.broadcasted_iota(jnp.int32, (ROWS, span), 1)
        allowed = (rows_at >= cols_at) & (seg_col[at : at + ROWS, :] == seg_row[...])
        bias[at : at + ROWS, :] = jnp.where(allowed, 0.0, MASK_VALUE).astype(F32)


def with_earlier(kernel, inputs, count):
    def run(*refs):
        kernel(*refs[:inputs], *refs[inputs + count :])

    return run


def any_specs(arrays):
    return [pl.BlockSpec(memory_space=pl.ANY)] * len(arrays)


def attention_forward_kernel(
    lin_ref, kv_ref, cos_ref, sin_ref, seg_col, seg_row,
    out_ref, q_ref, k_ref, v_ref, lse_ref,
    bias, k_low, k_high, v_low, v_high,
):
    slab_at = pl.program_id(0)
    span = lin_ref.shape[0]
    kv_slabs = kv_ref.shape[1] // (2 * LANES)

    @pl.when(slab_at == 0)
    def _():
        fill_bias(bias, seg_col, seg_row)
        for j in range(kv_slabs):
            lanes = slice(j * LANES, (j + 1) * LANES)
            lin = kv_ref[:, lanes]
            keys = (lin * cos_ref[...] + rotate_halves(lin) * sin_ref[...]).astype(BF16)
            k_ref[:, lanes] = keys
            spread_heads(keys, k_low, k_high, 2 * j)
            lanes = slice((kv_slabs + j) * LANES, (kv_slabs + j + 1) * LANES)
            values = kv_ref[:, lanes].astype(BF16)
            v_ref[:, slice(j * LANES, (j + 1) * LANES)] = values
            spread_heads(values, v_low, v_high, 2 * j)

    lin = lin_ref[...]
    q_ref[...] = (lin * cos_ref[...] + rotate_halves(lin) * sin_ref[...]).astype(BF16)
    kv_even, kv_odd = (2 * slab_at) // 3, (2 * slab_at + 1) // 3
    for at in range(0, span, ROWS):
        rows = slice(at, at + ROWS)
        queries = q_ref[rows, :]
        total = None
        stats = []
        for keys, values, kv_at in ((k_low, v_low, kv_even), (k_high, v_high, kv_odd)):
            upto = at + ROWS
            scores = dot(queries, keys[kv_at, :upto, :], NT) * SCORE_SCALE + bias[rows, :upto]
            highest = jnp.max(scores, axis=1, keepdims=True)
            weights = jnp.exp(scores - highest)
            summed = jnp.sum(weights, axis=1, keepdims=True)
            probability = (weights * (1.0 / summed)).astype(BF16)
            part = dot(probability, values[kv_at, :upto, :])
            total = part if total is None else total + part
            stats.append(highest + jnp.log(summed))
        out_ref[rows, :] = total.astype(BF16)
        spread = jnp.where(half_mask(ROWS, False), stats[0], stats[1])
        turned = spread.T
        lse_ref[0, 0:1, rows] = turned[0:1, :]
        lse_ref[0, 1:2, rows] = turned[HEAD_DIM : HEAD_DIM + 1, :]


def attention_forward(qkv_lin, cosine, sine, segment_row, earlier=()):
    span = qkv_lin.shape[0]
    q_width = MODEL_DIM // 2
    kv_width = (qkv_lin.shape[1] - q_width) // 2
    slabs, kv_heads = q_width // LANES, kv_width // HEAD_DIM
    whole = lambda shape: pl.BlockSpec(shape, lambda g: (0,) * len(shape))
    slab = pl.BlockSpec((span, LANES), lambda g: (0, g))
    q_lin, kv_lin = qkv_lin[:, :q_width], qkv_lin[:, q_width:]
    return pl.pallas_call(
        with_earlier(attention_forward_kernel, 6, len(earlier)),
        grid=(slabs,),
        in_specs=[
            slab, whole((span, 2 * kv_width)), whole((span, LANES)), whole((span, LANES)),
            whole((span, 1)), whole((1, span)),
        ]
        + any_specs(earlier),
        out_specs=[
            slab, slab, whole((span, kv_width)), whole((span, kv_width)),
            pl.BlockSpec((1, 8, span), lambda g: (g, 0, 0)),
        ],
        out_shape=[
            jax.ShapeDtypeStruct((span, q_width), BF16),
            jax.ShapeDtypeStruct((span, q_width), BF16),
            jax.ShapeDtypeStruct((span, kv_width), BF16),
            jax.ShapeDtypeStruct((span, kv_width), BF16),
            jax.ShapeDtypeStruct((slabs, 8, span), F32),
        ],
        scratch_shapes=[pltpu.VMEM((span, span), F32)]
        + [pltpu.VMEM((kv_heads, span, LANES), BF16)] * 4,
        compiler_params=pltpu.CompilerParams(vmem_limit_bytes=VMEM_BYTES),
        cost_estimate=pl.CostEstimate(
            flops=32 * slabs * span * span * LANES, bytes_accessed=16 * span * q_width,
            transcendentals=slabs * span * span,
        ),
        name="attention_forward",
    )(q_lin, kv_lin, cosine, sine, segment_row[:, None], segment_row[None, :], *earlier)


def attention_backward_kernel(
    q_ref, k_ref, v_ref, out_ref, grad_ref, cos_ref, sin_ref, seg_col, seg_row, lse_ref,
    dq_ref, dkv_ref,
    bias, k_low, k_high, v_low, v_high, dk_low, dk_high, dv_low, dv_high, dq_sum,
):
    slab_at = pl.program_id(0)
    span = q_ref.shape[0]
    kv_slabs = k_ref.shape[1] // LANES

    @pl.when(slab_at == 0)
    def _():
        for at in range(0, span, ROWS):
            keys_at = at + lax.broadcasted_iota(jnp.int32, (ROWS, span), 0)
            rows_at = lax.broadcasted_iota(jnp.int32, (ROWS, span), 1)
            allowed = (rows_at >= keys_at) & (seg_col[at : at + ROWS, :] == seg_row[...])
            bias[at : at + ROWS, :] = jnp.where(allowed, 0.0, MASK_VALUE).astype(F32)
        for j in range(kv_slabs):
            lanes = slice(j * LANES, (j + 1) * LANES)
            spread_heads(k_ref[:, lanes], k_low, k_high, 2 * j)
            spread_heads(v_ref[:, lanes], v_low, v_high, 2 * j)
        for sums in (dk_low, dk_high, dv_low, dv_high):
            sums[...] = jnp.zeros_like(sums)

    kv_even, kv_odd = (2 * slab_at) // 3, (2 * slab_at + 1) // 3
    for at in range(0, span, ROWS):
        rows = slice(at, at + ROWS)
        upto = at + ROWS
        queries, grads = q_ref[rows, :], grad_ref[rows, :]
        turned = (grads.astype(F32) * out_ref[rows, :].astype(F32)).T
        zero = jnp.zeros_like(queries)
        dq_part = None
        for upper, keys, values, dk_sum, dv_sum, kv_at in (
            (False, k_low, v_low, dk_low, dv_low, kv_even),
            (True, k_high, v_high, dk_high, dv_high, kv_odd),
        ):
            first = HEAD_DIM if upper else 0
            delta = jnp.sum(turned[first : first + HEAD_DIM, :], axis=0, keepdims=True)
            head = 1 if upper else 0
            total = lse_ref[0, head : head + 1, rows]
            keys_here = keys[kv_at, :upto, :]
            scores = dot(keys_here, queries, NT) * SCORE_SCALE + bias[:upto, rows]
            probability = jnp.exp(scores - total)
            prob_grad = dot(values[kv_at, :upto, :], grads, NT)
            score_grad = (probability * (prob_grad - delta)).astype(BF16)
            mask = half_mask(ROWS, upper)
            dv_sum[kv_at, :upto, :] += dot(
                probability.astype(BF16), jnp.where(mask, grads, zero)
            )
            dk_sum[kv_at, :upto, :] += dot(score_grad, jnp.where(mask, queries, zero))
            part = dot(score_grad, keys_here, TN)
            dq_part = part if dq_part is None else dq_part + part
        dq_sum[rows, :] = dq_part * SCORE_SCALE
    slab = dq_sum[...]
    dq_ref[...] = (slab * cos_ref[...] - rotate_halves(slab) * sin_ref[...]).astype(BF16)

    @pl.when(slab_at == pl.num_programs(0) - 1)
    def _():
        low = half_mask(span, False)

        def joined(sums_low, sums_high, j):
            one = sums_low[2 * j] + pltpu.roll(sums_high[2 * j], HEAD_DIM, 1)
            two = pltpu.roll(sums_low[2 * j + 1], HEAD_DIM, 1) + sums_high[2 * j + 1]
            return jnp.where(low, one, two)

        for j in range(kv_slabs):
            slab = joined(dk_low, dk_high, j) * SCORE_SCALE
            dkv_ref[:, j * LANES : (j + 1) * LANES] = (
                slab * cos_ref[...] - rotate_halves(slab) * sin_ref[...]
            ).astype(BF16)
            at = (kv_slabs + j) * LANES
            dkv_ref[:, at : at + LANES] = joined(dv_low, dv_high, j).astype(BF16)


def attention_backward(
    queries, keys, values, attended, grad, cosine, sine, segment_row, lse, earlier=()
):
    span, q_width = queries.shape
    kv_width = keys.shape[1]
    slabs, kv_heads = q_width // LANES, kv_width // HEAD_DIM
    whole = lambda shape: pl.BlockSpec(shape, lambda g: (0,) * len(shape))
    slab = pl.BlockSpec((span, LANES), lambda g: (0, g))
    return pl.pallas_call(
        with_earlier(attention_backward_kernel, 10, len(earlier)),
        grid=(slabs,),
        in_specs=[
            slab, whole((span, kv_width)), whole((span, kv_width)), slab, slab,
            whole((span, LANES)), whole((span, LANES)), whole((span, 1)), whole((1, span)),
            pl.BlockSpec((1, 8, span), lambda g: (g, 0, 0)),
        ]
        + any_specs(earlier),
        out_specs=[slab, whole((span, 2 * kv_width))],
        out_shape=[
            jax.ShapeDtypeStruct((span, q_width), BF16),
            jax.ShapeDtypeStruct((span, 2 * kv_width), BF16),
        ],
        scratch_shapes=[pltpu.VMEM((span, span), F32)]
        + [pltpu.VMEM((kv_heads, span, LANES), BF16)] * 4
        + [pltpu.VMEM((kv_heads, span, LANES), F32)] * 4
        + [pltpu.VMEM((span, LANES), F32)],
        compiler_params=pltpu.CompilerParams(vmem_limit_bytes=VMEM_BYTES),
        cost_estimate=pl.CostEstimate(
            flops=40 * slabs * span * span * LANES, bytes_accessed=16 * span * q_width,
            transcendentals=slabs * span * span,
        ),
        name="attention_backward",
    )(
        queries, keys, values, attended, grad, cosine, sine,
        segment_row[:, None], segment_row[None, :], lse, *earlier,
    )


EXPERT_ROWS = 256
EXPERT_VMEM = 61 * 1024 * 1024
SLOTS = 4
Z_FROM = (0, -1, 1, 2)
CHUNK = 2
LATE = 2
SENT = 2
MESH_ID = pl.DeviceIdType.MESH


def experts_kernel(
    inner, chunks, row_steps, x_ref, og_ref, xt_ref, ogt_ref, combine_ref, *refs
):
    pairs_ref, near_ref, far_ref, refs = *refs[:3], refs[3:]
    last_near = pairs_ref.at[chunks - 1]
    mix_ref, dx_ref, gate_ref, refs = *refs[:3], refs[3:]
    sum_refs, refs = refs[: SENT * SLOTS], refs[SENT * SLOTS :]
    near_outs, refs = refs[: chunks - SENT], refs[chunks - SENT :]
    far_outs, refs = refs[: chunks - SENT], refs[chunks - SENT :]
    part_outs, refs = refs[: SLOTS - 1], refs[SLOTS - 1 :]
    slots, arrived, held_both, held_down = refs[:4]
    weights, grads = slots.at[pl.ds(1, chunks)], slots
    near_sem, far_sem, z_send, z_recv, y_send, y_recv, sum_send, sum_recv, out_sem = refs[4:13]
    part_send, part_recv = refs[13:]
    step = pl.program_id(0)
    steps = row_steps + SLOTS
    chunk, turn = step // steps, step % steps
    block = x_ref.shape[1] // 16
    hidden = held_down.shape[1] // CHUNK
    both = 2 * hidden * CHUNK
    lane = lax.broadcasted_iota(jnp.int32, (EXPERT_ROWS, combine_ref.shape[1]), 1)

    me = lax.axis_index("dp")
    at = me // inner
    z, y = at // 4, at // 2 % 2
    spots = [(z + dz + 4) % 4 for dz in Z_FROM]
    across = me + (1 - 2 * y) * 2 * inner
    along = [me + (spot - z) * 4 * inner for spot in spots]

    def to(device):
        return {"dp": device}

    def near_piece(c, k):
        return pairs_ref.at[c] if k == 0 else near_ref.at[c, k - 1]

    def near_copy(c, k):
        return pltpu.make_async_copy(
            near_piece(c, k), weights.at[c, spots[k], y], near_sem.at[c, k]
        )

    def far_copy(c, k):
        return pltpu.make_async_copy(
            far_ref.at[c, k], weights.at[c, spots[k], 1 - y], far_sem.at[c, k]
        )

    def z_copy(k):
        here = weights.at[chunks - 1, z, y]
        return pltpu.make_async_remote_copy(
            last_near, here, z_send.at[k], z_recv.at[(0, 2, 1, 3)[k]],
            device_id=to(along[k]), device_id_type=MESH_ID,
        )

    def z_wait(k):
        place = weights.at[chunks - 1, spots[k], y]
        return pltpu.make_async_remote_copy(
            last_near, place, z_send.at[k], z_recv.at[k],
            device_id=to(along[k]), device_id_type=MESH_ID,
        )

    def y_copy(c, k):
        place = weights.at[c, spots[k], y]
        if c == chunks - 1:
            source = last_near if k == 0 else place
        else:
            source = near_piece(c, k)
        return pltpu.make_async_remote_copy(
            source, place, y_send.at[c - LATE, k], y_recv.at[c - LATE, k],
            device_id=to(across), device_id_type=MESH_ID,
        )

    def y_wait(c, k):
        place = weights.at[c, spots[k], 1 - y]
        return pltpu.make_async_remote_copy(
            place, place, y_send.at[c - LATE, k], y_recv.at[c - LATE, k],
            device_id=to(across), device_id_type=MESH_ID,
        )

    def sum_copy(c):
        return pltpu.make_async_remote_copy(
            grads.at[c, :, 1 - y], arrived.at[c], sum_send.at[c], sum_recv.at[c],
            device_id=to(across), device_id_type=MESH_ID,
        )

    def sum_out(c, k):
        return pltpu.make_async_copy(
            grads.at[c, spots[k], y], sum_refs[SLOTS * c + k], out_sem.at[c, k]
        )

    def near_out_copy(c, k):
        return pltpu.make_async_copy(
            grads.at[c, spots[k], y], near_outs[c - SENT].at[k], out_sem.at[c, k]
        )

    def far_out_copy(c, k):
        return pltpu.make_async_copy(
            grads.at[c, spots[k], 1 - y], far_outs[c - SENT].at[k], out_sem.at[c, SLOTS + k]
        )

    @pl.when(step == 0)
    def _():
        barrier = pltpu.get_barrier_semaphore()
        for device in [across] + along[1:]:
            pl.semaphore_signal(barrier, inc=1, device_id=to(device), device_id_type=MESH_ID)
        pl.semaphore_wait(barrier, SLOTS)
        for k in range(SLOTS):
            near_copy(0, k).start()
            far_copy(0, k).start()
        for c in range(LATE, chunks - 1):
            for k in range(SLOTS):
                y_copy(c, k).start()
        for k in range(1, SLOTS):
            z_copy(k).start()
        for c in range(1, chunks):
            for k in range(SLOTS):
                if c < chunks - 1 or k == 0:
                    near_copy(c, k).start()
                if c < LATE:
                    far_copy(c, k).start()

    for c in range(chunks):

        @pl.when(step == c * steps)
        def _():
            for k in range(SLOTS):
                if c < chunks - 1 or k == 0:
                    near_copy(c, k).wait()
                if c < LATE:
                    far_copy(c, k).wait()
                else:
                    y_wait(c, k).wait_recv()

    @pl.when(step == steps)
    def _():
        for k in range(SLOTS):
            if k > 0:
                z_wait(k).wait_recv()
            y_copy(chunks - 1, k).start()

    def add_arrived(c):
        sum_copy(c).wait_recv()
        for k in range(SLOTS):
            own = grads.at[c, spots[k], y]
            own[...] = (own[...].astype(F32) + arrived[c, spots[k]].astype(F32)).astype(BF16)

    def part_copy(k):
        return pltpu.make_async_remote_copy(
            grads.at[0, spots[k], y], part_outs[(0, 2, 1, 3)[k] - 1],
            part_send.at[k], part_recv.at[(0, 2, 1, 3)[k]],
            device_id=to(along[k]), device_id_type=MESH_ID,
        )

    def part_wait(k):
        return pltpu.make_async_remote_copy(
            grads.at[0, spots[k], y], part_outs[k - 1], part_send.at[k], part_recv.at[k],
            device_id=to(along[k]), device_id_type=MESH_ID,
        )

    @pl.when(step == 3 * steps + 2)
    def _():
        add_arrived(0)
        sum_out(0, 0).start()
        for k in range(1, SLOTS):
            part_copy(k).start()

    @pl.when(turn < row_steps)
    def _():
        rows = pl.ds(pl.multiple_of(turn * EXPERT_ROWS, EXPERT_ROWS), EXPERT_ROWS)
        width = x_ref.shape[1]
        for e in range(CHUNK):
            first = 2 * hidden * e
            w_both = weights[chunk, :, :, :, first : first + 2 * hidden].reshape(width, 2 * hidden)
            start = both + hidden * e
            w_down = weights[chunk, :, :, :, start : start + hidden].reshape(width, hidden)
            gate_up = dot(x_ref[...], w_both)
            raw = dot(og_ref[...], w_down) * RESIDUAL_SCALE
            gate, up = gate_up[:, :hidden], gate_up[:, hidden:]
            column = jnp.sum(
                jnp.where(lane == chunk * CHUNK + e, combine_ref[...], 0.0), axis=1, keepdims=True
            )
            sigmoid = 1.0 / (1.0 + jnp.exp(-gate))
            active = gate * sigmoid
            inner_value = (active * up).astype(BF16).astype(F32)
            held_down[rows, hidden * e : hidden * (e + 1)] = (inner_value * column).astype(BF16)
            gate_ref[0, :, e : e + 1] = jnp.sum(inner_value * raw, axis=1, keepdims=True)
            inner_grad = raw * column
            held_both[rows, first : first + hidden] = (
                inner_grad * up * sigmoid * (1.0 + gate * (1.0 - sigmoid))
            ).astype(BF16)
            held_both[rows, first + hidden : first + 2 * hidden] = (inner_grad * active).astype(BF16)
        for part in range(SLOTS):
            cols = slice(4 * block * part, 4 * block * (part + 1))
            w_both = weights[chunk, part, :, :, :both].reshape(4 * block, both)
            w_down = weights[chunk, part, :, :, both:].reshape(4 * block, hidden * CHUNK)
            mix_ref[0, :, cols] = dot(held_down[rows, :], w_down, NT).astype(BF16)
            dx_ref[0, :, cols] = dot(held_both[rows, :], w_both, NT).astype(BF16)

    @pl.when(turn >= row_steps)
    def _():
        part = turn - row_steps
        grads[chunk, part, :, :, :both] = (
            dot(xt_ref[...], held_both[...]).astype(BF16).reshape(2, 2 * block, both)
        )
        grads[chunk, part, :, :, both:] = (
            (dot(ogt_ref[...], held_down[...]) * RESIDUAL_SCALE)
            .astype(BF16)
            .reshape(2, 2 * block, hidden * CHUNK)
        )

    for c in range(chunks):

        @pl.when(step == (c + 1) * steps - 1)
        def _():
            if c < SENT:
                sum_copy(c).start()
            else:
                for k in range(SLOTS):
                    near_out_copy(c, k).start()
                    far_out_copy(c, k).start()

    @pl.when(step == chunks * steps - 1)
    def _():
        add_arrived(1)
        for k in range(SLOTS):
            sum_out(1, k).start()
        for c in range(SENT, chunks):
            for k in range(SLOTS):
                near_out_copy(c, k).wait()
                far_out_copy(c, k).wait()
        for c in range(SENT):
            sum_copy(c).wait_send()
        for k in range(SLOTS):
            sum_out(1, k).wait()
        sum_out(0, 0).wait()
        for c in range(LATE, chunks):
            for k in range(SLOTS):
                y_copy(c, k).wait_send()
        for k in range(1, SLOTS):
            z_copy(k).wait_send()
            part_copy(k).wait_send()
            part_wait(k).wait_recv()


def experts_pass(x, og, xt, ogt, combine, pairs, near, far):
    tokens, width = x.shape
    chunks, pair, columns = pairs.shape
    hidden = columns // (3 * CHUNK)
    row_steps = tokens // EXPERT_ROWS
    steps = row_steps + SLOTS
    inner = lax.axis_size("dp") // 16
    row_at = lambda s: (jnp.minimum(s % steps, row_steps - 1), 0)
    width_at = lambda s: (jnp.maximum(s % steps - row_steps, 0), 0)
    sum_at = lambda s: (s // steps, jnp.minimum(s % steps, row_steps - 1), 0)
    row = pl.BlockSpec((EXPERT_ROWS, width), row_at)
    turned = pl.BlockSpec((width // SLOTS, tokens), width_at)
    summed = pl.BlockSpec((1, EXPERT_ROWS, width), sum_at)
    anywhere = pl.BlockSpec(memory_space=pl.ANY)
    left = chunks - SENT
    dma = pltpu.SemaphoreType.DMA
    outs = pl.pallas_call(
        functools.partial(experts_kernel, inner, chunks, row_steps),
        grid=(chunks * steps,),
        in_specs=[row, row, turned, turned, pl.BlockSpec((EXPERT_ROWS, combine.shape[1]), row_at)]
        + [anywhere] * 3,
        out_specs=[summed, summed, pl.BlockSpec((1, EXPERT_ROWS, CHUNK), sum_at)]
        + [anywhere] * (SENT * SLOTS + 2 * left + SLOTS - 1),
        out_shape=[
            jax.ShapeDtypeStruct((chunks, tokens, width), BF16),
            jax.ShapeDtypeStruct((chunks, tokens, width), BF16),
            jax.ShapeDtypeStruct((chunks, tokens, CHUNK), F32),
        ]
        + [jax.ShapeDtypeStruct((pair, columns), BF16)] * (SENT * SLOTS)
        + [jax.ShapeDtypeStruct((SLOTS, pair, columns), BF16)] * (2 * left)
        + [jax.ShapeDtypeStruct((pair, columns), BF16)] * (SLOTS - 1),
        scratch_shapes=[
            pltpu.VMEM((chunks + 1, SLOTS, 2, pair, columns), BF16),
            pltpu.VMEM((SENT, SLOTS, pair, columns), BF16),
            pltpu.VMEM((tokens, 2 * hidden * CHUNK), BF16),
            pltpu.VMEM((tokens, hidden * CHUNK), BF16),
            dma((chunks, SLOTS)), dma((LATE, SLOTS)), dma((SLOTS,)), dma((SLOTS,)),
            dma((chunks - LATE, SLOTS)), dma((chunks - LATE, SLOTS)), dma((SENT,)), dma((SENT,)),
            dma((chunks, 2 * SLOTS)), dma((SLOTS,)), dma((SLOTS,)),
        ],
        compiler_params=pltpu.CompilerParams(
            vmem_limit_bytes=EXPERT_VMEM, collective_id=0, has_side_effects=True
        ),
        cost_estimate=pl.CostEstimate(
            flops=8 * tokens * width * chunks * columns,
            bytes_accessed=2 * chunks * width * columns, transcendentals=0,
        ),
        name="experts_pass",
    )(x, og, xt, ogt, combine, pairs, near, far)
    outs, rest = outs[:3], outs[3:]
    sums = [rest[SLOTS * c : SLOTS * (c + 1)] for c in range(SENT)]
    rest = rest[SENT * SLOTS :]
    return *outs, sums, rest[:left], rest[left : 2 * left], rest[2 * left :]


class Copies:
    def __init__(self, send, recv, local):
        self.send, self.recv, self.local = send, recv, local
        self.sends, self.recvs, self.locals, self.started = {}, {}, {}, []

    def remote(self, ends, name, arrives, device):
        sent = self.sends.setdefault(name, len(self.sends))
        got = self.recvs.setdefault(arrives, len(self.recvs))

        def make():
            source, target = ends()
            return pltpu.make_async_remote_copy(
                source, target, self.send.at[sent], self.recv.at[got],
                device_id=device, device_id_type=MESH_ID,
            )

        make().start()
        self.started.append(lambda: make().wait_send())

    def arrived(self, place, name, device):
        got = self.recvs.setdefault(name, len(self.recvs))
        pltpu.make_async_remote_copy(
            place, place, self.send.at[0], self.recv.at[got],
            device_id=device, device_id_type=MESH_ID,
        ).wait_recv()

    def copy(self, ends, name, wait_last=True):
        at = self.locals.setdefault(name, len(self.locals))

        def make():
            return pltpu.make_async_copy(*ends(), self.local.at[at])

        make().start()
        if wait_last:
            self.started.append(lambda: make().wait())
        return lambda: make().wait()

    def finish(self):
        for wait in self.started:
            wait()


class Neighbours:
    def __init__(self, inner):
        me = lax.axis_index("dp")
        at = me // inner
        self.core = lax.axis_index("tensor")
        self.z, self.y, self.x = at // 4, at // 2 % 2, at % 2
        self.spots = [(self.z + dz + 4) % 4 for dz in Z_FROM]
        self.along = [{"dp": me + (spot - self.z) * 4 * inner} for spot in self.spots]
        self.over_y = {"dp": me + (1 - 2 * self.y) * 2 * inner}
        self.over_x = {"dp": me + (1 - 2 * self.x) * inner}
        self.twin = {"tensor": 1 - self.core}
        self.blocks = {
            (k, other_y, other_x): self.spots[k] * 4
            + (1 - self.y if other_y else self.y) * 2
            + (1 - self.x if other_x else self.x)
            for k in range(SLOTS)
            for other_y in (0, 1)
            for other_x in (0, 1)
        }

    def greet(self):
        barrier = pltpu.get_barrier_semaphore()
        devices = [*self.along[1:], self.over_y, self.over_x, self.twin]
        for device in devices:
            pl.semaphore_signal(barrier, inc=1, device_id=device, device_id_type=MESH_ID)
        pl.semaphore_wait(barrier, len(devices))

    def block(self, k, other_y, other_x):
        return self.blocks[k, other_y, other_x]


BACK = (0, 2, 1, 3)


class Gather:
    def __init__(self, copies, near, shard, full, tag):
        self.copies, self.near, self.shard, self.full, self.tag = copies, near, shard, full, tag
        self.split = full.shape[2] // (2 * LANES) * LANES

    def source(self, k):
        return self.shard if k == 0 else self.full.at[self.near.block(k, 0, 0)]

    def begin(self):
        for k in range(1, SLOTS):
            self.copies.remote(
                lambda: (self.shard, self.full.at[self.near.block(0, 0, 0)]),
                (self.tag, "z", k), (self.tag, "z", BACK[k]), self.near.along[k],
            )
        self.full[self.near.block(0, 0, 0)] = self.shard[...]

    def spread(self, k):
        near, place = self.near, self.full.at[self.near.block(k, 0, 0)]
        if k > 0:
            self.copies.arrived(place, (self.tag, "z", k), near.along[k])
        for way, device in (("y", near.over_y), ("x", near.over_x)):
            name = (self.tag, way, k)
            self.copies.remote(
                lambda: (self.source(k), self.full.at[near.block(k, 0, 0)]), name, name, device
            )

    def cross(self, k):
        near = self.near
        from_y = self.full.at[near.block(k, 1, 0)]
        from_x = self.full.at[near.block(k, 0, 1)]
        self.copies.arrived(from_y, (self.tag, "y", k), near.over_y)
        self.copies.remote(
            lambda: (self.full.at[near.block(k, 1, 0), :, : self.split],) * 2,
            (self.tag, "one", k), (self.tag, "one", k), near.over_x,
        )
        self.copies.arrived(from_x, (self.tag, "x", k), near.over_x)
        self.copies.remote(
            lambda: (self.full.at[near.block(k, 0, 1), :, self.split :],) * 2,
            (self.tag, "two", k), (self.tag, "two", k), near.over_y,
        )

    def end(self):
        near = self.near
        for k in range(SLOTS):
            place = self.full.at[near.block(k, 1, 1)]
            self.copies.arrived(place.at[:, : self.split], (self.tag, "one", k), near.over_x)
            self.copies.arrived(place.at[:, self.split :], (self.tag, "two", k), near.over_y)


def roll_left(slab, lanes):
    return pltpu.roll(slab, LANES - lanes, 1)


def forward_kernel(
    inner, q_shard, o_shard, gateup_hbm, down_hbm, hidden_hbm, og_hbm, cos, sin, seg_col, seg_row,
    routes,
    q_full, o_full, small, normed, q_ref, k_ref, v_ref, attended, lse_ref, combine, combine_pair,
    middle_hbm, x_hbm, xt_hbm, og_pair, ogt_hbm, pairs_hbm, near_hbm, far_hbm,
    hidden, gateup, down, given, pairs, bias, k_low, k_high, v_low, v_high, part, part_got, x_own,
    middle, stage, turned, columns_out, columns_got, send, recv, local,
):
    near = Neighbours(inner)
    copies = Copies(send, recv, local)
    tokens, width = hidden.shape
    block = width // 16
    chunks = pairs.shape[0]
    hid = down.shape[1]
    q_width = q_ref.shape[1]
    kv_slabs = k_ref.shape[1] // LANES
    slabs = q_width // LANES
    qkv_width = q_width + 2 * k_ref.shape[1]
    experts = down.shape[0]
    each = 2 + experts
    half = tokens // 2
    tiles = tokens // ROWS
    x, core = near.x, near.core
    own_half = pl.ds(pl.multiple_of(core * half, half), half)
    mine = pl.ds(pl.multiple_of(tokens + core * half, half), half)
    theirs = pl.ds(pl.multiple_of(tokens + (1 - core) * half, half), half)

    near.greet()
    gather_q = Gather(copies, near, q_shard, q_full, "q")
    gather_o = Gather(copies, near, o_shard, o_full, "o")
    gather_q.begin()
    gather_q.spread(0)
    weights_in = [
        copies.copy(lambda: (gateup_hbm, gateup), "gateup", False),
        copies.copy(lambda: (down_hbm, down), "down", False),
    ]
    hidden_in = copies.copy(lambda: (hidden_hbm, hidden), "hidden", False)
    copies.copy(lambda: (og_hbm, og_pair.at[pl.ds(0, tokens)]), "og")

    def pack(c, mine):
        first = 2 * (chunks * (x if mine else 1 - x) + c)
        rows = pl.ds(pl.multiple_of(x * block, block), block)
        for e in range(CHUNK):
            for part_at in range(2):
                at = hid * (2 * e + part_at)
                value = gateup[first + e, part_at].astype(BF16)
                if mine:
                    pairs[c, rows, at : at + hid] = value
                else:
                    given[c, :, at : at + hid] = value
            at = hid * (2 * CHUNK + e)
            value = down[first + e].astype(F32).T.astype(BF16)
            if mine:
                pairs[c, rows, at : at + hid] = value
            else:
                given[c, :, at : at + hid] = value

    def swap(c):
        rows = pl.ds(pl.multiple_of(x * block, block), block)
        copies.remote(
            lambda: (given.at[c], pairs.at[c, rows]), ("s", c), ("s", c), near.over_x
        )

    def swapped(c):
        rows = pl.ds(pl.multiple_of((1 - x) * block, block), block)
        copies.arrived(pairs.at[c, rows], ("s", c), near.over_x)

    def ring_one(c):
        copies.remote(
            lambda: (pairs.at[c], near_hbm.at[c, 0]), ("up", c), ("r", c, 1), near.along[2]
        )
        copies.remote(
            lambda: (pairs.at[c], near_hbm.at[c, 1]), ("down", c), ("r", c, 2), near.along[1]
        )

    def ring_two(c):
        copies.arrived(near_hbm.at[c, 0], ("r", c, 1), near.along[1])
        copies.remote(
            lambda: (near_hbm.at[c, 0], near_hbm.at[c, 2]), ("two", c), ("r", c, 3), near.along[2]
        )

    def over_y(c, k):
        copies.remote(
            lambda: (pairs.at[c] if k == 0 else near_hbm.at[c, k - 1], far_hbm.at[c, k]),
            ("f", c, k), ("f", c, k), near.over_y,
        )

    def ring_got(c, k):
        copies.arrived(near_hbm.at[c, k - 1], ("r", c, k), near.along[k])

    def turn_tile(source, target, name, side):
        copies.copy(lambda: (source, stage.at[side]), (name, "in"), False)()
        turned[side] = stage[side].T
        return copies.copy(lambda: (turned.at[side], target), (name, "out"), False)

    waits = [None, None]

    def turn_next(source, target, name, side):
        if waits[side] is not None:
            waits[side]()
        waits[side] = turn_tile(source, target, name, side)

    for wait in weights_in:
        wait()
    pack(0, False)
    swap(0)
    pack(0, True)
    gather_q.spread(1)
    gather_q.spread(2)
    pack(1, False)
    pack(1, True)
    gather_q.cross(0)
    gather_q.spread(3)
    gather_o.begin()
    pack(2, False)
    pack(2, True)
    gather_q.cross(1)
    gather_q.cross(2)
    swapped(0)
    ring_one(0)
    over_y(0, 0)
    pack(3, False)
    pack(3, True)
    fill_bias(bias, seg_col, seg_row)
    gather_q.cross(3)
    gather_o.spread(0)
    for c in range(1, chunks):
        swap(c)
    for tile in range(tiles):
        rows = pl.ds(tile * ROWS, ROWS)
        turn_next(og_hbm.at[rows], ogt_hbm.at[:, rows], ("og", tile), tile % 2)
    hidden_in()
    gather_q.end()
    pieces = q_full[:, :, qkv_width:].reshape(width, LANES)
    wide = pieces.astype(F32)
    summed = wide + roll_left(wide, each) + roll_left(wide, 2 * each)
    small[...] = summed.T[: small.shape[0], :]

    def project(tile, carry):
        rows = pl.ds(pl.multiple_of(tile * ROWS, ROWS), ROWS)
        value = hidden[rows, :].astype(F32)
        inverse = lax.rsqrt(jnp.mean(value * value, axis=1, keepdims=True) + NORM_EPSILON)
        low = (value * inverse * small[0:1, :]).astype(BF16)
        normed[rows, :] = low
        cosine, sine = cos[rows, :], sin[rows, :]
        for g in range(slabs + 2 * kv_slabs):
            lanes = slice(g * LANES, (g + 1) * LANES)
            if g % 2 == 0:
                two = slice(g * LANES, (g + 2) * LANES)
                lin_two = dot(low, q_full[:, :, two].reshape(width, 2 * LANES))
            lin = lin_two[:, (g % 2) * LANES : (g % 2 + 1) * LANES]
            if g < slabs + kv_slabs:
                lin = lin * cosine + rotate_halves(lin) * sine
            if g < slabs:
                q_ref[rows, lanes] = lin.astype(BF16)
            elif g < slabs + kv_slabs:
                at = (g - slabs) * LANES
                k_ref[rows, at : at + LANES] = lin.astype(BF16)
            else:
                at = (g - slabs - kv_slabs) * LANES
                v_ref[rows, at : at + LANES] = lin.astype(BF16)

        @pl.when(tile == 0)
        def _():
            gather_o.spread(1)
            gather_o.spread(2)

        @pl.when(tile == 2)
        def _():
            gather_o.spread(3)
            gather_o.cross(0)

        return carry

    lax.fori_loop(0, tiles, project, 0)
    for j in range(kv_slabs):
        lanes = slice(j * LANES, (j + 1) * LANES)
        spread_heads(k_ref[:, lanes], k_low, k_high, 2 * j)
        spread_heads(v_ref[:, lanes], v_low, v_high, 2 * j)

    def attend(g, carry):
        lanes = pl.ds(pl.multiple_of(g * LANES, LANES), LANES)
        kv_even, kv_odd = (2 * g) // 3, (2 * g + 1) // 3
        for at in range(0, tokens, ROWS):
            rows = slice(at, at + ROWS)
            upto = at + ROWS
            queries = q_ref[rows, lanes]
            total = None
            stats = []
            for keys, values, kv_at in ((k_low, v_low, kv_even), (k_high, v_high, kv_odd)):
                scores = dot(queries, keys[kv_at, :upto, :], NT) * SCORE_SCALE + bias[rows, :upto]
                highest = jnp.max(scores, axis=1, keepdims=True)
                weights = jnp.exp(scores - highest)
                whole = jnp.sum(weights, axis=1, keepdims=True)
                probability = (weights * (1.0 / whole)).astype(BF16)
                one = dot(probability, values[kv_at, :upto, :])
                total = one if total is None else total + one
                stats.append(highest + jnp.log(whole))
            attended[rows, lanes] = total.astype(BF16)
            across = jnp.where(half_mask(ROWS, False), stats[0], stats[1]).T
            lse_ref[g, 0:1, rows] = across[0:1, :]
            lse_ref[g, 1:2, rows] = across[HEAD_DIM : HEAD_DIM + 1, :]

        @pl.when(g == 0)
        def _():
            gather_o.cross(1)
            gather_o.cross(2)
            ring_two(0)
            over_y(0, 1)
            swapped(1)
            ring_one(1)
            over_y(1, 0)

        @pl.when(g == 1)
        def _():
            gather_o.cross(3)
            ring_got(0, 2)
            over_y(0, 2)
            copies.remote(
                lambda: (og_hbm.at[own_half], og_pair.at[mine]), ("og",), ("og",), near.over_x
            )

        @pl.when(g == 3)
        def _():
            ring_got(0, 3)
            over_y(0, 3)
            swapped(2)
            ring_one(2)

        @pl.when(g == 4)
        def _():
            ring_two(1)
            over_y(1, 1)
            ring_got(1, 2)
            over_y(1, 2)
            gather_o.end()

        return carry

    lax.fori_loop(0, slabs, attend, 0)

    def project_out(step, carry):
        tile = (step + 2 * (1 - core)) % tiles
        rows = pl.ds(pl.multiple_of(tile * ROWS, ROWS), ROWS)
        low = attended[rows, :]
        for group in range(SLOTS):
            cols = slice(4 * block * group, 4 * block * (group + 1))
            weight = o_full[4 * group : 4 * (group + 1)].reshape(4 * block, q_width)
            part[rows, cols] = dot(low, weight, NT).astype(BF16)
        return carry

    for step in range(tiles):
        project_out(step, 0)
        tile = (step + 2 * (1 - core)) % tiles
        rows = pl.ds(pl.multiple_of(tile * ROWS, ROWS), ROWS)
        copies.remote(
            lambda rows=rows: (part.at[rows], part_got.at[rows]),
            ("p", step), ("p", step), near.twin,
        )
    router = q_full[:, :, qkv_width:].reshape(width, LANES)
    for step in range(tiles):
        tile = (step + 2 * core) % tiles
        rows = pl.ds(pl.multiple_of(tile * ROWS, ROWS), ROWS)
        copies.arrived(part_got.at[rows], ("p", step), near.twin)
        side = step % 2
        if step >= 2:
            middle_out[side]()
        elif step == 0:
            middle_out = [None, None]
        total = hidden[rows, :].astype(F32) + RESIDUAL_SCALE * (
            part[rows, :].astype(F32) + part_got[rows, :].astype(F32)
        )
        middle[side] = total
        middle_out[side] = copies.copy(
            lambda rows=rows, side=side: (middle.at[side], middle_hbm.at[rows]), ("m", step), False
        )
        inverse = lax.rsqrt(jnp.mean(total * total, axis=1, keepdims=True) + NORM_EPSILON)
        value = total * inverse * small[1:2, :]
        high = value.astype(BF16)
        x_own[rows, :] = high
        copies.copy(lambda rows=rows: (x_own.at[rows], x_hbm.at[rows]), ("x", step))
        if step < 2:
            there = pl.ds(pl.multiple_of(tokens + tile * ROWS, ROWS), ROWS)
            copies.remote(
                lambda rows=rows, there=there: (x_own.at[rows], x_hbm.at[there]),
                ("x", step), ("x", step), near.over_x,
            )
        rest = value - high.astype(F32)
        mid = rest.astype(BF16)
        low = (rest - mid.astype(F32)).astype(BF16)
        one, two, three = dot(high, router), dot(mid, router), dot(low, router)
        logits = one + roll_left(one, each) + roll_left(one, 2 * each) + two + roll_left(two, each)
        logits = roll_left(logits + three, 2)
        lane = lax.broadcasted_iota(jnp.int32, (ROWS, LANES), 1)
        chosen = lane < 0
        route = routes[rows, :]
        for k in range(routes.shape[1]):
            chosen = chosen | (route[:, k : k + 1] == lane)
        logits = jnp.where(chosen, logits, MASK_VALUE)
        powers = jnp.exp(logits - jnp.max(logits, axis=1, keepdims=True))
        powers = jnp.where(chosen, powers, 0.0)
        combine[rows, :] = powers * (1.0 / jnp.sum(powers, axis=1, keepdims=True))
        if step == 0:
            swapped(3)
            copies.copy(lambda: (pairs, pairs_hbm), "pairs")
        if step == 1:
            ring_got(1, 3)
            over_y(1, 3)
        if step == 2:
            ring_two(2)

    shares = experts // 2
    flipped = combine[...].T
    kept = jnp.where(x == 0, flipped[:shares, :], flipped[shares : 2 * shares, :])
    gone = jnp.where(x == 0, flipped[shares : 2 * shares, :], flipped[:shares, :])
    columns_out[...] = gone
    copies.remote(lambda: (columns_out, columns_got), ("c",), ("c",), near.over_x)
    combine_pair[:tokens, :] = kept.T

    copies.arrived(og_pair.at[mine], ("og",), near.over_x)
    copies.remote(lambda: (og_pair.at[mine],) * 2, ("og2",), ("og2",), near.twin)
    for tile in range(tiles):
        rows = pl.ds(tile * ROWS, ROWS)
        if waits[tile % 2] is not None:
            waits[tile % 2]()
        turned[tile % 2] = x_own[rows, :].T
        waits[tile % 2] = copies.copy(
            lambda rows=rows, side=tile % 2: (turned.at[side], xt_hbm.at[:, rows]),
            ("xt", tile), False,
        )
    for step in range(2):
        tile = (step + 2 * core) % tiles
        rows = pl.ds(pl.multiple_of(tokens + tile * ROWS, ROWS), ROWS)
        turn_next(og_pair.at[rows], ogt_hbm.at[:, rows], ("og", tiles + step), step)
    copies.arrived(columns_got, ("c",), near.over_x)
    combine_pair[tokens:, :] = columns_got[...].T
    copies.arrived(og_pair.at[theirs], ("og2",), near.twin)
    for step in range(2):
        tile = (step + 2 * (1 - core)) % tiles
        rows = pl.ds(pl.multiple_of(tokens + tile * ROWS, ROWS), ROWS)
        turn_next(og_pair.at[rows], ogt_hbm.at[:, rows], ("og", tiles + 2 + step), step)
    for step in range(2):
        tile = (step + 2 * core) % tiles
        rows = pl.ds(pl.multiple_of(tokens + tile * ROWS, ROWS), ROWS)
        copies.arrived(x_hbm.at[rows], ("x", step), near.over_x)
        copies.remote(
            lambda rows=rows: (x_hbm.at[rows],) * 2, ("x2", step), ("x2", step), near.twin
        )
        turn_next(x_hbm.at[rows], xt_hbm.at[:, rows], ("xt", tiles + step), step)
    for step in range(2):
        tile = (step + 2 * (1 - core)) % tiles
        rows = pl.ds(pl.multiple_of(tokens + tile * ROWS, ROWS), ROWS)
        copies.arrived(x_hbm.at[rows], ("x2", step), near.twin)
        turn_next(x_hbm.at[rows], xt_hbm.at[:, rows], ("xt", tiles + 2 + step), step)
    for wait in waits + middle_out:
        wait()
    ring_got(2, 2)
    ring_got(2, 3)
    for c in range(LATE):
        for k in range(SLOTS):
            copies.arrived(far_hbm.at[c, k], ("f", c, k), near.over_y)
    copies.finish()


def forward_pass(q_shard, o_shard, gateup, down, hidden, og, cosine, sine, segments, routes):
    tokens, width = hidden.shape
    experts, hid = down.shape[:2]
    block, q_columns = q_shard.shape
    q_width = o_shard.shape[1]
    kv_width = (q_columns - LANES - q_width) // 2
    slabs, kv_heads = q_width // LANES, kv_width // HEAD_DIM
    chunks = experts // (2 * CHUNK)
    columns = 3 * CHUNK * hid
    anywhere, vmem = pl.BlockSpec(memory_space=pl.ANY), vmem_spec()
    shape = jax.ShapeDtypeStruct
    inner = lax.axis_size("dp") // 16
    dma = pltpu.SemaphoreType.DMA
    return pl.pallas_call(
        functools.partial(forward_kernel, inner),
        in_specs=[vmem, vmem] + [anywhere] * 4 + [vmem] * 5,
        out_specs=[vmem] * 11 + [anywhere] * 8,
        out_shape=[
            shape((16, block, q_columns), BF16),
            shape((16, block, q_width), BF16),
            shape((24, width), F32),
            shape((tokens, width), BF16),
            shape((tokens, q_width), BF16),
            shape((tokens, kv_width), BF16),
            shape((tokens, kv_width), BF16),
            shape((tokens, q_width), BF16),
            shape((slabs, 8, tokens), F32),
            shape((tokens, LANES), F32),
            shape((2 * tokens, experts // 2), F32),
            shape((tokens, width), F32),
            shape((2 * tokens, width), BF16),
            shape((width, 2 * tokens), BF16),
            shape((2 * tokens, width), BF16),
            shape((width, 2 * tokens), BF16),
            shape((chunks, 2 * block, columns), BF16),
            shape((chunks - 1, SLOTS - 1, 2 * block, columns), BF16),
            shape((LATE, SLOTS, 2 * block, columns), BF16),
        ],
        scratch_shapes=[
            pltpu.VMEM((tokens, width), BF16),
            pltpu.VMEM(gateup.shape, gateup.dtype),
            pltpu.VMEM(down.shape, down.dtype),
            pltpu.VMEM((chunks, block, columns), BF16),
            pltpu.VMEM((chunks, 2 * block, columns), BF16),
            pltpu.VMEM((tokens, tokens), F32),
        ]
        + [pltpu.VMEM((kv_heads, tokens, LANES), BF16)] * 4
        + [pltpu.VMEM((tokens, width), BF16)] * 3
        + [
            pltpu.VMEM((2, ROWS, width), F32),
            pltpu.VMEM((2, ROWS, width), BF16),
            pltpu.VMEM((2, width, ROWS), BF16),
            pltpu.VMEM((experts // 2, tokens), F32),
            pltpu.VMEM((experts // 2, tokens), F32),
            dma((80,)), dma((80,)), dma((60,)),
        ],
        compiler_params=pltpu.CompilerParams(
            vmem_limit_bytes=EXPERT_VMEM, collective_id=1, has_side_effects=True
        ),
        name="forward_pass",
    )(
        q_shard, o_shard, gateup, down, hidden, og, cosine, sine,
        segments[:, None], segments[None, :], routes,
    )


def whole_call(kernel, values, outs, earlier=(), name=None):
    return pl.pallas_call(
        with_earlier(kernel, len(values), len(earlier)),
        in_specs=[vmem_spec()] * len(values) + any_specs(earlier),
        out_specs=[vmem_spec()] * len(outs),
        out_shape=[jax.ShapeDtypeStruct(shape, dtype) for shape, dtype in outs],
        compiler_params=pltpu.CompilerParams(vmem_limit_bytes=VMEM_BYTES),
        name=name,
    )(*values, *earlier)


def fence_kernel(*refs):
    count = len(refs) // 2
    for value, out in zip(refs[:count], refs[count:]):
        out[...] = value[...]


def fence_all(values, *earlier):
    return whole_call(fence_kernel, values, [(v.shape, v.dtype) for v in values], earlier, "fence")


def fence(value, *earlier):
    return fence_all([value], *earlier)[0]


def sum_y_kernel(near, got, *outs):
    for k, out in enumerate(outs):
        out[...] = (near[k].astype(F32) + got[k].astype(F32)).astype(BF16)


def sum_y(near, got, *earlier):
    outs = [(near.shape[1:], BF16)] * SLOTS
    return whole_call(sum_y_kernel, [near, got], outs, earlier, "sum_y")


def sum_z_kernel(x_at, *refs):
    kept, given = refs[-2:]
    half = kept.shape[1]
    for c in range(kept.shape[0]):
        parts = refs[SLOTS * c : SLOTS * (c + 1)]
        for rows, out in ((x_at[0], kept), (1 - x_at[0], given)):
            rows = pl.ds(pl.multiple_of(rows * half, half), half)
            total = parts[0][rows, :].astype(F32)
            for part in parts[1:]:
                total = total + part[rows, :].astype(F32)
            out[c] = total.astype(out.dtype)


def sum_z(x_at, chunks, *earlier):
    count = len(chunks)
    pair, columns = chunks[0][0].shape
    flat = [part for parts in chunks for part in parts]
    return pl.pallas_call(
        with_earlier(sum_z_kernel, 1 + len(flat), len(earlier)),
        in_specs=[smem_spec()] + [vmem_spec()] * len(flat) + any_specs(earlier),
        out_specs=[vmem_spec()] * 2,
        out_shape=[
            jax.ShapeDtypeStruct((count, pair // 2, columns), F32),
            jax.ShapeDtypeStruct((count, pair // 2, columns), BF16),
        ],
        compiler_params=pltpu.CompilerParams(vmem_limit_bytes=VMEM_BYTES),
        name="sum_z",
    )(x_at, *flat, *earlier)


def sum_parts_kernel(parts, out):
    total = parts[0].astype(F32)
    for c in range(1, parts.shape[0]):
        total = total + parts[c].astype(F32)
    out[...] = total.astype(BF16)


def sum_parts(parts, *earlier):
    chunks, tokens, width = parts.shape
    return pl.pallas_call(
        with_earlier(sum_parts_kernel, 1, len(earlier)),
        grid=(tokens // EXPERT_ROWS,),
        in_specs=[pl.BlockSpec((chunks, EXPERT_ROWS, width), lambda s: (0, s, 0))]
        + any_specs(earlier),
        out_specs=pl.BlockSpec((EXPERT_ROWS, width), lambda s: (s, 0)),
        out_shape=jax.ShapeDtypeStruct((tokens, width), BF16),
        compiler_params=pltpu.CompilerParams(vmem_limit_bytes=VMEM_BYTES),
        name="sum_parts",
    )(parts, *earlier)


def adam_experts_kernel(x_at, kept, got, *refs):
    states, outs = refs[:6], refs[6:]
    own = kept.shape[1]
    hidden = states[0].shape[3]
    mine = pl.program_id(0) // (pl.num_programs(0) // 2) == x_at[0]
    grad = jnp.where(mine, kept[0], got[0].astype(F32))
    for e in range(CHUNK):
        for part in range(2):
            first = hidden * (2 * e + part)
            results = adam_update(
                states[0][e, part], grad[:, first : first + hidden],
                states[1][e, part], states[2][e, part], MODEL_DIM ** (-0.5), WEIGHT_DECAY,
            )
            for out, result in zip(outs[:3], results):
                out[e, part] = result
        first = hidden * (2 * CHUNK + e)
        turned = grad[:, first : first + hidden].T
        results = adam_update(
            states[3][e], turned, states[4][e], states[5][e],
            max(1, F // 256) ** (-0.5), WEIGHT_DECAY,
        )
        for out, result in zip(outs[3:], results):
            out[e] = result


def adam_experts(x_at, kept, got, gateup, down):
    chunks, own, columns = kept.shape
    experts, hidden = down[0].shape[:2]
    share = pl.BlockSpec((1, own, columns), lambda j: (j % chunks, 0, 0))
    big = pl.BlockSpec((CHUNK, 2, own, hidden), lambda j: (j, 0, 0, 0))
    small = pl.BlockSpec((CHUNK, hidden, own), lambda j: (j, 0, 0))
    return pl.pallas_call(
        adam_experts_kernel,
        grid=(experts // CHUNK,),
        in_specs=[smem_spec(), share, share] + [big] * 3 + [small] * 3,
        out_specs=[big] * 3 + [small] * 3,
        out_shape=[jax.ShapeDtypeStruct(gateup[0].shape, F32)] * 3
        + [jax.ShapeDtypeStruct(down[0].shape, F32)] * 3,
        compiler_params=pltpu.CompilerParams(vmem_limit_bytes=VMEM_BYTES),
        name="adam_experts",
    )(x_at, kept, got, *gateup, *down)


def join_tokens_kernel(own, first, second, out, turned):
    half = own.shape[0] // 2
    for at, part in ((0, own[:half, :]), (half, own[half:, :]), (2 * half, first[...]), (3 * half, second[...])):
        out[at : at + half, :] = part
        turned[:, at : at + half] = part.T


def join_tokens(own, first, second, *earlier):
    tokens, width = own.shape
    return pl.pallas_call(
        with_earlier(join_tokens_kernel, 3, len(earlier)),
        in_specs=[vmem_spec()] * 3 + any_specs(earlier),
        out_specs=[vmem_spec()] * 2,
        out_shape=[
            jax.ShapeDtypeStruct((2 * tokens, width), own.dtype),
            jax.ShapeDtypeStruct((width, 2 * tokens), own.dtype),
        ],
        compiler_params=pltpu.CompilerParams(vmem_limit_bytes=VMEM_BYTES),
        name="join_tokens",
    )(own, first, second, *earlier)


def move(array, dz=0, dy=0, dx=0):
    total = lax.axis_size("dp")
    inner = total // 16
    pairs = []
    for at in range(16):
        z, y, x = at // 4, at // 2 % 2, at % 2
        to = ((z + dz) % 4) * 4 + (y ^ dy) * 2 + (x ^ dx)
        pairs += [(at * inner + i, to * inner + i) for i in range(inner)]
    return lax.ppermute(array, "dp", pairs)


def place():
    at = lax.axis_index("dp") // (lax.axis_size("dp") // 16)
    return at // 4, at // 2 % 2, at % 2


def inner_groups(total):
    inner = total // 16
    return [[at * inner + i for i in range(inner)] for at in range(16)]


def inner_gather(shard, axis):
    total = lax.axis_size("dp")
    if total == 16:
        return shard
    return lax.all_gather(
        shard, "dp", axis=axis, tiled=True, axis_index_groups=inner_groups(total)
    )


def inner_scatter(share, axis):
    total = lax.axis_size("dp")
    if total == 16:
        return share
    return lax.psum_scatter(
        share, "dp", scatter_dimension=axis, tiled=True, axis_index_groups=inner_groups(total)
    )


def block_rows(parts, rows):
    z, y, x = place()
    starts = []
    for dz, dy, dx in parts:
        starts.append((((z + dz + 4) % 4) * 4 + (y ^ dy) * 2 + (x ^ dx)) * rows)
    return jnp.stack(starts).astype(jnp.int32)


def gather_z(shard):
    return jnp.stack([shard] + [move(shard, dz=-dz) for dz in Z_FROM[1:]])


def gather_ring(shard):
    below, above = move(shard, dz=1), move(shard, dz=-1)
    return [shard, below, above, move(below, dz=1)]


def send_z(parts):
    return [move(parts[k].astype(BF16), dz=Z_FROM[k]) for k in range(1, SLOTS)]


def scatter_z(parts, moved=None):
    result = parts[0]
    for one in moved or send_z(parts):
        result = result + one.astype(F32)
    return result


def gather_plane(own):
    half = own.shape[-1] // 2
    along_y, along_x = move(own, dy=1), move(own, dx=1)
    both = (move(along_y[..., :half], dx=1), move(along_x[..., half:], dy=1))
    return own, along_y, along_x, *both


def scatter_plane(pieces):
    own, along_y, along_x, both_one, both_two = pieces
    half = both_one.shape[-1]
    got_one, got_two = move(both_one, dx=1), move(both_two, dy=1)
    pass_y = jnp.concatenate(
        [(along_y[..., :half].astype(F32) + got_one.astype(F32)).astype(BF16), along_y[..., half:]],
        axis=-1,
    )
    pass_x = jnp.concatenate(
        [along_x[..., :half], (along_x[..., half:].astype(F32) + got_two.astype(F32)).astype(BF16)],
        axis=-1,
    )
    got_y, got_x = move(pass_y, dy=1), move(pass_x, dx=1)
    return scatter_z(
        [
            own[k].astype(F32) + got_y[k].astype(F32) + got_x[k].astype(F32)
            for k in range(SLOTS)
        ]
    )


PLANE = [(dz, dy, dx) for dy, dx in ((0, 0), (1, 0), (0, 1), (1, 1)) for dz in Z_FROM]


def join_kernel(rows_at, *refs):
    pieces, out = refs[:-1], refs[-1]
    slots, own, width = pieces[0].shape
    half = width // 2
    for at in range(4 * slots):
        rows = pl.ds(pl.multiple_of(rows_at[at], own), own)
        group, slot = at // slots, at % slots
        if group < 3:
            out[rows, :] = pieces[group][slot]
        else:
            out[rows, :half] = pieces[3][slot]
            out[rows, half:] = pieces[4][slot]


def part_kernel(rows_at, whole, *pieces):
    slots, own, width = pieces[0].shape
    half = width // 2
    for at in range(4 * slots):
        rows = pl.ds(pl.multiple_of(rows_at[at], own), own)
        group, slot = at // slots, at % slots
        if group < 3:
            pieces[group][slot] = whole[rows, :]
        else:
            pieces[3][slot] = whole[rows, :half]
            pieces[4][slot] = whole[rows, half:]


def smem_spec():
    return pl.BlockSpec(memory_space=pltpu.SMEM)


def vmem_spec():
    return pl.BlockSpec(memory_space=pltpu.VMEM)


def join_blocks(rows_at, pieces, earlier=()):
    slots, own, width = pieces[0].shape
    return pl.pallas_call(
        with_earlier(join_kernel, 6, len(earlier)),
        in_specs=[smem_spec()] + [vmem_spec()] * 5 + any_specs(earlier),
        out_specs=vmem_spec(),
        out_shape=jax.ShapeDtypeStruct((4 * slots * own, width), BF16),
        compiler_params=pltpu.CompilerParams(vmem_limit_bytes=VMEM_BYTES),
        name="join_blocks",
    )(rows_at, *pieces, *earlier)


def part_blocks(rows_at, whole, earlier=()):
    own, width = whole.shape[0] // (4 * SLOTS), whole.shape[1]
    full = jax.ShapeDtypeStruct((SLOTS, own, width), BF16)
    half = jax.ShapeDtypeStruct((SLOTS, own, width // 2), BF16)
    return pl.pallas_call(
        with_earlier(part_kernel, 2, len(earlier)),
        in_specs=[smem_spec(), vmem_spec()] + any_specs(earlier),
        out_specs=[vmem_spec()] * 5,
        out_shape=[full] * 3 + [half] * 2,
        compiler_params=pltpu.CompilerParams(vmem_limit_bytes=VMEM_BYTES),
        name="part_blocks",
    )(rows_at, whole, *earlier)


def after(value, *earlier):
    marks = []
    for one in earlier:
        slots = one.shape[0] if one.shape[0] == SLOTS else 1
        lead, rest = (slots > 1) * 1, one.ndim - 1
        marks.append(lax.slice(one, (lead,) + (0,) * rest, (slots,) + (1,) * rest))
    return lax.optimization_barrier((value, *marks))[0]


def split_three(values):
    high = values.astype(BF16)
    rest = values - high.astype(F32)
    middle = rest.astype(BF16)
    low = (rest - middle.astype(F32)).astype(BF16)
    return [high, middle, low]


def swap_cores(part):
    return lax.ppermute(part, "tensor", [(0, 1), (1, 0)])


def pair_sum(part):
    return part.astype(F32) + swap_cores(part).astype(F32)


def norm_backward(values, inverse, gain_row, upstream):
    scaled = values * inverse
    weighted = upstream * gain_row
    mean_term = jnp.mean(weighted * scaled, axis=-1, keepdims=True)
    return (inverse * (weighted - scaled * mean_term), jnp.sum(upstream * scaled, axis=0))


def adam_update(value, gradient, mean_old, square_old, rate, decay):
    mean_new = FIRST_DECAY * mean_old + (1.0 - FIRST_DECAY) * gradient
    square_new = SECOND_DECAY * square_old + (1.0 - SECOND_DECAY) * gradient * gradient
    mean_hat = mean_new / (1.0 - FIRST_DECAY**STEP)
    square_hat = square_new / (1.0 - SECOND_DECAY**STEP)
    updated = value - rate * (mean_hat / (jnp.sqrt(square_hat) + ADAM_EPSILON) + decay * value)
    return (mean_new, square_new, updated)


def shards(
    hidden_in,
    out_grad,
    routes,
    segments,
    norm_gains,
    gains_mean,
    gains_square,
    w_query,
    query_mean,
    query_square,
    key_value_weight,
    key_value_first_moment,
    key_value_second_moment,
    w_out,
    out_mean,
    out_square,
    w_router,
    router_mean,
    router_square,
    w_gateup,
    gateup_mean,
    gateup_square,
    w_down,
    down_mean,
    down_square,
):
    tokens, width = hidden_in.shape
    own = w_query.shape[0]
    experts, hidden = w_down.shape[0], w_down.shape[1]
    q_width, kv_width = w_query.shape[1], key_value_weight.shape[2]
    qkv_width = q_width + 2 * kv_width
    each = 2 + experts
    half_experts = experts // 2
    block = width // 16
    z_at, y_at, x_at = place()
    core = lax.axis_index("tensor")
    plane_rows = block_rows(PLANE, block)
    qkv_shard = jnp.concatenate(
        [w_query.astype(BF16), key_value_weight[0].astype(BF16), key_value_weight[1].astype(BF16)]
        + split_three(jnp.concatenate([norm_gains.T, w_router], axis=1))
        + [jnp.zeros((own, LANES - 3 * each), BF16)],
        axis=1,
    )
    out_shard = w_out.T.astype(BF16)
    gateup_rows, down_rows = w_gateup, w_down
    if lax.axis_size("dp") > 16:
        gateup_rows = inner_gather(w_gateup.astype(BF16), 2)
        down_rows = inner_gather(w_down.astype(BF16), 2)
    chunks = experts // (2 * CHUNK)
    first = x_at == 0
    cosine, sine = rope_tables(seq_positions(segments))
    (
        qkv_blocks, out_blocks, small, normed_low, queries, keys, values, attended, lse,
        combine, combine_pair, middle, x_pair, x_turned, og_pair, og_turned, pairs, near, far,
    ) = forward_pass(
        inner_gather(qkv_shard, 0), inner_gather(out_shard, 0), gateup_rows, down_rows,
        hidden_in, out_grad, cosine, sine, segments, routes,
    )
    qkv_full = qkv_blocks.reshape(width, qkv_blocks.shape[2])[:, :qkv_width]
    output_full = out_blocks.reshape(width, q_width)
    gains_full, router_full = small[:2], small[2 : 2 + experts].T
    combine = combine[:, :experts]
    inputs = hidden_in.astype(F32)
    inverse_one = lax.rsqrt(jnp.mean(inputs * inputs, axis=-1, keepdims=True) + NORM_EPSILON)
    inverse_two = lax.rsqrt(jnp.mean(middle * middle, axis=-1, keepdims=True) + NORM_EPSILON)
    normed_two = middle * inverse_two * gains_full[1]

    def half_of(array, other=False):
        half = array.shape[0] // 2
        return lax.dynamic_slice_in_dim(array, half * ((1 - core) if other else core), half)

    def both_halves(mine):
        other = swap_cores(mine)
        lower = core == 0
        return jnp.where(lower, mine, other), jnp.where(lower, other, mine)

    mix_parts, dx_parts, gate_parts, z_parts, near_grads, far_grads, z_first = experts_pass(
        x_pair, og_pair, x_turned, og_turned, combine_pair, pairs, near, far
    )
    gate_pair = jnp.concatenate([gate_parts[c] for c in range(chunks)], axis=1)

    def to_neighbour(part):
        both = half_of(part).astype(F32) + swap_cores(half_of(part, other=True)).astype(F32)
        return jnp.concatenate(both_halves(move(both.astype(BF16), dx=1)))

    gate_got = move(gate_pair[tokens:], dx=1)
    gate_grad = pair_sum(
        jnp.concatenate(
            [
                jnp.where(first, gate_pair[:tokens], gate_got),
                jnp.where(first, gate_got, gate_pair[:tokens]),
            ],
            axis=1,
        )
    )
    z_got = [z_first]
    got_y = [move(far_grads[0], dy=1)]
    dx_pair = sum_parts(dx_parts)
    normed_two_part = pair_sum(dx_pair[:tokens]) + to_neighbour(dx_pair[tokens:]).astype(F32)
    z_got.append(send_z(z_parts[1]))
    got_y.append(move(fence(far_grads[1], got_y[0]), dy=1))

    logit_grad = combine * (gate_grad - jnp.sum(combine * gate_grad, axis=-1, keepdims=True))
    router_grad = jnp.dot(normed_two.T, logit_grad, precision=HIGHEST_PRECISION)
    normed_two_grad = normed_two_part + jnp.dot(
        logit_grad, router_full.T, precision=HIGHEST_PRECISION
    )
    middle_part, gain_two_grad = norm_backward(middle, inverse_two, gains_full[1], normed_two_grad)
    middle_grad = out_grad.astype(F32) + middle_part
    attention_back = (RESIDUAL_SCALE * middle_grad).astype(BF16)
    attended_grad = jnp.dot(attention_back, output_full, preferred_element_type=F32).astype(BF16)
    output_weight_grad = lax.dot_general(attention_back, attended, TN, preferred_element_type=F32)
    output_share = scatter_plane(
        part_blocks(plane_rows, output_weight_grad.astype(BF16))
    )
    query_grad, keyval_grad = attention_backward(
        queries, keys, values, attended, attended_grad, cosine, sine, segments, lse,
        earlier=got_y[:1],
    )
    for c in range(chunks - SENT):
        waits = (query_grad, *z_got[-1])
        z_parts.append(sum_y(near_grads[c], got_y[c], *waits))
        z_got.append(send_z(z_parts[-1]))
    qkv_grad = jnp.concatenate([query_grad, keyval_grad], axis=1)
    qkv_weight_grad = lax.dot_general(normed_low, qkv_grad, TN, preferred_element_type=F32)
    qkv_parts = part_blocks(
        plane_rows,
        jnp.concatenate(
            [
                qkv_weight_grad.astype(BF16),
                gain_two_grad[:, None].astype(BF16),
                router_grad.astype(BF16),
                jnp.zeros((width, 2 * LANES - 1 - experts), BF16),
            ],
            axis=1,
        ),
    )
    qkv_share = scatter_plane(qkv_parts)
    normed_part = lax.dot_general(qkv_grad, qkv_full, NT, preferred_element_type=F32)
    normed_grad = pair_sum(normed_part.astype(BF16))
    scaled = inputs * inverse_one
    weighted = normed_grad * gains_full[0]
    mean_term = jnp.mean(weighted * scaled, axis=-1, keepdims=True)
    input_grad = middle_grad + inverse_one * (weighted - scaled * mean_term)

    mix_pair = sum_parts(mix_parts, qkv_parts[0])
    expert_mix = pair_sum(mix_pair[:tokens]) + to_neighbour(mix_pair[tokens:]).astype(F32)
    block_out = (middle + RESIDUAL_SCALE * expert_mix).astype(BF16)
    kept_shares, got_shares = [], []
    x_here = x_at.astype(jnp.int32)[None]
    for low in range(0, chunks, 2):
        kept_share, given_share = sum_z(
            x_here,
            [[z_parts[c][0], *z_got[c]] for c in range(low, low + 2)],
            query_grad,
        )
        kept_shares.append(kept_share)
        got_shares.append(move(given_share, dx=1))
    kept_share = inner_scatter(jnp.concatenate(kept_shares), 1)
    got_share = inner_scatter(jnp.concatenate(got_shares), 1)

    output_share = inner_scatter(output_share, 0).T
    qkv_share = inner_scatter(qkv_share, 0)
    query_share = qkv_share[:, :q_width]
    keyval_share = jnp.stack(
        [qkv_share[:, q_width : q_width + kv_width], qkv_share[:, q_width + kv_width : qkv_width]]
    )
    gain_one_part = jnp.sum(w_query.astype(BF16).astype(F32) * query_share, axis=1) + jnp.sum(
        key_value_weight.astype(BF16).astype(F32) * keyval_share, axis=(0, 2)
    )
    gain_one_share = pair_sum(gain_one_part[None, :]) / norm_gains[:1]
    gains_share = jnp.concatenate([gain_one_share, qkv_share[:, qkv_width][None, :]])
    router_share = qkv_share[:, qkv_width + 1 : qkv_width + 1 + experts]

    gains_result = adam_update(norm_gains, gains_share, gains_mean, gains_square, GAIN_RATE, 0.0)
    query_result = adam_update(
        w_query, query_share, query_mean, query_square, (MODEL_DIM // 12) ** (-0.5), WEIGHT_DECAY
    )
    keyval_result = adam_update(
        key_value_weight,
        keyval_share,
        key_value_first_moment,
        key_value_second_moment,
        (MODEL_DIM // 12) ** (-0.5),
        WEIGHT_DECAY,
    )
    out_result = adam_update(
        w_out,
        output_share,
        out_mean,
        out_square,
        max(1, QUERY_HEADS * HEAD_DIM // 96) ** (-0.5),
        WEIGHT_DECAY,
    )
    router_result = adam_update(
        w_router, router_share, router_mean, router_square, (4 * MODEL_DIM) ** (-0.5), WEIGHT_DECAY
    )
    expert_results = adam_experts(
        x_here, kept_share, got_share,
        (w_gateup, gateup_mean, gateup_square), (w_down, down_mean, down_square),
    )
    return (
        (block_out, input_grad)
        + gains_result
        + query_result
        + keyval_result
        + out_result
        + router_result
        + tuple(expert_results)
    )


def solution(mesh):
    tokens, gains = P("dp", None), P(None, "dp")
    query, keyval, out = P("dp", "tensor"), P(None, "dp", "tensor"), P("tensor", "dp")
    router, gateup, down = P("dp", None), P(None, None, "dp", "tensor"), P(None, "tensor", "dp")
    states = tuple(
        spec for one in (gains, query, keyval, out, router, gateup, down) for spec in (one,) * 3
    )
    return jax.shard_map(
        shards,
        mesh=mesh,
        in_specs=(tokens, tokens, tokens, P("dp")) + states,
        out_specs=(tokens, tokens) + states,
        check_vma=False,
    )
```

```python
import functools

import jax
import jax.numpy as jnp
from jax import lax
from jax.experimental import pallas as pl
from jax.experimental.pallas import tpu as pltpu
from jax.sharding import PartitionSpec as P

MODEL_DIM = 1536
QUERY_HEADS = 24
HEAD_DIM = 64
F = 512
SEQUENCE_LENGTH = 1024
STEP = 10

NORM_EPSILON = 1e-06
SCORE_SCALE = 0.015625
RESIDUAL_SCALE = 0.22
ROPE_BASE = 10000.0
FIRST_DECAY = 0.9
SECOND_DECAY = 0.95
ADAM_EPSILON = 1e-08
WEIGHT_DECAY = 0.1
GAIN_RATE = 0.6
MASK_VALUE = -1e30
HIGHEST_PRECISION = lax.Precision.HIGHEST

BF16 = jnp.bfloat16
F32 = jnp.float32
LANES = 128
ROWS = 256
VMEM_BYTES = 58 * 1024 * 1024

NN = (((1,), (0,)), ((), ()))
NT = (((1,), (1,)), ((), ()))
TN = (((0,), (0,)), ((), ()))


def dot(a, b, dims=NN):
    return lax.dot_general(a, b, dims, preferred_element_type=F32)


def seq_positions(segment_row):
    counter = jnp.arange(segment_row.shape[0], dtype=jnp.int32)
    earlier = jnp.concatenate([segment_row[:1] - 1, segment_row[:-1]])
    starts = lax.cummax(jnp.where(segment_row != earlier, counter, 0), axis=0)
    return counter - starts


def rope_tables(positions):
    half_width = HEAD_DIM // 2
    frequency = ROPE_BASE ** (-2.0 * jnp.arange(half_width, dtype=F32) / HEAD_DIM)
    angles = positions.astype(F32)[:, None] * frequency[None, :]
    cosine, sine = jnp.cos(angles), jnp.sin(angles)
    return (
        jnp.concatenate([cosine] * 4, axis=1),
        jnp.concatenate([-sine, sine] * 2, axis=1),
    )


def rotate_halves(slab):
    lane = lax.broadcasted_iota(jnp.int32, slab.shape, 1)
    ahead = pltpu.roll(slab, LANES - HEAD_DIM // 2, 1)
    behind = pltpu.roll(slab, HEAD_DIM // 2, 1)
    return jnp.where(lane % HEAD_DIM < HEAD_DIM // 2, ahead, behind)


def half_mask(rows, upper):
    lane = lax.broadcasted_iota(jnp.int32, (rows, LANES), 1)
    return (lane >= HEAD_DIM) if upper else (lane < HEAD_DIM)


def spread_heads(slab, lower_out, upper_out, index):
    rows = slab.shape[0]
    moved = pltpu.roll(slab.astype(F32), HEAD_DIM, 1).astype(BF16)
    zero = jnp.zeros_like(slab)
    low, high = half_mask(rows, False), half_mask(rows, True)
    lower_out[index] = jnp.where(low, slab, zero)
    upper_out[index] = jnp.where(high, moved, zero)
    lower_out[index + 1] = jnp.where(low, moved, zero)
    upper_out[index + 1] = jnp.where(high, slab, zero)


def fill_bias(bias, seg_col, seg_row):
    span = bias.shape[0]
    for at in range(0, span, ROWS):
        rows_at = at + lax.broadcasted_iota(jnp.int32, (ROWS, span), 0)
        cols_at = lax.broadcasted_iota(jnp.int32, (ROWS, span), 1)
        allowed = (rows_at >= cols_at) & (seg_col[at : at + ROWS, :] == seg_row[...])
        bias[at : at + ROWS, :] = jnp.where(allowed, 0.0, MASK_VALUE).astype(F32)


def with_earlier(kernel, inputs, count):
    def run(*refs):
        kernel(*refs[:inputs], *refs[inputs + count :])

    return run


def any_specs(arrays):
    return [pl.BlockSpec(memory_space=pl.ANY)] * len(arrays)


def attention_forward_kernel(
    lin_ref, kv_ref, cos_ref, sin_ref, seg_col, seg_row,
    out_ref, q_ref, k_ref, v_ref, lse_ref,
    bias, k_low, k_high, v_low, v_high,
):
    slab_at = pl.program_id(0)
    span = lin_ref.shape[0]
    kv_slabs = kv_ref.shape[1] // (2 * LANES)

    @pl.when(slab_at == 0)
    def _():
        fill_bias(bias, seg_col, seg_row)
        for j in range(kv_slabs):
            lanes = slice(j * LANES, (j + 1) * LANES)
            lin = kv_ref[:, lanes]
            keys = (lin * cos_ref[...] + rotate_halves(lin) * sin_ref[...]).astype(BF16)
            k_ref[:, lanes] = keys
            spread_heads(keys, k_low, k_high, 2 * j)
            lanes = slice((kv_slabs + j) * LANES, (kv_slabs + j + 1) * LANES)
            values = kv_ref[:, lanes].astype(BF16)
            v_ref[:, slice(j * LANES, (j + 1) * LANES)] = values
            spread_heads(values, v_low, v_high, 2 * j)

    lin = lin_ref[...]
    q_ref[...] = (lin * cos_ref[...] + rotate_halves(lin) * sin_ref[...]).astype(BF16)
    kv_even, kv_odd = (2 * slab_at) // 3, (2 * slab_at + 1) // 3
    for at in range(0, span, ROWS):
        rows = slice(at, at + ROWS)
        queries = q_ref[rows, :]
        total = None
        stats = []
        for keys, values, kv_at in ((k_low, v_low, kv_even), (k_high, v_high, kv_odd)):
            upto = at + ROWS
            scores = dot(queries, keys[kv_at, :upto, :], NT) * SCORE_SCALE + bias[rows, :upto]
            highest = jnp.max(scores, axis=1, keepdims=True)
            weights = jnp.exp(scores - highest)
            summed = jnp.sum(weights, axis=1, keepdims=True)
            probability = (weights * (1.0 / summed)).astype(BF16)
            part = dot(probability, values[kv_at, :upto, :])
            total = part if total is None else total + part
            stats.append(highest + jnp.log(summed))
        out_ref[rows, :] = total.astype(BF16)
        spread = jnp.where(half_mask(ROWS, False), stats[0], stats[1])
        turned = spread.T
        lse_ref[0, 0:1, rows] = turned[0:1, :]
        lse_ref[0, 1:2, rows] = turned[HEAD_DIM : HEAD_DIM + 1, :]


def attention_forward(qkv_lin, cosine, sine, segment_row, earlier=()):
    span = qkv_lin.shape[0]
    q_width = MODEL_DIM // 2
    kv_width = (qkv_lin.shape[1] - q_width) // 2
    slabs, kv_heads = q_width // LANES, kv_width // HEAD_DIM
    whole = lambda shape: pl.BlockSpec(shape, lambda g: (0,) * len(shape))
    slab = pl.BlockSpec((span, LANES), lambda g: (0, g))
    q_lin, kv_lin = qkv_lin[:, :q_width], qkv_lin[:, q_width:]
    return pl.pallas_call(
        with_earlier(attention_forward_kernel, 6, len(earlier)),
        grid=(slabs,),
        in_specs=[
            slab, whole((span, 2 * kv_width)), whole((span, LANES)), whole((span, LANES)),
            whole((span, 1)), whole((1, span)),
        ]
        + any_specs(earlier),
        out_specs=[
            slab, slab, whole((span, kv_width)), whole((span, kv_width)),
            pl.BlockSpec((1, 8, span), lambda g: (g, 0, 0)),
        ],
        out_shape=[
            jax.ShapeDtypeStruct((span, q_width), BF16),
            jax.ShapeDtypeStruct((span, q_width), BF16),
            jax.ShapeDtypeStruct((span, kv_width), BF16),
            jax.ShapeDtypeStruct((span, kv_width), BF16),
            jax.ShapeDtypeStruct((slabs, 8, span), F32),
        ],
        scratch_shapes=[pltpu.VMEM((span, span), F32)]
        + [pltpu.VMEM((kv_heads, span, LANES), BF16)] * 4,
        compiler_params=pltpu.CompilerParams(vmem_limit_bytes=VMEM_BYTES),
        cost_estimate=pl.CostEstimate(
            flops=32 * slabs * span * span * LANES, bytes_accessed=16 * span * q_width,
            transcendentals=slabs * span * span,
        ),
        name="attention_forward",
    )(q_lin, kv_lin, cosine, sine, segment_row[:, None], segment_row[None, :], *earlier)


def attention_backward_kernel(
    q_ref, k_ref, v_ref, out_ref, grad_ref, cos_ref, sin_ref, seg_col, seg_row, lse_ref,
    dq_ref, dkv_ref,
    bias, k_low, k_high, v_low, v_high, dk_low, dk_high, dv_low, dv_high, dq_sum,
):
    slab_at = pl.program_id(0)
    span = q_ref.shape[0]
    kv_slabs = k_ref.shape[1] // LANES

    @pl.when(slab_at == 0)
    def _():
        for at in range(0, span, ROWS):
            keys_at = at + lax.broadcasted_iota(jnp.int32, (ROWS, span), 0)
            rows_at = lax.broadcasted_iota(jnp.int32, (ROWS, span), 1)
            allowed = (rows_at >= keys_at) & (seg_col[at : at + ROWS, :] == seg_row[...])
            bias[at : at + ROWS, :] = jnp.where(allowed, 0.0, MASK_VALUE).astype(F32)
        for j in range(kv_slabs):
            lanes = slice(j * LANES, (j + 1) * LANES)
            spread_heads(k_ref[:, lanes], k_low, k_high, 2 * j)
            spread_heads(v_ref[:, lanes], v_low, v_high, 2 * j)
        for sums in (dk_low, dk_high, dv_low, dv_high):
            sums[...] = jnp.zeros_like(sums)

    kv_even, kv_odd = (2 * slab_at) // 3, (2 * slab_at + 1) // 3
    for at in range(0, span, ROWS):
        rows = slice(at, at + ROWS)
        upto = at + ROWS
        queries, grads = q_ref[rows, :], grad_ref[rows, :]
        turned = (grads.astype(F32) * out_ref[rows, :].astype(F32)).T
        zero = jnp.zeros_like(queries)
        dq_part = None
        for upper, keys, values, dk_sum, dv_sum, kv_at in (
            (False, k_low, v_low, dk_low, dv_low, kv_even),
            (True, k_high, v_high, dk_high, dv_high, kv_odd),
        ):
            first = HEAD_DIM if upper else 0
            delta = jnp.sum(turned[first : first + HEAD_DIM, :], axis=0, keepdims=True)
            head = 1 if upper else 0
            total = lse_ref[0, head : head + 1, rows]
            keys_here = keys[kv_at, :upto, :]
            scores = dot(keys_here, queries, NT) * SCORE_SCALE + bias[:upto, rows]
            probability = jnp.exp(scores - total)
            prob_grad = dot(values[kv_at, :upto, :], grads, NT)
            score_grad = (probability * (prob_grad - delta)).astype(BF16)
            mask = half_mask(ROWS, upper)
            dv_sum[kv_at, :upto, :] += dot(
                probability.astype(BF16), jnp.where(mask, grads, zero)
            )
            dk_sum[kv_at, :upto, :] += dot(score_grad, jnp.where(mask, queries, zero))
            part = dot(score_grad, keys_here, TN)
            dq_part = part if dq_part is None else dq_part + part
        dq_sum[rows, :] = dq_part * SCORE_SCALE
    slab = dq_sum[...]
    dq_ref[...] = (slab * cos_ref[...] - rotate_halves(slab) * sin_ref[...]).astype(BF16)

    @pl.when(slab_at == pl.num_programs(0) - 1)
    def _():
        low = half_mask(span, False)

        def joined(sums_low, sums_high, j):
            one = sums_low[2 * j] + pltpu.roll(sums_high[2 * j], HEAD_DIM, 1)
            two = pltpu.roll(sums_low[2 * j + 1], HEAD_DIM, 1) + sums_high[2 * j + 1]
            return jnp.where(low, one, two)

        for j in range(kv_slabs):
            slab = joined(dk_low, dk_high, j) * SCORE_SCALE
            dkv_ref[:, j * LANES : (j + 1) * LANES] = (
                slab * cos_ref[...] - rotate_halves(slab) * sin_ref[...]
            ).astype(BF16)
            at = (kv_slabs + j) * LANES
            dkv_ref[:, at : at + LANES] = joined(dv_low, dv_high, j).astype(BF16)


def attention_backward(
    queries, keys, values, attended, grad, cosine, sine, segment_row, lse, earlier=()
):
    span, q_width = queries.shape
    kv_width = keys.shape[1]
    slabs, kv_heads = q_width // LANES, kv_width // HEAD_DIM
    whole = lambda shape: pl.BlockSpec(shape, lambda g: (0,) * len(shape))
    slab = pl.BlockSpec((span, LANES), lambda g: (0, g))
    return pl.pallas_call(
        with_earlier(attention_backward_kernel, 10, len(earlier)),
        grid=(slabs,),
        in_specs=[
            slab, whole((span, kv_width)), whole((span, kv_width)), slab, slab,
            whole((span, LANES)), whole((span, LANES)), whole((span, 1)), whole((1, span)),
            pl.BlockSpec((1, 8, span), lambda g: (g, 0, 0)),
        ]
        + any_specs(earlier),
        out_specs=[slab, whole((span, 2 * kv_width))],
        out_shape=[
            jax.ShapeDtypeStruct((span, q_width), BF16),
            jax.ShapeDtypeStruct((span, 2 * kv_width), BF16),
        ],
        scratch_shapes=[pltpu.VMEM((span, span), F32)]
        + [pltpu.VMEM((kv_heads, span, LANES), BF16)] * 4
        + [pltpu.VMEM((kv_heads, span, LANES), F32)] * 4
        + [pltpu.VMEM((span, LANES), F32)],
        compiler_params=pltpu.CompilerParams(vmem_limit_bytes=VMEM_BYTES),
        cost_estimate=pl.CostEstimate(
            flops=40 * slabs * span * span * LANES, bytes_accessed=16 * span * q_width,
            transcendentals=slabs * span * span,
        ),
        name="attention_backward",
    )(
        queries, keys, values, attended, grad, cosine, sine,
        segment_row[:, None], segment_row[None, :], lse, *earlier,
    )


EXPERT_ROWS = 256
EXPERT_VMEM = 63 * 1024 * 1024
SLOTS = 4
Z_FROM = (0, -1, 1, 2)
CHUNK = 2
LATE = 2
SENT = 2
MESH_ID = pl.DeviceIdType.MESH


def experts_kernel(
    inner, chunks, row_steps, x_ref, og_ref, xt_ref, ogt_ref, combine_ref,
    pairs_ref, near_ref, far_ref,
    dx_own, dx_twin, dx_other, mix_out, gate_out, *refs,
):
    keep_outs, refs = refs[:SENT], refs[SENT:]
    part_outs, refs = refs[:SENT], refs[SENT:]
    near_outs, refs = refs[: chunks - SENT], refs[chunks - SENT :]
    late_out, far_out, refs = refs[0], refs[1], refs[2:]
    slots, arrived, held_both, held_down, dx_sum, mix_sum, twin_rows = refs[:7]
    gates, gate_kept, gate_got, gate_full, gate_twin, send, recv, local = refs[7:]
    weights, grads = slots.at[pl.ds(1, chunks)], slots
    near = Neighbours(inner)
    copies = Copies(send, recv, local)
    z, y, x, core, spots = near.z, near.y, near.x, near.core, near.spots
    step = pl.program_id(0)
    steps = row_steps + SLOTS
    chunk, turn = step // steps, step % steps
    last = chunks - 1
    width = x_ref.shape[1]
    block = width // 16
    hidden = held_down.shape[1] // CHUNK
    both = 2 * hidden * CHUNK
    lane = lax.broadcasted_iota(jnp.int32, (EXPERT_ROWS, LANES), 1)
    tokens = dx_sum.shape[0] // 2
    tiles = tokens // EXPERT_ROWS
    tile = (turn + tiles) % row_steps
    rows = pl.ds(pl.multiple_of(tile * EXPERT_ROWS, EXPERT_ROWS), EXPERT_ROWS)

    def near_piece(c, k):
        return pairs_ref.at[c] if k == 0 else near_ref.at[c, k - 1]

    def near_copy(c, k):
        copies.copy(
            lambda c=c, k=k: (near_piece(c, k), weights.at[c, spots[k], y]), ("near", c, k), False
        )

    def near_wait(c, k):
        copies.wait_copy(
            lambda c=c, k=k: (near_piece(c, k), weights.at[c, spots[k], y]), ("near", c, k)
        )

    def far_ends(c, k):
        return far_ref.at[c, k], weights.at[c, spots[k], 1 - y]

    @pl.when(step == 0)
    def _():
        near.greet()
        gates[...] = jnp.zeros_like(gates)
        for k in range(SLOTS):
            near_copy(0, k)
            copies.copy(lambda k=k: far_ends(0, k), ("far", 0, k), False)
        copies.remote(
            lambda: (pairs_ref.at[last], weights.at[last, z, y]), ("y",), ("y",), near.over_y
        )
        for k in range(1, SLOTS):
            copies.remote(
                lambda: (pairs_ref.at[last], weights.at[last, z, y]),
                ("z", k), ("z", BACK[k]), near.along[k],
            )
        for c in range(LATE, last):
            for k in range(SLOTS):
                copies.remote(
                    lambda c=c, k=k: (near_piece(c, k), weights.at[c, spots[k], y]),
                    ("f", c, k), ("f", c, k), near.over_y,
                )
        for c in range(1, chunks):
            for k in range(SLOTS if c < last else 1):
                near_copy(c, k)
                if c < LATE:
                    copies.copy(lambda c=c, k=k: far_ends(c, k), ("far", c, k), False)

    @pl.when(step == row_steps)
    def _():
        copies.arrived(weights.at[last, z, 1 - y], ("y",), near.over_y)
        for k in range(1, SLOTS):
            copies.remote(
                lambda: (weights.at[last, z, 1 - y],) * 2,
                ("z2", k), ("z2", BACK[k]), near.along[k],
            )

    for c in range(chunks):

        @pl.when(step == c * steps)
        def _():
            for k in range(SLOTS):
                if c < last or k == 0:
                    near_wait(c, k)
                if c < LATE:
                    copies.wait_copy(lambda c=c, k=k: far_ends(c, k), ("far", c, k))
                elif c < last:
                    copies.arrived(weights.at[c, spots[k], 1 - y], ("f", c, k), near.over_y)
                elif k > 0:
                    copies.arrived(weights.at[c, spots[k], y], ("z", k), near.along[k])
                    copies.arrived(weights.at[c, spots[k], 1 - y], ("z2", k), near.along[k])

    def add_arrived(c):
        copies.arrived(arrived.at[c], ("sum", c), near.over_y)
        for k in range(SLOTS):
            own = grads.at[c, spots[k], y]
            own[...] = (own[...].astype(F32) + arrived[c, spots[k]].astype(F32)).astype(BF16)
        copies.copy(lambda c=c: (grads.at[c, z, y], keep_outs[c]), ("keep", c))
        for k in range(1, SLOTS):
            copies.remote(
                lambda c=c, k=k: (grads.at[c, spots[k], y], part_outs[c].at[BACK[k] - 1]),
                ("part", c, k), ("part", c, BACK[k]), near.along[k],
            )

    @pl.when(step == 2 * steps + row_steps - 2)
    def _():
        add_arrived(0)

    @pl.when(step == 3 * steps + 4)
    def _():
        add_arrived(1)

    @pl.when(turn < row_steps)
    def _():
        for e in range(CHUNK):
            first = 2 * hidden * e
            w_both = weights[chunk, :, :, :, first : first + 2 * hidden].reshape(width, 2 * hidden)
            start = both + hidden * e
            w_down = weights[chunk, :, :, :, start : start + hidden].reshape(width, hidden)
            gate_up = dot(x_ref[...], w_both)
            raw = dot(og_ref[...], w_down) * RESIDUAL_SCALE
            gate, up = gate_up[:, :hidden], gate_up[:, hidden:]
            gate_lane = lax.broadcasted_iota(
                jnp.int32, (EXPERT_ROWS, combine_ref.shape[1]), 1
            )
            column = jnp.sum(
                jnp.where(gate_lane == chunk * CHUNK + e, combine_ref[...], 0.0),
                axis=1, keepdims=True,
            )
            sigmoid = 1.0 / (1.0 + jnp.exp(-gate))
            active = gate * sigmoid
            inner_value = (active * up).astype(BF16).astype(F32)
            held_down[rows, hidden * e : hidden * (e + 1)] = (inner_value * column).astype(BF16)
            gates[rows, :] = jnp.where(
                lane == chunk * CHUNK + e,
                jnp.sum(inner_value * raw, axis=1, keepdims=True),
                gates[rows, :],
            )
            inner_grad = raw * column
            held_both[rows, first : first + hidden] = (
                inner_grad * up * sigmoid * (1.0 + gate * (1.0 - sigmoid))
            ).astype(BF16)
            held_both[rows, first + hidden : first + 2 * hidden] = (inner_grad * active).astype(BF16)

        def sums(add):
            for part in range(SLOTS):
                cols = slice(4 * block * part, 4 * block * (part + 1))
                w_both = weights[chunk, part, :, :, :both].reshape(4 * block, both)
                w_down = weights[chunk, part, :, :, both:].reshape(4 * block, hidden * CHUNK)
                mix = dot(held_down[rows, :], w_down, NT)
                dx = dot(held_both[rows, :], w_both, NT)
                if add:
                    mix = mix + mix_sum[rows, cols].astype(F32)
                    dx = dx + dx_sum[rows, cols].astype(F32)
                mix_sum[rows, cols] = mix.astype(BF16)
                dx_sum[rows, cols] = dx.astype(BF16)

        @pl.when(chunk == 0)
        def _():
            sums(False)

        @pl.when(chunk > 0)
        def _():
            sums(True)

    @pl.when(turn >= row_steps)
    def _():
        part = turn - row_steps
        grads[chunk, part, :, :, :both] = (
            dot(xt_ref[...], held_both[...]).astype(BF16).reshape(2, 2 * block, both)
        )
        grads[chunk, part, :, :, both:] = (
            (dot(ogt_ref[...], held_down[...]) * RESIDUAL_SCALE)
            .astype(BF16)
            .reshape(2, 2 * block, hidden * CHUNK)
        )

    begin = last * steps
    for i in range(2):
        for c in range(2):
            mine = pl.ds(tokens + (2 * c + i) * EXPERT_ROWS, EXPERT_ROWS)
            there = pl.ds((2 * c + i) * EXPERT_ROWS, EXPERT_ROWS)

            @pl.when((step == begin + 2 * c + i) & (core != c))
            def _():
                copies.remote(
                    lambda: (dx_sum.at[mine], twin_rows.at[i]), ("t", i), ("t", i), near.twin,
                    last=False,
                )

            @pl.when((step == begin + 2 + 2 * c + i) & (core == c))
            def _():
                copies.arrived(twin_rows.at[i], ("t", i), near.twin)
                dx_sum[mine, :] = (
                    dx_sum[mine, :].astype(F32) + twin_rows[i].astype(F32)
                ).astype(BF16)
                copies.remote(
                    lambda: (dx_sum.at[mine], dx_other.at[there]), ("o", i), ("o", i), near.over_x,
                    last=False,
                )

            @pl.when((step == begin + steps - 2 + i) & (core == c))
            def _():
                copies.arrived(dx_other.at[there], ("o", i), near.over_x)
                copies.remote(
                    lambda: (dx_other.at[there],) * 2, ("o2", i), ("o2", i), near.twin, last=False
                )

    for i in range(tiles):

        @pl.when(step == begin + tiles + i)
        def _():
            own = pl.ds(i * EXPERT_ROWS, EXPERT_ROWS)
            copies.copy(lambda own=own: (dx_sum.at[own], dx_own.at[own]), ("own", i))
            copies.remote(
                lambda own=own: (dx_sum.at[own], dx_twin.at[own]), ("own", i), ("own", i), near.twin
            )

    shares = gate_kept.shape[0]

    @pl.when(step == begin + row_steps)
    def _():
        copies.copy(lambda: (mix_sum, mix_out), "mix")
        turned = gates[...].T[:shares, :]
        gate_kept[...] = turned
        copies.remote(
            lambda: (gate_kept.at[:, pl.ds(tokens, tokens)], gate_got), ("g",), ("g",), near.over_x
        )

    @pl.when(step == begin + steps - 2)
    def _():
        copies.arrived(gate_got, ("g",), near.over_x)
        gate_full[pl.ds(pl.multiple_of(x * shares, shares), shares), :] = gate_kept[:, :tokens]
        gate_full[pl.ds(pl.multiple_of((1 - x) * shares, shares), shares), :] = gate_got[...]
        copies.remote(lambda: (gate_full, gate_twin), ("g2",), ("g2",), near.twin)

    for c in range(chunks):

        @pl.when(step == (c + 1) * steps - 1)
        def _():
            if c < SENT:
                copies.remote(
                    lambda c=c: (grads.at[c, :, 1 - y], arrived.at[c]),
                    ("sum", c), ("sum", c), near.over_y,
                )
            else:
                for k in range(SLOTS):
                    copies.copy(
                        lambda c=c, k=k: (grads.at[c, spots[k], y], near_outs[c - SENT].at[k]),
                        ("near out", c, k),
                    )
                    if c < last:
                        copies.remote(
                            lambda c=c, k=k: (grads.at[c, spots[k], 1 - y], late_out.at[k]),
                            ("late", k), ("late", k), near.over_y,
                        )
                    else:
                        copies.copy(
                            lambda c=c, k=k: (grads.at[c, spots[k], 1 - y], far_out.at[k]),
                            ("far out", k),
                        )

    @pl.when(step == chunks * steps - 1)
    def _():
        copies.arrived(gate_twin, ("g2",), near.twin)
        gate_out[...] = gate_full[...] + gate_twin[...]
        for i in range(tiles):
            copies.arrived(
                dx_twin.at[pl.ds(i * EXPERT_ROWS, EXPERT_ROWS)], ("own", i), near.twin
            )
        for i in range(2):
            for c in range(2):
                mine = pl.ds(tokens + (2 * c + i) * EXPERT_ROWS, EXPERT_ROWS)
                there = pl.ds((2 * c + i) * EXPERT_ROWS, EXPERT_ROWS)

                @pl.when(core != c)
                def _():
                    copies.sent(lambda: (dx_sum.at[mine], twin_rows.at[i]), ("t", i), near.twin)
                    copies.arrived(dx_other.at[there], ("o2", i), near.twin)

                @pl.when(core == c)
                def _():
                    copies.sent(
                        lambda: (dx_sum.at[mine], dx_other.at[there]), ("o", i), near.over_x
                    )
                    copies.sent(lambda: (dx_other.at[there],) * 2, ("o2", i), near.twin)

        for c in range(SENT):
            for k in range(1, SLOTS):
                copies.arrived(part_outs[c].at[k - 1], ("part", c, k), near.along[k])
        for k in range(SLOTS):
            copies.arrived(late_out.at[k], ("late", k), near.over_y)
        copies.finish()


def experts_pass(x, og, xt, ogt, combine, pairs, near, far):
    tokens, width = x.shape
    chunks, pair, columns = pairs.shape
    hidden = columns // (3 * CHUNK)
    shares = chunks * CHUNK
    row_steps = tokens // EXPERT_ROWS
    steps = row_steps + SLOTS
    inner = lax.axis_size("dp") // 16
    row_at = lambda s: ((jnp.minimum(s % steps, row_steps - 1) + row_steps // 2) % row_steps, 0)
    width_at = lambda s: (jnp.maximum(s % steps - row_steps, 0), 0)
    row = pl.BlockSpec((EXPERT_ROWS, width), row_at)
    turned = pl.BlockSpec((width // SLOTS, tokens), width_at)
    anywhere = pl.BlockSpec(memory_space=pl.ANY)
    left = chunks - SENT
    dma = pltpu.SemaphoreType.DMA
    shape = jax.ShapeDtypeStruct
    outs = pl.pallas_call(
        functools.partial(experts_kernel, inner, chunks, row_steps),
        grid=(chunks * steps,),
        in_specs=[row, row, turned, turned, pl.BlockSpec((EXPERT_ROWS, combine.shape[1]), row_at)]
        + [anywhere] * 3,
        out_specs=[anywhere] * 4
        + [pl.BlockSpec((2 * shares, tokens // 2), lambda s: (0, 0))]
        + [anywhere] * (2 * SENT + left + 2),
        out_shape=[shape((tokens // 2, width), BF16)] * 3
        + [shape((tokens, width), BF16), shape((2 * shares, tokens // 2), F32)]
        + [shape((pair, columns), BF16)] * SENT
        + [shape((SLOTS - 1, pair, columns), BF16)] * SENT
        + [shape((SLOTS, pair, columns), BF16)] * (left + 2),
        scratch_shapes=[
            pltpu.VMEM((chunks + 1, SLOTS, 2, pair, columns), BF16),
            pltpu.VMEM((SENT, SLOTS, pair, columns), BF16),
            pltpu.VMEM((tokens, 2 * hidden * CHUNK), BF16),
            pltpu.VMEM((tokens, hidden * CHUNK), BF16),
            pltpu.VMEM((tokens, width), BF16),
            pltpu.VMEM((tokens, width), BF16),
            pltpu.VMEM((2, EXPERT_ROWS, width), BF16),
            pltpu.VMEM((tokens, LANES), F32),
            pltpu.VMEM((shares, tokens), F32),
            pltpu.VMEM((shares, tokens // 2), F32),
            pltpu.VMEM((2 * shares, tokens // 2), F32),
            pltpu.VMEM((2 * shares, tokens // 2), F32),
            dma((48,)), dma((48,)), dma((48,)),
        ],
        compiler_params=pltpu.CompilerParams(
            vmem_limit_bytes=EXPERT_VMEM, collective_id=0, has_side_effects=True
        ),
        cost_estimate=pl.CostEstimate(
            flops=8 * tokens * width * chunks * columns,
            bytes_accessed=2 * chunks * width * columns, transcendentals=0,
        ),
        name="experts_pass",
    )(x, og, xt, ogt, combine, pairs, near, far)
    dx, mix, gate = outs[:3], outs[3], outs[4]
    rest = outs[5:]
    keep, parts, rest = rest[:SENT], rest[SENT : 2 * SENT], rest[2 * SENT :]
    return dx, mix, gate, keep, parts, rest[:left], rest[left], rest[left + 1]


class Copies:
    def __init__(self, send, recv, local):
        self.send, self.recv, self.local = send, recv, local
        self.sends, self.recvs, self.locals, self.started = {}, {}, {}, []

    def remote(self, ends, name, arrives, device, last=True):
        sent = self.sends.setdefault(name, len(self.sends))
        got = self.recvs.setdefault(arrives, len(self.recvs))

        def make():
            source, target = ends()
            return pltpu.make_async_remote_copy(
                source, target, self.send.at[sent], self.recv.at[got],
                device_id=device, device_id_type=MESH_ID,
            )

        make().start()
        if last:
            self.started.append(lambda: make().wait_send())

    def sent(self, ends, name, device):
        source, target = ends()
        pltpu.make_async_remote_copy(
            source, target, self.send.at[self.sends[name]], self.recv.at[0],
            device_id=device, device_id_type=MESH_ID,
        ).wait_send()

    def arrived(self, place, name, device):
        got = self.recvs.setdefault(name, len(self.recvs))
        pltpu.make_async_remote_copy(
            place, place, self.send.at[0], self.recv.at[got],
            device_id=device, device_id_type=MESH_ID,
        ).wait_recv()

    def copy(self, ends, name, wait_last=True):
        at = self.locals.setdefault(name, len(self.locals))

        def make():
            return pltpu.make_async_copy(*ends(), self.local.at[at])

        make().start()
        if wait_last:
            self.started.append(lambda: make().wait())
        return lambda: make().wait()

    def wait_copy(self, ends, name):
        pltpu.make_async_copy(*ends(), self.local.at[self.locals[name]]).wait()

    def finish(self):
        for wait in self.started:
            wait()


class Neighbours:
    def __init__(self, inner):
        me = lax.axis_index("dp")
        at = me // inner
        self.core = lax.axis_index("tensor")
        self.z, self.y, self.x = at // 4, at // 2 % 2, at % 2
        self.spots = [(self.z + dz + 4) % 4 for dz in Z_FROM]
        self.along = [{"dp": me + (spot - self.z) * 4 * inner} for spot in self.spots]
        self.over_y = {"dp": me + (1 - 2 * self.y) * 2 * inner}
        self.over_x = {"dp": me + (1 - 2 * self.x) * inner}
        self.twin = {"tensor": 1 - self.core}
        self.blocks = {
            (k, other_y, other_x): self.spots[k] * 4
            + (1 - self.y if other_y else self.y) * 2
            + (1 - self.x if other_x else self.x)
            for k in range(SLOTS)
            for other_y in (0, 1)
            for other_x in (0, 1)
        }

    def greet(self):
        barrier = pltpu.get_barrier_semaphore()
        devices = [*self.along[1:], self.over_y, self.over_x, self.twin]
        for device in devices:
            pl.semaphore_signal(barrier, inc=1, device_id=device, device_id_type=MESH_ID)
        pl.semaphore_wait(barrier, len(devices))

    def block(self, k, other_y, other_x):
        return self.blocks[k, other_y, other_x]


BACK = (0, 2, 1, 3)


class Gather:
    def __init__(self, copies, near, shard, full, tag):
        self.copies, self.near, self.shard, self.full, self.tag = copies, near, shard, full, tag
        self.split = full.shape[2] // (2 * LANES) * LANES

    def source(self, k):
        return self.shard if k == 0 else self.full.at[self.near.block(k, 0, 0)]

    def begin(self):
        for k in range(1, SLOTS):
            self.copies.remote(
                lambda: (self.shard, self.full.at[self.near.block(0, 0, 0)]),
                (self.tag, "z", k), (self.tag, "z", BACK[k]), self.near.along[k],
            )
        self.full[self.near.block(0, 0, 0)] = self.shard[...]

    def spread(self, k):
        near, place = self.near, self.full.at[self.near.block(k, 0, 0)]
        if k > 0:
            self.copies.arrived(place, (self.tag, "z", k), near.along[k])
        for way, device in (("y", near.over_y), ("x", near.over_x)):
            name = (self.tag, way, k)
            self.copies.remote(
                lambda: (self.source(k), self.full.at[near.block(k, 0, 0)]), name, name, device
            )

    def cross(self, k):
        near = self.near
        from_y = self.full.at[near.block(k, 1, 0)]
        from_x = self.full.at[near.block(k, 0, 1)]
        self.copies.arrived(from_y, (self.tag, "y", k), near.over_y)
        self.copies.remote(
            lambda: (self.full.at[near.block(k, 1, 0), :, : self.split],) * 2,
            (self.tag, "one", k), (self.tag, "one", k), near.over_x,
        )
        self.copies.arrived(from_x, (self.tag, "x", k), near.over_x)
        self.copies.remote(
            lambda: (self.full.at[near.block(k, 0, 1), :, self.split :],) * 2,
            (self.tag, "two", k), (self.tag, "two", k), near.over_y,
        )

    def end(self):
        near = self.near
        for k in range(SLOTS):
            place = self.full.at[near.block(k, 1, 1)]
            self.copies.arrived(place.at[:, : self.split], (self.tag, "one", k), near.over_x)
            self.copies.arrived(place.at[:, self.split :], (self.tag, "two", k), near.over_y)


def roll_left(slab, lanes):
    return pltpu.roll(slab, LANES - lanes, 1)


def forward_kernel(
    inner, q_shard, o_shard, gateup_hbm, down_hbm, hidden_hbm, og_hbm, cos, sin, seg_col, seg_row,
    routes,
    q_full, o_full, small, normed, q_ref, k_ref, v_ref, attended, lse_ref, combine, combine_pair,
    middle_hbm, x_hbm, xt_hbm, og_pair, ogt_hbm, pairs_hbm, near_hbm, far_hbm,
    hidden, gateup, down, given, pairs, bias, k_low, k_high, v_low, v_high, part, part_got, x_own,
    middle, stage, turned, columns_out, columns_got, send, recv, local,
):
    near = Neighbours(inner)
    copies = Copies(send, recv, local)
    tokens, width = hidden.shape
    block = width // 16
    chunks = pairs.shape[0]
    hid = down.shape[1]
    q_width = q_ref.shape[1]
    kv_slabs = k_ref.shape[1] // LANES
    slabs = q_width // LANES
    qkv_width = q_width + 2 * k_ref.shape[1]
    experts = down.shape[0]
    each = 2 + experts
    half = tokens // 2
    tiles = tokens // ROWS
    x, core = near.x, near.core
    own_half = pl.ds(pl.multiple_of(core * half, half), half)
    mine = pl.ds(pl.multiple_of(tokens + core * half, half), half)
    theirs = pl.ds(pl.multiple_of(tokens + (1 - core) * half, half), half)

    near.greet()
    gather_q = Gather(copies, near, q_shard, q_full, "q")
    gather_o = Gather(copies, near, o_shard, o_full, "o")
    gather_q.begin()
    gather_q.spread(0)
    weights_in = [
        copies.copy(lambda: (gateup_hbm, gateup), "gateup", False),
        copies.copy(lambda: (down_hbm, down), "down", False),
    ]
    hidden_in = copies.copy(lambda: (hidden_hbm, hidden), "hidden", False)
    copies.copy(lambda: (og_hbm, og_pair.at[pl.ds(0, tokens)]), "og")

    def pack(c, mine):
        first = 2 * (chunks * (x if mine else 1 - x) + c)
        rows = pl.ds(pl.multiple_of(x * block, block), block)
        for e in range(CHUNK):
            for part_at in range(2):
                at = hid * (2 * e + part_at)
                value = gateup[first + e, part_at].astype(BF16)
                if mine:
                    pairs[c, rows, at : at + hid] = value
                else:
                    given[c, :, at : at + hid] = value
            at = hid * (2 * CHUNK + e)
            value = down[first + e].astype(F32).T.astype(BF16)
            if mine:
                pairs[c, rows, at : at + hid] = value
            else:
                given[c, :, at : at + hid] = value

    def swap(c):
        rows = pl.ds(pl.multiple_of(x * block, block), block)
        copies.remote(
            lambda: (given.at[c], pairs.at[c, rows]), ("s", c), ("s", c), near.over_x
        )

    def swapped(c):
        rows = pl.ds(pl.multiple_of((1 - x) * block, block), block)
        copies.arrived(pairs.at[c, rows], ("s", c), near.over_x)

    def ring_one(c):
        copies.remote(
            lambda: (pairs.at[c], near_hbm.at[c, 0]), ("up", c), ("r", c, 1), near.along[2]
        )
        copies.remote(
            lambda: (pairs.at[c], near_hbm.at[c, 1]), ("down", c), ("r", c, 2), near.along[1]
        )

    def ring_two(c):
        copies.arrived(near_hbm.at[c, 0], ("r", c, 1), near.along[1])
        copies.remote(
            lambda: (near_hbm.at[c, 0], near_hbm.at[c, 2]), ("two", c), ("r", c, 3), near.along[2]
        )

    def over_y(c, k):
        copies.remote(
            lambda: (pairs.at[c] if k == 0 else near_hbm.at[c, k - 1], far_hbm.at[c, k]),
            ("f", c, k), ("f", c, k), near.over_y,
        )

    def ring_got(c, k):
        copies.arrived(near_hbm.at[c, k - 1], ("r", c, k), near.along[k])

    def turn_tile(source, target, name, side):
        copies.copy(lambda: (source, stage.at[side]), (name, "in"), False)()
        turned[side] = stage[side].T
        return copies.copy(lambda: (turned.at[side], target), (name, "out"), False)

    waits = [None, None]

    def turn_next(source, target, name, side):
        if waits[side] is not None:
            waits[side]()
        waits[side] = turn_tile(source, target, name, side)

    for wait in weights_in:
        wait()
    pack(0, False)
    swap(0)
    pack(0, True)
    gather_q.spread(1)
    gather_q.spread(2)
    pack(1, False)
    pack(1, True)
    gather_q.cross(0)
    gather_q.spread(3)
    gather_o.begin()
    pack(2, False)
    pack(2, True)
    gather_q.cross(1)
    gather_q.cross(2)
    swapped(0)
    ring_one(0)
    over_y(0, 0)
    pack(3, False)
    pack(3, True)
    fill_bias(bias, seg_col, seg_row)
    gather_q.cross(3)
    gather_o.spread(0)
    for c in range(1, chunks):
        swap(c)
    for tile in range(tiles):
        rows = pl.ds(tile * ROWS, ROWS)
        turn_next(og_hbm.at[rows], ogt_hbm.at[:, rows], ("og", tile), tile % 2)
    hidden_in()
    gather_q.end()
    pieces = q_full[:, :, qkv_width:].reshape(width, LANES)
    wide = pieces.astype(F32)
    summed = wide + roll_left(wide, each) + roll_left(wide, 2 * each)
    small[...] = summed.T[: small.shape[0], :]

    def project(tile, carry):
        rows = pl.ds(pl.multiple_of(tile * ROWS, ROWS), ROWS)
        value = hidden[rows, :].astype(F32)
        inverse = lax.rsqrt(jnp.mean(value * value, axis=1, keepdims=True) + NORM_EPSILON)
        low = (value * inverse * small[0:1, :]).astype(BF16)
        normed[rows, :] = low
        cosine, sine = cos[rows, :], sin[rows, :]
        for g in range(slabs + 2 * kv_slabs):
            lanes = slice(g * LANES, (g + 1) * LANES)
            if g % 2 == 0:
                two = slice(g * LANES, (g + 2) * LANES)
                lin_two = dot(low, q_full[:, :, two].reshape(width, 2 * LANES))
            lin = lin_two[:, (g % 2) * LANES : (g % 2 + 1) * LANES]
            if g < slabs + kv_slabs:
                lin = lin * cosine + rotate_halves(lin) * sine
            if g < slabs:
                q_ref[rows, lanes] = lin.astype(BF16)
            elif g < slabs + kv_slabs:
                at = (g - slabs) * LANES
                k_ref[rows, at : at + LANES] = lin.astype(BF16)
            else:
                at = (g - slabs - kv_slabs) * LANES
                v_ref[rows, at : at + LANES] = lin.astype(BF16)

        @pl.when(tile == 0)
        def _():
            gather_o.spread(1)
            gather_o.spread(2)

        @pl.when(tile == 2)
        def _():
            gather_o.spread(3)
            gather_o.cross(0)

        return carry

    lax.fori_loop(0, tiles, project, 0)
    for j in range(kv_slabs):
        lanes = slice(j * LANES, (j + 1) * LANES)
        spread_heads(k_ref[:, lanes], k_low, k_high, 2 * j)
        spread_heads(v_ref[:, lanes], v_low, v_high, 2 * j)

    def attend(g, carry):
        lanes = pl.ds(pl.multiple_of(g * LANES, LANES), LANES)
        kv_even, kv_odd = (2 * g) // 3, (2 * g + 1) // 3
        for at in range(0, tokens, ROWS):
            rows = slice(at, at + ROWS)
            upto = at + ROWS
            queries = q_ref[rows, lanes]
            total = None
            stats = []
            for keys, values, kv_at in ((k_low, v_low, kv_even), (k_high, v_high, kv_odd)):
                scores = dot(queries, keys[kv_at, :upto, :], NT) * SCORE_SCALE + bias[rows, :upto]
                highest = jnp.max(scores, axis=1, keepdims=True)
                weights = jnp.exp(scores - highest)
                whole = jnp.sum(weights, axis=1, keepdims=True)
                probability = (weights * (1.0 / whole)).astype(BF16)
                one = dot(probability, values[kv_at, :upto, :])
                total = one if total is None else total + one
                stats.append(highest + jnp.log(whole))
            attended[rows, lanes] = total.astype(BF16)
            across = jnp.where(half_mask(ROWS, False), stats[0], stats[1]).T
            lse_ref[g, 0:1, rows] = across[0:1, :]
            lse_ref[g, 1:2, rows] = across[HEAD_DIM : HEAD_DIM + 1, :]

        @pl.when(g == 0)
        def _():
            gather_o.cross(1)
            gather_o.cross(2)
            ring_two(0)
            over_y(0, 1)
            swapped(1)
            ring_one(1)
            over_y(1, 0)

        @pl.when(g == 1)
        def _():
            gather_o.cross(3)
            ring_got(0, 2)
            over_y(0, 2)
            copies.remote(
                lambda: (og_hbm.at[own_half], og_pair.at[mine]), ("og",), ("og",), near.over_x
            )

        @pl.when(g == 3)
        def _():
            ring_got(0, 3)
            over_y(0, 3)
            swapped(2)
            ring_one(2)

        @pl.when(g == 4)
        def _():
            ring_two(1)
            over_y(1, 1)
            ring_got(1, 2)
            over_y(1, 2)
            gather_o.end()

        return carry

    lax.fori_loop(0, slabs, attend, 0)

    def project_out(step, carry):
        tile = (step + 2 * (1 - core)) % tiles
        rows = pl.ds(pl.multiple_of(tile * ROWS, ROWS), ROWS)
        low = attended[rows, :]
        for group in range(SLOTS):
            cols = slice(4 * block * group, 4 * block * (group + 1))
            weight = o_full[4 * group : 4 * (group + 1)].reshape(4 * block, q_width)
            part[rows, cols] = dot(low, weight, NT).astype(BF16)
        return carry

    for step in range(tiles):
        project_out(step, 0)
        tile = (step + 2 * (1 - core)) % tiles
        rows = pl.ds(pl.multiple_of(tile * ROWS, ROWS), ROWS)
        copies.remote(
            lambda rows=rows: (part.at[rows], part_got.at[rows]),
            ("p", step), ("p", step), near.twin,
        )
    router = q_full[:, :, qkv_width:].reshape(width, LANES)
    for step in range(tiles):
        tile = (step + 2 * core) % tiles
        rows = pl.ds(pl.multiple_of(tile * ROWS, ROWS), ROWS)
        copies.arrived(part_got.at[rows], ("p", step), near.twin)
        side = step % 2
        if step >= 2:
            middle_out[side]()
        elif step == 0:
            middle_out = [None, None]
        total = hidden[rows, :].astype(F32) + RESIDUAL_SCALE * (
            part[rows, :].astype(F32) + part_got[rows, :].astype(F32)
        )
        middle[side] = total
        middle_out[side] = copies.copy(
            lambda rows=rows, side=side: (middle.at[side], middle_hbm.at[rows]), ("m", step), False
        )
        inverse = lax.rsqrt(jnp.mean(total * total, axis=1, keepdims=True) + NORM_EPSILON)
        value = total * inverse * small[1:2, :]
        high = value.astype(BF16)
        x_own[rows, :] = high
        copies.copy(lambda rows=rows: (x_own.at[rows], x_hbm.at[rows]), ("x", step))
        if step < 2:
            there = pl.ds(pl.multiple_of(tokens + tile * ROWS, ROWS), ROWS)
            copies.remote(
                lambda rows=rows, there=there: (x_own.at[rows], x_hbm.at[there]),
                ("x", step), ("x", step), near.over_x,
            )
        rest = value - high.astype(F32)
        mid = rest.astype(BF16)
        low = (rest - mid.astype(F32)).astype(BF16)
        one, two, three = dot(high, router), dot(mid, router), dot(low, router)
        logits = one + roll_left(one, each) + roll_left(one, 2 * each) + two + roll_left(two, each)
        logits = roll_left(logits + three, 2)
        lane = lax.broadcasted_iota(jnp.int32, (ROWS, LANES), 1)
        chosen = lane < 0
        route = routes[rows, :]
        for k in range(routes.shape[1]):
            chosen = chosen | (route[:, k : k + 1] == lane)
        logits = jnp.where(chosen, logits, MASK_VALUE)
        powers = jnp.exp(logits - jnp.max(logits, axis=1, keepdims=True))
        powers = jnp.where(chosen, powers, 0.0)
        combine[rows, :] = powers * (1.0 / jnp.sum(powers, axis=1, keepdims=True))
        if step == 0:
            swapped(3)
            copies.copy(lambda: (pairs, pairs_hbm), "pairs")
        if step == 1:
            ring_got(1, 3)
            over_y(1, 3)
        if step == 2:
            ring_two(2)

    shares = experts // 2
    flipped = combine[...].T
    kept = jnp.where(x == 0, flipped[:shares, :], flipped[shares : 2 * shares, :])
    gone = jnp.where(x == 0, flipped[shares : 2 * shares, :], flipped[:shares, :])
    columns_out[...] = gone
    copies.remote(lambda: (columns_out, columns_got), ("c",), ("c",), near.over_x)
    combine_pair[:tokens, :] = kept.T

    copies.arrived(og_pair.at[mine], ("og",), near.over_x)
    copies.remote(lambda: (og_pair.at[mine],) * 2, ("og2",), ("og2",), near.twin)
    for tile in range(tiles):
        rows = pl.ds(tile * ROWS, ROWS)
        if waits[tile % 2] is not None:
            waits[tile % 2]()
        turned[tile % 2] = x_own[rows, :].T
        waits[tile % 2] = copies.copy(
            lambda rows=rows, side=tile % 2: (turned.at[side], xt_hbm.at[:, rows]),
            ("xt", tile), False,
        )
    for step in range(2):
        tile = (step + 2 * core) % tiles
        rows = pl.ds(pl.multiple_of(tokens + tile * ROWS, ROWS), ROWS)
        turn_next(og_pair.at[rows], ogt_hbm.at[:, rows], ("og", tiles + step), step)
    copies.arrived(columns_got, ("c",), near.over_x)
    combine_pair[tokens:, :] = columns_got[...].T
    copies.arrived(og_pair.at[theirs], ("og2",), near.twin)
    for step in range(2):
        tile = (step + 2 * (1 - core)) % tiles
        rows = pl.ds(pl.multiple_of(tokens + tile * ROWS, ROWS), ROWS)
        turn_next(og_pair.at[rows], ogt_hbm.at[:, rows], ("og", tiles + 2 + step), step)
    for step in range(2):
        tile = (step + 2 * core) % tiles
        rows = pl.ds(pl.multiple_of(tokens + tile * ROWS, ROWS), ROWS)
        copies.arrived(x_hbm.at[rows], ("x", step), near.over_x)
        copies.remote(
            lambda rows=rows: (x_hbm.at[rows],) * 2, ("x2", step), ("x2", step), near.twin
        )
        turn_next(x_hbm.at[rows], xt_hbm.at[:, rows], ("xt", tiles + step), step)
    for step in range(2):
        tile = (step + 2 * (1 - core)) % tiles
        rows = pl.ds(pl.multiple_of(tokens + tile * ROWS, ROWS), ROWS)
        copies.arrived(x_hbm.at[rows], ("x2", step), near.twin)
        turn_next(x_hbm.at[rows], xt_hbm.at[:, rows], ("xt", tiles + 2 + step), step)
    for wait in waits + middle_out:
        wait()
    ring_got(2, 2)
    ring_got(2, 3)
    for c in range(LATE):
        for k in range(SLOTS):
            copies.arrived(far_hbm.at[c, k], ("f", c, k), near.over_y)
    copies.finish()


def forward_pass(q_shard, o_shard, gateup, down, hidden, og, cosine, sine, segments, routes):
    tokens, width = hidden.shape
    experts, hid = down.shape[:2]
    block, q_columns = q_shard.shape
    q_width = o_shard.shape[1]
    kv_width = (q_columns - LANES - q_width) // 2
    slabs, kv_heads = q_width // LANES, kv_width // HEAD_DIM
    chunks = experts // (2 * CHUNK)
    columns = 3 * CHUNK * hid
    anywhere, vmem = pl.BlockSpec(memory_space=pl.ANY), vmem_spec()
    shape = jax.ShapeDtypeStruct
    inner = lax.axis_size("dp") // 16
    dma = pltpu.SemaphoreType.DMA
    return pl.pallas_call(
        functools.partial(forward_kernel, inner),
        in_specs=[vmem, vmem] + [anywhere] * 4 + [vmem] * 5,
        out_specs=[vmem] * 11 + [anywhere] * 8,
        out_shape=[
            shape((16, block, q_columns), BF16),
            shape((16, block, q_width), BF16),
            shape((24, width), F32),
            shape((tokens, width), BF16),
            shape((tokens, q_width), BF16),
            shape((tokens, kv_width), BF16),
            shape((tokens, kv_width), BF16),
            shape((tokens, q_width), BF16),
            shape((slabs, 8, tokens), F32),
            shape((tokens, LANES), F32),
            shape((2 * tokens, experts // 2), F32),
            shape((tokens, width), F32),
            shape((2 * tokens, width), BF16),
            shape((width, 2 * tokens), BF16),
            shape((2 * tokens, width), BF16),
            shape((width, 2 * tokens), BF16),
            shape((chunks, 2 * block, columns), BF16),
            shape((chunks - 1, SLOTS - 1, 2 * block, columns), BF16),
            shape((LATE, SLOTS, 2 * block, columns), BF16),
        ],
        scratch_shapes=[
            pltpu.VMEM((tokens, width), BF16),
            pltpu.VMEM(gateup.shape, gateup.dtype),
            pltpu.VMEM(down.shape, down.dtype),
            pltpu.VMEM((chunks, block, columns), BF16),
            pltpu.VMEM((chunks, 2 * block, columns), BF16),
            pltpu.VMEM((tokens, tokens), F32),
        ]
        + [pltpu.VMEM((kv_heads, tokens, LANES), BF16)] * 4
        + [pltpu.VMEM((tokens, width), BF16)] * 3
        + [
            pltpu.VMEM((2, ROWS, width), F32),
            pltpu.VMEM((2, ROWS, width), BF16),
            pltpu.VMEM((2, width, ROWS), BF16),
            pltpu.VMEM((experts // 2, tokens), F32),
            pltpu.VMEM((experts // 2, tokens), F32),
            dma((80,)), dma((80,)), dma((60,)),
        ],
        compiler_params=pltpu.CompilerParams(
            vmem_limit_bytes=EXPERT_VMEM, collective_id=1, has_side_effects=True
        ),
        name="forward_pass",
    )(
        q_shard, o_shard, gateup, down, hidden, og, cosine, sine,
        segments[:, None], segments[None, :], routes,
    )


def whole_call(kernel, values, outs, earlier=(), name=None):
    return pl.pallas_call(
        with_earlier(kernel, len(values), len(earlier)),
        in_specs=[vmem_spec()] * len(values) + any_specs(earlier),
        out_specs=[vmem_spec()] * len(outs),
        out_shape=[jax.ShapeDtypeStruct(shape, dtype) for shape, dtype in outs],
        compiler_params=pltpu.CompilerParams(vmem_limit_bytes=VMEM_BYTES),
        name=name,
    )(*values, *earlier)


def fence_kernel(*refs):
    count = len(refs) // 2
    for value, out in zip(refs[:count], refs[count:]):
        out[...] = value[...]


def fence_all(values, *earlier):
    return whole_call(fence_kernel, values, [(v.shape, v.dtype) for v in values], earlier, "fence")


def fence(value, *earlier):
    return fence_all([value], *earlier)[0]


def sum_y_kernel(near, got, *outs):
    for k, out in enumerate(outs):
        out[...] = (near[k].astype(F32) + got[k].astype(F32)).astype(BF16)


def sum_y(near, got, *earlier):
    outs = [(near.shape[1:], BF16)] * SLOTS
    return whole_call(sum_y_kernel, [near, got], outs, earlier, "sum_y")


def sum_z_kernel(x_at, *refs):
    kept, given = refs[-2:]
    half = kept.shape[1]
    for c in range(kept.shape[0]):
        parts = refs[SLOTS * c : SLOTS * (c + 1)]
        for rows, out in ((x_at[0], kept), (1 - x_at[0], given)):
            rows = pl.ds(pl.multiple_of(rows * half, half), half)
            total = parts[0][rows, :].astype(F32)
            for part in parts[1:]:
                total = total + part[rows, :].astype(F32)
            out[c] = total.astype(out.dtype)


def sum_z(x_at, chunks, *earlier):
    count = len(chunks)
    pair, columns = chunks[0][0].shape
    flat = [part for parts in chunks for part in parts]
    return pl.pallas_call(
        with_earlier(sum_z_kernel, 1 + len(flat), len(earlier)),
        in_specs=[smem_spec()] + [vmem_spec()] * len(flat) + any_specs(earlier),
        out_specs=[vmem_spec()] * 2,
        out_shape=[
            jax.ShapeDtypeStruct((count, pair // 2, columns), F32),
            jax.ShapeDtypeStruct((count, pair // 2, columns), BF16),
        ],
        compiler_params=pltpu.CompilerParams(vmem_limit_bytes=VMEM_BYTES),
        name="sum_z",
    )(x_at, *flat, *earlier)


def sum_parts_kernel(parts, out):
    total = parts[0].astype(F32)
    for c in range(1, parts.shape[0]):
        total = total + parts[c].astype(F32)
    out[...] = total.astype(BF16)


def sum_parts(parts, *earlier):
    chunks, tokens, width = parts.shape
    return pl.pallas_call(
        with_earlier(sum_parts_kernel, 1, len(earlier)),
        grid=(tokens // EXPERT_ROWS,),
        in_specs=[pl.BlockSpec((chunks, EXPERT_ROWS, width), lambda s: (0, s, 0))]
        + any_specs(earlier),
        out_specs=pl.BlockSpec((EXPERT_ROWS, width), lambda s: (s, 0)),
        out_shape=jax.ShapeDtypeStruct((tokens, width), BF16),
        compiler_params=pltpu.CompilerParams(vmem_limit_bytes=VMEM_BYTES),
        name="sum_parts",
    )(parts, *earlier)


def adam_experts_kernel(x_at, kept, got, *refs):
    states, outs = refs[:6], refs[6:]
    own = kept.shape[1]
    hidden = states[0].shape[3]
    mine = pl.program_id(0) // (pl.num_programs(0) // 2) == x_at[0]
    grad = jnp.where(mine, kept[0], got[0].astype(F32))
    for e in range(CHUNK):
        for part in range(2):
            first = hidden * (2 * e + part)
            results = adam_update(
                states[0][e, part], grad[:, first : first + hidden],
                states[1][e, part], states[2][e, part], MODEL_DIM ** (-0.5), WEIGHT_DECAY,
            )
            for out, result in zip(outs[:3], results):
                out[e, part] = result
        first = hidden * (2 * CHUNK + e)
        turned = grad[:, first : first + hidden].T
        results = adam_update(
            states[3][e], turned, states[4][e], states[5][e],
            max(1, F // 256) ** (-0.5), WEIGHT_DECAY,
        )
        for out, result in zip(outs[3:], results):
            out[e] = result


def adam_experts(x_at, kept, got, gateup, down):
    chunks, own, columns = kept.shape
    experts, hidden = down[0].shape[:2]
    share = pl.BlockSpec((1, own, columns), lambda j: (j % chunks, 0, 0))
    big = pl.BlockSpec((CHUNK, 2, own, hidden), lambda j: (j, 0, 0, 0))
    small = pl.BlockSpec((CHUNK, hidden, own), lambda j: (j, 0, 0))
    return pl.pallas_call(
        adam_experts_kernel,
        grid=(experts // CHUNK,),
        in_specs=[smem_spec(), share, share] + [big] * 3 + [small] * 3,
        out_specs=[big] * 3 + [small] * 3,
        out_shape=[jax.ShapeDtypeStruct(gateup[0].shape, F32)] * 3
        + [jax.ShapeDtypeStruct(down[0].shape, F32)] * 3,
        compiler_params=pltpu.CompilerParams(vmem_limit_bytes=VMEM_BYTES),
        name="adam_experts",
    )(x_at, kept, got, *gateup, *down)


def join_tokens_kernel(own, first, second, out, turned):
    half = own.shape[0] // 2
    for at, part in ((0, own[:half, :]), (half, own[half:, :]), (2 * half, first[...]), (3 * half, second[...])):
        out[at : at + half, :] = part
        turned[:, at : at + half] = part.T


def join_tokens(own, first, second, *earlier):
    tokens, width = own.shape
    return pl.pallas_call(
        with_earlier(join_tokens_kernel, 3, len(earlier)),
        in_specs=[vmem_spec()] * 3 + any_specs(earlier),
        out_specs=[vmem_spec()] * 2,
        out_shape=[
            jax.ShapeDtypeStruct((2 * tokens, width), own.dtype),
            jax.ShapeDtypeStruct((width, 2 * tokens), own.dtype),
        ],
        compiler_params=pltpu.CompilerParams(vmem_limit_bytes=VMEM_BYTES),
        name="join_tokens",
    )(own, first, second, *earlier)


def move(array, dz=0, dy=0, dx=0):
    total = lax.axis_size("dp")
    inner = total // 16
    pairs = []
    for at in range(16):
        z, y, x = at // 4, at // 2 % 2, at % 2
        to = ((z + dz) % 4) * 4 + (y ^ dy) * 2 + (x ^ dx)
        pairs += [(at * inner + i, to * inner + i) for i in range(inner)]
    return lax.ppermute(array, "dp", pairs)


def place():
    at = lax.axis_index("dp") // (lax.axis_size("dp") // 16)
    return at // 4, at // 2 % 2, at % 2


def inner_groups(total):
    inner = total // 16
    return [[at * inner + i for i in range(inner)] for at in range(16)]


def inner_gather(shard, axis):
    total = lax.axis_size("dp")
    if total == 16:
        return shard
    return lax.all_gather(
        shard, "dp", axis=axis, tiled=True, axis_index_groups=inner_groups(total)
    )


def inner_scatter(share, axis):
    total = lax.axis_size("dp")
    if total == 16:
        return share
    return lax.psum_scatter(
        share, "dp", scatter_dimension=axis, tiled=True, axis_index_groups=inner_groups(total)
    )


def block_rows(parts, rows):
    z, y, x = place()
    starts = []
    for dz, dy, dx in parts:
        starts.append((((z + dz + 4) % 4) * 4 + (y ^ dy) * 2 + (x ^ dx)) * rows)
    return jnp.stack(starts).astype(jnp.int32)


def gather_z(shard):
    return jnp.stack([shard] + [move(shard, dz=-dz) for dz in Z_FROM[1:]])


def gather_ring(shard):
    below, above = move(shard, dz=1), move(shard, dz=-1)
    return [shard, below, above, move(below, dz=1)]


def send_z(parts):
    return [move(parts[k].astype(BF16), dz=Z_FROM[k]) for k in range(1, SLOTS)]


def scatter_z(parts, moved=None):
    result = parts[0]
    for one in moved or send_z(parts):
        result = result + one.astype(F32)
    return result


def gather_plane(own):
    half = own.shape[-1] // 2
    along_y, along_x = move(own, dy=1), move(own, dx=1)
    both = (move(along_y[..., :half], dx=1), move(along_x[..., half:], dy=1))
    return own, along_y, along_x, *both


def scatter_plane(pieces):
    own, along_y, along_x, both_one, both_two = pieces
    half = both_one.shape[-1]
    got_one, got_two = move(both_one, dx=1), move(both_two, dy=1)
    pass_y = jnp.concatenate(
        [(along_y[..., :half].astype(F32) + got_one.astype(F32)).astype(BF16), along_y[..., half:]],
        axis=-1,
    )
    pass_x = jnp.concatenate(
        [along_x[..., :half], (along_x[..., half:].astype(F32) + got_two.astype(F32)).astype(BF16)],
        axis=-1,
    )
    got_y, got_x = move(pass_y, dy=1), move(pass_x, dx=1)
    return scatter_z(
        [
            own[k].astype(F32) + got_y[k].astype(F32) + got_x[k].astype(F32)
            for k in range(SLOTS)
        ]
    )


PLANE = [(dz, dy, dx) for dy, dx in ((0, 0), (1, 0), (0, 1), (1, 1)) for dz in Z_FROM]


def join_kernel(rows_at, *refs):
    pieces, out = refs[:-1], refs[-1]
    slots, own, width = pieces[0].shape
    half = width // 2
    for at in range(4 * slots):
        rows = pl.ds(pl.multiple_of(rows_at[at], own), own)
        group, slot = at // slots, at % slots
        if group < 3:
            out[rows, :] = pieces[group][slot]
        else:
            out[rows, :half] = pieces[3][slot]
            out[rows, half:] = pieces[4][slot]


def part_kernel(rows_at, whole, *pieces):
    slots, own, width = pieces[0].shape
    half = width // 2
    for at in range(4 * slots):
        rows = pl.ds(pl.multiple_of(rows_at[at], own), own)
        group, slot = at // slots, at % slots
        if group < 3:
            pieces[group][slot] = whole[rows, :]
        else:
            pieces[3][slot] = whole[rows, :half]
            pieces[4][slot] = whole[rows, half:]


def smem_spec():
    return pl.BlockSpec(memory_space=pltpu.SMEM)


def vmem_spec():
    return pl.BlockSpec(memory_space=pltpu.VMEM)


def join_blocks(rows_at, pieces, earlier=()):
    slots, own, width = pieces[0].shape
    return pl.pallas_call(
        with_earlier(join_kernel, 6, len(earlier)),
        in_specs=[smem_spec()] + [vmem_spec()] * 5 + any_specs(earlier),
        out_specs=vmem_spec(),
        out_shape=jax.ShapeDtypeStruct((4 * slots * own, width), BF16),
        compiler_params=pltpu.CompilerParams(vmem_limit_bytes=VMEM_BYTES),
        name="join_blocks",
    )(rows_at, *pieces, *earlier)


def part_blocks(rows_at, whole, earlier=()):
    own, width = whole.shape[0] // (4 * SLOTS), whole.shape[1]
    full = jax.ShapeDtypeStruct((SLOTS, own, width), BF16)
    half = jax.ShapeDtypeStruct((SLOTS, own, width // 2), BF16)
    return pl.pallas_call(
        with_earlier(part_kernel, 2, len(earlier)),
        in_specs=[smem_spec(), vmem_spec()] + any_specs(earlier),
        out_specs=[vmem_spec()] * 5,
        out_shape=[full] * 3 + [half] * 2,
        compiler_params=pltpu.CompilerParams(vmem_limit_bytes=VMEM_BYTES),
        name="part_blocks",
    )(rows_at, whole, *earlier)


def after(value, *earlier):
    marks = []
    for one in earlier:
        slots = one.shape[0] if one.shape[0] == SLOTS else 1
        lead, rest = (slots > 1) * 1, one.ndim - 1
        marks.append(lax.slice(one, (lead,) + (0,) * rest, (slots,) + (1,) * rest))
    return lax.optimization_barrier((value, *marks))[0]


def split_three(values):
    high = values.astype(BF16)
    rest = values - high.astype(F32)
    middle = rest.astype(BF16)
    low = (rest - middle.astype(F32)).astype(BF16)
    return [high, middle, low]


def swap_cores(part):
    return lax.ppermute(part, "tensor", [(0, 1), (1, 0)])


def pair_sum(part):
    return part.astype(F32) + swap_cores(part).astype(F32)


def norm_backward(values, inverse, gain_row, upstream):
    scaled = values * inverse
    weighted = upstream * gain_row
    mean_term = jnp.mean(weighted * scaled, axis=-1, keepdims=True)
    return (inverse * (weighted - scaled * mean_term), jnp.sum(upstream * scaled, axis=0))


def adam_update(value, gradient, mean_old, square_old, rate, decay):
    mean_new = FIRST_DECAY * mean_old + (1.0 - FIRST_DECAY) * gradient
    square_new = SECOND_DECAY * square_old + (1.0 - SECOND_DECAY) * gradient * gradient
    mean_hat = mean_new / (1.0 - FIRST_DECAY**STEP)
    square_hat = square_new / (1.0 - SECOND_DECAY**STEP)
    updated = value - rate * (mean_hat / (jnp.sqrt(square_hat) + ADAM_EPSILON) + decay * value)
    return (mean_new, square_new, updated)


def shards(
    hidden_in,
    out_grad,
    routes,
    segments,
    norm_gains,
    gains_mean,
    gains_square,
    w_query,
    query_mean,
    query_square,
    key_value_weight,
    key_value_first_moment,
    key_value_second_moment,
    w_out,
    out_mean,
    out_square,
    w_router,
    router_mean,
    router_square,
    w_gateup,
    gateup_mean,
    gateup_square,
    w_down,
    down_mean,
    down_square,
):
    tokens, width = hidden_in.shape
    own = w_query.shape[0]
    experts, hidden = w_down.shape[0], w_down.shape[1]
    q_width, kv_width = w_query.shape[1], key_value_weight.shape[2]
    qkv_width = q_width + 2 * kv_width
    each = 2 + experts
    half_experts = experts // 2
    block = width // 16
    z_at, y_at, x_at = place()
    core = lax.axis_index("tensor")
    plane_rows = block_rows(PLANE, block)
    qkv_shard = jnp.concatenate(
        [w_query.astype(BF16), key_value_weight[0].astype(BF16), key_value_weight[1].astype(BF16)]
        + split_three(jnp.concatenate([norm_gains.T, w_router], axis=1))
        + [jnp.zeros((own, LANES - 3 * each), BF16)],
        axis=1,
    )
    out_shard = w_out.T.astype(BF16)
    gateup_rows, down_rows = w_gateup, w_down
    if lax.axis_size("dp") > 16:
        gateup_rows = inner_gather(w_gateup.astype(BF16), 2)
        down_rows = inner_gather(w_down.astype(BF16), 2)
    chunks = experts // (2 * CHUNK)
    first = x_at == 0
    cosine, sine = rope_tables(seq_positions(segments))
    (
        qkv_blocks, out_blocks, small, normed_low, queries, keys, values, attended, lse,
        combine, combine_pair, middle, x_pair, x_turned, og_pair, og_turned, pairs, near, far,
    ) = forward_pass(
        inner_gather(qkv_shard, 0), inner_gather(out_shard, 0), gateup_rows, down_rows,
        hidden_in, out_grad, cosine, sine, segments, routes,
    )
    qkv_full = qkv_blocks.reshape(width, qkv_blocks.shape[2])[:, :qkv_width]
    output_full = out_blocks.reshape(width, q_width)
    gains_full, router_full = small[:2], small[2 : 2 + experts].T
    combine = combine[:, :experts]
    inputs = hidden_in.astype(F32)
    inverse_one = lax.rsqrt(jnp.mean(inputs * inputs, axis=-1, keepdims=True) + NORM_EPSILON)
    inverse_two = lax.rsqrt(jnp.mean(middle * middle, axis=-1, keepdims=True) + NORM_EPSILON)
    normed_two = middle * inverse_two * gains_full[1]

    def half_of(array, other=False):
        half = array.shape[0] // 2
        return lax.dynamic_slice_in_dim(array, half * ((1 - core) if other else core), half)

    def both_halves(mine):
        other = swap_cores(mine)
        lower = core == 0
        return jnp.where(lower, mine, other), jnp.where(lower, other, mine)

    dx, mix_pair, gate_turned, keep, z_got, near_grads, late_got, far_grad = experts_pass(
        x_pair, og_pair, x_turned, og_turned, combine_pair, pairs, near, far
    )
    z_parts = [[one] for one in keep]
    z_got = [[one[k] for k in range(SLOTS - 1)] for one in z_got]
    got_y = [late_got, move(far_grad, dy=1)]
    gate_grad = gate_turned.T

    def to_neighbour(part):
        both = half_of(part).astype(F32) + swap_cores(half_of(part, other=True)).astype(F32)
        return jnp.concatenate(both_halves(move(both.astype(BF16), dx=1)))

    normed_two_part = (dx[0].astype(F32) + dx[1].astype(F32)) + dx[2].astype(F32)

    logit_grad = combine * (gate_grad - jnp.sum(combine * gate_grad, axis=-1, keepdims=True))
    router_grad = jnp.dot(normed_two.T, logit_grad, precision=HIGHEST_PRECISION)
    normed_two_grad = normed_two_part + jnp.dot(
        logit_grad, router_full.T, precision=HIGHEST_PRECISION
    )
    middle_part, gain_two_grad = norm_backward(middle, inverse_two, gains_full[1], normed_two_grad)
    middle_grad = out_grad.astype(F32) + middle_part
    attention_back = (RESIDUAL_SCALE * middle_grad).astype(BF16)
    attended_grad = jnp.dot(attention_back, output_full, preferred_element_type=F32).astype(BF16)
    output_weight_grad = lax.dot_general(attention_back, attended, TN, preferred_element_type=F32)
    output_share = scatter_plane(
        part_blocks(plane_rows, output_weight_grad.astype(BF16))
    )
    query_grad, keyval_grad = attention_backward(
        queries, keys, values, attended, attended_grad, cosine, sine, segments, lse,
    )
    for c in range(chunks - SENT):
        waits = z_got[-1] if c > 0 else ()
        z_parts.append(sum_y(near_grads[c], got_y[c], *waits))
        z_got.append(send_z(z_parts[-1]))
    qkv_grad = jnp.concatenate([query_grad, keyval_grad], axis=1)
    qkv_weight_grad = lax.dot_general(normed_low, qkv_grad, TN, preferred_element_type=F32)
    qkv_parts = part_blocks(
        plane_rows,
        jnp.concatenate(
            [
                qkv_weight_grad.astype(BF16),
                gain_two_grad[:, None].astype(BF16),
                router_grad.astype(BF16),
                jnp.zeros((width, 2 * LANES - 1 - experts), BF16),
            ],
            axis=1,
        ),
    )
    qkv_share = scatter_plane(qkv_parts)
    normed_part = lax.dot_general(qkv_grad, qkv_full, NT, preferred_element_type=F32)
    normed_grad = pair_sum(normed_part.astype(BF16))
    scaled = inputs * inverse_one
    weighted = normed_grad * gains_full[0]
    mean_term = jnp.mean(weighted * scaled, axis=-1, keepdims=True)
    input_grad = middle_grad + inverse_one * (weighted - scaled * mean_term)

    mix_pair = fence(mix_pair, qkv_parts[0])
    expert_mix = pair_sum(mix_pair[:tokens]) + to_neighbour(mix_pair[tokens:]).astype(F32)
    block_out = (middle + RESIDUAL_SCALE * expert_mix).astype(BF16)
    kept_shares, got_shares = [], []
    x_here = x_at.astype(jnp.int32)[None]
    for low in range(0, chunks, 2):
        kept_share, given_share = sum_z(
            x_here,
            [[z_parts[c][0], *z_got[c]] for c in range(low, low + 2)],
            query_grad,
        )
        kept_shares.append(kept_share)
        got_shares.append(move(given_share, dx=1))
    kept_share = inner_scatter(jnp.concatenate(kept_shares), 1)
    got_share = inner_scatter(jnp.concatenate(got_shares), 1)

    output_share = inner_scatter(output_share, 0).T
    qkv_share = inner_scatter(qkv_share, 0)
    query_share = qkv_share[:, :q_width]
    keyval_share = jnp.stack(
        [qkv_share[:, q_width : q_width + kv_width], qkv_share[:, q_width + kv_width : qkv_width]]
    )
    gain_one_part = jnp.sum(w_query.astype(BF16).astype(F32) * query_share, axis=1) + jnp.sum(
        key_value_weight.astype(BF16).astype(F32) * keyval_share, axis=(0, 2)
    )
    gain_one_share = pair_sum(gain_one_part[None, :]) / norm_gains[:1]
    gains_share = jnp.concatenate([gain_one_share, qkv_share[:, qkv_width][None, :]])
    router_share = qkv_share[:, qkv_width + 1 : qkv_width + 1 + experts]

    gains_result = adam_update(norm_gains, gains_share, gains_mean, gains_square, GAIN_RATE, 0.0)
    query_result = adam_update(
        w_query, query_share, query_mean, query_square, (MODEL_DIM // 12) ** (-0.5), WEIGHT_DECAY
    )
    keyval_result = adam_update(
        key_value_weight,
        keyval_share,
        key_value_first_moment,
        key_value_second_moment,
        (MODEL_DIM // 12) ** (-0.5),
        WEIGHT_DECAY,
    )
    out_result = adam_update(
        w_out,
        output_share,
        out_mean,
        out_square,
        max(1, QUERY_HEADS * HEAD_DIM // 96) ** (-0.5),
        WEIGHT_DECAY,
    )
    router_result = adam_update(
        w_router, router_share, router_mean, router_square, (4 * MODEL_DIM) ** (-0.5), WEIGHT_DECAY
    )
    expert_results = adam_experts(
        x_here, kept_share, got_share,
        (w_gateup, gateup_mean, gateup_square), (w_down, down_mean, down_square),
    )
    return (
        (block_out, input_grad)
        + gains_result
        + query_result
        + keyval_result
        + out_result
        + router_result
        + tuple(expert_results)
    )


def solution(mesh):
    tokens, gains = P("dp", None), P(None, "dp")
    query, keyval, out = P("dp", "tensor"), P(None, "dp", "tensor"), P("tensor", "dp")
    router, gateup, down = P("dp", None), P(None, None, "dp", "tensor"), P(None, "tensor", "dp")
    states = tuple(
        spec for one in (gains, query, keyval, out, router, gateup, down) for spec in (one,) * 3
    )
    return jax.shard_map(
        shards,
        mesh=mesh,
        in_specs=(tokens, tokens, tokens, P("dp")) + states,
        out_specs=(tokens, tokens) + states,
        check_vma=False,
    )
```

```python
import functools

import jax
import jax.numpy as jnp
from jax import lax
from jax.experimental import pallas as pl
from jax.experimental.pallas import tpu as pltpu
from jax.sharding import PartitionSpec as P

MODEL_DIM = 1536
QUERY_HEADS = 24
HEAD_DIM = 64
F = 512
SEQUENCE_LENGTH = 1024
STEP = 10

NORM_EPSILON = 1e-06
SCORE_SCALE = 0.015625
RESIDUAL_SCALE = 0.22
ROPE_BASE = 10000.0
FIRST_DECAY = 0.9
SECOND_DECAY = 0.95
ADAM_EPSILON = 1e-08
WEIGHT_DECAY = 0.1
GAIN_RATE = 0.6
MASK_VALUE = -1e30
HIGHEST_PRECISION = lax.Precision.HIGHEST

BF16 = jnp.bfloat16
F32 = jnp.float32
LANES = 128
ROWS = 256
VMEM_BYTES = 58 * 1024 * 1024

NN = (((1,), (0,)), ((), ()))
NT = (((1,), (1,)), ((), ()))
TN = (((0,), (0,)), ((), ()))


def dot(a, b, dims=NN):
    return lax.dot_general(a, b, dims, preferred_element_type=F32)


def seq_positions(segment_row):
    counter = jnp.arange(segment_row.shape[0], dtype=jnp.int32)
    earlier = jnp.concatenate([segment_row[:1] - 1, segment_row[:-1]])
    starts = lax.cummax(jnp.where(segment_row != earlier, counter, 0), axis=0)
    return counter - starts


def rope_tables(positions):
    half_width = HEAD_DIM // 2
    frequency = ROPE_BASE ** (-2.0 * jnp.arange(half_width, dtype=F32) / HEAD_DIM)
    angles = positions.astype(F32)[:, None] * frequency[None, :]
    cosine, sine = jnp.cos(angles), jnp.sin(angles)
    return (
        jnp.concatenate([cosine] * 4, axis=1),
        jnp.concatenate([-sine, sine] * 2, axis=1),
    )


def rotate_halves(slab):
    lane = lax.broadcasted_iota(jnp.int32, slab.shape, 1)
    ahead = pltpu.roll(slab, LANES - HEAD_DIM // 2, 1)
    behind = pltpu.roll(slab, HEAD_DIM // 2, 1)
    return jnp.where(lane % HEAD_DIM < HEAD_DIM // 2, ahead, behind)


def half_mask(rows, upper):
    lane = lax.broadcasted_iota(jnp.int32, (rows, LANES), 1)
    return (lane >= HEAD_DIM) if upper else (lane < HEAD_DIM)


def spread_heads(slab, lower_out, upper_out, index):
    rows = slab.shape[0]
    moved = pltpu.roll(slab.astype(F32), HEAD_DIM, 1).astype(BF16)
    zero = jnp.zeros_like(slab)
    low, high = half_mask(rows, False), half_mask(rows, True)
    lower_out[index] = jnp.where(low, slab, zero)
    upper_out[index] = jnp.where(high, moved, zero)
    lower_out[index + 1] = jnp.where(low, moved, zero)
    upper_out[index + 1] = jnp.where(high, slab, zero)


def fill_bias(bias, seg_col, seg_row):
    span = bias.shape[0]
    for at in range(0, span, ROWS):
        rows_at = at + lax.broadcasted_iota(jnp.int32, (ROWS, span), 0)
        cols_at = lax.broadcasted_iota(jnp.int32, (ROWS, span), 1)
        allowed = (rows_at >= cols_at) & (seg_col[at : at + ROWS, :] == seg_row[...])
        bias[at : at + ROWS, :] = jnp.where(allowed, 0.0, MASK_VALUE).astype(F32)


def with_earlier(kernel, inputs, count):
    def run(*refs):
        kernel(*refs[:inputs], *refs[inputs + count :])

    return run


def any_specs(arrays):
    return [pl.BlockSpec(memory_space=pl.ANY)] * len(arrays)


def attention_forward_kernel(
    lin_ref, kv_ref, cos_ref, sin_ref, seg_col, seg_row,
    out_ref, q_ref, k_ref, v_ref, lse_ref,
    bias, k_low, k_high, v_low, v_high,
):
    slab_at = pl.program_id(0)
    span = lin_ref.shape[0]
    kv_slabs = kv_ref.shape[1] // (2 * LANES)

    @pl.when(slab_at == 0)
    def _():
        fill_bias(bias, seg_col, seg_row)
        for j in range(kv_slabs):
            lanes = slice(j * LANES, (j + 1) * LANES)
            lin = kv_ref[:, lanes]
            keys = (lin * cos_ref[...] + rotate_halves(lin) * sin_ref[...]).astype(BF16)
            k_ref[:, lanes] = keys
            spread_heads(keys, k_low, k_high, 2 * j)
            lanes = slice((kv_slabs + j) * LANES, (kv_slabs + j + 1) * LANES)
            values = kv_ref[:, lanes].astype(BF16)
            v_ref[:, slice(j * LANES, (j + 1) * LANES)] = values
            spread_heads(values, v_low, v_high, 2 * j)

    lin = lin_ref[...]
    q_ref[...] = (lin * cos_ref[...] + rotate_halves(lin) * sin_ref[...]).astype(BF16)
    kv_even, kv_odd = (2 * slab_at) // 3, (2 * slab_at + 1) // 3
    for at in range(0, span, ROWS):
        rows = slice(at, at + ROWS)
        queries = q_ref[rows, :]
        total = None
        stats = []
        for keys, values, kv_at in ((k_low, v_low, kv_even), (k_high, v_high, kv_odd)):
            upto = at + ROWS
            scores = dot(queries, keys[kv_at, :upto, :], NT) * SCORE_SCALE + bias[rows, :upto]
            highest = jnp.max(scores, axis=1, keepdims=True)
            weights = jnp.exp(scores - highest)
            summed = jnp.sum(weights, axis=1, keepdims=True)
            probability = (weights * (1.0 / summed)).astype(BF16)
            part = dot(probability, values[kv_at, :upto, :])
            total = part if total is None else total + part
            stats.append(highest + jnp.log(summed))
        out_ref[rows, :] = total.astype(BF16)
        spread = jnp.where(half_mask(ROWS, False), stats[0], stats[1])
        turned = spread.T
        lse_ref[0, 0:1, rows] = turned[0:1, :]
        lse_ref[0, 1:2, rows] = turned[HEAD_DIM : HEAD_DIM + 1, :]


def attention_forward(qkv_lin, cosine, sine, segment_row, earlier=()):
    span = qkv_lin.shape[0]
    q_width = MODEL_DIM // 2
    kv_width = (qkv_lin.shape[1] - q_width) // 2
    slabs, kv_heads = q_width // LANES, kv_width // HEAD_DIM
    whole = lambda shape: pl.BlockSpec(shape, lambda g: (0,) * len(shape))
    slab = pl.BlockSpec((span, LANES), lambda g: (0, g))
    q_lin, kv_lin = qkv_lin[:, :q_width], qkv_lin[:, q_width:]
    return pl.pallas_call(
        with_earlier(attention_forward_kernel, 6, len(earlier)),
        grid=(slabs,),
        in_specs=[
            slab, whole((span, 2 * kv_width)), whole((span, LANES)), whole((span, LANES)),
            whole((span, 1)), whole((1, span)),
        ]
        + any_specs(earlier),
        out_specs=[
            slab, slab, whole((span, kv_width)), whole((span, kv_width)),
            pl.BlockSpec((1, 8, span), lambda g: (g, 0, 0)),
        ],
        out_shape=[
            jax.ShapeDtypeStruct((span, q_width), BF16),
            jax.ShapeDtypeStruct((span, q_width), BF16),
            jax.ShapeDtypeStruct((span, kv_width), BF16),
            jax.ShapeDtypeStruct((span, kv_width), BF16),
            jax.ShapeDtypeStruct((slabs, 8, span), F32),
        ],
        scratch_shapes=[pltpu.VMEM((span, span), F32)]
        + [pltpu.VMEM((kv_heads, span, LANES), BF16)] * 4,
        compiler_params=pltpu.CompilerParams(vmem_limit_bytes=VMEM_BYTES),
        cost_estimate=pl.CostEstimate(
            flops=32 * slabs * span * span * LANES, bytes_accessed=16 * span * q_width,
            transcendentals=slabs * span * span,
        ),
        name="attention_forward",
    )(q_lin, kv_lin, cosine, sine, segment_row[:, None], segment_row[None, :], *earlier)


def attention_backward_kernel(
    q_ref, k_ref, v_ref, out_ref, grad_ref, cos_ref, sin_ref, seg_col, seg_row, lse_ref,
    dq_ref, dkv_ref,
    bias, k_low, k_high, v_low, v_high, dk_low, dk_high, dv_low, dv_high, dq_sum,
):
    slab_at = pl.program_id(0)
    span = q_ref.shape[0]
    kv_slabs = k_ref.shape[1] // LANES

    @pl.when(slab_at == 0)
    def _():
        for at in range(0, span, ROWS):
            keys_at = at + lax.broadcasted_iota(jnp.int32, (ROWS, span), 0)
            rows_at = lax.broadcasted_iota(jnp.int32, (ROWS, span), 1)
            allowed = (rows_at >= keys_at) & (seg_col[at : at + ROWS, :] == seg_row[...])
            bias[at : at + ROWS, :] = jnp.where(allowed, 0.0, MASK_VALUE).astype(F32)
        for j in range(kv_slabs):
            lanes = slice(j * LANES, (j + 1) * LANES)
            spread_heads(k_ref[:, lanes], k_low, k_high, 2 * j)
            spread_heads(v_ref[:, lanes], v_low, v_high, 2 * j)
        for sums in (dk_low, dk_high, dv_low, dv_high):
            sums[...] = jnp.zeros_like(sums)

    kv_even, kv_odd = (2 * slab_at) // 3, (2 * slab_at + 1) // 3
    for at in range(0, span, ROWS):
        rows = slice(at, at + ROWS)
        upto = at + ROWS
        queries, grads = q_ref[rows, :], grad_ref[rows, :]
        turned = (grads.astype(F32) * out_ref[rows, :].astype(F32)).T
        zero = jnp.zeros_like(queries)
        dq_part = None
        for upper, keys, values, dk_sum, dv_sum, kv_at in (
            (False, k_low, v_low, dk_low, dv_low, kv_even),
            (True, k_high, v_high, dk_high, dv_high, kv_odd),
        ):
            first = HEAD_DIM if upper else 0
            delta = jnp.sum(turned[first : first + HEAD_DIM, :], axis=0, keepdims=True)
            head = 1 if upper else 0
            total = lse_ref[0, head : head + 1, rows]
            keys_here = keys[kv_at, :upto, :]
            scores = dot(keys_here, queries, NT) * SCORE_SCALE + bias[:upto, rows]
            probability = jnp.exp(scores - total)
            prob_grad = dot(values[kv_at, :upto, :], grads, NT)
            score_grad = (probability * (prob_grad - delta)).astype(BF16)
            mask = half_mask(ROWS, upper)
            dv_sum[kv_at, :upto, :] += dot(
                probability.astype(BF16), jnp.where(mask, grads, zero)
            )
            dk_sum[kv_at, :upto, :] += dot(score_grad, jnp.where(mask, queries, zero))
            part = dot(score_grad, keys_here, TN)
            dq_part = part if dq_part is None else dq_part + part
        dq_sum[rows, :] = dq_part * SCORE_SCALE
    slab = dq_sum[...]
    dq_ref[...] = (slab * cos_ref[...] - rotate_halves(slab) * sin_ref[...]).astype(BF16)

    @pl.when(slab_at == pl.num_programs(0) - 1)
    def _():
        low = half_mask(span, False)

        def joined(sums_low, sums_high, j):
            one = sums_low[2 * j] + pltpu.roll(sums_high[2 * j], HEAD_DIM, 1)
            two = pltpu.roll(sums_low[2 * j + 1], HEAD_DIM, 1) + sums_high[2 * j + 1]
            return jnp.where(low, one, two)

        for j in range(kv_slabs):
            slab = joined(dk_low, dk_high, j) * SCORE_SCALE
            dkv_ref[:, j * LANES : (j + 1) * LANES] = (
                slab * cos_ref[...] - rotate_halves(slab) * sin_ref[...]
            ).astype(BF16)
            at = (kv_slabs + j) * LANES
            dkv_ref[:, at : at + LANES] = joined(dv_low, dv_high, j).astype(BF16)


def attention_backward(
    queries, keys, values, attended, grad, cosine, sine, segment_row, lse, earlier=()
):
    span, q_width = queries.shape
    kv_width = keys.shape[1]
    slabs, kv_heads = q_width // LANES, kv_width // HEAD_DIM
    whole = lambda shape: pl.BlockSpec(shape, lambda g: (0,) * len(shape))
    slab = pl.BlockSpec((span, LANES), lambda g: (0, g))
    return pl.pallas_call(
        with_earlier(attention_backward_kernel, 10, len(earlier)),
        grid=(slabs,),
        in_specs=[
            slab, whole((span, kv_width)), whole((span, kv_width)), slab, slab,
            whole((span, LANES)), whole((span, LANES)), whole((span, 1)), whole((1, span)),
            pl.BlockSpec((1, 8, span), lambda g: (g, 0, 0)),
        ]
        + any_specs(earlier),
        out_specs=[slab, whole((span, 2 * kv_width))],
        out_shape=[
            jax.ShapeDtypeStruct((span, q_width), BF16),
            jax.ShapeDtypeStruct((span, 2 * kv_width), BF16),
        ],
        scratch_shapes=[pltpu.VMEM((span, span), F32)]
        + [pltpu.VMEM((kv_heads, span, LANES), BF16)] * 4
        + [pltpu.VMEM((kv_heads, span, LANES), F32)] * 4
        + [pltpu.VMEM((span, LANES), F32)],
        compiler_params=pltpu.CompilerParams(vmem_limit_bytes=VMEM_BYTES),
        cost_estimate=pl.CostEstimate(
            flops=40 * slabs * span * span * LANES, bytes_accessed=16 * span * q_width,
            transcendentals=slabs * span * span,
        ),
        name="attention_backward",
    )(
        queries, keys, values, attended, grad, cosine, sine,
        segment_row[:, None], segment_row[None, :], lse, *earlier,
    )


EXPERT_ROWS = 256
EXPERT_VMEM = 63 * 1024 * 1024
SLOTS = 4
Z_FROM = (0, -1, 1, 2)
CHUNK = 2
LATE = 2
SENT = 2
MESH_ID = pl.DeviceIdType.MESH


def experts_kernel(
    inner, chunks, row_steps, x_ref, og_ref, xt_ref, ogt_ref, combine_ref,
    pairs_ref, near_ref, far_ref,
    dx_own, dx_twin, dx_other, mix_out, gate_out, *refs,
):
    keep_outs, refs = refs[:SENT], refs[SENT:]
    part_outs, refs = refs[:SENT], refs[SENT:]
    near_outs, refs = refs[: chunks - SENT], refs[chunks - SENT :]
    late_out, far_out, refs = refs[0], refs[1], refs[2:]
    slots, arrived, held_both, held_down, dx_sum, mix_sum, twin_rows = refs[:7]
    gates, gate_kept, gate_got, gate_full, gate_twin, send, recv, local = refs[7:]
    weights, grads = slots.at[pl.ds(1, chunks)], slots
    near = Neighbours(inner)
    copies = Copies(send, recv, local)
    z, y, x, core, spots = near.z, near.y, near.x, near.core, near.spots
    step = pl.program_id(0)
    steps = row_steps + SLOTS
    chunk, turn = step // steps, step % steps
    last = chunks - 1
    width = x_ref.shape[1]
    block = width // 16
    hidden = held_down.shape[1] // CHUNK
    both = 2 * hidden * CHUNK
    lane = lax.broadcasted_iota(jnp.int32, (EXPERT_ROWS, LANES), 1)
    tokens = dx_sum.shape[0] // 2
    tiles = tokens // EXPERT_ROWS
    tile = (turn + tiles) % row_steps
    rows = pl.ds(pl.multiple_of(tile * EXPERT_ROWS, EXPERT_ROWS), EXPERT_ROWS)

    def near_piece(c, k):
        return pairs_ref.at[c] if k == 0 else near_ref.at[c, k - 1]

    def near_copy(c, k):
        copies.copy(
            lambda c=c, k=k: (near_piece(c, k), weights.at[c, spots[k], y]), ("near", c, k), False
        )

    def near_wait(c, k):
        copies.wait_copy(
            lambda c=c, k=k: (near_piece(c, k), weights.at[c, spots[k], y]), ("near", c, k)
        )

    def far_ends(c, k):
        return far_ref.at[c, k], weights.at[c, spots[k], 1 - y]

    @pl.when(step == 0)
    def _():
        near.greet()
        gates[...] = jnp.zeros_like(gates)
        for k in range(SLOTS):
            near_copy(0, k)
            copies.copy(lambda k=k: far_ends(0, k), ("far", 0, k), False)
        copies.remote(
            lambda: (pairs_ref.at[last], weights.at[last, z, y]), ("y",), ("y",), near.over_y
        )
        for k in range(1, SLOTS):
            copies.remote(
                lambda: (pairs_ref.at[last], weights.at[last, z, y]),
                ("z", k), ("z", BACK[k]), near.along[k],
            )
        for c in range(LATE, last):
            for k in range(SLOTS):
                copies.remote(
                    lambda c=c, k=k: (near_piece(c, k), weights.at[c, spots[k], y]),
                    ("f", c, k), ("f", c, k), near.over_y,
                )
        for c in range(1, chunks):
            for k in range(SLOTS if c < last else 1):
                near_copy(c, k)
                if c < LATE:
                    copies.copy(lambda c=c, k=k: far_ends(c, k), ("far", c, k), False)

    @pl.when(step == row_steps)
    def _():
        copies.arrived(weights.at[last, z, 1 - y], ("y",), near.over_y)
        for k in range(1, SLOTS):
            copies.remote(
                lambda: (weights.at[last, z, 1 - y],) * 2,
                ("z2", k), ("z2", BACK[k]), near.along[k],
            )

    for c in range(chunks):

        @pl.when(step == c * steps)
        def _():
            for k in range(SLOTS):
                if c < last or k == 0:
                    near_wait(c, k)
                if c < LATE:
                    copies.wait_copy(lambda c=c, k=k: far_ends(c, k), ("far", c, k))
                elif c < last:
                    copies.arrived(weights.at[c, spots[k], 1 - y], ("f", c, k), near.over_y)
                elif k > 0:
                    copies.arrived(weights.at[c, spots[k], y], ("z", k), near.along[k])
                    copies.arrived(weights.at[c, spots[k], 1 - y], ("z2", k), near.along[k])

    def add_arrived(c):
        copies.arrived(arrived.at[c], ("sum", c), near.over_y)
        for k in range(SLOTS):
            own = grads.at[c, spots[k], y]
            own[...] = (own[...].astype(F32) + arrived[c, spots[k]].astype(F32)).astype(BF16)
        copies.copy(lambda c=c: (grads.at[c, z, y], keep_outs[c]), ("keep", c))
        for k in range(1, SLOTS):
            copies.remote(
                lambda c=c, k=k: (grads.at[c, spots[k], y], part_outs[c].at[BACK[k] - 1]),
                ("part", c, k), ("part", c, BACK[k]), near.along[k],
            )

    @pl.when(step == 2 * steps + row_steps - 2)
    def _():
        add_arrived(0)

    @pl.when(step == 3 * steps + 4)
    def _():
        add_arrived(1)

    @pl.when(turn < row_steps)
    def _():
        for e in range(CHUNK):
            first = 2 * hidden * e
            w_both = weights[chunk, :, :, :, first : first + 2 * hidden].reshape(width, 2 * hidden)
            start = both + hidden * e
            w_down = weights[chunk, :, :, :, start : start + hidden].reshape(width, hidden)
            gate_up = dot(x_ref[...], w_both)
            raw = dot(og_ref[...], w_down) * RESIDUAL_SCALE
            gate, up = gate_up[:, :hidden], gate_up[:, hidden:]
            gate_lane = lax.broadcasted_iota(
                jnp.int32, (EXPERT_ROWS, combine_ref.shape[1]), 1
            )
            column = jnp.sum(
                jnp.where(gate_lane == chunk * CHUNK + e, combine_ref[...], 0.0),
                axis=1, keepdims=True,
            )
            sigmoid = 1.0 / (1.0 + jnp.exp(-gate))
            active = gate * sigmoid
            inner_value = (active * up).astype(BF16).astype(F32)
            held_down[rows, hidden * e : hidden * (e + 1)] = (inner_value * column).astype(BF16)
            gates[rows, :] = jnp.where(
                lane == chunk * CHUNK + e,
                jnp.sum(inner_value * raw, axis=1, keepdims=True),
                gates[rows, :],
            )
            inner_grad = raw * column
            held_both[rows, first : first + hidden] = (
                inner_grad * up * sigmoid * (1.0 + gate * (1.0 - sigmoid))
            ).astype(BF16)
            held_both[rows, first + hidden : first + 2 * hidden] = (inner_grad * active).astype(BF16)

        def sums(add):
            for part in range(SLOTS):
                cols = slice(4 * block * part, 4 * block * (part + 1))
                w_both = weights[chunk, part, :, :, :both].reshape(4 * block, both)
                w_down = weights[chunk, part, :, :, both:].reshape(4 * block, hidden * CHUNK)
                mix = dot(held_down[rows, :], w_down, NT)
                dx = dot(held_both[rows, :], w_both, NT)
                if add:
                    mix = mix + mix_sum[rows, cols].astype(F32)
                    dx = dx + dx_sum[rows, cols].astype(F32)
                mix_sum[rows, cols] = mix.astype(BF16)
                dx_sum[rows, cols] = dx.astype(BF16)

        @pl.when(chunk == 0)
        def _():
            sums(False)

        @pl.when(chunk > 0)
        def _():
            sums(True)

    @pl.when(turn >= row_steps)
    def _():
        part = turn - row_steps
        grads[chunk, part, :, :, :both] = (
            dot(xt_ref[...], held_both[...]).astype(BF16).reshape(2, 2 * block, both)
        )
        grads[chunk, part, :, :, both:] = (
            (dot(ogt_ref[...], held_down[...]) * RESIDUAL_SCALE)
            .astype(BF16)
            .reshape(2, 2 * block, hidden * CHUNK)
        )

    begin = last * steps
    for i in range(2):
        for c in range(2):
            mine = pl.ds(tokens + (2 * c + i) * EXPERT_ROWS, EXPERT_ROWS)
            there = pl.ds((2 * c + i) * EXPERT_ROWS, EXPERT_ROWS)

            @pl.when((step == begin + 2 * c + i) & (core != c))
            def _():
                copies.remote(
                    lambda: (dx_sum.at[mine], twin_rows.at[i]), ("t", i), ("t", i), near.twin,
                    last=False,
                )

            @pl.when((step == begin + 2 + 2 * c + i) & (core == c))
            def _():
                copies.arrived(twin_rows.at[i], ("t", i), near.twin)
                dx_sum[mine, :] = (
                    dx_sum[mine, :].astype(F32) + twin_rows[i].astype(F32)
                ).astype(BF16)
                copies.remote(
                    lambda: (dx_sum.at[mine], dx_other.at[there]), ("o", i), ("o", i), near.over_x,
                    last=False,
                )

            @pl.when((step == begin + steps - 2 + i) & (core == c))
            def _():
                copies.arrived(dx_other.at[there], ("o", i), near.over_x)
                copies.remote(
                    lambda: (dx_other.at[there],) * 2, ("o2", i), ("o2", i), near.twin, last=False
                )

    for i in range(tiles):

        @pl.when(step == begin + tiles + i)
        def _():
            own = pl.ds(i * EXPERT_ROWS, EXPERT_ROWS)
            copies.copy(lambda own=own: (dx_sum.at[own], dx_own.at[own]), ("own", i))
            copies.remote(
                lambda own=own: (dx_sum.at[own], dx_twin.at[own]), ("own", i), ("own", i), near.twin
            )

    shares = gate_kept.shape[0]

    @pl.when(step == begin + row_steps)
    def _():
        copies.copy(lambda: (mix_sum, mix_out), "mix")
        turned = gates[...].T[:shares, :]
        gate_kept[...] = turned
        copies.remote(
            lambda: (gate_kept.at[:, pl.ds(tokens, tokens)], gate_got), ("g",), ("g",), near.over_x
        )

    @pl.when(step == begin + steps - 2)
    def _():
        copies.arrived(gate_got, ("g",), near.over_x)
        gate_full[pl.ds(pl.multiple_of(x * shares, shares), shares), :] = gate_kept[:, :tokens]
        gate_full[pl.ds(pl.multiple_of((1 - x) * shares, shares), shares), :] = gate_got[...]
        copies.remote(lambda: (gate_full, gate_twin), ("g2",), ("g2",), near.twin)

    for c in range(chunks):

        @pl.when(step == (c + 1) * steps - 1)
        def _():
            if c < SENT:
                copies.remote(
                    lambda c=c: (grads.at[c, :, 1 - y], arrived.at[c]),
                    ("sum", c), ("sum", c), near.over_y,
                )
            else:
                for k in range(SLOTS):
                    copies.copy(
                        lambda c=c, k=k: (grads.at[c, spots[k], y], near_outs[c - SENT].at[k]),
                        ("near out", c, k),
                    )
                    if c < last:
                        copies.remote(
                            lambda c=c, k=k: (grads.at[c, spots[k], 1 - y], late_out.at[k]),
                            ("late", k), ("late", k), near.over_y,
                        )
                    else:
                        copies.copy(
                            lambda c=c, k=k: (grads.at[c, spots[k], 1 - y], far_out.at[k]),
                            ("far out", k),
                        )

    @pl.when(step == chunks * steps - 1)
    def _():
        copies.arrived(gate_twin, ("g2",), near.twin)
        gate_out[...] = gate_full[...] + gate_twin[...]
        for i in range(tiles):
            copies.arrived(
                dx_twin.at[pl.ds(i * EXPERT_ROWS, EXPERT_ROWS)], ("own", i), near.twin
            )
        for i in range(2):
            for c in range(2):
                mine = pl.ds(tokens + (2 * c + i) * EXPERT_ROWS, EXPERT_ROWS)
                there = pl.ds((2 * c + i) * EXPERT_ROWS, EXPERT_ROWS)

                @pl.when(core != c)
                def _():
                    copies.sent(lambda: (dx_sum.at[mine], twin_rows.at[i]), ("t", i), near.twin)
                    copies.arrived(dx_other.at[there], ("o2", i), near.twin)

                @pl.when(core == c)
                def _():
                    copies.sent(
                        lambda: (dx_sum.at[mine], dx_other.at[there]), ("o", i), near.over_x
                    )
                    copies.sent(lambda: (dx_other.at[there],) * 2, ("o2", i), near.twin)

        for c in range(SENT):
            for k in range(1, SLOTS):
                copies.arrived(part_outs[c].at[k - 1], ("part", c, k), near.along[k])
        for k in range(SLOTS):
            copies.arrived(late_out.at[k], ("late", k), near.over_y)
        copies.finish()


def experts_pass(x, og, xt, ogt, combine, pairs, near, far):
    tokens, width = x.shape
    chunks, pair, columns = pairs.shape
    hidden = columns // (3 * CHUNK)
    shares = chunks * CHUNK
    row_steps = tokens // EXPERT_ROWS
    steps = row_steps + SLOTS
    inner = lax.axis_size("dp") // 16
    row_at = lambda s: ((jnp.minimum(s % steps, row_steps - 1) + row_steps // 2) % row_steps, 0)
    width_at = lambda s: (jnp.maximum(s % steps - row_steps, 0), 0)
    row = pl.BlockSpec((EXPERT_ROWS, width), row_at)
    turned = pl.BlockSpec((width // SLOTS, tokens), width_at)
    anywhere = pl.BlockSpec(memory_space=pl.ANY)
    left = chunks - SENT
    dma = pltpu.SemaphoreType.DMA
    shape = jax.ShapeDtypeStruct
    outs = pl.pallas_call(
        functools.partial(experts_kernel, inner, chunks, row_steps),
        grid=(chunks * steps,),
        in_specs=[row, row, turned, turned, pl.BlockSpec((EXPERT_ROWS, combine.shape[1]), row_at)]
        + [anywhere] * 3,
        out_specs=[anywhere] * 4
        + [pl.BlockSpec((2 * shares, tokens // 2), lambda s: (0, 0))]
        + [anywhere] * (2 * SENT + left + 2),
        out_shape=[shape((tokens // 2, width), BF16)] * 3
        + [shape((tokens, width), BF16), shape((2 * shares, tokens // 2), F32)]
        + [shape((pair, columns), BF16)] * SENT
        + [shape((SLOTS - 1, pair, columns), BF16)] * SENT
        + [shape((SLOTS, pair, columns), BF16)] * (left + 2),
        scratch_shapes=[
            pltpu.VMEM((chunks + 1, SLOTS, 2, pair, columns), BF16),
            pltpu.VMEM((SENT, SLOTS, pair, columns), BF16),
            pltpu.VMEM((tokens, 2 * hidden * CHUNK), BF16),
            pltpu.VMEM((tokens, hidden * CHUNK), BF16),
            pltpu.VMEM((tokens, width), BF16),
            pltpu.VMEM((tokens, width), BF16),
            pltpu.VMEM((2, EXPERT_ROWS, width), BF16),
            pltpu.VMEM((tokens, LANES), F32),
            pltpu.VMEM((shares, tokens), F32),
            pltpu.VMEM((shares, tokens // 2), F32),
            pltpu.VMEM((2 * shares, tokens // 2), F32),
            pltpu.VMEM((2 * shares, tokens // 2), F32),
            dma((48,)), dma((48,)), dma((48,)),
        ],
        compiler_params=pltpu.CompilerParams(
            vmem_limit_bytes=EXPERT_VMEM, collective_id=0, has_side_effects=True
        ),
        cost_estimate=pl.CostEstimate(
            flops=8 * tokens * width * chunks * columns,
            bytes_accessed=2 * chunks * width * columns, transcendentals=0,
        ),
        name="experts_pass",
    )(x, og, xt, ogt, combine, pairs, near, far)
    dx, mix, gate = outs[:3], outs[3], outs[4]
    rest = outs[5:]
    keep, parts, rest = rest[:SENT], rest[SENT : 2 * SENT], rest[2 * SENT :]
    return dx, mix, gate, keep, parts, rest[:left], rest[left], rest[left + 1]


class Copies:
    def __init__(self, send, recv, local):
        self.send, self.recv, self.local = send, recv, local
        self.sends, self.recvs, self.locals, self.started = {}, {}, {}, []

    def remote(self, ends, name, arrives, device, last=True):
        sent = self.sends.setdefault(name, len(self.sends))
        got = self.recvs.setdefault(arrives, len(self.recvs))

        def make():
            source, target = ends()
            return pltpu.make_async_remote_copy(
                source, target, self.send.at[sent], self.recv.at[got],
                device_id=device, device_id_type=MESH_ID,
            )

        make().start()
        if last:
            self.started.append(lambda: make().wait_send())

    def sent(self, ends, name, device):
        source, target = ends()
        pltpu.make_async_remote_copy(
            source, target, self.send.at[self.sends[name]], self.recv.at[0],
            device_id=device, device_id_type=MESH_ID,
        ).wait_send()

    def arrived(self, place, name, device):
        got = self.recvs.setdefault(name, len(self.recvs))
        pltpu.make_async_remote_copy(
            place, place, self.send.at[0], self.recv.at[got],
            device_id=device, device_id_type=MESH_ID,
        ).wait_recv()

    def copy(self, ends, name, wait_last=True):
        at = self.locals.setdefault(name, len(self.locals))

        def make():
            return pltpu.make_async_copy(*ends(), self.local.at[at])

        make().start()
        if wait_last:
            self.started.append(lambda: make().wait())
        return lambda: make().wait()

    def wait_copy(self, ends, name):
        pltpu.make_async_copy(*ends(), self.local.at[self.locals[name]]).wait()

    def finish(self):
        for wait in self.started:
            wait()


class Neighbours:
    def __init__(self, inner):
        me = lax.axis_index("dp")
        at = me // inner
        self.core = lax.axis_index("tensor")
        self.z, self.y, self.x = at // 4, at // 2 % 2, at % 2
        self.spots = [(self.z + dz + 4) % 4 for dz in Z_FROM]
        self.along = [{"dp": me + (spot - self.z) * 4 * inner} for spot in self.spots]
        self.over_y = {"dp": me + (1 - 2 * self.y) * 2 * inner}
        self.over_x = {"dp": me + (1 - 2 * self.x) * inner}
        self.twin = {"tensor": 1 - self.core}
        self.blocks = {
            (k, other_y, other_x): self.spots[k] * 4
            + (1 - self.y if other_y else self.y) * 2
            + (1 - self.x if other_x else self.x)
            for k in range(SLOTS)
            for other_y in (0, 1)
            for other_x in (0, 1)
        }

    def greet(self):
        barrier = pltpu.get_barrier_semaphore()
        devices = [*self.along[1:], self.over_y, self.over_x, self.twin]
        for device in devices:
            pl.semaphore_signal(barrier, inc=1, device_id=device, device_id_type=MESH_ID)
        pl.semaphore_wait(barrier, len(devices))

    def block(self, k, other_y, other_x):
        return self.blocks[k, other_y, other_x]


BACK = (0, 2, 1, 3)


class Gather:
    def __init__(self, copies, near, shard, full, tag):
        self.copies, self.near, self.shard, self.full, self.tag = copies, near, shard, full, tag
        self.split = full.shape[2] // (2 * LANES) * LANES

    def source(self, k):
        return self.shard if k == 0 else self.full.at[self.near.block(k, 0, 0)]

    def begin(self):
        for k in range(1, SLOTS):
            self.copies.remote(
                lambda: (self.shard, self.full.at[self.near.block(0, 0, 0)]),
                (self.tag, "z", k), (self.tag, "z", BACK[k]), self.near.along[k],
            )
        self.full[self.near.block(0, 0, 0)] = self.shard[...]

    def spread(self, k):
        near, place = self.near, self.full.at[self.near.block(k, 0, 0)]
        if k > 0:
            self.copies.arrived(place, (self.tag, "z", k), near.along[k])
        for way, device in (("y", near.over_y), ("x", near.over_x)):
            name = (self.tag, way, k)
            self.copies.remote(
                lambda: (self.source(k), self.full.at[near.block(k, 0, 0)]), name, name, device
            )

    def cross(self, k):
        near = self.near
        from_y = self.full.at[near.block(k, 1, 0)]
        from_x = self.full.at[near.block(k, 0, 1)]
        self.copies.arrived(from_y, (self.tag, "y", k), near.over_y)
        self.copies.remote(
            lambda: (self.full.at[near.block(k, 1, 0), :, : self.split],) * 2,
            (self.tag, "one", k), (self.tag, "one", k), near.over_x,
        )
        self.copies.arrived(from_x, (self.tag, "x", k), near.over_x)
        self.copies.remote(
            lambda: (self.full.at[near.block(k, 0, 1), :, self.split :],) * 2,
            (self.tag, "two", k), (self.tag, "two", k), near.over_y,
        )

    def end(self):
        near = self.near
        for k in range(SLOTS):
            place = self.full.at[near.block(k, 1, 1)]
            self.copies.arrived(place.at[:, : self.split], (self.tag, "one", k), near.over_x)
            self.copies.arrived(place.at[:, self.split :], (self.tag, "two", k), near.over_y)


def roll_left(slab, lanes):
    return pltpu.roll(slab, LANES - lanes, 1)


def forward_kernel(
    inner, q_shard, o_shard, gateup_hbm, down_hbm, hidden_hbm, og_hbm, cos, sin, seg_col, seg_row,
    routes,
    q_full, o_full, small, normed, q_ref, k_ref, v_ref, attended, lse_ref, combine, combine_pair,
    middle_hbm, x_hbm, xt_hbm, og_pair, ogt_hbm, pairs_hbm, near_hbm, far_hbm,
    hidden, gateup, down, given, pairs, bias, k_low, k_high, v_low, v_high, part, part_got, x_own,
    middle, stage, turned, columns_out, columns_got, send, recv, local,
):
    near = Neighbours(inner)
    copies = Copies(send, recv, local)
    tokens, width = hidden.shape
    block = width // 16
    chunks = pairs.shape[0]
    hid = down.shape[2]
    q_width = q_ref.shape[1]
    kv_slabs = k_ref.shape[1] // LANES
    slabs = q_width // LANES
    qkv_width = q_width + 2 * k_ref.shape[1]
    experts = down.shape[0]
    each = 2 + experts
    half = tokens // 2
    tiles = tokens // ROWS
    x, core = near.x, near.core
    own_half = pl.ds(pl.multiple_of(core * half, half), half)
    mine = pl.ds(pl.multiple_of(tokens + core * half, half), half)
    theirs = pl.ds(pl.multiple_of(tokens + (1 - core) * half, half), half)

    near.greet()
    gather_q = Gather(copies, near, q_shard, q_full, "q")
    gather_o = Gather(copies, near, o_shard, o_full, "o")
    gather_q.begin()
    gather_q.spread(0)
    weights_in = [
        copies.copy(lambda: (gateup_hbm, gateup), "gateup", False),
        copies.copy(lambda: (down_hbm, down), "down", False),
    ]
    hidden_in = copies.copy(lambda: (hidden_hbm, hidden), "hidden", False)
    copies.copy(lambda: (og_hbm, og_pair.at[pl.ds(0, tokens)]), "og")

    def pack(c, mine):
        first = 2 * (chunks * (x if mine else 1 - x) + c)
        rows = pl.ds(pl.multiple_of(x * block, block), block)
        for e in range(CHUNK):
            for part_at in range(2):
                at = hid * (2 * e + part_at)
                value = gateup[first + e, part_at].astype(BF16)
                if mine:
                    pairs[c, rows, at : at + hid] = value
                else:
                    given[c, :, at : at + hid] = value
            at = hid * (2 * CHUNK + e)
            value = down[first + e].astype(BF16)
            if mine:
                pairs[c, rows, at : at + hid] = value
            else:
                given[c, :, at : at + hid] = value

    def swap(c):
        rows = pl.ds(pl.multiple_of(x * block, block), block)
        copies.remote(
            lambda: (given.at[c], pairs.at[c, rows]), ("s", c), ("s", c), near.over_x
        )

    def swapped(c):
        rows = pl.ds(pl.multiple_of((1 - x) * block, block), block)
        copies.arrived(pairs.at[c, rows], ("s", c), near.over_x)

    def ring_one(c):
        copies.remote(
            lambda: (pairs.at[c], near_hbm.at[c, 0]), ("up", c), ("r", c, 1), near.along[2]
        )
        copies.remote(
            lambda: (pairs.at[c], near_hbm.at[c, 1]), ("down", c), ("r", c, 2), near.along[1]
        )

    def ring_two(c):
        copies.arrived(near_hbm.at[c, 0], ("r", c, 1), near.along[1])
        copies.remote(
            lambda: (near_hbm.at[c, 0], near_hbm.at[c, 2]), ("two", c), ("r", c, 3), near.along[2]
        )

    def over_y(c, k):
        copies.remote(
            lambda: (pairs.at[c] if k == 0 else near_hbm.at[c, k - 1], far_hbm.at[c, k]),
            ("f", c, k), ("f", c, k), near.over_y,
        )

    def ring_got(c, k):
        copies.arrived(near_hbm.at[c, k - 1], ("r", c, k), near.along[k])

    def turn_tile(source, target, name, side):
        copies.copy(lambda: (source, stage.at[side]), (name, "in"), False)()
        turned[side] = stage[side].T
        return copies.copy(lambda: (turned.at[side], target), (name, "out"), False)

    waits = [None, None]

    def turn_next(source, target, name, side):
        if waits[side] is not None:
            waits[side]()
        waits[side] = turn_tile(source, target, name, side)

    for wait in weights_in:
        wait()
    pack(0, False)
    swap(0)
    pack(0, True)
    gather_q.spread(1)
    gather_q.spread(2)
    pack(1, False)
    pack(1, True)
    gather_q.cross(0)
    gather_q.spread(3)
    gather_o.begin()
    pack(2, False)
    pack(2, True)
    gather_q.cross(1)
    gather_q.cross(2)
    swapped(0)
    ring_one(0)
    over_y(0, 0)
    pack(3, False)
    pack(3, True)
    fill_bias(bias, seg_col, seg_row)
    gather_q.cross(3)
    gather_o.spread(0)
    for c in range(1, chunks):
        swap(c)
    for tile in range(tiles):
        rows = pl.ds(tile * ROWS, ROWS)
        turn_next(og_hbm.at[rows], ogt_hbm.at[:, rows], ("og", tile), tile % 2)
    hidden_in()
    gather_q.end()
    pieces = q_full[:, :, qkv_width:].reshape(width, LANES)
    wide = pieces.astype(F32)
    summed = wide + roll_left(wide, each) + roll_left(wide, 2 * each)
    small[...] = summed.T[: small.shape[0], :]

    def project(tile, carry):
        rows = pl.ds(pl.multiple_of(tile * ROWS, ROWS), ROWS)
        value = hidden[rows, :].astype(F32)
        inverse = lax.rsqrt(jnp.mean(value * value, axis=1, keepdims=True) + NORM_EPSILON)
        low = (value * inverse * small[0:1, :]).astype(BF16)
        normed[:, rows] = low.T
        cosine, sine = cos[rows, :], sin[rows, :]
        for g in range(slabs + 2 * kv_slabs):
            lanes = slice(g * LANES, (g + 1) * LANES)
            if g % 2 == 0:
                two = slice(g * LANES, (g + 2) * LANES)
                lin_two = dot(low, q_full[:, :, two].reshape(width, 2 * LANES))
            lin = lin_two[:, (g % 2) * LANES : (g % 2 + 1) * LANES]
            if g < slabs + kv_slabs:
                lin = lin * cosine + rotate_halves(lin) * sine
            if g < slabs:
                q_ref[rows, lanes] = lin.astype(BF16)
            elif g < slabs + kv_slabs:
                at = (g - slabs) * LANES
                k_ref[rows, at : at + LANES] = lin.astype(BF16)
            else:
                at = (g - slabs - kv_slabs) * LANES
                v_ref[rows, at : at + LANES] = lin.astype(BF16)

        @pl.when(tile == 0)
        def _():
            gather_o.spread(1)
            gather_o.spread(2)

        @pl.when(tile == 2)
        def _():
            gather_o.spread(3)
            gather_o.cross(0)

        return carry

    lax.fori_loop(0, tiles, project, 0)
    for j in range(kv_slabs):
        lanes = slice(j * LANES, (j + 1) * LANES)
        spread_heads(k_ref[:, lanes], k_low, k_high, 2 * j)
        spread_heads(v_ref[:, lanes], v_low, v_high, 2 * j)

    def attend(g, carry):
        lanes = pl.ds(pl.multiple_of(g * LANES, LANES), LANES)
        kv_even, kv_odd = (2 * g) // 3, (2 * g + 1) // 3
        for at in range(0, tokens, ROWS):
            rows = slice(at, at + ROWS)
            upto = at + ROWS
            queries = q_ref[rows, lanes]
            total = None
            stats = []
            for keys, values, kv_at in ((k_low, v_low, kv_even), (k_high, v_high, kv_odd)):
                scores = dot(queries, keys[kv_at, :upto, :], NT) * SCORE_SCALE + bias[rows, :upto]
                highest = jnp.max(scores, axis=1, keepdims=True)
                weights = jnp.exp(scores - highest)
                whole = jnp.sum(weights, axis=1, keepdims=True)
                probability = (weights * (1.0 / whole)).astype(BF16)
                one = dot(probability, values[kv_at, :upto, :])
                total = one if total is None else total + one
                stats.append(highest + jnp.log(whole))
            attended[rows, lanes] = total.astype(BF16)
            across = jnp.where(half_mask(ROWS, False), stats[0], stats[1]).T
            lse_ref[g, 0:1, rows] = across[0:1, :]
            lse_ref[g, 1:2, rows] = across[HEAD_DIM : HEAD_DIM + 1, :]

        @pl.when(g == 0)
        def _():
            gather_o.cross(1)
            gather_o.cross(2)
            ring_two(0)
            over_y(0, 1)
            swapped(1)
            ring_one(1)
            over_y(1, 0)

        @pl.when(g == 1)
        def _():
            gather_o.cross(3)
            ring_got(0, 2)
            over_y(0, 2)
            copies.remote(
                lambda: (og_hbm.at[own_half], og_pair.at[mine]), ("og",), ("og",), near.over_x
            )

        @pl.when(g == 3)
        def _():
            ring_got(0, 3)
            over_y(0, 3)
            swapped(2)
            ring_one(2)

        @pl.when(g == 4)
        def _():
            ring_two(1)
            over_y(1, 1)
            ring_got(1, 2)
            over_y(1, 2)
            gather_o.end()

        return carry

    lax.fori_loop(0, slabs, attend, 0)

    def project_out(step, carry):
        tile = (step + 2 * (1 - core)) % tiles
        rows = pl.ds(pl.multiple_of(tile * ROWS, ROWS), ROWS)
        low = attended[rows, :]
        for group in range(SLOTS):
            cols = slice(4 * block * group, 4 * block * (group + 1))
            weight = o_full[4 * group : 4 * (group + 1)].reshape(4 * block, q_width)
            part[rows, cols] = dot(low, weight, NT).astype(BF16)
        return carry

    for step in range(tiles):
        project_out(step, 0)
        tile = (step + 2 * (1 - core)) % tiles
        rows = pl.ds(pl.multiple_of(tile * ROWS, ROWS), ROWS)
        copies.remote(
            lambda rows=rows: (part.at[rows], part_got.at[rows]),
            ("p", step), ("p", step), near.twin,
        )
    router = q_full[:, :, qkv_width:].reshape(width, LANES)
    for step in range(tiles):
        tile = (step + 2 * core) % tiles
        rows = pl.ds(pl.multiple_of(tile * ROWS, ROWS), ROWS)
        copies.arrived(part_got.at[rows], ("p", step), near.twin)
        side = step % 2
        if step >= 2:
            middle_out[side]()
        elif step == 0:
            middle_out = [None, None]
        total = hidden[rows, :].astype(F32) + RESIDUAL_SCALE * (
            part[rows, :].astype(F32) + part_got[rows, :].astype(F32)
        )
        middle[side] = total
        middle_out[side] = copies.copy(
            lambda rows=rows, side=side: (middle.at[side], middle_hbm.at[rows]), ("m", step), False
        )
        inverse = lax.rsqrt(jnp.mean(total * total, axis=1, keepdims=True) + NORM_EPSILON)
        value = total * inverse * small[1:2, :]
        high = value.astype(BF16)
        x_own[rows, :] = high
        copies.copy(lambda rows=rows: (x_own.at[rows], x_hbm.at[rows]), ("x", step))
        if step < 2:
            there = pl.ds(pl.multiple_of(tokens + tile * ROWS, ROWS), ROWS)
            copies.remote(
                lambda rows=rows, there=there: (x_own.at[rows], x_hbm.at[there]),
                ("x", step), ("x", step), near.over_x,
            )
        rest = value - high.astype(F32)
        mid = rest.astype(BF16)
        low = (rest - mid.astype(F32)).astype(BF16)
        one, two, three = dot(high, router), dot(mid, router), dot(low, router)
        logits = one + roll_left(one, each) + roll_left(one, 2 * each) + two + roll_left(two, each)
        logits = roll_left(logits + three, 2)
        lane = lax.broadcasted_iota(jnp.int32, (ROWS, LANES), 1)
        chosen = lane < 0
        route = routes[rows, :]
        for k in range(routes.shape[1]):
            chosen = chosen | (route[:, k : k + 1] == lane)
        logits = jnp.where(chosen, logits, MASK_VALUE)
        powers = jnp.exp(logits - jnp.max(logits, axis=1, keepdims=True))
        powers = jnp.where(chosen, powers, 0.0)
        combine[rows, :] = powers * (1.0 / jnp.sum(powers, axis=1, keepdims=True))
        if step == 0:
            swapped(3)
            copies.copy(lambda: (pairs, pairs_hbm), "pairs")
        if step == 1:
            ring_got(1, 3)
            over_y(1, 3)
        if step == 2:
            ring_two(2)

    shares = experts // 2
    flipped = combine[...].T
    kept = jnp.where(x == 0, flipped[:shares, :], flipped[shares : 2 * shares, :])
    gone = jnp.where(x == 0, flipped[shares : 2 * shares, :], flipped[:shares, :])
    columns_out[...] = gone
    copies.remote(lambda: (columns_out, columns_got), ("c",), ("c",), near.over_x)
    combine_pair[:tokens, :] = kept.T

    copies.arrived(og_pair.at[mine], ("og",), near.over_x)
    copies.remote(lambda: (og_pair.at[mine],) * 2, ("og2",), ("og2",), near.twin)
    for tile in range(tiles):
        rows = pl.ds(tile * ROWS, ROWS)
        if waits[tile % 2] is not None:
            waits[tile % 2]()
        turned[tile % 2] = x_own[rows, :].T
        waits[tile % 2] = copies.copy(
            lambda rows=rows, side=tile % 2: (turned.at[side], xt_hbm.at[:, rows]),
            ("xt", tile), False,
        )
    for step in range(2):
        tile = (step + 2 * core) % tiles
        rows = pl.ds(pl.multiple_of(tokens + tile * ROWS, ROWS), ROWS)
        turn_next(og_pair.at[rows], ogt_hbm.at[:, rows], ("og", tiles + step), step)
    copies.arrived(columns_got, ("c",), near.over_x)
    combine_pair[tokens:, :] = columns_got[...].T
    copies.arrived(og_pair.at[theirs], ("og2",), near.twin)
    for step in range(2):
        tile = (step + 2 * (1 - core)) % tiles
        rows = pl.ds(pl.multiple_of(tokens + tile * ROWS, ROWS), ROWS)
        turn_next(og_pair.at[rows], ogt_hbm.at[:, rows], ("og", tiles + 2 + step), step)
    for step in range(2):
        tile = (step + 2 * core) % tiles
        rows = pl.ds(pl.multiple_of(tokens + tile * ROWS, ROWS), ROWS)
        copies.arrived(x_hbm.at[rows], ("x", step), near.over_x)
        copies.remote(
            lambda rows=rows: (x_hbm.at[rows],) * 2, ("x2", step), ("x2", step), near.twin
        )
        turn_next(x_hbm.at[rows], xt_hbm.at[:, rows], ("xt", tiles + step), step)
    for step in range(2):
        tile = (step + 2 * (1 - core)) % tiles
        rows = pl.ds(pl.multiple_of(tokens + tile * ROWS, ROWS), ROWS)
        copies.arrived(x_hbm.at[rows], ("x2", step), near.twin)
        turn_next(x_hbm.at[rows], xt_hbm.at[:, rows], ("xt", tiles + 2 + step), step)
    for wait in waits + middle_out:
        wait()
    ring_got(2, 2)
    ring_got(2, 3)
    for c in range(LATE):
        for k in range(SLOTS):
            copies.arrived(far_hbm.at[c, k], ("f", c, k), near.over_y)
    copies.finish()


def forward_pass(q_shard, o_shard, gateup, down, hidden, og, cosine, sine, segments, routes):
    tokens, width = hidden.shape
    experts, hid = down.shape[0], down.shape[2]
    block, q_columns = q_shard.shape
    q_width = o_shard.shape[1]
    kv_width = (q_columns - LANES - q_width) // 2
    slabs, kv_heads = q_width // LANES, kv_width // HEAD_DIM
    chunks = experts // (2 * CHUNK)
    columns = 3 * CHUNK * hid
    anywhere, vmem = pl.BlockSpec(memory_space=pl.ANY), vmem_spec()
    shape = jax.ShapeDtypeStruct
    inner = lax.axis_size("dp") // 16
    dma = pltpu.SemaphoreType.DMA
    return pl.pallas_call(
        functools.partial(forward_kernel, inner),
        in_specs=[vmem, vmem] + [anywhere] * 4 + [vmem] * 5,
        out_specs=[vmem] * 11 + [anywhere] * 8,
        out_shape=[
            shape((16, block, q_columns), BF16),
            shape((16, block, q_width), BF16),
            shape((24, width), F32),
            shape((width, tokens), BF16),
            shape((tokens, q_width), BF16),
            shape((tokens, kv_width), BF16),
            shape((tokens, kv_width), BF16),
            shape((tokens, q_width), BF16),
            shape((slabs, 8, tokens), F32),
            shape((tokens, LANES), F32),
            shape((2 * tokens, experts // 2), F32),
            shape((tokens, width), F32),
            shape((2 * tokens, width), BF16),
            shape((width, 2 * tokens), BF16),
            shape((2 * tokens, width), BF16),
            shape((width, 2 * tokens), BF16),
            shape((chunks, 2 * block, columns), BF16),
            shape((chunks - 1, SLOTS - 1, 2 * block, columns), BF16),
            shape((LATE, SLOTS, 2 * block, columns), BF16),
        ],
        scratch_shapes=[
            pltpu.VMEM((tokens, width), BF16),
            pltpu.VMEM(gateup.shape, gateup.dtype),
            pltpu.VMEM(down.shape, down.dtype),
            pltpu.VMEM((chunks, block, columns), BF16),
            pltpu.VMEM((chunks, 2 * block, columns), BF16),
            pltpu.VMEM((tokens, tokens), F32),
        ]
        + [pltpu.VMEM((kv_heads, tokens, LANES), BF16)] * 4
        + [pltpu.VMEM((tokens, width), BF16)] * 3
        + [
            pltpu.VMEM((2, ROWS, width), F32),
            pltpu.VMEM((2, ROWS, width), BF16),
            pltpu.VMEM((2, width, ROWS), BF16),
            pltpu.VMEM((experts // 2, tokens), F32),
            pltpu.VMEM((experts // 2, tokens), F32),
            dma((80,)), dma((80,)), dma((60,)),
        ],
        compiler_params=pltpu.CompilerParams(
            vmem_limit_bytes=EXPERT_VMEM, collective_id=1, has_side_effects=True
        ),
        name="forward_pass",
    )(
        q_shard, o_shard, gateup, down, hidden, og, cosine, sine,
        segments[:, None], segments[None, :], routes,
    )


class Scatter:
    def __init__(self, copies, near, grad, one, two, got_y, got_x, got_z, share, tag):
        self.copies, self.near, self.grad, self.share, self.tag = copies, near, grad, share, tag
        self.one, self.two, self.got_y, self.got_x, self.got_z = one, two, got_y, got_x, got_z
        self.split = one.shape[2]

    def begin(self, k):
        near = self.near
        self.copies.remote(
            lambda: (self.grad.at[near.block(k, 1, 1), :, : self.split], self.one.at[k]),
            (self.tag, "one", k), (self.tag, "one", k), near.over_x,
        )
        self.copies.remote(
            lambda: (self.grad.at[near.block(k, 1, 1), :, self.split :], self.two.at[k]),
            (self.tag, "two", k), (self.tag, "two", k), near.over_y,
        )

    def cross(self, k):
        near, grad, split = self.near, self.grad, self.split
        self.copies.arrived(self.one.at[k], (self.tag, "one", k), near.over_x)
        at = near.block(k, 1, 0)
        grad[at, :, :split] = (
            grad[at, :, :split].astype(F32) + self.one[k].astype(F32)
        ).astype(BF16)
        self.copies.remote(
            lambda: (grad.at[near.block(k, 1, 0)], self.got_y.at[k]),
            (self.tag, "y", k), (self.tag, "y", k), near.over_y,
        )
        self.copies.arrived(self.two.at[k], (self.tag, "two", k), near.over_y)
        at = near.block(k, 0, 1)
        grad[at, :, split:] = (
            grad[at, :, split:].astype(F32) + self.two[k].astype(F32)
        ).astype(BF16)
        self.copies.remote(
            lambda: (grad.at[near.block(k, 0, 1)], self.got_x.at[k]),
            (self.tag, "x", k), (self.tag, "x", k), near.over_x,
        )

    def plane(self, k):
        near, grad = self.near, self.grad
        self.copies.arrived(self.got_y.at[k], (self.tag, "y", k), near.over_y)
        self.copies.arrived(self.got_x.at[k], (self.tag, "x", k), near.over_x)
        at = near.block(k, 0, 0)
        total = grad[at].astype(F32) + self.got_y[k].astype(F32) + self.got_x[k].astype(F32)
        if k == 0:
            self.share[...] = total
            return
        grad[at] = total.astype(BF16)
        self.copies.remote(
            lambda: (grad.at[near.block(k, 0, 0)], self.got_z.at[BACK[k] - 1]),
            (self.tag, "z", k), (self.tag, "z", BACK[k]), near.along[k],
        )

    def end(self):
        for k in range(1, SLOTS):
            self.copies.arrived(self.got_z.at[k - 1], (self.tag, "z", k), self.near.along[k])
            self.share[...] = self.share[...] + self.got_z[k - 1].astype(F32)


STRIP = 128


def backward_kernel(
    inner,
    o_full, q_ref, k_ref, v_ref, attended, lse_ref, cos, sin, seg_col, seg_row, small, combine,
    gate_turned, q_hbm, normed_hbm, hidden_hbm, og_hbm, middle_hbm, dx_own, dx_twin, dx_other,
    mix_pair, *refs,
):
    keeps, refs = refs[:SENT], refs[SENT:]
    parts, refs = refs[:SENT], refs[SENT:]
    near_two, near_three, late_got, far_three = refs[:4]
    q_share, o_share, input_grad, block_out, kept_out, given_got, mid_grad, far_got = refs[4:12]
    z_two, z_three, mix_twin, mix_half, mix_other = refs[12:17]
    (
        attended_grad, lin_grad, o_grad, q_grad, o_one, o_two, o_y, o_x, o_z,
        q_one, q_two, q_y, q_x, q_z, part_got, pieces, z_send, z_keep, given, kept,
        strips, wide_in, wide_out, strip_out, router_rows, gate_columns, small_sum,
        send, recv, local, strip_sem, wide_sem, out_sem,
    ) = refs[17:]
    near = Neighbours(inner)
    copies = Copies(send, recv, local)
    tokens, width = hidden_hbm.shape
    block = width // 16
    x, core = near.x, near.core
    half = tokens // 2
    q_width = q_ref.shape[1]
    kv_width = k_ref.shape[1]
    kv_slabs, slabs = kv_width // LANES, q_width // LANES
    qkv_width = q_width + 2 * kv_width
    experts = gate_turned.shape[0]
    each = 2 + experts
    strip_count = tokens // STRIP
    ours = pl.ds(0, tokens)
    half_mine = pl.ds(pl.multiple_of(tokens + core * half, half), half)
    half_other = pl.ds(pl.multiple_of(tokens + (1 - core) * half, half), half)
    there = pl.ds(pl.multiple_of(core * half, half), half)
    not_there = pl.ds(pl.multiple_of((1 - core) * half, half), half)
    rows_kept = pl.ds(pl.multiple_of(x * block, block), block)
    rows_given = pl.ds(pl.multiple_of((1 - x) * block, block), block)
    scatter_o = Scatter(copies, near, o_grad, o_one, o_two, o_y, o_x, o_z, o_share, "o")
    scatter_q = Scatter(copies, near, q_grad, q_one, q_two, q_y, q_x, q_z, q_share, "q")
    z_gots = [*parts, z_two, z_three]

    def sum_along_y(c, own, got, z_got, first):
        for pair in ((1, 2), (3, 0)):
            waits = []
            for i, k in enumerate(pair):
                waits.append(
                    copies.copy(lambda k=k, i=i: (own.at[k], pieces.at[2 * i]), (c, "a", k), False)
                )
                waits.append(
                    copies.copy(
                        lambda k=k, i=i: (got.at[k], pieces.at[2 * i + 1]), (c, "b", k), False
                    )
                )
            for wait in waits:
                wait()
            for i, k in enumerate(pair):
                total = pieces[2 * i].astype(F32) + pieces[2 * i + 1].astype(F32)
                if k == 0:
                    z_keep[c - SENT] = total.astype(BF16)
                    continue
                if not first:
                    copies.sent(
                        lambda: (z_send.at[k - 1], z_two.at[BACK[k] - 1]), (2, "z", k),
                        near.along[k],
                    )
                z_send[k - 1] = total.astype(BF16)
                copies.remote(
                    lambda k=k: (z_send.at[k - 1], z_got.at[BACK[k] - 1]),
                    (c, "z", k), (c, "z", BACK[k]), near.along[k], last=not first,
                )

    def load_chunk(c):
        waits = []
        for k in range(SLOTS):
            if k == 0 and c >= SENT:
                continue
            if c >= SENT:
                copies.arrived(z_gots[c].at[k - 1], (c, "z", k), near.along[k])
            waits.append(
                copies.copy(
                    lambda k=k: (keeps[c] if k == 0 else z_gots[c].at[k - 1], pieces.at[k]),
                    (c, "sum", k), False,
                )
            )
        return waits

    def sum_chunk(c, waits):
        for wait in waits:
            wait()
        if c >= 2:
            copies.wait_copy(lambda: (kept.at[c % 2], kept_out.at[c - 2]), ("kept", c - 2))
        for rows, mine in ((rows_kept, True), (rows_given, False)):
            total = (pieces[0, rows, :] if c < SENT else z_keep[c - SENT, rows, :]).astype(F32)
            for k in range(1, SLOTS):
                total = total + pieces[k, rows, :].astype(F32)
            if mine:
                kept[c % 2] = total
            else:
                given[c] = total.astype(BF16)
        copies.copy(lambda: (kept.at[c % 2], kept_out.at[c]), ("kept", c), c >= 2)
        copies.remote(
            lambda: (given.at[c], given_got.at[c]), ("given", c), ("given", c), near.over_x
        )

    def strip_rows(t):
        return pl.ds(pl.multiple_of(t * STRIP, STRIP), STRIP)

    def strip_loads(t, sources, wide):
        side = t % 2
        rows = strip_rows(t)
        loads = [
            pltpu.make_async_copy(source.at[rows], strips.at[i, side], strip_sem.at[i, side])
            for i, source in enumerate(sources)
        ]
        if wide is not None:
            loads.append(
                pltpu.make_async_copy(wide.at[rows], wide_in.at[side], wide_sem.at[side])
            )
        return loads

    def strip_store(t, source, target):
        side = t % 2
        return pltpu.make_async_copy(
            source.at[side], target.at[strip_rows(t)], out_sem.at[side]
        )

    def over_strips(sources, wide, source, target, compute):
        for load in strip_loads(0, sources, wide):
            load.start()

        def one(t, carry):
            side = t % 2

            @pl.when(t + 1 < strip_count)
            def _():
                for load in strip_loads(t + 1, sources, wide):
                    load.start()

            for load in strip_loads(t, sources, wide):
                load.wait()

            @pl.when(t >= 2)
            def _():
                strip_store(t - 2, source, target).wait()

            compute(t, side)
            strip_store(t, source, target).start()
            return carry

        lax.fori_loop(0, strip_count, one, 0)
        for t in (strip_count - 2, strip_count - 1):
            strip_store(t, source, target).wait()

    near.greet()
    for k in (1, 2, 3, 0):
        copies.remote(
            lambda k=k: (far_three.at[k], far_got.at[k]), ("far", k), ("far", k), near.over_y
        )
    copies.remote(
        lambda: (mix_pair.at[half_other], mix_half), ("mh",), ("mh",), near.twin
    )
    copies.remote(lambda: (mix_pair.at[ours], mix_twin), ("mt",), ("mt",), near.twin)
    sum_along_y(2, near_two, late_got, z_two, True)

    router = small[2 : 2 + experts, :]
    high = router.astype(BF16).astype(F32)
    mid = (router - high).astype(BF16).astype(F32)
    low = router - high - mid
    router_rows[...] = jnp.concatenate(
        [high, mid, low, high, mid, high, jnp.zeros((LANES - 6 * experts, width), F32)]
    ).astype(BF16)
    gate_columns[...] = jnp.concatenate(
        [gate_turned[...], jnp.zeros((LANES - experts, tokens), F32)]
    ).T
    small_sum[...] = jnp.zeros_like(small_sum)

    def middle_part(turned_back):
        def compute(t, side):
            rows = strip_rows(t)
            upstream = strips[0, side].astype(F32) + strips[1, side].astype(F32)
            upstream = upstream + strips[2, side].astype(F32)
            middle = wide_in[side]
            inverse = lax.rsqrt(jnp.mean(middle * middle, axis=1, keepdims=True) + NORM_EPSILON)
            gain = small[1:2, :]
            scaled = middle * inverse
            normed = scaled * gain
            gates, grads = combine[rows, :], gate_columns[rows, :]
            logit = gates * (grads - jnp.sum(gates * grads, axis=1, keepdims=True))
            one = logit.astype(BF16).astype(F32)
            two = (logit - one).astype(BF16).astype(F32)
            three = (logit - one - two).astype(BF16).astype(F32)

            def moved(piece, by):
                return pltpu.roll(piece, by * experts, 1)

            row = one + moved(one, 1) + moved(one, 2) + moved(two, 3) + moved(two, 4)
            row = (row + moved(three, 5)).astype(BF16)
            upstream = upstream + dot(row, router_rows[...])
            weighted = upstream * gain
            mean_term = jnp.mean(weighted * scaled, axis=1, keepdims=True)
            grad = strips[3, side].astype(F32) + inverse * (weighted - scaled * mean_term)
            wide_out[side] = grad
            small_sum[0:1, :] += jnp.sum(upstream * scaled, axis=0, keepdims=True)
            back = (RESIDUAL_SCALE * grad).astype(BF16)
            turned_back[:, rows] = back.T
            attended_grad[rows, :] = dot(back, o_full[...].reshape(width, q_width)).astype(BF16)
            columns = (one + moved(two, 1) + moved(three, 2)).T[: 3 * experts, :].astype(BF16)
            n_one = normed.astype(BF16)
            rest = normed - n_one.astype(F32)
            n_two = rest.astype(BF16)
            n_three = (rest - n_two.astype(F32)).astype(BF16)
            a, b, c = dot(columns, n_one), dot(columns, n_two), dot(columns, n_three)
            e = experts
            small_sum[8 : 8 + e, :] += (
                a[:e] + a[e : 2 * e] + a[2 * e :] + b[:e] + b[e : 2 * e] + c[:e]
            )

        over_strips([dx_own, dx_twin, dx_other, og_hbm], middle_hbm, wide_out, mid_grad, compute)
        for group in range(SLOTS):
            rows = slice(4 * block * group, 4 * block * (group + 1))
            o_grad[4 * group : 4 * (group + 1)] = (
                dot(turned_back[rows, :], attended[...]).astype(BF16).reshape(4, block, q_width)
            )

    pl.run_scoped(middle_part, pltpu.VMEM((width, tokens), BF16))
    for k in (1, 2, 3, 0):
        scatter_o.begin(k)

    mix_source = [mix_pair.at[half_mine], mix_half]

    def send_mix():
        copies.arrived(mix_half, ("mh",), near.twin)
        for i in range(half // STRIP):
            rows = pl.ds(i * STRIP, STRIP)
            whole = pl.ds(pl.multiple_of(tokens + core * half + i * STRIP, STRIP), STRIP)
            one = copies.copy(
                lambda: (mix_pair.at[whole], strips.at[0, i % 2]), ("m0", i), False
            )
            two = copies.copy(
                lambda: (mix_half.at[rows], strips.at[1, i % 2]), ("m1", i), False
            )
            one()
            two()
            if i >= 2:
                copies.wait_copy(
                    lambda: (strip_out.at[i % 2], mix_half.at[rows]), ("m2", i - 2)
                )
            strip_out[i % 2] = (
                strips[0, i % 2].astype(F32) + strips[1, i % 2].astype(F32)
            ).astype(BF16)
            copies.copy(lambda: (strip_out.at[i % 2], mix_half.at[rows]), ("m2", i), False)
        for i in (half // STRIP - 2, half // STRIP - 1):
            copies.wait_copy(
                lambda: (strip_out.at[i % 2], mix_half.at[pl.ds(i * STRIP, STRIP)]), ("m2", i)
            )
        copies.remote(lambda: (mix_half, mix_other.at[there]), ("mo",), ("mo",), near.over_x)

    def attention_part(bias0, bias1, bias2, bias3, k_low, k_high, v_low, v_high, dk, dv, dq):
        biases = (bias0, bias1, bias2, bias3)
        for at, bias in enumerate(biases):
            upto = bias.shape[0]
            keys_at = lax.broadcasted_iota(jnp.int32, bias.shape, 0)
            rows_at = at * ROWS + lax.broadcasted_iota(jnp.int32, bias.shape, 1)
            same = seg_col[:upto, :] == seg_row[:, at * ROWS : (at + 1) * ROWS]
            bias[...] = jnp.where((rows_at >= keys_at) & same, 0.0, MASK_VALUE).astype(F32)
        for j in range(kv_slabs):
            lanes = slice(j * LANES, (j + 1) * LANES)
            spread_heads(k_ref[:, lanes], k_low, k_high, 2 * j)
            spread_heads(v_ref[:, lanes], v_low, v_high, 2 * j)
        dk[...] = jnp.zeros_like(dk)
        dv[...] = jnp.zeros_like(dv)

        def slab(g, carry):
            lanes = pl.ds(pl.multiple_of(g * LANES, LANES), LANES)
            kv_even, kv_odd = (2 * g) // 3, (2 * g + 1) // 3
            for at, bias in enumerate(biases):
                rows = slice(at * ROWS, (at + 1) * ROWS)
                upto = (at + 1) * ROWS
                queries, grads = q_ref[rows, lanes], attended_grad[rows, lanes]
                turned = (grads.astype(F32) * attended[rows, lanes].astype(F32)).T
                zero = jnp.zeros_like(queries)
                dq_part = None
                for upper, keys, values, kv_at in (
                    (False, k_low, v_low, kv_even), (True, k_high, v_high, kv_odd)
                ):
                    first = HEAD_DIM if upper else 0
                    delta = jnp.sum(turned[first : first + HEAD_DIM, :], axis=0, keepdims=True)
                    head = 1 if upper else 0
                    total = lse_ref[g, head : head + 1, rows]
                    keys_here = keys[kv_at, :upto, :]
                    scores = dot(keys_here, queries, NT) * SCORE_SCALE + bias[...]
                    probability = jnp.exp(scores - total)
                    prob_grad = dot(values[kv_at, :upto, :], grads, NT)
                    score_grad = (probability * (prob_grad - delta)).astype(BF16)
                    mask = half_mask(ROWS, upper)
                    dv[kv_at, :upto, :] += dot(
                        probability.astype(BF16), jnp.where(mask, grads, zero)
                    )
                    dk[kv_at, :upto, :] += dot(score_grad, jnp.where(mask, queries, zero))
                    one = dot(score_grad, keys_here, TN)
                    dq_part = one if dq_part is None else dq_part + one
                dq[rows, :] = dq_part * SCORE_SCALE
            whole = dq[...]
            lin_grad[:, lanes] = (
                whole * cos[...] - rotate_halves(whole) * sin[...]
            ).astype(BF16)

            @pl.when(g == 0)
            def _():
                for k in (1, 2, 3, 0):
                    scatter_o.cross(k)
                sum_chunk(0, load_chunk(0))

            @pl.when(g == 1)
            def _():
                send_mix()

            @pl.when(g == 2)
            def _():
                for k in (1, 2, 3, 0):
                    scatter_o.plane(k)
                sum_chunk(1, load_chunk(1))

            @pl.when(g == 4)
            def _():
                for k in (1, 2, 3, 0):
                    copies.arrived(far_got.at[k], ("far", k), near.over_y)
                sum_along_y(3, near_three, far_got, z_three, False)
                scatter_o.end()

            return carry

        lax.fori_loop(0, slabs, slab, 0)
        low = half_mask(tokens, False)

        def joined(sums, j):
            one, two = sums[2 * j], sums[2 * j + 1]
            one = one + pltpu.roll(one, HEAD_DIM, 1)
            two = two + pltpu.roll(two, HEAD_DIM, 1)
            return jnp.where(low, one, two)

        for j in range(kv_slabs):
            at = q_width + j * LANES
            whole = joined(dk, j) * SCORE_SCALE
            lin_grad[:, at : at + LANES] = (
                whole * cos[...] - rotate_halves(whole) * sin[...]
            ).astype(BF16)
            at = at + kv_width
            lin_grad[:, at : at + LANES] = joined(dv, j).astype(BF16)

    kv_shape = (2 * kv_slabs, tokens, LANES)
    pl.run_scoped(
        attention_part,
        *[pltpu.VMEM(((at + 1) * ROWS, ROWS), F32) for at in range(tokens // ROWS)],
        *[pltpu.VMEM(kv_shape, BF16)] * 4,
        *[pltpu.VMEM(kv_shape, F32)] * 2,
        pltpu.VMEM((tokens, LANES), F32),
    )

    def last_part(normed_turned, q_full, part):
        normed_in = copies.copy(lambda: (normed_hbm, normed_turned), "normed", False)
        weights_in = copies.copy(lambda: (q_hbm, q_full), "q weights", False)
        columns = jnp.concatenate(
            [
                small_sum[0:1, :], small_sum[8 : 8 + experts, :],
                jnp.zeros((LANES - 1 - experts, width), F32),
            ]
        ).T
        q_grad[:, :, qkv_width:] = columns.astype(BF16).reshape(16, block, LANES)
        normed_in()
        for k in (1, 2, 3, 0):
            spot = near.spots[k]
            rows = pl.ds(pl.multiple_of(spot * 4 * block, 4 * block), 4 * block)
            q_grad[pl.ds(spot * 4, 4), :, :qkv_width] = (
                dot(normed_turned[rows, :], lin_grad[...])
                .astype(BF16)
                .reshape(4, block, qkv_width)
            )
            scatter_q.begin(k)
        weights_in()

        def project(tile):
            rows = pl.ds(tile * ROWS, ROWS)
            for group in range(SLOTS):
                cols = slice(4 * block * group, 4 * block * (group + 1))
                weight = q_full[4 * group : 4 * (group + 1), :, :qkv_width]
                part[rows, cols] = dot(
                    lin_grad[rows, :], weight.reshape(4 * block, qkv_width), NT
                ).astype(BF16)
            copies.remote(
                lambda: (part.at[rows], part_got.at[rows]), ("n", tile), ("n", tile), near.twin,
                last=False,
            )

        project(0)
        project(1)
        for k in (1, 2, 3, 0):
            scatter_q.cross(k)
        project(2)
        project(3)
        copies.arrived(mix_other.at[there], ("mo",), near.over_x)
        copies.remote(lambda: (mix_other.at[there],) * 2, ("m2",), ("m2",), near.twin)
        sum_chunk(2, load_chunk(2))
        for k in (1, 2, 3, 0):
            scatter_q.plane(k)
        for tile in range(tokens // ROWS):
            rows = pl.ds(tile * ROWS, ROWS)
            copies.arrived(part_got.at[rows], ("n", tile), near.twin)

        def finish_rows(t, side):
            rows = strip_rows(t)
            value = strips[0, side].astype(F32)
            inverse = lax.rsqrt(jnp.mean(value * value, axis=1, keepdims=True) + NORM_EPSILON)
            upstream = part[rows, :].astype(F32) + part_got[rows, :].astype(F32)
            scaled = value * inverse
            weighted = upstream * small[0:1, :]
            mean_term = jnp.mean(weighted * scaled, axis=1, keepdims=True)
            wide_out[side] = wide_in[side] + inverse * (weighted - scaled * mean_term)

        over_strips([hidden_hbm], mid_grad, wide_out, input_grad, finish_rows)
        for tile in range(tokens // ROWS):
            rows = pl.ds(tile * ROWS, ROWS)
            copies.sent(lambda: (part.at[rows], part_got.at[rows]), ("n", tile), near.twin)

    pl.run_scoped(
        last_part,
        pltpu.VMEM((width, tokens), BF16), pltpu.VMEM(q_hbm.shape, BF16),
        pltpu.VMEM((tokens, width), BF16),
    )
    copies.arrived(mix_twin, ("mt",), near.twin)
    copies.arrived(mix_other.at[not_there], ("m2",), near.twin)

    def mix_rows(t, side):
        mix = strips[0, side].astype(F32) + strips[1, side].astype(F32)
        mix = mix + strips[2, side].astype(F32)
        strip_out[side] = (wide_in[side] + RESIDUAL_SCALE * mix).astype(BF16)

    over_strips([mix_pair, mix_twin, mix_other], middle_hbm, strip_out, block_out, mix_rows)
    sum_chunk(3, load_chunk(3))
    scatter_q.end()
    for c in range(2 * SENT):
        copies.arrived(given_got.at[c], ("given", c), near.over_x)
    copies.finish()


def backward_pass(
    o_full, q, k, v, attended, lse, cosine, sine, segments, small, combine, gate_turned,
    q_full, normed, hidden, og, middle, dx, mix, keep, parts, near_grads, late, far,
):
    tokens, width = hidden.shape
    q_width, kv_width = q.shape[1], k.shape[1]
    block, q_columns = q_full.shape[1:]
    qkv_width = q_width + 2 * kv_width
    pair, columns = keep[0].shape
    chunks = 2 * SENT
    experts = gate_turned.shape[0]
    anywhere, vmem = pl.BlockSpec(memory_space=pl.ANY), vmem_spec()
    shape = jax.ShapeDtypeStruct
    dma = pltpu.SemaphoreType.DMA
    inner = lax.axis_size("dp") // 16

    def scatter_scratch(total):
        split = total // (2 * LANES) * LANES
        return [
            pltpu.VMEM((SLOTS, block, split), BF16),
            pltpu.VMEM((SLOTS, block, total - split), BF16),
            pltpu.VMEM((SLOTS, block, total), BF16),
            pltpu.VMEM((SLOTS, block, total), BF16),
            pltpu.VMEM((SLOTS - 1, block, total), BF16),
        ]

    values = (
        o_full, q, k, v, attended, lse, cosine, sine, segments[:, None], segments[None, :],
        small, combine, gate_turned,
    )
    far_values = (
        q_full, normed, hidden, og, middle, *dx, mix, *keep, *parts, *near_grads, late, far,
    )
    return pl.pallas_call(
        functools.partial(backward_kernel, inner),
        in_specs=[vmem] * len(values) + [anywhere] * len(far_values),
        out_specs=[vmem] * 2 + [anywhere] * 11,
        out_shape=[
            shape((block, q_columns), F32),
            shape((block, q_width), F32),
            shape((tokens, width), F32),
            shape((tokens, width), BF16),
            shape((chunks, block, columns), F32),
            shape((chunks, block, columns), BF16),
            shape((tokens, width), F32),
            shape((SLOTS, pair, columns), BF16),
            shape((SLOTS - 1, pair, columns), BF16),
            shape((SLOTS - 1, pair, columns), BF16),
            shape((tokens, width), BF16),
            shape((tokens // 2, width), BF16),
            shape((tokens, width), BF16),
        ],
        scratch_shapes=[
            pltpu.VMEM((tokens, q_width), BF16),
            pltpu.VMEM((tokens, qkv_width), BF16),
            pltpu.VMEM((16, block, q_width), BF16),
            pltpu.VMEM((16, block, q_columns), BF16),
        ]
        + scatter_scratch(q_width)
        + scatter_scratch(q_columns)
        + [
            pltpu.VMEM((tokens, width), BF16),
            pltpu.VMEM((SLOTS, pair, columns), BF16),
            pltpu.VMEM((SLOTS - 1, pair, columns), BF16),
            pltpu.VMEM((2, pair, columns), BF16),
            pltpu.VMEM((chunks, block, columns), BF16),
            pltpu.VMEM((2, block, columns), F32),
            pltpu.VMEM((4, 2, STRIP, width), BF16),
            pltpu.VMEM((2, STRIP, width), F32),
            pltpu.VMEM((2, STRIP, width), F32),
            pltpu.VMEM((2, STRIP, width), BF16),
            pltpu.VMEM((LANES, width), BF16),
            pltpu.VMEM((tokens, LANES), F32),
            pltpu.VMEM((8 + experts, width), F32),
            dma((80,)), dma((80,)), dma((60,)), dma((4, 2)), dma((2,)), dma((2,)),
        ],
        compiler_params=pltpu.CompilerParams(
            vmem_limit_bytes=EXPERT_VMEM, collective_id=2, has_side_effects=True
        ),
        name="backward_pass",
    )(*values, *far_values)


def whole_call(kernel, values, outs, earlier=(), name=None):
    return pl.pallas_call(
        with_earlier(kernel, len(values), len(earlier)),
        in_specs=[vmem_spec()] * len(values) + any_specs(earlier),
        out_specs=[vmem_spec()] * len(outs),
        out_shape=[jax.ShapeDtypeStruct(shape, dtype) for shape, dtype in outs],
        compiler_params=pltpu.CompilerParams(vmem_limit_bytes=VMEM_BYTES),
        name=name,
    )(*values, *earlier)


def fence_kernel(*refs):
    count = len(refs) // 2
    for value, out in zip(refs[:count], refs[count:]):
        out[...] = value[...]


def fence_all(values, *earlier):
    return whole_call(fence_kernel, values, [(v.shape, v.dtype) for v in values], earlier, "fence")


def fence(value, *earlier):
    return fence_all([value], *earlier)[0]


def sum_y_kernel(near, got, *outs):
    for k, out in enumerate(outs):
        out[...] = (near[k].astype(F32) + got[k].astype(F32)).astype(BF16)


def sum_y(near, got, *earlier):
    outs = [(near.shape[1:], BF16)] * SLOTS
    return whole_call(sum_y_kernel, [near, got], outs, earlier, "sum_y")


def sum_z_kernel(x_at, *refs):
    kept, given = refs[-2:]
    half = kept.shape[1]
    for c in range(kept.shape[0]):
        parts = refs[SLOTS * c : SLOTS * (c + 1)]
        for rows, out in ((x_at[0], kept), (1 - x_at[0], given)):
            rows = pl.ds(pl.multiple_of(rows * half, half), half)
            total = parts[0][rows, :].astype(F32)
            for part in parts[1:]:
                total = total + part[rows, :].astype(F32)
            out[c] = total.astype(out.dtype)


def sum_z(x_at, chunks, *earlier):
    count = len(chunks)
    pair, columns = chunks[0][0].shape
    flat = [part for parts in chunks for part in parts]
    return pl.pallas_call(
        with_earlier(sum_z_kernel, 1 + len(flat), len(earlier)),
        in_specs=[smem_spec()] + [vmem_spec()] * len(flat) + any_specs(earlier),
        out_specs=[vmem_spec()] * 2,
        out_shape=[
            jax.ShapeDtypeStruct((count, pair // 2, columns), F32),
            jax.ShapeDtypeStruct((count, pair // 2, columns), BF16),
        ],
        compiler_params=pltpu.CompilerParams(vmem_limit_bytes=VMEM_BYTES),
        name="sum_z",
    )(x_at, *flat, *earlier)


def sum_parts_kernel(parts, out):
    total = parts[0].astype(F32)
    for c in range(1, parts.shape[0]):
        total = total + parts[c].astype(F32)
    out[...] = total.astype(BF16)


def sum_parts(parts, *earlier):
    chunks, tokens, width = parts.shape
    return pl.pallas_call(
        with_earlier(sum_parts_kernel, 1, len(earlier)),
        grid=(tokens // EXPERT_ROWS,),
        in_specs=[pl.BlockSpec((chunks, EXPERT_ROWS, width), lambda s: (0, s, 0))]
        + any_specs(earlier),
        out_specs=pl.BlockSpec((EXPERT_ROWS, width), lambda s: (s, 0)),
        out_shape=jax.ShapeDtypeStruct((tokens, width), BF16),
        compiler_params=pltpu.CompilerParams(vmem_limit_bytes=VMEM_BYTES),
        name="sum_parts",
    )(parts, *earlier)


def adam_experts_kernel(x_at, kept, got, *refs):
    states, outs = refs[:6], refs[6:]
    own = kept.shape[1]
    hidden = states[0].shape[3]
    mine = pl.program_id(0) // (pl.num_programs(0) // 2) == x_at[0]
    grad = jnp.where(mine, kept[0], got[0].astype(F32))
    for e in range(CHUNK):
        for part in range(2):
            first = hidden * (2 * e + part)
            results = adam_update(
                states[0][e, part], grad[:, first : first + hidden],
                states[1][e, part], states[2][e, part], MODEL_DIM ** (-0.5), WEIGHT_DECAY,
            )
            for out, result in zip(outs[:3], results):
                out[e, part] = result
        first = hidden * (2 * CHUNK + e)
        results = adam_update(
            states[3][e], grad[:, first : first + hidden], states[4][e], states[5][e],
            max(1, F // 256) ** (-0.5), WEIGHT_DECAY,
        )
        for out, result in zip(outs[3:], results):
            out[e] = result


def adam_experts(x_at, kept, got, gateup, down):
    chunks, own, columns = kept.shape
    experts, hidden = down[0].shape[0], down[0].shape[2]
    share = pl.BlockSpec((1, own, columns), lambda j: (j % chunks, 0, 0))
    big = pl.BlockSpec((CHUNK, 2, own, hidden), lambda j: (j, 0, 0, 0))
    small = pl.BlockSpec((CHUNK, own, hidden), lambda j: (j, 0, 0))
    return pl.pallas_call(
        adam_experts_kernel,
        grid=(experts // CHUNK,),
        in_specs=[smem_spec(), share, share] + [big] * 3 + [small] * 3,
        out_specs=[big] * 3 + [small] * 3,
        out_shape=[jax.ShapeDtypeStruct(gateup[0].shape, F32)] * 3
        + [jax.ShapeDtypeStruct(down[0].shape, F32)] * 3,
        compiler_params=pltpu.CompilerParams(vmem_limit_bytes=VMEM_BYTES),
        name="adam_experts",
    )(x_at, kept, got, *gateup, *down)


def join_tokens_kernel(own, first, second, out, turned):
    half = own.shape[0] // 2
    for at, part in ((0, own[:half, :]), (half, own[half:, :]), (2 * half, first[...]), (3 * half, second[...])):
        out[at : at + half, :] = part
        turned[:, at : at + half] = part.T


def join_tokens(own, first, second, *earlier):
    tokens, width = own.shape
    return pl.pallas_call(
        with_earlier(join_tokens_kernel, 3, len(earlier)),
        in_specs=[vmem_spec()] * 3 + any_specs(earlier),
        out_specs=[vmem_spec()] * 2,
        out_shape=[
            jax.ShapeDtypeStruct((2 * tokens, width), own.dtype),
            jax.ShapeDtypeStruct((width, 2 * tokens), own.dtype),
        ],
        compiler_params=pltpu.CompilerParams(vmem_limit_bytes=VMEM_BYTES),
        name="join_tokens",
    )(own, first, second, *earlier)


def move(array, dz=0, dy=0, dx=0):
    total = lax.axis_size("dp")
    inner = total // 16
    pairs = []
    for at in range(16):
        z, y, x = at // 4, at // 2 % 2, at % 2
        to = ((z + dz) % 4) * 4 + (y ^ dy) * 2 + (x ^ dx)
        pairs += [(at * inner + i, to * inner + i) for i in range(inner)]
    return lax.ppermute(array, "dp", pairs)


def place():
    at = lax.axis_index("dp") // (lax.axis_size("dp") // 16)
    return at // 4, at // 2 % 2, at % 2


def inner_groups(total):
    inner = total // 16
    return [[at * inner + i for i in range(inner)] for at in range(16)]


def inner_gather(shard, axis):
    total = lax.axis_size("dp")
    if total == 16:
        return shard
    return lax.all_gather(
        shard, "dp", axis=axis, tiled=True, axis_index_groups=inner_groups(total)
    )


def inner_scatter(share, axis):
    total = lax.axis_size("dp")
    if total == 16:
        return share
    return lax.psum_scatter(
        share, "dp", scatter_dimension=axis, tiled=True, axis_index_groups=inner_groups(total)
    )


def block_rows(parts, rows):
    z, y, x = place()
    starts = []
    for dz, dy, dx in parts:
        starts.append((((z + dz + 4) % 4) * 4 + (y ^ dy) * 2 + (x ^ dx)) * rows)
    return jnp.stack(starts).astype(jnp.int32)


def gather_z(shard):
    return jnp.stack([shard] + [move(shard, dz=-dz) for dz in Z_FROM[1:]])


def gather_ring(shard):
    below, above = move(shard, dz=1), move(shard, dz=-1)
    return [shard, below, above, move(below, dz=1)]


def send_z(parts):
    return [move(parts[k].astype(BF16), dz=Z_FROM[k]) for k in range(1, SLOTS)]


def scatter_z(parts, moved=None):
    result = parts[0]
    for one in moved or send_z(parts):
        result = result + one.astype(F32)
    return result


def gather_plane(own):
    half = own.shape[-1] // 2
    along_y, along_x = move(own, dy=1), move(own, dx=1)
    both = (move(along_y[..., :half], dx=1), move(along_x[..., half:], dy=1))
    return own, along_y, along_x, *both


def scatter_plane(pieces):
    own, along_y, along_x, both_one, both_two = pieces
    half = both_one.shape[-1]
    got_one, got_two = move(both_one, dx=1), move(both_two, dy=1)
    pass_y = jnp.concatenate(
        [(along_y[..., :half].astype(F32) + got_one.astype(F32)).astype(BF16), along_y[..., half:]],
        axis=-1,
    )
    pass_x = jnp.concatenate(
        [along_x[..., :half], (along_x[..., half:].astype(F32) + got_two.astype(F32)).astype(BF16)],
        axis=-1,
    )
    got_y, got_x = move(pass_y, dy=1), move(pass_x, dx=1)
    return scatter_z(
        [
            own[k].astype(F32) + got_y[k].astype(F32) + got_x[k].astype(F32)
            for k in range(SLOTS)
        ]
    )


PLANE = [(dz, dy, dx) for dy, dx in ((0, 0), (1, 0), (0, 1), (1, 1)) for dz in Z_FROM]


def join_kernel(rows_at, *refs):
    pieces, out = refs[:-1], refs[-1]
    slots, own, width = pieces[0].shape
    half = width // 2
    for at in range(4 * slots):
        rows = pl.ds(pl.multiple_of(rows_at[at], own), own)
        group, slot = at // slots, at % slots
        if group < 3:
            out[rows, :] = pieces[group][slot]
        else:
            out[rows, :half] = pieces[3][slot]
            out[rows, half:] = pieces[4][slot]


def part_kernel(rows_at, whole, *pieces):
    slots, own, width = pieces[0].shape
    half = width // 2
    for at in range(4 * slots):
        rows = pl.ds(pl.multiple_of(rows_at[at], own), own)
        group, slot = at // slots, at % slots
        if group < 3:
            pieces[group][slot] = whole[rows, :]
        else:
            pieces[3][slot] = whole[rows, :half]
            pieces[4][slot] = whole[rows, half:]


def smem_spec():
    return pl.BlockSpec(memory_space=pltpu.SMEM)


def vmem_spec():
    return pl.BlockSpec(memory_space=pltpu.VMEM)


def join_blocks(rows_at, pieces, earlier=()):
    slots, own, width = pieces[0].shape
    return pl.pallas_call(
        with_earlier(join_kernel, 6, len(earlier)),
        in_specs=[smem_spec()] + [vmem_spec()] * 5 + any_specs(earlier),
        out_specs=vmem_spec(),
        out_shape=jax.ShapeDtypeStruct((4 * slots * own, width), BF16),
        compiler_params=pltpu.CompilerParams(vmem_limit_bytes=VMEM_BYTES),
        name="join_blocks",
    )(rows_at, *pieces, *earlier)


def part_blocks(rows_at, whole, earlier=()):
    own, width = whole.shape[0] // (4 * SLOTS), whole.shape[1]
    full = jax.ShapeDtypeStruct((SLOTS, own, width), BF16)
    half = jax.ShapeDtypeStruct((SLOTS, own, width // 2), BF16)
    return pl.pallas_call(
        with_earlier(part_kernel, 2, len(earlier)),
        in_specs=[smem_spec(), vmem_spec()] + any_specs(earlier),
        out_specs=[vmem_spec()] * 5,
        out_shape=[full] * 3 + [half] * 2,
        compiler_params=pltpu.CompilerParams(vmem_limit_bytes=VMEM_BYTES),
        name="part_blocks",
    )(rows_at, whole, *earlier)


def after(value, *earlier):
    marks = []
    for one in earlier:
        slots = one.shape[0] if one.shape[0] == SLOTS else 1
        lead, rest = (slots > 1) * 1, one.ndim - 1
        marks.append(lax.slice(one, (lead,) + (0,) * rest, (slots,) + (1,) * rest))
    return lax.optimization_barrier((value, *marks))[0]


def split_three(values):
    high = values.astype(BF16)
    rest = values - high.astype(F32)
    middle = rest.astype(BF16)
    low = (rest - middle.astype(F32)).astype(BF16)
    return [high, middle, low]


def swap_cores(part):
    return lax.ppermute(part, "tensor", [(0, 1), (1, 0)])


def pair_sum(part):
    return part.astype(F32) + swap_cores(part).astype(F32)


def norm_backward(values, inverse, gain_row, upstream):
    scaled = values * inverse
    weighted = upstream * gain_row
    mean_term = jnp.mean(weighted * scaled, axis=-1, keepdims=True)
    return (inverse * (weighted - scaled * mean_term), jnp.sum(upstream * scaled, axis=0))


def adam_update(value, gradient, mean_old, square_old, rate, decay):
    mean_new = FIRST_DECAY * mean_old + (1.0 - FIRST_DECAY) * gradient
    square_new = SECOND_DECAY * square_old + (1.0 - SECOND_DECAY) * gradient * gradient
    mean_hat = mean_new / (1.0 - FIRST_DECAY**STEP)
    square_hat = square_new / (1.0 - SECOND_DECAY**STEP)
    updated = value - rate * (mean_hat / (jnp.sqrt(square_hat) + ADAM_EPSILON) + decay * value)
    return (mean_new, square_new, updated)


def shards(
    hidden_in,
    out_grad,
    routes,
    segments,
    norm_gains,
    gains_mean,
    gains_square,
    w_query,
    query_mean,
    query_square,
    key_value_weight,
    key_value_first_moment,
    key_value_second_moment,
    w_out,
    out_mean,
    out_square,
    w_router,
    router_mean,
    router_square,
    w_gateup,
    gateup_mean,
    gateup_square,
    w_down,
    down_mean,
    down_square,
):
    tokens, width = hidden_in.shape
    own = w_query.shape[0]
    experts, hidden = w_down.shape[0], w_down.shape[1]
    q_width, kv_width = w_query.shape[1], key_value_weight.shape[2]
    qkv_width = q_width + 2 * kv_width
    each = 2 + experts
    half_experts = experts // 2
    block = width // 16
    z_at, y_at, x_at = place()
    core = lax.axis_index("tensor")
    plane_rows = block_rows(PLANE, block)
    qkv_shard = jnp.concatenate(
        [w_query.astype(BF16), key_value_weight[0].astype(BF16), key_value_weight[1].astype(BF16)]
        + split_three(jnp.concatenate([norm_gains.T, w_router], axis=1))
        + [jnp.zeros((own, LANES - 3 * each), BF16)],
        axis=1,
    )
    out_shard = w_out.T.astype(BF16)
    turned_down = [one.transpose(0, 2, 1) for one in (w_down, down_mean, down_square)]
    gateup_rows, down_rows = w_gateup, turned_down[0]
    if lax.axis_size("dp") > 16:
        gateup_rows = inner_gather(w_gateup.astype(BF16), 2)
        down_rows = inner_gather(down_rows.astype(BF16), 1)
    chunks = experts // (2 * CHUNK)
    first = x_at == 0
    cosine, sine = rope_tables(seq_positions(segments))
    (
        qkv_blocks, out_blocks, small, normed_low, queries, keys, values, attended, lse,
        combine, combine_pair, middle, x_pair, x_turned, og_pair, og_turned, pairs, near, far,
    ) = forward_pass(
        inner_gather(qkv_shard, 0), inner_gather(out_shard, 0), gateup_rows, down_rows,
        hidden_in, out_grad, cosine, sine, segments, routes,
    )
    dx, mix_pair, gate_turned, keep, z_got, near_grads, late_got, far_grad = experts_pass(
        x_pair, og_pair, x_turned, og_turned, combine_pair, pairs, near, far
    )
    qkv_share, output_share, input_grad, block_out, kept_share, got_share = backward_pass(
        out_blocks, queries, keys, values, attended, lse, cosine, sine, segments, small, combine,
        gate_turned, qkv_blocks, normed_low, hidden_in, out_grad, middle, dx, mix_pair, keep,
        z_got, near_grads, late_got, far_grad,
    )[:6]
    kept_share, got_share = inner_scatter(kept_share, 1), inner_scatter(got_share, 1)
    x_here = x_at.astype(jnp.int32)[None]
    output_share = inner_scatter(output_share, 0).T
    qkv_share = inner_scatter(qkv_share, 0)
    query_share = qkv_share[:, :q_width]
    keyval_share = jnp.stack(
        [qkv_share[:, q_width : q_width + kv_width], qkv_share[:, q_width + kv_width : qkv_width]]
    )
    gain_one_part = jnp.sum(w_query.astype(BF16).astype(F32) * query_share, axis=1) + jnp.sum(
        key_value_weight.astype(BF16).astype(F32) * keyval_share, axis=(0, 2)
    )
    gain_one_share = pair_sum(gain_one_part[None, :]) / norm_gains[:1]
    gains_share = jnp.concatenate([gain_one_share, qkv_share[:, qkv_width][None, :]])
    router_share = qkv_share[:, qkv_width + 1 : qkv_width + 1 + experts]

    gains_result = adam_update(norm_gains, gains_share, gains_mean, gains_square, GAIN_RATE, 0.0)
    query_result = adam_update(
        w_query, query_share, query_mean, query_square, (MODEL_DIM // 12) ** (-0.5), WEIGHT_DECAY
    )
    keyval_result = adam_update(
        key_value_weight,
        keyval_share,
        key_value_first_moment,
        key_value_second_moment,
        (MODEL_DIM // 12) ** (-0.5),
        WEIGHT_DECAY,
    )
    out_result = adam_update(
        w_out,
        output_share,
        out_mean,
        out_square,
        max(1, QUERY_HEADS * HEAD_DIM // 96) ** (-0.5),
        WEIGHT_DECAY,
    )
    router_result = adam_update(
        w_router, router_share, router_mean, router_square, (4 * MODEL_DIM) ** (-0.5), WEIGHT_DECAY
    )
    expert_results = adam_experts(
        x_here, kept_share, got_share,
        (w_gateup, gateup_mean, gateup_square), turned_down,
    )
    expert_results = [*expert_results[:3], *(one.transpose(0, 2, 1) for one in expert_results[3:])]
    return (
        (block_out, input_grad)
        + gains_result
        + query_result
        + keyval_result
        + out_result
        + router_result
        + tuple(expert_results)
    )


def solution(mesh):
    tokens, gains = P("dp", None), P(None, "dp")
    query, keyval, out = P("dp", "tensor"), P(None, "dp", "tensor"), P("tensor", "dp")
    router, gateup, down = P("dp", None), P(None, None, "dp", "tensor"), P(None, "tensor", "dp")
    states = tuple(
        spec for one in (gains, query, keyval, out, router, gateup, down) for spec in (one,) * 3
    )
    return jax.shard_map(
        shards,
        mesh=mesh,
        in_specs=(tokens, tokens, tokens, P("dp")) + states,
        out_specs=(tokens, tokens) + states,
        check_vma=False,
    )
```

```python
import functools

import jax
import jax.numpy as jnp
from jax import lax
from jax.experimental import pallas as pl
from jax.experimental.pallas import tpu as pltpu
from jax.sharding import PartitionSpec as P

MODEL_DIM = 1536
QUERY_HEADS = 24
HEAD_DIM = 64
F = 512
SEQUENCE_LENGTH = 1024
STEP = 10

NORM_EPSILON = 1e-06
SCORE_SCALE = 0.015625
RESIDUAL_SCALE = 0.22
ROPE_BASE = 10000.0
FIRST_DECAY = 0.9
SECOND_DECAY = 0.95
ADAM_EPSILON = 1e-08
WEIGHT_DECAY = 0.1
GAIN_RATE = 0.6
MASK_VALUE = -1e30
HIGHEST_PRECISION = lax.Precision.HIGHEST

BF16 = jnp.bfloat16
F32 = jnp.float32
LANES = 128
ROWS = 256
VMEM_BYTES = 58 * 1024 * 1024

NN = (((1,), (0,)), ((), ()))
NT = (((1,), (1,)), ((), ()))
TN = (((0,), (0,)), ((), ()))


def dot(a, b, dims=NN):
    return lax.dot_general(a, b, dims, preferred_element_type=F32)


def seq_positions(segment_row):
    counter = jnp.arange(segment_row.shape[0], dtype=jnp.int32)
    earlier = jnp.concatenate([segment_row[:1] - 1, segment_row[:-1]])
    starts = lax.cummax(jnp.where(segment_row != earlier, counter, 0), axis=0)
    return counter - starts


def rope_tables(positions):
    half_width = HEAD_DIM // 2
    frequency = ROPE_BASE ** (-2.0 * jnp.arange(half_width, dtype=F32) / HEAD_DIM)
    angles = positions.astype(F32)[:, None] * frequency[None, :]
    cosine, sine = jnp.cos(angles), jnp.sin(angles)
    return (
        jnp.concatenate([cosine] * 4, axis=1),
        jnp.concatenate([-sine, sine] * 2, axis=1),
    )


def rotate_halves(slab):
    lane = lax.broadcasted_iota(jnp.int32, slab.shape, 1)
    ahead = pltpu.roll(slab, LANES - HEAD_DIM // 2, 1)
    behind = pltpu.roll(slab, HEAD_DIM // 2, 1)
    return jnp.where(lane % HEAD_DIM < HEAD_DIM // 2, ahead, behind)


def half_mask(rows, upper):
    lane = lax.broadcasted_iota(jnp.int32, (rows, LANES), 1)
    return (lane >= HEAD_DIM) if upper else (lane < HEAD_DIM)


def spread_heads(slab, lower_out, upper_out, index):
    rows = slab.shape[0]
    moved = pltpu.roll(slab.astype(F32), HEAD_DIM, 1).astype(BF16)
    zero = jnp.zeros_like(slab)
    low, high = half_mask(rows, False), half_mask(rows, True)
    lower_out[index] = jnp.where(low, slab, zero)
    upper_out[index] = jnp.where(high, moved, zero)
    lower_out[index + 1] = jnp.where(low, moved, zero)
    upper_out[index + 1] = jnp.where(high, slab, zero)


def fill_bias(bias, seg_col, seg_row):
    span = bias.shape[0]
    for at in range(0, span, ROWS):
        rows_at = at + lax.broadcasted_iota(jnp.int32, (ROWS, span), 0)
        cols_at = lax.broadcasted_iota(jnp.int32, (ROWS, span), 1)
        allowed = (rows_at >= cols_at) & (seg_col[at : at + ROWS, :] == seg_row[...])
        bias[at : at + ROWS, :] = jnp.where(allowed, 0.0, MASK_VALUE).astype(F32)


def with_earlier(kernel, inputs, count):
    def run(*refs):
        kernel(*refs[:inputs], *refs[inputs + count :])

    return run


def any_specs(arrays):
    return [pl.BlockSpec(memory_space=pl.ANY)] * len(arrays)


def attention_forward_kernel(
    lin_ref, kv_ref, cos_ref, sin_ref, seg_col, seg_row,
    out_ref, q_ref, k_ref, v_ref, lse_ref,
    bias, k_low, k_high, v_low, v_high,
):
    slab_at = pl.program_id(0)
    span = lin_ref.shape[0]
    kv_slabs = kv_ref.shape[1] // (2 * LANES)

    @pl.when(slab_at == 0)
    def _():
        fill_bias(bias, seg_col, seg_row)
        for j in range(kv_slabs):
            lanes = slice(j * LANES, (j + 1) * LANES)
            lin = kv_ref[:, lanes]
            keys = (lin * cos_ref[...] + rotate_halves(lin) * sin_ref[...]).astype(BF16)
            k_ref[:, lanes] = keys
            spread_heads(keys, k_low, k_high, 2 * j)
            lanes = slice((kv_slabs + j) * LANES, (kv_slabs + j + 1) * LANES)
            values = kv_ref[:, lanes].astype(BF16)
            v_ref[:, slice(j * LANES, (j + 1) * LANES)] = values
            spread_heads(values, v_low, v_high, 2 * j)

    lin = lin_ref[...]
    q_ref[...] = (lin * cos_ref[...] + rotate_halves(lin) * sin_ref[...]).astype(BF16)
    kv_even, kv_odd = (2 * slab_at) // 3, (2 * slab_at + 1) // 3
    for at in range(0, span, ROWS):
        rows = slice(at, at + ROWS)
        queries = q_ref[rows, :]
        total = None
        stats = []
        for keys, values, kv_at in ((k_low, v_low, kv_even), (k_high, v_high, kv_odd)):
            upto = at + ROWS
            scores = dot(queries, keys[kv_at, :upto, :], NT) * SCORE_SCALE + bias[rows, :upto]
            highest = jnp.max(scores, axis=1, keepdims=True)
            weights = jnp.exp(scores - highest)
            summed = jnp.sum(weights, axis=1, keepdims=True)
            probability = (weights * (1.0 / summed)).astype(BF16)
            part = dot(probability, values[kv_at, :upto, :])
            total = part if total is None else total + part
            stats.append(highest + jnp.log(summed))
        out_ref[rows, :] = total.astype(BF16)
        spread = jnp.where(half_mask(ROWS, False), stats[0], stats[1])
        turned = spread.T
        lse_ref[0, 0:1, rows] = turned[0:1, :]
        lse_ref[0, 1:2, rows] = turned[HEAD_DIM : HEAD_DIM + 1, :]


def attention_forward(qkv_lin, cosine, sine, segment_row, earlier=()):
    span = qkv_lin.shape[0]
    q_width = MODEL_DIM // 2
    kv_width = (qkv_lin.shape[1] - q_width) // 2
    slabs, kv_heads = q_width // LANES, kv_width // HEAD_DIM
    whole = lambda shape: pl.BlockSpec(shape, lambda g: (0,) * len(shape))
    slab = pl.BlockSpec((span, LANES), lambda g: (0, g))
    q_lin, kv_lin = qkv_lin[:, :q_width], qkv_lin[:, q_width:]
    return pl.pallas_call(
        with_earlier(attention_forward_kernel, 6, len(earlier)),
        grid=(slabs,),
        in_specs=[
            slab, whole((span, 2 * kv_width)), whole((span, LANES)), whole((span, LANES)),
            whole((span, 1)), whole((1, span)),
        ]
        + any_specs(earlier),
        out_specs=[
            slab, slab, whole((span, kv_width)), whole((span, kv_width)),
            pl.BlockSpec((1, 8, span), lambda g: (g, 0, 0)),
        ],
        out_shape=[
            jax.ShapeDtypeStruct((span, q_width), BF16),
            jax.ShapeDtypeStruct((span, q_width), BF16),
            jax.ShapeDtypeStruct((span, kv_width), BF16),
            jax.ShapeDtypeStruct((span, kv_width), BF16),
            jax.ShapeDtypeStruct((slabs, 8, span), F32),
        ],
        scratch_shapes=[pltpu.VMEM((span, span), F32)]
        + [pltpu.VMEM((kv_heads, span, LANES), BF16)] * 4,
        compiler_params=pltpu.CompilerParams(vmem_limit_bytes=VMEM_BYTES),
        cost_estimate=pl.CostEstimate(
            flops=32 * slabs * span * span * LANES, bytes_accessed=16 * span * q_width,
            transcendentals=slabs * span * span,
        ),
        name="attention_forward",
    )(q_lin, kv_lin, cosine, sine, segment_row[:, None], segment_row[None, :], *earlier)


def attention_backward_kernel(
    q_ref, k_ref, v_ref, out_ref, grad_ref, cos_ref, sin_ref, seg_col, seg_row, lse_ref,
    dq_ref, dkv_ref,
    bias, k_low, k_high, v_low, v_high, dk_low, dk_high, dv_low, dv_high, dq_sum,
):
    slab_at = pl.program_id(0)
    span = q_ref.shape[0]
    kv_slabs = k_ref.shape[1] // LANES

    @pl.when(slab_at == 0)
    def _():
        for at in range(0, span, ROWS):
            keys_at = at + lax.broadcasted_iota(jnp.int32, (ROWS, span), 0)
            rows_at = lax.broadcasted_iota(jnp.int32, (ROWS, span), 1)
            allowed = (rows_at >= keys_at) & (seg_col[at : at + ROWS, :] == seg_row[...])
            bias[at : at + ROWS, :] = jnp.where(allowed, 0.0, MASK_VALUE).astype(F32)
        for j in range(kv_slabs):
            lanes = slice(j * LANES, (j + 1) * LANES)
            spread_heads(k_ref[:, lanes], k_low, k_high, 2 * j)
            spread_heads(v_ref[:, lanes], v_low, v_high, 2 * j)
        for sums in (dk_low, dk_high, dv_low, dv_high):
            sums[...] = jnp.zeros_like(sums)

    kv_even, kv_odd = (2 * slab_at) // 3, (2 * slab_at + 1) // 3
    for at in range(0, span, ROWS):
        rows = slice(at, at + ROWS)
        upto = at + ROWS
        queries, grads = q_ref[rows, :], grad_ref[rows, :]
        turned = (grads.astype(F32) * out_ref[rows, :].astype(F32)).T
        zero = jnp.zeros_like(queries)
        dq_part = None
        for upper, keys, values, dk_sum, dv_sum, kv_at in (
            (False, k_low, v_low, dk_low, dv_low, kv_even),
            (True, k_high, v_high, dk_high, dv_high, kv_odd),
        ):
            first = HEAD_DIM if upper else 0
            delta = jnp.sum(turned[first : first + HEAD_DIM, :], axis=0, keepdims=True)
            head = 1 if upper else 0
            total = lse_ref[0, head : head + 1, rows]
            keys_here = keys[kv_at, :upto, :]
            scores = dot(keys_here, queries, NT) * SCORE_SCALE + bias[:upto, rows]
            probability = jnp.exp(scores - total)
            prob_grad = dot(values[kv_at, :upto, :], grads, NT)
            score_grad = (probability * (prob_grad - delta)).astype(BF16)
            mask = half_mask(ROWS, upper)
            dv_sum[kv_at, :upto, :] += dot(
                probability.astype(BF16), jnp.where(mask, grads, zero)
            )
            dk_sum[kv_at, :upto, :] += dot(score_grad, jnp.where(mask, queries, zero))
            part = dot(score_grad, keys_here, TN)
            dq_part = part if dq_part is None else dq_part + part
        dq_sum[rows, :] = dq_part * SCORE_SCALE
    slab = dq_sum[...]
    dq_ref[...] = (slab * cos_ref[...] - rotate_halves(slab) * sin_ref[...]).astype(BF16)

    @pl.when(slab_at == pl.num_programs(0) - 1)
    def _():
        low = half_mask(span, False)

        def joined(sums_low, sums_high, j):
            one = sums_low[2 * j] + pltpu.roll(sums_high[2 * j], HEAD_DIM, 1)
            two = pltpu.roll(sums_low[2 * j + 1], HEAD_DIM, 1) + sums_high[2 * j + 1]
            return jnp.where(low, one, two)

        for j in range(kv_slabs):
            slab = joined(dk_low, dk_high, j) * SCORE_SCALE
            dkv_ref[:, j * LANES : (j + 1) * LANES] = (
                slab * cos_ref[...] - rotate_halves(slab) * sin_ref[...]
            ).astype(BF16)
            at = (kv_slabs + j) * LANES
            dkv_ref[:, at : at + LANES] = joined(dv_low, dv_high, j).astype(BF16)


def attention_backward(
    queries, keys, values, attended, grad, cosine, sine, segment_row, lse, earlier=()
):
    span, q_width = queries.shape
    kv_width = keys.shape[1]
    slabs, kv_heads = q_width // LANES, kv_width // HEAD_DIM
    whole = lambda shape: pl.BlockSpec(shape, lambda g: (0,) * len(shape))
    slab = pl.BlockSpec((span, LANES), lambda g: (0, g))
    return pl.pallas_call(
        with_earlier(attention_backward_kernel, 10, len(earlier)),
        grid=(slabs,),
        in_specs=[
            slab, whole((span, kv_width)), whole((span, kv_width)), slab, slab,
            whole((span, LANES)), whole((span, LANES)), whole((span, 1)), whole((1, span)),
            pl.BlockSpec((1, 8, span), lambda g: (g, 0, 0)),
        ]
        + any_specs(earlier),
        out_specs=[slab, whole((span, 2 * kv_width))],
        out_shape=[
            jax.ShapeDtypeStruct((span, q_width), BF16),
            jax.ShapeDtypeStruct((span, 2 * kv_width), BF16),
        ],
        scratch_shapes=[pltpu.VMEM((span, span), F32)]
        + [pltpu.VMEM((kv_heads, span, LANES), BF16)] * 4
        + [pltpu.VMEM((kv_heads, span, LANES), F32)] * 4
        + [pltpu.VMEM((span, LANES), F32)],
        compiler_params=pltpu.CompilerParams(vmem_limit_bytes=VMEM_BYTES),
        cost_estimate=pl.CostEstimate(
            flops=40 * slabs * span * span * LANES, bytes_accessed=16 * span * q_width,
            transcendentals=slabs * span * span,
        ),
        name="attention_backward",
    )(
        queries, keys, values, attended, grad, cosine, sine,
        segment_row[:, None], segment_row[None, :], lse, *earlier,
    )


EXPERT_ROWS = 256
EXPERT_VMEM = 63 * 1024 * 1024
SLOTS = 4
Z_FROM = (0, -1, 1, 2)
CHUNK = 2
LATE = 2
SENT = 2
MESH_ID = pl.DeviceIdType.MESH


def experts_kernel(
    inner, chunks, row_steps, x_ref, og_ref, xt_ref, ogt_ref, combine_ref,
    pairs_ref, near_ref, far_ref,
    dx_own, dx_twin, dx_other, mix_out, gate_out, *refs,
):
    keep_outs, refs = refs[:SENT], refs[SENT:]
    part_outs, refs = refs[:SENT], refs[SENT:]
    near_outs, refs = refs[: chunks - SENT], refs[chunks - SENT :]
    late_out, first_out, far_out, refs = *refs[:3], refs[3:]
    slots, arrived, held_both, held_down, dx_sum, mix_sum, twin_rows = refs[:7]
    gates, gate_kept, gate_got, gate_full, gate_twin, send, recv, local = refs[7:]
    weights, grads = slots.at[pl.ds(1, chunks)], slots
    near = Neighbours(inner)
    copies = Copies(send, recv, local)
    z, y, x, core, spots = near.z, near.y, near.x, near.core, near.spots
    step = pl.program_id(0)
    steps = row_steps + SLOTS
    chunk, turn = step // steps, step % steps
    last = chunks - 1
    width = x_ref.shape[1]
    block = width // 16
    hidden = held_down.shape[1] // CHUNK
    both = 2 * hidden * CHUNK
    lane = lax.broadcasted_iota(jnp.int32, (EXPERT_ROWS, LANES), 1)
    tokens = dx_sum.shape[0] // 2
    tiles = tokens // EXPERT_ROWS
    tile = (turn + tiles) % row_steps
    rows = pl.ds(pl.multiple_of(tile * EXPERT_ROWS, EXPERT_ROWS), EXPERT_ROWS)

    def near_piece(c, k):
        return pairs_ref.at[c] if k == 0 else near_ref.at[c, k - 1]

    def near_copy(c, k):
        copies.copy(
            lambda c=c, k=k: (near_piece(c, k), weights.at[c, spots[k], y]), ("near", c, k), False
        )

    def near_wait(c, k):
        copies.wait_copy(
            lambda c=c, k=k: (near_piece(c, k), weights.at[c, spots[k], y]), ("near", c, k)
        )

    def far_ends(c, k):
        return far_ref.at[c, k], weights.at[c, spots[k], 1 - y]

    @pl.when(step == 0)
    def _():
        near.greet()
        gates[...] = jnp.zeros_like(gates)
        for k in range(SLOTS):
            near_copy(0, k)
            copies.copy(lambda k=k: far_ends(0, k), ("far", 0, k), False)
        copies.remote(
            lambda: (pairs_ref.at[last], weights.at[last, z, y]), ("y",), ("y",), near.over_y
        )
        for k in range(1, SLOTS):
            copies.remote(
                lambda: (pairs_ref.at[last], weights.at[last, z, y]),
                ("z", k), ("z", BACK[k]), near.along[k],
            )
        for c in range(LATE, last):
            for k in range(1, SLOTS):
                copies.remote(
                    lambda c=c, k=k: (near_piece(c, k), weights.at[c, spots[k], y]),
                    ("f", c, k), ("f", c, k), near.over_y,
                )
        for c in range(1, chunks):
            for k in range(SLOTS if c < last else 1):
                near_copy(c, k)
                if c < LATE or (c < last and k == 0):
                    copies.copy(lambda c=c, k=k: far_ends(c, k), ("far", c, k), False)

    @pl.when(step == row_steps)
    def _():
        copies.arrived(weights.at[last, z, 1 - y], ("y",), near.over_y)
        for k in range(1, SLOTS):
            copies.remote(
                lambda: (weights.at[last, z, 1 - y],) * 2,
                ("z2", k), ("z2", BACK[k]), near.along[k],
            )

    for c in range(chunks):

        @pl.when(step == c * steps)
        def _():
            for k in range(SLOTS):
                if c < last or k == 0:
                    near_wait(c, k)
                if c < LATE or (c < last and k == 0):
                    copies.wait_copy(lambda c=c, k=k: far_ends(c, k), ("far", c, k))
                elif c < last:
                    copies.arrived(weights.at[c, spots[k], 1 - y], ("f", c, k), near.over_y)
                elif k > 0:
                    copies.arrived(weights.at[c, spots[k], y], ("z", k), near.along[k])
                    copies.arrived(weights.at[c, spots[k], 1 - y], ("z2", k), near.along[k])

    def add_arrived(c):
        copies.arrived(arrived.at[c], ("sum", c), near.over_y)
        for k in range(SLOTS):
            own = grads.at[c, spots[k], y]
            own[...] = (own[...].astype(F32) + arrived[c, spots[k]].astype(F32)).astype(BF16)
        copies.copy(lambda c=c: (grads.at[c, z, y], keep_outs[c]), ("keep", c))
        for k in range(1, SLOTS):
            copies.remote(
                lambda c=c, k=k: (grads.at[c, spots[k], y], part_outs[c].at[BACK[k] - 1]),
                ("part", c, k), ("part", c, BACK[k]), near.along[k],
            )

    @pl.when(step == 2 * steps + 3)
    def _():
        add_arrived(0)

    @pl.when(step == 3 * steps + 3)
    def _():
        add_arrived(1)

    @pl.when(turn < row_steps)
    def _():
        for e in range(CHUNK):
            first = 2 * hidden * e
            w_both = weights[chunk, :, :, :, first : first + 2 * hidden].reshape(width, 2 * hidden)
            start = both + hidden * e
            w_down = weights[chunk, :, :, :, start : start + hidden].reshape(width, hidden)
            gate_up = dot(x_ref[...], w_both)
            raw = dot(og_ref[...], w_down) * RESIDUAL_SCALE
            gate, up = gate_up[:, :hidden], gate_up[:, hidden:]
            gate_lane = lax.broadcasted_iota(
                jnp.int32, (EXPERT_ROWS, combine_ref.shape[1]), 1
            )
            column = jnp.sum(
                jnp.where(gate_lane == chunk * CHUNK + e, combine_ref[...], 0.0),
                axis=1, keepdims=True,
            )
            sigmoid = 1.0 / (1.0 + jnp.exp(-gate))
            active = gate * sigmoid
            inner_value = (active * up).astype(BF16).astype(F32)
            held_down[rows, hidden * e : hidden * (e + 1)] = (inner_value * column).astype(BF16)
            gates[rows, :] = jnp.where(
                lane == chunk * CHUNK + e,
                jnp.sum(inner_value * raw, axis=1, keepdims=True),
                gates[rows, :],
            )
            inner_grad = raw * column
            held_both[rows, first : first + hidden] = (
                inner_grad * up * sigmoid * (1.0 + gate * (1.0 - sigmoid))
            ).astype(BF16)
            held_both[rows, first + hidden : first + 2 * hidden] = (inner_grad * active).astype(BF16)

        def sums(add):
            for part in range(SLOTS):
                cols = slice(4 * block * part, 4 * block * (part + 1))
                w_both = weights[chunk, part, :, :, :both].reshape(4 * block, both)
                w_down = weights[chunk, part, :, :, both:].reshape(4 * block, hidden * CHUNK)
                mix = dot(held_down[rows, :], w_down, NT)
                dx = dot(held_both[rows, :], w_both, NT)
                if add:
                    mix = mix + mix_sum[rows, cols].astype(F32)
                    dx = dx + dx_sum[rows, cols].astype(F32)
                mix_sum[rows, cols] = mix.astype(BF16)
                dx_sum[rows, cols] = dx.astype(BF16)

        @pl.when(chunk == 0)
        def _():
            sums(False)

        @pl.when(chunk > 0)
        def _():
            sums(True)

    @pl.when(turn >= row_steps)
    def _():
        part = turn - row_steps
        grads[chunk, part, :, :, :both] = (
            dot(xt_ref[...], held_both[...]).astype(BF16).reshape(2, 2 * block, both)
        )
        grads[chunk, part, :, :, both:] = (
            (dot(ogt_ref[...], held_down[...]) * RESIDUAL_SCALE)
            .astype(BF16)
            .reshape(2, 2 * block, hidden * CHUNK)
        )

    begin = last * steps
    for i in range(2):
        for c in range(2):
            mine = pl.ds(tokens + (2 * c + i) * EXPERT_ROWS, EXPERT_ROWS)
            there = pl.ds((2 * c + i) * EXPERT_ROWS, EXPERT_ROWS)

            @pl.when((step == begin + 2 * c + i) & (core != c))
            def _():
                copies.remote(
                    lambda: (dx_sum.at[mine], twin_rows.at[i]), ("t", i), ("t", i), near.twin,
                    last=False,
                )

            @pl.when((step == begin + 2 + 2 * c + i) & (core == c))
            def _():
                copies.arrived(twin_rows.at[i], ("t", i), near.twin)
                dx_sum[mine, :] = (
                    dx_sum[mine, :].astype(F32) + twin_rows[i].astype(F32)
                ).astype(BF16)
                copies.remote(
                    lambda: (dx_sum.at[mine], dx_other.at[there]), ("o", i), ("o", i), near.over_x,
                    last=False,
                )

            @pl.when((step == begin + steps - 2 + i) & (core == c))
            def _():
                copies.arrived(dx_other.at[there], ("o", i), near.over_x)
                copies.remote(
                    lambda: (dx_other.at[there],) * 2, ("o2", i), ("o2", i), near.twin, last=False
                )

    for i in range(tiles):

        @pl.when(step == begin + tiles + i)
        def _():
            own = pl.ds(i * EXPERT_ROWS, EXPERT_ROWS)
            copies.copy(lambda own=own: (dx_sum.at[own], dx_own.at[own]), ("own", i))
            copies.remote(
                lambda own=own: (dx_sum.at[own], dx_twin.at[own]), ("own", i), ("own", i), near.twin
            )

    shares = gate_kept.shape[0]

    @pl.when(step == begin + row_steps)
    def _():
        copies.copy(lambda: (mix_sum, mix_out), "mix")
        turned = gates[...].T[:shares, :]
        gate_kept[...] = turned
        copies.remote(
            lambda: (gate_kept.at[:, pl.ds(tokens, tokens)], gate_got), ("g",), ("g",), near.over_x
        )

    @pl.when(step == begin + steps - 2)
    def _():
        copies.arrived(gate_got, ("g",), near.over_x)
        gate_full[pl.ds(pl.multiple_of(x * shares, shares), shares), :] = gate_kept[:, :tokens]
        gate_full[pl.ds(pl.multiple_of((1 - x) * shares, shares), shares), :] = gate_got[...]
        copies.remote(lambda: (gate_full, gate_twin), ("g2",), ("g2",), near.twin)

    for c in range(chunks):

        @pl.when(step == (c + 1) * steps - 1)
        def _():
            if c < SENT:
                copies.remote(
                    lambda c=c: (grads.at[c, :, 1 - y], arrived.at[c]),
                    ("sum", c), ("sum", c), near.over_y,
                )
            else:
                for k in range(SLOTS):
                    copies.copy(
                        lambda c=c, k=k: (grads.at[c, spots[k], y], near_outs[c - SENT].at[k]),
                        ("near out", c, k),
                    )
                    if c < last and k == 0:
                        copies.copy(lambda c=c: (grads.at[c, z, 1 - y], first_out), "first out")
                    elif c < last:
                        copies.remote(
                            lambda c=c, k=k: (grads.at[c, spots[k], 1 - y], late_out.at[k - 1]),
                            ("late", k), ("late", k), near.over_y,
                        )
                    else:
                        copies.copy(
                            lambda c=c, k=k: (grads.at[c, spots[k], 1 - y], far_out.at[k]),
                            ("far out", k),
                        )

    @pl.when(step == chunks * steps - 1)
    def _():
        copies.arrived(gate_twin, ("g2",), near.twin)
        gate_out[...] = gate_full[...] + gate_twin[...]
        for i in range(tiles):
            copies.arrived(
                dx_twin.at[pl.ds(i * EXPERT_ROWS, EXPERT_ROWS)], ("own", i), near.twin
            )
        for i in range(2):
            for c in range(2):
                mine = pl.ds(tokens + (2 * c + i) * EXPERT_ROWS, EXPERT_ROWS)
                there = pl.ds((2 * c + i) * EXPERT_ROWS, EXPERT_ROWS)

                @pl.when(core != c)
                def _():
                    copies.sent(lambda: (dx_sum.at[mine], twin_rows.at[i]), ("t", i), near.twin)
                    copies.arrived(dx_other.at[there], ("o2", i), near.twin)

                @pl.when(core == c)
                def _():
                    copies.sent(
                        lambda: (dx_sum.at[mine], dx_other.at[there]), ("o", i), near.over_x
                    )
                    copies.sent(lambda: (dx_other.at[there],) * 2, ("o2", i), near.twin)

        for c in range(SENT):
            for k in range(1, SLOTS):
                copies.arrived(part_outs[c].at[k - 1], ("part", c, k), near.along[k])
        for k in range(1, SLOTS):
            copies.arrived(late_out.at[k - 1], ("late", k), near.over_y)
        copies.finish()


def experts_pass(x, og, xt, ogt, combine, pairs, near, far):
    tokens, width = x.shape
    chunks, pair, columns = pairs.shape
    hidden = columns // (3 * CHUNK)
    shares = chunks * CHUNK
    row_steps = tokens // EXPERT_ROWS
    steps = row_steps + SLOTS
    inner = lax.axis_size("dp") // 16
    row_at = lambda s: ((jnp.minimum(s % steps, row_steps - 1) + row_steps // 2) % row_steps, 0)
    width_at = lambda s: (jnp.maximum(s % steps - row_steps, 0), 0)
    row = pl.BlockSpec((EXPERT_ROWS, width), row_at)
    turned = pl.BlockSpec((width // SLOTS, tokens), width_at)
    anywhere = pl.BlockSpec(memory_space=pl.ANY)
    left = chunks - SENT
    dma = pltpu.SemaphoreType.DMA
    shape = jax.ShapeDtypeStruct
    outs = pl.pallas_call(
        functools.partial(experts_kernel, inner, chunks, row_steps),
        grid=(chunks * steps,),
        in_specs=[row, row, turned, turned, pl.BlockSpec((EXPERT_ROWS, combine.shape[1]), row_at)]
        + [anywhere] * 3,
        out_specs=[anywhere] * 4
        + [pl.BlockSpec((2 * shares, tokens // 2), lambda s: (0, 0))]
        + [anywhere] * (2 * SENT + left + 3),
        out_shape=[shape((tokens // 2, width), BF16)] * 3
        + [shape((tokens, width), BF16), shape((2 * shares, tokens // 2), F32)]
        + [shape((pair, columns), BF16)] * SENT
        + [shape((SLOTS - 1, pair, columns), BF16)] * SENT
        + [shape((SLOTS, pair, columns), BF16)] * left
        + [shape((SLOTS - 1, pair, columns), BF16), shape((pair, columns), BF16)]
        + [shape((SLOTS, pair, columns), BF16)],
        scratch_shapes=[
            pltpu.VMEM((chunks + 1, SLOTS, 2, pair, columns), BF16),
            pltpu.VMEM((SENT, SLOTS, pair, columns), BF16),
            pltpu.VMEM((tokens, 2 * hidden * CHUNK), BF16),
            pltpu.VMEM((tokens, hidden * CHUNK), BF16),
            pltpu.VMEM((tokens, width), BF16),
            pltpu.VMEM((tokens, width), BF16),
            pltpu.VMEM((2, EXPERT_ROWS, width), BF16),
            pltpu.VMEM((tokens, LANES), F32),
            pltpu.VMEM((shares, tokens), F32),
            pltpu.VMEM((shares, tokens // 2), F32),
            pltpu.VMEM((2 * shares, tokens // 2), F32),
            pltpu.VMEM((2 * shares, tokens // 2), F32),
            dma((48,)), dma((48,)), dma((48,)),
        ],
        compiler_params=pltpu.CompilerParams(
            vmem_limit_bytes=EXPERT_VMEM, collective_id=0, has_side_effects=True
        ),
        cost_estimate=pl.CostEstimate(
            flops=8 * tokens * width * chunks * columns,
            bytes_accessed=2 * chunks * width * columns, transcendentals=0,
        ),
        name="experts_pass",
    )(x, og, xt, ogt, combine, pairs, near, far)
    dx, mix, gate = outs[:3], outs[3], outs[4]
    rest = outs[5:]
    keep, parts, rest = rest[:SENT], rest[SENT : 2 * SENT], rest[2 * SENT :]
    return dx, mix, gate, keep, parts, rest[:left], rest[left:]


class Copies:
    def __init__(self, send, recv, local):
        self.send, self.recv, self.local = send, recv, local
        self.sends, self.recvs, self.locals, self.started = {}, {}, {}, []

    def remote(self, ends, name, arrives, device, last=True):
        sent = self.sends.setdefault(name, len(self.sends))
        got = self.recvs.setdefault(arrives, len(self.recvs))

        def make():
            source, target = ends()
            return pltpu.make_async_remote_copy(
                source, target, self.send.at[sent], self.recv.at[got],
                device_id=device, device_id_type=MESH_ID,
            )

        make().start()
        if last:
            self.started.append(lambda: make().wait_send())

    def sent(self, ends, name, device):
        source, target = ends()
        pltpu.make_async_remote_copy(
            source, target, self.send.at[self.sends[name]], self.recv.at[0],
            device_id=device, device_id_type=MESH_ID,
        ).wait_send()

    def arrived(self, place, name, device):
        got = self.recvs.setdefault(name, len(self.recvs))
        pltpu.make_async_remote_copy(
            place, place, self.send.at[0], self.recv.at[got],
            device_id=device, device_id_type=MESH_ID,
        ).wait_recv()

    def copy(self, ends, name, wait_last=True):
        at = self.locals.setdefault(name, len(self.locals))

        def make():
            return pltpu.make_async_copy(*ends(), self.local.at[at])

        make().start()
        if wait_last:
            self.started.append(lambda: make().wait())
        return lambda: make().wait()

    def wait_copy(self, ends, name):
        pltpu.make_async_copy(*ends(), self.local.at[self.locals[name]]).wait()

    def finish(self):
        for wait in self.started:
            wait()


class Neighbours:
    def __init__(self, inner):
        me = lax.axis_index("dp")
        at = me // inner
        self.core = lax.axis_index("tensor")
        self.z, self.y, self.x = at // 4, at // 2 % 2, at % 2
        self.spots = [(self.z + dz + 4) % 4 for dz in Z_FROM]
        self.along = [{"dp": me + (spot - self.z) * 4 * inner} for spot in self.spots]
        self.over_y = {"dp": me + (1 - 2 * self.y) * 2 * inner}
        self.over_x = {"dp": me + (1 - 2 * self.x) * inner}
        self.twin = {"tensor": 1 - self.core}
        self.blocks = {
            (k, other_y, other_x): self.spots[k] * 4
            + (1 - self.y if other_y else self.y) * 2
            + (1 - self.x if other_x else self.x)
            for k in range(SLOTS)
            for other_y in (0, 1)
            for other_x in (0, 1)
        }

    def greet(self):
        barrier = pltpu.get_barrier_semaphore()
        devices = [*self.along[1:], self.over_y, self.over_x, self.twin]
        for device in devices:
            pl.semaphore_signal(barrier, inc=1, device_id=device, device_id_type=MESH_ID)
        pl.semaphore_wait(barrier, len(devices))

    def block(self, k, other_y, other_x):
        return self.blocks[k, other_y, other_x]


BACK = (0, 2, 1, 3)


class Gather:
    def __init__(self, copies, near, shard, full, tag):
        self.copies, self.near, self.shard, self.full, self.tag = copies, near, shard, full, tag
        self.split = full.shape[2] // (2 * LANES) * LANES

    def source(self, k):
        return self.shard if k == 0 else self.full.at[self.near.block(k, 0, 0)]

    def begin(self):
        for k in range(1, SLOTS):
            self.copies.remote(
                lambda: (self.shard, self.full.at[self.near.block(0, 0, 0)]),
                (self.tag, "z", k), (self.tag, "z", BACK[k]), self.near.along[k],
            )
        self.full[self.near.block(0, 0, 0)] = self.shard[...]

    def spread(self, k):
        near, place = self.near, self.full.at[self.near.block(k, 0, 0)]
        if k > 0:
            self.copies.arrived(place, (self.tag, "z", k), near.along[k])
        for way, device in (("y", near.over_y), ("x", near.over_x)):
            name = (self.tag, way, k)
            self.copies.remote(
                lambda: (self.source(k), self.full.at[near.block(k, 0, 0)]), name, name, device
            )

    def cross(self, k):
        near = self.near
        from_y = self.full.at[near.block(k, 1, 0)]
        from_x = self.full.at[near.block(k, 0, 1)]
        self.copies.arrived(from_y, (self.tag, "y", k), near.over_y)
        self.copies.remote(
            lambda: (self.full.at[near.block(k, 1, 0), :, : self.split],) * 2,
            (self.tag, "one", k), (self.tag, "one", k), near.over_x,
        )
        self.copies.arrived(from_x, (self.tag, "x", k), near.over_x)
        self.copies.remote(
            lambda: (self.full.at[near.block(k, 0, 1), :, self.split :],) * 2,
            (self.tag, "two", k), (self.tag, "two", k), near.over_y,
        )

    def end(self):
        near = self.near
        for k in range(SLOTS):
            place = self.full.at[near.block(k, 1, 1)]
            self.copies.arrived(place.at[:, : self.split], (self.tag, "one", k), near.over_x)
            self.copies.arrived(place.at[:, self.split :], (self.tag, "two", k), near.over_y)


def roll_left(slab, lanes):
    return pltpu.roll(slab, LANES - lanes, 1)


def forward_kernel(
    inner, q_shard, o_shard, gateup_hbm, down_hbm, hidden_hbm, og_hbm, cos, sin, seg_col, seg_row,
    routes,
    q_full, o_full, small, normed, q_ref, k_ref, v_ref, attended, lse_ref, combine, combine_pair,
    middle_hbm, x_hbm, xt_hbm, og_pair, ogt_hbm, pairs_hbm, near_hbm, far_hbm,
    hidden, gateup, down, given, pairs, bias, k_low, k_high, v_low, v_high, part, part_got, x_own, x_got,
    middle, stage, turned, columns_out, columns_got, send, recv, local,
):
    near = Neighbours(inner)
    copies = Copies(send, recv, local)
    tokens, width = hidden.shape
    block = width // 16
    chunks = pairs.shape[0]
    hid = down.shape[2]
    q_width = q_ref.shape[1]
    kv_slabs = k_ref.shape[1] // LANES
    slabs = q_width // LANES
    qkv_width = q_width + 2 * k_ref.shape[1]
    experts = down.shape[0]
    each = 2 + experts
    half = tokens // 2
    tiles = tokens // ROWS
    x, core = near.x, near.core
    own_half = pl.ds(pl.multiple_of(core * half, half), half)
    mine = pl.ds(pl.multiple_of(tokens + core * half, half), half)
    theirs = pl.ds(pl.multiple_of(tokens + (1 - core) * half, half), half)

    near.greet()
    gather_q = Gather(copies, near, q_shard, q_full, "q")
    gather_o = Gather(copies, near, o_shard, o_full, "o")
    gather_q.begin()
    gather_q.spread(0)
    weights_in = [
        copies.copy(lambda: (gateup_hbm, gateup), "gateup", False),
        copies.copy(lambda: (down_hbm, down), "down", False),
    ]
    hidden_in = copies.copy(lambda: (hidden_hbm, hidden), "hidden", False)
    copies.copy(lambda: (og_hbm, og_pair.at[pl.ds(0, tokens)]), "og")

    def pack(c, mine):
        first = 2 * (chunks * (x if mine else 1 - x) + c)
        rows = pl.ds(pl.multiple_of(x * block, block), block)
        for e in range(CHUNK):
            for part_at in range(2):
                at = hid * (2 * e + part_at)
                value = gateup[first + e, part_at].astype(BF16)
                if mine:
                    pairs[c, rows, at : at + hid] = value
                else:
                    given[c, :, at : at + hid] = value
            at = hid * (2 * CHUNK + e)
            value = down[first + e].astype(BF16)
            if mine:
                pairs[c, rows, at : at + hid] = value
            else:
                given[c, :, at : at + hid] = value

    def swap(c):
        rows = pl.ds(pl.multiple_of(x * block, block), block)
        copies.remote(
            lambda: (given.at[c], pairs.at[c, rows]), ("s", c), ("s", c), near.over_x
        )

    def swapped(c):
        rows = pl.ds(pl.multiple_of((1 - x) * block, block), block)
        copies.arrived(pairs.at[c, rows], ("s", c), near.over_x)

    def ring_one(c):
        copies.remote(
            lambda: (pairs.at[c], near_hbm.at[c, 0]), ("up", c), ("r", c, 1), near.along[2]
        )
        copies.remote(
            lambda: (pairs.at[c], near_hbm.at[c, 1]), ("down", c), ("r", c, 2), near.along[1]
        )

    def ring_two(c):
        copies.arrived(near_hbm.at[c, 0], ("r", c, 1), near.along[1])
        copies.remote(
            lambda: (near_hbm.at[c, 0], near_hbm.at[c, 2]), ("two", c), ("r", c, 3), near.along[2]
        )

    def over_y(c, k):
        copies.remote(
            lambda: (pairs.at[c] if k == 0 else near_hbm.at[c, k - 1], far_hbm.at[c, k]),
            ("f", c, k), ("f", c, k), near.over_y,
        )

    def ring_got(c, k):
        copies.arrived(near_hbm.at[c, k - 1], ("r", c, k), near.along[k])

    def turn_tile(source, target, name, side):
        copies.copy(lambda: (source, stage.at[side]), (name, "in"), False)()
        turned[side] = stage[side].T
        return copies.copy(lambda: (turned.at[side], target), (name, "out"), False)

    waits = [None, None]

    def turn_next(source, target, name, side):
        if waits[side] is not None:
            waits[side]()
        waits[side] = turn_tile(source, target, name, side)

    for wait in weights_in:
        wait()
    pack(0, False)
    swap(0)
    pack(0, True)
    gather_q.spread(1)
    gather_q.spread(2)
    pack(1, False)
    pack(1, True)
    gather_q.cross(0)
    gather_q.spread(3)
    gather_o.begin()
    pack(2, False)
    pack(2, True)
    gather_q.cross(1)
    gather_q.cross(2)
    swapped(0)
    ring_one(0)
    pack(3, False)
    pack(3, True)
    fill_bias(bias, seg_col, seg_row)
    gather_q.cross(3)
    over_y(0, 0)
    gather_o.spread(0)
    for c in range(1, chunks):
        swap(c)
    for tile in range(tiles):
        rows = pl.ds(tile * ROWS, ROWS)
        turn_next(og_hbm.at[rows], ogt_hbm.at[:, rows], ("og", tile), tile % 2)
    hidden_in()
    gather_q.end()
    pieces = q_full[:, :, qkv_width:].reshape(width, LANES)
    wide = pieces.astype(F32)
    summed = wide + roll_left(wide, each) + roll_left(wide, 2 * each)
    small[...] = summed.T[: small.shape[0], :]

    def project(tile, carry):
        rows = pl.ds(pl.multiple_of(tile * ROWS, ROWS), ROWS)
        value = hidden[rows, :].astype(F32)
        inverse = lax.rsqrt(jnp.mean(value * value, axis=1, keepdims=True) + NORM_EPSILON)
        low = (value * inverse * small[0:1, :]).astype(BF16)
        normed[:, rows] = low.T
        cosine, sine = cos[rows, :], sin[rows, :]
        for g in range(slabs + 2 * kv_slabs):
            lanes = slice(g * LANES, (g + 1) * LANES)
            if g % 2 == 0:
                two = slice(g * LANES, (g + 2) * LANES)
                lin_two = dot(low, q_full[:, :, two].reshape(width, 2 * LANES))
            lin = lin_two[:, (g % 2) * LANES : (g % 2 + 1) * LANES]
            if g < slabs + kv_slabs:
                lin = lin * cosine + rotate_halves(lin) * sine
            if g < slabs:
                q_ref[rows, lanes] = lin.astype(BF16)
            elif g < slabs + kv_slabs:
                at = (g - slabs) * LANES
                k_ref[rows, at : at + LANES] = lin.astype(BF16)
            else:
                at = (g - slabs - kv_slabs) * LANES
                v_ref[rows, at : at + LANES] = lin.astype(BF16)

        @pl.when(tile == 0)
        def _():
            gather_o.spread(1)
            gather_o.spread(2)

        @pl.when(tile == 2)
        def _():
            gather_o.spread(3)
            gather_o.cross(0)

        return carry

    lax.fori_loop(0, tiles, project, 0)
    for j in range(kv_slabs):
        lanes = slice(j * LANES, (j + 1) * LANES)
        spread_heads(k_ref[:, lanes], k_low, k_high, 2 * j)
        spread_heads(v_ref[:, lanes], v_low, v_high, 2 * j)

    def attend(g, carry):
        lanes = pl.ds(pl.multiple_of(g * LANES, LANES), LANES)
        kv_even, kv_odd = (2 * g) // 3, (2 * g + 1) // 3
        for at in range(0, tokens, ROWS):
            rows = slice(at, at + ROWS)
            upto = at + ROWS
            queries = q_ref[rows, lanes]
            total = None
            stats = []
            for keys, values, kv_at in ((k_low, v_low, kv_even), (k_high, v_high, kv_odd)):
                scores = dot(queries, keys[kv_at, :upto, :], NT) * SCORE_SCALE + bias[rows, :upto]
                highest = jnp.max(scores, axis=1, keepdims=True)
                weights = jnp.exp(scores - highest)
                whole = jnp.sum(weights, axis=1, keepdims=True)
                probability = (weights * (1.0 / whole)).astype(BF16)
                one = dot(probability, values[kv_at, :upto, :])
                total = one if total is None else total + one
                stats.append(highest + jnp.log(whole))
            attended[rows, lanes] = total.astype(BF16)
            across = jnp.where(half_mask(ROWS, False), stats[0], stats[1]).T
            lse_ref[g, 0:1, rows] = across[0:1, :]
            lse_ref[g, 1:2, rows] = across[HEAD_DIM : HEAD_DIM + 1, :]

        @pl.when(g == 0)
        def _():
            gather_o.cross(1)
            gather_o.cross(2)
            ring_two(0)
            over_y(0, 1)
            swapped(1)
            ring_one(1)
            over_y(1, 0)

        @pl.when(g == 1)
        def _():
            gather_o.cross(3)
            ring_got(0, 2)
            over_y(0, 2)
            copies.remote(
                lambda: (og_hbm.at[own_half], og_pair.at[mine]), ("og",), ("og",), near.over_x
            )

        @pl.when(g == slabs - 1)
        def _():
            ring_got(0, 3)
            over_y(0, 3)
            gather_o.end()

        return carry

    lax.fori_loop(0, slabs, attend, 0)

    def project_out(step, carry):
        tile = (step + 2 * (1 - core)) % tiles
        rows = pl.ds(pl.multiple_of(tile * ROWS, ROWS), ROWS)
        low = attended[rows, :]
        for group in range(SLOTS):
            cols = slice(4 * block * group, 4 * block * (group + 1))
            weight = o_full[4 * group : 4 * (group + 1)].reshape(4 * block, q_width)
            part[rows, cols] = dot(low, weight, NT).astype(BF16)
        return carry

    for step in range(tiles):
        project_out(step, 0)
        tile = (step + 2 * (1 - core)) % tiles
        rows = pl.ds(pl.multiple_of(tile * ROWS, ROWS), ROWS)
        copies.remote(
            lambda rows=rows: (part.at[rows], part_got.at[rows]),
            ("p", step), ("p", step), near.twin,
        )
    swapped(2)
    ring_one(2)
    over_y(2, 0)
    router = q_full[:, :, qkv_width:].reshape(width, LANES)
    for step in range(tiles):
        tile = (step + 2 * core) % tiles
        rows = pl.ds(pl.multiple_of(tile * ROWS, ROWS), ROWS)
        copies.arrived(part_got.at[rows], ("p", step), near.twin)
        side = step % 2
        if step >= 2:
            middle_out[side]()
        elif step == 0:
            middle_out = [None, None]
        total = hidden[rows, :].astype(F32) + RESIDUAL_SCALE * (
            part[rows, :].astype(F32) + part_got[rows, :].astype(F32)
        )
        middle[side] = total
        middle_out[side] = copies.copy(
            lambda rows=rows, side=side: (middle.at[side], middle_hbm.at[rows]), ("m", step), False
        )
        inverse = lax.rsqrt(jnp.mean(total * total, axis=1, keepdims=True) + NORM_EPSILON)
        value = total * inverse * small[1:2, :]
        high = value.astype(BF16)
        x_own[rows, :] = high
        copies.copy(lambda rows=rows: (x_own.at[rows], x_hbm.at[rows]), ("x", step))
        if step < 2:
            copies.remote(
                lambda rows=rows: (x_own.at[rows], x_got.at[rows]),
                ("x", step), ("x", step), near.over_x,
            )
        rest = value - high.astype(F32)
        mid = rest.astype(BF16)
        low = (rest - mid.astype(F32)).astype(BF16)
        one, two, three = dot(high, router), dot(mid, router), dot(low, router)
        logits = one + roll_left(one, each) + roll_left(one, 2 * each) + two + roll_left(two, each)
        logits = roll_left(logits + three, 2)
        lane = lax.broadcasted_iota(jnp.int32, (ROWS, LANES), 1)
        chosen = lane < 0
        route = routes[rows, :]
        for k in range(routes.shape[1]):
            chosen = chosen | (route[:, k : k + 1] == lane)
        logits = jnp.where(chosen, logits, MASK_VALUE)
        powers = jnp.exp(logits - jnp.max(logits, axis=1, keepdims=True))
        powers = jnp.where(chosen, powers, 0.0)
        combine[rows, :] = powers * (1.0 / jnp.sum(powers, axis=1, keepdims=True))
        if step == 0:
            swapped(3)
            copies.copy(lambda: (pairs, pairs_hbm), "pairs")
        if step == 1:
            ring_two(1)
            over_y(1, 1)
            ring_got(1, 2)
            over_y(1, 2)

    shares = experts // 2
    flipped = combine[...].T
    kept = jnp.where(x == 0, flipped[:shares, :], flipped[shares : 2 * shares, :])
    gone = jnp.where(x == 0, flipped[shares : 2 * shares, :], flipped[:shares, :])
    columns_out[...] = gone
    copies.remote(lambda: (columns_out, columns_got), ("c",), ("c",), near.over_x)
    combine_pair[:tokens, :] = kept.T

    copies.arrived(og_pair.at[mine], ("og",), near.over_x)
    copies.remote(lambda: (og_pair.at[mine],) * 2, ("og2",), ("og2",), near.twin)
    for tile in range(tiles):
        rows = pl.ds(tile * ROWS, ROWS)
        if waits[tile % 2] is not None:
            waits[tile % 2]()
        turned[tile % 2] = x_own[rows, :].T
        waits[tile % 2] = copies.copy(
            lambda rows=rows, side=tile % 2: (turned.at[side], xt_hbm.at[:, rows]),
            ("xt", tile), False,
        )
    ring_two(2)
    ring_got(1, 3)
    over_y(1, 3)
    copies.arrived(columns_got, ("c",), near.over_x)
    combine_pair[tokens:, :] = columns_got[...].T
    copies.arrived(og_pair.at[theirs], ("og2",), near.twin)
    order = [(step + 2 * core) % tiles for step in range(2)]
    order += [(step + 2 * (1 - core)) % tiles for step in range(2)]

    def og_rows(step):
        return pl.ds(pl.multiple_of(tokens + order[step] * ROWS, ROWS), ROWS)

    def og_load(step):
        return copies.copy(
            lambda: (og_pair.at[og_rows(step)], stage.at[step % 2]), ("ogin", step), False
        )

    loaded = og_load(0)
    for step in range(tiles):
        loaded()
        if step + 1 < tiles:
            loaded = og_load(step + 1)
        side = step % 2
        waits[side]()
        turned[side] = stage[side].T
        waits[side] = copies.copy(
            lambda step=step, side=side: (turned.at[side], ogt_hbm.at[:, og_rows(step)]),
            ("ogt", step), False,
        )
    for step in range(tiles):
        rows = pl.ds(pl.multiple_of(order[step] * ROWS, ROWS), ROWS)
        there = pl.ds(pl.multiple_of(tokens + order[step] * ROWS, ROWS), ROWS)
        if step < 2:
            copies.arrived(x_got.at[rows], ("x", step), near.over_x)
            copies.remote(
                lambda rows=rows: (x_got.at[rows],) * 2, ("x2", step), ("x2", step), near.twin
            )
        else:
            copies.arrived(x_got.at[rows], ("x2", step - 2), near.twin)
        copies.copy(
            lambda rows=rows, there=there: (x_got.at[rows], x_hbm.at[there]), ("xg", step)
        )
        side = step % 2
        waits[side]()
        turned[side] = x_got[rows, :].T
        waits[side] = copies.copy(
            lambda there=there, side=side: (turned.at[side], xt_hbm.at[:, there]),
            ("xgt", step), False,
        )
    for wait in waits + middle_out:
        wait()
    ring_got(2, 2)
    ring_got(2, 3)
    for c in range(LATE + 1):
        for k in range(SLOTS if c < LATE else 1):
            copies.arrived(far_hbm.at[c, k], ("f", c, k), near.over_y)
    copies.finish()


def forward_pass(q_shard, o_shard, gateup, down, hidden, og, cosine, sine, segments, routes):
    tokens, width = hidden.shape
    experts, hid = down.shape[0], down.shape[2]
    block, q_columns = q_shard.shape
    q_width = o_shard.shape[1]
    kv_width = (q_columns - LANES - q_width) // 2
    slabs, kv_heads = q_width // LANES, kv_width // HEAD_DIM
    chunks = experts // (2 * CHUNK)
    columns = 3 * CHUNK * hid
    anywhere, vmem = pl.BlockSpec(memory_space=pl.ANY), vmem_spec()
    shape = jax.ShapeDtypeStruct
    inner = lax.axis_size("dp") // 16
    dma = pltpu.SemaphoreType.DMA
    return pl.pallas_call(
        functools.partial(forward_kernel, inner),
        in_specs=[vmem, vmem] + [anywhere] * 4 + [vmem] * 5,
        out_specs=[vmem] * 11 + [anywhere] * 8,
        out_shape=[
            shape((16, block, q_columns), BF16),
            shape((16, block, q_width), BF16),
            shape((24, width), F32),
            shape((width, tokens), BF16),
            shape((tokens, q_width), BF16),
            shape((tokens, kv_width), BF16),
            shape((tokens, kv_width), BF16),
            shape((tokens, q_width), BF16),
            shape((slabs, 8, tokens), F32),
            shape((tokens, LANES), F32),
            shape((2 * tokens, experts // 2), F32),
            shape((tokens, width), F32),
            shape((2 * tokens, width), BF16),
            shape((width, 2 * tokens), BF16),
            shape((2 * tokens, width), BF16),
            shape((width, 2 * tokens), BF16),
            shape((chunks, 2 * block, columns), BF16),
            shape((chunks - 1, SLOTS - 1, 2 * block, columns), BF16),
            shape((LATE + 1, SLOTS, 2 * block, columns), BF16),
        ],
        scratch_shapes=[
            pltpu.VMEM((tokens, width), BF16),
            pltpu.VMEM(gateup.shape, gateup.dtype),
            pltpu.VMEM(down.shape, down.dtype),
            pltpu.VMEM((chunks, block, columns), BF16),
            pltpu.VMEM((chunks, 2 * block, columns), BF16),
            pltpu.VMEM((tokens, tokens), F32),
        ]
        + [pltpu.VMEM((kv_heads, tokens, LANES), BF16)] * 4
        + [pltpu.VMEM((tokens, width), BF16)] * 4
        + [
            pltpu.VMEM((2, ROWS, width), F32),
            pltpu.VMEM((2, ROWS, width), BF16),
            pltpu.VMEM((2, width, ROWS), BF16),
            pltpu.VMEM((experts // 2, tokens), F32),
            pltpu.VMEM((experts // 2, tokens), F32),
            dma((80,)), dma((80,)), dma((60,)),
        ],
        compiler_params=pltpu.CompilerParams(
            vmem_limit_bytes=EXPERT_VMEM, collective_id=1, has_side_effects=True
        ),
        name="forward_pass",
    )(
        q_shard, o_shard, gateup, down, hidden, og, cosine, sine,
        segments[:, None], segments[None, :], routes,
    )


class Scatter:
    def __init__(self, copies, near, grad, one, two, got_y, got_x, got_z, share, tag):
        self.copies, self.near, self.grad, self.share, self.tag = copies, near, grad, share, tag
        self.one, self.two, self.got_y, self.got_x, self.got_z = one, two, got_y, got_x, got_z
        self.split = one.shape[2]

    def begin(self, k):
        near = self.near
        self.copies.remote(
            lambda: (self.grad.at[near.block(k, 1, 1), :, : self.split], self.one.at[k]),
            (self.tag, "one", k), (self.tag, "one", k), near.over_x,
        )
        self.copies.remote(
            lambda: (self.grad.at[near.block(k, 1, 1), :, self.split :], self.two.at[k]),
            (self.tag, "two", k), (self.tag, "two", k), near.over_y,
        )

    def cross(self, k):
        near, grad, split = self.near, self.grad, self.split
        self.copies.arrived(self.one.at[k], (self.tag, "one", k), near.over_x)
        at = near.block(k, 1, 0)
        grad[at, :, :split] = (
            grad[at, :, :split].astype(F32) + self.one[k].astype(F32)
        ).astype(BF16)
        self.copies.remote(
            lambda: (grad.at[near.block(k, 1, 0)], self.got_y.at[k]),
            (self.tag, "y", k), (self.tag, "y", k), near.over_y,
        )
        self.copies.arrived(self.two.at[k], (self.tag, "two", k), near.over_y)
        at = near.block(k, 0, 1)
        grad[at, :, split:] = (
            grad[at, :, split:].astype(F32) + self.two[k].astype(F32)
        ).astype(BF16)
        self.copies.remote(
            lambda: (grad.at[near.block(k, 0, 1)], self.got_x.at[k]),
            (self.tag, "x", k), (self.tag, "x", k), near.over_x,
        )

    def plane(self, k):
        near, grad = self.near, self.grad
        self.copies.arrived(self.got_y.at[k], (self.tag, "y", k), near.over_y)
        self.copies.arrived(self.got_x.at[k], (self.tag, "x", k), near.over_x)
        at = near.block(k, 0, 0)
        total = grad[at].astype(F32) + self.got_y[k].astype(F32) + self.got_x[k].astype(F32)
        if k == 0:
            self.share[...] = total
            return
        grad[at] = total.astype(BF16)
        self.copies.remote(
            lambda: (grad.at[near.block(k, 0, 0)], self.got_z.at[BACK[k] - 1]),
            (self.tag, "z", k), (self.tag, "z", BACK[k]), near.along[k],
        )

    def end(self):
        for k in range(1, SLOTS):
            self.copies.arrived(self.got_z.at[k - 1], (self.tag, "z", k), self.near.along[k])
            self.share[...] = self.share[...] + self.got_z[k - 1].astype(F32)


STRIP = 128


def backward_kernel(
    inner,
    o_full, q_ref, k_ref, v_ref, attended, lse_ref, cos, sin, seg_col, seg_row, small, combine,
    gate_turned, q_hbm, normed_hbm, hidden_hbm, og_hbm, middle_hbm, dx_own, dx_twin, dx_other,
    mix_pair, *refs,
):
    keeps, refs = refs[:SENT], refs[SENT:]
    parts, refs = refs[:SENT], refs[SENT:]
    near_two, near_three, late_got, far_first, far_three = refs[:5]
    q_share, o_share, input_grad, block_out, kept_out, given_got, mid_grad = refs[5:12]
    far_got, first_got, z_two, z_three, mix_twin, mix_half, mix_other = refs[12:19]
    (
        attended_grad, lin_grad, o_grad, q_grad, o_one, o_two, o_y, o_x, o_z,
        q_one, q_two, q_y, q_x, q_z, part_got, pieces, z_send, z_keep, given, kept,
        strips, wide_in, wide_out, strip_out, router_rows, gate_columns, small_sum,
        send, recv, local, strip_sem, wide_sem, out_sem,
    ) = refs[19:]
    near = Neighbours(inner)
    copies = Copies(send, recv, local)
    tokens, width = hidden_hbm.shape
    block = width // 16
    x, core = near.x, near.core
    half = tokens // 2
    q_width = q_ref.shape[1]
    kv_width = k_ref.shape[1]
    kv_slabs, slabs = kv_width // LANES, q_width // LANES
    qkv_width = q_width + 2 * kv_width
    experts = gate_turned.shape[0]
    each = 2 + experts
    strip_count = tokens // STRIP
    ours = pl.ds(0, tokens)
    half_mine = pl.ds(pl.multiple_of(tokens + core * half, half), half)
    half_other = pl.ds(pl.multiple_of(tokens + (1 - core) * half, half), half)
    there = pl.ds(pl.multiple_of(core * half, half), half)
    not_there = pl.ds(pl.multiple_of((1 - core) * half, half), half)
    rows_kept = pl.ds(pl.multiple_of(x * block, block), block)
    rows_given = pl.ds(pl.multiple_of((1 - x) * block, block), block)
    scatter_o = Scatter(copies, near, o_grad, o_one, o_two, o_y, o_x, o_z, o_share, "o")
    scatter_q = Scatter(copies, near, q_grad, q_one, q_two, q_y, q_x, q_z, q_share, "q")
    z_gots = [*parts, z_two, z_three]

    def y_ends(c, k):
        if c == SENT:
            return near_two.at[k], first_got if k == 0 else late_got.at[k - 1]
        return near_three.at[k], far_got.at[k]

    def y_load(c, k, i, which):
        if 0 in which:
            copies.copy(lambda: (y_ends(c, k)[0], pieces.at[2 * i]), ("own", c, k), False)
        if 1 in which:
            copies.copy(lambda: (y_ends(c, k)[1], pieces.at[2 * i + 1]), ("got", c, k), False)

    def y_sum(c, k, i):
        copies.wait_copy(lambda: (y_ends(c, k)[0], pieces.at[2 * i]), ("own", c, k))
        copies.wait_copy(lambda: (y_ends(c, k)[1], pieces.at[2 * i + 1]), ("got", c, k))
        total = (pieces[2 * i].astype(F32) + pieces[2 * i + 1].astype(F32)).astype(BF16)
        if k == 0:
            z_keep[c - SENT] = total
            return
        if c > SENT:
            copies.sent(
                lambda: (z_send.at[k - 1], z_two.at[BACK[k] - 1]), (SENT, "z", k), near.along[k]
            )
        z_send[k - 1] = total
        copies.remote(
            lambda: (z_send.at[k - 1], z_gots[c].at[BACK[k] - 1]),
            (c, "z", k), (c, "z", BACK[k]), near.along[k], last=c > SENT,
        )

    def far_arrived(k):
        copies.arrived(far_got.at[k], ("far", k), near.over_y)

    def chunk_ends(c, k):
        return keeps[c] if k == 0 else z_gots[c].at[k - 1], pieces.at[k]

    def load_chunk(c):
        for k in range(1 if c >= SENT else 0, SLOTS):
            if c >= SENT:
                copies.arrived(z_gots[c].at[k - 1], (c, "z", k), near.along[k])
            copies.copy(lambda k=k: chunk_ends(c, k), (c, "sum", k), False)

    def sum_chunk(c):
        for k in range(1 if c >= SENT else 0, SLOTS):
            copies.wait_copy(lambda: chunk_ends(c, k), (c, "sum", k))
        if c >= 2:
            copies.wait_copy(lambda: (kept.at[c % 2], kept_out.at[c - 2]), ("kept", c - 2))
        for rows, mine in ((rows_kept, True), (rows_given, False)):
            total = (pieces[0, rows, :] if c < SENT else z_keep[c - SENT, rows, :]).astype(F32)
            for k in range(1, SLOTS):
                total = total + pieces[k, rows, :].astype(F32)
            if mine:
                kept[c % 2] = total
            else:
                given[c] = total.astype(BF16)
        copies.copy(lambda: (kept.at[c % 2], kept_out.at[c]), ("kept", c), c >= 2)
        copies.remote(
            lambda: (given.at[c], given_got.at[c]), ("given", c), ("given", c), near.over_x
        )

    def strip_rows(t):
        return pl.ds(pl.multiple_of(t * STRIP, STRIP), STRIP)

    def strip_loads(t, sources, wide):
        side = t % 2
        rows = strip_rows(t)
        loads = [
            pltpu.make_async_copy(source.at[rows], strips.at[i, side], strip_sem.at[i, side])
            for i, source in enumerate(sources)
        ]
        if wide is not None:
            loads.append(
                pltpu.make_async_copy(wide.at[rows], wide_in.at[side], wide_sem.at[side])
            )
        return loads

    def strip_store(t, source, target):
        side = t % 2
        return pltpu.make_async_copy(
            source.at[side], target.at[strip_rows(t)], out_sem.at[side]
        )

    def over_strips(sources, wide, source, target, compute):
        for load in strip_loads(0, sources, wide):
            load.start()

        def one(t, carry):
            side = t % 2

            @pl.when(t + 1 < strip_count)
            def _():
                for load in strip_loads(t + 1, sources, wide):
                    load.start()

            for load in strip_loads(t, sources, wide):
                load.wait()

            @pl.when(t >= 2)
            def _():
                strip_store(t - 2, source, target).wait()

            compute(t, side)
            strip_store(t, source, target).start()
            return carry

        lax.fori_loop(0, strip_count, one, 0)
        for t in (strip_count - 2, strip_count - 1):
            strip_store(t, source, target).wait()

    for i, k in enumerate((1, 2)):
        y_load(SENT, k, i, (0, 1))
    near.greet()
    for k in (1, 2, 3, 0):
        copies.remote(
            lambda k=k: (far_three.at[k], far_got.at[k]), ("far", k), ("far", k), near.over_y
        )
    copies.remote(lambda: (far_first, first_got), ("first",), ("first",), near.over_y)
    copies.remote(
        lambda: (mix_pair.at[half_other], mix_half), ("mh",), ("mh",), near.twin
    )
    copies.remote(lambda: (mix_pair.at[ours], mix_twin), ("mt",), ("mt",), near.twin)
    y_sum(SENT, 1, 0)
    y_load(SENT, 3, 0, (0, 1))
    y_sum(SENT, 2, 1)
    y_sum(SENT, 3, 0)
    load_chunk(0)

    router = small[2 : 2 + experts, :]
    high = router.astype(BF16).astype(F32)
    mid = (router - high).astype(BF16).astype(F32)
    low = router - high - mid
    router_rows[...] = jnp.concatenate(
        [high, mid, low, high, mid, high, jnp.zeros((LANES - 6 * experts, width), F32)]
    ).astype(BF16)
    gate_columns[...] = jnp.concatenate(
        [gate_turned[...], jnp.zeros((LANES - experts, tokens), F32)]
    ).T
    small_sum[...] = jnp.zeros_like(small_sum)

    def middle_part(turned_back):
        def compute(t, side):
            rows = strip_rows(t)
            upstream = strips[0, side].astype(F32) + strips[1, side].astype(F32)
            upstream = upstream + strips[2, side].astype(F32)
            middle = wide_in[side]
            inverse = lax.rsqrt(jnp.mean(middle * middle, axis=1, keepdims=True) + NORM_EPSILON)
            gain = small[1:2, :]
            scaled = middle * inverse
            normed = scaled * gain
            gates, grads = combine[rows, :], gate_columns[rows, :]
            logit = gates * (grads - jnp.sum(gates * grads, axis=1, keepdims=True))
            one = logit.astype(BF16).astype(F32)
            two = (logit - one).astype(BF16).astype(F32)
            three = (logit - one - two).astype(BF16).astype(F32)

            def moved(piece, by):
                return pltpu.roll(piece, by * experts, 1)

            row = one + moved(one, 1) + moved(one, 2) + moved(two, 3) + moved(two, 4)
            row = (row + moved(three, 5)).astype(BF16)
            upstream = upstream + dot(row, router_rows[...])
            weighted = upstream * gain
            mean_term = jnp.mean(weighted * scaled, axis=1, keepdims=True)
            grad = strips[3, side].astype(F32) + inverse * (weighted - scaled * mean_term)
            wide_out[side] = grad
            small_sum[0:1, :] += jnp.sum(upstream * scaled, axis=0, keepdims=True)
            back = (RESIDUAL_SCALE * grad).astype(BF16)
            turned_back[:, rows] = back.T
            attended_grad[rows, :] = dot(back, o_full[...].reshape(width, q_width)).astype(BF16)
            columns = (one + moved(two, 1) + moved(three, 2)).T[: 3 * experts, :].astype(BF16)
            n_one = normed.astype(BF16)
            rest = normed - n_one.astype(F32)
            n_two = rest.astype(BF16)
            n_three = (rest - n_two.astype(F32)).astype(BF16)
            a, b, c = dot(columns, n_one), dot(columns, n_two), dot(columns, n_three)
            e = experts
            small_sum[8 : 8 + e, :] += (
                a[:e] + a[e : 2 * e] + a[2 * e :] + b[:e] + b[e : 2 * e] + c[:e]
            )

        over_strips([dx_own, dx_twin, dx_other, og_hbm], middle_hbm, wide_out, mid_grad, compute)
        for group in range(SLOTS):
            rows = slice(4 * block * group, 4 * block * (group + 1))
            o_grad[4 * group : 4 * (group + 1)] = (
                dot(turned_back[rows, :], attended[...]).astype(BF16).reshape(4, block, q_width)
            )

    pl.run_scoped(middle_part, pltpu.VMEM((width, tokens), BF16))
    for k in (1, 2, 3, 0):
        scatter_o.begin(k)

    def mix_load(i):
        rows = pl.ds(i * STRIP, STRIP)
        whole = pl.ds(pl.multiple_of(tokens + core * half + i * STRIP, STRIP), STRIP)
        return [
            copies.copy(lambda: (mix_pair.at[whole], strips.at[0, i % 2]), ("m0", i), False),
            copies.copy(lambda: (mix_half.at[rows], strips.at[1, i % 2]), ("m1", i), False),
        ]

    def send_mix():
        count = half // STRIP
        loads = mix_load(0)
        for i in range(count):
            rows = pl.ds(i * STRIP, STRIP)
            for load in loads:
                load()
            if i + 1 < count:
                loads = mix_load(i + 1)
            if i >= 2:
                copies.wait_copy(
                    lambda: (strip_out.at[i % 2], mix_half.at[rows]), ("m2", i - 2)
                )
            strip_out[i % 2] = (
                strips[0, i % 2].astype(F32) + strips[1, i % 2].astype(F32)
            ).astype(BF16)
            copies.copy(
                lambda i=i, rows=rows: (strip_out.at[i % 2], mix_half.at[rows]), ("m2", i), False
            )
        for i in (count - 2, count - 1):
            copies.wait_copy(
                lambda: (strip_out.at[i % 2], mix_half.at[pl.ds(i * STRIP, STRIP)]), ("m2", i)
            )
        copies.remote(lambda: (mix_half, mix_other.at[there]), ("mo",), ("mo",), near.over_x)

    def attention_part(bias0, bias1, bias2, bias3, k_low, k_high, v_low, v_high, dk, dv, dq):
        biases = (bias0, bias1, bias2, bias3)
        for at, bias in enumerate(biases):
            upto = bias.shape[0]
            keys_at = lax.broadcasted_iota(jnp.int32, bias.shape, 0)
            rows_at = at * ROWS + lax.broadcasted_iota(jnp.int32, bias.shape, 1)
            same = seg_col[:upto, :] == seg_row[:, at * ROWS : (at + 1) * ROWS]
            bias[...] = jnp.where((rows_at >= keys_at) & same, 0.0, MASK_VALUE).astype(F32)
        for j in range(kv_slabs):
            lanes = slice(j * LANES, (j + 1) * LANES)
            spread_heads(k_ref[:, lanes], k_low, k_high, 2 * j)
            spread_heads(v_ref[:, lanes], v_low, v_high, 2 * j)
        dk[...] = jnp.zeros_like(dk)
        dv[...] = jnp.zeros_like(dv)

        def slab(g, carry):
            lanes = pl.ds(pl.multiple_of(g * LANES, LANES), LANES)
            kv_even, kv_odd = (2 * g) // 3, (2 * g + 1) // 3
            for at, bias in enumerate(biases):
                rows = slice(at * ROWS, (at + 1) * ROWS)
                upto = (at + 1) * ROWS
                queries, grads = q_ref[rows, lanes], attended_grad[rows, lanes]
                turned = (grads.astype(F32) * attended[rows, lanes].astype(F32)).T
                zero = jnp.zeros_like(queries)
                dq_part = None
                for upper, keys, values, kv_at in (
                    (False, k_low, v_low, kv_even), (True, k_high, v_high, kv_odd)
                ):
                    first = HEAD_DIM if upper else 0
                    delta = jnp.sum(turned[first : first + HEAD_DIM, :], axis=0, keepdims=True)
                    head = 1 if upper else 0
                    total = lse_ref[g, head : head + 1, rows]
                    keys_here = keys[kv_at, :upto, :]
                    scores = dot(keys_here, queries, NT) * SCORE_SCALE + bias[...]
                    probability = jnp.exp(scores - total)
                    prob_grad = dot(values[kv_at, :upto, :], grads, NT)
                    score_grad = (probability * (prob_grad - delta)).astype(BF16)
                    mask = half_mask(ROWS, upper)
                    dv[kv_at, :upto, :] += dot(
                        probability.astype(BF16), jnp.where(mask, grads, zero)
                    )
                    dk[kv_at, :upto, :] += dot(score_grad, jnp.where(mask, queries, zero))
                    one = dot(score_grad, keys_here, TN)
                    dq_part = one if dq_part is None else dq_part + one
                dq[rows, :] = dq_part * SCORE_SCALE
            whole = dq[...]
            lin_grad[:, lanes] = (
                whole * cos[...] - rotate_halves(whole) * sin[...]
            ).astype(BF16)

            @pl.when(g == 0)
            def _():
                for k in (1, 2, 3, 0):
                    scatter_o.cross(k)
                sum_chunk(0)
                load_chunk(1)

            @pl.when(g == 1)
            def _():
                copies.arrived(mix_half, ("mh",), near.twin)
                send_mix()

            @pl.when(g == 2)
            def _():
                for k in (1, 2, 3, 0):
                    scatter_o.plane(k)
                sum_chunk(1)
                y_load(SENT + 1, 1, 0, (0,))
                y_load(SENT + 1, 2, 1, (0,))

            @pl.when(g == 4)
            def _():
                far_arrived(1)
                y_load(SENT + 1, 1, 0, (1,))
                far_arrived(2)
                y_load(SENT + 1, 2, 1, (1,))
                scatter_o.end()

            @pl.when(g == slabs - 1)
            def _():
                y_sum(SENT + 1, 1, 0)
                y_sum(SENT + 1, 2, 1)
                far_arrived(3)
                y_load(SENT + 1, 3, 0, (0, 1))

            return carry

        lax.fori_loop(0, slabs, slab, 0)
        low = half_mask(tokens, False)

        def joined(sums, j):
            one, two = sums[2 * j], sums[2 * j + 1]
            one = one + pltpu.roll(one, HEAD_DIM, 1)
            two = two + pltpu.roll(two, HEAD_DIM, 1)
            return jnp.where(low, one, two)

        for j in range(kv_slabs):
            at = q_width + j * LANES
            whole = joined(dk, j) * SCORE_SCALE
            lin_grad[:, at : at + LANES] = (
                whole * cos[...] - rotate_halves(whole) * sin[...]
            ).astype(BF16)
            at = at + kv_width
            lin_grad[:, at : at + LANES] = joined(dv, j).astype(BF16)

    kv_shape = (2 * kv_slabs, tokens, LANES)
    pl.run_scoped(
        attention_part,
        *[pltpu.VMEM(((at + 1) * ROWS, ROWS), F32) for at in range(tokens // ROWS)],
        *[pltpu.VMEM(kv_shape, BF16)] * 4,
        *[pltpu.VMEM(kv_shape, F32)] * 2,
        pltpu.VMEM((tokens, LANES), F32),
    )

    def last_part(normed_turned, q_full, part):
        normed_in = copies.copy(lambda: (normed_hbm, normed_turned), "normed", False)
        weights_in = copies.copy(lambda: (q_hbm, q_full), "q weights", False)
        columns = jnp.concatenate(
            [
                small_sum[0:1, :], small_sum[8 : 8 + experts, :],
                jnp.zeros((LANES - 1 - experts, width), F32),
            ]
        ).T
        q_grad[:, :, qkv_width:] = columns.astype(BF16).reshape(16, block, LANES)
        normed_in()
        for k in (1, 2, 3, 0):
            spot = near.spots[k]
            rows = pl.ds(pl.multiple_of(spot * 4 * block, 4 * block), 4 * block)
            q_grad[pl.ds(spot * 4, 4), :, :qkv_width] = (
                dot(normed_turned[rows, :], lin_grad[...])
                .astype(BF16)
                .reshape(4, block, qkv_width)
            )
            scatter_q.begin(k)
        y_sum(SENT + 1, 3, 0)
        far_arrived(0)
        y_load(SENT + 1, 0, 0, (0, 1))
        copies.arrived(first_got, ("first",), near.over_y)
        y_load(SENT, 0, 1, (0, 1))
        weights_in()

        def project(tile):
            rows = pl.ds(tile * ROWS, ROWS)
            for group in range(SLOTS):
                cols = slice(4 * block * group, 4 * block * (group + 1))
                weight = q_full[4 * group : 4 * (group + 1), :, :qkv_width]
                part[rows, cols] = dot(
                    lin_grad[rows, :], weight.reshape(4 * block, qkv_width), NT
                ).astype(BF16)
            copies.remote(
                lambda: (part.at[rows], part_got.at[rows]), ("n", tile), ("n", tile), near.twin,
                last=False,
            )

        project(0)
        y_sum(SENT + 1, 0, 0)
        y_sum(SENT, 0, 1)
        load_chunk(2)
        project(1)
        for k in (1, 2, 3, 0):
            scatter_q.cross(k)
        project(2)
        project(3)
        copies.arrived(mix_other.at[there], ("mo",), near.over_x)
        copies.remote(lambda: (mix_other.at[there],) * 2, ("m2",), ("m2",), near.twin)
        sum_chunk(2)
        for k in (1, 2, 3, 0):
            scatter_q.plane(k)
        for tile in range(tokens // ROWS):
            rows = pl.ds(tile * ROWS, ROWS)
            copies.arrived(part_got.at[rows], ("n", tile), near.twin)

        def finish_rows(t, side):
            rows = strip_rows(t)
            value = strips[0, side].astype(F32)
            inverse = lax.rsqrt(jnp.mean(value * value, axis=1, keepdims=True) + NORM_EPSILON)
            upstream = part[rows, :].astype(F32) + part_got[rows, :].astype(F32)
            scaled = value * inverse
            weighted = upstream * small[0:1, :]
            mean_term = jnp.mean(weighted * scaled, axis=1, keepdims=True)
            wide_out[side] = wide_in[side] + inverse * (weighted - scaled * mean_term)

        over_strips([hidden_hbm], mid_grad, wide_out, input_grad, finish_rows)
        for tile in range(tokens // ROWS):
            rows = pl.ds(tile * ROWS, ROWS)
            copies.sent(lambda: (part.at[rows], part_got.at[rows]), ("n", tile), near.twin)

    pl.run_scoped(
        last_part,
        pltpu.VMEM((width, tokens), BF16), pltpu.VMEM(q_hbm.shape, BF16),
        pltpu.VMEM((tokens, width), BF16),
    )
    copies.arrived(mix_twin, ("mt",), near.twin)
    copies.arrived(mix_other.at[not_there], ("m2",), near.twin)

    def mix_rows(t, side):
        mix = strips[0, side].astype(F32) + strips[1, side].astype(F32)
        mix = mix + strips[2, side].astype(F32)
        strip_out[side] = (wide_in[side] + RESIDUAL_SCALE * mix).astype(BF16)

    over_strips([mix_pair, mix_twin, mix_other], middle_hbm, strip_out, block_out, mix_rows)
    load_chunk(3)
    sum_chunk(3)
    scatter_q.end()
    for c in range(2 * SENT):
        copies.arrived(given_got.at[c], ("given", c), near.over_x)
    copies.finish()


def backward_pass(
    o_full, q, k, v, attended, lse, cosine, sine, segments, small, combine, gate_turned,
    q_full, normed, hidden, og, middle, dx, mix, keep, parts, near_grads, far_grads,
):
    tokens, width = hidden.shape
    q_width, kv_width = q.shape[1], k.shape[1]
    block, q_columns = q_full.shape[1:]
    qkv_width = q_width + 2 * kv_width
    pair, columns = keep[0].shape
    chunks = 2 * SENT
    experts = gate_turned.shape[0]
    anywhere, vmem = pl.BlockSpec(memory_space=pl.ANY), vmem_spec()
    shape = jax.ShapeDtypeStruct
    dma = pltpu.SemaphoreType.DMA
    inner = lax.axis_size("dp") // 16

    def scatter_scratch(total):
        split = total // (2 * LANES) * LANES
        return [
            pltpu.VMEM((SLOTS, block, split), BF16),
            pltpu.VMEM((SLOTS, block, total - split), BF16),
            pltpu.VMEM((SLOTS, block, total), BF16),
            pltpu.VMEM((SLOTS, block, total), BF16),
            pltpu.VMEM((SLOTS - 1, block, total), BF16),
        ]

    values = (
        o_full, q, k, v, attended, lse, cosine, sine, segments[:, None], segments[None, :],
        small, combine, gate_turned,
    )
    far_values = (
        q_full, normed, hidden, og, middle, *dx, mix, *keep, *parts, *near_grads, *far_grads,
    )
    return pl.pallas_call(
        functools.partial(backward_kernel, inner),
        in_specs=[vmem] * len(values) + [anywhere] * len(far_values),
        out_specs=[vmem] * 2 + [anywhere] * 12,
        out_shape=[
            shape((block, q_columns), F32),
            shape((block, q_width), F32),
            shape((tokens, width), F32),
            shape((tokens, width), BF16),
            shape((chunks, block, columns), F32),
            shape((chunks, block, columns), BF16),
            shape((tokens, width), F32),
            shape((SLOTS, pair, columns), BF16),
            shape((pair, columns), BF16),
            shape((SLOTS - 1, pair, columns), BF16),
            shape((SLOTS - 1, pair, columns), BF16),
            shape((tokens, width), BF16),
            shape((tokens // 2, width), BF16),
            shape((tokens, width), BF16),
        ],
        scratch_shapes=[
            pltpu.VMEM((tokens, q_width), BF16),
            pltpu.VMEM((tokens, qkv_width), BF16),
            pltpu.VMEM((16, block, q_width), BF16),
            pltpu.VMEM((16, block, q_columns), BF16),
        ]
        + scatter_scratch(q_width)
        + scatter_scratch(q_columns)
        + [
            pltpu.VMEM((tokens, width), BF16),
            pltpu.VMEM((SLOTS, pair, columns), BF16),
            pltpu.VMEM((SLOTS - 1, pair, columns), BF16),
            pltpu.VMEM((2, pair, columns), BF16),
            pltpu.VMEM((chunks, block, columns), BF16),
            pltpu.VMEM((2, block, columns), F32),
            pltpu.VMEM((4, 2, STRIP, width), BF16),
            pltpu.VMEM((2, STRIP, width), F32),
            pltpu.VMEM((2, STRIP, width), F32),
            pltpu.VMEM((2, STRIP, width), BF16),
            pltpu.VMEM((LANES, width), BF16),
            pltpu.VMEM((tokens, LANES), F32),
            pltpu.VMEM((8 + experts, width), F32),
            dma((80,)), dma((80,)), dma((60,)), dma((4, 2)), dma((2,)), dma((2,)),
        ],
        compiler_params=pltpu.CompilerParams(
            vmem_limit_bytes=EXPERT_VMEM, collective_id=2, has_side_effects=True
        ),
        name="backward_pass",
    )(*values, *far_values)


def whole_call(kernel, values, outs, earlier=(), name=None):
    return pl.pallas_call(
        with_earlier(kernel, len(values), len(earlier)),
        in_specs=[vmem_spec()] * len(values) + any_specs(earlier),
        out_specs=[vmem_spec()] * len(outs),
        out_shape=[jax.ShapeDtypeStruct(shape, dtype) for shape, dtype in outs],
        compiler_params=pltpu.CompilerParams(vmem_limit_bytes=VMEM_BYTES),
        name=name,
    )(*values, *earlier)


def fence_kernel(*refs):
    count = len(refs) // 2
    for value, out in zip(refs[:count], refs[count:]):
        out[...] = value[...]


def fence_all(values, *earlier):
    return whole_call(fence_kernel, values, [(v.shape, v.dtype) for v in values], earlier, "fence")


def fence(value, *earlier):
    return fence_all([value], *earlier)[0]


def sum_y_kernel(near, got, *outs):
    for k, out in enumerate(outs):
        out[...] = (near[k].astype(F32) + got[k].astype(F32)).astype(BF16)


def sum_y(near, got, *earlier):
    outs = [(near.shape[1:], BF16)] * SLOTS
    return whole_call(sum_y_kernel, [near, got], outs, earlier, "sum_y")


def sum_z_kernel(x_at, *refs):
    kept, given = refs[-2:]
    half = kept.shape[1]
    for c in range(kept.shape[0]):
        parts = refs[SLOTS * c : SLOTS * (c + 1)]
        for rows, out in ((x_at[0], kept), (1 - x_at[0], given)):
            rows = pl.ds(pl.multiple_of(rows * half, half), half)
            total = parts[0][rows, :].astype(F32)
            for part in parts[1:]:
                total = total + part[rows, :].astype(F32)
            out[c] = total.astype(out.dtype)


def sum_z(x_at, chunks, *earlier):
    count = len(chunks)
    pair, columns = chunks[0][0].shape
    flat = [part for parts in chunks for part in parts]
    return pl.pallas_call(
        with_earlier(sum_z_kernel, 1 + len(flat), len(earlier)),
        in_specs=[smem_spec()] + [vmem_spec()] * len(flat) + any_specs(earlier),
        out_specs=[vmem_spec()] * 2,
        out_shape=[
            jax.ShapeDtypeStruct((count, pair // 2, columns), F32),
            jax.ShapeDtypeStruct((count, pair // 2, columns), BF16),
        ],
        compiler_params=pltpu.CompilerParams(vmem_limit_bytes=VMEM_BYTES),
        name="sum_z",
    )(x_at, *flat, *earlier)


def sum_parts_kernel(parts, out):
    total = parts[0].astype(F32)
    for c in range(1, parts.shape[0]):
        total = total + parts[c].astype(F32)
    out[...] = total.astype(BF16)


def sum_parts(parts, *earlier):
    chunks, tokens, width = parts.shape
    return pl.pallas_call(
        with_earlier(sum_parts_kernel, 1, len(earlier)),
        grid=(tokens // EXPERT_ROWS,),
        in_specs=[pl.BlockSpec((chunks, EXPERT_ROWS, width), lambda s: (0, s, 0))]
        + any_specs(earlier),
        out_specs=pl.BlockSpec((EXPERT_ROWS, width), lambda s: (s, 0)),
        out_shape=jax.ShapeDtypeStruct((tokens, width), BF16),
        compiler_params=pltpu.CompilerParams(vmem_limit_bytes=VMEM_BYTES),
        name="sum_parts",
    )(parts, *earlier)


def adam_experts_kernel(x_at, kept, got, *refs):
    states, outs = refs[:6], refs[6:]
    own = kept.shape[1]
    hidden = states[0].shape[3]
    mine = pl.program_id(0) // (pl.num_programs(0) // 2) == x_at[0]
    grad = jnp.where(mine, kept[0], got[0].astype(F32))
    for e in range(CHUNK):
        for part in range(2):
            first = hidden * (2 * e + part)
            results = adam_update(
                states[0][e, part], grad[:, first : first + hidden],
                states[1][e, part], states[2][e, part], MODEL_DIM ** (-0.5), WEIGHT_DECAY,
            )
            for out, result in zip(outs[:3], results):
                out[e, part] = result
        first = hidden * (2 * CHUNK + e)
        results = adam_update(
            states[3][e], grad[:, first : first + hidden], states[4][e], states[5][e],
            max(1, F // 256) ** (-0.5), WEIGHT_DECAY,
        )
        for out, result in zip(outs[3:], results):
            out[e] = result


def adam_experts(x_at, kept, got, gateup, down):
    chunks, own, columns = kept.shape
    experts, hidden = down[0].shape[0], down[0].shape[2]
    share = pl.BlockSpec((1, own, columns), lambda j: (j % chunks, 0, 0))
    big = pl.BlockSpec((CHUNK, 2, own, hidden), lambda j: (j, 0, 0, 0))
    small = pl.BlockSpec((CHUNK, own, hidden), lambda j: (j, 0, 0))
    return pl.pallas_call(
        adam_experts_kernel,
        grid=(experts // CHUNK,),
        in_specs=[smem_spec(), share, share] + [big] * 3 + [small] * 3,
        out_specs=[big] * 3 + [small] * 3,
        out_shape=[jax.ShapeDtypeStruct(gateup[0].shape, F32)] * 3
        + [jax.ShapeDtypeStruct(down[0].shape, F32)] * 3,
        compiler_params=pltpu.CompilerParams(vmem_limit_bytes=VMEM_BYTES),
        name="adam_experts",
    )(x_at, kept, got, *gateup, *down)


def join_tokens_kernel(own, first, second, out, turned):
    half = own.shape[0] // 2
    for at, part in ((0, own[:half, :]), (half, own[half:, :]), (2 * half, first[...]), (3 * half, second[...])):
        out[at : at + half, :] = part
        turned[:, at : at + half] = part.T


def join_tokens(own, first, second, *earlier):
    tokens, width = own.shape
    return pl.pallas_call(
        with_earlier(join_tokens_kernel, 3, len(earlier)),
        in_specs=[vmem_spec()] * 3 + any_specs(earlier),
        out_specs=[vmem_spec()] * 2,
        out_shape=[
            jax.ShapeDtypeStruct((2 * tokens, width), own.dtype),
            jax.ShapeDtypeStruct((width, 2 * tokens), own.dtype),
        ],
        compiler_params=pltpu.CompilerParams(vmem_limit_bytes=VMEM_BYTES),
        name="join_tokens",
    )(own, first, second, *earlier)


def move(array, dz=0, dy=0, dx=0):
    total = lax.axis_size("dp")
    inner = total // 16
    pairs = []
    for at in range(16):
        z, y, x = at // 4, at // 2 % 2, at % 2
        to = ((z + dz) % 4) * 4 + (y ^ dy) * 2 + (x ^ dx)
        pairs += [(at * inner + i, to * inner + i) for i in range(inner)]
    return lax.ppermute(array, "dp", pairs)


def place():
    at = lax.axis_index("dp") // (lax.axis_size("dp") // 16)
    return at // 4, at // 2 % 2, at % 2


def inner_groups(total):
    inner = total // 16
    return [[at * inner + i for i in range(inner)] for at in range(16)]


def inner_gather(shard, axis):
    total = lax.axis_size("dp")
    if total == 16:
        return shard
    return lax.all_gather(
        shard, "dp", axis=axis, tiled=True, axis_index_groups=inner_groups(total)
    )


def inner_scatter(share, axis):
    total = lax.axis_size("dp")
    if total == 16:
        return share
    return lax.psum_scatter(
        share, "dp", scatter_dimension=axis, tiled=True, axis_index_groups=inner_groups(total)
    )


def block_rows(parts, rows):
    z, y, x = place()
    starts = []
    for dz, dy, dx in parts:
        starts.append((((z + dz + 4) % 4) * 4 + (y ^ dy) * 2 + (x ^ dx)) * rows)
    return jnp.stack(starts).astype(jnp.int32)


def gather_z(shard):
    return jnp.stack([shard] + [move(shard, dz=-dz) for dz in Z_FROM[1:]])


def gather_ring(shard):
    below, above = move(shard, dz=1), move(shard, dz=-1)
    return [shard, below, above, move(below, dz=1)]


def send_z(parts):
    return [move(parts[k].astype(BF16), dz=Z_FROM[k]) for k in range(1, SLOTS)]


def scatter_z(parts, moved=None):
    result = parts[0]
    for one in moved or send_z(parts):
        result = result + one.astype(F32)
    return result


def gather_plane(own):
    half = own.shape[-1] // 2
    along_y, along_x = move(own, dy=1), move(own, dx=1)
    both = (move(along_y[..., :half], dx=1), move(along_x[..., half:], dy=1))
    return own, along_y, along_x, *both


def scatter_plane(pieces):
    own, along_y, along_x, both_one, both_two = pieces
    half = both_one.shape[-1]
    got_one, got_two = move(both_one, dx=1), move(both_two, dy=1)
    pass_y = jnp.concatenate(
        [(along_y[..., :half].astype(F32) + got_one.astype(F32)).astype(BF16), along_y[..., half:]],
        axis=-1,
    )
    pass_x = jnp.concatenate(
        [along_x[..., :half], (along_x[..., half:].astype(F32) + got_two.astype(F32)).astype(BF16)],
        axis=-1,
    )
    got_y, got_x = move(pass_y, dy=1), move(pass_x, dx=1)
    return scatter_z(
        [
            own[k].astype(F32) + got_y[k].astype(F32) + got_x[k].astype(F32)
            for k in range(SLOTS)
        ]
    )


PLANE = [(dz, dy, dx) for dy, dx in ((0, 0), (1, 0), (0, 1), (1, 1)) for dz in Z_FROM]


def join_kernel(rows_at, *refs):
    pieces, out = refs[:-1], refs[-1]
    slots, own, width = pieces[0].shape
    half = width // 2
    for at in range(4 * slots):
        rows = pl.ds(pl.multiple_of(rows_at[at], own), own)
        group, slot = at // slots, at % slots
        if group < 3:
            out[rows, :] = pieces[group][slot]
        else:
            out[rows, :half] = pieces[3][slot]
            out[rows, half:] = pieces[4][slot]


def part_kernel(rows_at, whole, *pieces):
    slots, own, width = pieces[0].shape
    half = width // 2
    for at in range(4 * slots):
        rows = pl.ds(pl.multiple_of(rows_at[at], own), own)
        group, slot = at // slots, at % slots
        if group < 3:
            pieces[group][slot] = whole[rows, :]
        else:
            pieces[3][slot] = whole[rows, :half]
            pieces[4][slot] = whole[rows, half:]


def smem_spec():
    return pl.BlockSpec(memory_space=pltpu.SMEM)


def vmem_spec():
    return pl.BlockSpec(memory_space=pltpu.VMEM)


def join_blocks(rows_at, pieces, earlier=()):
    slots, own, width = pieces[0].shape
    return pl.pallas_call(
        with_earlier(join_kernel, 6, len(earlier)),
        in_specs=[smem_spec()] + [vmem_spec()] * 5 + any_specs(earlier),
        out_specs=vmem_spec(),
        out_shape=jax.ShapeDtypeStruct((4 * slots * own, width), BF16),
        compiler_params=pltpu.CompilerParams(vmem_limit_bytes=VMEM_BYTES),
        name="join_blocks",
    )(rows_at, *pieces, *earlier)


def part_blocks(rows_at, whole, earlier=()):
    own, width = whole.shape[0] // (4 * SLOTS), whole.shape[1]
    full = jax.ShapeDtypeStruct((SLOTS, own, width), BF16)
    half = jax.ShapeDtypeStruct((SLOTS, own, width // 2), BF16)
    return pl.pallas_call(
        with_earlier(part_kernel, 2, len(earlier)),
        in_specs=[smem_spec(), vmem_spec()] + any_specs(earlier),
        out_specs=[vmem_spec()] * 5,
        out_shape=[full] * 3 + [half] * 2,
        compiler_params=pltpu.CompilerParams(vmem_limit_bytes=VMEM_BYTES),
        name="part_blocks",
    )(rows_at, whole, *earlier)


def after(value, *earlier):
    marks = []
    for one in earlier:
        slots = one.shape[0] if one.shape[0] == SLOTS else 1
        lead, rest = (slots > 1) * 1, one.ndim - 1
        marks.append(lax.slice(one, (lead,) + (0,) * rest, (slots,) + (1,) * rest))
    return lax.optimization_barrier((value, *marks))[0]


def split_three(values):
    high = values.astype(BF16)
    rest = values - high.astype(F32)
    middle = rest.astype(BF16)
    low = (rest - middle.astype(F32)).astype(BF16)
    return [high, middle, low]


def swap_cores(part):
    return lax.ppermute(part, "tensor", [(0, 1), (1, 0)])


def pair_sum(part):
    return part.astype(F32) + swap_cores(part).astype(F32)


def norm_backward(values, inverse, gain_row, upstream):
    scaled = values * inverse
    weighted = upstream * gain_row
    mean_term = jnp.mean(weighted * scaled, axis=-1, keepdims=True)
    return (inverse * (weighted - scaled * mean_term), jnp.sum(upstream * scaled, axis=0))


def adam_update(value, gradient, mean_old, square_old, rate, decay):
    mean_new = FIRST_DECAY * mean_old + (1.0 - FIRST_DECAY) * gradient
    square_new = SECOND_DECAY * square_old + (1.0 - SECOND_DECAY) * gradient * gradient
    mean_hat = mean_new / (1.0 - FIRST_DECAY**STEP)
    square_hat = square_new / (1.0 - SECOND_DECAY**STEP)
    updated = value - rate * (mean_hat / (jnp.sqrt(square_hat) + ADAM_EPSILON) + decay * value)
    return (mean_new, square_new, updated)


def shards(
    hidden_in,
    out_grad,
    routes,
    segments,
    norm_gains,
    gains_mean,
    gains_square,
    w_query,
    query_mean,
    query_square,
    key_value_weight,
    key_value_first_moment,
    key_value_second_moment,
    w_out,
    out_mean,
    out_square,
    w_router,
    router_mean,
    router_square,
    w_gateup,
    gateup_mean,
    gateup_square,
    w_down,
    down_mean,
    down_square,
):
    tokens, width = hidden_in.shape
    own = w_query.shape[0]
    experts, hidden = w_down.shape[0], w_down.shape[1]
    q_width, kv_width = w_query.shape[1], key_value_weight.shape[2]
    qkv_width = q_width + 2 * kv_width
    each = 2 + experts
    half_experts = experts // 2
    block = width // 16
    z_at, y_at, x_at = place()
    core = lax.axis_index("tensor")
    plane_rows = block_rows(PLANE, block)
    qkv_shard = jnp.concatenate(
        [w_query.astype(BF16), key_value_weight[0].astype(BF16), key_value_weight[1].astype(BF16)]
        + split_three(jnp.concatenate([norm_gains.T, w_router], axis=1))
        + [jnp.zeros((own, LANES - 3 * each), BF16)],
        axis=1,
    )
    out_shard = w_out.T.astype(BF16)
    turned_down = [one.transpose(0, 2, 1) for one in (w_down, down_mean, down_square)]
    gateup_rows, down_rows = w_gateup, turned_down[0]
    if lax.axis_size("dp") > 16:
        gateup_rows = inner_gather(w_gateup.astype(BF16), 2)
        down_rows = inner_gather(down_rows.astype(BF16), 1)
    chunks = experts // (2 * CHUNK)
    first = x_at == 0
    cosine, sine = rope_tables(seq_positions(segments))
    (
        qkv_blocks, out_blocks, small, normed_low, queries, keys, values, attended, lse,
        combine, combine_pair, middle, x_pair, x_turned, og_pair, og_turned, pairs, near, far,
    ) = forward_pass(
        inner_gather(qkv_shard, 0), inner_gather(out_shard, 0), gateup_rows, down_rows,
        hidden_in, out_grad, cosine, sine, segments, routes,
    )
    dx, mix_pair, gate_turned, keep, z_got, near_grads, far_grads = experts_pass(
        x_pair, og_pair, x_turned, og_turned, combine_pair, pairs, near, far
    )
    qkv_share, output_share, input_grad, block_out, kept_share, got_share = backward_pass(
        out_blocks, queries, keys, values, attended, lse, cosine, sine, segments, small, combine,
        gate_turned, qkv_blocks, normed_low, hidden_in, out_grad, middle, dx, mix_pair, keep,
        z_got, near_grads, far_grads,
    )[:6]
    kept_share, got_share = inner_scatter(kept_share, 1), inner_scatter(got_share, 1)
    x_here = x_at.astype(jnp.int32)[None]
    output_share = inner_scatter(output_share, 0).T
    qkv_share = inner_scatter(qkv_share, 0)
    query_share = qkv_share[:, :q_width]
    keyval_share = jnp.stack(
        [qkv_share[:, q_width : q_width + kv_width], qkv_share[:, q_width + kv_width : qkv_width]]
    )
    gain_one_part = jnp.sum(w_query.astype(BF16).astype(F32) * query_share, axis=1) + jnp.sum(
        key_value_weight.astype(BF16).astype(F32) * keyval_share, axis=(0, 2)
    )
    gain_one_share = pair_sum(gain_one_part[None, :]) / norm_gains[:1]
    gains_share = jnp.concatenate([gain_one_share, qkv_share[:, qkv_width][None, :]])
    router_share = qkv_share[:, qkv_width + 1 : qkv_width + 1 + experts]

    gains_result = adam_update(norm_gains, gains_share, gains_mean, gains_square, GAIN_RATE, 0.0)
    query_result = adam_update(
        w_query, query_share, query_mean, query_square, (MODEL_DIM // 12) ** (-0.5), WEIGHT_DECAY
    )
    keyval_result = adam_update(
        key_value_weight,
        keyval_share,
        key_value_first_moment,
        key_value_second_moment,
        (MODEL_DIM // 12) ** (-0.5),
        WEIGHT_DECAY,
    )
    out_result = adam_update(
        w_out,
        output_share,
        out_mean,
        out_square,
        max(1, QUERY_HEADS * HEAD_DIM // 96) ** (-0.5),
        WEIGHT_DECAY,
    )
    router_result = adam_update(
        w_router, router_share, router_mean, router_square, (4 * MODEL_DIM) ** (-0.5), WEIGHT_DECAY
    )
    expert_results = adam_experts(
        x_here, kept_share, got_share,
        (w_gateup, gateup_mean, gateup_square), turned_down,
    )
    expert_results = [*expert_results[:3], *(one.transpose(0, 2, 1) for one in expert_results[3:])]
    return (
        (block_out, input_grad)
        + gains_result
        + query_result
        + keyval_result
        + out_result
        + router_result
        + tuple(expert_results)
    )


def solution(mesh):
    tokens, gains = P("dp", None), P(None, "dp")
    query, keyval, out = P("dp", "tensor"), P(None, "dp", "tensor"), P("tensor", "dp")
    router, gateup, down = P("dp", None), P(None, None, "dp", "tensor"), P(None, "tensor", "dp")
    states = tuple(
        spec for one in (gains, query, keyval, out, router, gateup, down) for spec in (one,) * 3
    )
    return jax.shard_map(
        shards,
        mesh=mesh,
        in_specs=(tokens, tokens, tokens, P("dp")) + states,
        out_specs=(tokens, tokens) + states,
        check_vma=False,
    )
```

```python
import functools

import jax
import jax.numpy as jnp
from jax import lax
from jax.experimental import pallas as pl
from jax.experimental.pallas import tpu as pltpu
from jax.sharding import PartitionSpec as P

MODEL_DIM = 1536
QUERY_HEADS = 24
HEAD_DIM = 64
F = 512
SEQUENCE_LENGTH = 1024
STEP = 10

NORM_EPSILON = 1e-06
SCORE_SCALE = 0.015625
RESIDUAL_SCALE = 0.22
ROPE_BASE = 10000.0
FIRST_DECAY = 0.9
SECOND_DECAY = 0.95
ADAM_EPSILON = 1e-08
WEIGHT_DECAY = 0.1
GAIN_RATE = 0.6
MASK_VALUE = -1e30
HIGHEST_PRECISION = lax.Precision.HIGHEST

BF16 = jnp.bfloat16
F32 = jnp.float32
LANES = 128
ROWS = 256
VMEM_BYTES = 58 * 1024 * 1024

NN = (((1,), (0,)), ((), ()))
NT = (((1,), (1,)), ((), ()))
TN = (((0,), (0,)), ((), ()))


def dot(a, b, dims=NN):
    return lax.dot_general(a, b, dims, preferred_element_type=F32)


def seq_positions(segment_row):
    counter = jnp.arange(segment_row.shape[0], dtype=jnp.int32)
    earlier = jnp.concatenate([segment_row[:1] - 1, segment_row[:-1]])
    starts = lax.cummax(jnp.where(segment_row != earlier, counter, 0), axis=0)
    return counter - starts


def rope_tables(positions):
    half_width = HEAD_DIM // 2
    frequency = ROPE_BASE ** (-2.0 * jnp.arange(half_width, dtype=F32) / HEAD_DIM)
    angles = positions.astype(F32)[:, None] * frequency[None, :]
    cosine, sine = jnp.cos(angles), jnp.sin(angles)
    return (
        jnp.concatenate([cosine] * 4, axis=1),
        jnp.concatenate([-sine, sine] * 2, axis=1),
    )


def rotate_halves(slab):
    lane = lax.broadcasted_iota(jnp.int32, slab.shape, 1)
    ahead = pltpu.roll(slab, LANES - HEAD_DIM // 2, 1)
    behind = pltpu.roll(slab, HEAD_DIM // 2, 1)
    return jnp.where(lane % HEAD_DIM < HEAD_DIM // 2, ahead, behind)


def few_rows(count, base=None):
    for r in range(0, count, 16):
        yield pl.ds(r, 16) if base is None else pl.ds(pl.multiple_of(base + r, 16), 16)


def half_mask(rows, upper):
    lane = lax.broadcasted_iota(jnp.int32, (rows, LANES), 1)
    return (lane >= HEAD_DIM) if upper else (lane < HEAD_DIM)


def spread_heads(slab, lower_out, upper_out, index):
    rows = slab.shape[0]
    moved = pltpu.roll(slab.astype(F32), HEAD_DIM, 1).astype(BF16)
    zero = jnp.zeros_like(slab)
    low, high = half_mask(rows, False), half_mask(rows, True)
    lower_out[index] = jnp.where(low, slab, zero)
    upper_out[index] = jnp.where(high, moved, zero)
    lower_out[index + 1] = jnp.where(low, moved, zero)
    upper_out[index + 1] = jnp.where(high, slab, zero)


def fill_bias(bias, seg_col, seg_row):
    span = bias.shape[0]
    for at in range(0, span, ROWS):
        rows_at = at + lax.broadcasted_iota(jnp.int32, (ROWS, span), 0)
        cols_at = lax.broadcasted_iota(jnp.int32, (ROWS, span), 1)
        allowed = (rows_at >= cols_at) & (seg_col[at : at + ROWS, :] == seg_row[...])
        bias[at : at + ROWS, :] = jnp.where(allowed, 0.0, MASK_VALUE).astype(F32)


def with_earlier(kernel, inputs, count):
    def run(*refs):
        kernel(*refs[:inputs], *refs[inputs + count :])

    return run


def any_specs(arrays):
    return [pl.BlockSpec(memory_space=pl.ANY)] * len(arrays)


def attention_forward_kernel(
    lin_ref, kv_ref, cos_ref, sin_ref, seg_col, seg_row,
    out_ref, q_ref, k_ref, v_ref, lse_ref,
    bias, k_low, k_high, v_low, v_high,
):
    slab_at = pl.program_id(0)
    span = lin_ref.shape[0]
    kv_slabs = kv_ref.shape[1] // (2 * LANES)

    @pl.when(slab_at == 0)
    def _():
        fill_bias(bias, seg_col, seg_row)
        for j in range(kv_slabs):
            lanes = slice(j * LANES, (j + 1) * LANES)
            lin = kv_ref[:, lanes]
            keys = (lin * cos_ref[...] + rotate_halves(lin) * sin_ref[...]).astype(BF16)
            k_ref[:, lanes] = keys
            spread_heads(keys, k_low, k_high, 2 * j)
            lanes = slice((kv_slabs + j) * LANES, (kv_slabs + j + 1) * LANES)
            values = kv_ref[:, lanes].astype(BF16)
            v_ref[:, slice(j * LANES, (j + 1) * LANES)] = values
            spread_heads(values, v_low, v_high, 2 * j)

    lin = lin_ref[...]
    q_ref[...] = (lin * cos_ref[...] + rotate_halves(lin) * sin_ref[...]).astype(BF16)
    kv_even, kv_odd = (2 * slab_at) // 3, (2 * slab_at + 1) // 3
    for at in range(0, span, ROWS):
        rows = slice(at, at + ROWS)
        queries = q_ref[rows, :]
        total = None
        stats = []
        for keys, values, kv_at in ((k_low, v_low, kv_even), (k_high, v_high, kv_odd)):
            upto = at + ROWS
            scores = dot(queries, keys[kv_at, :upto, :], NT) * SCORE_SCALE + bias[rows, :upto]
            highest = jnp.max(scores, axis=1, keepdims=True)
            weights = jnp.exp(scores - highest)
            summed = jnp.sum(weights, axis=1, keepdims=True)
            probability = (weights * (1.0 / summed)).astype(BF16)
            part = dot(probability, values[kv_at, :upto, :])
            total = part if total is None else total + part
            stats.append(highest + jnp.log(summed))
        out_ref[rows, :] = total.astype(BF16)
        spread = jnp.where(half_mask(ROWS, False), stats[0], stats[1])
        turned = spread.T
        lse_ref[0, 0:1, rows] = turned[0:1, :]
        lse_ref[0, 1:2, rows] = turned[HEAD_DIM : HEAD_DIM + 1, :]


def attention_forward(qkv_lin, cosine, sine, segment_row, earlier=()):
    span = qkv_lin.shape[0]
    q_width = MODEL_DIM // 2
    kv_width = (qkv_lin.shape[1] - q_width) // 2
    slabs, kv_heads = q_width // LANES, kv_width // HEAD_DIM
    whole = lambda shape: pl.BlockSpec(shape, lambda g: (0,) * len(shape))
    slab = pl.BlockSpec((span, LANES), lambda g: (0, g))
    q_lin, kv_lin = qkv_lin[:, :q_width], qkv_lin[:, q_width:]
    return pl.pallas_call(
        with_earlier(attention_forward_kernel, 6, len(earlier)),
        grid=(slabs,),
        in_specs=[
            slab, whole((span, 2 * kv_width)), whole((span, LANES)), whole((span, LANES)),
            whole((span, 1)), whole((1, span)),
        ]
        + any_specs(earlier),
        out_specs=[
            slab, slab, whole((span, kv_width)), whole((span, kv_width)),
            pl.BlockSpec((1, 8, span), lambda g: (g, 0, 0)),
        ],
        out_shape=[
            jax.ShapeDtypeStruct((span, q_width), BF16),
            jax.ShapeDtypeStruct((span, q_width), BF16),
            jax.ShapeDtypeStruct((span, kv_width), BF16),
            jax.ShapeDtypeStruct((span, kv_width), BF16),
            jax.ShapeDtypeStruct((slabs, 8, span), F32),
        ],
        scratch_shapes=[pltpu.VMEM((span, span), F32)]
        + [pltpu.VMEM((kv_heads, span, LANES), BF16)] * 4,
        compiler_params=pltpu.CompilerParams(vmem_limit_bytes=VMEM_BYTES),
        cost_estimate=pl.CostEstimate(
            flops=32 * slabs * span * span * LANES, bytes_accessed=16 * span * q_width,
            transcendentals=slabs * span * span,
        ),
        name="attention_forward",
    )(q_lin, kv_lin, cosine, sine, segment_row[:, None], segment_row[None, :], *earlier)


def attention_backward_kernel(
    q_ref, k_ref, v_ref, out_ref, grad_ref, cos_ref, sin_ref, seg_col, seg_row, lse_ref,
    dq_ref, dkv_ref,
    bias, k_low, k_high, v_low, v_high, dk_low, dk_high, dv_low, dv_high, dq_sum,
):
    slab_at = pl.program_id(0)
    span = q_ref.shape[0]
    kv_slabs = k_ref.shape[1] // LANES

    @pl.when(slab_at == 0)
    def _():
        for at in range(0, span, ROWS):
            keys_at = at + lax.broadcasted_iota(jnp.int32, (ROWS, span), 0)
            rows_at = lax.broadcasted_iota(jnp.int32, (ROWS, span), 1)
            allowed = (rows_at >= keys_at) & (seg_col[at : at + ROWS, :] == seg_row[...])
            bias[at : at + ROWS, :] = jnp.where(allowed, 0.0, MASK_VALUE).astype(F32)
        for j in range(kv_slabs):
            lanes = slice(j * LANES, (j + 1) * LANES)
            spread_heads(k_ref[:, lanes], k_low, k_high, 2 * j)
            spread_heads(v_ref[:, lanes], v_low, v_high, 2 * j)
        for sums in (dk_low, dk_high, dv_low, dv_high):
            sums[...] = jnp.zeros_like(sums)

    kv_even, kv_odd = (2 * slab_at) // 3, (2 * slab_at + 1) // 3
    for at in range(0, span, ROWS):
        rows = slice(at, at + ROWS)
        upto = at + ROWS
        queries, grads = q_ref[rows, :], grad_ref[rows, :]
        turned = (grads.astype(F32) * out_ref[rows, :].astype(F32)).T
        zero = jnp.zeros_like(queries)
        dq_part = None
        for upper, keys, values, dk_sum, dv_sum, kv_at in (
            (False, k_low, v_low, dk_low, dv_low, kv_even),
            (True, k_high, v_high, dk_high, dv_high, kv_odd),
        ):
            first = HEAD_DIM if upper else 0
            delta = jnp.sum(turned[first : first + HEAD_DIM, :], axis=0, keepdims=True)
            head = 1 if upper else 0
            total = lse_ref[0, head : head + 1, rows]
            keys_here = keys[kv_at, :upto, :]
            scores = dot(keys_here, queries, NT) * SCORE_SCALE + bias[:upto, rows]
            probability = jnp.exp(scores - total)
            prob_grad = dot(values[kv_at, :upto, :], grads, NT)
            score_grad = (probability * (prob_grad - delta)).astype(BF16)
            mask = half_mask(ROWS, upper)
            dv_sum[kv_at, :upto, :] += dot(
                probability.astype(BF16), jnp.where(mask, grads, zero)
            )
            dk_sum[kv_at, :upto, :] += dot(score_grad, jnp.where(mask, queries, zero))
            part = dot(score_grad, keys_here, TN)
            dq_part = part if dq_part is None else dq_part + part
        dq_sum[rows, :] = dq_part * SCORE_SCALE
    slab = dq_sum[...]
    dq_ref[...] = (slab * cos_ref[...] - rotate_halves(slab) * sin_ref[...]).astype(BF16)

    @pl.when(slab_at == pl.num_programs(0) - 1)
    def _():
        low = half_mask(span, False)

        def joined(sums_low, sums_high, j):
            one = sums_low[2 * j] + pltpu.roll(sums_high[2 * j], HEAD_DIM, 1)
            two = pltpu.roll(sums_low[2 * j + 1], HEAD_DIM, 1) + sums_high[2 * j + 1]
            return jnp.where(low, one, two)

        for j in range(kv_slabs):
            slab = joined(dk_low, dk_high, j) * SCORE_SCALE
            dkv_ref[:, j * LANES : (j + 1) * LANES] = (
                slab * cos_ref[...] - rotate_halves(slab) * sin_ref[...]
            ).astype(BF16)
            at = (kv_slabs + j) * LANES
            dkv_ref[:, at : at + LANES] = joined(dv_low, dv_high, j).astype(BF16)


def attention_backward(
    queries, keys, values, attended, grad, cosine, sine, segment_row, lse, earlier=()
):
    span, q_width = queries.shape
    kv_width = keys.shape[1]
    slabs, kv_heads = q_width // LANES, kv_width // HEAD_DIM
    whole = lambda shape: pl.BlockSpec(shape, lambda g: (0,) * len(shape))
    slab = pl.BlockSpec((span, LANES), lambda g: (0, g))
    return pl.pallas_call(
        with_earlier(attention_backward_kernel, 10, len(earlier)),
        grid=(slabs,),
        in_specs=[
            slab, whole((span, kv_width)), whole((span, kv_width)), slab, slab,
            whole((span, LANES)), whole((span, LANES)), whole((span, 1)), whole((1, span)),
            pl.BlockSpec((1, 8, span), lambda g: (g, 0, 0)),
        ]
        + any_specs(earlier),
        out_specs=[slab, whole((span, 2 * kv_width))],
        out_shape=[
            jax.ShapeDtypeStruct((span, q_width), BF16),
            jax.ShapeDtypeStruct((span, 2 * kv_width), BF16),
        ],
        scratch_shapes=[pltpu.VMEM((span, span), F32)]
        + [pltpu.VMEM((kv_heads, span, LANES), BF16)] * 4
        + [pltpu.VMEM((kv_heads, span, LANES), F32)] * 4
        + [pltpu.VMEM((span, LANES), F32)],
        compiler_params=pltpu.CompilerParams(vmem_limit_bytes=VMEM_BYTES),
        cost_estimate=pl.CostEstimate(
            flops=40 * slabs * span * span * LANES, bytes_accessed=16 * span * q_width,
            transcendentals=slabs * span * span,
        ),
        name="attention_backward",
    )(
        queries, keys, values, attended, grad, cosine, sine,
        segment_row[:, None], segment_row[None, :], lse, *earlier,
    )


EXPERT_ROWS = 256
EXPERT_VMEM = 63 * 1024 * 1024
SLOTS = 4
Z_FROM = (0, -1, 1, 2)
CHUNK = 2
LATE = 2
SENT = 2
MESH_ID = pl.DeviceIdType.MESH


def experts_kernel(
    inner, chunks, row_steps, x_ref, og_ref, xt_ref, ogt_ref, combine_ref,
    pairs_ref, near_ref, far_ref,
    dx_own, dx_twin, dx_other, mix_out, gate_out, *refs,
):
    keep_outs, refs = refs[:SENT], refs[SENT:]
    part_outs, refs = refs[:SENT], refs[SENT:]
    near_outs, refs = refs[: chunks - SENT], refs[chunks - SENT :]
    late_out, first_out, far_out, refs = *refs[:3], refs[3:]
    slots, arrived, held_both, held_down, dx_sum, mix_sum, twin_rows = refs[:7]
    gates, gate_kept, gate_got, gate_full, gate_twin, send, recv, local = refs[7:]
    weights, grads = slots.at[pl.ds(1, chunks)], slots
    near = Neighbours(inner)
    copies = Copies(send, recv, local)
    z, y, x, core, spots = near.z, near.y, near.x, near.core, near.spots
    step = pl.program_id(0)
    steps = row_steps + SLOTS
    chunk, turn = step // steps, step % steps
    last = chunks - 1
    width = x_ref.shape[1]
    block = width // 16
    hidden = held_down.shape[1] // CHUNK
    both = 2 * hidden * CHUNK
    lane = lax.broadcasted_iota(jnp.int32, (EXPERT_ROWS, LANES), 1)
    tokens = dx_sum.shape[0] // 2
    tiles = tokens // EXPERT_ROWS
    tile = (turn + tiles) % row_steps
    rows = pl.ds(pl.multiple_of(tile * EXPERT_ROWS, EXPERT_ROWS), EXPERT_ROWS)

    def near_piece(c, k):
        return pairs_ref.at[c] if k == 0 else near_ref.at[c, k - 1]

    def near_copy(c, k):
        copies.copy(
            lambda c=c, k=k: (near_piece(c, k), weights.at[c, spots[k], y]), ("near", c, k), False
        )

    def near_wait(c, k):
        copies.wait_copy(
            lambda c=c, k=k: (near_piece(c, k), weights.at[c, spots[k], y]), ("near", c, k)
        )

    def far_ends(c, k):
        return far_ref.at[c, k], weights.at[c, spots[k], 1 - y]

    @pl.when(step == 0)
    def _():
        near.greet()
        gates[...] = jnp.zeros_like(gates)
        for k in range(SLOTS):
            near_copy(0, k)
            copies.copy(lambda k=k: far_ends(0, k), ("far", 0, k), False)
        copies.remote(
            lambda: (pairs_ref.at[last], weights.at[last, z, y]), ("y",), ("y",), near.over_y
        )
        for k in range(1, SLOTS):
            copies.remote(
                lambda: (pairs_ref.at[last], weights.at[last, z, y]),
                ("z", k), ("z", BACK[k]), near.along[k],
            )
        for c in range(LATE, last):
            for k in range(1, SLOTS):
                copies.remote(
                    lambda c=c, k=k: (near_piece(c, k), weights.at[c, spots[k], y]),
                    ("f", c, k), ("f", c, k), near.over_y,
                )
        for c in range(1, chunks):
            for k in range(SLOTS if c < last else 1):
                near_copy(c, k)
                if c < LATE or (c < last and k == 0):
                    copies.copy(lambda c=c, k=k: far_ends(c, k), ("far", c, k), False)

    @pl.when(step == row_steps)
    def _():
        copies.arrived(weights.at[last, z, 1 - y], ("y",), near.over_y)
        for k in range(1, SLOTS):
            copies.remote(
                lambda: (weights.at[last, z, 1 - y],) * 2,
                ("z2", k), ("z2", BACK[k]), near.along[k],
            )

    for c in range(chunks):

        @pl.when(step == c * steps)
        def _():
            for k in range(SLOTS):
                if c < last or k == 0:
                    near_wait(c, k)
                if c < LATE or (c < last and k == 0):
                    copies.wait_copy(lambda c=c, k=k: far_ends(c, k), ("far", c, k))
                elif c < last:
                    copies.arrived(weights.at[c, spots[k], 1 - y], ("f", c, k), near.over_y)
                elif k > 0:
                    copies.arrived(weights.at[c, spots[k], y], ("z", k), near.along[k])
                    copies.arrived(weights.at[c, spots[k], 1 - y], ("z2", k), near.along[k])

    def add_arrived(c):
        copies.arrived(arrived.at[c], ("sum", c), near.over_y)
        for k in range(SLOTS):
            own = grads.at[c, spots[k], y]
            for here in few_rows(own.shape[0]):
                own[here, :] = (
                    own[here, :].astype(F32) + arrived[c, spots[k], here, :].astype(F32)
                ).astype(BF16)
        copies.copy(lambda c=c: (grads.at[c, z, y], keep_outs[c]), ("keep", c))
        for k in range(1, SLOTS):
            copies.remote(
                lambda c=c, k=k: (grads.at[c, spots[k], y], part_outs[c].at[BACK[k] - 1]),
                ("part", c, k), ("part", c, BACK[k]), near.along[k],
            )

    @pl.when(step == 2 * steps + 3)
    def _():
        add_arrived(0)

    @pl.when(step == 3 * steps + 3)
    def _():
        add_arrived(1)

    @pl.when(turn < row_steps)
    def _():
        for e in range(CHUNK):
            first = 2 * hidden * e
            w_both = weights[chunk, :, :, :, first : first + 2 * hidden].reshape(width, 2 * hidden)
            start = both + hidden * e
            w_down = weights[chunk, :, :, :, start : start + hidden].reshape(width, hidden)
            gate_up = dot(x_ref[...], w_both)
            raw = dot(og_ref[...], w_down) * RESIDUAL_SCALE
            gate, up = gate_up[:, :hidden], gate_up[:, hidden:]
            gate_lane = lax.broadcasted_iota(
                jnp.int32, (EXPERT_ROWS, combine_ref.shape[1]), 1
            )
            column = jnp.sum(
                jnp.where(gate_lane == chunk * CHUNK + e, combine_ref[...], 0.0),
                axis=1, keepdims=True,
            )
            sigmoid = 1.0 / (1.0 + jnp.exp(-gate))
            active = gate * sigmoid
            inner_value = (active * up).astype(BF16).astype(F32)
            held_down[rows, hidden * e : hidden * (e + 1)] = (inner_value * column).astype(BF16)
            gates[rows, :] = jnp.where(
                lane == chunk * CHUNK + e,
                jnp.sum(inner_value * raw, axis=1, keepdims=True),
                gates[rows, :],
            )
            inner_grad = raw * column
            held_both[rows, first : first + hidden] = (
                inner_grad * up * sigmoid * (1.0 + gate * (1.0 - sigmoid))
            ).astype(BF16)
            held_both[rows, first + hidden : first + 2 * hidden] = (inner_grad * active).astype(BF16)

        def sums(add):
            for part in range(SLOTS):
                cols = slice(4 * block * part, 4 * block * (part + 1))
                w_both = weights[chunk, part, :, :, :both].reshape(4 * block, both)
                w_down = weights[chunk, part, :, :, both:].reshape(4 * block, hidden * CHUNK)
                mix = dot(held_down[rows, :], w_down, NT)
                dx = dot(held_both[rows, :], w_both, NT)
                if add:
                    mix = mix + mix_sum[rows, cols].astype(F32)
                    dx = dx + dx_sum[rows, cols].astype(F32)
                mix_sum[rows, cols] = mix.astype(BF16)
                dx_sum[rows, cols] = dx.astype(BF16)

        @pl.when(chunk == 0)
        def _():
            sums(False)

        @pl.when(chunk > 0)
        def _():
            sums(True)

    @pl.when(turn >= row_steps)
    def _():
        part = turn - row_steps
        grads[chunk, part, :, :, :both] = (
            dot(xt_ref[...], held_both[...]).astype(BF16).reshape(2, 2 * block, both)
        )
        grads[chunk, part, :, :, both:] = (
            (dot(ogt_ref[...], held_down[...]) * RESIDUAL_SCALE)
            .astype(BF16)
            .reshape(2, 2 * block, hidden * CHUNK)
        )

    begin = last * steps
    for i in range(2):
        for c in range(2):
            mine = pl.ds(tokens + (2 * c + i) * EXPERT_ROWS, EXPERT_ROWS)
            there = pl.ds((2 * c + i) * EXPERT_ROWS, EXPERT_ROWS)

            @pl.when((step == begin + 2 * c + i) & (core != c))
            def _():
                copies.remote(
                    lambda: (dx_sum.at[mine], twin_rows.at[i]), ("t", i), ("t", i), near.twin,
                    last=False,
                )

            @pl.when((step == begin + 2 + 2 * c + i) & (core == c))
            def _():
                copies.arrived(twin_rows.at[i], ("t", i), near.twin)
                for here in few_rows(EXPERT_ROWS):
                    at = pl.ds(mine.start + here.start, 16)
                    dx_sum[at, :] = (
                        dx_sum[at, :].astype(F32) + twin_rows[i, here, :].astype(F32)
                    ).astype(BF16)
                copies.remote(
                    lambda: (dx_sum.at[mine], dx_other.at[there]), ("o", i), ("o", i), near.over_x,
                    last=False,
                )

            @pl.when((step == begin + steps - 2 + i) & (core == c))
            def _():
                copies.arrived(dx_other.at[there], ("o", i), near.over_x)
                copies.remote(
                    lambda: (dx_other.at[there],) * 2, ("o2", i), ("o2", i), near.twin, last=False
                )

    for i in range(tiles):

        @pl.when(step == begin + tiles + i)
        def _():
            own = pl.ds(i * EXPERT_ROWS, EXPERT_ROWS)
            copies.copy(lambda own=own: (dx_sum.at[own], dx_own.at[own]), ("own", i))
            copies.remote(
                lambda own=own: (dx_sum.at[own], dx_twin.at[own]), ("own", i), ("own", i), near.twin
            )

    shares = gate_kept.shape[0]

    @pl.when(step == begin + row_steps)
    def _():
        copies.copy(lambda: (mix_sum, mix_out), "mix")
        turned = gates[...].T[:shares, :]
        gate_kept[...] = turned
        copies.remote(
            lambda: (gate_kept.at[:, pl.ds(tokens, tokens)], gate_got), ("g",), ("g",), near.over_x
        )

    @pl.when(step == begin + steps - 2)
    def _():
        copies.arrived(gate_got, ("g",), near.over_x)
        gate_full[pl.ds(pl.multiple_of(x * shares, shares), shares), :] = gate_kept[:, :tokens]
        gate_full[pl.ds(pl.multiple_of((1 - x) * shares, shares), shares), :] = gate_got[...]
        copies.remote(lambda: (gate_full, gate_twin), ("g2",), ("g2",), near.twin)

    for c in range(chunks):

        @pl.when(step == (c + 1) * steps - 1)
        def _():
            if c < SENT:
                copies.remote(
                    lambda c=c: (grads.at[c, :, 1 - y], arrived.at[c]),
                    ("sum", c), ("sum", c), near.over_y,
                )
            else:
                for k in range(SLOTS):
                    copies.copy(
                        lambda c=c, k=k: (grads.at[c, spots[k], y], near_outs[c - SENT].at[k]),
                        ("near out", c, k),
                    )
                    if c < last and k == 0:
                        copies.copy(lambda c=c: (grads.at[c, z, 1 - y], first_out), "first out")
                    elif c < last:
                        copies.remote(
                            lambda c=c, k=k: (grads.at[c, spots[k], 1 - y], late_out.at[k - 1]),
                            ("late", k), ("late", k), near.over_y,
                        )
                    else:
                        copies.copy(
                            lambda c=c, k=k: (grads.at[c, spots[k], 1 - y], far_out.at[k]),
                            ("far out", k),
                        )

    @pl.when(step == chunks * steps - 1)
    def _():
        copies.arrived(gate_twin, ("g2",), near.twin)
        gate_out[...] = gate_full[...] + gate_twin[...]
        for i in range(tiles):
            copies.arrived(
                dx_twin.at[pl.ds(i * EXPERT_ROWS, EXPERT_ROWS)], ("own", i), near.twin
            )
        for i in range(2):
            for c in range(2):
                mine = pl.ds(tokens + (2 * c + i) * EXPERT_ROWS, EXPERT_ROWS)
                there = pl.ds((2 * c + i) * EXPERT_ROWS, EXPERT_ROWS)

                @pl.when(core != c)
                def _():
                    copies.sent(lambda: (dx_sum.at[mine], twin_rows.at[i]), ("t", i), near.twin)
                    copies.arrived(dx_other.at[there], ("o2", i), near.twin)

                @pl.when(core == c)
                def _():
                    copies.sent(
                        lambda: (dx_sum.at[mine], dx_other.at[there]), ("o", i), near.over_x
                    )
                    copies.sent(lambda: (dx_other.at[there],) * 2, ("o2", i), near.twin)

        for c in range(SENT):
            for k in range(1, SLOTS):
                copies.arrived(part_outs[c].at[k - 1], ("part", c, k), near.along[k])
        for k in range(1, SLOTS):
            copies.arrived(late_out.at[k - 1], ("late", k), near.over_y)
        copies.finish()


def experts_pass(x, og, xt, ogt, combine, pairs, near, far):
    tokens, width = x.shape
    chunks, pair, columns = pairs.shape
    hidden = columns // (3 * CHUNK)
    shares = chunks * CHUNK
    row_steps = tokens // EXPERT_ROWS
    steps = row_steps + SLOTS
    inner = lax.axis_size("dp") // 16
    row_at = lambda s: ((jnp.minimum(s % steps, row_steps - 1) + row_steps // 2) % row_steps, 0)
    width_at = lambda s: (jnp.maximum(s % steps - row_steps, 0), 0)
    row = pl.BlockSpec((EXPERT_ROWS, width), row_at)
    turned = pl.BlockSpec((width // SLOTS, tokens), width_at)
    anywhere = pl.BlockSpec(memory_space=pl.ANY)
    left = chunks - SENT
    dma = pltpu.SemaphoreType.DMA
    shape = jax.ShapeDtypeStruct
    outs = pl.pallas_call(
        functools.partial(experts_kernel, inner, chunks, row_steps),
        grid=(chunks * steps,),
        in_specs=[row, row, turned, turned, pl.BlockSpec((EXPERT_ROWS, combine.shape[1]), row_at)]
        + [anywhere] * 3,
        out_specs=[anywhere] * 4
        + [pl.BlockSpec((2 * shares, tokens // 2), lambda s: (0, 0))]
        + [anywhere] * (2 * SENT + left + 3),
        out_shape=[shape((tokens // 2, width), BF16)] * 3
        + [shape((tokens, width), BF16), shape((2 * shares, tokens // 2), F32)]
        + [shape((pair, columns), BF16)] * SENT
        + [shape((SLOTS - 1, pair, columns), BF16)] * SENT
        + [shape((SLOTS, pair, columns), BF16)] * left
        + [shape((SLOTS - 1, pair, columns), BF16), shape((pair, columns), BF16)]
        + [shape((SLOTS, pair, columns), BF16)],
        scratch_shapes=[
            pltpu.VMEM((chunks + 1, SLOTS, 2, pair, columns), BF16),
            pltpu.VMEM((SENT, SLOTS, pair, columns), BF16),
            pltpu.VMEM((tokens, 2 * hidden * CHUNK), BF16),
            pltpu.VMEM((tokens, hidden * CHUNK), BF16),
            pltpu.VMEM((tokens, width), BF16),
            pltpu.VMEM((tokens, width), BF16),
            pltpu.VMEM((2, EXPERT_ROWS, width), BF16),
            pltpu.VMEM((tokens, LANES), F32),
            pltpu.VMEM((shares, tokens), F32),
            pltpu.VMEM((shares, tokens // 2), F32),
            pltpu.VMEM((2 * shares, tokens // 2), F32),
            pltpu.VMEM((2 * shares, tokens // 2), F32),
            dma((48,)), dma((48,)), dma((48,)),
        ],
        compiler_params=pltpu.CompilerParams(
            vmem_limit_bytes=EXPERT_VMEM, collective_id=0, has_side_effects=True
        ),
        cost_estimate=pl.CostEstimate(
            flops=8 * tokens * width * chunks * columns,
            bytes_accessed=2 * chunks * width * columns, transcendentals=0,
        ),
        name="experts_pass",
    )(x, og, xt, ogt, combine, pairs, near, far)
    dx, mix, gate = outs[:3], outs[3], outs[4]
    rest = outs[5:]
    keep, parts, rest = rest[:SENT], rest[SENT : 2 * SENT], rest[2 * SENT :]
    return dx, mix, gate, keep, parts, rest[:left], rest[left:]


class Copies:
    def __init__(self, send, recv, local):
        self.send, self.recv, self.local = send, recv, local
        self.sends, self.recvs, self.locals, self.started = {}, {}, {}, []

    def remote(self, ends, name, arrives, device, last=True):
        sent = self.sends.setdefault(name, len(self.sends))
        got = self.recvs.setdefault(arrives, len(self.recvs))

        def make():
            source, target = ends()
            return pltpu.make_async_remote_copy(
                source, target, self.send.at[sent], self.recv.at[got],
                device_id=device, device_id_type=MESH_ID,
            )

        make().start()
        if last:
            self.started.append(lambda: make().wait_send())

    def sent(self, ends, name, device):
        source, target = ends()
        pltpu.make_async_remote_copy(
            source, target, self.send.at[self.sends[name]], self.recv.at[0],
            device_id=device, device_id_type=MESH_ID,
        ).wait_send()

    def arrived(self, place, name, device):
        got = self.recvs.setdefault(name, len(self.recvs))
        pltpu.make_async_remote_copy(
            place, place, self.send.at[0], self.recv.at[got],
            device_id=device, device_id_type=MESH_ID,
        ).wait_recv()

    def copy(self, ends, name, wait_last=True):
        at = self.locals.setdefault(name, len(self.locals))

        def make():
            return pltpu.make_async_copy(*ends(), self.local.at[at])

        make().start()
        if wait_last:
            self.started.append(lambda: make().wait())
        return lambda: make().wait()

    def wait_copy(self, ends, name):
        pltpu.make_async_copy(*ends(), self.local.at[self.locals[name]]).wait()

    def finish(self):
        for wait in self.started:
            wait()


class Neighbours:
    def __init__(self, inner):
        me = lax.axis_index("dp")
        at = me // inner
        self.core = lax.axis_index("tensor")
        self.z, self.y, self.x = at // 4, at // 2 % 2, at % 2
        self.spots = [(self.z + dz + 4) % 4 for dz in Z_FROM]
        self.along = [{"dp": me + (spot - self.z) * 4 * inner} for spot in self.spots]
        self.over_y = {"dp": me + (1 - 2 * self.y) * 2 * inner}
        self.over_x = {"dp": me + (1 - 2 * self.x) * inner}
        self.twin = {"tensor": 1 - self.core}
        self.blocks = {
            (k, other_y, other_x): self.spots[k] * 4
            + (1 - self.y if other_y else self.y) * 2
            + (1 - self.x if other_x else self.x)
            for k in range(SLOTS)
            for other_y in (0, 1)
            for other_x in (0, 1)
        }

    def greet(self):
        barrier = pltpu.get_barrier_semaphore()
        devices = [*self.along[1:], self.over_y, self.over_x, self.twin]
        for device in devices:
            pl.semaphore_signal(barrier, inc=1, device_id=device, device_id_type=MESH_ID)
        pl.semaphore_wait(barrier, len(devices))

    def block(self, k, other_y, other_x):
        return self.blocks[k, other_y, other_x]


BACK = (0, 2, 1, 3)


class Gather:
    def __init__(self, copies, near, shard, full, tag):
        self.copies, self.near, self.shard, self.full, self.tag = copies, near, shard, full, tag
        self.split = full.shape[2] // (2 * LANES) * LANES

    def source(self, k):
        return self.shard if k == 0 else self.full.at[self.near.block(k, 0, 0)]

    def begin(self):
        for k in range(1, SLOTS):
            self.copies.remote(
                lambda: (self.shard, self.full.at[self.near.block(0, 0, 0)]),
                (self.tag, "z", k), (self.tag, "z", BACK[k]), self.near.along[k],
            )
        self.full[self.near.block(0, 0, 0)] = self.shard[...]

    def spread(self, k):
        near, place = self.near, self.full.at[self.near.block(k, 0, 0)]
        if k > 0:
            self.copies.arrived(place, (self.tag, "z", k), near.along[k])
        for way, device in (("y", near.over_y), ("x", near.over_x)):
            name = (self.tag, way, k)
            self.copies.remote(
                lambda: (self.source(k), self.full.at[near.block(k, 0, 0)]), name, name, device
            )

    def cross(self, k):
        near = self.near
        from_y = self.full.at[near.block(k, 1, 0)]
        from_x = self.full.at[near.block(k, 0, 1)]
        self.copies.arrived(from_y, (self.tag, "y", k), near.over_y)
        self.copies.remote(
            lambda: (self.full.at[near.block(k, 1, 0), :, : self.split],) * 2,
            (self.tag, "one", k), (self.tag, "one", k), near.over_x,
        )
        self.copies.arrived(from_x, (self.tag, "x", k), near.over_x)
        self.copies.remote(
            lambda: (self.full.at[near.block(k, 0, 1), :, self.split :],) * 2,
            (self.tag, "two", k), (self.tag, "two", k), near.over_y,
        )

    def end(self):
        near = self.near
        for k in range(SLOTS):
            place = self.full.at[near.block(k, 1, 1)]
            self.copies.arrived(place.at[:, : self.split], (self.tag, "one", k), near.over_x)
            self.copies.arrived(place.at[:, self.split :], (self.tag, "two", k), near.over_y)


def roll_left(slab, lanes):
    return pltpu.roll(slab, LANES - lanes, 1)


def forward_kernel(
    inner, q_shard, o_shard, gateup_hbm, down_hbm, hidden_hbm, og_hbm, cos, sin, seg_col, seg_row,
    routes,
    q_full, o_full, small, normed, q_ref, k_ref, v_ref, attended, lse_ref, combine, combine_pair,
    middle_hbm, x_hbm, xt_hbm, og_pair, ogt_hbm, pairs_hbm, near_hbm, far_hbm,
    hidden, gateup, down, given, pairs, bias, k_low, k_high, v_low, v_high, part, part_got, x_own, x_got,
    middle, stage, turned, columns_out, columns_got, send, recv, local,
):
    near = Neighbours(inner)
    copies = Copies(send, recv, local)
    tokens, width = hidden.shape
    block = width // 16
    chunks = pairs.shape[0]
    hid = down.shape[2]
    q_width = q_ref.shape[1]
    kv_slabs = k_ref.shape[1] // LANES
    slabs = q_width // LANES
    qkv_width = q_width + 2 * k_ref.shape[1]
    experts = down.shape[0]
    each = 2 + experts
    half = tokens // 2
    tiles = tokens // ROWS
    x, core = near.x, near.core
    own_half = pl.ds(pl.multiple_of(core * half, half), half)
    mine = pl.ds(pl.multiple_of(tokens + core * half, half), half)
    theirs = pl.ds(pl.multiple_of(tokens + (1 - core) * half, half), half)

    near.greet()
    gather_q = Gather(copies, near, q_shard, q_full, "q")
    gather_o = Gather(copies, near, o_shard, o_full, "o")
    gather_q.begin()
    gather_q.spread(0)
    weights_in = [
        copies.copy(lambda: (gateup_hbm, gateup), "gateup", False),
        copies.copy(lambda: (down_hbm, down), "down", False),
    ]
    hidden_in = copies.copy(lambda: (hidden_hbm, hidden), "hidden", False)
    copies.copy(lambda: (og_hbm, og_pair.at[pl.ds(0, tokens)]), "og")

    def pack(c, mine):
        first = 2 * (chunks * (x if mine else 1 - x) + c)
        rows = pl.ds(pl.multiple_of(x * block, block), block)
        for e in range(CHUNK):
            for part_at in range(2):
                at = hid * (2 * e + part_at)
                value = gateup[first + e, part_at].astype(BF16)
                if mine:
                    pairs[c, rows, at : at + hid] = value
                else:
                    given[c, :, at : at + hid] = value
            at = hid * (2 * CHUNK + e)
            value = down[first + e].astype(BF16)
            if mine:
                pairs[c, rows, at : at + hid] = value
            else:
                given[c, :, at : at + hid] = value

    def swap(c):
        rows = pl.ds(pl.multiple_of(x * block, block), block)
        copies.remote(
            lambda: (given.at[c], pairs.at[c, rows]), ("s", c), ("s", c), near.over_x
        )

    def swapped(c):
        rows = pl.ds(pl.multiple_of((1 - x) * block, block), block)
        copies.arrived(pairs.at[c, rows], ("s", c), near.over_x)

    def ring_one(c):
        copies.remote(
            lambda: (pairs.at[c], near_hbm.at[c, 0]), ("up", c), ("r", c, 1), near.along[2]
        )
        copies.remote(
            lambda: (pairs.at[c], near_hbm.at[c, 1]), ("down", c), ("r", c, 2), near.along[1]
        )

    def ring_two(c):
        copies.arrived(near_hbm.at[c, 0], ("r", c, 1), near.along[1])
        copies.remote(
            lambda: (near_hbm.at[c, 0], near_hbm.at[c, 2]), ("two", c), ("r", c, 3), near.along[2]
        )

    def over_y(c, k):
        copies.remote(
            lambda: (pairs.at[c] if k == 0 else near_hbm.at[c, k - 1], far_hbm.at[c, k]),
            ("f", c, k), ("f", c, k), near.over_y,
        )

    def ring_got(c, k):
        copies.arrived(near_hbm.at[c, k - 1], ("r", c, k), near.along[k])

    def turn_tile(source, target, name, side):
        copies.copy(lambda: (source, stage.at[side]), (name, "in"), False)()
        turned[side] = stage[side].T
        return copies.copy(lambda: (turned.at[side], target), (name, "out"), False)

    waits = [None, None]

    def turn_next(source, target, name, side):
        if waits[side] is not None:
            waits[side]()
        waits[side] = turn_tile(source, target, name, side)

    for wait in weights_in:
        wait()
    pack(0, False)
    swap(0)
    pack(0, True)
    gather_q.spread(1)
    gather_q.spread(2)
    pack(1, False)
    pack(1, True)
    gather_q.cross(0)
    gather_q.spread(3)
    gather_o.begin()
    pack(2, False)
    pack(2, True)
    gather_q.cross(1)
    gather_q.cross(2)
    swapped(0)
    ring_one(0)
    pack(3, False)
    pack(3, True)
    fill_bias(bias, seg_col, seg_row)
    gather_q.cross(3)
    over_y(0, 0)
    gather_o.spread(0)
    for c in range(1, chunks):
        swap(c)
    for tile in range(tiles):
        rows = pl.ds(tile * ROWS, ROWS)
        turn_next(og_hbm.at[rows], ogt_hbm.at[:, rows], ("og", tile), tile % 2)
    hidden_in()
    gather_q.end()
    pieces = q_full[:, :, qkv_width:].reshape(width, LANES)
    wide = pieces.astype(F32)
    summed = wide + roll_left(wide, each) + roll_left(wide, 2 * each)
    small[...] = summed.T[: small.shape[0], :]

    def project(tile, carry):
        rows = pl.ds(pl.multiple_of(tile * ROWS, ROWS), ROWS)
        for here in few_rows(ROWS):
            value = hidden[pl.ds(pl.multiple_of(tile * ROWS + here.start, 16), 16), :].astype(F32)
            inverse = lax.rsqrt(jnp.mean(value * value, axis=1, keepdims=True) + NORM_EPSILON)
            stage[0, here, :] = (value * inverse * small[0:1, :]).astype(BF16)
        low = stage[0]
        normed[:, rows] = low.T
        cosine, sine = cos[rows, :], sin[rows, :]
        for g in range(slabs + 2 * kv_slabs):
            lanes = slice(g * LANES, (g + 1) * LANES)
            if g % 2 == 0:
                two = slice(g * LANES, (g + 2) * LANES)
                lin_two = dot(low, q_full[:, :, two].reshape(width, 2 * LANES))
            lin = lin_two[:, (g % 2) * LANES : (g % 2 + 1) * LANES]
            if g < slabs + kv_slabs:
                lin = lin * cosine + rotate_halves(lin) * sine
            if g < slabs:
                q_ref[rows, lanes] = lin.astype(BF16)
            elif g < slabs + kv_slabs:
                at = (g - slabs) * LANES
                k_ref[rows, at : at + LANES] = lin.astype(BF16)
            else:
                at = (g - slabs - kv_slabs) * LANES
                v_ref[rows, at : at + LANES] = lin.astype(BF16)

        @pl.when(tile == 0)
        def _():
            gather_o.spread(1)
            gather_o.spread(2)

        @pl.when(tile == 2)
        def _():
            gather_o.spread(3)
            gather_o.cross(0)

        return carry

    lax.fori_loop(0, tiles, project, 0)
    for j in range(kv_slabs):
        lanes = slice(j * LANES, (j + 1) * LANES)
        spread_heads(k_ref[:, lanes], k_low, k_high, 2 * j)
        spread_heads(v_ref[:, lanes], v_low, v_high, 2 * j)

    def attend(g, carry):
        lanes = pl.ds(pl.multiple_of(g * LANES, LANES), LANES)
        kv_even, kv_odd = (2 * g) // 3, (2 * g + 1) // 3
        for at in range(0, tokens, ROWS):
            rows = slice(at, at + ROWS)
            upto = at + ROWS
            queries = q_ref[rows, lanes]
            total = None
            stats = []
            for keys, values, kv_at in ((k_low, v_low, kv_even), (k_high, v_high, kv_odd)):
                scores = dot(queries, keys[kv_at, :upto, :], NT) * SCORE_SCALE + bias[rows, :upto]
                highest = jnp.max(scores, axis=1, keepdims=True)
                weights = jnp.exp(scores - highest)
                whole = jnp.sum(weights, axis=1, keepdims=True)
                probability = (weights * (1.0 / whole)).astype(BF16)
                one = dot(probability, values[kv_at, :upto, :])
                total = one if total is None else total + one
                stats.append(highest + jnp.log(whole))
            attended[rows, lanes] = total.astype(BF16)
            across = jnp.where(half_mask(ROWS, False), stats[0], stats[1]).T
            lse_ref[g, 0:1, rows] = across[0:1, :]
            lse_ref[g, 1:2, rows] = across[HEAD_DIM : HEAD_DIM + 1, :]

        @pl.when(g == 0)
        def _():
            gather_o.cross(1)
            gather_o.cross(2)
            ring_two(0)
            over_y(0, 1)
            swapped(1)
            ring_one(1)
            over_y(1, 0)

        @pl.when(g == 1)
        def _():
            gather_o.cross(3)
            ring_got(0, 2)
            over_y(0, 2)
            copies.remote(
                lambda: (og_hbm.at[own_half], og_pair.at[mine]), ("og",), ("og",), near.over_x
            )

        @pl.when(g == slabs - 1)
        def _():
            ring_got(0, 3)
            over_y(0, 3)
            gather_o.end()

        return carry

    lax.fori_loop(0, slabs, attend, 0)

    def project_out(step, carry):
        tile = (step + 2 * (1 - core)) % tiles
        rows = pl.ds(pl.multiple_of(tile * ROWS, ROWS), ROWS)
        low = attended[rows, :]
        for group in range(SLOTS):
            cols = slice(4 * block * group, 4 * block * (group + 1))
            weight = o_full[4 * group : 4 * (group + 1)].reshape(4 * block, q_width)
            part[rows, cols] = dot(low, weight, NT).astype(BF16)
        return carry

    for step in range(tiles):
        project_out(step, 0)
        tile = (step + 2 * (1 - core)) % tiles
        rows = pl.ds(pl.multiple_of(tile * ROWS, ROWS), ROWS)
        copies.remote(
            lambda rows=rows: (part.at[rows], part_got.at[rows]),
            ("p", step), ("p", step), near.twin,
        )
    swapped(2)
    ring_one(2)
    over_y(2, 0)
    router = q_full[:, :, qkv_width:].reshape(width, LANES)
    for step in range(tiles):
        tile = (step + 2 * core) % tiles
        rows = pl.ds(pl.multiple_of(tile * ROWS, ROWS), ROWS)
        copies.arrived(part_got.at[rows], ("p", step), near.twin)
        side = step % 2
        if step >= 2:
            middle_out[side]()
        elif step == 0:
            middle_out = [None, None]
        for here in few_rows(ROWS):
            at = pl.ds(pl.multiple_of(tile * ROWS + here.start, 16), 16)
            total = hidden[at, :].astype(F32) + RESIDUAL_SCALE * (
                part[at, :].astype(F32) + part_got[at, :].astype(F32)
            )
            middle[side, here, :] = total
            inverse = lax.rsqrt(jnp.mean(total * total, axis=1, keepdims=True) + NORM_EPSILON)
            value = total * inverse * small[1:2, :]
            high = value.astype(BF16)
            x_own[at, :] = high
            rest = value - high.astype(F32)
            mid = rest.astype(BF16)
            stage[0, here, :] = mid
            stage[1, here, :] = (rest - mid.astype(F32)).astype(BF16)
        middle_out[side] = copies.copy(
            lambda rows=rows, side=side: (middle.at[side], middle_hbm.at[rows]), ("m", step), False
        )
        copies.copy(lambda rows=rows: (x_own.at[rows], x_hbm.at[rows]), ("x", step))
        if step < 2:
            copies.remote(
                lambda rows=rows: (x_own.at[rows], x_got.at[rows]),
                ("x", step), ("x", step), near.over_x,
            )
        one, two, three = dot(x_own[rows, :], router), dot(stage[0], router), dot(stage[1], router)
        logits = one + roll_left(one, each) + roll_left(one, 2 * each) + two + roll_left(two, each)
        logits = roll_left(logits + three, 2)
        lane = lax.broadcasted_iota(jnp.int32, (ROWS, LANES), 1)
        chosen = lane < 0
        route = routes[rows, :]
        for k in range(routes.shape[1]):
            chosen = chosen | (route[:, k : k + 1] == lane)
        logits = jnp.where(chosen, logits, MASK_VALUE)
        powers = jnp.exp(logits - jnp.max(logits, axis=1, keepdims=True))
        powers = jnp.where(chosen, powers, 0.0)
        combine[rows, :] = powers * (1.0 / jnp.sum(powers, axis=1, keepdims=True))
        if step == 0:
            swapped(3)
            copies.copy(lambda: (pairs, pairs_hbm), "pairs")
        if step == 1:
            ring_two(1)
            over_y(1, 1)
            ring_got(1, 2)
            over_y(1, 2)

    shares = experts // 2
    flipped = combine[...].T
    kept = jnp.where(x == 0, flipped[:shares, :], flipped[shares : 2 * shares, :])
    gone = jnp.where(x == 0, flipped[shares : 2 * shares, :], flipped[:shares, :])
    columns_out[...] = gone
    copies.remote(lambda: (columns_out, columns_got), ("c",), ("c",), near.over_x)
    combine_pair[:tokens, :] = kept.T

    copies.arrived(og_pair.at[mine], ("og",), near.over_x)
    copies.remote(lambda: (og_pair.at[mine],) * 2, ("og2",), ("og2",), near.twin)
    for tile in range(tiles):
        rows = pl.ds(tile * ROWS, ROWS)
        if waits[tile % 2] is not None:
            waits[tile % 2]()
        turned[tile % 2] = x_own[rows, :].T
        waits[tile % 2] = copies.copy(
            lambda rows=rows, side=tile % 2: (turned.at[side], xt_hbm.at[:, rows]),
            ("xt", tile), False,
        )
    ring_two(2)
    ring_got(1, 3)
    over_y(1, 3)
    copies.arrived(columns_got, ("c",), near.over_x)
    combine_pair[tokens:, :] = columns_got[...].T
    copies.arrived(og_pair.at[theirs], ("og2",), near.twin)
    order = [(step + 2 * core) % tiles for step in range(2)]
    order += [(step + 2 * (1 - core)) % tiles for step in range(2)]

    def og_rows(step):
        return pl.ds(pl.multiple_of(tokens + order[step] * ROWS, ROWS), ROWS)

    def og_load(step):
        return copies.copy(
            lambda: (og_pair.at[og_rows(step)], stage.at[step % 2]), ("ogin", step), False
        )

    loaded = og_load(0)
    for step in range(tiles):
        loaded()
        if step + 1 < tiles:
            loaded = og_load(step + 1)
        side = step % 2
        waits[side]()
        turned[side] = stage[side].T
        waits[side] = copies.copy(
            lambda step=step, side=side: (turned.at[side], ogt_hbm.at[:, og_rows(step)]),
            ("ogt", step), False,
        )
    for step in range(tiles):
        rows = pl.ds(pl.multiple_of(order[step] * ROWS, ROWS), ROWS)
        there = pl.ds(pl.multiple_of(tokens + order[step] * ROWS, ROWS), ROWS)
        if step < 2:
            copies.arrived(x_got.at[rows], ("x", step), near.over_x)
            copies.remote(
                lambda rows=rows: (x_got.at[rows],) * 2, ("x2", step), ("x2", step), near.twin
            )
        else:
            copies.arrived(x_got.at[rows], ("x2", step - 2), near.twin)
        copies.copy(
            lambda rows=rows, there=there: (x_got.at[rows], x_hbm.at[there]), ("xg", step)
        )
        side = step % 2
        waits[side]()
        turned[side] = x_got[rows, :].T
        waits[side] = copies.copy(
            lambda there=there, side=side: (turned.at[side], xt_hbm.at[:, there]),
            ("xgt", step), False,
        )
    for wait in waits + middle_out:
        wait()
    ring_got(2, 2)
    ring_got(2, 3)
    for c in range(LATE + 1):
        for k in range(SLOTS if c < LATE else 1):
            copies.arrived(far_hbm.at[c, k], ("f", c, k), near.over_y)
    copies.finish()


def forward_pass(q_shard, o_shard, gateup, down, hidden, og, cosine, sine, segments, routes):
    tokens, width = hidden.shape
    experts, hid = down.shape[0], down.shape[2]
    block, q_columns = q_shard.shape
    q_width = o_shard.shape[1]
    kv_width = (q_columns - LANES - q_width) // 2
    slabs, kv_heads = q_width // LANES, kv_width // HEAD_DIM
    chunks = experts // (2 * CHUNK)
    columns = 3 * CHUNK * hid
    anywhere, vmem = pl.BlockSpec(memory_space=pl.ANY), vmem_spec()
    shape = jax.ShapeDtypeStruct
    inner = lax.axis_size("dp") // 16
    dma = pltpu.SemaphoreType.DMA
    return pl.pallas_call(
        functools.partial(forward_kernel, inner),
        in_specs=[vmem, vmem] + [anywhere] * 4 + [vmem] * 5,
        out_specs=[vmem] * 11 + [anywhere] * 8,
        out_shape=[
            shape((16, block, q_columns), BF16),
            shape((16, block, q_width), BF16),
            shape((24, width), F32),
            shape((width, tokens), BF16),
            shape((tokens, q_width), BF16),
            shape((tokens, kv_width), BF16),
            shape((tokens, kv_width), BF16),
            shape((tokens, q_width), BF16),
            shape((slabs, 8, tokens), F32),
            shape((tokens, LANES), F32),
            shape((2 * tokens, experts // 2), F32),
            shape((tokens, width), F32),
            shape((2 * tokens, width), BF16),
            shape((width, 2 * tokens), BF16),
            shape((2 * tokens, width), BF16),
            shape((width, 2 * tokens), BF16),
            shape((chunks, 2 * block, columns), BF16),
            shape((chunks - 1, SLOTS - 1, 2 * block, columns), BF16),
            shape((LATE + 1, SLOTS, 2 * block, columns), BF16),
        ],
        scratch_shapes=[
            pltpu.VMEM((tokens, width), BF16),
            pltpu.VMEM(gateup.shape, gateup.dtype),
            pltpu.VMEM(down.shape, down.dtype),
            pltpu.VMEM((chunks, block, columns), BF16),
            pltpu.VMEM((chunks, 2 * block, columns), BF16),
            pltpu.VMEM((tokens, tokens), F32),
        ]
        + [pltpu.VMEM((kv_heads, tokens, LANES), BF16)] * 4
        + [pltpu.VMEM((tokens, width), BF16)] * 4
        + [
            pltpu.VMEM((2, ROWS, width), F32),
            pltpu.VMEM((2, ROWS, width), BF16),
            pltpu.VMEM((2, width, ROWS), BF16),
            pltpu.VMEM((experts // 2, tokens), F32),
            pltpu.VMEM((experts // 2, tokens), F32),
            dma((80,)), dma((80,)), dma((60,)),
        ],
        compiler_params=pltpu.CompilerParams(
            vmem_limit_bytes=EXPERT_VMEM, collective_id=1, has_side_effects=True
        ),
        name="forward_pass",
    )(
        q_shard, o_shard, gateup, down, hidden, og, cosine, sine,
        segments[:, None], segments[None, :], routes,
    )


class Scatter:
    def __init__(self, copies, near, grad, one, two, got_y, got_x, got_z, share, tag):
        self.copies, self.near, self.grad, self.share, self.tag = copies, near, grad, share, tag
        self.one, self.two, self.got_y, self.got_x, self.got_z = one, two, got_y, got_x, got_z
        self.split = one.shape[2]

    def begin(self, k):
        near = self.near
        self.copies.remote(
            lambda: (self.grad.at[near.block(k, 1, 1), :, : self.split], self.one.at[k]),
            (self.tag, "one", k), (self.tag, "one", k), near.over_x,
        )
        self.copies.remote(
            lambda: (self.grad.at[near.block(k, 1, 1), :, self.split :], self.two.at[k]),
            (self.tag, "two", k), (self.tag, "two", k), near.over_y,
        )

    def cross(self, k):
        near, grad, split = self.near, self.grad, self.split
        self.copies.arrived(self.one.at[k], (self.tag, "one", k), near.over_x)
        at = near.block(k, 1, 0)
        for here in few_rows(grad.shape[1]):
            grad[at, here, :split] = (
                grad[at, here, :split].astype(F32) + self.one[k, here, :].astype(F32)
            ).astype(BF16)
        self.copies.remote(
            lambda: (grad.at[near.block(k, 1, 0)], self.got_y.at[k]),
            (self.tag, "y", k), (self.tag, "y", k), near.over_y,
        )
        self.copies.arrived(self.two.at[k], (self.tag, "two", k), near.over_y)
        at = near.block(k, 0, 1)
        for here in few_rows(grad.shape[1]):
            grad[at, here, split:] = (
                grad[at, here, split:].astype(F32) + self.two[k, here, :].astype(F32)
            ).astype(BF16)
        self.copies.remote(
            lambda: (grad.at[near.block(k, 0, 1)], self.got_x.at[k]),
            (self.tag, "x", k), (self.tag, "x", k), near.over_x,
        )

    def plane(self, k):
        near, grad = self.near, self.grad
        self.copies.arrived(self.got_y.at[k], (self.tag, "y", k), near.over_y)
        self.copies.arrived(self.got_x.at[k], (self.tag, "x", k), near.over_x)
        at = near.block(k, 0, 0)
        for here in few_rows(grad.shape[1]):
            total = grad[at, here, :].astype(F32) + self.got_y[k, here, :].astype(F32)
            total = total + self.got_x[k, here, :].astype(F32)
            if k == 0:
                self.share[here, :] = total
            else:
                grad[at, here, :] = total.astype(BF16)
        if k == 0:
            return
        self.copies.remote(
            lambda: (grad.at[near.block(k, 0, 0)], self.got_z.at[BACK[k] - 1]),
            (self.tag, "z", k), (self.tag, "z", BACK[k]), near.along[k],
        )

    def end(self):
        for k in range(1, SLOTS):
            self.copies.arrived(self.got_z.at[k - 1], (self.tag, "z", k), self.near.along[k])
            for here in few_rows(self.share.shape[0]):
                self.share[here, :] = self.share[here, :] + self.got_z[k - 1, here, :].astype(F32)


STRIP = 128


def backward_kernel(
    inner,
    o_full, q_ref, k_ref, v_ref, attended, lse_ref, cos, sin, seg_col, seg_row, small, combine,
    gate_turned, q_hbm, normed_hbm, hidden_hbm, og_hbm, middle_hbm, dx_own, dx_twin, dx_other,
    mix_pair, *refs,
):
    keeps, refs = refs[:SENT], refs[SENT:]
    parts, refs = refs[:SENT], refs[SENT:]
    near_two, near_three, late_got, far_first, far_three = refs[:5]
    q_share, o_share, input_grad, block_out, kept_out, given_got, mid_grad = refs[5:12]
    far_got, first_got, z_two, z_three, mix_twin, mix_half, mix_other = refs[12:19]
    (
        attended_grad, lin_grad, o_grad, q_grad, o_one, o_two, o_y, o_x, o_z,
        q_one, q_two, q_y, q_x, q_z, part_got, pieces, z_send, z_keep, given, kept,
        strips, wide_in, wide_out, strip_out, router_rows, gate_columns, small_sum,
        send, recv, local, strip_sem, wide_sem, out_sem,
    ) = refs[19:]
    near = Neighbours(inner)
    copies = Copies(send, recv, local)
    tokens, width = hidden_hbm.shape
    block = width // 16
    x, core = near.x, near.core
    half = tokens // 2
    q_width = q_ref.shape[1]
    kv_width = k_ref.shape[1]
    kv_slabs, slabs = kv_width // LANES, q_width // LANES
    qkv_width = q_width + 2 * kv_width
    experts = gate_turned.shape[0]
    each = 2 + experts
    strip_count = tokens // STRIP
    ours = pl.ds(0, tokens)
    half_mine = pl.ds(pl.multiple_of(tokens + core * half, half), half)
    half_other = pl.ds(pl.multiple_of(tokens + (1 - core) * half, half), half)
    there = pl.ds(pl.multiple_of(core * half, half), half)
    not_there = pl.ds(pl.multiple_of((1 - core) * half, half), half)
    scatter_o = Scatter(copies, near, o_grad, o_one, o_two, o_y, o_x, o_z, o_share, "o")
    scatter_q = Scatter(copies, near, q_grad, q_one, q_two, q_y, q_x, q_z, q_share, "q")
    z_gots = [*parts, z_two, z_three]

    def y_ends(c, k):
        if c == SENT:
            return near_two.at[k], first_got if k == 0 else late_got.at[k - 1]
        return near_three.at[k], far_got.at[k]

    def y_load(c, k, i, which):
        if 0 in which:
            copies.copy(lambda: (y_ends(c, k)[0], pieces.at[2 * i]), ("own", c, k), False)
        if 1 in which:
            copies.copy(lambda: (y_ends(c, k)[1], pieces.at[2 * i + 1]), ("got", c, k), False)

    def y_sum(c, k, i):
        copies.wait_copy(lambda: (y_ends(c, k)[0], pieces.at[2 * i]), ("own", c, k))
        copies.wait_copy(lambda: (y_ends(c, k)[1], pieces.at[2 * i + 1]), ("got", c, k))
        if k > 0 and c > SENT:
            copies.sent(
                lambda: (z_send.at[k - 1], z_two.at[BACK[k] - 1]), (SENT, "z", k), near.along[k]
            )
        target = z_keep.at[c - SENT] if k == 0 else z_send.at[k - 1]
        for here in few_rows(target.shape[0]):
            target[here, :] = (
                pieces[2 * i, here, :].astype(F32) + pieces[2 * i + 1, here, :].astype(F32)
            ).astype(BF16)
        if k == 0:
            return
        copies.remote(
            lambda: (z_send.at[k - 1], z_gots[c].at[BACK[k] - 1]),
            (c, "z", k), (c, "z", BACK[k]), near.along[k], last=c > SENT,
        )

    def far_arrived(k):
        copies.arrived(far_got.at[k], ("far", k), near.over_y)

    def chunk_ends(c, k):
        return keeps[c] if k == 0 else z_gots[c].at[k - 1], pieces.at[k]

    def load_chunk(c):
        for k in range(1 if c >= SENT else 0, SLOTS):
            if c >= SENT:
                copies.arrived(z_gots[c].at[k - 1], (c, "z", k), near.along[k])
            copies.copy(lambda k=k: chunk_ends(c, k), (c, "sum", k), False)

    def sum_chunk(c):
        for k in range(1 if c >= SENT else 0, SLOTS):
            copies.wait_copy(lambda: chunk_ends(c, k), (c, "sum", k))
        if c >= 2:
            copies.wait_copy(lambda: (kept.at[c % 2], kept_out.at[c - 2]), ("kept", c - 2))
        for base, mine in ((x * block, True), ((1 - x) * block, False)):
            for here, rows in zip(few_rows(block), few_rows(block, base)):
                total = (pieces[0, rows, :] if c < SENT else z_keep[c - SENT, rows, :]).astype(F32)
                for k in range(1, SLOTS):
                    total = total + pieces[k, rows, :].astype(F32)
                if mine:
                    kept[c % 2, here, :] = total
                else:
                    given[c, here, :] = total.astype(BF16)
        copies.copy(lambda: (kept.at[c % 2], kept_out.at[c]), ("kept", c), c >= 2)
        copies.remote(
            lambda: (given.at[c], given_got.at[c]), ("given", c), ("given", c), near.over_x
        )

    def strip_rows(t):
        return pl.ds(pl.multiple_of(t * STRIP, STRIP), STRIP)

    def strip_loads(t, sources, wide):
        side = t % 2
        rows = strip_rows(t)
        loads = [
            pltpu.make_async_copy(source.at[rows], strips.at[i, side], strip_sem.at[i, side])
            for i, source in enumerate(sources)
        ]
        if wide is not None:
            loads.append(
                pltpu.make_async_copy(wide.at[rows], wide_in.at[side], wide_sem.at[side])
            )
        return loads

    def strip_store(t, source, target):
        side = t % 2
        return pltpu.make_async_copy(
            source.at[side], target.at[strip_rows(t)], out_sem.at[side]
        )

    def over_strips(sources, wide, source, target, compute):
        for load in strip_loads(0, sources, wide):
            load.start()

        def one(t, carry):
            side = t % 2

            @pl.when(t + 1 < strip_count)
            def _():
                for load in strip_loads(t + 1, sources, wide):
                    load.start()

            for load in strip_loads(t, sources, wide):
                load.wait()

            @pl.when(t >= 2)
            def _():
                strip_store(t - 2, source, target).wait()

            compute(t, side)
            strip_store(t, source, target).start()
            return carry

        lax.fori_loop(0, strip_count, one, 0)
        for t in (strip_count - 2, strip_count - 1):
            strip_store(t, source, target).wait()

    for i, k in enumerate((1, 2)):
        y_load(SENT, k, i, (0, 1))
    near.greet()
    for k in (1, 2, 3, 0):
        copies.remote(
            lambda k=k: (far_three.at[k], far_got.at[k]), ("far", k), ("far", k), near.over_y
        )
    copies.remote(lambda: (far_first, first_got), ("first",), ("first",), near.over_y)
    copies.remote(
        lambda: (mix_pair.at[half_other], mix_half), ("mh",), ("mh",), near.twin
    )
    copies.remote(lambda: (mix_pair.at[ours], mix_twin), ("mt",), ("mt",), near.twin)
    y_sum(SENT, 1, 0)
    y_load(SENT, 3, 0, (0, 1))
    y_sum(SENT, 2, 1)
    y_sum(SENT, 3, 0)
    load_chunk(0)

    router = small[2 : 2 + experts, :]
    high = router.astype(BF16).astype(F32)
    mid = (router - high).astype(BF16).astype(F32)
    low = router - high - mid
    router_rows[...] = jnp.concatenate(
        [high, mid, low, high, mid, high, jnp.zeros((LANES - 6 * experts, width), F32)]
    ).astype(BF16)
    gate_columns[...] = jnp.concatenate(
        [gate_turned[...], jnp.zeros((LANES - experts, tokens), F32)]
    ).T
    small_sum[...] = jnp.zeros_like(small_sum)

    def middle_part(turned_back):
        def compute(t, side):
            rows = strip_rows(t)
            gates, grads = combine[rows, :], gate_columns[rows, :]
            logit = gates * (grads - jnp.sum(gates * grads, axis=1, keepdims=True))
            one = logit.astype(BF16).astype(F32)
            two = (logit - one).astype(BF16).astype(F32)
            three = (logit - one - two).astype(BF16).astype(F32)

            def moved(piece, by):
                return pltpu.roll(piece, by * experts, 1)

            row = one + moved(one, 1) + moved(one, 2) + moved(two, 3) + moved(two, 4)
            row = (row + moved(three, 5)).astype(BF16)
            wide_out[side] = dot(row, router_rows[...])
            gain = small[1:2, :]
            gain_part = None
            back, n_one, n_two, n_three = (
                strip_out.at[0], strip_out.at[1], z_keep.at[0], z_keep.at[1]
            )
            for here in few_rows(STRIP):
                upstream = strips[0, side, here, :].astype(F32) + strips[1, side, here, :].astype(F32)
                upstream = upstream + strips[2, side, here, :].astype(F32)
                upstream = upstream + wide_out[side, here, :]
                middle = wide_in[side, here, :]
                inverse = lax.rsqrt(jnp.mean(middle * middle, axis=1, keepdims=True) + NORM_EPSILON)
                scaled = middle * inverse
                weighted = upstream * gain
                mean_term = jnp.mean(weighted * scaled, axis=1, keepdims=True)
                grad = strips[3, side, here, :].astype(F32) + inverse * (
                    weighted - scaled * mean_term
                )
                wide_out[side, here, :] = grad
                back[here, :] = (RESIDUAL_SCALE * grad).astype(BF16)
                gained = jnp.sum(upstream * scaled, axis=0, keepdims=True)
                gain_part = gained if gain_part is None else gain_part + gained
                normed = scaled * gain
                piece = normed.astype(BF16)
                n_one[here, :] = piece
                rest = normed - piece.astype(F32)
                piece = rest.astype(BF16)
                n_two[here, :] = piece
                n_three[here, :] = (rest - piece.astype(F32)).astype(BF16)
            small_sum[0:1, :] += gain_part
            strip = pl.ds(0, STRIP)
            turned_back[:, rows] = back[...].T
            attended_grad[rows, :] = dot(back[...], o_full[...].reshape(width, q_width)).astype(BF16)
            columns = (one + moved(two, 1) + moved(three, 2)).T[: 3 * experts, :].astype(BF16)
            a, b, c = (
                dot(columns, n_one[...]), dot(columns, n_two[strip, :]), dot(columns, n_three[strip, :])
            )
            e = experts
            small_sum[8 : 8 + e, :] += (
                a[:e] + a[e : 2 * e] + a[2 * e :] + b[:e] + b[e : 2 * e] + c[:e]
            )

        over_strips([dx_own, dx_twin, dx_other, og_hbm], middle_hbm, wide_out, mid_grad, compute)
        for group in range(SLOTS):
            rows = slice(4 * block * group, 4 * block * (group + 1))
            o_grad[4 * group : 4 * (group + 1)] = (
                dot(turned_back[rows, :], attended[...]).astype(BF16).reshape(4, block, q_width)
            )

    pl.run_scoped(middle_part, pltpu.VMEM((width, tokens), BF16))
    for k in (1, 2, 3, 0):
        scatter_o.begin(k)

    def mix_load(i):
        rows = pl.ds(i * STRIP, STRIP)
        whole = pl.ds(pl.multiple_of(tokens + core * half + i * STRIP, STRIP), STRIP)
        return [
            copies.copy(lambda: (mix_pair.at[whole], strips.at[0, i % 2]), ("m0", i), False),
            copies.copy(lambda: (mix_half.at[rows], strips.at[1, i % 2]), ("m1", i), False),
        ]

    def send_mix():
        count = half // STRIP
        loads = mix_load(0)
        for i in range(count):
            rows = pl.ds(i * STRIP, STRIP)
            for load in loads:
                load()
            if i + 1 < count:
                loads = mix_load(i + 1)
            if i >= 2:
                copies.wait_copy(
                    lambda: (strip_out.at[i % 2], mix_half.at[rows]), ("m2", i - 2)
                )
            for here in few_rows(STRIP):
                strip_out[i % 2, here, :] = (
                    strips[0, i % 2, here, :].astype(F32) + strips[1, i % 2, here, :].astype(F32)
                ).astype(BF16)
            copies.copy(
                lambda i=i, rows=rows: (strip_out.at[i % 2], mix_half.at[rows]), ("m2", i), False
            )
        for i in (count - 2, count - 1):
            copies.wait_copy(
                lambda: (strip_out.at[i % 2], mix_half.at[pl.ds(i * STRIP, STRIP)]), ("m2", i)
            )
        copies.remote(lambda: (mix_half, mix_other.at[there]), ("mo",), ("mo",), near.over_x)

    def attention_part(bias0, bias1, bias2, bias3, k_low, k_high, v_low, v_high, dk, dv, dq):
        biases = (bias0, bias1, bias2, bias3)
        for at, bias in enumerate(biases):
            upto = bias.shape[0]
            keys_at = lax.broadcasted_iota(jnp.int32, bias.shape, 0)
            rows_at = at * ROWS + lax.broadcasted_iota(jnp.int32, bias.shape, 1)
            same = seg_col[:upto, :] == seg_row[:, at * ROWS : (at + 1) * ROWS]
            bias[...] = jnp.where((rows_at >= keys_at) & same, 0.0, MASK_VALUE).astype(F32)
        for j in range(kv_slabs):
            lanes = slice(j * LANES, (j + 1) * LANES)
            spread_heads(k_ref[:, lanes], k_low, k_high, 2 * j)
            spread_heads(v_ref[:, lanes], v_low, v_high, 2 * j)
        dk[...] = jnp.zeros_like(dk)
        dv[...] = jnp.zeros_like(dv)

        def slab(g, carry):
            lanes = pl.ds(pl.multiple_of(g * LANES, LANES), LANES)
            kv_even, kv_odd = (2 * g) // 3, (2 * g + 1) // 3
            for at, bias in enumerate(biases):
                rows = slice(at * ROWS, (at + 1) * ROWS)
                upto = (at + 1) * ROWS
                queries, grads = q_ref[rows, lanes], attended_grad[rows, lanes]
                turned = (grads.astype(F32) * attended[rows, lanes].astype(F32)).T
                zero = jnp.zeros_like(queries)
                dq_part = None
                for upper, keys, values, kv_at in (
                    (False, k_low, v_low, kv_even), (True, k_high, v_high, kv_odd)
                ):
                    first = HEAD_DIM if upper else 0
                    delta = jnp.sum(turned[first : first + HEAD_DIM, :], axis=0, keepdims=True)
                    head = 1 if upper else 0
                    total = lse_ref[g, head : head + 1, rows]
                    keys_here = keys[kv_at, :upto, :]
                    scores = dot(keys_here, queries, NT) * SCORE_SCALE + bias[...]
                    probability = jnp.exp(scores - total)
                    prob_grad = dot(values[kv_at, :upto, :], grads, NT)
                    score_grad = (probability * (prob_grad - delta)).astype(BF16)
                    mask = half_mask(ROWS, upper)
                    dv[kv_at, :upto, :] += dot(
                        probability.astype(BF16), jnp.where(mask, grads, zero)
                    )
                    dk[kv_at, :upto, :] += dot(score_grad, jnp.where(mask, queries, zero))
                    one = dot(score_grad, keys_here, TN)
                    dq_part = one if dq_part is None else dq_part + one
                dq[rows, :] = dq_part * SCORE_SCALE
            whole = dq[...]
            lin_grad[:, lanes] = (
                whole * cos[...] - rotate_halves(whole) * sin[...]
            ).astype(BF16)

            @pl.when(g == 0)
            def _():
                for k in (1, 2, 3, 0):
                    scatter_o.cross(k)
                sum_chunk(0)
                load_chunk(1)

            @pl.when(g == 1)
            def _():
                copies.arrived(mix_half, ("mh",), near.twin)
                send_mix()

            @pl.when(g == 2)
            def _():
                for k in (1, 2, 3, 0):
                    scatter_o.plane(k)
                sum_chunk(1)
                y_load(SENT + 1, 1, 0, (0,))
                y_load(SENT + 1, 2, 1, (0,))

            @pl.when(g == 3)
            def _():
                far_arrived(1)
                y_load(SENT + 1, 1, 0, (1,))
                far_arrived(2)
                y_load(SENT + 1, 2, 1, (1,))
                far_arrived(3)
                y_sum(SENT + 1, 1, 0)
                y_load(SENT + 1, 3, 0, (0, 1))
                y_sum(SENT + 1, 2, 1)
                y_sum(SENT + 1, 3, 0)

            @pl.when(g == 4)
            def _():
                scatter_o.end()
                far_arrived(0)
                y_load(SENT + 1, 0, 0, (0, 1))
                copies.arrived(first_got, ("first",), near.over_y)
                y_load(SENT, 0, 1, (0, 1))

            @pl.when(g == slabs - 1)
            def _():
                y_sum(SENT + 1, 0, 0)
                y_sum(SENT, 0, 1)
                load_chunk(2)

            return carry

        lax.fori_loop(0, slabs, slab, 0)
        low = half_mask(tokens, False)

        def joined(sums, j):
            one, two = sums[2 * j], sums[2 * j + 1]
            one = one + pltpu.roll(one, HEAD_DIM, 1)
            two = two + pltpu.roll(two, HEAD_DIM, 1)
            return jnp.where(low, one, two)

        for j in range(kv_slabs):
            at = q_width + j * LANES
            whole = joined(dk, j) * SCORE_SCALE
            lin_grad[:, at : at + LANES] = (
                whole * cos[...] - rotate_halves(whole) * sin[...]
            ).astype(BF16)
            at = at + kv_width
            lin_grad[:, at : at + LANES] = joined(dv, j).astype(BF16)

    kv_shape = (2 * kv_slabs, tokens, LANES)
    pl.run_scoped(
        attention_part,
        *[pltpu.VMEM(((at + 1) * ROWS, ROWS), F32) for at in range(tokens // ROWS)],
        *[pltpu.VMEM(kv_shape, BF16)] * 4,
        *[pltpu.VMEM(kv_shape, F32)] * 2,
        pltpu.VMEM((tokens, LANES), F32),
    )

    def last_part(normed_turned, q_full, part):
        normed_in = copies.copy(lambda: (normed_hbm, normed_turned), "normed", False)
        weights_in = copies.copy(lambda: (q_hbm, q_full), "q weights", False)
        columns = jnp.concatenate(
            [
                small_sum[0:1, :], small_sum[8 : 8 + experts, :],
                jnp.zeros((LANES - 1 - experts, width), F32),
            ]
        ).T
        q_grad[:, :, qkv_width:] = columns.astype(BF16).reshape(16, block, LANES)
        normed_in()
        for k in (1, 2, 3, 0):
            spot = near.spots[k]
            rows = pl.ds(pl.multiple_of(spot * 4 * block, 4 * block), 4 * block)
            q_grad[pl.ds(spot * 4, 4), :, :qkv_width] = (
                dot(normed_turned[rows, :], lin_grad[...])
                .astype(BF16)
                .reshape(4, block, qkv_width)
            )
            scatter_q.begin(k)
        weights_in()

        def project(tile):
            rows = pl.ds(tile * ROWS, ROWS)
            for group in range(SLOTS):
                cols = slice(4 * block * group, 4 * block * (group + 1))
                weight = q_full[4 * group : 4 * (group + 1), :, :qkv_width]
                part[rows, cols] = dot(
                    lin_grad[rows, :], weight.reshape(4 * block, qkv_width), NT
                ).astype(BF16)
            copies.remote(
                lambda: (part.at[rows], part_got.at[rows]), ("n", tile), ("n", tile), near.twin,
                last=False,
            )

        project(0)
        project(1)
        for k in (1, 2, 3, 0):
            scatter_q.cross(k)
        project(2)
        project(3)
        copies.arrived(mix_other.at[there], ("mo",), near.over_x)
        copies.remote(lambda: (mix_other.at[there],) * 2, ("m2",), ("m2",), near.twin)
        sum_chunk(2)
        for k in (1, 2, 3, 0):
            scatter_q.plane(k)
        for tile in range(tokens // ROWS):
            rows = pl.ds(tile * ROWS, ROWS)
            copies.arrived(part_got.at[rows], ("n", tile), near.twin)

        def finish_rows(t, side):
            for here in few_rows(STRIP):
                at = pl.ds(pl.multiple_of(t * STRIP + here.start, 16), 16)
                value = strips[0, side, here, :].astype(F32)
                inverse = lax.rsqrt(jnp.mean(value * value, axis=1, keepdims=True) + NORM_EPSILON)
                upstream = part[at, :].astype(F32) + part_got[at, :].astype(F32)
                scaled = value * inverse
                weighted = upstream * small[0:1, :]
                mean_term = jnp.mean(weighted * scaled, axis=1, keepdims=True)
                wide_out[side, here, :] = wide_in[side, here, :] + inverse * (
                    weighted - scaled * mean_term
                )

        over_strips([hidden_hbm], mid_grad, wide_out, input_grad, finish_rows)
        for tile in range(tokens // ROWS):
            rows = pl.ds(tile * ROWS, ROWS)
            copies.sent(lambda: (part.at[rows], part_got.at[rows]), ("n", tile), near.twin)

    pl.run_scoped(
        last_part,
        pltpu.VMEM((width, tokens), BF16), pltpu.VMEM(q_hbm.shape, BF16),
        pltpu.VMEM((tokens, width), BF16),
    )
    copies.arrived(mix_twin, ("mt",), near.twin)
    copies.arrived(mix_other.at[not_there], ("m2",), near.twin)

    def mix_rows(t, side):
        for here in few_rows(STRIP):
            mix = strips[0, side, here, :].astype(F32) + strips[1, side, here, :].astype(F32)
            mix = mix + strips[2, side, here, :].astype(F32)
            strip_out[side, here, :] = (wide_in[side, here, :] + RESIDUAL_SCALE * mix).astype(BF16)

    over_strips([mix_pair, mix_twin, mix_other], middle_hbm, strip_out, block_out, mix_rows)
    load_chunk(3)
    sum_chunk(3)
    scatter_q.end()
    for c in range(2 * SENT):
        copies.arrived(given_got.at[c], ("given", c), near.over_x)
    copies.finish()


def backward_pass(
    o_full, q, k, v, attended, lse, cosine, sine, segments, small, combine, gate_turned,
    q_full, normed, hidden, og, middle, dx, mix, keep, parts, near_grads, far_grads,
):
    tokens, width = hidden.shape
    q_width, kv_width = q.shape[1], k.shape[1]
    block, q_columns = q_full.shape[1:]
    qkv_width = q_width + 2 * kv_width
    pair, columns = keep[0].shape
    chunks = 2 * SENT
    experts = gate_turned.shape[0]
    anywhere, vmem = pl.BlockSpec(memory_space=pl.ANY), vmem_spec()
    shape = jax.ShapeDtypeStruct
    dma = pltpu.SemaphoreType.DMA
    inner = lax.axis_size("dp") // 16

    def scatter_scratch(total):
        split = total // (2 * LANES) * LANES
        return [
            pltpu.VMEM((SLOTS, block, split), BF16),
            pltpu.VMEM((SLOTS, block, total - split), BF16),
            pltpu.VMEM((SLOTS, block, total), BF16),
            pltpu.VMEM((SLOTS, block, total), BF16),
            pltpu.VMEM((SLOTS - 1, block, total), BF16),
        ]

    values = (
        o_full, q, k, v, attended, lse, cosine, sine, segments[:, None], segments[None, :],
        small, combine, gate_turned,
    )
    far_values = (
        q_full, normed, hidden, og, middle, *dx, mix, *keep, *parts, *near_grads, *far_grads,
    )
    return pl.pallas_call(
        functools.partial(backward_kernel, inner),
        in_specs=[vmem] * len(values) + [anywhere] * len(far_values),
        out_specs=[vmem] * 2 + [anywhere] * 12,
        out_shape=[
            shape((block, q_columns), F32),
            shape((block, q_width), F32),
            shape((tokens, width), F32),
            shape((tokens, width), BF16),
            shape((chunks, block, columns), F32),
            shape((chunks, block, columns), BF16),
            shape((tokens, width), F32),
            shape((SLOTS, pair, columns), BF16),
            shape((pair, columns), BF16),
            shape((SLOTS - 1, pair, columns), BF16),
            shape((SLOTS - 1, pair, columns), BF16),
            shape((tokens, width), BF16),
            shape((tokens // 2, width), BF16),
            shape((tokens, width), BF16),
        ],
        scratch_shapes=[
            pltpu.VMEM((tokens, q_width), BF16),
            pltpu.VMEM((tokens, qkv_width), BF16),
            pltpu.VMEM((16, block, q_width), BF16),
            pltpu.VMEM((16, block, q_columns), BF16),
        ]
        + scatter_scratch(q_width)
        + scatter_scratch(q_columns)
        + [
            pltpu.VMEM((tokens, width), BF16),
            pltpu.VMEM((SLOTS, pair, columns), BF16),
            pltpu.VMEM((SLOTS - 1, pair, columns), BF16),
            pltpu.VMEM((2, pair, columns), BF16),
            pltpu.VMEM((chunks, block, columns), BF16),
            pltpu.VMEM((2, block, columns), F32),
            pltpu.VMEM((4, 2, STRIP, width), BF16),
            pltpu.VMEM((2, STRIP, width), F32),
            pltpu.VMEM((2, STRIP, width), F32),
            pltpu.VMEM((2, STRIP, width), BF16),
            pltpu.VMEM((LANES, width), BF16),
            pltpu.VMEM((tokens, LANES), F32),
            pltpu.VMEM((8 + experts, width), F32),
            dma((80,)), dma((80,)), dma((60,)), dma((4, 2)), dma((2,)), dma((2,)),
        ],
        compiler_params=pltpu.CompilerParams(
            vmem_limit_bytes=EXPERT_VMEM, collective_id=2, has_side_effects=True
        ),
        name="backward_pass",
    )(*values, *far_values)


def whole_call(kernel, values, outs, earlier=(), name=None):
    return pl.pallas_call(
        with_earlier(kernel, len(values), len(earlier)),
        in_specs=[vmem_spec()] * len(values) + any_specs(earlier),
        out_specs=[vmem_spec()] * len(outs),
        out_shape=[jax.ShapeDtypeStruct(shape, dtype) for shape, dtype in outs],
        compiler_params=pltpu.CompilerParams(vmem_limit_bytes=VMEM_BYTES),
        name=name,
    )(*values, *earlier)


def fence_kernel(*refs):
    count = len(refs) // 2
    for value, out in zip(refs[:count], refs[count:]):
        out[...] = value[...]


def fence_all(values, *earlier):
    return whole_call(fence_kernel, values, [(v.shape, v.dtype) for v in values], earlier, "fence")


def fence(value, *earlier):
    return fence_all([value], *earlier)[0]


def sum_y_kernel(near, got, *outs):
    for k, out in enumerate(outs):
        out[...] = (near[k].astype(F32) + got[k].astype(F32)).astype(BF16)


def sum_y(near, got, *earlier):
    outs = [(near.shape[1:], BF16)] * SLOTS
    return whole_call(sum_y_kernel, [near, got], outs, earlier, "sum_y")


def sum_z_kernel(x_at, *refs):
    kept, given = refs[-2:]
    half = kept.shape[1]
    for c in range(kept.shape[0]):
        parts = refs[SLOTS * c : SLOTS * (c + 1)]
        for rows, out in ((x_at[0], kept), (1 - x_at[0], given)):
            rows = pl.ds(pl.multiple_of(rows * half, half), half)
            total = parts[0][rows, :].astype(F32)
            for part in parts[1:]:
                total = total + part[rows, :].astype(F32)
            out[c] = total.astype(out.dtype)


def sum_z(x_at, chunks, *earlier):
    count = len(chunks)
    pair, columns = chunks[0][0].shape
    flat = [part for parts in chunks for part in parts]
    return pl.pallas_call(
        with_earlier(sum_z_kernel, 1 + len(flat), len(earlier)),
        in_specs=[smem_spec()] + [vmem_spec()] * len(flat) + any_specs(earlier),
        out_specs=[vmem_spec()] * 2,
        out_shape=[
            jax.ShapeDtypeStruct((count, pair // 2, columns), F32),
            jax.ShapeDtypeStruct((count, pair // 2, columns), BF16),
        ],
        compiler_params=pltpu.CompilerParams(vmem_limit_bytes=VMEM_BYTES),
        name="sum_z",
    )(x_at, *flat, *earlier)


def sum_parts_kernel(parts, out):
    total = parts[0].astype(F32)
    for c in range(1, parts.shape[0]):
        total = total + parts[c].astype(F32)
    out[...] = total.astype(BF16)


def sum_parts(parts, *earlier):
    chunks, tokens, width = parts.shape
    return pl.pallas_call(
        with_earlier(sum_parts_kernel, 1, len(earlier)),
        grid=(tokens // EXPERT_ROWS,),
        in_specs=[pl.BlockSpec((chunks, EXPERT_ROWS, width), lambda s: (0, s, 0))]
        + any_specs(earlier),
        out_specs=pl.BlockSpec((EXPERT_ROWS, width), lambda s: (s, 0)),
        out_shape=jax.ShapeDtypeStruct((tokens, width), BF16),
        compiler_params=pltpu.CompilerParams(vmem_limit_bytes=VMEM_BYTES),
        name="sum_parts",
    )(parts, *earlier)


def adam_experts_kernel(x_at, kept, got, *refs):
    states, outs = refs[:6], refs[6:]
    own = kept.shape[1]
    hidden = states[0].shape[3]
    mine = pl.program_id(0) // (pl.num_programs(0) // 2) == x_at[0]
    grad = jnp.where(mine, kept[0], got[0].astype(F32))
    for e in range(CHUNK):
        for part in range(2):
            first = hidden * (2 * e + part)
            results = adam_update(
                states[0][e, part], grad[:, first : first + hidden],
                states[1][e, part], states[2][e, part], MODEL_DIM ** (-0.5), WEIGHT_DECAY,
            )
            for out, result in zip(outs[:3], results):
                out[e, part] = result
        first = hidden * (2 * CHUNK + e)
        results = adam_update(
            states[3][e], grad[:, first : first + hidden], states[4][e], states[5][e],
            max(1, F // 256) ** (-0.5), WEIGHT_DECAY,
        )
        for out, result in zip(outs[3:], results):
            out[e] = result


def adam_experts(x_at, kept, got, gateup, down):
    chunks, own, columns = kept.shape
    experts, hidden = down[0].shape[0], down[0].shape[2]
    share = pl.BlockSpec((1, own, columns), lambda j: (j % chunks, 0, 0))
    big = pl.BlockSpec((CHUNK, 2, own, hidden), lambda j: (j, 0, 0, 0))
    small = pl.BlockSpec((CHUNK, own, hidden), lambda j: (j, 0, 0))
    return pl.pallas_call(
        adam_experts_kernel,
        grid=(experts // CHUNK,),
        in_specs=[smem_spec(), share, share] + [big] * 3 + [small] * 3,
        out_specs=[big] * 3 + [small] * 3,
        out_shape=[jax.ShapeDtypeStruct(gateup[0].shape, F32)] * 3
        + [jax.ShapeDtypeStruct(down[0].shape, F32)] * 3,
        compiler_params=pltpu.CompilerParams(vmem_limit_bytes=VMEM_BYTES),
        name="adam_experts",
    )(x_at, kept, got, *gateup, *down)


def join_tokens_kernel(own, first, second, out, turned):
    half = own.shape[0] // 2
    for at, part in ((0, own[:half, :]), (half, own[half:, :]), (2 * half, first[...]), (3 * half, second[...])):
        out[at : at + half, :] = part
        turned[:, at : at + half] = part.T


def join_tokens(own, first, second, *earlier):
    tokens, width = own.shape
    return pl.pallas_call(
        with_earlier(join_tokens_kernel, 3, len(earlier)),
        in_specs=[vmem_spec()] * 3 + any_specs(earlier),
        out_specs=[vmem_spec()] * 2,
        out_shape=[
            jax.ShapeDtypeStruct((2 * tokens, width), own.dtype),
            jax.ShapeDtypeStruct((width, 2 * tokens), own.dtype),
        ],
        compiler_params=pltpu.CompilerParams(vmem_limit_bytes=VMEM_BYTES),
        name="join_tokens",
    )(own, first, second, *earlier)


def move(array, dz=0, dy=0, dx=0):
    total = lax.axis_size("dp")
    inner = total // 16
    pairs = []
    for at in range(16):
        z, y, x = at // 4, at // 2 % 2, at % 2
        to = ((z + dz) % 4) * 4 + (y ^ dy) * 2 + (x ^ dx)
        pairs += [(at * inner + i, to * inner + i) for i in range(inner)]
    return lax.ppermute(array, "dp", pairs)


def place():
    at = lax.axis_index("dp") // (lax.axis_size("dp") // 16)
    return at // 4, at // 2 % 2, at % 2


def inner_groups(total):
    inner = total // 16
    return [[at * inner + i for i in range(inner)] for at in range(16)]


def inner_gather(shard, axis):
    total = lax.axis_size("dp")
    if total == 16:
        return shard
    return lax.all_gather(
        shard, "dp", axis=axis, tiled=True, axis_index_groups=inner_groups(total)
    )


def inner_scatter(share, axis):
    total = lax.axis_size("dp")
    if total == 16:
        return share
    return lax.psum_scatter(
        share, "dp", scatter_dimension=axis, tiled=True, axis_index_groups=inner_groups(total)
    )


def block_rows(parts, rows):
    z, y, x = place()
    starts = []
    for dz, dy, dx in parts:
        starts.append((((z + dz + 4) % 4) * 4 + (y ^ dy) * 2 + (x ^ dx)) * rows)
    return jnp.stack(starts).astype(jnp.int32)


def gather_z(shard):
    return jnp.stack([shard] + [move(shard, dz=-dz) for dz in Z_FROM[1:]])


def gather_ring(shard):
    below, above = move(shard, dz=1), move(shard, dz=-1)
    return [shard, below, above, move(below, dz=1)]


def send_z(parts):
    return [move(parts[k].astype(BF16), dz=Z_FROM[k]) for k in range(1, SLOTS)]


def scatter_z(parts, moved=None):
    result = parts[0]
    for one in moved or send_z(parts):
        result = result + one.astype(F32)
    return result


def gather_plane(own):
    half = own.shape[-1] // 2
    along_y, along_x = move(own, dy=1), move(own, dx=1)
    both = (move(along_y[..., :half], dx=1), move(along_x[..., half:], dy=1))
    return own, along_y, along_x, *both


def scatter_plane(pieces):
    own, along_y, along_x, both_one, both_two = pieces
    half = both_one.shape[-1]
    got_one, got_two = move(both_one, dx=1), move(both_two, dy=1)
    pass_y = jnp.concatenate(
        [(along_y[..., :half].astype(F32) + got_one.astype(F32)).astype(BF16), along_y[..., half:]],
        axis=-1,
    )
    pass_x = jnp.concatenate(
        [along_x[..., :half], (along_x[..., half:].astype(F32) + got_two.astype(F32)).astype(BF16)],
        axis=-1,
    )
    got_y, got_x = move(pass_y, dy=1), move(pass_x, dx=1)
    return scatter_z(
        [
            own[k].astype(F32) + got_y[k].astype(F32) + got_x[k].astype(F32)
            for k in range(SLOTS)
        ]
    )


PLANE = [(dz, dy, dx) for dy, dx in ((0, 0), (1, 0), (0, 1), (1, 1)) for dz in Z_FROM]


def join_kernel(rows_at, *refs):
    pieces, out = refs[:-1], refs[-1]
    slots, own, width = pieces[0].shape
    half = width // 2
    for at in range(4 * slots):
        rows = pl.ds(pl.multiple_of(rows_at[at], own), own)
        group, slot = at // slots, at % slots
        if group < 3:
            out[rows, :] = pieces[group][slot]
        else:
            out[rows, :half] = pieces[3][slot]
            out[rows, half:] = pieces[4][slot]


def part_kernel(rows_at, whole, *pieces):
    slots, own, width = pieces[0].shape
    half = width // 2
    for at in range(4 * slots):
        rows = pl.ds(pl.multiple_of(rows_at[at], own), own)
        group, slot = at // slots, at % slots
        if group < 3:
            pieces[group][slot] = whole[rows, :]
        else:
            pieces[3][slot] = whole[rows, :half]
            pieces[4][slot] = whole[rows, half:]


def smem_spec():
    return pl.BlockSpec(memory_space=pltpu.SMEM)


def vmem_spec():
    return pl.BlockSpec(memory_space=pltpu.VMEM)


def join_blocks(rows_at, pieces, earlier=()):
    slots, own, width = pieces[0].shape
    return pl.pallas_call(
        with_earlier(join_kernel, 6, len(earlier)),
        in_specs=[smem_spec()] + [vmem_spec()] * 5 + any_specs(earlier),
        out_specs=vmem_spec(),
        out_shape=jax.ShapeDtypeStruct((4 * slots * own, width), BF16),
        compiler_params=pltpu.CompilerParams(vmem_limit_bytes=VMEM_BYTES),
        name="join_blocks",
    )(rows_at, *pieces, *earlier)


def part_blocks(rows_at, whole, earlier=()):
    own, width = whole.shape[0] // (4 * SLOTS), whole.shape[1]
    full = jax.ShapeDtypeStruct((SLOTS, own, width), BF16)
    half = jax.ShapeDtypeStruct((SLOTS, own, width // 2), BF16)
    return pl.pallas_call(
        with_earlier(part_kernel, 2, len(earlier)),
        in_specs=[smem_spec(), vmem_spec()] + any_specs(earlier),
        out_specs=[vmem_spec()] * 5,
        out_shape=[full] * 3 + [half] * 2,
        compiler_params=pltpu.CompilerParams(vmem_limit_bytes=VMEM_BYTES),
        name="part_blocks",
    )(rows_at, whole, *earlier)


def after(value, *earlier):
    marks = []
    for one in earlier:
        slots = one.shape[0] if one.shape[0] == SLOTS else 1
        lead, rest = (slots > 1) * 1, one.ndim - 1
        marks.append(lax.slice(one, (lead,) + (0,) * rest, (slots,) + (1,) * rest))
    return lax.optimization_barrier((value, *marks))[0]


def split_three(values):
    high = values.astype(BF16)
    rest = values - high.astype(F32)
    middle = rest.astype(BF16)
    low = (rest - middle.astype(F32)).astype(BF16)
    return [high, middle, low]


def swap_cores(part):
    return lax.ppermute(part, "tensor", [(0, 1), (1, 0)])


def pair_sum(part):
    return part.astype(F32) + swap_cores(part).astype(F32)


def norm_backward(values, inverse, gain_row, upstream):
    scaled = values * inverse
    weighted = upstream * gain_row
    mean_term = jnp.mean(weighted * scaled, axis=-1, keepdims=True)
    return (inverse * (weighted - scaled * mean_term), jnp.sum(upstream * scaled, axis=0))


def adam_update(value, gradient, mean_old, square_old, rate, decay):
    mean_new = FIRST_DECAY * mean_old + (1.0 - FIRST_DECAY) * gradient
    square_new = SECOND_DECAY * square_old + (1.0 - SECOND_DECAY) * gradient * gradient
    mean_hat = mean_new / (1.0 - FIRST_DECAY**STEP)
    square_hat = square_new / (1.0 - SECOND_DECAY**STEP)
    updated = value - rate * (mean_hat / (jnp.sqrt(square_hat) + ADAM_EPSILON) + decay * value)
    return (mean_new, square_new, updated)


def shards(
    hidden_in,
    out_grad,
    routes,
    segments,
    norm_gains,
    gains_mean,
    gains_square,
    w_query,
    query_mean,
    query_square,
    key_value_weight,
    key_value_first_moment,
    key_value_second_moment,
    w_out,
    out_mean,
    out_square,
    w_router,
    router_mean,
    router_square,
    w_gateup,
    gateup_mean,
    gateup_square,
    w_down,
    down_mean,
    down_square,
):
    tokens, width = hidden_in.shape
    own = w_query.shape[0]
    experts, hidden = w_down.shape[0], w_down.shape[1]
    q_width, kv_width = w_query.shape[1], key_value_weight.shape[2]
    qkv_width = q_width + 2 * kv_width
    each = 2 + experts
    half_experts = experts // 2
    block = width // 16
    z_at, y_at, x_at = place()
    core = lax.axis_index("tensor")
    plane_rows = block_rows(PLANE, block)
    qkv_shard = jnp.concatenate(
        [w_query.astype(BF16), key_value_weight[0].astype(BF16), key_value_weight[1].astype(BF16)]
        + split_three(jnp.concatenate([norm_gains.T, w_router], axis=1))
        + [jnp.zeros((own, LANES - 3 * each), BF16)],
        axis=1,
    )
    out_shard = w_out.T.astype(BF16)
    turned_down = [one.transpose(0, 2, 1) for one in (w_down, down_mean, down_square)]
    gateup_rows, down_rows = w_gateup, turned_down[0]
    if lax.axis_size("dp") > 16:
        gateup_rows = inner_gather(w_gateup.astype(BF16), 2)
        down_rows = inner_gather(down_rows.astype(BF16), 1)
    chunks = experts // (2 * CHUNK)
    first = x_at == 0
    cosine, sine = rope_tables(seq_positions(segments))
    (
        qkv_blocks, out_blocks, small, normed_low, queries, keys, values, attended, lse,
        combine, combine_pair, middle, x_pair, x_turned, og_pair, og_turned, pairs, near, far,
    ) = forward_pass(
        inner_gather(qkv_shard, 0), inner_gather(out_shard, 0), gateup_rows, down_rows,
        hidden_in, out_grad, cosine, sine, segments, routes,
    )
    dx, mix_pair, gate_turned, keep, z_got, near_grads, far_grads = experts_pass(
        x_pair, og_pair, x_turned, og_turned, combine_pair, pairs, near, far
    )
    qkv_share, output_share, input_grad, block_out, kept_share, got_share = backward_pass(
        out_blocks, queries, keys, values, attended, lse, cosine, sine, segments, small, combine,
        gate_turned, qkv_blocks, normed_low, hidden_in, out_grad, middle, dx, mix_pair, keep,
        z_got, near_grads, far_grads,
    )[:6]
    kept_share, got_share = inner_scatter(kept_share, 1), inner_scatter(got_share, 1)
    x_here = x_at.astype(jnp.int32)[None]
    output_share = inner_scatter(output_share, 0).T
    qkv_share = inner_scatter(qkv_share, 0)
    query_share = qkv_share[:, :q_width]
    keyval_share = jnp.stack(
        [qkv_share[:, q_width : q_width + kv_width], qkv_share[:, q_width + kv_width : qkv_width]]
    )
    gain_one_part = jnp.sum(w_query.astype(BF16).astype(F32) * query_share, axis=1) + jnp.sum(
        key_value_weight.astype(BF16).astype(F32) * keyval_share, axis=(0, 2)
    )
    gain_one_share = pair_sum(gain_one_part[None, :]) / norm_gains[:1]
    gains_share = jnp.concatenate([gain_one_share, qkv_share[:, qkv_width][None, :]])
    router_share = qkv_share[:, qkv_width + 1 : qkv_width + 1 + experts]

    gains_result = adam_update(norm_gains, gains_share, gains_mean, gains_square, GAIN_RATE, 0.0)
    query_result = adam_update(
        w_query, query_share, query_mean, query_square, (MODEL_DIM // 12) ** (-0.5), WEIGHT_DECAY
    )
    keyval_result = adam_update(
        key_value_weight,
        keyval_share,
        key_value_first_moment,
        key_value_second_moment,
        (MODEL_DIM // 12) ** (-0.5),
        WEIGHT_DECAY,
    )
    out_result = adam_update(
        w_out,
        output_share,
        out_mean,
        out_square,
        max(1, QUERY_HEADS * HEAD_DIM // 96) ** (-0.5),
        WEIGHT_DECAY,
    )
    router_result = adam_update(
        w_router, router_share, router_mean, router_square, (4 * MODEL_DIM) ** (-0.5), WEIGHT_DECAY
    )
    expert_results = adam_experts(
        x_here, kept_share, got_share,
        (w_gateup, gateup_mean, gateup_square), turned_down,
    )
    expert_results = [*expert_results[:3], *(one.transpose(0, 2, 1) for one in expert_results[3:])]
    return (
        (block_out, input_grad)
        + gains_result
        + query_result
        + keyval_result
        + out_result
        + router_result
        + tuple(expert_results)
    )


def solution(mesh):
    tokens, gains = P("dp", None), P(None, "dp")
    query, keyval, out = P("dp", "tensor"), P(None, "dp", "tensor"), P("tensor", "dp")
    router, gateup, down = P("dp", None), P(None, None, "dp", "tensor"), P(None, "tensor", "dp")
    states = tuple(
        spec for one in (gains, query, keyval, out, router, gateup, down) for spec in (one,) * 3
    )
    return jax.shard_map(
        shards,
        mesh=mesh,
        in_specs=(tokens, tokens, tokens, P("dp")) + states,
        out_specs=(tokens, tokens) + states,
        check_vma=False,
    )
```

```python
import functools

import jax
import jax.numpy as jnp
from jax import lax
from jax.experimental import pallas as pl
from jax.experimental.pallas import tpu as pltpu
from jax.sharding import PartitionSpec as P

MODEL_DIM = 1536
QUERY_HEADS = 24
HEAD_DIM = 64
F = 512
SEQUENCE_LENGTH = 1024
STEP = 10

NORM_EPSILON = 1e-06
SCORE_SCALE = 0.015625
RESIDUAL_SCALE = 0.22
ROPE_BASE = 10000.0
FIRST_DECAY = 0.9
SECOND_DECAY = 0.95
ADAM_EPSILON = 1e-08
WEIGHT_DECAY = 0.1
GAIN_RATE = 0.6
MASK_VALUE = -1e30
HIGHEST_PRECISION = lax.Precision.HIGHEST

BF16 = jnp.bfloat16
F32 = jnp.float32
LANES = 128
ROWS = 256
VMEM_BYTES = 58 * 1024 * 1024

NN = (((1,), (0,)), ((), ()))
NT = (((1,), (1,)), ((), ()))
TN = (((0,), (0,)), ((), ()))


def dot(a, b, dims=NN):
    return lax.dot_general(a, b, dims, preferred_element_type=F32)


def seq_positions(segment_row):
    counter = jnp.arange(segment_row.shape[0], dtype=jnp.int32)
    earlier = jnp.concatenate([segment_row[:1] - 1, segment_row[:-1]])
    starts = lax.cummax(jnp.where(segment_row != earlier, counter, 0), axis=0)
    return counter - starts


def rope_tables(positions):
    half_width = HEAD_DIM // 2
    frequency = ROPE_BASE ** (-2.0 * jnp.arange(half_width, dtype=F32) / HEAD_DIM)
    angles = positions.astype(F32)[:, None] * frequency[None, :]
    cosine, sine = jnp.cos(angles), jnp.sin(angles)
    return (
        jnp.concatenate([cosine] * 4, axis=1),
        jnp.concatenate([-sine, sine] * 2, axis=1),
    )


def rotate_halves(slab):
    lane = lax.broadcasted_iota(jnp.int32, slab.shape, 1)
    ahead = pltpu.roll(slab, LANES - HEAD_DIM // 2, 1)
    behind = pltpu.roll(slab, HEAD_DIM // 2, 1)
    return jnp.where(lane % HEAD_DIM < HEAD_DIM // 2, ahead, behind)


def few_rows(count, base=None):
    for r in range(0, count, 16):
        yield pl.ds(r, 16) if base is None else pl.ds(pl.multiple_of(base + r, 16), 16)


def half_mask(rows, upper):
    lane = lax.broadcasted_iota(jnp.int32, (rows, LANES), 1)
    return (lane >= HEAD_DIM) if upper else (lane < HEAD_DIM)


def spread_heads(slab, lower_out, upper_out, index):
    rows = slab.shape[0]
    moved = pltpu.roll(slab.astype(F32), HEAD_DIM, 1).astype(BF16)
    zero = jnp.zeros_like(slab)
    low, high = half_mask(rows, False), half_mask(rows, True)
    lower_out[index] = jnp.where(low, slab, zero)
    upper_out[index] = jnp.where(high, moved, zero)
    lower_out[index + 1] = jnp.where(low, moved, zero)
    upper_out[index + 1] = jnp.where(high, slab, zero)


def fill_bias(bias, seg_col, seg_row):
    span = bias.shape[0]
    for at in range(0, span, ROWS):
        rows_at = at + lax.broadcasted_iota(jnp.int32, (ROWS, span), 0)
        cols_at = lax.broadcasted_iota(jnp.int32, (ROWS, span), 1)
        allowed = (rows_at >= cols_at) & (seg_col[at : at + ROWS, :] == seg_row[...])
        bias[at : at + ROWS, :] = jnp.where(allowed, 0.0, MASK_VALUE).astype(F32)


def with_earlier(kernel, inputs, count):
    def run(*refs):
        kernel(*refs[:inputs], *refs[inputs + count :])

    return run


def any_specs(arrays):
    return [pl.BlockSpec(memory_space=pl.ANY)] * len(arrays)


def attention_forward_kernel(
    lin_ref, kv_ref, cos_ref, sin_ref, seg_col, seg_row,
    out_ref, q_ref, k_ref, v_ref, lse_ref,
    bias, k_low, k_high, v_low, v_high,
):
    slab_at = pl.program_id(0)
    span = lin_ref.shape[0]
    kv_slabs = kv_ref.shape[1] // (2 * LANES)

    @pl.when(slab_at == 0)
    def _():
        fill_bias(bias, seg_col, seg_row)
        for j in range(kv_slabs):
            lanes = slice(j * LANES, (j + 1) * LANES)
            lin = kv_ref[:, lanes]
            keys = (lin * cos_ref[...] + rotate_halves(lin) * sin_ref[...]).astype(BF16)
            k_ref[:, lanes] = keys
            spread_heads(keys, k_low, k_high, 2 * j)
            lanes = slice((kv_slabs + j) * LANES, (kv_slabs + j + 1) * LANES)
            values = kv_ref[:, lanes].astype(BF16)
            v_ref[:, slice(j * LANES, (j + 1) * LANES)] = values
            spread_heads(values, v_low, v_high, 2 * j)

    lin = lin_ref[...]
    q_ref[...] = (lin * cos_ref[...] + rotate_halves(lin) * sin_ref[...]).astype(BF16)
    kv_even, kv_odd = (2 * slab_at) // 3, (2 * slab_at + 1) // 3
    for at in range(0, span, ROWS):
        rows = slice(at, at + ROWS)
        queries = q_ref[rows, :]
        total = None
        stats = []
        for keys, values, kv_at in ((k_low, v_low, kv_even), (k_high, v_high, kv_odd)):
            upto = at + ROWS
            scores = dot(queries, keys[kv_at, :upto, :], NT) * SCORE_SCALE + bias[rows, :upto]
            highest = jnp.max(scores, axis=1, keepdims=True)
            weights = jnp.exp(scores - highest)
            summed = jnp.sum(weights, axis=1, keepdims=True)
            probability = (weights * (1.0 / summed)).astype(BF16)
            part = dot(probability, values[kv_at, :upto, :])
            total = part if total is None else total + part
            stats.append(highest + jnp.log(summed))
        out_ref[rows, :] = total.astype(BF16)
        spread = jnp.where(half_mask(ROWS, False), stats[0], stats[1])
        turned = spread.T
        lse_ref[0, 0:1, rows] = turned[0:1, :]
        lse_ref[0, 1:2, rows] = turned[HEAD_DIM : HEAD_DIM + 1, :]


def attention_forward(qkv_lin, cosine, sine, segment_row, earlier=()):
    span = qkv_lin.shape[0]
    q_width = MODEL_DIM // 2
    kv_width = (qkv_lin.shape[1] - q_width) // 2
    slabs, kv_heads = q_width // LANES, kv_width // HEAD_DIM
    whole = lambda shape: pl.BlockSpec(shape, lambda g: (0,) * len(shape))
    slab = pl.BlockSpec((span, LANES), lambda g: (0, g))
    q_lin, kv_lin = qkv_lin[:, :q_width], qkv_lin[:, q_width:]
    return pl.pallas_call(
        with_earlier(attention_forward_kernel, 6, len(earlier)),
        grid=(slabs,),
        in_specs=[
            slab, whole((span, 2 * kv_width)), whole((span, LANES)), whole((span, LANES)),
            whole((span, 1)), whole((1, span)),
        ]
        + any_specs(earlier),
        out_specs=[
            slab, slab, whole((span, kv_width)), whole((span, kv_width)),
            pl.BlockSpec((1, 8, span), lambda g: (g, 0, 0)),
        ],
        out_shape=[
            jax.ShapeDtypeStruct((span, q_width), BF16),
            jax.ShapeDtypeStruct((span, q_width), BF16),
            jax.ShapeDtypeStruct((span, kv_width), BF16),
            jax.ShapeDtypeStruct((span, kv_width), BF16),
            jax.ShapeDtypeStruct((slabs, 8, span), F32),
        ],
        scratch_shapes=[pltpu.VMEM((span, span), F32)]
        + [pltpu.VMEM((kv_heads, span, LANES), BF16)] * 4,
        compiler_params=pltpu.CompilerParams(vmem_limit_bytes=VMEM_BYTES),
        cost_estimate=pl.CostEstimate(
            flops=32 * slabs * span * span * LANES, bytes_accessed=16 * span * q_width,
            transcendentals=slabs * span * span,
        ),
        name="attention_forward",
    )(q_lin, kv_lin, cosine, sine, segment_row[:, None], segment_row[None, :], *earlier)


def attention_backward_kernel(
    q_ref, k_ref, v_ref, out_ref, grad_ref, cos_ref, sin_ref, seg_col, seg_row, lse_ref,
    dq_ref, dkv_ref,
    bias, k_low, k_high, v_low, v_high, dk_low, dk_high, dv_low, dv_high, dq_sum,
):
    slab_at = pl.program_id(0)
    span = q_ref.shape[0]
    kv_slabs = k_ref.shape[1] // LANES

    @pl.when(slab_at == 0)
    def _():
        for at in range(0, span, ROWS):
            keys_at = at + lax.broadcasted_iota(jnp.int32, (ROWS, span), 0)
            rows_at = lax.broadcasted_iota(jnp.int32, (ROWS, span), 1)
            allowed = (rows_at >= keys_at) & (seg_col[at : at + ROWS, :] == seg_row[...])
            bias[at : at + ROWS, :] = jnp.where(allowed, 0.0, MASK_VALUE).astype(F32)
        for j in range(kv_slabs):
            lanes = slice(j * LANES, (j + 1) * LANES)
            spread_heads(k_ref[:, lanes], k_low, k_high, 2 * j)
            spread_heads(v_ref[:, lanes], v_low, v_high, 2 * j)
        for sums in (dk_low, dk_high, dv_low, dv_high):
            sums[...] = jnp.zeros_like(sums)

    kv_even, kv_odd = (2 * slab_at) // 3, (2 * slab_at + 1) // 3
    for at in range(0, span, ROWS):
        rows = slice(at, at + ROWS)
        upto = at + ROWS
        queries, grads = q_ref[rows, :], grad_ref[rows, :]
        turned = (grads.astype(F32) * out_ref[rows, :].astype(F32)).T
        zero = jnp.zeros_like(queries)
        dq_part = None
        for upper, keys, values, dk_sum, dv_sum, kv_at in (
            (False, k_low, v_low, dk_low, dv_low, kv_even),
            (True, k_high, v_high, dk_high, dv_high, kv_odd),
        ):
            first = HEAD_DIM if upper else 0
            delta = jnp.sum(turned[first : first + HEAD_DIM, :], axis=0, keepdims=True)
            head = 1 if upper else 0
            total = lse_ref[0, head : head + 1, rows]
            keys_here = keys[kv_at, :upto, :]
            scores = dot(keys_here, queries, NT) * SCORE_SCALE + bias[:upto, rows]
            probability = jnp.exp(scores - total)
            prob_grad = dot(values[kv_at, :upto, :], grads, NT)
            score_grad = (probability * (prob_grad - delta)).astype(BF16)
            mask = half_mask(ROWS, upper)
            dv_sum[kv_at, :upto, :] += dot(
                probability.astype(BF16), jnp.where(mask, grads, zero)
            )
            dk_sum[kv_at, :upto, :] += dot(score_grad, jnp.where(mask, queries, zero))
            part = dot(score_grad, keys_here, TN)
            dq_part = part if dq_part is None else dq_part + part
        dq_sum[rows, :] = dq_part * SCORE_SCALE
    slab = dq_sum[...]
    dq_ref[...] = (slab * cos_ref[...] - rotate_halves(slab) * sin_ref[...]).astype(BF16)

    @pl.when(slab_at == pl.num_programs(0) - 1)
    def _():
        low = half_mask(span, False)

        def joined(sums_low, sums_high, j):
            one = sums_low[2 * j] + pltpu.roll(sums_high[2 * j], HEAD_DIM, 1)
            two = pltpu.roll(sums_low[2 * j + 1], HEAD_DIM, 1) + sums_high[2 * j + 1]
            return jnp.where(low, one, two)

        for j in range(kv_slabs):
            slab = joined(dk_low, dk_high, j) * SCORE_SCALE
            dkv_ref[:, j * LANES : (j + 1) * LANES] = (
                slab * cos_ref[...] - rotate_halves(slab) * sin_ref[...]
            ).astype(BF16)
            at = (kv_slabs + j) * LANES
            dkv_ref[:, at : at + LANES] = joined(dv_low, dv_high, j).astype(BF16)


def attention_backward(
    queries, keys, values, attended, grad, cosine, sine, segment_row, lse, earlier=()
):
    span, q_width = queries.shape
    kv_width = keys.shape[1]
    slabs, kv_heads = q_width // LANES, kv_width // HEAD_DIM
    whole = lambda shape: pl.BlockSpec(shape, lambda g: (0,) * len(shape))
    slab = pl.BlockSpec((span, LANES), lambda g: (0, g))
    return pl.pallas_call(
        with_earlier(attention_backward_kernel, 10, len(earlier)),
        grid=(slabs,),
        in_specs=[
            slab, whole((span, kv_width)), whole((span, kv_width)), slab, slab,
            whole((span, LANES)), whole((span, LANES)), whole((span, 1)), whole((1, span)),
            pl.BlockSpec((1, 8, span), lambda g: (g, 0, 0)),
        ]
        + any_specs(earlier),
        out_specs=[slab, whole((span, 2 * kv_width))],
        out_shape=[
            jax.ShapeDtypeStruct((span, q_width), BF16),
            jax.ShapeDtypeStruct((span, 2 * kv_width), BF16),
        ],
        scratch_shapes=[pltpu.VMEM((span, span), F32)]
        + [pltpu.VMEM((kv_heads, span, LANES), BF16)] * 4
        + [pltpu.VMEM((kv_heads, span, LANES), F32)] * 4
        + [pltpu.VMEM((span, LANES), F32)],
        compiler_params=pltpu.CompilerParams(vmem_limit_bytes=VMEM_BYTES),
        cost_estimate=pl.CostEstimate(
            flops=40 * slabs * span * span * LANES, bytes_accessed=16 * span * q_width,
            transcendentals=slabs * span * span,
        ),
        name="attention_backward",
    )(
        queries, keys, values, attended, grad, cosine, sine,
        segment_row[:, None], segment_row[None, :], lse, *earlier,
    )


EXPERT_ROWS = 256
EXPERT_VMEM = 63 * 1024 * 1024
SLOTS = 4
Z_FROM = (0, -1, 1, 2)
CHUNK = 2
LATE = 2
SENT = 2
MESH_ID = pl.DeviceIdType.MESH


def experts_kernel(
    inner, chunks, row_steps, x_ref, og_ref, xt_ref, ogt_ref, combine_ref,
    pairs_ref, near_ref, far_ref,
    dx_own, dx_twin, dx_other, mix_out, gate_out, *refs,
):
    keep_outs, refs = refs[:SENT], refs[SENT:]
    part_outs, refs = refs[:SENT], refs[SENT:]
    near_outs, refs = refs[: chunks - SENT], refs[chunks - SENT :]
    late_out, first_out, far_out, refs = *refs[:3], refs[3:]
    slots, arrived, held_both, held_down, dx_sum, mix_sum, twin_rows, twin_mix = refs[:8]
    gates, gate_kept, gate_got, gate_full, gate_twin, send, recv, local = refs[8:]
    weights, grads = slots.at[pl.ds(1, chunks)], slots
    near = Neighbours(inner)
    copies = Copies(send, recv, local)
    z, y, x, core, spots = near.z, near.y, near.x, near.core, near.spots
    step = pl.program_id(0)
    steps = row_steps + SLOTS
    chunk, turn = step // steps, step % steps
    last = chunks - 1
    width = x_ref.shape[1]
    block = width // 16
    hidden = held_down.shape[1] // CHUNK
    both = 2 * hidden * CHUNK
    lane = lax.broadcasted_iota(jnp.int32, (EXPERT_ROWS, LANES), 1)
    tokens = dx_sum.shape[0] // 2
    tiles = tokens // EXPERT_ROWS
    tile = (turn + tiles) % row_steps
    rows = pl.ds(pl.multiple_of(tile * EXPERT_ROWS, EXPERT_ROWS), EXPERT_ROWS)

    def near_piece(c, k):
        return pairs_ref.at[c] if k == 0 else near_ref.at[c, k - 1]

    def near_copy(c, k):
        copies.copy(
            lambda c=c, k=k: (near_piece(c, k), weights.at[c, spots[k], y]), ("near", c, k), False
        )

    def near_wait(c, k):
        copies.wait_copy(
            lambda c=c, k=k: (near_piece(c, k), weights.at[c, spots[k], y]), ("near", c, k)
        )

    def far_ends(c, k):
        return far_ref.at[c, k], weights.at[c, spots[k], 1 - y]

    @pl.when(step == 0)
    def _():
        near.greet()
        gates[...] = jnp.zeros_like(gates)
        for k in range(SLOTS):
            near_copy(0, k)
            copies.copy(lambda k=k: far_ends(0, k), ("far", 0, k), False)
        copies.remote(
            lambda: (pairs_ref.at[last], weights.at[last, z, y]), ("y",), ("y",), near.over_y
        )
        for k in range(1, SLOTS):
            copies.remote(
                lambda: (pairs_ref.at[last], weights.at[last, z, y]),
                ("z", k), ("z", BACK[k]), near.along[k],
            )
        for c in range(LATE, last):
            for k in range(1, SLOTS):
                copies.remote(
                    lambda c=c, k=k: (near_piece(c, k), weights.at[c, spots[k], y]),
                    ("f", c, k), ("f", c, k), near.over_y,
                )
        for c in range(1, chunks):
            for k in range(SLOTS if c < last else 1):
                near_copy(c, k)
                if c < LATE or (c < last and k == 0):
                    copies.copy(lambda c=c, k=k: far_ends(c, k), ("far", c, k), False)

    @pl.when(step == steps)
    def _():
        copies.arrived(weights.at[last, z, 1 - y], ("y",), near.over_y)
        for k in range(1, SLOTS):
            copies.remote(
                lambda: (weights.at[last, z, 1 - y],) * 2,
                ("z2", k), ("z2", BACK[k]), near.along[k],
            )

    for c in range(chunks):

        @pl.when(step == c * steps)
        def _():
            for k in range(SLOTS):
                if c < last or k == 0:
                    near_wait(c, k)
                if c < LATE or (c < last and k == 0):
                    copies.wait_copy(lambda c=c, k=k: far_ends(c, k), ("far", c, k))
                elif c < last:
                    copies.arrived(weights.at[c, spots[k], 1 - y], ("f", c, k), near.over_y)
                elif k > 0:
                    copies.arrived(weights.at[c, spots[k], y], ("z", k), near.along[k])
                    copies.arrived(weights.at[c, spots[k], 1 - y], ("z2", k), near.along[k])

    def add_arrived(c):
        copies.arrived(arrived.at[c], ("sum", c), near.over_y)
        for k in range(SLOTS):
            own = grads.at[c, spots[k], y]
            for here in few_rows(own.shape[0]):
                own[here, :] = (
                    own[here, :].astype(F32) + arrived[c, spots[k], here, :].astype(F32)
                ).astype(BF16)
        copies.copy(lambda c=c: (grads.at[c, z, y], keep_outs[c]), ("keep", c))
        for k in range(1, SLOTS):
            copies.remote(
                lambda c=c, k=k: (grads.at[c, spots[k], y], part_outs[c].at[BACK[k] - 1]),
                ("part", c, k), ("part", c, BACK[k]), near.along[k],
            )

    @pl.when(step == 2 * steps + 3)
    def _():
        add_arrived(0)

    @pl.when(step == 3 * steps + 3)
    def _():
        add_arrived(1)

    @pl.when(turn < row_steps)
    def _():
        for e in range(CHUNK):
            first = 2 * hidden * e
            w_both = weights[chunk, :, :, :, first : first + 2 * hidden].reshape(width, 2 * hidden)
            start = both + hidden * e
            w_down = weights[chunk, :, :, :, start : start + hidden].reshape(width, hidden)
            gate_up = dot(x_ref[...], w_both)
            raw = dot(og_ref[...], w_down) * RESIDUAL_SCALE
            gate, up = gate_up[:, :hidden], gate_up[:, hidden:]
            gate_lane = lax.broadcasted_iota(
                jnp.int32, (EXPERT_ROWS, combine_ref.shape[1]), 1
            )
            column = jnp.sum(
                jnp.where(gate_lane == chunk * CHUNK + e, combine_ref[...], 0.0),
                axis=1, keepdims=True,
            )
            sigmoid = 1.0 / (1.0 + jnp.exp(-gate))
            active = gate * sigmoid
            inner_value = (active * up).astype(BF16).astype(F32)
            held_down[rows, hidden * e : hidden * (e + 1)] = (inner_value * column).astype(BF16)
            gates[rows, :] = jnp.where(
                lane == chunk * CHUNK + e,
                jnp.sum(inner_value * raw, axis=1, keepdims=True),
                gates[rows, :],
            )
            inner_grad = raw * column
            held_both[rows, first : first + hidden] = (
                inner_grad * up * sigmoid * (1.0 + gate * (1.0 - sigmoid))
            ).astype(BF16)
            held_both[rows, first + hidden : first + 2 * hidden] = (inner_grad * active).astype(BF16)

        def sums(add):
            for part in range(SLOTS):
                cols = slice(4 * block * part, 4 * block * (part + 1))
                w_both = weights[chunk, part, :, :, :both].reshape(4 * block, both)
                w_down = weights[chunk, part, :, :, both:].reshape(4 * block, hidden * CHUNK)
                mix = dot(held_down[rows, :], w_down, NT)
                dx = dot(held_both[rows, :], w_both, NT)
                if add:
                    mix = mix + mix_sum[rows, cols].astype(F32)
                    dx = dx + dx_sum[rows, cols].astype(F32)
                mix_sum[rows, cols] = mix.astype(BF16)
                dx_sum[rows, cols] = dx.astype(BF16)

        @pl.when(chunk == 0)
        def _():
            sums(False)

        @pl.when(chunk > 0)
        def _():
            sums(True)

    @pl.when(turn >= row_steps)
    def _():
        part = turn - row_steps
        grads[chunk, part, :, :, :both] = (
            dot(xt_ref[...], held_both[...]).astype(BF16).reshape(2, 2 * block, both)
        )
        grads[chunk, part, :, :, both:] = (
            (dot(ogt_ref[...], held_down[...]) * RESIDUAL_SCALE)
            .astype(BF16)
            .reshape(2, 2 * block, hidden * CHUNK)
        )

    begin = last * steps
    for i in range(2):
        for c in range(2):
            mine = pl.ds(tokens + (2 * c + i) * EXPERT_ROWS, EXPERT_ROWS)
            there = pl.ds((2 * c + i) * EXPERT_ROWS, EXPERT_ROWS)

            @pl.when((step == begin + 2 * c + i) & (core != c))
            def _():
                for name, total, got in (("t", dx_sum, twin_rows), ("mt", mix_sum, twin_mix)):
                    copies.remote(
                        lambda: (total.at[mine], got.at[i]), (name, i), (name, i), near.twin,
                        last=False,
                    )

            @pl.when((step == begin + 2 + 2 * c + i) & (core == c))
            def _():
                for name, total, got in (("t", dx_sum, twin_rows), ("mt", mix_sum, twin_mix)):
                    copies.arrived(got.at[i], (name, i), near.twin)
                    for here in few_rows(EXPERT_ROWS):
                        at = pl.ds(mine.start + here.start, 16)
                        total[at, :] = (
                            total[at, :].astype(F32) + got[i, here, :].astype(F32)
                        ).astype(BF16)
                copies.remote(
                    lambda: (dx_sum.at[mine], dx_other.at[there]), ("o", i), ("o", i), near.over_x,
                    last=False,
                )

            @pl.when((step == begin + steps - 2 + i) & (core == c))
            def _():
                copies.arrived(dx_other.at[there], ("o", i), near.over_x)
                copies.remote(
                    lambda: (dx_other.at[there],) * 2, ("o2", i), ("o2", i), near.twin, last=False
                )

    for i in range(tiles):

        @pl.when(step == begin + tiles + i)
        def _():
            own = pl.ds(i * EXPERT_ROWS, EXPERT_ROWS)
            copies.copy(lambda own=own: (dx_sum.at[own], dx_own.at[own]), ("own", i))
            copies.remote(
                lambda own=own: (dx_sum.at[own], dx_twin.at[own]), ("own", i), ("own", i), near.twin
            )

    shares = gate_kept.shape[0]

    @pl.when(step == begin + row_steps)
    def _():
        copies.copy(lambda: (mix_sum, mix_out), "mix")
        turned = gates[...].T[:shares, :]
        gate_kept[...] = turned
        copies.remote(
            lambda: (gate_kept.at[:, pl.ds(tokens, tokens)], gate_got), ("g",), ("g",), near.over_x
        )

    @pl.when(step == begin + steps - 2)
    def _():
        copies.arrived(gate_got, ("g",), near.over_x)
        gate_full[pl.ds(pl.multiple_of(x * shares, shares), shares), :] = gate_kept[:, :tokens]
        gate_full[pl.ds(pl.multiple_of((1 - x) * shares, shares), shares), :] = gate_got[...]
        copies.remote(lambda: (gate_full, gate_twin), ("g2",), ("g2",), near.twin)

    for c in range(chunks):

        @pl.when(step == (c + 1) * steps - 1)
        def _():
            if c < SENT:
                copies.remote(
                    lambda c=c: (grads.at[c, :, 1 - y], arrived.at[c]),
                    ("sum", c), ("sum", c), near.over_y,
                )
            else:
                for k in range(SLOTS):
                    copies.copy(
                        lambda c=c, k=k: (grads.at[c, spots[k], y], near_outs[c - SENT].at[k]),
                        ("near out", c, k),
                    )
                    if c < last and k == 0:
                        copies.copy(lambda c=c: (grads.at[c, z, 1 - y], first_out), "first out")
                    elif c < last:
                        copies.remote(
                            lambda c=c, k=k: (grads.at[c, spots[k], 1 - y], late_out.at[k - 1]),
                            ("late", k), ("late", k), near.over_y,
                        )
                    else:
                        copies.copy(
                            lambda c=c, k=k: (grads.at[c, spots[k], 1 - y], far_out.at[k]),
                            ("far out", k),
                        )

    @pl.when(step == chunks * steps - 1)
    def _():
        copies.arrived(gate_twin, ("g2",), near.twin)
        gate_out[...] = gate_full[...] + gate_twin[...]
        for i in range(tiles):
            copies.arrived(
                dx_twin.at[pl.ds(i * EXPERT_ROWS, EXPERT_ROWS)], ("own", i), near.twin
            )
        for i in range(2):
            for c in range(2):
                mine = pl.ds(tokens + (2 * c + i) * EXPERT_ROWS, EXPERT_ROWS)
                there = pl.ds((2 * c + i) * EXPERT_ROWS, EXPERT_ROWS)

                @pl.when(core != c)
                def _():
                    copies.sent(lambda: (dx_sum.at[mine], twin_rows.at[i]), ("t", i), near.twin)
                    copies.sent(lambda: (mix_sum.at[mine], twin_mix.at[i]), ("mt", i), near.twin)
                    copies.arrived(dx_other.at[there], ("o2", i), near.twin)

                @pl.when(core == c)
                def _():
                    copies.sent(
                        lambda: (dx_sum.at[mine], dx_other.at[there]), ("o", i), near.over_x
                    )
                    copies.sent(lambda: (dx_other.at[there],) * 2, ("o2", i), near.twin)

        for c in range(SENT):
            for k in range(1, SLOTS):
                copies.arrived(part_outs[c].at[k - 1], ("part", c, k), near.along[k])
        for k in range(1, SLOTS):
            copies.arrived(late_out.at[k - 1], ("late", k), near.over_y)
        copies.finish()


def experts_pass(x, og, xt, ogt, combine, pairs, near, far):
    tokens, width = x.shape
    chunks, pair, columns = pairs.shape
    hidden = columns // (3 * CHUNK)
    shares = chunks * CHUNK
    row_steps = tokens // EXPERT_ROWS
    steps = row_steps + SLOTS
    inner = lax.axis_size("dp") // 16
    row_at = lambda s: ((jnp.minimum(s % steps, row_steps - 1) + row_steps // 2) % row_steps, 0)
    width_at = lambda s: (jnp.maximum(s % steps - row_steps, 0), 0)
    row = pl.BlockSpec((EXPERT_ROWS, width), row_at)
    turned = pl.BlockSpec((width // SLOTS, tokens), width_at)
    anywhere = pl.BlockSpec(memory_space=pl.ANY)
    left = chunks - SENT
    dma = pltpu.SemaphoreType.DMA
    shape = jax.ShapeDtypeStruct
    outs = pl.pallas_call(
        functools.partial(experts_kernel, inner, chunks, row_steps),
        grid=(chunks * steps,),
        in_specs=[row, row, turned, turned, pl.BlockSpec((EXPERT_ROWS, combine.shape[1]), row_at)]
        + [anywhere] * 3,
        out_specs=[anywhere] * 4
        + [pl.BlockSpec((2 * shares, tokens // 2), lambda s: (0, 0))]
        + [anywhere] * (2 * SENT + left + 3),
        out_shape=[shape((tokens // 2, width), BF16)] * 3
        + [shape((tokens, width), BF16), shape((2 * shares, tokens // 2), F32)]
        + [shape((pair, columns), BF16)] * SENT
        + [shape((SLOTS - 1, pair, columns), BF16)] * SENT
        + [shape((SLOTS, pair, columns), BF16)] * left
        + [shape((SLOTS - 1, pair, columns), BF16), shape((pair, columns), BF16)]
        + [shape((SLOTS, pair, columns), BF16)],
        scratch_shapes=[
            pltpu.VMEM((chunks + 1, SLOTS, 2, pair, columns), BF16),
            pltpu.VMEM((SENT, SLOTS, pair, columns), BF16),
            pltpu.VMEM((tokens, 2 * hidden * CHUNK), BF16),
            pltpu.VMEM((tokens, hidden * CHUNK), BF16),
            pltpu.VMEM((tokens, width), BF16),
            pltpu.VMEM((tokens, width), BF16),
            pltpu.VMEM((2, EXPERT_ROWS, width), BF16),
            pltpu.VMEM((2, EXPERT_ROWS, width), BF16),
            pltpu.VMEM((tokens, LANES), F32),
            pltpu.VMEM((shares, tokens), F32),
            pltpu.VMEM((shares, tokens // 2), F32),
            pltpu.VMEM((2 * shares, tokens // 2), F32),
            pltpu.VMEM((2 * shares, tokens // 2), F32),
            dma((48,)), dma((48,)), dma((48,)),
        ],
        compiler_params=pltpu.CompilerParams(
            vmem_limit_bytes=EXPERT_VMEM, collective_id=0, has_side_effects=True
        ),
        cost_estimate=pl.CostEstimate(
            flops=8 * tokens * width * chunks * columns,
            bytes_accessed=2 * chunks * width * columns, transcendentals=0,
        ),
        name="experts_pass",
    )(x, og, xt, ogt, combine, pairs, near, far)
    dx, mix, gate = outs[:3], outs[3], outs[4]
    rest = outs[5:]
    keep, parts, rest = rest[:SENT], rest[SENT : 2 * SENT], rest[2 * SENT :]
    return dx, mix, gate, keep, parts, rest[:left], rest[left:]


class Copies:
    def __init__(self, send, recv, local):
        self.send, self.recv, self.local = send, recv, local
        self.sends, self.recvs, self.locals, self.started = {}, {}, {}, []

    def remote(self, ends, name, arrives, device, last=True):
        sent = self.sends.setdefault(name, len(self.sends))
        got = self.recvs.setdefault(arrives, len(self.recvs))

        def make():
            source, target = ends()
            return pltpu.make_async_remote_copy(
                source, target, self.send.at[sent], self.recv.at[got],
                device_id=device, device_id_type=MESH_ID,
            )

        make().start()
        if last:
            self.started.append(lambda: make().wait_send())

    def sent(self, ends, name, device):
        source, target = ends()
        pltpu.make_async_remote_copy(
            source, target, self.send.at[self.sends[name]], self.recv.at[0],
            device_id=device, device_id_type=MESH_ID,
        ).wait_send()

    def arrived(self, place, name, device):
        got = self.recvs.setdefault(name, len(self.recvs))
        pltpu.make_async_remote_copy(
            place, place, self.send.at[0], self.recv.at[got],
            device_id=device, device_id_type=MESH_ID,
        ).wait_recv()

    def copy(self, ends, name, wait_last=True):
        at = self.locals.setdefault(name, len(self.locals))

        def make():
            return pltpu.make_async_copy(*ends(), self.local.at[at])

        make().start()
        if wait_last:
            self.started.append(lambda: make().wait())
        return lambda: make().wait()

    def wait_copy(self, ends, name):
        pltpu.make_async_copy(*ends(), self.local.at[self.locals[name]]).wait()

    def finish(self):
        for wait in self.started:
            wait()


class Neighbours:
    def __init__(self, inner):
        me = lax.axis_index("dp")
        at = me // inner
        self.core = lax.axis_index("tensor")
        self.z, self.y, self.x = at // 4, at // 2 % 2, at % 2
        self.spots = [(self.z + dz + 4) % 4 for dz in Z_FROM]
        self.along = [{"dp": me + (spot - self.z) * 4 * inner} for spot in self.spots]
        self.over_y = {"dp": me + (1 - 2 * self.y) * 2 * inner}
        self.over_x = {"dp": me + (1 - 2 * self.x) * inner}
        self.twin = {"tensor": 1 - self.core}
        self.blocks = {
            (k, other_y, other_x): self.spots[k] * 4
            + (1 - self.y if other_y else self.y) * 2
            + (1 - self.x if other_x else self.x)
            for k in range(SLOTS)
            for other_y in (0, 1)
            for other_x in (0, 1)
        }

    def greet(self):
        barrier = pltpu.get_barrier_semaphore()
        devices = [*self.along[1:], self.over_y, self.over_x, self.twin]
        for device in devices:
            pl.semaphore_signal(barrier, inc=1, device_id=device, device_id_type=MESH_ID)
        pl.semaphore_wait(barrier, len(devices))

    def block(self, k, other_y, other_x):
        return self.blocks[k, other_y, other_x]


BACK = (0, 2, 1, 3)


class Gather:
    def __init__(self, copies, near, shard, full, tag):
        self.copies, self.near, self.shard, self.full, self.tag = copies, near, shard, full, tag
        self.split = full.shape[2] // (2 * LANES) * LANES

    def source(self, k):
        return self.shard if k == 0 else self.full.at[self.near.block(k, 0, 0)]

    def begin(self):
        near, mine = self.near, self.near.block(0, 0, 0)
        for way, slot in ((2, 1), (1, 2)):
            self.copies.remote(
                lambda: (self.shard, self.full.at[mine]),
                (self.tag, "z", way), (self.tag, "z", slot), near.along[way],
            )
        self.full[mine] = self.shard[...]

    def second(self):
        near, below = self.near, self.near.block(1, 0, 0)
        self.copies.arrived(self.full.at[below], (self.tag, "z", 1), near.along[1])
        self.copies.remote(
            lambda: (self.full.at[below],) * 2, (self.tag, "z", 3), (self.tag, "z", 3), near.along[2]
        )

    def spread(self, k):
        near, place = self.near, self.full.at[self.near.block(k, 0, 0)]
        if k > 1:
            self.copies.arrived(place, (self.tag, "z", k), near.along[k])
        for way, device in (("y", near.over_y), ("x", near.over_x)):
            name = (self.tag, way, k)
            self.copies.remote(
                lambda: (self.source(k), self.full.at[near.block(k, 0, 0)]), name, name, device
            )

    def cross(self, k):
        near = self.near
        from_y = self.full.at[near.block(k, 1, 0)]
        from_x = self.full.at[near.block(k, 0, 1)]
        self.copies.arrived(from_y, (self.tag, "y", k), near.over_y)
        self.copies.remote(
            lambda: (self.full.at[near.block(k, 1, 0), :, : self.split],) * 2,
            (self.tag, "one", k), (self.tag, "one", k), near.over_x,
        )
        self.copies.arrived(from_x, (self.tag, "x", k), near.over_x)
        self.copies.remote(
            lambda: (self.full.at[near.block(k, 0, 1), :, self.split :],) * 2,
            (self.tag, "two", k), (self.tag, "two", k), near.over_y,
        )

    def end(self):
        near = self.near
        for k in range(SLOTS):
            place = self.full.at[near.block(k, 1, 1)]
            self.copies.arrived(place.at[:, : self.split], (self.tag, "one", k), near.over_x)
            self.copies.arrived(place.at[:, self.split :], (self.tag, "two", k), near.over_y)


def roll_left(slab, lanes):
    return pltpu.roll(slab, LANES - lanes, 1)


def forward_kernel(
    inner, q_shard, o_shard, gateup_hbm, down_hbm, hidden_hbm, og_hbm, cos, sin, seg_col, seg_row,
    routes,
    q_full, o_full, small, normed, q_ref, k_ref, v_ref, attended, lse_ref, combine, combine_pair,
    middle_hbm, x_hbm, xt_hbm, og_pair, ogt_hbm, pairs_hbm, near_hbm, far_hbm,
    hidden, gateup, down, given, pairs, bias, k_low, k_high, v_low, v_high, part, part_got, x_own, x_got,
    middle, stage, turned, columns_out, columns_got, send, recv, local,
):
    near = Neighbours(inner)
    copies = Copies(send, recv, local)
    tokens, width = hidden.shape
    block = width // 16
    chunks = pairs.shape[0]
    hid = down.shape[2]
    q_width = q_ref.shape[1]
    kv_slabs = k_ref.shape[1] // LANES
    slabs = q_width // LANES
    qkv_width = q_width + 2 * k_ref.shape[1]
    experts = down.shape[0]
    each = 2 + experts
    half = tokens // 2
    tiles = tokens // ROWS
    x, core = near.x, near.core
    own_half = pl.ds(pl.multiple_of(core * half, half), half)
    mine = pl.ds(pl.multiple_of(tokens + core * half, half), half)
    theirs = pl.ds(pl.multiple_of(tokens + (1 - core) * half, half), half)

    near.greet()
    gather_q = Gather(copies, near, q_shard, q_full, "q")
    gather_o = Gather(copies, near, o_shard, o_full, "o")
    gather_q.begin()
    gather_q.spread(0)
    weights_in = [
        copies.copy(lambda: (gateup_hbm, gateup), "gateup", False),
        copies.copy(lambda: (down_hbm, down), "down", False),
    ]
    hidden_in = copies.copy(lambda: (hidden_hbm, hidden), "hidden", False)
    copies.copy(lambda: (og_hbm, og_pair.at[pl.ds(0, tokens)]), "og")

    def pack(c, mine):
        first = 2 * (chunks * (x if mine else 1 - x) + c)
        rows = pl.ds(pl.multiple_of(x * block, block), block)
        for e in range(CHUNK):
            for part_at in range(2):
                at = hid * (2 * e + part_at)
                value = gateup[first + e, part_at].astype(BF16)
                if mine:
                    pairs[c, rows, at : at + hid] = value
                else:
                    given[c, :, at : at + hid] = value
            at = hid * (2 * CHUNK + e)
            value = down[first + e].astype(BF16)
            if mine:
                pairs[c, rows, at : at + hid] = value
            else:
                given[c, :, at : at + hid] = value

    def swap(c):
        rows = pl.ds(pl.multiple_of(x * block, block), block)
        copies.remote(
            lambda: (given.at[c], pairs.at[c, rows]), ("s", c), ("s", c), near.over_x
        )

    def swapped(c):
        rows = pl.ds(pl.multiple_of((1 - x) * block, block), block)
        copies.arrived(pairs.at[c, rows], ("s", c), near.over_x)

    def ring_one(c):
        copies.remote(
            lambda: (pairs.at[c], near_hbm.at[c, 0]), ("up", c), ("r", c, 1), near.along[2]
        )
        copies.remote(
            lambda: (pairs.at[c], near_hbm.at[c, 1]), ("down", c), ("r", c, 2), near.along[1]
        )

    def ring_two(c):
        copies.arrived(near_hbm.at[c, 0], ("r", c, 1), near.along[1])
        copies.remote(
            lambda: (near_hbm.at[c, 0], near_hbm.at[c, 2]), ("two", c), ("r", c, 3), near.along[2]
        )

    def over_y(c, k):
        copies.remote(
            lambda: (pairs.at[c] if k == 0 else near_hbm.at[c, k - 1], far_hbm.at[c, k]),
            ("f", c, k), ("f", c, k), near.over_y,
        )

    def ring_got(c, k):
        copies.arrived(near_hbm.at[c, k - 1], ("r", c, k), near.along[k])

    def turn_tile(source, target, name, side):
        copies.copy(lambda: (source, stage.at[side]), (name, "in"), False)()
        turned[side] = stage[side].T
        return copies.copy(lambda: (turned.at[side], target), (name, "out"), False)

    waits = [None, None]

    def turn_next(source, target, name, side):
        if waits[side] is not None:
            waits[side]()
        waits[side] = turn_tile(source, target, name, side)

    for wait in weights_in:
        wait()
    pack(0, False)
    pack(0, True)
    gather_q.second()
    gather_q.spread(1)
    gather_q.spread(2)
    gather_q.cross(0)
    pack(1, False)
    pack(1, True)
    pack(2, False)
    gather_q.cross(1)
    gather_q.cross(2)
    gather_q.spread(3)
    swap(0)
    pack(2, True)
    pack(3, False)
    pack(3, True)
    fill_bias(bias, seg_col, seg_row)
    gather_q.cross(3)
    gather_o.begin()
    gather_o.spread(0)
    swap(1)
    for tile in range(tiles):
        rows = pl.ds(tile * ROWS, ROWS)
        turn_next(og_hbm.at[rows], ogt_hbm.at[:, rows], ("og", tile), tile % 2)
    hidden_in()
    gather_q.end()
    pieces = q_full[:, :, qkv_width:].reshape(width, LANES)
    wide = pieces.astype(F32)
    summed = wide + roll_left(wide, each) + roll_left(wide, 2 * each)
    small[...] = summed.T[: small.shape[0], :]
    swapped(0)
    ring_one(0)
    over_y(0, 0)
    swap(2)
    swap(3)

    def project(tile, carry):
        rows = pl.ds(pl.multiple_of(tile * ROWS, ROWS), ROWS)
        for here in few_rows(ROWS):
            value = hidden[pl.ds(pl.multiple_of(tile * ROWS + here.start, 16), 16), :].astype(F32)
            inverse = lax.rsqrt(jnp.mean(value * value, axis=1, keepdims=True) + NORM_EPSILON)
            stage[0, here, :] = (value * inverse * small[0:1, :]).astype(BF16)
        low = stage[0]
        normed[:, rows] = low.T
        cosine, sine = cos[rows, :], sin[rows, :]
        for g in range(slabs + 2 * kv_slabs):
            lanes = slice(g * LANES, (g + 1) * LANES)
            if g % 2 == 0:
                two = slice(g * LANES, (g + 2) * LANES)
                lin_two = dot(low, q_full[:, :, two].reshape(width, 2 * LANES))
            lin = lin_two[:, (g % 2) * LANES : (g % 2 + 1) * LANES]
            if g < slabs + kv_slabs:
                lin = lin * cosine + rotate_halves(lin) * sine
            if g < slabs:
                q_ref[rows, lanes] = lin.astype(BF16)
            elif g < slabs + kv_slabs:
                at = (g - slabs) * LANES
                k_ref[rows, at : at + LANES] = lin.astype(BF16)
            else:
                at = (g - slabs - kv_slabs) * LANES
                v_ref[rows, at : at + LANES] = lin.astype(BF16)

        @pl.when(tile == 1)
        def _():
            gather_o.second()
            gather_o.spread(1)

        @pl.when(tile == 2)
        def _():
            gather_o.spread(2)
            gather_o.cross(0)

        return carry

    lax.fori_loop(0, tiles, project, 0)
    for j in range(kv_slabs):
        lanes = slice(j * LANES, (j + 1) * LANES)
        spread_heads(k_ref[:, lanes], k_low, k_high, 2 * j)
        spread_heads(v_ref[:, lanes], v_low, v_high, 2 * j)

    def attend(g, carry):
        lanes = pl.ds(pl.multiple_of(g * LANES, LANES), LANES)
        kv_even, kv_odd = (2 * g) // 3, (2 * g + 1) // 3
        for at in range(0, tokens, ROWS):
            rows = slice(at, at + ROWS)
            upto = at + ROWS
            queries = q_ref[rows, lanes]
            total = None
            stats = []
            for keys, values, kv_at in ((k_low, v_low, kv_even), (k_high, v_high, kv_odd)):
                scores = dot(queries, keys[kv_at, :upto, :], NT) * SCORE_SCALE + bias[rows, :upto]
                highest = jnp.max(scores, axis=1, keepdims=True)
                weights = jnp.exp(scores - highest)
                whole = jnp.sum(weights, axis=1, keepdims=True)
                probability = (weights * (1.0 / whole)).astype(BF16)
                one = dot(probability, values[kv_at, :upto, :])
                total = one if total is None else total + one
                stats.append(highest + jnp.log(whole))
            attended[rows, lanes] = total.astype(BF16)
            across = jnp.where(half_mask(ROWS, False), stats[0], stats[1]).T
            lse_ref[g, 0:1, rows] = across[0:1, :]
            lse_ref[g, 1:2, rows] = across[HEAD_DIM : HEAD_DIM + 1, :]

        @pl.when(g == 0)
        def _():
            gather_o.spread(3)
            gather_o.cross(1)
            gather_o.cross(2)

        @pl.when(g == 1)
        def _():
            ring_two(0)
            over_y(0, 1)
            ring_got(0, 2)
            over_y(0, 2)
            swapped(1)
            ring_one(1)
            over_y(1, 0)
            copies.remote(
                lambda: (og_hbm.at[own_half], og_pair.at[mine]), ("og",), ("og",), near.over_x
            )

        @pl.when(g == 2)
        def _():
            gather_o.cross(3)

        @pl.when(g == 4)
        def _():
            gather_o.end()

        @pl.when(g == slabs - 1)
        def _():
            ring_got(0, 3)
            over_y(0, 3)
            swapped(2)
            ring_one(2)
            over_y(2, 0)

        return carry

    lax.fori_loop(0, slabs, attend, 0)

    def project_out(step, carry):
        tile = (step + 2 * (1 - core)) % tiles
        rows = pl.ds(pl.multiple_of(tile * ROWS, ROWS), ROWS)
        low = attended[rows, :]
        for group in range(SLOTS):
            cols = slice(4 * block * group, 4 * block * (group + 1))
            weight = o_full[4 * group : 4 * (group + 1)].reshape(4 * block, q_width)
            part[rows, cols] = dot(low, weight, NT).astype(BF16)
        return carry

    for step in range(tiles):
        project_out(step, 0)
        tile = (step + 2 * (1 - core)) % tiles
        rows = pl.ds(pl.multiple_of(tile * ROWS, ROWS), ROWS)
        copies.remote(
            lambda rows=rows: (part.at[rows], part_got.at[rows]),
            ("p", step), ("p", step), near.twin,
        )
    router = q_full[:, :, qkv_width:].reshape(width, LANES)
    for step in range(tiles):
        tile = (step + 2 * core) % tiles
        rows = pl.ds(pl.multiple_of(tile * ROWS, ROWS), ROWS)
        copies.arrived(part_got.at[rows], ("p", step), near.twin)
        side = step % 2
        if step >= 2:
            middle_out[side]()
        elif step == 0:
            middle_out = [None, None]
        for here in few_rows(ROWS):
            at = pl.ds(pl.multiple_of(tile * ROWS + here.start, 16), 16)
            total = hidden[at, :].astype(F32) + RESIDUAL_SCALE * (
                part[at, :].astype(F32) + part_got[at, :].astype(F32)
            )
            middle[side, here, :] = total
            inverse = lax.rsqrt(jnp.mean(total * total, axis=1, keepdims=True) + NORM_EPSILON)
            value = total * inverse * small[1:2, :]
            high = value.astype(BF16)
            x_own[at, :] = high
            rest = value - high.astype(F32)
            mid = rest.astype(BF16)
            stage[0, here, :] = mid
            stage[1, here, :] = (rest - mid.astype(F32)).astype(BF16)
        middle_out[side] = copies.copy(
            lambda rows=rows, side=side: (middle.at[side], middle_hbm.at[rows]), ("m", step), False
        )
        copies.copy(lambda rows=rows: (x_own.at[rows], x_hbm.at[rows]), ("x", step))
        if step < 2:
            copies.remote(
                lambda rows=rows: (x_own.at[rows], x_got.at[rows]),
                ("x", step), ("x", step), near.over_x,
            )
        one, two, three = dot(x_own[rows, :], router), dot(stage[0], router), dot(stage[1], router)
        logits = one + roll_left(one, each) + roll_left(one, 2 * each) + two + roll_left(two, each)
        logits = roll_left(logits + three, 2)
        lane = lax.broadcasted_iota(jnp.int32, (ROWS, LANES), 1)
        chosen = lane < 0
        route = routes[rows, :]
        for k in range(routes.shape[1]):
            chosen = chosen | (route[:, k : k + 1] == lane)
        logits = jnp.where(chosen, logits, MASK_VALUE)
        powers = jnp.exp(logits - jnp.max(logits, axis=1, keepdims=True))
        powers = jnp.where(chosen, powers, 0.0)
        combine[rows, :] = powers * (1.0 / jnp.sum(powers, axis=1, keepdims=True))
        if step == 0:
            swapped(3)
            copies.copy(lambda: (pairs, pairs_hbm), "pairs")
        if step == 1:
            ring_two(1)
            over_y(1, 1)
            ring_got(1, 2)
            over_y(1, 2)

    shares = experts // 2
    flipped = combine[...].T
    kept = jnp.where(x == 0, flipped[:shares, :], flipped[shares : 2 * shares, :])
    gone = jnp.where(x == 0, flipped[shares : 2 * shares, :], flipped[:shares, :])
    columns_out[...] = gone
    copies.remote(lambda: (columns_out, columns_got), ("c",), ("c",), near.over_x)
    combine_pair[:tokens, :] = kept.T
    ring_two(2)
    ring_got(1, 3)
    over_y(1, 3)

    copies.arrived(og_pair.at[mine], ("og",), near.over_x)
    copies.remote(lambda: (og_pair.at[mine],) * 2, ("og2",), ("og2",), near.twin)
    for tile in range(tiles):
        rows = pl.ds(tile * ROWS, ROWS)
        if waits[tile % 2] is not None:
            waits[tile % 2]()
        turned[tile % 2] = x_own[rows, :].T
        waits[tile % 2] = copies.copy(
            lambda rows=rows, side=tile % 2: (turned.at[side], xt_hbm.at[:, rows]),
            ("xt", tile), False,
        )
    copies.arrived(columns_got, ("c",), near.over_x)
    combine_pair[tokens:, :] = columns_got[...].T
    copies.arrived(og_pair.at[theirs], ("og2",), near.twin)
    order = [(step + 2 * core) % tiles for step in range(2)]
    order += [(step + 2 * (1 - core)) % tiles for step in range(2)]

    def og_rows(step):
        return pl.ds(pl.multiple_of(tokens + order[step] * ROWS, ROWS), ROWS)

    def og_load(step):
        return copies.copy(
            lambda: (og_pair.at[og_rows(step)], stage.at[step % 2]), ("ogin", step), False
        )

    loaded = og_load(0)
    for step in range(tiles):
        loaded()
        if step + 1 < tiles:
            loaded = og_load(step + 1)
        side = step % 2
        waits[side]()
        turned[side] = stage[side].T
        waits[side] = copies.copy(
            lambda step=step, side=side: (turned.at[side], ogt_hbm.at[:, og_rows(step)]),
            ("ogt", step), False,
        )
    for step in range(tiles):
        rows = pl.ds(pl.multiple_of(order[step] * ROWS, ROWS), ROWS)
        there = pl.ds(pl.multiple_of(tokens + order[step] * ROWS, ROWS), ROWS)
        if step < 2:
            copies.arrived(x_got.at[rows], ("x", step), near.over_x)
            copies.remote(
                lambda rows=rows: (x_got.at[rows],) * 2, ("x2", step), ("x2", step), near.twin
            )
        else:
            copies.arrived(x_got.at[rows], ("x2", step - 2), near.twin)
        copies.copy(
            lambda rows=rows, there=there: (x_got.at[rows], x_hbm.at[there]), ("xg", step)
        )
        side = step % 2
        waits[side]()
        turned[side] = x_got[rows, :].T
        waits[side] = copies.copy(
            lambda there=there, side=side: (turned.at[side], xt_hbm.at[:, there]),
            ("xgt", step), False,
        )
    for wait in waits + middle_out:
        wait()
    ring_got(2, 2)
    ring_got(2, 3)
    for c in range(LATE + 1):
        for k in range(SLOTS if c < LATE else 1):
            copies.arrived(far_hbm.at[c, k], ("f", c, k), near.over_y)
    copies.finish()


def forward_pass(q_shard, o_shard, gateup, down, hidden, og, cosine, sine, segments, routes):
    tokens, width = hidden.shape
    experts, hid = down.shape[0], down.shape[2]
    block, q_columns = q_shard.shape
    q_width = o_shard.shape[1]
    kv_width = (q_columns - LANES - q_width) // 2
    slabs, kv_heads = q_width // LANES, kv_width // HEAD_DIM
    chunks = experts // (2 * CHUNK)
    columns = 3 * CHUNK * hid
    anywhere, vmem = pl.BlockSpec(memory_space=pl.ANY), vmem_spec()
    shape = jax.ShapeDtypeStruct
    inner = lax.axis_size("dp") // 16
    dma = pltpu.SemaphoreType.DMA
    return pl.pallas_call(
        functools.partial(forward_kernel, inner),
        in_specs=[vmem, vmem] + [anywhere] * 4 + [vmem] * 5,
        out_specs=[vmem] * 11 + [anywhere] * 8,
        out_shape=[
            shape((16, block, q_columns), BF16),
            shape((16, block, q_width), BF16),
            shape((24, width), F32),
            shape((width, tokens), BF16),
            shape((tokens, q_width), BF16),
            shape((tokens, kv_width), BF16),
            shape((tokens, kv_width), BF16),
            shape((tokens, q_width), BF16),
            shape((slabs, 8, tokens), F32),
            shape((tokens, LANES), F32),
            shape((2 * tokens, experts // 2), F32),
            shape((tokens, width), F32),
            shape((2 * tokens, width), BF16),
            shape((width, 2 * tokens), BF16),
            shape((2 * tokens, width), BF16),
            shape((width, 2 * tokens), BF16),
            shape((chunks, 2 * block, columns), BF16),
            shape((chunks - 1, SLOTS - 1, 2 * block, columns), BF16),
            shape((LATE + 1, SLOTS, 2 * block, columns), BF16),
        ],
        scratch_shapes=[
            pltpu.VMEM((tokens, width), BF16),
            pltpu.VMEM(gateup.shape, gateup.dtype),
            pltpu.VMEM(down.shape, down.dtype),
            pltpu.VMEM((chunks, block, columns), BF16),
            pltpu.VMEM((chunks, 2 * block, columns), BF16),
            pltpu.VMEM((tokens, tokens), F32),
        ]
        + [pltpu.VMEM((kv_heads, tokens, LANES), BF16)] * 4
        + [pltpu.VMEM((tokens, width), BF16)] * 4
        + [
            pltpu.VMEM((2, ROWS, width), F32),
            pltpu.VMEM((2, ROWS, width), BF16),
            pltpu.VMEM((2, width, ROWS), BF16),
            pltpu.VMEM((experts // 2, tokens), F32),
            pltpu.VMEM((experts // 2, tokens), F32),
            dma((80,)), dma((80,)), dma((60,)),
        ],
        compiler_params=pltpu.CompilerParams(
            vmem_limit_bytes=EXPERT_VMEM, collective_id=1, has_side_effects=True
        ),
        name="forward_pass",
    )(
        q_shard, o_shard, gateup, down, hidden, og, cosine, sine,
        segments[:, None], segments[None, :], routes,
    )


class Scatter:
    def __init__(self, copies, near, grad, one, two, got_y, got_x, got_z, share, tag):
        self.copies, self.near, self.grad, self.share, self.tag = copies, near, grad, share, tag
        self.one, self.two, self.got_y, self.got_x, self.got_z = one, two, got_y, got_x, got_z
        self.split = one.shape[2]

    def begin(self, k):
        near = self.near
        self.copies.remote(
            lambda: (self.grad.at[near.block(k, 1, 1), :, : self.split], self.one.at[k]),
            (self.tag, "one", k), (self.tag, "one", k), near.over_x,
        )
        self.copies.remote(
            lambda: (self.grad.at[near.block(k, 1, 1), :, self.split :], self.two.at[k]),
            (self.tag, "two", k), (self.tag, "two", k), near.over_y,
        )

    def cross(self, k):
        near, grad, split = self.near, self.grad, self.split
        self.copies.arrived(self.one.at[k], (self.tag, "one", k), near.over_x)
        at = near.block(k, 1, 0)
        for here in few_rows(grad.shape[1]):
            grad[at, here, :split] = (
                grad[at, here, :split].astype(F32) + self.one[k, here, :].astype(F32)
            ).astype(BF16)
        self.copies.remote(
            lambda: (grad.at[near.block(k, 1, 0)], self.got_y.at[k]),
            (self.tag, "y", k), (self.tag, "y", k), near.over_y,
        )
        self.copies.arrived(self.two.at[k], (self.tag, "two", k), near.over_y)
        at = near.block(k, 0, 1)
        for here in few_rows(grad.shape[1]):
            grad[at, here, split:] = (
                grad[at, here, split:].astype(F32) + self.two[k, here, :].astype(F32)
            ).astype(BF16)
        self.copies.remote(
            lambda: (grad.at[near.block(k, 0, 1)], self.got_x.at[k]),
            (self.tag, "x", k), (self.tag, "x", k), near.over_x,
        )

    def plane(self, k):
        near, grad = self.near, self.grad
        self.copies.arrived(self.got_y.at[k], (self.tag, "y", k), near.over_y)
        self.copies.arrived(self.got_x.at[k], (self.tag, "x", k), near.over_x)
        at = near.block(k, 0, 0)
        for here in few_rows(grad.shape[1]):
            total = grad[at, here, :].astype(F32) + self.got_y[k, here, :].astype(F32)
            total = total + self.got_x[k, here, :].astype(F32)
            if k == 0:
                self.share[here, :] = total
            else:
                grad[at, here, :] = total.astype(BF16)
        if k == 0:
            return
        self.copies.remote(
            lambda: (grad.at[near.block(k, 0, 0)], self.got_z.at[BACK[k] - 1]),
            (self.tag, "z", k), (self.tag, "z", BACK[k]), near.along[k],
        )

    def end(self):
        for k in range(1, SLOTS):
            self.copies.arrived(self.got_z.at[k - 1], (self.tag, "z", k), self.near.along[k])
            for here in few_rows(self.share.shape[0]):
                self.share[here, :] = self.share[here, :] + self.got_z[k - 1, here, :].astype(F32)


STRIP = 128


def backward_kernel(
    inner,
    o_full, q_ref, k_ref, v_ref, attended, lse_ref, cos, sin, seg_col, seg_row, small, combine,
    gate_turned, q_hbm, normed_hbm, hidden_hbm, og_hbm, middle_hbm, dx_own, dx_twin, dx_other,
    mix_pair, *refs,
):
    keeps, refs = refs[:SENT], refs[SENT:]
    parts, refs = refs[:SENT], refs[SENT:]
    near_two, near_three, late_got, far_first, far_three = refs[:5]
    q_share, o_share, input_grad, block_out, kept_out, given_got, mid_grad = refs[5:12]
    far_got, first_got, z_two, z_three, mix_twin, mix_other = refs[12:18]
    (
        attended_grad, lin_grad, o_grad, q_grad, o_one, o_two, o_y, o_x, o_z,
        q_one, q_two, q_y, q_x, q_z, part_got, pieces, z_send, z_keep, given, kept,
        strips, wide_in, wide_out, strip_out, router_rows, gate_columns, small_sum,
        send, recv, local, strip_sem, wide_sem, out_sem,
    ) = refs[18:]
    near = Neighbours(inner)
    copies = Copies(send, recv, local)
    tokens, width = hidden_hbm.shape
    block = width // 16
    x, core = near.x, near.core
    half = tokens // 2
    q_width = q_ref.shape[1]
    kv_width = k_ref.shape[1]
    kv_slabs, slabs = kv_width // LANES, q_width // LANES
    qkv_width = q_width + 2 * kv_width
    experts = gate_turned.shape[0]
    each = 2 + experts
    strip_count = tokens // STRIP
    ours = pl.ds(0, tokens)
    half_mine = pl.ds(pl.multiple_of(tokens + core * half, half), half)
    there = pl.ds(pl.multiple_of(core * half, half), half)
    not_there = pl.ds(pl.multiple_of((1 - core) * half, half), half)
    scatter_o = Scatter(copies, near, o_grad, o_one, o_two, o_y, o_x, o_z, o_share, "o")
    scatter_q = Scatter(copies, near, q_grad, q_one, q_two, q_y, q_x, q_z, q_share, "q")
    z_gots = [*parts, z_two, z_three]

    def y_ends(c, k):
        if c == SENT:
            return near_two.at[k], first_got if k == 0 else late_got.at[k - 1]
        return near_three.at[k], far_got.at[k]

    def y_load(c, k, i, which):
        if 0 in which:
            copies.copy(lambda: (y_ends(c, k)[0], pieces.at[2 * i]), ("own", c, k), False)
        if 1 in which:
            copies.copy(lambda: (y_ends(c, k)[1], pieces.at[2 * i + 1]), ("got", c, k), False)

    def y_sum(c, k, i):
        copies.wait_copy(lambda: (y_ends(c, k)[0], pieces.at[2 * i]), ("own", c, k))
        copies.wait_copy(lambda: (y_ends(c, k)[1], pieces.at[2 * i + 1]), ("got", c, k))
        if k > 0 and c > SENT:
            copies.sent(
                lambda: (z_send.at[k - 1], z_two.at[BACK[k] - 1]), (SENT, "z", k), near.along[k]
            )
        target = z_keep.at[c - SENT] if k == 0 else z_send.at[k - 1]
        for here in few_rows(target.shape[0]):
            target[here, :] = (
                pieces[2 * i, here, :].astype(F32) + pieces[2 * i + 1, here, :].astype(F32)
            ).astype(BF16)
        if k == 0:
            return
        copies.remote(
            lambda: (z_send.at[k - 1], z_gots[c].at[BACK[k] - 1]),
            (c, "z", k), (c, "z", BACK[k]), near.along[k], last=c > SENT,
        )

    def far_arrived(k):
        copies.arrived(far_got.at[k], ("far", k), near.over_y)

    def chunk_ends(c, k):
        return keeps[c] if k == 0 else z_gots[c].at[k - 1], pieces.at[k]

    def load_chunk(c):
        for k in range(1 if c >= SENT else 0, SLOTS):
            if c >= SENT:
                copies.arrived(z_gots[c].at[k - 1], (c, "z", k), near.along[k])
            copies.copy(lambda k=k: chunk_ends(c, k), (c, "sum", k), False)

    def sum_chunk(c):
        for k in range(1 if c >= SENT else 0, SLOTS):
            copies.wait_copy(lambda: chunk_ends(c, k), (c, "sum", k))
        if c >= 2:
            copies.wait_copy(lambda: (kept.at[c % 2], kept_out.at[c - 2]), ("kept", c - 2))
        for base, mine in ((x * block, True), ((1 - x) * block, False)):
            for here, rows in zip(few_rows(block), few_rows(block, base)):
                total = (pieces[0, rows, :] if c < SENT else z_keep[c - SENT, rows, :]).astype(F32)
                for k in range(1, SLOTS):
                    total = total + pieces[k, rows, :].astype(F32)
                if mine:
                    kept[c % 2, here, :] = total
                else:
                    given[c, here, :] = total.astype(BF16)
        copies.copy(lambda: (kept.at[c % 2], kept_out.at[c]), ("kept", c), c >= 2)
        copies.remote(
            lambda: (given.at[c], given_got.at[c]), ("given", c), ("given", c), near.over_x
        )

    def strip_rows(t):
        return pl.ds(pl.multiple_of(t * STRIP, STRIP), STRIP)

    def strip_loads(t, sources, wide):
        side = t % 2
        rows = strip_rows(t)
        loads = [
            pltpu.make_async_copy(source.at[rows], strips.at[i, side], strip_sem.at[i, side])
            for i, source in enumerate(sources)
        ]
        if wide is not None:
            loads.append(
                pltpu.make_async_copy(wide.at[rows], wide_in.at[side], wide_sem.at[side])
            )
        return loads

    def strip_store(t, source, target):
        side = t % 2
        return pltpu.make_async_copy(
            source.at[side], target.at[strip_rows(t)], out_sem.at[side]
        )

    def over_strips(sources, wide, source, target, compute):
        for load in strip_loads(0, sources, wide):
            load.start()

        def one(t, carry):
            side = t % 2

            @pl.when(t + 1 < strip_count)
            def _():
                for load in strip_loads(t + 1, sources, wide):
                    load.start()

            for load in strip_loads(t, sources, wide):
                load.wait()

            @pl.when(t >= 2)
            def _():
                strip_store(t - 2, source, target).wait()

            compute(t, side)
            strip_store(t, source, target).start()
            return carry

        lax.fori_loop(0, strip_count, one, 0)
        for t in (strip_count - 2, strip_count - 1):
            strip_store(t, source, target).wait()

    for i, k in enumerate((1, 2)):
        y_load(SENT, k, i, (0, 1))
    near.greet()
    for k in (1, 2, 3, 0):
        copies.remote(
            lambda k=k: (far_three.at[k], far_got.at[k]), ("far", k), ("far", k), near.over_y
        )
    copies.remote(lambda: (far_first, first_got), ("first",), ("first",), near.over_y)
    copies.remote(
        lambda: (mix_pair.at[half_mine], mix_other.at[there]), ("mo",), ("mo",), near.over_x
    )
    copies.remote(lambda: (mix_pair.at[ours], mix_twin), ("mt",), ("mt",), near.twin)
    y_sum(SENT, 1, 0)
    y_load(SENT, 3, 0, (0, 1))
    y_sum(SENT, 2, 1)
    y_sum(SENT, 3, 0)
    load_chunk(0)

    router = small[2 : 2 + experts, :]
    high = router.astype(BF16).astype(F32)
    mid = (router - high).astype(BF16).astype(F32)
    low = router - high - mid
    router_rows[...] = jnp.concatenate(
        [high, mid, low, high, mid, high, jnp.zeros((LANES - 6 * experts, width), F32)]
    ).astype(BF16)
    gate_columns[...] = jnp.concatenate(
        [gate_turned[...], jnp.zeros((LANES - experts, tokens), F32)]
    ).T
    small_sum[...] = jnp.zeros_like(small_sum)

    def middle_part(turned_back):
        def compute(t, side):
            rows = strip_rows(t)
            gates, grads = combine[rows, :], gate_columns[rows, :]
            logit = gates * (grads - jnp.sum(gates * grads, axis=1, keepdims=True))
            one = logit.astype(BF16).astype(F32)
            two = (logit - one).astype(BF16).astype(F32)
            three = (logit - one - two).astype(BF16).astype(F32)

            def moved(piece, by):
                return pltpu.roll(piece, by * experts, 1)

            row = one + moved(one, 1) + moved(one, 2) + moved(two, 3) + moved(two, 4)
            row = (row + moved(three, 5)).astype(BF16)
            wide_out[side] = dot(row, router_rows[...])
            gain = small[1:2, :]
            gain_part = None
            back, n_one, n_two, n_three = (
                strip_out.at[0], strip_out.at[1], z_keep.at[0], z_keep.at[1]
            )
            for here in few_rows(STRIP):
                upstream = strips[0, side, here, :].astype(F32) + strips[1, side, here, :].astype(F32)
                upstream = upstream + strips[2, side, here, :].astype(F32)
                upstream = upstream + wide_out[side, here, :]
                middle = wide_in[side, here, :]
                inverse = lax.rsqrt(jnp.mean(middle * middle, axis=1, keepdims=True) + NORM_EPSILON)
                scaled = middle * inverse
                weighted = upstream * gain
                mean_term = jnp.mean(weighted * scaled, axis=1, keepdims=True)
                grad = strips[3, side, here, :].astype(F32) + inverse * (
                    weighted - scaled * mean_term
                )
                wide_out[side, here, :] = grad
                back[here, :] = (RESIDUAL_SCALE * grad).astype(BF16)
                gained = jnp.sum(upstream * scaled, axis=0, keepdims=True)
                gain_part = gained if gain_part is None else gain_part + gained
                normed = scaled * gain
                piece = normed.astype(BF16)
                n_one[here, :] = piece
                rest = normed - piece.astype(F32)
                piece = rest.astype(BF16)
                n_two[here, :] = piece
                n_three[here, :] = (rest - piece.astype(F32)).astype(BF16)
            small_sum[0:1, :] += gain_part
            strip = pl.ds(0, STRIP)
            turned_back[:, rows] = back[...].T
            attended_grad[rows, :] = dot(back[...], o_full[...].reshape(width, q_width)).astype(BF16)
            columns = (one + moved(two, 1) + moved(three, 2)).T[: 3 * experts, :].astype(BF16)
            a, b, c = (
                dot(columns, n_one[...]), dot(columns, n_two[strip, :]), dot(columns, n_three[strip, :])
            )
            e = experts
            small_sum[8 : 8 + e, :] += (
                a[:e] + a[e : 2 * e] + a[2 * e :] + b[:e] + b[e : 2 * e] + c[:e]
            )

        over_strips([dx_own, dx_twin, dx_other, og_hbm], middle_hbm, wide_out, mid_grad, compute)
        for group in range(SLOTS):
            rows = slice(4 * block * group, 4 * block * (group + 1))
            o_grad[4 * group : 4 * (group + 1)] = (
                dot(turned_back[rows, :], attended[...]).astype(BF16).reshape(4, block, q_width)
            )

    pl.run_scoped(middle_part, pltpu.VMEM((width, tokens), BF16))
    for k in (1, 2, 3, 0):
        scatter_o.begin(k)

    def attention_part(bias0, bias1, bias2, bias3, k_low, k_high, v_low, v_high, dk, dv, dq):
        biases = (bias0, bias1, bias2, bias3)
        for at, bias in enumerate(biases):
            upto = bias.shape[0]
            keys_at = lax.broadcasted_iota(jnp.int32, bias.shape, 0)
            rows_at = at * ROWS + lax.broadcasted_iota(jnp.int32, bias.shape, 1)
            same = seg_col[:upto, :] == seg_row[:, at * ROWS : (at + 1) * ROWS]
            bias[...] = jnp.where((rows_at >= keys_at) & same, 0.0, MASK_VALUE).astype(F32)
        for j in range(kv_slabs):
            lanes = slice(j * LANES, (j + 1) * LANES)
            spread_heads(k_ref[:, lanes], k_low, k_high, 2 * j)
            spread_heads(v_ref[:, lanes], v_low, v_high, 2 * j)
        dk[...] = jnp.zeros_like(dk)
        dv[...] = jnp.zeros_like(dv)

        def slab(g, carry):
            lanes = pl.ds(pl.multiple_of(g * LANES, LANES), LANES)
            kv_even, kv_odd = (2 * g) // 3, (2 * g + 1) // 3
            for at, bias in enumerate(biases):
                rows = slice(at * ROWS, (at + 1) * ROWS)
                upto = (at + 1) * ROWS
                queries, grads = q_ref[rows, lanes], attended_grad[rows, lanes]
                turned = (grads.astype(F32) * attended[rows, lanes].astype(F32)).T
                zero = jnp.zeros_like(queries)
                dq_part = None
                for upper, keys, values, kv_at in (
                    (False, k_low, v_low, kv_even), (True, k_high, v_high, kv_odd)
                ):
                    first = HEAD_DIM if upper else 0
                    delta = jnp.sum(turned[first : first + HEAD_DIM, :], axis=0, keepdims=True)
                    head = 1 if upper else 0
                    total = lse_ref[g, head : head + 1, rows]
                    keys_here = keys[kv_at, :upto, :]
                    scores = dot(keys_here, queries, NT) * SCORE_SCALE + bias[...]
                    probability = jnp.exp(scores - total)
                    prob_grad = dot(values[kv_at, :upto, :], grads, NT)
                    score_grad = (probability * (prob_grad - delta)).astype(BF16)
                    mask = half_mask(ROWS, upper)
                    dv[kv_at, :upto, :] += dot(
                        probability.astype(BF16), jnp.where(mask, grads, zero)
                    )
                    dk[kv_at, :upto, :] += dot(score_grad, jnp.where(mask, queries, zero))
                    one = dot(score_grad, keys_here, TN)
                    dq_part = one if dq_part is None else dq_part + one
                dq[rows, :] = dq_part * SCORE_SCALE
            whole = dq[...]
            lin_grad[:, lanes] = (
                whole * cos[...] - rotate_halves(whole) * sin[...]
            ).astype(BF16)

            @pl.when(g == 1)
            def _():
                for k in (1, 2, 3, 0):
                    scatter_o.cross(k)

            @pl.when(g == 2)
            def _():
                sum_chunk(0)
                y_load(SENT + 1, 1, 0, (0,))
                y_load(SENT + 1, 2, 1, (0,))

            @pl.when(g == 3)
            def _():
                far_arrived(1)
                y_load(SENT + 1, 1, 0, (1,))
                far_arrived(2)
                y_load(SENT + 1, 2, 1, (1,))
                far_arrived(3)
                y_sum(SENT + 1, 1, 0)
                y_load(SENT + 1, 3, 0, (0, 1))
                y_sum(SENT + 1, 2, 1)
                y_sum(SENT + 1, 3, 0)
                load_chunk(1)

            @pl.when(g == 4)
            def _():
                for k in (1, 2, 3, 0):
                    scatter_o.plane(k)
                sum_chunk(1)
                far_arrived(0)
                y_load(SENT + 1, 0, 0, (0, 1))
                copies.arrived(first_got, ("first",), near.over_y)
                y_load(SENT, 0, 1, (0, 1))

            return carry

        lax.fori_loop(0, slabs, slab, 0)
        low = half_mask(tokens, False)

        def joined(sums, j):
            one, two = sums[2 * j], sums[2 * j + 1]
            one = one + pltpu.roll(one, HEAD_DIM, 1)
            two = two + pltpu.roll(two, HEAD_DIM, 1)
            return jnp.where(low, one, two)

        for j in range(kv_slabs):
            at = q_width + j * LANES
            whole = joined(dk, j) * SCORE_SCALE
            lin_grad[:, at : at + LANES] = (
                whole * cos[...] - rotate_halves(whole) * sin[...]
            ).astype(BF16)
            at = at + kv_width
            lin_grad[:, at : at + LANES] = joined(dv, j).astype(BF16)

    kv_shape = (2 * kv_slabs, tokens, LANES)
    pl.run_scoped(
        attention_part,
        *[pltpu.VMEM(((at + 1) * ROWS, ROWS), F32) for at in range(tokens // ROWS)],
        *[pltpu.VMEM(kv_shape, BF16)] * 4,
        *[pltpu.VMEM(kv_shape, F32)] * 2,
        pltpu.VMEM((tokens, LANES), F32),
    )

    def last_part(normed_turned, q_full, part):
        normed_in = copies.copy(lambda: (normed_hbm, normed_turned), "normed", False)
        weights_in = copies.copy(lambda: (q_hbm, q_full), "q weights", False)
        columns = jnp.concatenate(
            [
                small_sum[0:1, :], small_sum[8 : 8 + experts, :],
                jnp.zeros((LANES - 1 - experts, width), F32),
            ]
        ).T
        q_grad[:, :, qkv_width:] = columns.astype(BF16).reshape(16, block, LANES)
        normed_in()
        for k in (1, 2, 3, 0):
            spot = near.spots[k]
            rows = pl.ds(pl.multiple_of(spot * 4 * block, 4 * block), 4 * block)
            q_grad[pl.ds(spot * 4, 4), :, :qkv_width] = (
                dot(normed_turned[rows, :], lin_grad[...])
                .astype(BF16)
                .reshape(4, block, qkv_width)
            )
            scatter_q.begin(k)
        weights_in()

        def project(tile):
            rows = pl.ds(tile * ROWS, ROWS)
            for group in range(SLOTS):
                cols = slice(4 * block * group, 4 * block * (group + 1))
                weight = q_full[4 * group : 4 * (group + 1), :, :qkv_width]
                part[rows, cols] = dot(
                    lin_grad[rows, :], weight.reshape(4 * block, qkv_width), NT
                ).astype(BF16)
            copies.remote(
                lambda: (part.at[rows], part_got.at[rows]), ("n", tile), ("n", tile), near.twin,
                last=False,
            )

        project(0)
        project(1)
        for k in (1, 2, 3, 0):
            scatter_q.cross(k)
        y_sum(SENT + 1, 0, 0)
        y_sum(SENT, 0, 1)
        load_chunk(2)
        project(2)
        project(3)
        scatter_o.end()
        copies.arrived(mix_other.at[there], ("mo",), near.over_x)
        copies.remote(lambda: (mix_other.at[there],) * 2, ("m2",), ("m2",), near.twin)
        sum_chunk(2)
        for tile in range(tokens // ROWS):
            rows = pl.ds(tile * ROWS, ROWS)
            copies.arrived(part_got.at[rows], ("n", tile), near.twin)

        def finish_rows(t, side):
            for here in few_rows(STRIP):
                at = pl.ds(pl.multiple_of(t * STRIP + here.start, 16), 16)
                value = strips[0, side, here, :].astype(F32)
                inverse = lax.rsqrt(jnp.mean(value * value, axis=1, keepdims=True) + NORM_EPSILON)
                upstream = part[at, :].astype(F32) + part_got[at, :].astype(F32)
                scaled = value * inverse
                weighted = upstream * small[0:1, :]
                mean_term = jnp.mean(weighted * scaled, axis=1, keepdims=True)
                wide_out[side, here, :] = wide_in[side, here, :] + inverse * (
                    weighted - scaled * mean_term
                )

        over_strips([hidden_hbm], mid_grad, wide_out, input_grad, finish_rows)
        for k in (1, 2, 3, 0):
            scatter_q.plane(k)
        load_chunk(3)
        for tile in range(tokens // ROWS):
            rows = pl.ds(tile * ROWS, ROWS)
            copies.sent(lambda: (part.at[rows], part_got.at[rows]), ("n", tile), near.twin)

    pl.run_scoped(
        last_part,
        pltpu.VMEM((width, tokens), BF16), pltpu.VMEM(q_hbm.shape, BF16),
        pltpu.VMEM((tokens, width), BF16),
    )
    sum_chunk(3)
    copies.arrived(mix_twin, ("mt",), near.twin)
    copies.arrived(mix_other.at[not_there], ("m2",), near.twin)

    def mix_rows(t, side):
        for here in few_rows(STRIP):
            mix = strips[0, side, here, :].astype(F32) + strips[1, side, here, :].astype(F32)
            mix = mix + strips[2, side, here, :].astype(F32)
            strip_out[side, here, :] = (wide_in[side, here, :] + RESIDUAL_SCALE * mix).astype(BF16)

    over_strips([mix_pair, mix_twin, mix_other], middle_hbm, strip_out, block_out, mix_rows)
    scatter_q.end()
    for c in range(2 * SENT):
        copies.arrived(given_got.at[c], ("given", c), near.over_x)
    copies.finish()


def backward_pass(
    o_full, q, k, v, attended, lse, cosine, sine, segments, small, combine, gate_turned,
    q_full, normed, hidden, og, middle, dx, mix, keep, parts, near_grads, far_grads,
):
    tokens, width = hidden.shape
    q_width, kv_width = q.shape[1], k.shape[1]
    block, q_columns = q_full.shape[1:]
    qkv_width = q_width + 2 * kv_width
    pair, columns = keep[0].shape
    chunks = 2 * SENT
    experts = gate_turned.shape[0]
    anywhere, vmem = pl.BlockSpec(memory_space=pl.ANY), vmem_spec()
    shape = jax.ShapeDtypeStruct
    dma = pltpu.SemaphoreType.DMA
    inner = lax.axis_size("dp") // 16

    def scatter_scratch(total):
        split = total // (2 * LANES) * LANES
        return [
            pltpu.VMEM((SLOTS, block, split), BF16),
            pltpu.VMEM((SLOTS, block, total - split), BF16),
            pltpu.VMEM((SLOTS, block, total), BF16),
            pltpu.VMEM((SLOTS, block, total), BF16),
            pltpu.VMEM((SLOTS - 1, block, total), BF16),
        ]

    values = (
        o_full, q, k, v, attended, lse, cosine, sine, segments[:, None], segments[None, :],
        small, combine, gate_turned,
    )
    far_values = (
        q_full, normed, hidden, og, middle, *dx, mix, *keep, *parts, *near_grads, *far_grads,
    )
    return pl.pallas_call(
        functools.partial(backward_kernel, inner),
        in_specs=[vmem] * len(values) + [anywhere] * len(far_values),
        out_specs=[vmem] * 2 + [anywhere] * 11,
        out_shape=[
            shape((block, q_columns), F32),
            shape((block, q_width), F32),
            shape((tokens, width), F32),
            shape((tokens, width), BF16),
            shape((chunks, block, columns), F32),
            shape((chunks, block, columns), BF16),
            shape((tokens, width), F32),
            shape((SLOTS, pair, columns), BF16),
            shape((pair, columns), BF16),
            shape((SLOTS - 1, pair, columns), BF16),
            shape((SLOTS - 1, pair, columns), BF16),
            shape((tokens, width), BF16),
            shape((tokens, width), BF16),
        ],
        scratch_shapes=[
            pltpu.VMEM((tokens, q_width), BF16),
            pltpu.VMEM((tokens, qkv_width), BF16),
            pltpu.VMEM((16, block, q_width), BF16),
            pltpu.VMEM((16, block, q_columns), BF16),
        ]
        + scatter_scratch(q_width)
        + scatter_scratch(q_columns)
        + [
            pltpu.VMEM((tokens, width), BF16),
            pltpu.VMEM((SLOTS, pair, columns), BF16),
            pltpu.VMEM((SLOTS - 1, pair, columns), BF16),
            pltpu.VMEM((2, pair, columns), BF16),
            pltpu.VMEM((chunks, block, columns), BF16),
            pltpu.VMEM((2, block, columns), F32),
            pltpu.VMEM((4, 2, STRIP, width), BF16),
            pltpu.VMEM((2, STRIP, width), F32),
            pltpu.VMEM((2, STRIP, width), F32),
            pltpu.VMEM((2, STRIP, width), BF16),
            pltpu.VMEM((LANES, width), BF16),
            pltpu.VMEM((tokens, LANES), F32),
            pltpu.VMEM((8 + experts, width), F32),
            dma((80,)), dma((80,)), dma((60,)), dma((4, 2)), dma((2,)), dma((2,)),
        ],
        compiler_params=pltpu.CompilerParams(
            vmem_limit_bytes=EXPERT_VMEM, collective_id=2, has_side_effects=True
        ),
        name="backward_pass",
    )(*values, *far_values)


def whole_call(kernel, values, outs, earlier=(), name=None):
    return pl.pallas_call(
        with_earlier(kernel, len(values), len(earlier)),
        in_specs=[vmem_spec()] * len(values) + any_specs(earlier),
        out_specs=[vmem_spec()] * len(outs),
        out_shape=[jax.ShapeDtypeStruct(shape, dtype) for shape, dtype in outs],
        compiler_params=pltpu.CompilerParams(vmem_limit_bytes=VMEM_BYTES),
        name=name,
    )(*values, *earlier)


def fence_kernel(*refs):
    count = len(refs) // 2
    for value, out in zip(refs[:count], refs[count:]):
        out[...] = value[...]


def fence_all(values, *earlier):
    return whole_call(fence_kernel, values, [(v.shape, v.dtype) for v in values], earlier, "fence")


def fence(value, *earlier):
    return fence_all([value], *earlier)[0]


def sum_y_kernel(near, got, *outs):
    for k, out in enumerate(outs):
        out[...] = (near[k].astype(F32) + got[k].astype(F32)).astype(BF16)


def sum_y(near, got, *earlier):
    outs = [(near.shape[1:], BF16)] * SLOTS
    return whole_call(sum_y_kernel, [near, got], outs, earlier, "sum_y")


def sum_z_kernel(x_at, *refs):
    kept, given = refs[-2:]
    half = kept.shape[1]
    for c in range(kept.shape[0]):
        parts = refs[SLOTS * c : SLOTS * (c + 1)]
        for rows, out in ((x_at[0], kept), (1 - x_at[0], given)):
            rows = pl.ds(pl.multiple_of(rows * half, half), half)
            total = parts[0][rows, :].astype(F32)
            for part in parts[1:]:
                total = total + part[rows, :].astype(F32)
            out[c] = total.astype(out.dtype)


def sum_z(x_at, chunks, *earlier):
    count = len(chunks)
    pair, columns = chunks[0][0].shape
    flat = [part for parts in chunks for part in parts]
    return pl.pallas_call(
        with_earlier(sum_z_kernel, 1 + len(flat), len(earlier)),
        in_specs=[smem_spec()] + [vmem_spec()] * len(flat) + any_specs(earlier),
        out_specs=[vmem_spec()] * 2,
        out_shape=[
            jax.ShapeDtypeStruct((count, pair // 2, columns), F32),
            jax.ShapeDtypeStruct((count, pair // 2, columns), BF16),
        ],
        compiler_params=pltpu.CompilerParams(vmem_limit_bytes=VMEM_BYTES),
        name="sum_z",
    )(x_at, *flat, *earlier)


def sum_parts_kernel(parts, out):
    total = parts[0].astype(F32)
    for c in range(1, parts.shape[0]):
        total = total + parts[c].astype(F32)
    out[...] = total.astype(BF16)


def sum_parts(parts, *earlier):
    chunks, tokens, width = parts.shape
    return pl.pallas_call(
        with_earlier(sum_parts_kernel, 1, len(earlier)),
        grid=(tokens // EXPERT_ROWS,),
        in_specs=[pl.BlockSpec((chunks, EXPERT_ROWS, width), lambda s: (0, s, 0))]
        + any_specs(earlier),
        out_specs=pl.BlockSpec((EXPERT_ROWS, width), lambda s: (s, 0)),
        out_shape=jax.ShapeDtypeStruct((tokens, width), BF16),
        compiler_params=pltpu.CompilerParams(vmem_limit_bytes=VMEM_BYTES),
        name="sum_parts",
    )(parts, *earlier)


def adam_experts_kernel(x_at, kept, got, *refs):
    states, outs = refs[:6], refs[6:]
    own = kept.shape[1]
    hidden = states[0].shape[3]
    mine = pl.program_id(0) // (pl.num_programs(0) // 2) == x_at[0]
    grad = jnp.where(mine, kept[0], got[0].astype(F32))
    for e in range(CHUNK):
        for part in range(2):
            first = hidden * (2 * e + part)
            results = adam_update(
                states[0][e, part], grad[:, first : first + hidden],
                states[1][e, part], states[2][e, part], MODEL_DIM ** (-0.5), WEIGHT_DECAY,
            )
            for out, result in zip(outs[:3], results):
                out[e, part] = result
        first = hidden * (2 * CHUNK + e)
        results = adam_update(
            states[3][e], grad[:, first : first + hidden], states[4][e], states[5][e],
            max(1, F // 256) ** (-0.5), WEIGHT_DECAY,
        )
        for out, result in zip(outs[3:], results):
            out[e] = result


def adam_experts(x_at, kept, got, gateup, down):
    chunks, own, columns = kept.shape
    experts, hidden = down[0].shape[0], down[0].shape[2]
    share = pl.BlockSpec((1, own, columns), lambda j: (j % chunks, 0, 0))
    big = pl.BlockSpec((CHUNK, 2, own, hidden), lambda j: (j, 0, 0, 0))
    small = pl.BlockSpec((CHUNK, own, hidden), lambda j: (j, 0, 0))
    return pl.pallas_call(
        adam_experts_kernel,
        grid=(experts // CHUNK,),
        in_specs=[smem_spec(), share, share] + [big] * 3 + [small] * 3,
        out_specs=[big] * 3 + [small] * 3,
        out_shape=[jax.ShapeDtypeStruct(gateup[0].shape, F32)] * 3
        + [jax.ShapeDtypeStruct(down[0].shape, F32)] * 3,
        compiler_params=pltpu.CompilerParams(vmem_limit_bytes=VMEM_BYTES),
        name="adam_experts",
    )(x_at, kept, got, *gateup, *down)


def join_tokens_kernel(own, first, second, out, turned):
    half = own.shape[0] // 2
    for at, part in ((0, own[:half, :]), (half, own[half:, :]), (2 * half, first[...]), (3 * half, second[...])):
        out[at : at + half, :] = part
        turned[:, at : at + half] = part.T


def join_tokens(own, first, second, *earlier):
    tokens, width = own.shape
    return pl.pallas_call(
        with_earlier(join_tokens_kernel, 3, len(earlier)),
        in_specs=[vmem_spec()] * 3 + any_specs(earlier),
        out_specs=[vmem_spec()] * 2,
        out_shape=[
            jax.ShapeDtypeStruct((2 * tokens, width), own.dtype),
            jax.ShapeDtypeStruct((width, 2 * tokens), own.dtype),
        ],
        compiler_params=pltpu.CompilerParams(vmem_limit_bytes=VMEM_BYTES),
        name="join_tokens",
    )(own, first, second, *earlier)


def move(array, dz=0, dy=0, dx=0):
    total = lax.axis_size("dp")
    inner = total // 16
    pairs = []
    for at in range(16):
        z, y, x = at // 4, at // 2 % 2, at % 2
        to = ((z + dz) % 4) * 4 + (y ^ dy) * 2 + (x ^ dx)
        pairs += [(at * inner + i, to * inner + i) for i in range(inner)]
    return lax.ppermute(array, "dp", pairs)


def place():
    at = lax.axis_index("dp") // (lax.axis_size("dp") // 16)
    return at // 4, at // 2 % 2, at % 2


def inner_groups(total):
    inner = total // 16
    return [[at * inner + i for i in range(inner)] for at in range(16)]


def inner_gather(shard, axis):
    total = lax.axis_size("dp")
    if total == 16:
        return shard
    return lax.all_gather(
        shard, "dp", axis=axis, tiled=True, axis_index_groups=inner_groups(total)
    )


def inner_scatter(share, axis):
    total = lax.axis_size("dp")
    if total == 16:
        return share
    return lax.psum_scatter(
        share, "dp", scatter_dimension=axis, tiled=True, axis_index_groups=inner_groups(total)
    )


def block_rows(parts, rows):
    z, y, x = place()
    starts = []
    for dz, dy, dx in parts:
        starts.append((((z + dz + 4) % 4) * 4 + (y ^ dy) * 2 + (x ^ dx)) * rows)
    return jnp.stack(starts).astype(jnp.int32)


def gather_z(shard):
    return jnp.stack([shard] + [move(shard, dz=-dz) for dz in Z_FROM[1:]])


def gather_ring(shard):
    below, above = move(shard, dz=1), move(shard, dz=-1)
    return [shard, below, above, move(below, dz=1)]


def send_z(parts):
    return [move(parts[k].astype(BF16), dz=Z_FROM[k]) for k in range(1, SLOTS)]


def scatter_z(parts, moved=None):
    result = parts[0]
    for one in moved or send_z(parts):
        result = result + one.astype(F32)
    return result


def gather_plane(own):
    half = own.shape[-1] // 2
    along_y, along_x = move(own, dy=1), move(own, dx=1)
    both = (move(along_y[..., :half], dx=1), move(along_x[..., half:], dy=1))
    return own, along_y, along_x, *both


def scatter_plane(pieces):
    own, along_y, along_x, both_one, both_two = pieces
    half = both_one.shape[-1]
    got_one, got_two = move(both_one, dx=1), move(both_two, dy=1)
    pass_y = jnp.concatenate(
        [(along_y[..., :half].astype(F32) + got_one.astype(F32)).astype(BF16), along_y[..., half:]],
        axis=-1,
    )
    pass_x = jnp.concatenate(
        [along_x[..., :half], (along_x[..., half:].astype(F32) + got_two.astype(F32)).astype(BF16)],
        axis=-1,
    )
    got_y, got_x = move(pass_y, dy=1), move(pass_x, dx=1)
    return scatter_z(
        [
            own[k].astype(F32) + got_y[k].astype(F32) + got_x[k].astype(F32)
            for k in range(SLOTS)
        ]
    )


PLANE = [(dz, dy, dx) for dy, dx in ((0, 0), (1, 0), (0, 1), (1, 1)) for dz in Z_FROM]


def join_kernel(rows_at, *refs):
    pieces, out = refs[:-1], refs[-1]
    slots, own, width = pieces[0].shape
    half = width // 2
    for at in range(4 * slots):
        rows = pl.ds(pl.multiple_of(rows_at[at], own), own)
        group, slot = at // slots, at % slots
        if group < 3:
            out[rows, :] = pieces[group][slot]
        else:
            out[rows, :half] = pieces[3][slot]
            out[rows, half:] = pieces[4][slot]


def part_kernel(rows_at, whole, *pieces):
    slots, own, width = pieces[0].shape
    half = width // 2
    for at in range(4 * slots):
        rows = pl.ds(pl.multiple_of(rows_at[at], own), own)
        group, slot = at // slots, at % slots
        if group < 3:
            pieces[group][slot] = whole[rows, :]
        else:
            pieces[3][slot] = whole[rows, :half]
            pieces[4][slot] = whole[rows, half:]


def smem_spec():
    return pl.BlockSpec(memory_space=pltpu.SMEM)


def vmem_spec():
    return pl.BlockSpec(memory_space=pltpu.VMEM)


def join_blocks(rows_at, pieces, earlier=()):
    slots, own, width = pieces[0].shape
    return pl.pallas_call(
        with_earlier(join_kernel, 6, len(earlier)),
        in_specs=[smem_spec()] + [vmem_spec()] * 5 + any_specs(earlier),
        out_specs=vmem_spec(),
        out_shape=jax.ShapeDtypeStruct((4 * slots * own, width), BF16),
        compiler_params=pltpu.CompilerParams(vmem_limit_bytes=VMEM_BYTES),
        name="join_blocks",
    )(rows_at, *pieces, *earlier)


def part_blocks(rows_at, whole, earlier=()):
    own, width = whole.shape[0] // (4 * SLOTS), whole.shape[1]
    full = jax.ShapeDtypeStruct((SLOTS, own, width), BF16)
    half = jax.ShapeDtypeStruct((SLOTS, own, width // 2), BF16)
    return pl.pallas_call(
        with_earlier(part_kernel, 2, len(earlier)),
        in_specs=[smem_spec(), vmem_spec()] + any_specs(earlier),
        out_specs=[vmem_spec()] * 5,
        out_shape=[full] * 3 + [half] * 2,
        compiler_params=pltpu.CompilerParams(vmem_limit_bytes=VMEM_BYTES),
        name="part_blocks",
    )(rows_at, whole, *earlier)


def after(value, *earlier):
    marks = []
    for one in earlier:
        slots = one.shape[0] if one.shape[0] == SLOTS else 1
        lead, rest = (slots > 1) * 1, one.ndim - 1
        marks.append(lax.slice(one, (lead,) + (0,) * rest, (slots,) + (1,) * rest))
    return lax.optimization_barrier((value, *marks))[0]


def split_three(values):
    high = values.astype(BF16)
    rest = values - high.astype(F32)
    middle = rest.astype(BF16)
    low = (rest - middle.astype(F32)).astype(BF16)
    return [high, middle, low]


def swap_cores(part):
    return lax.ppermute(part, "tensor", [(0, 1), (1, 0)])


def pair_sum(part):
    return part.astype(F32) + swap_cores(part).astype(F32)


def norm_backward(values, inverse, gain_row, upstream):
    scaled = values * inverse
    weighted = upstream * gain_row
    mean_term = jnp.mean(weighted * scaled, axis=-1, keepdims=True)
    return (inverse * (weighted - scaled * mean_term), jnp.sum(upstream * scaled, axis=0))


def adam_update(value, gradient, mean_old, square_old, rate, decay):
    mean_new = FIRST_DECAY * mean_old + (1.0 - FIRST_DECAY) * gradient
    square_new = SECOND_DECAY * square_old + (1.0 - SECOND_DECAY) * gradient * gradient
    mean_hat = mean_new / (1.0 - FIRST_DECAY**STEP)
    square_hat = square_new / (1.0 - SECOND_DECAY**STEP)
    updated = value - rate * (mean_hat / (jnp.sqrt(square_hat) + ADAM_EPSILON) + decay * value)
    return (mean_new, square_new, updated)


def shards(
    hidden_in,
    out_grad,
    routes,
    segments,
    norm_gains,
    gains_mean,
    gains_square,
    w_query,
    query_mean,
    query_square,
    key_value_weight,
    key_value_first_moment,
    key_value_second_moment,
    w_out,
    out_mean,
    out_square,
    w_router,
    router_mean,
    router_square,
    w_gateup,
    gateup_mean,
    gateup_square,
    w_down,
    down_mean,
    down_square,
):
    tokens, width = hidden_in.shape
    own = w_query.shape[0]
    experts, hidden = w_down.shape[0], w_down.shape[1]
    q_width, kv_width = w_query.shape[1], key_value_weight.shape[2]
    qkv_width = q_width + 2 * kv_width
    each = 2 + experts
    half_experts = experts // 2
    block = width // 16
    z_at, y_at, x_at = place()
    core = lax.axis_index("tensor")
    plane_rows = block_rows(PLANE, block)
    qkv_shard = jnp.concatenate(
        [w_query.astype(BF16), key_value_weight[0].astype(BF16), key_value_weight[1].astype(BF16)]
        + split_three(jnp.concatenate([norm_gains.T, w_router], axis=1))
        + [jnp.zeros((own, LANES - 3 * each), BF16)],
        axis=1,
    )
    out_shard = w_out.T.astype(BF16)
    turned_down = [one.transpose(0, 2, 1) for one in (w_down, down_mean, down_square)]
    gateup_rows, down_rows = w_gateup, turned_down[0]
    if lax.axis_size("dp") > 16:
        gateup_rows = inner_gather(w_gateup.astype(BF16), 2)
        down_rows = inner_gather(down_rows.astype(BF16), 1)
    chunks = experts // (2 * CHUNK)
    first = x_at == 0
    cosine, sine = rope_tables(seq_positions(segments))
    (
        qkv_blocks, out_blocks, small, normed_low, queries, keys, values, attended, lse,
        combine, combine_pair, middle, x_pair, x_turned, og_pair, og_turned, pairs, near, far,
    ) = forward_pass(
        inner_gather(qkv_shard, 0), inner_gather(out_shard, 0), gateup_rows, down_rows,
        hidden_in, out_grad, cosine, sine, segments, routes,
    )
    dx, mix_pair, gate_turned, keep, z_got, near_grads, far_grads = experts_pass(
        x_pair, og_pair, x_turned, og_turned, combine_pair, pairs, near, far
    )
    qkv_share, output_share, input_grad, block_out, kept_share, got_share = backward_pass(
        out_blocks, queries, keys, values, attended, lse, cosine, sine, segments, small, combine,
        gate_turned, qkv_blocks, normed_low, hidden_in, out_grad, middle, dx, mix_pair, keep,
        z_got, near_grads, far_grads,
    )[:6]
    kept_share, got_share = inner_scatter(kept_share, 1), inner_scatter(got_share, 1)
    x_here = x_at.astype(jnp.int32)[None]
    output_share = inner_scatter(output_share, 0).T
    qkv_share = inner_scatter(qkv_share, 0)
    query_share = qkv_share[:, :q_width]
    keyval_share = jnp.stack(
        [qkv_share[:, q_width : q_width + kv_width], qkv_share[:, q_width + kv_width : qkv_width]]
    )
    gain_one_part = jnp.sum(w_query.astype(BF16).astype(F32) * query_share, axis=1) + jnp.sum(
        key_value_weight.astype(BF16).astype(F32) * keyval_share, axis=(0, 2)
    )
    gain_one_share = pair_sum(gain_one_part[None, :]) / norm_gains[:1]
    gains_share = jnp.concatenate([gain_one_share, qkv_share[:, qkv_width][None, :]])
    router_share = qkv_share[:, qkv_width + 1 : qkv_width + 1 + experts]

    gains_result = adam_update(norm_gains, gains_share, gains_mean, gains_square, GAIN_RATE, 0.0)
    query_result = adam_update(
        w_query, query_share, query_mean, query_square, (MODEL_DIM // 12) ** (-0.5), WEIGHT_DECAY
    )
    keyval_result = adam_update(
        key_value_weight,
        keyval_share,
        key_value_first_moment,
        key_value_second_moment,
        (MODEL_DIM // 12) ** (-0.5),
        WEIGHT_DECAY,
    )
    out_result = adam_update(
        w_out,
        output_share,
        out_mean,
        out_square,
        max(1, QUERY_HEADS * HEAD_DIM // 96) ** (-0.5),
        WEIGHT_DECAY,
    )
    router_result = adam_update(
        w_router, router_share, router_mean, router_square, (4 * MODEL_DIM) ** (-0.5), WEIGHT_DECAY
    )
    expert_results = adam_experts(
        x_here, kept_share, got_share,
        (w_gateup, gateup_mean, gateup_square), turned_down,
    )
    expert_results = [*expert_results[:3], *(one.transpose(0, 2, 1) for one in expert_results[3:])]
    return (
        (block_out, input_grad)
        + gains_result
        + query_result
        + keyval_result
        + out_result
        + router_result
        + tuple(expert_results)
    )


def solution(mesh):
    tokens, gains = P("dp", None), P(None, "dp")
    query, keyval, out = P("dp", "tensor"), P(None, "dp", "tensor"), P("tensor", "dp")
    router, gateup, down = P("dp", None), P(None, None, "dp", "tensor"), P(None, "tensor", "dp")
    states = tuple(
        spec for one in (gains, query, keyval, out, router, gateup, down) for spec in (one,) * 3
    )
    return jax.shard_map(
        shards,
        mesh=mesh,
        in_specs=(tokens, tokens, tokens, P("dp")) + states,
        out_specs=(tokens, tokens) + states,
        check_vma=False,
    )
```

```python
import functools

import jax
import jax.numpy as jnp
from jax import lax
from jax.experimental import pallas as pl
from jax.experimental.pallas import tpu as pltpu
from jax.sharding import PartitionSpec as P

MODEL_DIM = 1536
QUERY_HEADS = 24
HEAD_DIM = 64
F = 512
SEQUENCE_LENGTH = 1024
STEP = 10

NORM_EPSILON = 1e-06
SCORE_SCALE = 0.015625
RESIDUAL_SCALE = 0.22
ROPE_BASE = 10000.0
FIRST_DECAY = 0.9
SECOND_DECAY = 0.95
ADAM_EPSILON = 1e-08
WEIGHT_DECAY = 0.1
GAIN_RATE = 0.6
MASK_VALUE = -1e30
HIGHEST_PRECISION = lax.Precision.HIGHEST

BF16 = jnp.bfloat16
F32 = jnp.float32
LANES = 128
ROWS = 256
VMEM_BYTES = 58 * 1024 * 1024

NN = (((1,), (0,)), ((), ()))
NT = (((1,), (1,)), ((), ()))
TN = (((0,), (0,)), ((), ()))


def dot(a, b, dims=NN):
    return lax.dot_general(a, b, dims, preferred_element_type=F32)


def seq_positions(segment_row):
    counter = jnp.arange(segment_row.shape[0], dtype=jnp.int32)
    earlier = jnp.concatenate([segment_row[:1] - 1, segment_row[:-1]])
    starts = lax.cummax(jnp.where(segment_row != earlier, counter, 0), axis=0)
    return counter - starts


def rope_tables(positions):
    half_width = HEAD_DIM // 2
    frequency = ROPE_BASE ** (-2.0 * jnp.arange(half_width, dtype=F32) / HEAD_DIM)
    angles = positions.astype(F32)[:, None] * frequency[None, :]
    cosine, sine = jnp.cos(angles), jnp.sin(angles)
    return (
        jnp.concatenate([cosine] * 4, axis=1),
        jnp.concatenate([-sine, sine] * 2, axis=1),
    )


def rotate_halves(slab):
    lane = lax.broadcasted_iota(jnp.int32, slab.shape, 1)
    ahead = pltpu.roll(slab, LANES - HEAD_DIM // 2, 1)
    behind = pltpu.roll(slab, HEAD_DIM // 2, 1)
    return jnp.where(lane % HEAD_DIM < HEAD_DIM // 2, ahead, behind)


def few_rows(count, base=None):
    for r in range(0, count, 16):
        yield pl.ds(r, 16) if base is None else pl.ds(pl.multiple_of(base + r, 16), 16)


def half_mask(rows, upper):
    lane = lax.broadcasted_iota(jnp.int32, (rows, LANES), 1)
    return (lane >= HEAD_DIM) if upper else (lane < HEAD_DIM)


def spread_heads(slab, lower_out, upper_out, index):
    rows = slab.shape[0]
    moved = pltpu.roll(slab.astype(F32), HEAD_DIM, 1).astype(BF16)
    zero = jnp.zeros_like(slab)
    low, high = half_mask(rows, False), half_mask(rows, True)
    lower_out[index] = jnp.where(low, slab, zero)
    upper_out[index] = jnp.where(high, moved, zero)
    lower_out[index + 1] = jnp.where(low, moved, zero)
    upper_out[index + 1] = jnp.where(high, slab, zero)


def fill_bias(bias, seg_col, seg_row):
    span = bias.shape[0]
    for at in range(0, span, ROWS):
        rows_at = at + lax.broadcasted_iota(jnp.int32, (ROWS, span), 0)
        cols_at = lax.broadcasted_iota(jnp.int32, (ROWS, span), 1)
        allowed = (rows_at >= cols_at) & (seg_col[at : at + ROWS, :] == seg_row[...])
        bias[at : at + ROWS, :] = jnp.where(allowed, 0.0, MASK_VALUE).astype(F32)


def with_earlier(kernel, inputs, count):
    def run(*refs):
        kernel(*refs[:inputs], *refs[inputs + count :])

    return run


def any_specs(arrays):
    return [pl.BlockSpec(memory_space=pl.ANY)] * len(arrays)


def attention_forward_kernel(
    lin_ref, kv_ref, cos_ref, sin_ref, seg_col, seg_row,
    out_ref, q_ref, k_ref, v_ref, lse_ref,
    bias, k_low, k_high, v_low, v_high,
):
    slab_at = pl.program_id(0)
    span = lin_ref.shape[0]
    kv_slabs = kv_ref.shape[1] // (2 * LANES)

    @pl.when(slab_at == 0)
    def _():
        fill_bias(bias, seg_col, seg_row)
        for j in range(kv_slabs):
            lanes = slice(j * LANES, (j + 1) * LANES)
            lin = kv_ref[:, lanes]
            keys = (lin * cos_ref[...] + rotate_halves(lin) * sin_ref[...]).astype(BF16)
            k_ref[:, lanes] = keys
            spread_heads(keys, k_low, k_high, 2 * j)
            lanes = slice((kv_slabs + j) * LANES, (kv_slabs + j + 1) * LANES)
            values = kv_ref[:, lanes].astype(BF16)
            v_ref[:, slice(j * LANES, (j + 1) * LANES)] = values
            spread_heads(values, v_low, v_high, 2 * j)

    lin = lin_ref[...]
    q_ref[...] = (lin * cos_ref[...] + rotate_halves(lin) * sin_ref[...]).astype(BF16)
    kv_even, kv_odd = (2 * slab_at) // 3, (2 * slab_at + 1) // 3
    for at in range(0, span, ROWS):
        rows = slice(at, at + ROWS)
        queries = q_ref[rows, :]
        total = None
        stats = []
        for keys, values, kv_at in ((k_low, v_low, kv_even), (k_high, v_high, kv_odd)):
            upto = at + ROWS
            scores = dot(queries, keys[kv_at, :upto, :], NT) * SCORE_SCALE + bias[rows, :upto]
            highest = jnp.max(scores, axis=1, keepdims=True)
            weights = jnp.exp(scores - highest)
            summed = jnp.sum(weights, axis=1, keepdims=True)
            probability = (weights * (1.0 / summed)).astype(BF16)
            part = dot(probability, values[kv_at, :upto, :])
            total = part if total is None else total + part
            stats.append(highest + jnp.log(summed))
        out_ref[rows, :] = total.astype(BF16)
        spread = jnp.where(half_mask(ROWS, False), stats[0], stats[1])
        turned = spread.T
        lse_ref[0, 0:1, rows] = turned[0:1, :]
        lse_ref[0, 1:2, rows] = turned[HEAD_DIM : HEAD_DIM + 1, :]


def attention_forward(qkv_lin, cosine, sine, segment_row, earlier=()):
    span = qkv_lin.shape[0]
    q_width = MODEL_DIM // 2
    kv_width = (qkv_lin.shape[1] - q_width) // 2
    slabs, kv_heads = q_width // LANES, kv_width // HEAD_DIM
    whole = lambda shape: pl.BlockSpec(shape, lambda g: (0,) * len(shape))
    slab = pl.BlockSpec((span, LANES), lambda g: (0, g))
    q_lin, kv_lin = qkv_lin[:, :q_width], qkv_lin[:, q_width:]
    return pl.pallas_call(
        with_earlier(attention_forward_kernel, 6, len(earlier)),
        grid=(slabs,),
        in_specs=[
            slab, whole((span, 2 * kv_width)), whole((span, LANES)), whole((span, LANES)),
            whole((span, 1)), whole((1, span)),
        ]
        + any_specs(earlier),
        out_specs=[
            slab, slab, whole((span, kv_width)), whole((span, kv_width)),
            pl.BlockSpec((1, 8, span), lambda g: (g, 0, 0)),
        ],
        out_shape=[
            jax.ShapeDtypeStruct((span, q_width), BF16),
            jax.ShapeDtypeStruct((span, q_width), BF16),
            jax.ShapeDtypeStruct((span, kv_width), BF16),
            jax.ShapeDtypeStruct((span, kv_width), BF16),
            jax.ShapeDtypeStruct((slabs, 8, span), F32),
        ],
        scratch_shapes=[pltpu.VMEM((span, span), F32)]
        + [pltpu.VMEM((kv_heads, span, LANES), BF16)] * 4,
        compiler_params=pltpu.CompilerParams(vmem_limit_bytes=VMEM_BYTES),
        cost_estimate=pl.CostEstimate(
            flops=32 * slabs * span * span * LANES, bytes_accessed=16 * span * q_width,
            transcendentals=slabs * span * span,
        ),
        name="attention_forward",
    )(q_lin, kv_lin, cosine, sine, segment_row[:, None], segment_row[None, :], *earlier)


def attention_backward_kernel(
    q_ref, k_ref, v_ref, out_ref, grad_ref, cos_ref, sin_ref, seg_col, seg_row, lse_ref,
    dq_ref, dkv_ref,
    bias, k_low, k_high, v_low, v_high, dk_low, dk_high, dv_low, dv_high, dq_sum,
):
    slab_at = pl.program_id(0)
    span = q_ref.shape[0]
    kv_slabs = k_ref.shape[1] // LANES

    @pl.when(slab_at == 0)
    def _():
        for at in range(0, span, ROWS):
            keys_at = at + lax.broadcasted_iota(jnp.int32, (ROWS, span), 0)
            rows_at = lax.broadcasted_iota(jnp.int32, (ROWS, span), 1)
            allowed = (rows_at >= keys_at) & (seg_col[at : at + ROWS, :] == seg_row[...])
            bias[at : at + ROWS, :] = jnp.where(allowed, 0.0, MASK_VALUE).astype(F32)
        for j in range(kv_slabs):
            lanes = slice(j * LANES, (j + 1) * LANES)
            spread_heads(k_ref[:, lanes], k_low, k_high, 2 * j)
            spread_heads(v_ref[:, lanes], v_low, v_high, 2 * j)
        for sums in (dk_low, dk_high, dv_low, dv_high):
            sums[...] = jnp.zeros_like(sums)

    kv_even, kv_odd = (2 * slab_at) // 3, (2 * slab_at + 1) // 3
    for at in range(0, span, ROWS):
        rows = slice(at, at + ROWS)
        upto = at + ROWS
        queries, grads = q_ref[rows, :], grad_ref[rows, :]
        turned = (grads.astype(F32) * out_ref[rows, :].astype(F32)).T
        zero = jnp.zeros_like(queries)
        dq_part = None
        for upper, keys, values, dk_sum, dv_sum, kv_at in (
            (False, k_low, v_low, dk_low, dv_low, kv_even),
            (True, k_high, v_high, dk_high, dv_high, kv_odd),
        ):
            first = HEAD_DIM if upper else 0
            delta = jnp.sum(turned[first : first + HEAD_DIM, :], axis=0, keepdims=True)
            head = 1 if upper else 0
            total = lse_ref[0, head : head + 1, rows]
            keys_here = keys[kv_at, :upto, :]
            scores = dot(keys_here, queries, NT) * SCORE_SCALE + bias[:upto, rows]
            probability = jnp.exp(scores - total)
            prob_grad = dot(values[kv_at, :upto, :], grads, NT)
            score_grad = (probability * (prob_grad - delta)).astype(BF16)
            mask = half_mask(ROWS, upper)
            dv_sum[kv_at, :upto, :] += dot(
                probability.astype(BF16), jnp.where(mask, grads, zero)
            )
            dk_sum[kv_at, :upto, :] += dot(score_grad, jnp.where(mask, queries, zero))
            part = dot(score_grad, keys_here, TN)
            dq_part = part if dq_part is None else dq_part + part
        dq_sum[rows, :] = dq_part * SCORE_SCALE
    slab = dq_sum[...]
    dq_ref[...] = (slab * cos_ref[...] - rotate_halves(slab) * sin_ref[...]).astype(BF16)

    @pl.when(slab_at == pl.num_programs(0) - 1)
    def _():
        low = half_mask(span, False)

        def joined(sums_low, sums_high, j):
            one = sums_low[2 * j] + pltpu.roll(sums_high[2 * j], HEAD_DIM, 1)
            two = pltpu.roll(sums_low[2 * j + 1], HEAD_DIM, 1) + sums_high[2 * j + 1]
            return jnp.where(low, one, two)

        for j in range(kv_slabs):
            slab = joined(dk_low, dk_high, j) * SCORE_SCALE
            dkv_ref[:, j * LANES : (j + 1) * LANES] = (
                slab * cos_ref[...] - rotate_halves(slab) * sin_ref[...]
            ).astype(BF16)
            at = (kv_slabs + j) * LANES
            dkv_ref[:, at : at + LANES] = joined(dv_low, dv_high, j).astype(BF16)


def attention_backward(
    queries, keys, values, attended, grad, cosine, sine, segment_row, lse, earlier=()
):
    span, q_width = queries.shape
    kv_width = keys.shape[1]
    slabs, kv_heads = q_width // LANES, kv_width // HEAD_DIM
    whole = lambda shape: pl.BlockSpec(shape, lambda g: (0,) * len(shape))
    slab = pl.BlockSpec((span, LANES), lambda g: (0, g))
    return pl.pallas_call(
        with_earlier(attention_backward_kernel, 10, len(earlier)),
        grid=(slabs,),
        in_specs=[
            slab, whole((span, kv_width)), whole((span, kv_width)), slab, slab,
            whole((span, LANES)), whole((span, LANES)), whole((span, 1)), whole((1, span)),
            pl.BlockSpec((1, 8, span), lambda g: (g, 0, 0)),
        ]
        + any_specs(earlier),
        out_specs=[slab, whole((span, 2 * kv_width))],
        out_shape=[
            jax.ShapeDtypeStruct((span, q_width), BF16),
            jax.ShapeDtypeStruct((span, 2 * kv_width), BF16),
        ],
        scratch_shapes=[pltpu.VMEM((span, span), F32)]
        + [pltpu.VMEM((kv_heads, span, LANES), BF16)] * 4
        + [pltpu.VMEM((kv_heads, span, LANES), F32)] * 4
        + [pltpu.VMEM((span, LANES), F32)],
        compiler_params=pltpu.CompilerParams(vmem_limit_bytes=VMEM_BYTES),
        cost_estimate=pl.CostEstimate(
            flops=40 * slabs * span * span * LANES, bytes_accessed=16 * span * q_width,
            transcendentals=slabs * span * span,
        ),
        name="attention_backward",
    )(
        queries, keys, values, attended, grad, cosine, sine,
        segment_row[:, None], segment_row[None, :], lse, *earlier,
    )


EXPERT_ROWS = 256
EXPERT_VMEM = 63 * 1024 * 1024
SLOTS = 4
Z_FROM = (0, -1, 1, 2)
CHUNK = 2
LATE = 2
SENT = 2
MESH_ID = pl.DeviceIdType.MESH


def experts_kernel(
    inner, chunks, row_steps, x_ref, og_ref, xt_ref, ogt_ref, combine_ref,
    pairs_ref, near_ref, far_ref,
    dx_own, dx_twin, dx_other, mix_out, gate_out, *refs,
):
    keep_outs, refs = refs[:SENT], refs[SENT:]
    part_outs, refs = refs[:SENT], refs[SENT:]
    near_outs, refs = refs[: chunks - SENT], refs[chunks - SENT :]
    late_out, first_out, far_out, refs = *refs[:3], refs[3:]
    slots, arrived, held_both, held_down, dx_sum, mix_sum, twin_rows, twin_mix = refs[:8]
    gates, gate_kept, gate_got, gate_full, gate_twin, send, recv, local = refs[8:]
    weights, grads = slots.at[pl.ds(1, chunks)], slots
    near = Neighbours(inner)
    copies = Copies(send, recv, local)
    z, y, x, core, spots = near.z, near.y, near.x, near.core, near.spots
    step = pl.program_id(0)
    steps = row_steps + SLOTS
    chunk, turn = step // steps, step % steps
    last = chunks - 1
    width = x_ref.shape[1]
    block = width // 16
    hidden = held_down.shape[1] // CHUNK
    both = 2 * hidden * CHUNK
    lane = lax.broadcasted_iota(jnp.int32, (EXPERT_ROWS, LANES), 1)
    tokens = dx_sum.shape[0] // 2
    tiles = tokens // EXPERT_ROWS
    tile = (turn + tiles) % row_steps
    rows = pl.ds(pl.multiple_of(tile * EXPERT_ROWS, EXPERT_ROWS), EXPERT_ROWS)

    def near_piece(c, k):
        return pairs_ref.at[c] if k == 0 else near_ref.at[c, k - 1]

    def near_copy(c, k):
        copies.copy(
            lambda c=c, k=k: (near_piece(c, k), weights.at[c, spots[k], y]), ("near", c, k), False
        )

    def near_wait(c, k):
        copies.wait_copy(
            lambda c=c, k=k: (near_piece(c, k), weights.at[c, spots[k], y]), ("near", c, k)
        )

    def far_ends(c, k):
        return far_ref.at[c, k], weights.at[c, spots[k], 1 - y]

    @pl.when(step == 0)
    def _():
        near.greet()
        gates[...] = jnp.zeros_like(gates)
        for k in range(SLOTS):
            near_copy(0, k)
            copies.copy(lambda k=k: far_ends(0, k), ("far", 0, k), False)
        copies.remote(
            lambda: (pairs_ref.at[last], weights.at[last, z, y]), ("y",), ("y",), near.over_y
        )
        for k in range(1, SLOTS):
            copies.remote(
                lambda: (pairs_ref.at[last], weights.at[last, z, y]),
                ("z", k), ("z", BACK[k]), near.along[k],
            )
        for c in range(LATE, last):
            for k in range(1, SLOTS):
                copies.remote(
                    lambda c=c, k=k: (near_piece(c, k), weights.at[c, spots[k], y]),
                    ("f", c, k), ("f", c, k), near.over_y,
                )
        for c in range(1, chunks):
            for k in range(SLOTS if c < last else 1):
                near_copy(c, k)
                if c < LATE or (c < last and k == 0):
                    copies.copy(lambda c=c, k=k: far_ends(c, k), ("far", c, k), False)

    @pl.when(step == steps)
    def _():
        copies.arrived(weights.at[last, z, 1 - y], ("y",), near.over_y)
        for k in range(1, SLOTS):
            copies.remote(
                lambda: (weights.at[last, z, 1 - y],) * 2,
                ("z2", k), ("z2", BACK[k]), near.along[k],
            )

    for c in range(chunks):

        @pl.when(step == c * steps)
        def _():
            for k in range(SLOTS):
                if c < last or k == 0:
                    near_wait(c, k)
                if c < LATE or (c < last and k == 0):
                    copies.wait_copy(lambda c=c, k=k: far_ends(c, k), ("far", c, k))
                elif c < last:
                    copies.arrived(weights.at[c, spots[k], 1 - y], ("f", c, k), near.over_y)
                elif k > 0:
                    copies.arrived(weights.at[c, spots[k], y], ("z", k), near.along[k])
                    copies.arrived(weights.at[c, spots[k], 1 - y], ("z2", k), near.along[k])

    def add_arrived(c):
        copies.arrived(arrived.at[c], ("sum", c), near.over_y)
        for k in range(SLOTS):
            own = grads.at[c, spots[k], y]
            for here in few_rows(own.shape[0]):
                own[here, :] = (
                    own[here, :].astype(F32) + arrived[c, spots[k], here, :].astype(F32)
                ).astype(BF16)
        copies.copy(lambda c=c: (grads.at[c, z, y], keep_outs[c]), ("keep", c))
        for k in range(1, SLOTS):
            copies.remote(
                lambda c=c, k=k: (grads.at[c, spots[k], y], part_outs[c].at[BACK[k] - 1]),
                ("part", c, k), ("part", c, BACK[k]), near.along[k],
            )

    @pl.when(step == 2 * steps + 3)
    def _():
        add_arrived(0)

    @pl.when(step == 3 * steps + 3)
    def _():
        add_arrived(1)

    @pl.when(turn < row_steps)
    def _():
        for e in range(CHUNK):
            first = 2 * hidden * e
            w_both = weights[chunk, :, :, :, first : first + 2 * hidden].reshape(width, 2 * hidden)
            start = both + hidden * e
            w_down = weights[chunk, :, :, :, start : start + hidden].reshape(width, hidden)
            gate_up = dot(x_ref[...], w_both)
            raw = dot(og_ref[...], w_down) * RESIDUAL_SCALE
            gate, up = gate_up[:, :hidden], gate_up[:, hidden:]
            gate_lane = lax.broadcasted_iota(
                jnp.int32, (EXPERT_ROWS, combine_ref.shape[1]), 1
            )
            column = jnp.sum(
                jnp.where(gate_lane == chunk * CHUNK + e, combine_ref[...], 0.0),
                axis=1, keepdims=True,
            )
            sigmoid = 1.0 / (1.0 + jnp.exp(-gate))
            active = gate * sigmoid
            inner_value = (active * up).astype(BF16).astype(F32)
            held_down[rows, hidden * e : hidden * (e + 1)] = (inner_value * column).astype(BF16)
            gates[rows, :] = jnp.where(
                lane == chunk * CHUNK + e,
                jnp.sum(inner_value * raw, axis=1, keepdims=True),
                gates[rows, :],
            )
            inner_grad = raw * column
            held_both[rows, first : first + hidden] = (
                inner_grad * up * sigmoid * (1.0 + gate * (1.0 - sigmoid))
            ).astype(BF16)
            held_both[rows, first + hidden : first + 2 * hidden] = (inner_grad * active).astype(BF16)

        def sums(add):
            for part in range(SLOTS):
                cols = slice(4 * block * part, 4 * block * (part + 1))
                w_both = weights[chunk, part, :, :, :both].reshape(4 * block, both)
                w_down = weights[chunk, part, :, :, both:].reshape(4 * block, hidden * CHUNK)
                mix = dot(held_down[rows, :], w_down, NT)
                dx = dot(held_both[rows, :], w_both, NT)
                if add:
                    mix = mix + mix_sum[rows, cols].astype(F32)
                    dx = dx + dx_sum[rows, cols].astype(F32)
                mix_sum[rows, cols] = mix.astype(BF16)
                dx_sum[rows, cols] = dx.astype(BF16)

        @pl.when(chunk == 0)
        def _():
            sums(False)

        @pl.when(chunk > 0)
        def _():
            sums(True)

    @pl.when(turn >= row_steps)
    def _():
        part = turn - row_steps
        grads[chunk, part, :, :, :both] = (
            dot(xt_ref[...], held_both[...]).astype(BF16).reshape(2, 2 * block, both)
        )
        grads[chunk, part, :, :, both:] = (
            (dot(ogt_ref[...], held_down[...]) * RESIDUAL_SCALE)
            .astype(BF16)
            .reshape(2, 2 * block, hidden * CHUNK)
        )

    begin = last * steps
    for i in range(2):
        for c in range(2):
            mine = pl.ds(tokens + (2 * c + i) * EXPERT_ROWS, EXPERT_ROWS)
            there = pl.ds((2 * c + i) * EXPERT_ROWS, EXPERT_ROWS)

            @pl.when((step == begin + 2 * c + i) & (core != c))
            def _():
                for name, total, got in (("t", dx_sum, twin_rows), ("mt", mix_sum, twin_mix)):
                    copies.remote(
                        lambda: (total.at[mine], got.at[i]), (name, i), (name, i), near.twin,
                        last=False,
                    )

            @pl.when((step == begin + 2 + 2 * c + i) & (core == c))
            def _():
                for name, total, got in (("t", dx_sum, twin_rows), ("mt", mix_sum, twin_mix)):
                    copies.arrived(got.at[i], (name, i), near.twin)
                    for here in few_rows(EXPERT_ROWS):
                        at = pl.ds(mine.start + here.start, 16)
                        total[at, :] = (
                            total[at, :].astype(F32) + got[i, here, :].astype(F32)
                        ).astype(BF16)
                copies.remote(
                    lambda: (dx_sum.at[mine], dx_other.at[there]), ("o", i), ("o", i), near.over_x,
                    last=False,
                )

            @pl.when((step == begin + steps - 2 + i) & (core == c))
            def _():
                copies.arrived(dx_other.at[there], ("o", i), near.over_x)
                copies.remote(
                    lambda: (dx_other.at[there],) * 2, ("o2", i), ("o2", i), near.twin, last=False
                )

    for i in range(tiles):

        @pl.when(step == begin + tiles + i)
        def _():
            own = pl.ds(i * EXPERT_ROWS, EXPERT_ROWS)
            copies.copy(lambda own=own: (dx_sum.at[own], dx_own.at[own]), ("own", i))
            copies.remote(
                lambda own=own: (dx_sum.at[own], dx_twin.at[own]), ("own", i), ("own", i), near.twin
            )

    shares = gate_kept.shape[0]

    @pl.when(step == begin + row_steps)
    def _():
        copies.copy(lambda: (mix_sum, mix_out), "mix")
        turned = gates[...].T[:shares, :]
        gate_kept[...] = turned
        copies.remote(
            lambda: (gate_kept.at[:, pl.ds(tokens, tokens)], gate_got), ("g",), ("g",), near.over_x
        )

    @pl.when(step == begin + steps - 2)
    def _():
        copies.arrived(gate_got, ("g",), near.over_x)
        gate_full[pl.ds(pl.multiple_of(x * shares, shares), shares), :] = gate_kept[:, :tokens]
        gate_full[pl.ds(pl.multiple_of((1 - x) * shares, shares), shares), :] = gate_got[...]
        copies.remote(lambda: (gate_full, gate_twin), ("g2",), ("g2",), near.twin)

    for c in range(chunks):

        @pl.when(step == (c + 1) * steps - 1)
        def _():
            if c < SENT:
                copies.remote(
                    lambda c=c: (grads.at[c, :, 1 - y], arrived.at[c]),
                    ("sum", c), ("sum", c), near.over_y,
                )
            else:
                for k in range(SLOTS):
                    copies.copy(
                        lambda c=c, k=k: (grads.at[c, spots[k], y], near_outs[c - SENT].at[k]),
                        ("near out", c, k),
                    )
                    if c < last and k == 0:
                        copies.copy(lambda c=c: (grads.at[c, z, 1 - y], first_out), "first out")
                    elif c < last:
                        copies.remote(
                            lambda c=c, k=k: (grads.at[c, spots[k], 1 - y], late_out.at[k - 1]),
                            ("late", k), ("late", k), near.over_y,
                        )
                    else:
                        copies.copy(
                            lambda c=c, k=k: (grads.at[c, spots[k], 1 - y], far_out.at[k]),
                            ("far out", k),
                        )

    @pl.when(step == chunks * steps - 1)
    def _():
        copies.arrived(gate_twin, ("g2",), near.twin)
        gate_out[...] = gate_full[...] + gate_twin[...]
        for i in range(tiles):
            copies.arrived(
                dx_twin.at[pl.ds(i * EXPERT_ROWS, EXPERT_ROWS)], ("own", i), near.twin
            )
        for i in range(2):
            for c in range(2):
                mine = pl.ds(tokens + (2 * c + i) * EXPERT_ROWS, EXPERT_ROWS)
                there = pl.ds((2 * c + i) * EXPERT_ROWS, EXPERT_ROWS)

                @pl.when(core != c)
                def _():
                    copies.sent(lambda: (dx_sum.at[mine], twin_rows.at[i]), ("t", i), near.twin)
                    copies.sent(lambda: (mix_sum.at[mine], twin_mix.at[i]), ("mt", i), near.twin)
                    copies.arrived(dx_other.at[there], ("o2", i), near.twin)

                @pl.when(core == c)
                def _():
                    copies.sent(
                        lambda: (dx_sum.at[mine], dx_other.at[there]), ("o", i), near.over_x
                    )
                    copies.sent(lambda: (dx_other.at[there],) * 2, ("o2", i), near.twin)

        for c in range(SENT):
            for k in range(1, SLOTS):
                copies.arrived(part_outs[c].at[k - 1], ("part", c, k), near.along[k])
        for k in range(1, SLOTS):
            copies.arrived(late_out.at[k - 1], ("late", k), near.over_y)
        copies.finish()


def experts_pass(x, og, xt, ogt, combine, pairs, near, far):
    tokens, width = x.shape
    chunks, pair, columns = pairs.shape
    hidden = columns // (3 * CHUNK)
    shares = chunks * CHUNK
    row_steps = tokens // EXPERT_ROWS
    steps = row_steps + SLOTS
    inner = lax.axis_size("dp") // 16
    row_at = lambda s: ((jnp.minimum(s % steps, row_steps - 1) + row_steps // 2) % row_steps, 0)
    width_at = lambda s: (jnp.maximum(s % steps - row_steps, 0), 0)
    row = pl.BlockSpec((EXPERT_ROWS, width), row_at)
    turned = pl.BlockSpec((width // SLOTS, tokens), width_at)
    anywhere = pl.BlockSpec(memory_space=pl.ANY)
    left = chunks - SENT
    dma = pltpu.SemaphoreType.DMA
    shape = jax.ShapeDtypeStruct
    outs = pl.pallas_call(
        functools.partial(experts_kernel, inner, chunks, row_steps),
        grid=(chunks * steps,),
        in_specs=[row, row, turned, turned, pl.BlockSpec((EXPERT_ROWS, combine.shape[1]), row_at)]
        + [anywhere] * 3,
        out_specs=[anywhere] * 4
        + [pl.BlockSpec((2 * shares, tokens // 2), lambda s: (0, 0))]
        + [anywhere] * (2 * SENT + left + 3),
        out_shape=[shape((tokens // 2, width), BF16)] * 3
        + [shape((tokens, width), BF16), shape((2 * shares, tokens // 2), F32)]
        + [shape((pair, columns), BF16)] * SENT
        + [shape((SLOTS - 1, pair, columns), BF16)] * SENT
        + [shape((SLOTS, pair, columns), BF16)] * left
        + [shape((SLOTS - 1, pair, columns), BF16), shape((pair, columns), BF16)]
        + [shape((SLOTS, pair, columns), BF16)],
        scratch_shapes=[
            pltpu.VMEM((chunks + 1, SLOTS, 2, pair, columns), BF16),
            pltpu.VMEM((SENT, SLOTS, pair, columns), BF16),
            pltpu.VMEM((tokens, 2 * hidden * CHUNK), BF16),
            pltpu.VMEM((tokens, hidden * CHUNK), BF16),
            pltpu.VMEM((tokens, width), BF16),
            pltpu.VMEM((tokens, width), BF16),
            pltpu.VMEM((2, EXPERT_ROWS, width), BF16),
            pltpu.VMEM((2, EXPERT_ROWS, width), BF16),
            pltpu.VMEM((tokens, LANES), F32),
            pltpu.VMEM((shares, tokens), F32),
            pltpu.VMEM((shares, tokens // 2), F32),
            pltpu.VMEM((2 * shares, tokens // 2), F32),
            pltpu.VMEM((2 * shares, tokens // 2), F32),
            dma((48,)), dma((48,)), dma((48,)),
        ],
        compiler_params=pltpu.CompilerParams(
            vmem_limit_bytes=EXPERT_VMEM, collective_id=0, has_side_effects=True
        ),
        cost_estimate=pl.CostEstimate(
            flops=8 * tokens * width * chunks * columns,
            bytes_accessed=2 * chunks * width * columns, transcendentals=0,
        ),
        name="experts_pass",
    )(x, og, xt, ogt, combine, pairs, near, far)
    dx, mix, gate = outs[:3], outs[3], outs[4]
    rest = outs[5:]
    keep, parts, rest = rest[:SENT], rest[SENT : 2 * SENT], rest[2 * SENT :]
    return dx, mix, gate, keep, parts, rest[:left], rest[left:]


class Copies:
    def __init__(self, send, recv, local):
        self.send, self.recv, self.local = send, recv, local
        self.sends, self.recvs, self.locals, self.started = {}, {}, {}, []

    def remote(self, ends, name, arrives, device, last=True):
        sent = self.sends.setdefault(name, len(self.sends))
        got = self.recvs.setdefault(arrives, len(self.recvs))

        def make():
            source, target = ends()
            return pltpu.make_async_remote_copy(
                source, target, self.send.at[sent], self.recv.at[got],
                device_id=device, device_id_type=MESH_ID,
            )

        make().start()
        if last:
            self.started.append(lambda: make().wait_send())

    def sent(self, ends, name, device):
        source, target = ends()
        pltpu.make_async_remote_copy(
            source, target, self.send.at[self.sends[name]], self.recv.at[0],
            device_id=device, device_id_type=MESH_ID,
        ).wait_send()

    def arrived(self, place, name, device):
        got = self.recvs.setdefault(name, len(self.recvs))
        pltpu.make_async_remote_copy(
            place, place, self.send.at[0], self.recv.at[got],
            device_id=device, device_id_type=MESH_ID,
        ).wait_recv()

    def copy(self, ends, name, wait_last=True):
        at = self.locals.setdefault(name, len(self.locals))

        def make():
            return pltpu.make_async_copy(*ends(), self.local.at[at])

        make().start()
        if wait_last:
            self.started.append(lambda: make().wait())
        return lambda: make().wait()

    def wait_copy(self, ends, name):
        pltpu.make_async_copy(*ends(), self.local.at[self.locals[name]]).wait()

    def finish(self):
        for wait in self.started:
            wait()


class Neighbours:
    def __init__(self, inner):
        me = lax.axis_index("dp")
        at = me // inner
        self.core = lax.axis_index("tensor")
        self.z, self.y, self.x = at // 4, at // 2 % 2, at % 2
        self.spots = [(self.z + dz + 4) % 4 for dz in Z_FROM]
        self.along = [{"dp": me + (spot - self.z) * 4 * inner} for spot in self.spots]
        self.over_y = {"dp": me + (1 - 2 * self.y) * 2 * inner}
        self.over_x = {"dp": me + (1 - 2 * self.x) * inner}
        self.twin = {"tensor": 1 - self.core}
        self.blocks = {
            (k, other_y, other_x): self.spots[k] * 4
            + (1 - self.y if other_y else self.y) * 2
            + (1 - self.x if other_x else self.x)
            for k in range(SLOTS)
            for other_y in (0, 1)
            for other_x in (0, 1)
        }

    def greet(self):
        barrier = pltpu.get_barrier_semaphore()
        devices = [*self.along[1:], self.over_y, self.over_x, self.twin]
        for device in devices:
            pl.semaphore_signal(barrier, inc=1, device_id=device, device_id_type=MESH_ID)
        pl.semaphore_wait(barrier, len(devices))

    def block(self, k, other_y, other_x):
        return self.blocks[k, other_y, other_x]


BACK = (0, 2, 1, 3)


class Gather:
    def __init__(self, copies, near, shard, full, tag):
        self.copies, self.near, self.shard, self.full, self.tag = copies, near, shard, full, tag
        self.split = full.shape[2] // (2 * LANES) * LANES

    def source(self, k):
        return self.shard if k == 0 else self.full.at[self.near.block(k, 0, 0)]

    def begin(self):
        for k in range(1, SLOTS):
            self.copies.remote(
                lambda: (self.shard, self.full.at[self.near.block(0, 0, 0)]),
                (self.tag, "z", k), (self.tag, "z", BACK[k]), self.near.along[k],
            )
        self.full[self.near.block(0, 0, 0)] = self.shard[...]

    def spread(self, k):
        near, place = self.near, self.full.at[self.near.block(k, 0, 0)]
        if k > 0:
            self.copies.arrived(place, (self.tag, "z", k), near.along[k])
        for way, device in (("y", near.over_y), ("x", near.over_x)):
            name = (self.tag, way, k)
            self.copies.remote(
                lambda: (self.source(k), self.full.at[near.block(k, 0, 0)]), name, name, device
            )

    def cross(self, k):
        near = self.near
        from_y = self.full.at[near.block(k, 1, 0)]
        from_x = self.full.at[near.block(k, 0, 1)]
        self.copies.arrived(from_y, (self.tag, "y", k), near.over_y)
        self.copies.remote(
            lambda: (self.full.at[near.block(k, 1, 0), :, : self.split],) * 2,
            (self.tag, "one", k), (self.tag, "one", k), near.over_x,
        )
        self.copies.arrived(from_x, (self.tag, "x", k), near.over_x)
        self.copies.remote(
            lambda: (self.full.at[near.block(k, 0, 1), :, self.split :],) * 2,
            (self.tag, "two", k), (self.tag, "two", k), near.over_y,
        )

    def end(self):
        near = self.near
        for k in range(SLOTS):
            place = self.full.at[near.block(k, 1, 1)]
            self.copies.arrived(place.at[:, : self.split], (self.tag, "one", k), near.over_x)
            self.copies.arrived(place.at[:, self.split :], (self.tag, "two", k), near.over_y)


def roll_left(slab, lanes):
    return pltpu.roll(slab, LANES - lanes, 1)


def forward_kernel(
    inner, w_query, w_keyval, w_out, w_router, gains, frequency, seg_row, routes,
    gateup_hbm, down_hbm, hidden_hbm, og_hbm,
    q_full, o_full, small, normed, q_ref, k_ref, v_ref, attended, lse_ref, combine, combine_pair,
    cos, sin, seg_col, middle_hbm, x_hbm, xt_hbm, og_pair, ogt_hbm, pairs_hbm, near_hbm, far_hbm,
    hidden, gateup, down, given, pairs, bias, k_low, k_high, v_low, v_high, part, part_got, x_own, x_got,
    middle, stage, turned, columns_out, columns_got, q_shard, o_shard, send, recv, local,
):
    near = Neighbours(inner)
    copies = Copies(send, recv, local)
    tokens, width = hidden.shape
    block = width // 16
    chunks = pairs.shape[0]
    hid = down.shape[2]
    q_width = q_ref.shape[1]
    kv_slabs = k_ref.shape[1] // LANES
    slabs = q_width // LANES
    qkv_width = q_width + 2 * k_ref.shape[1]
    experts = down.shape[0]
    each = 2 + experts
    half = tokens // 2
    tiles = tokens // ROWS
    x, core = near.x, near.core
    own_half = pl.ds(pl.multiple_of(core * half, half), half)
    mine = pl.ds(pl.multiple_of(tokens + core * half, half), half)
    theirs = pl.ds(pl.multiple_of(tokens + (1 - core) * half, half), half)

    weights_in = [
        copies.copy(lambda: (gateup_hbm, gateup), "gateup", False),
        copies.copy(lambda: (down_hbm, down), "down", False),
    ]
    hidden_in = copies.copy(lambda: (hidden_hbm, hidden), "hidden", False)
    kv_width = k_ref.shape[1]
    q_shard[:, :q_width] = w_query[...].astype(BF16)
    q_shard[:, q_width : q_width + kv_width] = w_keyval[0].astype(BF16)
    q_shard[:, q_width + kv_width : qkv_width] = w_keyval[1].astype(BF16)
    o_shard[...] = w_out[...].astype(BF16)
    cos[:block, :] = jnp.zeros((block, LANES), F32)
    cos[:block, :experts] = w_router[...]
    value = jnp.concatenate([gains[...], jnp.zeros((LANES - 2, block), F32)]).T
    value = value + pltpu.roll(cos[:block, :], 2, 1)
    high = value.astype(BF16).astype(F32)
    mid = (value - high).astype(BF16).astype(F32)
    low = value - high - mid
    value = high + pltpu.roll(mid, each, 1) + pltpu.roll(low, 2 * each, 1)
    q_shard[:, qkv_width:] = value.astype(BF16)
    near.greet()
    gather_q = Gather(copies, near, q_shard, q_full, "q")
    gather_o = Gather(copies, near, o_shard, o_full, "o")
    gather_q.begin()
    gather_q.spread(0)
    copies.copy(lambda: (og_hbm, og_pair.at[pl.ds(0, tokens)]), "og")
    segment = seg_row[...].astype(F32)
    seg_col[...] = jnp.broadcast_to(segment, (8, tokens)).T[:, :1]

    def pack(c, mine):
        first = 2 * (chunks * (x if mine else 1 - x) + c)
        rows = pl.ds(pl.multiple_of(x * block, block), block)
        for e in range(CHUNK):
            for part_at in range(2):
                at = hid * (2 * e + part_at)
                value = gateup[first + e, part_at].astype(BF16)
                if mine:
                    pairs[c, rows, at : at + hid] = value
                else:
                    given[c, :, at : at + hid] = value
            at = hid * (2 * CHUNK + e)
            value = down[first + e].astype(BF16)
            if mine:
                pairs[c, rows, at : at + hid] = value
            else:
                given[c, :, at : at + hid] = value

    def swap(c):
        rows = pl.ds(pl.multiple_of(x * block, block), block)
        copies.remote(
            lambda: (given.at[c], pairs.at[c, rows]), ("s", c), ("s", c), near.over_x
        )

    def swapped(c):
        rows = pl.ds(pl.multiple_of((1 - x) * block, block), block)
        copies.arrived(pairs.at[c, rows], ("s", c), near.over_x)

    def ring_one(c):
        copies.remote(
            lambda: (pairs.at[c], near_hbm.at[c, 0]), ("up", c), ("r", c, 1), near.along[2]
        )
        copies.remote(
            lambda: (pairs.at[c], near_hbm.at[c, 1]), ("down", c), ("r", c, 2), near.along[1]
        )

    def ring_two(c):
        copies.arrived(near_hbm.at[c, 0], ("r", c, 1), near.along[1])
        copies.remote(
            lambda: (near_hbm.at[c, 0], near_hbm.at[c, 2]), ("two", c), ("r", c, 3), near.along[2]
        )

    def over_y(c, k):
        copies.remote(
            lambda: (pairs.at[c] if k == 0 else near_hbm.at[c, k - 1], far_hbm.at[c, k]),
            ("f", c, k), ("f", c, k), near.over_y,
        )

    def ring_got(c, k):
        copies.arrived(near_hbm.at[c, k - 1], ("r", c, k), near.along[k])

    def turn_tile(source, target, name, side):
        copies.copy(lambda: (source, stage.at[side]), (name, "in"), False)()
        turned[side] = stage[side].T
        return copies.copy(lambda: (turned.at[side], target), (name, "out"), False)

    waits = [None, None]

    def turn_next(source, target, name, side):
        if waits[side] is not None:
            waits[side]()
        waits[side] = turn_tile(source, target, name, side)

    for wait in weights_in:
        wait()
    pack(0, False)
    swap(0)
    pack(0, True)
    gather_q.spread(1)
    gather_q.spread(2)
    pack(1, False)
    pack(1, True)
    gather_q.cross(0)
    gather_q.spread(3)
    half_width = HEAD_DIM // 2
    lane = lax.broadcasted_iota(jnp.int32, (ROWS, LANES), 1)
    for at in range(0, tokens, ROWS):
        rows = slice(at, at + ROWS)
        earlier = jnp.where(segment < seg_col[rows, :], 1.0, 0.0)
        position = (at + lax.broadcasted_iota(jnp.int32, (ROWS, 1), 0)).astype(F32)
        position = position - jnp.sum(earlier, axis=1, keepdims=True)
        angle = position * frequency[...]
        cos[rows, :] = jnp.cos(angle)
        wave = jnp.sin(angle)
        sin[rows, :] = jnp.where(lane % HEAD_DIM < half_width, -wave, wave)
    gather_q.cross(1)
    gather_q.cross(2)
    gather_q.cross(3)
    gather_o.begin()
    gather_o.spread(0)
    swap(1)
    pack(2, False)
    pack(2, True)
    pack(3, False)
    pack(3, True)
    fill_bias(bias, seg_col, segment)
    for tile in range(tiles):
        rows = pl.ds(tile * ROWS, ROWS)
        turn_next(og_hbm.at[rows], ogt_hbm.at[:, rows], ("og", tile), tile % 2)
    hidden_in()
    gather_q.end()
    pieces = q_full[:, :, qkv_width:].reshape(width, LANES)
    wide = pieces.astype(F32)
    summed = wide + roll_left(wide, each) + roll_left(wide, 2 * each)
    small[...] = summed.T[: small.shape[0], :]
    swapped(0)
    ring_one(0)
    over_y(0, 0)
    swap(2)
    swap(3)

    def project(tile, carry):
        rows = pl.ds(pl.multiple_of(tile * ROWS, ROWS), ROWS)
        for here in few_rows(ROWS):
            value = hidden[pl.ds(pl.multiple_of(tile * ROWS + here.start, 16), 16), :].astype(F32)
            inverse = lax.rsqrt(jnp.mean(value * value, axis=1, keepdims=True) + NORM_EPSILON)
            stage[0, here, :] = (value * inverse * small[0:1, :]).astype(BF16)
        low = stage[0]
        normed[:, rows] = low.T
        cosine, sine = cos[rows, :], sin[rows, :]
        for g in range(slabs + 2 * kv_slabs):
            lanes = slice(g * LANES, (g + 1) * LANES)
            if g % 2 == 0:
                two = slice(g * LANES, (g + 2) * LANES)
                lin_two = dot(low, q_full[:, :, two].reshape(width, 2 * LANES))
            lin = lin_two[:, (g % 2) * LANES : (g % 2 + 1) * LANES]
            if g < slabs + kv_slabs:
                lin = lin * cosine + rotate_halves(lin) * sine
            if g < slabs:
                q_ref[rows, lanes] = lin.astype(BF16)
            elif g < slabs + kv_slabs:
                at = (g - slabs) * LANES
                k_ref[rows, at : at + LANES] = lin.astype(BF16)
            else:
                at = (g - slabs - kv_slabs) * LANES
                v_ref[rows, at : at + LANES] = lin.astype(BF16)

        @pl.when(tile == 1)
        def _():
            gather_o.spread(1)

        @pl.when(tile == 2)
        def _():
            gather_o.spread(2)
            gather_o.cross(0)

        return carry

    lax.fori_loop(0, tiles, project, 0)
    for j in range(kv_slabs):
        lanes = slice(j * LANES, (j + 1) * LANES)
        spread_heads(k_ref[:, lanes], k_low, k_high, 2 * j)
        spread_heads(v_ref[:, lanes], v_low, v_high, 2 * j)

    def attend(g, carry):
        lanes = pl.ds(pl.multiple_of(g * LANES, LANES), LANES)
        kv_even, kv_odd = (2 * g) // 3, (2 * g + 1) // 3
        for at in range(0, tokens, ROWS):
            rows = slice(at, at + ROWS)
            upto = at + ROWS
            queries = q_ref[rows, lanes]
            total = None
            stats = []
            for keys, values, kv_at in ((k_low, v_low, kv_even), (k_high, v_high, kv_odd)):
                scores = dot(queries, keys[kv_at, :upto, :], NT) * SCORE_SCALE + bias[rows, :upto]
                highest = jnp.max(scores, axis=1, keepdims=True)
                weights = jnp.exp(scores - highest)
                whole = jnp.sum(weights, axis=1, keepdims=True)
                probability = (weights * (1.0 / whole)).astype(BF16)
                one = dot(probability, values[kv_at, :upto, :])
                total = one if total is None else total + one
                stats.append(highest + jnp.log(whole))
            attended[rows, lanes] = total.astype(BF16)
            across = jnp.where(half_mask(ROWS, False), stats[0], stats[1]).T
            lse_ref[g, 0:1, rows] = across[0:1, :]
            lse_ref[g, 1:2, rows] = across[HEAD_DIM : HEAD_DIM + 1, :]

        @pl.when(g == 0)
        def _():
            gather_o.spread(3)
            gather_o.cross(1)
            gather_o.cross(2)

        @pl.when(g == 1)
        def _():
            ring_two(0)
            over_y(0, 1)
            ring_got(0, 2)
            over_y(0, 2)
            swapped(1)
            ring_one(1)
            over_y(1, 0)
            copies.remote(
                lambda: (og_hbm.at[own_half], og_pair.at[mine]), ("og",), ("og",), near.over_x
            )

        @pl.when(g == 2)
        def _():
            gather_o.cross(3)

        @pl.when(g == 4)
        def _():
            gather_o.end()

        @pl.when(g == slabs - 1)
        def _():
            ring_got(0, 3)
            over_y(0, 3)
            swapped(2)
            ring_one(2)
            over_y(2, 0)

        return carry

    lax.fori_loop(0, slabs, attend, 0)

    def project_out(step, carry):
        tile = (step + 2 * (1 - core)) % tiles
        rows = pl.ds(pl.multiple_of(tile * ROWS, ROWS), ROWS)
        low = attended[rows, :]
        for group in range(SLOTS):
            cols = slice(4 * block * group, 4 * block * (group + 1))
            weight = o_full[4 * group : 4 * (group + 1)].reshape(4 * block, q_width)
            part[rows, cols] = dot(low, weight, NT).astype(BF16)
        return carry

    for step in range(tiles):
        project_out(step, 0)
        tile = (step + 2 * (1 - core)) % tiles
        rows = pl.ds(pl.multiple_of(tile * ROWS, ROWS), ROWS)
        copies.remote(
            lambda rows=rows: (part.at[rows], part_got.at[rows]),
            ("p", step), ("p", step), near.twin,
        )
    router = q_full[:, :, qkv_width:].reshape(width, LANES)
    for step in range(tiles):
        tile = (step + 2 * core) % tiles
        rows = pl.ds(pl.multiple_of(tile * ROWS, ROWS), ROWS)
        copies.arrived(part_got.at[rows], ("p", step), near.twin)
        side = step % 2
        if step >= 2:
            middle_out[side]()
        elif step == 0:
            middle_out = [None, None]
        for here in few_rows(ROWS):
            at = pl.ds(pl.multiple_of(tile * ROWS + here.start, 16), 16)
            total = hidden[at, :].astype(F32) + RESIDUAL_SCALE * (
                part[at, :].astype(F32) + part_got[at, :].astype(F32)
            )
            middle[side, here, :] = total
            inverse = lax.rsqrt(jnp.mean(total * total, axis=1, keepdims=True) + NORM_EPSILON)
            value = total * inverse * small[1:2, :]
            high = value.astype(BF16)
            x_own[at, :] = high
            rest = value - high.astype(F32)
            mid = rest.astype(BF16)
            stage[0, here, :] = mid
            stage[1, here, :] = (rest - mid.astype(F32)).astype(BF16)
        middle_out[side] = copies.copy(
            lambda rows=rows, side=side: (middle.at[side], middle_hbm.at[rows]), ("m", step), False
        )
        copies.copy(lambda rows=rows: (x_own.at[rows], x_hbm.at[rows]), ("x", step))
        if step < 2:
            copies.remote(
                lambda rows=rows: (x_own.at[rows], x_got.at[rows]),
                ("x", step), ("x", step), near.over_x,
            )
        one, two, three = dot(x_own[rows, :], router), dot(stage[0], router), dot(stage[1], router)
        logits = one + roll_left(one, each) + roll_left(one, 2 * each) + two + roll_left(two, each)
        logits = roll_left(logits + three, 2)
        lane = lax.broadcasted_iota(jnp.int32, (ROWS, LANES), 1)
        chosen = lane < 0
        route = routes[:, rows].astype(F32).T
        for k in range(routes.shape[0]):
            chosen = chosen | (route[:, k : k + 1] == lane.astype(F32))
        logits = jnp.where(chosen, logits, MASK_VALUE)
        powers = jnp.exp(logits - jnp.max(logits, axis=1, keepdims=True))
        powers = jnp.where(chosen, powers, 0.0)
        combine[rows, :] = powers * (1.0 / jnp.sum(powers, axis=1, keepdims=True))
        if step == 0:
            swapped(3)
            copies.copy(lambda: (pairs, pairs_hbm), "pairs")
        if step == 1:
            ring_two(1)
            over_y(1, 1)
            ring_got(1, 2)
            over_y(1, 2)

    shares = experts // 2
    flipped = combine[...].T
    kept = jnp.where(x == 0, flipped[:shares, :], flipped[shares : 2 * shares, :])
    gone = jnp.where(x == 0, flipped[shares : 2 * shares, :], flipped[:shares, :])
    columns_out[...] = gone
    copies.remote(lambda: (columns_out, columns_got), ("c",), ("c",), near.over_x)
    combine_pair[:tokens, :] = kept.T
    ring_two(2)
    ring_got(1, 3)
    over_y(1, 3)

    copies.arrived(og_pair.at[mine], ("og",), near.over_x)
    copies.remote(lambda: (og_pair.at[mine],) * 2, ("og2",), ("og2",), near.twin)
    for tile in range(tiles):
        rows = pl.ds(tile * ROWS, ROWS)
        if waits[tile % 2] is not None:
            waits[tile % 2]()
        turned[tile % 2] = x_own[rows, :].T
        waits[tile % 2] = copies.copy(
            lambda rows=rows, side=tile % 2: (turned.at[side], xt_hbm.at[:, rows]),
            ("xt", tile), False,
        )
    copies.arrived(columns_got, ("c",), near.over_x)
    combine_pair[tokens:, :] = columns_got[...].T
    copies.arrived(og_pair.at[theirs], ("og2",), near.twin)
    order = [(step + 2 * core) % tiles for step in range(2)]
    order += [(step + 2 * (1 - core)) % tiles for step in range(2)]

    def og_rows(step):
        return pl.ds(pl.multiple_of(tokens + order[step] * ROWS, ROWS), ROWS)

    def og_load(step):
        return copies.copy(
            lambda: (og_pair.at[og_rows(step)], stage.at[step % 2]), ("ogin", step), False
        )

    loaded = og_load(0)
    for step in range(tiles):
        loaded()
        if step + 1 < tiles:
            loaded = og_load(step + 1)
        side = step % 2
        waits[side]()
        turned[side] = stage[side].T
        waits[side] = copies.copy(
            lambda step=step, side=side: (turned.at[side], ogt_hbm.at[:, og_rows(step)]),
            ("ogt", step), False,
        )
    for step in range(tiles):
        rows = pl.ds(pl.multiple_of(order[step] * ROWS, ROWS), ROWS)
        there = pl.ds(pl.multiple_of(tokens + order[step] * ROWS, ROWS), ROWS)
        if step < 2:
            copies.arrived(x_got.at[rows], ("x", step), near.over_x)
            copies.remote(
                lambda rows=rows: (x_got.at[rows],) * 2, ("x2", step), ("x2", step), near.twin
            )
        else:
            copies.arrived(x_got.at[rows], ("x2", step - 2), near.twin)
        copies.copy(
            lambda rows=rows, there=there: (x_got.at[rows], x_hbm.at[there]), ("xg", step)
        )
        side = step % 2
        waits[side]()
        turned[side] = x_got[rows, :].T
        waits[side] = copies.copy(
            lambda there=there, side=side: (turned.at[side], xt_hbm.at[:, there]),
            ("xgt", step), False,
        )
    for wait in waits + middle_out:
        wait()
    ring_got(2, 2)
    ring_got(2, 3)
    for c in range(LATE + 1):
        for k in range(SLOTS if c < LATE else 1):
            copies.arrived(far_hbm.at[c, k], ("f", c, k), near.over_y)
    copies.finish()


def forward_pass(weights, frequency, segments, routes, gateup, down, hidden, og):
    tokens, width = hidden.shape
    experts, hid = down.shape[0], down.shape[2]
    block, q_width = weights[0].shape
    kv_width = weights[1].shape[2]
    q_columns = q_width + 2 * kv_width + LANES
    slabs, kv_heads = q_width // LANES, kv_width // HEAD_DIM
    chunks = experts // (2 * CHUNK)
    columns = 3 * CHUNK * hid
    anywhere, vmem = pl.BlockSpec(memory_space=pl.ANY), vmem_spec()
    shape = jax.ShapeDtypeStruct
    inner = lax.axis_size("dp") // 16
    dma = pltpu.SemaphoreType.DMA
    return pl.pallas_call(
        functools.partial(forward_kernel, inner),
        in_specs=[vmem] * 8 + [anywhere] * 4,
        out_specs=[vmem] * 14 + [anywhere] * 8,
        out_shape=[
            shape((16, block, q_columns), BF16),
            shape((16, block, q_width), BF16),
            shape((24, width), F32),
            shape((width, tokens), BF16),
            shape((tokens, q_width), BF16),
            shape((tokens, kv_width), BF16),
            shape((tokens, kv_width), BF16),
            shape((tokens, q_width), BF16),
            shape((slabs, 8, tokens), F32),
            shape((tokens, LANES), F32),
            shape((2 * tokens, experts // 2), F32),
            shape((tokens, LANES), F32),
            shape((tokens, LANES), F32),
            shape((tokens, 1), F32),
            shape((tokens, width), F32),
            shape((2 * tokens, width), BF16),
            shape((width, 2 * tokens), BF16),
            shape((2 * tokens, width), BF16),
            shape((width, 2 * tokens), BF16),
            shape((chunks, 2 * block, columns), BF16),
            shape((chunks - 1, SLOTS - 1, 2 * block, columns), BF16),
            shape((LATE + 1, SLOTS, 2 * block, columns), BF16),
        ],
        scratch_shapes=[
            pltpu.VMEM((tokens, width), BF16),
            pltpu.VMEM(gateup.shape, gateup.dtype),
            pltpu.VMEM(down.shape, down.dtype),
            pltpu.VMEM((chunks, block, columns), BF16),
            pltpu.VMEM((chunks, 2 * block, columns), BF16),
            pltpu.VMEM((tokens, tokens), F32),
        ]
        + [pltpu.VMEM((kv_heads, tokens, LANES), BF16)] * 4
        + [pltpu.VMEM((tokens, width), BF16)] * 4
        + [
            pltpu.VMEM((2, ROWS, width), F32),
            pltpu.VMEM((2, ROWS, width), BF16),
            pltpu.VMEM((2, width, ROWS), BF16),
            pltpu.VMEM((experts // 2, tokens), F32),
            pltpu.VMEM((experts // 2, tokens), F32),
            pltpu.VMEM((block, q_columns), BF16),
            pltpu.VMEM((block, q_width), BF16),
            dma((80,)), dma((80,)), dma((60,)),
        ],
        compiler_params=pltpu.CompilerParams(
            vmem_limit_bytes=EXPERT_VMEM, collective_id=1, has_side_effects=True
        ),
        name="forward_pass",
    )(*weights, frequency, segments[None, :], routes.T, gateup, down, hidden, og)


class Scatter:
    def __init__(self, copies, near, grad, one, two, got_y, got_x, got_z, share, tag):
        self.copies, self.near, self.grad, self.share, self.tag = copies, near, grad, share, tag
        self.one, self.two, self.got_y, self.got_x, self.got_z = one, two, got_y, got_x, got_z
        self.split = one.shape[2]

    def begin(self, k):
        near = self.near
        self.copies.remote(
            lambda: (self.grad.at[near.block(k, 1, 1), :, : self.split], self.one.at[k]),
            (self.tag, "one", k), (self.tag, "one", k), near.over_x,
        )
        self.copies.remote(
            lambda: (self.grad.at[near.block(k, 1, 1), :, self.split :], self.two.at[k]),
            (self.tag, "two", k), (self.tag, "two", k), near.over_y,
        )

    def cross(self, k):
        near, grad, split = self.near, self.grad, self.split
        self.copies.arrived(self.one.at[k], (self.tag, "one", k), near.over_x)
        at = near.block(k, 1, 0)
        for here in few_rows(grad.shape[1]):
            grad[at, here, :split] = (
                grad[at, here, :split].astype(F32) + self.one[k, here, :].astype(F32)
            ).astype(BF16)
        self.copies.remote(
            lambda: (grad.at[near.block(k, 1, 0)], self.got_y.at[k]),
            (self.tag, "y", k), (self.tag, "y", k), near.over_y,
        )
        self.copies.arrived(self.two.at[k], (self.tag, "two", k), near.over_y)
        at = near.block(k, 0, 1)
        for here in few_rows(grad.shape[1]):
            grad[at, here, split:] = (
                grad[at, here, split:].astype(F32) + self.two[k, here, :].astype(F32)
            ).astype(BF16)
        self.copies.remote(
            lambda: (grad.at[near.block(k, 0, 1)], self.got_x.at[k]),
            (self.tag, "x", k), (self.tag, "x", k), near.over_x,
        )

    def plane(self, k):
        near, grad = self.near, self.grad
        self.copies.arrived(self.got_y.at[k], (self.tag, "y", k), near.over_y)
        self.copies.arrived(self.got_x.at[k], (self.tag, "x", k), near.over_x)
        at = near.block(k, 0, 0)
        for here in few_rows(grad.shape[1]):
            total = grad[at, here, :].astype(F32) + self.got_y[k, here, :].astype(F32)
            total = total + self.got_x[k, here, :].astype(F32)
            if k == 0:
                self.share[here, :] = total
            else:
                grad[at, here, :] = total.astype(BF16)
        if k == 0:
            return
        self.copies.remote(
            lambda: (grad.at[near.block(k, 0, 0)], self.got_z.at[BACK[k] - 1]),
            (self.tag, "z", k), (self.tag, "z", BACK[k]), near.along[k],
        )

    def end(self):
        for k in range(1, SLOTS):
            self.copies.arrived(self.got_z.at[k - 1], (self.tag, "z", k), self.near.along[k])
            for here in few_rows(self.share.shape[0]):
                self.share[here, :] = self.share[here, :] + self.got_z[k - 1, here, :].astype(F32)


STRIP = 128


def backward_kernel(
    inner,
    o_full, q_ref, k_ref, v_ref, attended, lse_ref, cos, sin, seg_col, seg_row, small, combine,
    gate_turned, q_hbm, normed_hbm, hidden_hbm, og_hbm, middle_hbm, dx_own, dx_twin, dx_other,
    mix_pair, *refs,
):
    keeps, refs = refs[:SENT], refs[SENT:]
    parts, refs = refs[:SENT], refs[SENT:]
    near_two, near_three, late_got, far_first, far_three = refs[:5]
    q_share, o_share, input_grad, block_out, kept_out, given_got, mid_grad = refs[5:12]
    far_got, first_got, z_two, z_three, mix_twin, mix_other = refs[12:18]
    (
        attended_grad, lin_grad, o_grad, q_grad, o_one, o_two, o_y, o_x, o_z,
        q_one, q_two, q_y, q_x, q_z, part_got, pieces, z_send, z_keep, given, kept,
        strips, wide_in, wide_out, strip_out, router_rows, gate_columns, small_sum,
        send, recv, local, strip_sem, wide_sem, out_sem,
    ) = refs[18:]
    near = Neighbours(inner)
    copies = Copies(send, recv, local)
    tokens, width = hidden_hbm.shape
    block = width // 16
    x, core = near.x, near.core
    half = tokens // 2
    q_width = q_ref.shape[1]
    kv_width = k_ref.shape[1]
    kv_slabs, slabs = kv_width // LANES, q_width // LANES
    qkv_width = q_width + 2 * kv_width
    experts = gate_turned.shape[0]
    each = 2 + experts
    strip_count = tokens // STRIP
    ours = pl.ds(0, tokens)
    half_mine = pl.ds(pl.multiple_of(tokens + core * half, half), half)
    there = pl.ds(pl.multiple_of(core * half, half), half)
    not_there = pl.ds(pl.multiple_of((1 - core) * half, half), half)
    scatter_o = Scatter(copies, near, o_grad, o_one, o_two, o_y, o_x, o_z, o_share, "o")
    scatter_q = Scatter(copies, near, q_grad, q_one, q_two, q_y, q_x, q_z, q_share, "q")
    z_gots = [*parts, z_two, z_three]

    def y_ends(c, k):
        if c == SENT:
            return near_two.at[k], first_got if k == 0 else late_got.at[k - 1]
        return near_three.at[k], far_got.at[k]

    def y_load(c, k, i, which):
        if 0 in which:
            copies.copy(lambda: (y_ends(c, k)[0], pieces.at[2 * i]), ("own", c, k), False)
        if 1 in which:
            copies.copy(lambda: (y_ends(c, k)[1], pieces.at[2 * i + 1]), ("got", c, k), False)

    def y_sum(c, k, i):
        copies.wait_copy(lambda: (y_ends(c, k)[0], pieces.at[2 * i]), ("own", c, k))
        copies.wait_copy(lambda: (y_ends(c, k)[1], pieces.at[2 * i + 1]), ("got", c, k))
        if k > 0 and c > SENT:
            copies.sent(
                lambda: (z_send.at[k - 1], z_two.at[BACK[k] - 1]), (SENT, "z", k), near.along[k]
            )
        target = z_keep.at[c - SENT] if k == 0 else z_send.at[k - 1]
        for here in few_rows(target.shape[0]):
            target[here, :] = (
                pieces[2 * i, here, :].astype(F32) + pieces[2 * i + 1, here, :].astype(F32)
            ).astype(BF16)
        if k == 0:
            return
        copies.remote(
            lambda: (z_send.at[k - 1], z_gots[c].at[BACK[k] - 1]),
            (c, "z", k), (c, "z", BACK[k]), near.along[k], last=c > SENT,
        )

    def far_arrived(k):
        copies.arrived(far_got.at[k], ("far", k), near.over_y)

    def chunk_ends(c, k):
        return keeps[c] if k == 0 else z_gots[c].at[k - 1], pieces.at[k]

    def load_chunk(c):
        for k in range(1 if c >= SENT else 0, SLOTS):
            if c >= SENT:
                copies.arrived(z_gots[c].at[k - 1], (c, "z", k), near.along[k])
            copies.copy(lambda k=k: chunk_ends(c, k), (c, "sum", k), False)

    def sum_chunk(c):
        for k in range(1 if c >= SENT else 0, SLOTS):
            copies.wait_copy(lambda: chunk_ends(c, k), (c, "sum", k))
        if c >= 2:
            copies.wait_copy(lambda: (kept.at[c % 2], kept_out.at[c - 2]), ("kept", c - 2))
        for base, mine in ((x * block, True), ((1 - x) * block, False)):
            for here, rows in zip(few_rows(block), few_rows(block, base)):
                total = (pieces[0, rows, :] if c < SENT else z_keep[c - SENT, rows, :]).astype(F32)
                for k in range(1, SLOTS):
                    total = total + pieces[k, rows, :].astype(F32)
                if mine:
                    kept[c % 2, here, :] = total
                else:
                    given[c, here, :] = total.astype(BF16)
        copies.copy(lambda: (kept.at[c % 2], kept_out.at[c]), ("kept", c), c >= 2)
        copies.remote(
            lambda: (given.at[c], given_got.at[c]), ("given", c), ("given", c), near.over_x
        )

    def strip_rows(t):
        return pl.ds(pl.multiple_of(t * STRIP, STRIP), STRIP)

    def strip_loads(t, sources, wide):
        side = t % 2
        rows = strip_rows(t)
        loads = [
            pltpu.make_async_copy(source.at[rows], strips.at[i, side], strip_sem.at[i, side])
            for i, source in enumerate(sources)
        ]
        if wide is not None:
            loads.append(
                pltpu.make_async_copy(wide.at[rows], wide_in.at[side], wide_sem.at[side])
            )
        return loads

    def strip_store(t, source, target):
        side = t % 2
        return pltpu.make_async_copy(
            source.at[side], target.at[strip_rows(t)], out_sem.at[side]
        )

    def over_strips(sources, wide, source, target, compute):
        for load in strip_loads(0, sources, wide):
            load.start()

        def one(t, carry):
            side = t % 2

            @pl.when(t + 1 < strip_count)
            def _():
                for load in strip_loads(t + 1, sources, wide):
                    load.start()

            for load in strip_loads(t, sources, wide):
                load.wait()

            @pl.when(t >= 2)
            def _():
                strip_store(t - 2, source, target).wait()

            compute(t, side)
            strip_store(t, source, target).start()
            return carry

        lax.fori_loop(0, strip_count, one, 0)
        for t in (strip_count - 2, strip_count - 1):
            strip_store(t, source, target).wait()

    for i, k in enumerate((1, 2)):
        y_load(SENT, k, i, (0, 1))
    near.greet()
    for k in (1, 2, 3, 0):
        copies.remote(
            lambda k=k: (far_three.at[k], far_got.at[k]), ("far", k), ("far", k), near.over_y
        )
    copies.remote(lambda: (far_first, first_got), ("first",), ("first",), near.over_y)
    copies.remote(
        lambda: (mix_pair.at[half_mine], mix_other.at[there]), ("mo",), ("mo",), near.over_x
    )
    copies.remote(lambda: (mix_pair.at[ours], mix_twin), ("mt",), ("mt",), near.twin)
    y_sum(SENT, 1, 0)
    y_load(SENT, 3, 0, (0, 1))
    y_sum(SENT, 2, 1)
    y_sum(SENT, 3, 0)
    load_chunk(0)

    router = small[2 : 2 + experts, :]
    high = router.astype(BF16).astype(F32)
    mid = (router - high).astype(BF16).astype(F32)
    low = router - high - mid
    router_rows[...] = jnp.concatenate(
        [high, mid, low, high, mid, high, jnp.zeros((LANES - 6 * experts, width), F32)]
    ).astype(BF16)
    gate_columns[...] = jnp.concatenate(
        [gate_turned[...], jnp.zeros((LANES - experts, tokens), F32)]
    ).T
    small_sum[...] = jnp.zeros_like(small_sum)

    def middle_part(turned_back):
        def compute(t, side):
            rows = strip_rows(t)
            gates, grads = combine[rows, :], gate_columns[rows, :]
            logit = gates * (grads - jnp.sum(gates * grads, axis=1, keepdims=True))
            one = logit.astype(BF16).astype(F32)
            two = (logit - one).astype(BF16).astype(F32)
            three = (logit - one - two).astype(BF16).astype(F32)

            def moved(piece, by):
                return pltpu.roll(piece, by * experts, 1)

            row = one + moved(one, 1) + moved(one, 2) + moved(two, 3) + moved(two, 4)
            row = (row + moved(three, 5)).astype(BF16)
            wide_out[side] = dot(row, router_rows[...])
            gain = small[1:2, :]
            gain_part = None
            back, n_one, n_two, n_three = (
                strip_out.at[0], strip_out.at[1], z_keep.at[0], z_keep.at[1]
            )
            for here in few_rows(STRIP):
                upstream = strips[0, side, here, :].astype(F32) + strips[1, side, here, :].astype(F32)
                upstream = upstream + strips[2, side, here, :].astype(F32)
                upstream = upstream + wide_out[side, here, :]
                middle = wide_in[side, here, :]
                inverse = lax.rsqrt(jnp.mean(middle * middle, axis=1, keepdims=True) + NORM_EPSILON)
                scaled = middle * inverse
                weighted = upstream * gain
                mean_term = jnp.mean(weighted * scaled, axis=1, keepdims=True)
                grad = strips[3, side, here, :].astype(F32) + inverse * (
                    weighted - scaled * mean_term
                )
                wide_out[side, here, :] = grad
                back[here, :] = (RESIDUAL_SCALE * grad).astype(BF16)
                gained = jnp.sum(upstream * scaled, axis=0, keepdims=True)
                gain_part = gained if gain_part is None else gain_part + gained
                normed = scaled * gain
                piece = normed.astype(BF16)
                n_one[here, :] = piece
                rest = normed - piece.astype(F32)
                piece = rest.astype(BF16)
                n_two[here, :] = piece
                n_three[here, :] = (rest - piece.astype(F32)).astype(BF16)
            small_sum[0:1, :] += gain_part
            strip = pl.ds(0, STRIP)
            turned_back[:, rows] = back[...].T
            attended_grad[rows, :] = dot(back[...], o_full[...].reshape(width, q_width)).astype(BF16)
            columns = (one + moved(two, 1) + moved(three, 2)).T[: 3 * experts, :].astype(BF16)
            a, b, c = (
                dot(columns, n_one[...]), dot(columns, n_two[strip, :]), dot(columns, n_three[strip, :])
            )
            e = experts
            small_sum[8 : 8 + e, :] += (
                a[:e] + a[e : 2 * e] + a[2 * e :] + b[:e] + b[e : 2 * e] + c[:e]
            )

        over_strips([dx_own, dx_twin, dx_other, og_hbm], middle_hbm, wide_out, mid_grad, compute)
        for group in range(SLOTS):
            rows = slice(4 * block * group, 4 * block * (group + 1))
            o_grad[4 * group : 4 * (group + 1)] = (
                dot(turned_back[rows, :], attended[...]).astype(BF16).reshape(4, block, q_width)
            )

    pl.run_scoped(middle_part, pltpu.VMEM((width, tokens), BF16))
    for k in (1, 2, 3, 0):
        scatter_o.begin(k)

    def attention_part(bias0, bias1, bias2, bias3, k_low, k_high, v_low, v_high, dk, dv, dq):
        biases = (bias0, bias1, bias2, bias3)
        for at, bias in enumerate(biases):
            upto = bias.shape[0]
            keys_at = lax.broadcasted_iota(jnp.int32, bias.shape, 0)
            rows_at = at * ROWS + lax.broadcasted_iota(jnp.int32, bias.shape, 1)
            same = seg_col[:upto, :] == seg_row[:, at * ROWS : (at + 1) * ROWS].astype(F32)
            bias[...] = jnp.where((rows_at >= keys_at) & same, 0.0, MASK_VALUE).astype(F32)
        for j in range(kv_slabs):
            lanes = slice(j * LANES, (j + 1) * LANES)
            spread_heads(k_ref[:, lanes], k_low, k_high, 2 * j)
            spread_heads(v_ref[:, lanes], v_low, v_high, 2 * j)
        dk[...] = jnp.zeros_like(dk)
        dv[...] = jnp.zeros_like(dv)

        def slab(g, carry):
            lanes = pl.ds(pl.multiple_of(g * LANES, LANES), LANES)
            kv_even, kv_odd = (2 * g) // 3, (2 * g + 1) // 3
            for at, bias in enumerate(biases):
                rows = slice(at * ROWS, (at + 1) * ROWS)
                upto = (at + 1) * ROWS
                queries, grads = q_ref[rows, lanes], attended_grad[rows, lanes]
                turned = (grads.astype(F32) * attended[rows, lanes].astype(F32)).T
                zero = jnp.zeros_like(queries)
                dq_part = None
                for upper, keys, values, kv_at in (
                    (False, k_low, v_low, kv_even), (True, k_high, v_high, kv_odd)
                ):
                    first = HEAD_DIM if upper else 0
                    delta = jnp.sum(turned[first : first + HEAD_DIM, :], axis=0, keepdims=True)
                    head = 1 if upper else 0
                    total = lse_ref[g, head : head + 1, rows]
                    keys_here = keys[kv_at, :upto, :]
                    scores = dot(keys_here, queries, NT) * SCORE_SCALE + bias[...]
                    probability = jnp.exp(scores - total)
                    prob_grad = dot(values[kv_at, :upto, :], grads, NT)
                    score_grad = (probability * (prob_grad - delta)).astype(BF16)
                    mask = half_mask(ROWS, upper)
                    dv[kv_at, :upto, :] += dot(
                        probability.astype(BF16), jnp.where(mask, grads, zero)
                    )
                    dk[kv_at, :upto, :] += dot(score_grad, jnp.where(mask, queries, zero))
                    one = dot(score_grad, keys_here, TN)
                    dq_part = one if dq_part is None else dq_part + one
                dq[rows, :] = dq_part * SCORE_SCALE
            whole = dq[...]
            lin_grad[:, lanes] = (
                whole * cos[...] - rotate_halves(whole) * sin[...]
            ).astype(BF16)

            @pl.when(g == 1)
            def _():
                for k in (1, 2, 3, 0):
                    scatter_o.cross(k)

            @pl.when(g == 2)
            def _():
                sum_chunk(0)
                y_load(SENT + 1, 1, 0, (0,))
                y_load(SENT + 1, 2, 1, (0,))

            @pl.when(g == 3)
            def _():
                far_arrived(1)
                y_load(SENT + 1, 1, 0, (1,))
                far_arrived(2)
                y_load(SENT + 1, 2, 1, (1,))
                far_arrived(3)
                y_sum(SENT + 1, 1, 0)
                y_load(SENT + 1, 3, 0, (0, 1))
                y_sum(SENT + 1, 2, 1)
                y_sum(SENT + 1, 3, 0)
                load_chunk(1)

            @pl.when(g == 4)
            def _():
                for k in (1, 2, 3, 0):
                    scatter_o.plane(k)
                sum_chunk(1)
                far_arrived(0)
                y_load(SENT + 1, 0, 0, (0, 1))
                copies.arrived(first_got, ("first",), near.over_y)
                y_load(SENT, 0, 1, (0, 1))

            return carry

        lax.fori_loop(0, slabs, slab, 0)
        low = half_mask(tokens, False)

        def joined(sums, j):
            one, two = sums[2 * j], sums[2 * j + 1]
            one = one + pltpu.roll(one, HEAD_DIM, 1)
            two = two + pltpu.roll(two, HEAD_DIM, 1)
            return jnp.where(low, one, two)

        for j in range(kv_slabs):
            at = q_width + j * LANES
            whole = joined(dk, j) * SCORE_SCALE
            lin_grad[:, at : at + LANES] = (
                whole * cos[...] - rotate_halves(whole) * sin[...]
            ).astype(BF16)
            at = at + kv_width
            lin_grad[:, at : at + LANES] = joined(dv, j).astype(BF16)

    kv_shape = (2 * kv_slabs, tokens, LANES)
    pl.run_scoped(
        attention_part,
        *[pltpu.VMEM(((at + 1) * ROWS, ROWS), F32) for at in range(tokens // ROWS)],
        *[pltpu.VMEM(kv_shape, BF16)] * 4,
        *[pltpu.VMEM(kv_shape, F32)] * 2,
        pltpu.VMEM((tokens, LANES), F32),
    )

    def last_part(normed_turned, q_full, part):
        normed_in = copies.copy(lambda: (normed_hbm, normed_turned), "normed", False)
        weights_in = copies.copy(lambda: (q_hbm, q_full), "q weights", False)
        columns = jnp.concatenate(
            [
                small_sum[0:1, :], small_sum[8 : 8 + experts, :],
                jnp.zeros((LANES - 1 - experts, width), F32),
            ]
        ).T
        q_grad[:, :, qkv_width:] = columns.astype(BF16).reshape(16, block, LANES)
        normed_in()
        for k in (1, 2, 3, 0):
            spot = near.spots[k]
            rows = pl.ds(pl.multiple_of(spot * 4 * block, 4 * block), 4 * block)
            q_grad[pl.ds(spot * 4, 4), :, :qkv_width] = (
                dot(normed_turned[rows, :], lin_grad[...])
                .astype(BF16)
                .reshape(4, block, qkv_width)
            )
            scatter_q.begin(k)
        weights_in()

        def project(tile):
            rows = pl.ds(tile * ROWS, ROWS)
            for group in range(SLOTS):
                cols = slice(4 * block * group, 4 * block * (group + 1))
                weight = q_full[4 * group : 4 * (group + 1), :, :qkv_width]
                part[rows, cols] = dot(
                    lin_grad[rows, :], weight.reshape(4 * block, qkv_width), NT
                ).astype(BF16)
            copies.remote(
                lambda: (part.at[rows], part_got.at[rows]), ("n", tile), ("n", tile), near.twin,
                last=False,
            )

        project(0)
        project(1)
        for k in (1, 2, 3, 0):
            scatter_q.cross(k)
        y_sum(SENT + 1, 0, 0)
        y_sum(SENT, 0, 1)
        load_chunk(2)
        project(2)
        project(3)
        scatter_o.end()
        copies.arrived(mix_other.at[there], ("mo",), near.over_x)
        copies.remote(lambda: (mix_other.at[there],) * 2, ("m2",), ("m2",), near.twin)
        sum_chunk(2)
        for tile in range(tokens // ROWS):
            rows = pl.ds(tile * ROWS, ROWS)
            copies.arrived(part_got.at[rows], ("n", tile), near.twin)

        def finish_rows(t, side):
            for here in few_rows(STRIP):
                at = pl.ds(pl.multiple_of(t * STRIP + here.start, 16), 16)
                value = strips[0, side, here, :].astype(F32)
                inverse = lax.rsqrt(jnp.mean(value * value, axis=1, keepdims=True) + NORM_EPSILON)
                upstream = part[at, :].astype(F32) + part_got[at, :].astype(F32)
                scaled = value * inverse
                weighted = upstream * small[0:1, :]
                mean_term = jnp.mean(weighted * scaled, axis=1, keepdims=True)
                wide_out[side, here, :] = wide_in[side, here, :] + inverse * (
                    weighted - scaled * mean_term
                )

        over_strips([hidden_hbm], mid_grad, wide_out, input_grad, finish_rows)
        for k in (1, 2, 3, 0):
            scatter_q.plane(k)
        load_chunk(3)
        for tile in range(tokens // ROWS):
            rows = pl.ds(tile * ROWS, ROWS)
            copies.sent(lambda: (part.at[rows], part_got.at[rows]), ("n", tile), near.twin)

    pl.run_scoped(
        last_part,
        pltpu.VMEM((width, tokens), BF16), pltpu.VMEM(q_hbm.shape, BF16),
        pltpu.VMEM((tokens, width), BF16),
    )
    sum_chunk(3)
    copies.arrived(mix_twin, ("mt",), near.twin)
    copies.arrived(mix_other.at[not_there], ("m2",), near.twin)

    def mix_rows(t, side):
        for here in few_rows(STRIP):
            mix = strips[0, side, here, :].astype(F32) + strips[1, side, here, :].astype(F32)
            mix = mix + strips[2, side, here, :].astype(F32)
            strip_out[side, here, :] = (wide_in[side, here, :] + RESIDUAL_SCALE * mix).astype(BF16)

    over_strips([mix_pair, mix_twin, mix_other], middle_hbm, strip_out, block_out, mix_rows)
    scatter_q.end()
    for c in range(2 * SENT):
        copies.arrived(given_got.at[c], ("given", c), near.over_x)
    copies.finish()


def backward_pass(
    o_full, q, k, v, attended, lse, cosine, sine, seg_col, segments, small, combine, gate_turned,
    q_full, normed, hidden, og, middle, dx, mix, keep, parts, near_grads, far_grads,
):
    tokens, width = hidden.shape
    q_width, kv_width = q.shape[1], k.shape[1]
    block, q_columns = q_full.shape[1:]
    qkv_width = q_width + 2 * kv_width
    pair, columns = keep[0].shape
    chunks = 2 * SENT
    experts = gate_turned.shape[0]
    anywhere, vmem = pl.BlockSpec(memory_space=pl.ANY), vmem_spec()
    shape = jax.ShapeDtypeStruct
    dma = pltpu.SemaphoreType.DMA
    inner = lax.axis_size("dp") // 16

    def scatter_scratch(total):
        split = total // (2 * LANES) * LANES
        return [
            pltpu.VMEM((SLOTS, block, split), BF16),
            pltpu.VMEM((SLOTS, block, total - split), BF16),
            pltpu.VMEM((SLOTS, block, total), BF16),
            pltpu.VMEM((SLOTS, block, total), BF16),
            pltpu.VMEM((SLOTS - 1, block, total), BF16),
        ]

    values = (
        o_full, q, k, v, attended, lse, cosine, sine, seg_col, segments[None, :],
        small, combine, gate_turned,
    )
    far_values = (
        q_full, normed, hidden, og, middle, *dx, mix, *keep, *parts, *near_grads, *far_grads,
    )
    return pl.pallas_call(
        functools.partial(backward_kernel, inner),
        in_specs=[vmem] * len(values) + [anywhere] * len(far_values),
        out_specs=[vmem] * 2 + [anywhere] * 11,
        out_shape=[
            shape((block, q_columns), F32),
            shape((block, q_width), F32),
            shape((tokens, width), F32),
            shape((tokens, width), BF16),
            shape((chunks, block, columns), F32),
            shape((chunks, block, columns), BF16),
            shape((tokens, width), F32),
            shape((SLOTS, pair, columns), BF16),
            shape((pair, columns), BF16),
            shape((SLOTS - 1, pair, columns), BF16),
            shape((SLOTS - 1, pair, columns), BF16),
            shape((tokens, width), BF16),
            shape((tokens, width), BF16),
        ],
        scratch_shapes=[
            pltpu.VMEM((tokens, q_width), BF16),
            pltpu.VMEM((tokens, qkv_width), BF16),
            pltpu.VMEM((16, block, q_width), BF16),
            pltpu.VMEM((16, block, q_columns), BF16),
        ]
        + scatter_scratch(q_width)
        + scatter_scratch(q_columns)
        + [
            pltpu.VMEM((tokens, width), BF16),
            pltpu.VMEM((SLOTS, pair, columns), BF16),
            pltpu.VMEM((SLOTS - 1, pair, columns), BF16),
            pltpu.VMEM((2, pair, columns), BF16),
            pltpu.VMEM((chunks, block, columns), BF16),
            pltpu.VMEM((2, block, columns), F32),
            pltpu.VMEM((4, 2, STRIP, width), BF16),
            pltpu.VMEM((2, STRIP, width), F32),
            pltpu.VMEM((2, STRIP, width), F32),
            pltpu.VMEM((2, STRIP, width), BF16),
            pltpu.VMEM((LANES, width), BF16),
            pltpu.VMEM((tokens, LANES), F32),
            pltpu.VMEM((8 + experts, width), F32),
            dma((80,)), dma((80,)), dma((60,)), dma((4, 2)), dma((2,)), dma((2,)),
        ],
        compiler_params=pltpu.CompilerParams(
            vmem_limit_bytes=EXPERT_VMEM, collective_id=2, has_side_effects=True
        ),
        name="backward_pass",
    )(*values, *far_values)


def whole_call(kernel, values, outs, earlier=(), name=None):
    return pl.pallas_call(
        with_earlier(kernel, len(values), len(earlier)),
        in_specs=[vmem_spec()] * len(values) + any_specs(earlier),
        out_specs=[vmem_spec()] * len(outs),
        out_shape=[jax.ShapeDtypeStruct(shape, dtype) for shape, dtype in outs],
        compiler_params=pltpu.CompilerParams(vmem_limit_bytes=VMEM_BYTES),
        name=name,
    )(*values, *earlier)


def fence_kernel(*refs):
    count = len(refs) // 2
    for value, out in zip(refs[:count], refs[count:]):
        out[...] = value[...]


def fence_all(values, *earlier):
    return whole_call(fence_kernel, values, [(v.shape, v.dtype) for v in values], earlier, "fence")


def fence(value, *earlier):
    return fence_all([value], *earlier)[0]


def sum_y_kernel(near, got, *outs):
    for k, out in enumerate(outs):
        out[...] = (near[k].astype(F32) + got[k].astype(F32)).astype(BF16)


def sum_y(near, got, *earlier):
    outs = [(near.shape[1:], BF16)] * SLOTS
    return whole_call(sum_y_kernel, [near, got], outs, earlier, "sum_y")


def sum_z_kernel(x_at, *refs):
    kept, given = refs[-2:]
    half = kept.shape[1]
    for c in range(kept.shape[0]):
        parts = refs[SLOTS * c : SLOTS * (c + 1)]
        for rows, out in ((x_at[0], kept), (1 - x_at[0], given)):
            rows = pl.ds(pl.multiple_of(rows * half, half), half)
            total = parts[0][rows, :].astype(F32)
            for part in parts[1:]:
                total = total + part[rows, :].astype(F32)
            out[c] = total.astype(out.dtype)


def sum_z(x_at, chunks, *earlier):
    count = len(chunks)
    pair, columns = chunks[0][0].shape
    flat = [part for parts in chunks for part in parts]
    return pl.pallas_call(
        with_earlier(sum_z_kernel, 1 + len(flat), len(earlier)),
        in_specs=[smem_spec()] + [vmem_spec()] * len(flat) + any_specs(earlier),
        out_specs=[vmem_spec()] * 2,
        out_shape=[
            jax.ShapeDtypeStruct((count, pair // 2, columns), F32),
            jax.ShapeDtypeStruct((count, pair // 2, columns), BF16),
        ],
        compiler_params=pltpu.CompilerParams(vmem_limit_bytes=VMEM_BYTES),
        name="sum_z",
    )(x_at, *flat, *earlier)


def sum_parts_kernel(parts, out):
    total = parts[0].astype(F32)
    for c in range(1, parts.shape[0]):
        total = total + parts[c].astype(F32)
    out[...] = total.astype(BF16)


def sum_parts(parts, *earlier):
    chunks, tokens, width = parts.shape
    return pl.pallas_call(
        with_earlier(sum_parts_kernel, 1, len(earlier)),
        grid=(tokens // EXPERT_ROWS,),
        in_specs=[pl.BlockSpec((chunks, EXPERT_ROWS, width), lambda s: (0, s, 0))]
        + any_specs(earlier),
        out_specs=pl.BlockSpec((EXPERT_ROWS, width), lambda s: (s, 0)),
        out_shape=jax.ShapeDtypeStruct((tokens, width), BF16),
        compiler_params=pltpu.CompilerParams(vmem_limit_bytes=VMEM_BYTES),
        name="sum_parts",
    )(parts, *earlier)


def adam_attention_kernel(q_share, o_share, *refs):
    states, outs = refs[:9], refs[9:18]
    gain_part = refs[18]
    q_width, kv_width = states[0].shape[1], states[3].shape[2]
    rate = (MODEL_DIM // 12) ** (-0.5)
    grad = q_share[:, :q_width]
    total = jnp.sum(states[0][...].astype(BF16).astype(F32) * grad, axis=1, keepdims=True)
    results = [
        adam_update(states[0][...], grad, states[1][...], states[2][...], rate, WEIGHT_DECAY)
    ]
    for out, result in zip(outs[:3], results[0]):
        out[...] = result
    for c in range(2):
        first = q_width + c * kv_width
        grad = q_share[:, first : first + kv_width]
        value = states[3][c]
        total = total + jnp.sum(value.astype(BF16).astype(F32) * grad, axis=1, keepdims=True)
        results = adam_update(value, grad, states[4][c], states[5][c], rate, WEIGHT_DECAY)
        for out, result in zip(outs[3:6], results):
            out[c] = result
    gain_part[...] = total
    results = adam_update(
        states[6][...], o_share[...], states[7][...], states[8][...],
        max(1, QUERY_HEADS * HEAD_DIM // 96) ** (-0.5), WEIGHT_DECAY,
    )
    for out, result in zip(outs[6:], results):
        out[...] = result


def adam_attention(q_share, o_share, states):
    outs = [(one.shape, F32) for one in states] + [((q_share.shape[0], 1), F32)]
    return whole_call(adam_attention_kernel, [q_share, o_share, *states], outs, (), "adam_attention")


def adam_experts_kernel(x_at, kept, got, *refs):
    states, outs = refs[:6], refs[6:]
    own = kept.shape[1]
    hidden = states[0].shape[3]
    mine = pl.program_id(0) // (pl.num_programs(0) // 2) == x_at[0]
    grad = jnp.where(mine, kept[0], got[0].astype(F32))
    for e in range(CHUNK):
        for part in range(2):
            first = hidden * (2 * e + part)
            results = adam_update(
                states[0][e, part], grad[:, first : first + hidden],
                states[1][e, part], states[2][e, part], MODEL_DIM ** (-0.5), WEIGHT_DECAY,
            )
            for out, result in zip(outs[:3], results):
                out[e, part] = result
        first = hidden * (2 * CHUNK + e)
        results = adam_update(
            states[3][e], grad[:, first : first + hidden], states[4][e], states[5][e],
            max(1, F // 256) ** (-0.5), WEIGHT_DECAY,
        )
        for out, result in zip(outs[3:], results):
            out[e] = result


def adam_experts(x_at, kept, got, gateup, down):
    chunks, own, columns = kept.shape
    experts, hidden = down[0].shape[0], down[0].shape[2]
    share = pl.BlockSpec((1, own, columns), lambda j: (j % chunks, 0, 0))
    big = pl.BlockSpec((CHUNK, 2, own, hidden), lambda j: (j, 0, 0, 0))
    small = pl.BlockSpec((CHUNK, own, hidden), lambda j: (j, 0, 0))
    return pl.pallas_call(
        adam_experts_kernel,
        grid=(experts // CHUNK,),
        in_specs=[smem_spec(), share, share] + [big] * 3 + [small] * 3,
        out_specs=[big] * 3 + [small] * 3,
        out_shape=[jax.ShapeDtypeStruct(gateup[0].shape, F32)] * 3
        + [jax.ShapeDtypeStruct(down[0].shape, F32)] * 3,
        compiler_params=pltpu.CompilerParams(vmem_limit_bytes=VMEM_BYTES),
        name="adam_experts",
    )(x_at, kept, got, *gateup, *down)


def join_tokens_kernel(own, first, second, out, turned):
    half = own.shape[0] // 2
    for at, part in ((0, own[:half, :]), (half, own[half:, :]), (2 * half, first[...]), (3 * half, second[...])):
        out[at : at + half, :] = part
        turned[:, at : at + half] = part.T


def join_tokens(own, first, second, *earlier):
    tokens, width = own.shape
    return pl.pallas_call(
        with_earlier(join_tokens_kernel, 3, len(earlier)),
        in_specs=[vmem_spec()] * 3 + any_specs(earlier),
        out_specs=[vmem_spec()] * 2,
        out_shape=[
            jax.ShapeDtypeStruct((2 * tokens, width), own.dtype),
            jax.ShapeDtypeStruct((width, 2 * tokens), own.dtype),
        ],
        compiler_params=pltpu.CompilerParams(vmem_limit_bytes=VMEM_BYTES),
        name="join_tokens",
    )(own, first, second, *earlier)


def move(array, dz=0, dy=0, dx=0):
    total = lax.axis_size("dp")
    inner = total // 16
    pairs = []
    for at in range(16):
        z, y, x = at // 4, at // 2 % 2, at % 2
        to = ((z + dz) % 4) * 4 + (y ^ dy) * 2 + (x ^ dx)
        pairs += [(at * inner + i, to * inner + i) for i in range(inner)]
    return lax.ppermute(array, "dp", pairs)


def place():
    at = lax.axis_index("dp") // (lax.axis_size("dp") // 16)
    return at // 4, at // 2 % 2, at % 2


def inner_groups(total):
    inner = total // 16
    return [[at * inner + i for i in range(inner)] for at in range(16)]


def inner_gather(shard, axis):
    total = lax.axis_size("dp")
    if total == 16:
        return shard
    return lax.all_gather(
        shard, "dp", axis=axis, tiled=True, axis_index_groups=inner_groups(total)
    )


def inner_scatter(share, axis):
    total = lax.axis_size("dp")
    if total == 16:
        return share
    return lax.psum_scatter(
        share, "dp", scatter_dimension=axis, tiled=True, axis_index_groups=inner_groups(total)
    )


def block_rows(parts, rows):
    z, y, x = place()
    starts = []
    for dz, dy, dx in parts:
        starts.append((((z + dz + 4) % 4) * 4 + (y ^ dy) * 2 + (x ^ dx)) * rows)
    return jnp.stack(starts).astype(jnp.int32)


def gather_z(shard):
    return jnp.stack([shard] + [move(shard, dz=-dz) for dz in Z_FROM[1:]])


def gather_ring(shard):
    below, above = move(shard, dz=1), move(shard, dz=-1)
    return [shard, below, above, move(below, dz=1)]


def send_z(parts):
    return [move(parts[k].astype(BF16), dz=Z_FROM[k]) for k in range(1, SLOTS)]


def scatter_z(parts, moved=None):
    result = parts[0]
    for one in moved or send_z(parts):
        result = result + one.astype(F32)
    return result


def gather_plane(own):
    half = own.shape[-1] // 2
    along_y, along_x = move(own, dy=1), move(own, dx=1)
    both = (move(along_y[..., :half], dx=1), move(along_x[..., half:], dy=1))
    return own, along_y, along_x, *both


def scatter_plane(pieces):
    own, along_y, along_x, both_one, both_two = pieces
    half = both_one.shape[-1]
    got_one, got_two = move(both_one, dx=1), move(both_two, dy=1)
    pass_y = jnp.concatenate(
        [(along_y[..., :half].astype(F32) + got_one.astype(F32)).astype(BF16), along_y[..., half:]],
        axis=-1,
    )
    pass_x = jnp.concatenate(
        [along_x[..., :half], (along_x[..., half:].astype(F32) + got_two.astype(F32)).astype(BF16)],
        axis=-1,
    )
    got_y, got_x = move(pass_y, dy=1), move(pass_x, dx=1)
    return scatter_z(
        [
            own[k].astype(F32) + got_y[k].astype(F32) + got_x[k].astype(F32)
            for k in range(SLOTS)
        ]
    )


PLANE = [(dz, dy, dx) for dy, dx in ((0, 0), (1, 0), (0, 1), (1, 1)) for dz in Z_FROM]


def join_kernel(rows_at, *refs):
    pieces, out = refs[:-1], refs[-1]
    slots, own, width = pieces[0].shape
    half = width // 2
    for at in range(4 * slots):
        rows = pl.ds(pl.multiple_of(rows_at[at], own), own)
        group, slot = at // slots, at % slots
        if group < 3:
            out[rows, :] = pieces[group][slot]
        else:
            out[rows, :half] = pieces[3][slot]
            out[rows, half:] = pieces[4][slot]


def part_kernel(rows_at, whole, *pieces):
    slots, own, width = pieces[0].shape
    half = width // 2
    for at in range(4 * slots):
        rows = pl.ds(pl.multiple_of(rows_at[at], own), own)
        group, slot = at // slots, at % slots
        if group < 3:
            pieces[group][slot] = whole[rows, :]
        else:
            pieces[3][slot] = whole[rows, :half]
            pieces[4][slot] = whole[rows, half:]


def smem_spec():
    return pl.BlockSpec(memory_space=pltpu.SMEM)


def vmem_spec():
    return pl.BlockSpec(memory_space=pltpu.VMEM)


def join_blocks(rows_at, pieces, earlier=()):
    slots, own, width = pieces[0].shape
    return pl.pallas_call(
        with_earlier(join_kernel, 6, len(earlier)),
        in_specs=[smem_spec()] + [vmem_spec()] * 5 + any_specs(earlier),
        out_specs=vmem_spec(),
        out_shape=jax.ShapeDtypeStruct((4 * slots * own, width), BF16),
        compiler_params=pltpu.CompilerParams(vmem_limit_bytes=VMEM_BYTES),
        name="join_blocks",
    )(rows_at, *pieces, *earlier)


def part_blocks(rows_at, whole, earlier=()):
    own, width = whole.shape[0] // (4 * SLOTS), whole.shape[1]
    full = jax.ShapeDtypeStruct((SLOTS, own, width), BF16)
    half = jax.ShapeDtypeStruct((SLOTS, own, width // 2), BF16)
    return pl.pallas_call(
        with_earlier(part_kernel, 2, len(earlier)),
        in_specs=[smem_spec(), vmem_spec()] + any_specs(earlier),
        out_specs=[vmem_spec()] * 5,
        out_shape=[full] * 3 + [half] * 2,
        compiler_params=pltpu.CompilerParams(vmem_limit_bytes=VMEM_BYTES),
        name="part_blocks",
    )(rows_at, whole, *earlier)


def after(value, *earlier):
    marks = []
    for one in earlier:
        slots = one.shape[0] if one.shape[0] == SLOTS else 1
        lead, rest = (slots > 1) * 1, one.ndim - 1
        marks.append(lax.slice(one, (lead,) + (0,) * rest, (slots,) + (1,) * rest))
    return lax.optimization_barrier((value, *marks))[0]


def split_three(values):
    high = values.astype(BF16)
    rest = values - high.astype(F32)
    middle = rest.astype(BF16)
    low = (rest - middle.astype(F32)).astype(BF16)
    return [high, middle, low]


def swap_cores(part):
    return lax.ppermute(part, "tensor", [(0, 1), (1, 0)])


def pair_sum(part):
    return part.astype(F32) + swap_cores(part).astype(F32)


def norm_backward(values, inverse, gain_row, upstream):
    scaled = values * inverse
    weighted = upstream * gain_row
    mean_term = jnp.mean(weighted * scaled, axis=-1, keepdims=True)
    return (inverse * (weighted - scaled * mean_term), jnp.sum(upstream * scaled, axis=0))


def adam_update(value, gradient, mean_old, square_old, rate, decay):
    mean_new = FIRST_DECAY * mean_old + (1.0 - FIRST_DECAY) * gradient
    square_new = SECOND_DECAY * square_old + (1.0 - SECOND_DECAY) * gradient * gradient
    mean_hat = mean_new / (1.0 - FIRST_DECAY**STEP)
    square_hat = square_new / (1.0 - SECOND_DECAY**STEP)
    updated = value - rate * (mean_hat / (jnp.sqrt(square_hat) + ADAM_EPSILON) + decay * value)
    return (mean_new, square_new, updated)


def shards(
    hidden_in,
    out_grad,
    routes,
    segments,
    norm_gains,
    gains_mean,
    gains_square,
    w_query,
    query_mean,
    query_square,
    key_value_weight,
    key_value_first_moment,
    key_value_second_moment,
    w_out,
    out_mean,
    out_square,
    w_router,
    router_mean,
    router_square,
    w_gateup,
    gateup_mean,
    gateup_square,
    w_down,
    down_mean,
    down_square,
):
    tokens, width = hidden_in.shape
    own = w_query.shape[0]
    experts, hidden = w_down.shape[0], w_down.shape[1]
    q_width, kv_width = w_query.shape[1], key_value_weight.shape[2]
    qkv_width = q_width + 2 * kv_width
    each = 2 + experts
    half_experts = experts // 2
    block = width // 16
    z_at, y_at, x_at = place()
    core = lax.axis_index("tensor")
    plane_rows = block_rows(PLANE, block)
    turned_down = [one.transpose(0, 2, 1) for one in (w_down, down_mean, down_square)]
    gateup_rows, down_rows = w_gateup, turned_down[0]
    if lax.axis_size("dp") > 16:
        gateup_rows = inner_gather(w_gateup.astype(BF16), 2)
        down_rows = inner_gather(down_rows.astype(BF16), 1)
    chunks = experts // (2 * CHUNK)
    first = x_at == 0
    half_width = HEAD_DIM // 2
    frequency = ROPE_BASE ** (-2.0 * jnp.arange(half_width, dtype=F32) / HEAD_DIM)
    frequency = jnp.concatenate([frequency] * 4)[None, :]
    turned_out = [one.T for one in (w_out, out_mean, out_square)]
    weights = (
        inner_gather(w_query, 0), inner_gather(key_value_weight, 1),
        inner_gather(turned_out[0], 0), inner_gather(w_router, 0), inner_gather(norm_gains, 1),
    )
    (
        qkv_blocks, out_blocks, small, normed_low, queries, keys, values, attended, lse,
        combine, combine_pair, cosine, sine, seg_col,
        middle, x_pair, x_turned, og_pair, og_turned, pairs, near, far,
    ) = forward_pass(
        weights, frequency, segments, routes, gateup_rows, down_rows, hidden_in, out_grad
    )
    dx, mix_pair, gate_turned, keep, z_got, near_grads, far_grads = experts_pass(
        x_pair, og_pair, x_turned, og_turned, combine_pair, pairs, near, far
    )
    qkv_share, output_share, input_grad, block_out, kept_share, got_share = backward_pass(
        out_blocks, queries, keys, values, attended, lse, cosine, sine, seg_col, segments, small,
        combine, gate_turned, qkv_blocks, normed_low, hidden_in, out_grad, middle, dx, mix_pair, keep,
        z_got, near_grads, far_grads,
    )[:6]
    kept_share, got_share = inner_scatter(kept_share, 1), inner_scatter(got_share, 1)
    x_here = x_at.astype(jnp.int32)[None]
    output_share = inner_scatter(output_share, 0)
    qkv_share = inner_scatter(qkv_share, 0)
    *attention_results, gain_one_part = adam_attention(
        qkv_share, output_share,
        [
            w_query, query_mean, query_square, key_value_weight, key_value_first_moment,
            key_value_second_moment, *turned_out,
        ],
    )
    gain_one_share = pair_sum(gain_one_part.T) / norm_gains[:1]
    gains_share = jnp.concatenate([gain_one_share, qkv_share[:, qkv_width][None, :]])
    router_share = qkv_share[:, qkv_width + 1 : qkv_width + 1 + experts]

    gains_result = adam_update(norm_gains, gains_share, gains_mean, gains_square, GAIN_RATE, 0.0)
    router_result = adam_update(
        w_router, router_share, router_mean, router_square, (4 * MODEL_DIM) ** (-0.5), WEIGHT_DECAY
    )
    expert_results = adam_experts(
        x_here, kept_share, got_share,
        (w_gateup, gateup_mean, gateup_square), turned_down,
    )
    expert_results = [*expert_results[:3], *(one.transpose(0, 2, 1) for one in expert_results[3:])]
    return (
        (block_out, input_grad)
        + gains_result
        + tuple(attention_results[:6])
        + tuple(one.T for one in attention_results[6:])
        + router_result
        + tuple(expert_results)
    )


def solution(mesh):
    tokens, gains = P("dp", None), P(None, "dp")
    query, keyval, out = P("dp", "tensor"), P(None, "dp", "tensor"), P("tensor", "dp")
    router, gateup, down = P("dp", None), P(None, None, "dp", "tensor"), P(None, "tensor", "dp")
    states = tuple(
        spec for one in (gains, query, keyval, out, router, gateup, down) for spec in (one,) * 3
    )
    return jax.shard_map(
        shards,
        mesh=mesh,
        in_specs=(tokens, tokens, tokens, P("dp")) + states,
        out_specs=(tokens, tokens) + states,
        check_vma=False,
    )
```

```python
import functools

import jax
import jax.numpy as jnp
from jax import lax
from jax.experimental import pallas as pl
from jax.experimental.pallas import tpu as pltpu
from jax.sharding import PartitionSpec as P

MODEL_DIM = 1536
QUERY_HEADS = 24
HEAD_DIM = 64
F = 512
SEQUENCE_LENGTH = 1024
STEP = 10

NORM_EPSILON = 1e-06
SCORE_SCALE = 0.015625
RESIDUAL_SCALE = 0.22
ROPE_BASE = 10000.0
FIRST_DECAY = 0.9
SECOND_DECAY = 0.95
ADAM_EPSILON = 1e-08
WEIGHT_DECAY = 0.1
GAIN_RATE = 0.6
MASK_VALUE = -1e30
HIGHEST_PRECISION = lax.Precision.HIGHEST

BF16 = jnp.bfloat16
F32 = jnp.float32
LANES = 128
ROWS = 256
VMEM_BYTES = 58 * 1024 * 1024

NN = (((1,), (0,)), ((), ()))
NT = (((1,), (1,)), ((), ()))
TN = (((0,), (0,)), ((), ()))


def dot(a, b, dims=NN):
    return lax.dot_general(a, b, dims, preferred_element_type=F32)


def seq_positions(segment_row):
    counter = jnp.arange(segment_row.shape[0], dtype=jnp.int32)
    earlier = jnp.concatenate([segment_row[:1] - 1, segment_row[:-1]])
    starts = lax.cummax(jnp.where(segment_row != earlier, counter, 0), axis=0)
    return counter - starts


def rope_tables(positions):
    half_width = HEAD_DIM // 2
    frequency = ROPE_BASE ** (-2.0 * jnp.arange(half_width, dtype=F32) / HEAD_DIM)
    angles = positions.astype(F32)[:, None] * frequency[None, :]
    cosine, sine = jnp.cos(angles), jnp.sin(angles)
    return (
        jnp.concatenate([cosine] * 4, axis=1),
        jnp.concatenate([-sine, sine] * 2, axis=1),
    )


def rotate_halves(slab):
    lane = lax.broadcasted_iota(jnp.int32, slab.shape, 1)
    ahead = pltpu.roll(slab, LANES - HEAD_DIM // 2, 1)
    behind = pltpu.roll(slab, HEAD_DIM // 2, 1)
    return jnp.where(lane % HEAD_DIM < HEAD_DIM // 2, ahead, behind)


def few_rows(count, base=None):
    for r in range(0, count, 16):
        yield pl.ds(r, 16) if base is None else pl.ds(pl.multiple_of(base + r, 16), 16)


def half_mask(rows, upper):
    lane = lax.broadcasted_iota(jnp.int32, (rows, LANES), 1)
    return (lane >= HEAD_DIM) if upper else (lane < HEAD_DIM)


def spread_heads(slab, lower_out, upper_out, index):
    rows = slab.shape[0]
    moved = pltpu.roll(slab.astype(F32), HEAD_DIM, 1).astype(BF16)
    zero = jnp.zeros_like(slab)
    low, high = half_mask(rows, False), half_mask(rows, True)
    lower_out[index] = jnp.where(low, slab, zero)
    upper_out[index] = jnp.where(high, moved, zero)
    lower_out[index + 1] = jnp.where(low, moved, zero)
    upper_out[index + 1] = jnp.where(high, slab, zero)


def fill_bias(bias, seg_col, seg_row):
    span = bias.shape[0]
    for at in range(0, span, ROWS):
        rows_at = at + lax.broadcasted_iota(jnp.int32, (ROWS, span), 0)
        cols_at = lax.broadcasted_iota(jnp.int32, (ROWS, span), 1)
        allowed = (rows_at >= cols_at) & (seg_col[at : at + ROWS, :] == seg_row[...])
        bias[at : at + ROWS, :] = jnp.where(allowed, 0.0, MASK_VALUE).astype(F32)


def with_earlier(kernel, inputs, count):
    def run(*refs):
        kernel(*refs[:inputs], *refs[inputs + count :])

    return run


def any_specs(arrays):
    return [pl.BlockSpec(memory_space=pl.ANY)] * len(arrays)


def attention_forward_kernel(
    lin_ref, kv_ref, cos_ref, sin_ref, seg_col, seg_row,
    out_ref, q_ref, k_ref, v_ref, lse_ref,
    bias, k_low, k_high, v_low, v_high,
):
    slab_at = pl.program_id(0)
    span = lin_ref.shape[0]
    kv_slabs = kv_ref.shape[1] // (2 * LANES)

    @pl.when(slab_at == 0)
    def _():
        fill_bias(bias, seg_col, seg_row)
        for j in range(kv_slabs):
            lanes = slice(j * LANES, (j + 1) * LANES)
            lin = kv_ref[:, lanes]
            keys = (lin * cos_ref[...] + rotate_halves(lin) * sin_ref[...]).astype(BF16)
            k_ref[:, lanes] = keys
            spread_heads(keys, k_low, k_high, 2 * j)
            lanes = slice((kv_slabs + j) * LANES, (kv_slabs + j + 1) * LANES)
            values = kv_ref[:, lanes].astype(BF16)
            v_ref[:, slice(j * LANES, (j + 1) * LANES)] = values
            spread_heads(values, v_low, v_high, 2 * j)

    lin = lin_ref[...]
    q_ref[...] = (lin * cos_ref[...] + rotate_halves(lin) * sin_ref[...]).astype(BF16)
    kv_even, kv_odd = (2 * slab_at) // 3, (2 * slab_at + 1) // 3
    for at in range(0, span, ROWS):
        rows = slice(at, at + ROWS)
        queries = q_ref[rows, :]
        total = None
        stats = []
        for keys, values, kv_at in ((k_low, v_low, kv_even), (k_high, v_high, kv_odd)):
            upto = at + ROWS
            scores = dot(queries, keys[kv_at, :upto, :], NT) * SCORE_SCALE + bias[rows, :upto]
            highest = jnp.max(scores, axis=1, keepdims=True)
            weights = jnp.exp(scores - highest)
            summed = jnp.sum(weights, axis=1, keepdims=True)
            probability = (weights * (1.0 / summed)).astype(BF16)
            part = dot(probability, values[kv_at, :upto, :])
            total = part if total is None else total + part
            stats.append(highest + jnp.log(summed))
        out_ref[rows, :] = total.astype(BF16)
        spread = jnp.where(half_mask(ROWS, False), stats[0], stats[1])
        turned = spread.T
        lse_ref[0, 0:1, rows] = turned[0:1, :]
        lse_ref[0, 1:2, rows] = turned[HEAD_DIM : HEAD_DIM + 1, :]


def attention_forward(qkv_lin, cosine, sine, segment_row, earlier=()):
    span = qkv_lin.shape[0]
    q_width = MODEL_DIM // 2
    kv_width = (qkv_lin.shape[1] - q_width) // 2
    slabs, kv_heads = q_width // LANES, kv_width // HEAD_DIM
    whole = lambda shape: pl.BlockSpec(shape, lambda g: (0,) * len(shape))
    slab = pl.BlockSpec((span, LANES), lambda g: (0, g))
    q_lin, kv_lin = qkv_lin[:, :q_width], qkv_lin[:, q_width:]
    return pl.pallas_call(
        with_earlier(attention_forward_kernel, 6, len(earlier)),
        grid=(slabs,),
        in_specs=[
            slab, whole((span, 2 * kv_width)), whole((span, LANES)), whole((span, LANES)),
            whole((span, 1)), whole((1, span)),
        ]
        + any_specs(earlier),
        out_specs=[
            slab, slab, whole((span, kv_width)), whole((span, kv_width)),
            pl.BlockSpec((1, 8, span), lambda g: (g, 0, 0)),
        ],
        out_shape=[
            jax.ShapeDtypeStruct((span, q_width), BF16),
            jax.ShapeDtypeStruct((span, q_width), BF16),
            jax.ShapeDtypeStruct((span, kv_width), BF16),
            jax.ShapeDtypeStruct((span, kv_width), BF16),
            jax.ShapeDtypeStruct((slabs, 8, span), F32),
        ],
        scratch_shapes=[pltpu.VMEM((span, span), F32)]
        + [pltpu.VMEM((kv_heads, span, LANES), BF16)] * 4,
        compiler_params=pltpu.CompilerParams(vmem_limit_bytes=VMEM_BYTES),
        cost_estimate=pl.CostEstimate(
            flops=32 * slabs * span * span * LANES, bytes_accessed=16 * span * q_width,
            transcendentals=slabs * span * span,
        ),
        name="attention_forward",
    )(q_lin, kv_lin, cosine, sine, segment_row[:, None], segment_row[None, :], *earlier)


def attention_backward_kernel(
    q_ref, k_ref, v_ref, out_ref, grad_ref, cos_ref, sin_ref, seg_col, seg_row, lse_ref,
    dq_ref, dkv_ref,
    bias, k_low, k_high, v_low, v_high, dk_low, dk_high, dv_low, dv_high, dq_sum,
):
    slab_at = pl.program_id(0)
    span = q_ref.shape[0]
    kv_slabs = k_ref.shape[1] // LANES

    @pl.when(slab_at == 0)
    def _():
        for at in range(0, span, ROWS):
            keys_at = at + lax.broadcasted_iota(jnp.int32, (ROWS, span), 0)
            rows_at = lax.broadcasted_iota(jnp.int32, (ROWS, span), 1)
            allowed = (rows_at >= keys_at) & (seg_col[at : at + ROWS, :] == seg_row[...])
            bias[at : at + ROWS, :] = jnp.where(allowed, 0.0, MASK_VALUE).astype(F32)
        for j in range(kv_slabs):
            lanes = slice(j * LANES, (j + 1) * LANES)
            spread_heads(k_ref[:, lanes], k_low, k_high, 2 * j)
            spread_heads(v_ref[:, lanes], v_low, v_high, 2 * j)
        for sums in (dk_low, dk_high, dv_low, dv_high):
            sums[...] = jnp.zeros_like(sums)

    kv_even, kv_odd = (2 * slab_at) // 3, (2 * slab_at + 1) // 3
    for at in range(0, span, ROWS):
        rows = slice(at, at + ROWS)
        upto = at + ROWS
        queries, grads = q_ref[rows, :], grad_ref[rows, :]
        turned = (grads.astype(F32) * out_ref[rows, :].astype(F32)).T
        zero = jnp.zeros_like(queries)
        dq_part = None
        for upper, keys, values, dk_sum, dv_sum, kv_at in (
            (False, k_low, v_low, dk_low, dv_low, kv_even),
            (True, k_high, v_high, dk_high, dv_high, kv_odd),
        ):
            first = HEAD_DIM if upper else 0
            delta = jnp.sum(turned[first : first + HEAD_DIM, :], axis=0, keepdims=True)
            head = 1 if upper else 0
            total = lse_ref[0, head : head + 1, rows]
            keys_here = keys[kv_at, :upto, :]
            scores = dot(keys_here, queries, NT) * SCORE_SCALE + bias[:upto, rows]
            probability = jnp.exp(scores - total)
            prob_grad = dot(values[kv_at, :upto, :], grads, NT)
            score_grad = (probability * (prob_grad - delta)).astype(BF16)
            mask = half_mask(ROWS, upper)
            dv_sum[kv_at, :upto, :] += dot(
                probability.astype(BF16), jnp.where(mask, grads, zero)
            )
            dk_sum[kv_at, :upto, :] += dot(score_grad, jnp.where(mask, queries, zero))
            part = dot(score_grad, keys_here, TN)
            dq_part = part if dq_part is None else dq_part + part
        dq_sum[rows, :] = dq_part * SCORE_SCALE
    slab = dq_sum[...]
    dq_ref[...] = (slab * cos_ref[...] - rotate_halves(slab) * sin_ref[...]).astype(BF16)

    @pl.when(slab_at == pl.num_programs(0) - 1)
    def _():
        low = half_mask(span, False)

        def joined(sums_low, sums_high, j):
            one = sums_low[2 * j] + pltpu.roll(sums_high[2 * j], HEAD_DIM, 1)
            two = pltpu.roll(sums_low[2 * j + 1], HEAD_DIM, 1) + sums_high[2 * j + 1]
            return jnp.where(low, one, two)

        for j in range(kv_slabs):
            slab = joined(dk_low, dk_high, j) * SCORE_SCALE
            dkv_ref[:, j * LANES : (j + 1) * LANES] = (
                slab * cos_ref[...] - rotate_halves(slab) * sin_ref[...]
            ).astype(BF16)
            at = (kv_slabs + j) * LANES
            dkv_ref[:, at : at + LANES] = joined(dv_low, dv_high, j).astype(BF16)


def attention_backward(
    queries, keys, values, attended, grad, cosine, sine, segment_row, lse, earlier=()
):
    span, q_width = queries.shape
    kv_width = keys.shape[1]
    slabs, kv_heads = q_width // LANES, kv_width // HEAD_DIM
    whole = lambda shape: pl.BlockSpec(shape, lambda g: (0,) * len(shape))
    slab = pl.BlockSpec((span, LANES), lambda g: (0, g))
    return pl.pallas_call(
        with_earlier(attention_backward_kernel, 10, len(earlier)),
        grid=(slabs,),
        in_specs=[
            slab, whole((span, kv_width)), whole((span, kv_width)), slab, slab,
            whole((span, LANES)), whole((span, LANES)), whole((span, 1)), whole((1, span)),
            pl.BlockSpec((1, 8, span), lambda g: (g, 0, 0)),
        ]
        + any_specs(earlier),
        out_specs=[slab, whole((span, 2 * kv_width))],
        out_shape=[
            jax.ShapeDtypeStruct((span, q_width), BF16),
            jax.ShapeDtypeStruct((span, 2 * kv_width), BF16),
        ],
        scratch_shapes=[pltpu.VMEM((span, span), F32)]
        + [pltpu.VMEM((kv_heads, span, LANES), BF16)] * 4
        + [pltpu.VMEM((kv_heads, span, LANES), F32)] * 4
        + [pltpu.VMEM((span, LANES), F32)],
        compiler_params=pltpu.CompilerParams(vmem_limit_bytes=VMEM_BYTES),
        cost_estimate=pl.CostEstimate(
            flops=40 * slabs * span * span * LANES, bytes_accessed=16 * span * q_width,
            transcendentals=slabs * span * span,
        ),
        name="attention_backward",
    )(
        queries, keys, values, attended, grad, cosine, sine,
        segment_row[:, None], segment_row[None, :], lse, *earlier,
    )


EXPERT_ROWS = 256
EXPERT_VMEM = 63 * 1024 * 1024
SLOTS = 4
Z_FROM = (0, -1, 1, 2)
CHUNK = 2
LATE = 2
SENT = 2
MESH_ID = pl.DeviceIdType.MESH


def experts_kernel(
    inner, chunks, row_steps, x_ref, og_ref, xt_ref, ogt_ref, combine_ref,
    pairs_ref, near_ref, far_ref,
    dx_own, dx_twin, dx_other, mix_out, gate_out, *refs,
):
    keep_outs, refs = refs[:SENT], refs[SENT:]
    part_outs, refs = refs[:SENT], refs[SENT:]
    near_outs, refs = refs[: chunks - SENT], refs[chunks - SENT :]
    late_out, first_out, far_out, refs = *refs[:3], refs[3:]
    slots, arrived, held_both, held_down, dx_sum, mix_sum, twin_rows, twin_mix = refs[:8]
    gates, gate_kept, gate_got, gate_full, gate_twin, send, recv, local = refs[8:]
    weights, grads = slots.at[pl.ds(1, chunks)], slots
    near = Neighbours(inner)
    copies = Copies(send, recv, local)
    z, y, x, core, spots = near.z, near.y, near.x, near.core, near.spots
    step = pl.program_id(0)
    steps = row_steps + SLOTS
    chunk, turn = step // steps, step % steps
    last = chunks - 1
    width = x_ref.shape[1]
    block = width // 16
    hidden = held_down.shape[1] // CHUNK
    both = 2 * hidden * CHUNK
    lane = lax.broadcasted_iota(jnp.int32, (EXPERT_ROWS, LANES), 1)
    tokens = dx_sum.shape[0] // 2
    tiles = tokens // EXPERT_ROWS
    tile = (turn + tiles) % row_steps
    rows = pl.ds(pl.multiple_of(tile * EXPERT_ROWS, EXPERT_ROWS), EXPERT_ROWS)

    def near_piece(c, k):
        return pairs_ref.at[c] if k == 0 else near_ref.at[c, k - 1]

    def near_copy(c, k):
        copies.copy(
            lambda c=c, k=k: (near_piece(c, k), weights.at[c, spots[k], y]), ("near", c, k), False
        )

    def near_wait(c, k):
        copies.wait_copy(
            lambda c=c, k=k: (near_piece(c, k), weights.at[c, spots[k], y]), ("near", c, k)
        )

    def far_ends(c, k):
        return far_ref.at[c, k], weights.at[c, spots[k], 1 - y]

    @pl.when(step == 0)
    def _():
        near.greet()
        gates[...] = jnp.zeros_like(gates)
        for k in range(SLOTS):
            near_copy(0, k)
            copies.copy(lambda k=k: far_ends(0, k), ("far", 0, k), False)
        copies.remote(
            lambda: (pairs_ref.at[last], weights.at[last, z, y]), ("y",), ("y",), near.over_y
        )
        for k in range(1, SLOTS):
            copies.remote(
                lambda: (pairs_ref.at[last], weights.at[last, z, y]),
                ("z", k), ("z", BACK[k]), near.along[k],
            )
        for c in range(LATE, last):
            for k in range(1, SLOTS):
                copies.remote(
                    lambda c=c, k=k: (near_piece(c, k), weights.at[c, spots[k], y]),
                    ("f", c, k), ("f", c, k), near.over_y,
                )
        for c in range(1, chunks):
            for k in range(SLOTS if c < last else 1):
                near_copy(c, k)
                if c < LATE or (c < last and k == 0):
                    copies.copy(lambda c=c, k=k: far_ends(c, k), ("far", c, k), False)

    @pl.when(step == steps)
    def _():
        copies.arrived(weights.at[last, z, 1 - y], ("y",), near.over_y)
        for k in range(1, SLOTS):
            copies.remote(
                lambda: (weights.at[last, z, 1 - y],) * 2,
                ("z2", k), ("z2", BACK[k]), near.along[k],
            )

    for c in range(chunks):

        @pl.when(step == c * steps)
        def _():
            for k in range(SLOTS):
                if c < last or k == 0:
                    near_wait(c, k)
                if c < LATE or (c < last and k == 0):
                    copies.wait_copy(lambda c=c, k=k: far_ends(c, k), ("far", c, k))
                elif c < last:
                    copies.arrived(weights.at[c, spots[k], 1 - y], ("f", c, k), near.over_y)
                elif k > 0:
                    copies.arrived(weights.at[c, spots[k], y], ("z", k), near.along[k])
                    copies.arrived(weights.at[c, spots[k], 1 - y], ("z2", k), near.along[k])

    def add_arrived(c):
        copies.arrived(arrived.at[c], ("sum", c), near.over_y)
        for k in range(SLOTS):
            own = grads.at[c, spots[k], y]
            for here in few_rows(own.shape[0]):
                own[here, :] = (
                    own[here, :].astype(F32) + arrived[c, spots[k], here, :].astype(F32)
                ).astype(BF16)
        copies.copy(lambda c=c: (grads.at[c, z, y], keep_outs[c]), ("keep", c))
        for k in range(1, SLOTS):
            copies.remote(
                lambda c=c, k=k: (grads.at[c, spots[k], y], part_outs[c].at[BACK[k] - 1]),
                ("part", c, k), ("part", c, BACK[k]), near.along[k],
            )

    @pl.when(step == 2 * steps + 3)
    def _():
        add_arrived(0)

    @pl.when(step == 3 * steps + 3)
    def _():
        add_arrived(1)

    @pl.when(turn < row_steps)
    def _():
        for e in range(CHUNK):
            first = 2 * hidden * e
            w_both = weights[chunk, :, :, :, first : first + 2 * hidden].reshape(width, 2 * hidden)
            start = both + hidden * e
            w_down = weights[chunk, :, :, :, start : start + hidden].reshape(width, hidden)
            gate_up = dot(x_ref[...], w_both)
            raw = dot(og_ref[...], w_down) * RESIDUAL_SCALE
            gate, up = gate_up[:, :hidden], gate_up[:, hidden:]
            gate_lane = lax.broadcasted_iota(
                jnp.int32, (EXPERT_ROWS, combine_ref.shape[1]), 1
            )
            column = jnp.sum(
                jnp.where(gate_lane == chunk * CHUNK + e, combine_ref[...], 0.0),
                axis=1, keepdims=True,
            )
            sigmoid = 1.0 / (1.0 + jnp.exp(-gate))
            active = gate * sigmoid
            inner_value = (active * up).astype(BF16).astype(F32)
            held_down[rows, hidden * e : hidden * (e + 1)] = (inner_value * column).astype(BF16)
            gates[rows, :] = jnp.where(
                lane == chunk * CHUNK + e,
                jnp.sum(inner_value * raw, axis=1, keepdims=True),
                gates[rows, :],
            )
            inner_grad = raw * column
            held_both[rows, first : first + hidden] = (
                inner_grad * up * sigmoid * (1.0 + gate * (1.0 - sigmoid))
            ).astype(BF16)
            held_both[rows, first + hidden : first + 2 * hidden] = (inner_grad * active).astype(BF16)

        def sums(add):
            for part in range(SLOTS):
                cols = slice(4 * block * part, 4 * block * (part + 1))
                w_both = weights[chunk, part, :, :, :both].reshape(4 * block, both)
                w_down = weights[chunk, part, :, :, both:].reshape(4 * block, hidden * CHUNK)
                mix = dot(held_down[rows, :], w_down, NT)
                dx = dot(held_both[rows, :], w_both, NT)
                if add:
                    mix = mix + mix_sum[rows, cols].astype(F32)
                    dx = dx + dx_sum[rows, cols].astype(F32)
                mix_sum[rows, cols] = mix.astype(BF16)
                dx_sum[rows, cols] = dx.astype(BF16)

        @pl.when(chunk == 0)
        def _():
            sums(False)

        @pl.when(chunk > 0)
        def _():
            sums(True)

    @pl.when(turn >= row_steps)
    def _():
        part = turn - row_steps
        grads[chunk, part, :, :, :both] = (
            dot(xt_ref[...], held_both[...]).astype(BF16).reshape(2, 2 * block, both)
        )
        grads[chunk, part, :, :, both:] = (
            (dot(ogt_ref[...], held_down[...]) * RESIDUAL_SCALE)
            .astype(BF16)
            .reshape(2, 2 * block, hidden * CHUNK)
        )

    begin = last * steps
    for i in range(2):
        for c in range(2):
            mine = pl.ds(tokens + (2 * c + i) * EXPERT_ROWS, EXPERT_ROWS)
            there = pl.ds((2 * c + i) * EXPERT_ROWS, EXPERT_ROWS)

            @pl.when((step == begin + 2 * c + i) & (core != c))
            def _():
                for name, total, got in (("t", dx_sum, twin_rows), ("mt", mix_sum, twin_mix)):
                    copies.remote(
                        lambda: (total.at[mine], got.at[i]), (name, i), (name, i), near.twin,
                        last=False,
                    )

            @pl.when((step == begin + 2 + 2 * c + i) & (core == c))
            def _():
                for name, total, got in (("t", dx_sum, twin_rows), ("mt", mix_sum, twin_mix)):
                    copies.arrived(got.at[i], (name, i), near.twin)
                    for here in few_rows(EXPERT_ROWS):
                        at = pl.ds(mine.start + here.start, 16)
                        total[at, :] = (
                            total[at, :].astype(F32) + got[i, here, :].astype(F32)
                        ).astype(BF16)
                copies.remote(
                    lambda: (dx_sum.at[mine], dx_other.at[there]), ("o", i), ("o", i), near.over_x,
                    last=False,
                )

            @pl.when((step == begin + steps - 2 + i) & (core == c))
            def _():
                copies.arrived(dx_other.at[there], ("o", i), near.over_x)
                copies.remote(
                    lambda: (dx_other.at[there],) * 2, ("o2", i), ("o2", i), near.twin, last=False
                )

    for i in range(tiles):

        @pl.when(step == begin + tiles + i)
        def _():
            own = pl.ds(i * EXPERT_ROWS, EXPERT_ROWS)
            copies.copy(lambda own=own: (dx_sum.at[own], dx_own.at[own]), ("own", i))
            copies.remote(
                lambda own=own: (dx_sum.at[own], dx_twin.at[own]), ("own", i), ("own", i), near.twin
            )

    shares = gate_kept.shape[0]

    @pl.when(step == begin + row_steps)
    def _():
        copies.copy(lambda: (mix_sum, mix_out), "mix")
        turned = gates[...].T[:shares, :]
        gate_kept[...] = turned
        copies.remote(
            lambda: (gate_kept.at[:, pl.ds(tokens, tokens)], gate_got), ("g",), ("g",), near.over_x
        )

    @pl.when(step == begin + steps - 2)
    def _():
        copies.arrived(gate_got, ("g",), near.over_x)
        gate_full[pl.ds(pl.multiple_of(x * shares, shares), shares), :] = gate_kept[:, :tokens]
        gate_full[pl.ds(pl.multiple_of((1 - x) * shares, shares), shares), :] = gate_got[...]
        copies.remote(lambda: (gate_full, gate_twin), ("g2",), ("g2",), near.twin)

    for c in range(chunks):

        @pl.when(step == (c + 1) * steps - 1)
        def _():
            if c < SENT:
                copies.remote(
                    lambda c=c: (grads.at[c, :, 1 - y], arrived.at[c]),
                    ("sum", c), ("sum", c), near.over_y,
                )
            else:
                for k in range(SLOTS):
                    copies.copy(
                        lambda c=c, k=k: (grads.at[c, spots[k], y], near_outs[c - SENT].at[k]),
                        ("near out", c, k),
                    )
                    if c < last and k == 0:
                        copies.copy(lambda c=c: (grads.at[c, z, 1 - y], first_out), "first out")
                    elif c < last:
                        copies.remote(
                            lambda c=c, k=k: (grads.at[c, spots[k], 1 - y], late_out.at[k - 1]),
                            ("late", k), ("late", k), near.over_y,
                        )
                    else:
                        copies.copy(
                            lambda c=c, k=k: (grads.at[c, spots[k], 1 - y], far_out.at[k]),
                            ("far out", k),
                        )

    @pl.when(step == chunks * steps - 1)
    def _():
        copies.arrived(gate_twin, ("g2",), near.twin)
        gate_out[...] = gate_full[...] + gate_twin[...]
        for i in range(tiles):
            copies.arrived(
                dx_twin.at[pl.ds(i * EXPERT_ROWS, EXPERT_ROWS)], ("own", i), near.twin
            )
        for i in range(2):
            for c in range(2):
                mine = pl.ds(tokens + (2 * c + i) * EXPERT_ROWS, EXPERT_ROWS)
                there = pl.ds((2 * c + i) * EXPERT_ROWS, EXPERT_ROWS)

                @pl.when(core != c)
                def _():
                    copies.sent(lambda: (dx_sum.at[mine], twin_rows.at[i]), ("t", i), near.twin)
                    copies.sent(lambda: (mix_sum.at[mine], twin_mix.at[i]), ("mt", i), near.twin)
                    copies.arrived(dx_other.at[there], ("o2", i), near.twin)

                @pl.when(core == c)
                def _():
                    copies.sent(
                        lambda: (dx_sum.at[mine], dx_other.at[there]), ("o", i), near.over_x
                    )
                    copies.sent(lambda: (dx_other.at[there],) * 2, ("o2", i), near.twin)

        for c in range(SENT):
            for k in range(1, SLOTS):
                copies.arrived(part_outs[c].at[k - 1], ("part", c, k), near.along[k])
        for k in range(1, SLOTS):
            copies.arrived(late_out.at[k - 1], ("late", k), near.over_y)
        copies.finish()


def experts_pass(x, og, xt, ogt, combine, pairs, near, far):
    tokens, width = x.shape
    chunks, pair, columns = pairs.shape
    hidden = columns // (3 * CHUNK)
    shares = chunks * CHUNK
    row_steps = tokens // EXPERT_ROWS
    steps = row_steps + SLOTS
    inner = lax.axis_size("dp") // 16
    row_at = lambda s: ((jnp.minimum(s % steps, row_steps - 1) + row_steps // 2) % row_steps, 0)
    width_at = lambda s: (jnp.maximum(s % steps - row_steps, 0), 0)
    row = pl.BlockSpec((EXPERT_ROWS, width), row_at)
    turned = pl.BlockSpec((width // SLOTS, tokens), width_at)
    anywhere = pl.BlockSpec(memory_space=pl.ANY)
    left = chunks - SENT
    dma = pltpu.SemaphoreType.DMA
    shape = jax.ShapeDtypeStruct
    outs = pl.pallas_call(
        functools.partial(experts_kernel, inner, chunks, row_steps),
        grid=(chunks * steps,),
        in_specs=[row, row, turned, turned, pl.BlockSpec((EXPERT_ROWS, combine.shape[1]), row_at)]
        + [anywhere] * 3,
        out_specs=[anywhere] * 4
        + [pl.BlockSpec((2 * shares, tokens // 2), lambda s: (0, 0))]
        + [anywhere] * (2 * SENT + left + 3),
        out_shape=[shape((tokens // 2, width), BF16)] * 3
        + [shape((tokens, width), BF16), shape((2 * shares, tokens // 2), F32)]
        + [shape((pair, columns), BF16)] * SENT
        + [shape((SLOTS - 1, pair, columns), BF16)] * SENT
        + [shape((SLOTS, pair, columns), BF16)] * left
        + [shape((SLOTS - 1, pair, columns), BF16), shape((pair, columns), BF16)]
        + [shape((SLOTS, pair, columns), BF16)],
        scratch_shapes=[
            pltpu.VMEM((chunks + 1, SLOTS, 2, pair, columns), BF16),
            pltpu.VMEM((SENT, SLOTS, pair, columns), BF16),
            pltpu.VMEM((tokens, 2 * hidden * CHUNK), BF16),
            pltpu.VMEM((tokens, hidden * CHUNK), BF16),
            pltpu.VMEM((tokens, width), BF16),
            pltpu.VMEM((tokens, width), BF16),
            pltpu.VMEM((2, EXPERT_ROWS, width), BF16),
            pltpu.VMEM((2, EXPERT_ROWS, width), BF16),
            pltpu.VMEM((tokens, LANES), F32),
            pltpu.VMEM((shares, tokens), F32),
            pltpu.VMEM((shares, tokens // 2), F32),
            pltpu.VMEM((2 * shares, tokens // 2), F32),
            pltpu.VMEM((2 * shares, tokens // 2), F32),
            dma((48,)), dma((48,)), dma((48,)),
        ],
        compiler_params=pltpu.CompilerParams(
            vmem_limit_bytes=EXPERT_VMEM, collective_id=0, has_side_effects=True
        ),
        cost_estimate=pl.CostEstimate(
            flops=8 * tokens * width * chunks * columns,
            bytes_accessed=2 * chunks * width * columns, transcendentals=0,
        ),
        name="experts_pass",
    )(x, og, xt, ogt, combine, pairs, near, far)
    dx, mix, gate = outs[:3], outs[3], outs[4]
    rest = outs[5:]
    keep, parts, rest = rest[:SENT], rest[SENT : 2 * SENT], rest[2 * SENT :]
    return dx, mix, gate, keep, parts, rest[:left], rest[left:]


class Copies:
    def __init__(self, send, recv, local):
        self.send, self.recv, self.local = send, recv, local
        self.sends, self.recvs, self.locals, self.started = {}, {}, {}, []

    def remote(self, ends, name, arrives, device, last=True):
        sent = self.sends.setdefault(name, len(self.sends))
        got = self.recvs.setdefault(arrives, len(self.recvs))

        def make():
            source, target = ends()
            return pltpu.make_async_remote_copy(
                source, target, self.send.at[sent], self.recv.at[got],
                device_id=device, device_id_type=MESH_ID,
            )

        make().start()
        if last:
            self.started.append(lambda: make().wait_send())

    def sent(self, ends, name, device):
        source, target = ends()
        pltpu.make_async_remote_copy(
            source, target, self.send.at[self.sends[name]], self.recv.at[0],
            device_id=device, device_id_type=MESH_ID,
        ).wait_send()

    def arrived(self, place, name, device):
        got = self.recvs.setdefault(name, len(self.recvs))
        pltpu.make_async_remote_copy(
            place, place, self.send.at[0], self.recv.at[got],
            device_id=device, device_id_type=MESH_ID,
        ).wait_recv()

    def copy(self, ends, name, wait_last=True):
        at = self.locals.setdefault(name, len(self.locals))

        def make():
            return pltpu.make_async_copy(*ends(), self.local.at[at])

        make().start()
        if wait_last:
            self.started.append(lambda: make().wait())
        return lambda: make().wait()

    def wait_copy(self, ends, name):
        pltpu.make_async_copy(*ends(), self.local.at[self.locals[name]]).wait()

    def finish(self):
        for wait in self.started:
            wait()


class Neighbours:
    def __init__(self, inner):
        me = lax.axis_index("dp")
        at = me // inner
        self.core = lax.axis_index("tensor")
        self.z, self.y, self.x = at // 4, at // 2 % 2, at % 2
        self.spots = [(self.z + dz + 4) % 4 for dz in Z_FROM]
        self.along = [{"dp": me + (spot - self.z) * 4 * inner} for spot in self.spots]
        self.over_y = {"dp": me + (1 - 2 * self.y) * 2 * inner}
        self.over_x = {"dp": me + (1 - 2 * self.x) * inner}
        self.twin = {"tensor": 1 - self.core}
        self.blocks = {
            (k, other_y, other_x): self.spots[k] * 4
            + (1 - self.y if other_y else self.y) * 2
            + (1 - self.x if other_x else self.x)
            for k in range(SLOTS)
            for other_y in (0, 1)
            for other_x in (0, 1)
        }

    def greet(self):
        barrier = pltpu.get_barrier_semaphore()
        devices = [*self.along[1:], self.over_y, self.over_x, self.twin]
        for device in devices:
            pl.semaphore_signal(barrier, inc=1, device_id=device, device_id_type=MESH_ID)
        pl.semaphore_wait(barrier, len(devices))

    def block(self, k, other_y, other_x):
        return self.blocks[k, other_y, other_x]


BACK = (0, 2, 1, 3)


class Gather:
    def __init__(self, copies, near, shard, full, tag):
        self.copies, self.near, self.shard, self.full, self.tag = copies, near, shard, full, tag
        self.split = full.shape[2] // (2 * LANES) * LANES

    def source(self, k):
        return self.shard if k == 0 else self.full.at[self.near.block(k, 0, 0)]

    def begin(self):
        for k in range(1, SLOTS):
            self.copies.remote(
                lambda: (self.shard, self.full.at[self.near.block(0, 0, 0)]),
                (self.tag, "z", k), (self.tag, "z", BACK[k]), self.near.along[k],
            )
        self.full[self.near.block(0, 0, 0)] = self.shard[...]

    def spread(self, k):
        near, place = self.near, self.full.at[self.near.block(k, 0, 0)]
        if k > 0:
            self.copies.arrived(place, (self.tag, "z", k), near.along[k])
        for way, device in (("y", near.over_y), ("x", near.over_x)):
            name = (self.tag, way, k)
            self.copies.remote(
                lambda: (self.source(k), self.full.at[near.block(k, 0, 0)]), name, name, device
            )

    def cross(self, k):
        near = self.near
        from_y = self.full.at[near.block(k, 1, 0)]
        from_x = self.full.at[near.block(k, 0, 1)]
        self.copies.arrived(from_y, (self.tag, "y", k), near.over_y)
        self.copies.remote(
            lambda: (self.full.at[near.block(k, 1, 0), :, : self.split],) * 2,
            (self.tag, "one", k), (self.tag, "one", k), near.over_x,
        )
        self.copies.arrived(from_x, (self.tag, "x", k), near.over_x)
        self.copies.remote(
            lambda: (self.full.at[near.block(k, 0, 1), :, self.split :],) * 2,
            (self.tag, "two", k), (self.tag, "two", k), near.over_y,
        )

    def end(self):
        near = self.near
        for k in range(SLOTS):
            place = self.full.at[near.block(k, 1, 1)]
            self.copies.arrived(place.at[:, : self.split], (self.tag, "one", k), near.over_x)
            self.copies.arrived(place.at[:, self.split :], (self.tag, "two", k), near.over_y)


def roll_left(slab, lanes):
    return pltpu.roll(slab, LANES - lanes, 1)


def forward_kernel(
    inner, w_query, w_keyval, w_out, w_router, gains, frequency, seg_row, routes,
    gateup_hbm, down_hbm, hidden_hbm, og_hbm,
    small, combine, combine_pair, seg_col,
    q_full_out, o_full_out, normed_out, q_out, k_out, v_out, attended_out, lse_out, cos_out, sin_out,
    middle_hbm, x_hbm, xt_hbm, og_pair, ogt_hbm, pairs_hbm, near_hbm, far_hbm,
    hidden, gateup, down, given, pairs, bias, k_low, k_high, v_low, v_high, part, part_got, x_own, x_got,
    middle, stage, turned, columns_out, columns_got, q_shard, o_shard,
    q_full, o_full, normed, q_ref, k_ref, v_ref, attended, lse_ref, cos, sin, send, recv, local,
):
    near = Neighbours(inner)
    copies = Copies(send, recv, local)
    tokens, width = hidden.shape
    block = width // 16
    chunks = pairs.shape[0]
    hid = down.shape[2]
    q_width = q_ref.shape[1]
    kv_slabs = k_ref.shape[1] // LANES
    slabs = q_width // LANES
    qkv_width = q_width + 2 * k_ref.shape[1]
    experts = down.shape[0]
    each = 2 + experts
    half = tokens // 2
    tiles = tokens // ROWS
    x, core = near.x, near.core
    own_half = pl.ds(pl.multiple_of(core * half, half), half)
    mine = pl.ds(pl.multiple_of(tokens + core * half, half), half)
    theirs = pl.ds(pl.multiple_of(tokens + (1 - core) * half, half), half)

    weights_in = [
        copies.copy(lambda: (gateup_hbm, gateup), "gateup", False),
        copies.copy(lambda: (down_hbm, down), "down", False),
    ]
    hidden_in = copies.copy(lambda: (hidden_hbm, hidden), "hidden", False)
    kv_width = k_ref.shape[1]
    q_shard[:, :q_width] = w_query[...].astype(BF16)
    q_shard[:, q_width : q_width + kv_width] = w_keyval[0].astype(BF16)
    q_shard[:, q_width + kv_width : qkv_width] = w_keyval[1].astype(BF16)
    o_shard[...] = w_out[...].astype(BF16)
    cos[:block, :] = jnp.zeros((block, LANES), F32)
    cos[:block, :experts] = w_router[...]
    value = jnp.concatenate([gains[...], jnp.zeros((LANES - 2, block), F32)]).T
    value = value + pltpu.roll(cos[:block, :], 2, 1)
    high = value.astype(BF16).astype(F32)
    mid = (value - high).astype(BF16).astype(F32)
    low = value - high - mid
    value = high + pltpu.roll(mid, each, 1) + pltpu.roll(low, 2 * each, 1)
    q_shard[:, qkv_width:] = value.astype(BF16)
    near.greet()
    gather_q = Gather(copies, near, q_shard, q_full, "q")
    gather_o = Gather(copies, near, o_shard, o_full, "o")
    gather_q.begin()
    gather_q.spread(0)
    copies.copy(lambda: (og_hbm, og_pair.at[pl.ds(0, tokens)]), "og")
    segment = seg_row[...].astype(F32)
    seg_col[...] = jnp.broadcast_to(segment, (8, tokens)).T[:, :1]

    def pack(c, mine):
        first = 2 * (chunks * (x if mine else 1 - x) + c)
        rows = pl.ds(pl.multiple_of(x * block, block), block)
        for e in range(CHUNK):
            for part_at in range(2):
                at = hid * (2 * e + part_at)
                value = gateup[first + e, part_at].astype(BF16)
                if mine:
                    pairs[c, rows, at : at + hid] = value
                else:
                    given[c, :, at : at + hid] = value
            at = hid * (2 * CHUNK + e)
            value = down[first + e].astype(BF16)
            if mine:
                pairs[c, rows, at : at + hid] = value
            else:
                given[c, :, at : at + hid] = value

    def swap(c):
        rows = pl.ds(pl.multiple_of(x * block, block), block)
        copies.remote(
            lambda: (given.at[c], pairs.at[c, rows]), ("s", c), ("s", c), near.over_x
        )

    def swapped(c):
        rows = pl.ds(pl.multiple_of((1 - x) * block, block), block)
        copies.arrived(pairs.at[c, rows], ("s", c), near.over_x)

    def ring_one(c):
        copies.remote(
            lambda: (pairs.at[c], near_hbm.at[c, 0]), ("up", c), ("r", c, 1), near.along[2]
        )
        copies.remote(
            lambda: (pairs.at[c], near_hbm.at[c, 1]), ("down", c), ("r", c, 2), near.along[1]
        )

    def ring_two(c):
        copies.arrived(near_hbm.at[c, 0], ("r", c, 1), near.along[1])
        copies.remote(
            lambda: (near_hbm.at[c, 0], near_hbm.at[c, 2]), ("two", c), ("r", c, 3), near.along[2]
        )

    def over_y(c, k):
        copies.remote(
            lambda: (pairs.at[c] if k == 0 else near_hbm.at[c, k - 1], far_hbm.at[c, k]),
            ("f", c, k), ("f", c, k), near.over_y,
        )

    def far_one(c):
        copies.arrived(far_hbm.at[c, 0], ("f", c, 0), near.over_y)
        copies.remote(
            lambda: (far_hbm.at[c, 0], far_hbm.at[c, 1]), ("fup", c), ("f", c, 1), near.along[2]
        )
        copies.remote(
            lambda: (far_hbm.at[c, 0], far_hbm.at[c, 2]), ("fdown", c), ("f", c, 2), near.along[1]
        )

    def far_two(c):
        copies.arrived(far_hbm.at[c, 1], ("f", c, 1), near.along[1])
        copies.remote(
            lambda: (far_hbm.at[c, 1], far_hbm.at[c, 3]), ("ftwo", c), ("f", c, 3), near.along[2]
        )

    def ring_got(c, k):
        copies.arrived(near_hbm.at[c, k - 1], ("r", c, k), near.along[k])

    def turn_tile(source, target, name, side):
        copies.copy(lambda: (source, stage.at[side]), (name, "in"), False)()
        turned[side] = stage[side].T
        return copies.copy(lambda: (turned.at[side], target), (name, "out"), False)

    waits = [None, None]

    def turn_next(source, target, name, side):
        if waits[side] is not None:
            waits[side]()
        waits[side] = turn_tile(source, target, name, side)

    for wait in weights_in:
        wait()
    pack(0, False)
    swap(0)
    pack(0, True)
    gather_q.spread(1)
    gather_q.spread(2)
    pack(1, False)
    pack(1, True)
    gather_q.cross(0)
    gather_q.spread(3)
    half_width = HEAD_DIM // 2
    lane = lax.broadcasted_iota(jnp.int32, (ROWS, LANES), 1)
    for at in range(0, tokens, ROWS):
        rows = slice(at, at + ROWS)
        earlier = jnp.where(segment < seg_col[rows, :], 1.0, 0.0)
        position = (at + lax.broadcasted_iota(jnp.int32, (ROWS, 1), 0)).astype(F32)
        position = position - jnp.sum(earlier, axis=1, keepdims=True)
        angle = position * frequency[...]
        cos[rows, :] = jnp.cos(angle)
        wave = jnp.sin(angle)
        sin[rows, :] = jnp.where(lane % HEAD_DIM < half_width, -wave, wave)
    gather_q.cross(1)
    gather_q.cross(2)
    gather_q.cross(3)
    gather_o.begin()
    gather_o.spread(0)
    swap(1)
    pack(2, False)
    pack(2, True)
    pack(3, False)
    pack(3, True)
    fill_bias(bias, seg_col, segment)
    for tile in range(tiles):
        rows = pl.ds(tile * ROWS, ROWS)
        turn_next(og_hbm.at[rows], ogt_hbm.at[:, rows], ("og", tile), tile % 2)
    hidden_in()
    gather_q.end()
    pieces = q_full[:, :, qkv_width:].reshape(width, LANES)
    wide = pieces.astype(F32)
    summed = wide + roll_left(wide, each) + roll_left(wide, 2 * each)
    small[...] = summed.T[: small.shape[0], :]
    copies.copy(lambda: (q_full, q_full_out), "q full")
    copies.copy(lambda: (cos, cos_out), "cos")
    copies.copy(lambda: (sin, sin_out), "sin")
    swapped(0)
    ring_one(0)
    over_y(0, 0)
    swap(2)
    swap(3)

    def project(tile, carry):
        rows = pl.ds(pl.multiple_of(tile * ROWS, ROWS), ROWS)
        for here in few_rows(ROWS):
            value = hidden[pl.ds(pl.multiple_of(tile * ROWS + here.start, 16), 16), :].astype(F32)
            inverse = lax.rsqrt(jnp.mean(value * value, axis=1, keepdims=True) + NORM_EPSILON)
            stage[0, here, :] = (value * inverse * small[0:1, :]).astype(BF16)
        low = stage[0]
        normed[:, rows] = low.T
        cosine, sine = cos[rows, :], sin[rows, :]
        for g in range(slabs + 2 * kv_slabs):
            lanes = slice(g * LANES, (g + 1) * LANES)
            if g % 2 == 0:
                two = slice(g * LANES, (g + 2) * LANES)
                lin_two = dot(low, q_full[:, :, two].reshape(width, 2 * LANES))
            lin = lin_two[:, (g % 2) * LANES : (g % 2 + 1) * LANES]
            if g < slabs + kv_slabs:
                lin = lin * cosine + rotate_halves(lin) * sine
            if g < slabs:
                q_ref[rows, lanes] = lin.astype(BF16)
            elif g < slabs + kv_slabs:
                at = (g - slabs) * LANES
                k_ref[rows, at : at + LANES] = lin.astype(BF16)
            else:
                at = (g - slabs - kv_slabs) * LANES
                v_ref[rows, at : at + LANES] = lin.astype(BF16)

        @pl.when(tile == 1)
        def _():
            gather_o.spread(1)

        @pl.when(tile == 2)
        def _():
            gather_o.spread(2)
            gather_o.cross(0)
            swapped(1)
            ring_one(1)
            over_y(1, 0)

        return carry

    lax.fori_loop(0, tiles, project, 0)
    copies.copy(lambda: (normed, normed_out), "normed")
    copies.copy(lambda: (q_ref, q_out), "q")
    copies.copy(lambda: (k_ref, k_out), "k")
    copies.copy(lambda: (v_ref, v_out), "v")
    for j in range(kv_slabs):
        lanes = slice(j * LANES, (j + 1) * LANES)
        spread_heads(k_ref[:, lanes], k_low, k_high, 2 * j)
        spread_heads(v_ref[:, lanes], v_low, v_high, 2 * j)

    def attend(g, carry):
        lanes = pl.ds(pl.multiple_of(g * LANES, LANES), LANES)
        kv_even, kv_odd = (2 * g) // 3, (2 * g + 1) // 3
        for at in range(0, tokens, ROWS):
            rows = slice(at, at + ROWS)
            upto = at + ROWS
            queries = q_ref[rows, lanes]
            total = None
            stats = []
            for keys, values, kv_at in ((k_low, v_low, kv_even), (k_high, v_high, kv_odd)):
                scores = dot(queries, keys[kv_at, :upto, :], NT) * SCORE_SCALE + bias[rows, :upto]
                highest = jnp.max(scores, axis=1, keepdims=True)
                weights = jnp.exp(scores - highest)
                whole = jnp.sum(weights, axis=1, keepdims=True)
                probability = (weights * (1.0 / whole)).astype(BF16)
                one = dot(probability, values[kv_at, :upto, :])
                total = one if total is None else total + one
                stats.append(highest + jnp.log(whole))
            attended[rows, lanes] = total.astype(BF16)
            across = jnp.where(half_mask(ROWS, False), stats[0], stats[1]).T
            lse_ref[g, 0:1, rows] = across[0:1, :]
            lse_ref[g, 1:2, rows] = across[HEAD_DIM : HEAD_DIM + 1, :]

        @pl.when(g == 0)
        def _():
            gather_o.spread(3)
            gather_o.cross(1)
            gather_o.cross(2)

        @pl.when(g == 1)
        def _():
            ring_got(0, 2)
            over_y(0, 2)
            copies.remote(
                lambda: (og_hbm.at[own_half], og_pair.at[mine]), ("og",), ("og",), near.over_x
            )

        @pl.when(g == 2)
        def _():
            gather_o.cross(3)
            ring_two(0)
            over_y(0, 1)

        @pl.when(g == 4)
        def _():
            gather_o.end()
            swapped(2)
            ring_one(2)
            over_y(2, 0)
            ring_got(0, 3)
            over_y(0, 3)

        return carry

    lax.fori_loop(0, slabs, attend, 0)
    copies.copy(lambda: (o_full, o_full_out), "o full")
    copies.copy(lambda: (attended, attended_out), "attended")
    copies.copy(lambda: (lse_ref, lse_out), "lse")

    def project_out(step, carry):
        tile = (step + 2 * (1 - core)) % tiles
        rows = pl.ds(pl.multiple_of(tile * ROWS, ROWS), ROWS)
        low = attended[rows, :]
        for group in range(SLOTS):
            cols = slice(4 * block * group, 4 * block * (group + 1))
            weight = o_full[4 * group : 4 * (group + 1)].reshape(4 * block, q_width)
            part[rows, cols] = dot(low, weight, NT).astype(BF16)
        return carry

    for step in range(tiles):
        project_out(step, 0)
        tile = (step + 2 * (1 - core)) % tiles
        rows = pl.ds(pl.multiple_of(tile * ROWS, ROWS), ROWS)
        copies.remote(
            lambda rows=rows: (part.at[rows], part_got.at[rows]),
            ("p", step), ("p", step), near.twin,
        )
    router = q_full[:, :, qkv_width:].reshape(width, LANES)
    for step in range(tiles):
        tile = (step + 2 * core) % tiles
        rows = pl.ds(pl.multiple_of(tile * ROWS, ROWS), ROWS)
        copies.arrived(part_got.at[rows], ("p", step), near.twin)
        side = step % 2
        if step >= 2:
            middle_out[side]()
        elif step == 0:
            middle_out = [None, None]
        for here in few_rows(ROWS):
            at = pl.ds(pl.multiple_of(tile * ROWS + here.start, 16), 16)
            total = hidden[at, :].astype(F32) + RESIDUAL_SCALE * (
                part[at, :].astype(F32) + part_got[at, :].astype(F32)
            )
            middle[side, here, :] = total
            inverse = lax.rsqrt(jnp.mean(total * total, axis=1, keepdims=True) + NORM_EPSILON)
            value = total * inverse * small[1:2, :]
            high = value.astype(BF16)
            x_own[at, :] = high
            rest = value - high.astype(F32)
            mid = rest.astype(BF16)
            stage[0, here, :] = mid
            stage[1, here, :] = (rest - mid.astype(F32)).astype(BF16)
        middle_out[side] = copies.copy(
            lambda rows=rows, side=side: (middle.at[side], middle_hbm.at[rows]), ("m", step), False
        )
        copies.copy(lambda rows=rows: (x_own.at[rows], x_hbm.at[rows]), ("x", step))
        if step < 2:
            copies.remote(
                lambda rows=rows: (x_own.at[rows], x_got.at[rows]),
                ("x", step), ("x", step), near.over_x,
            )
        one, two, three = dot(x_own[rows, :], router), dot(stage[0], router), dot(stage[1], router)
        logits = one + roll_left(one, each) + roll_left(one, 2 * each) + two + roll_left(two, each)
        logits = roll_left(logits + three, 2)
        lane = lax.broadcasted_iota(jnp.int32, (ROWS, LANES), 1)
        chosen = lane < 0
        route = routes[:, rows].astype(F32).T
        for k in range(routes.shape[0]):
            chosen = chosen | (route[:, k : k + 1] == lane.astype(F32))
        logits = jnp.where(chosen, logits, MASK_VALUE)
        powers = jnp.exp(logits - jnp.max(logits, axis=1, keepdims=True))
        powers = jnp.where(chosen, powers, 0.0)
        combine[rows, :] = powers * (1.0 / jnp.sum(powers, axis=1, keepdims=True))
        if step == 0:
            swapped(3)
            copies.copy(lambda: (pairs, pairs_hbm), "pairs")
        if step == 1:
            far_one(1)
            far_two(1)
        if step == 2:
            ring_two(2)

    shares = experts // 2
    flipped = combine[...].T
    kept = jnp.where(x == 0, flipped[:shares, :], flipped[shares : 2 * shares, :])
    gone = jnp.where(x == 0, flipped[shares : 2 * shares, :], flipped[:shares, :])
    columns_out[...] = gone
    copies.remote(lambda: (columns_out, columns_got), ("c",), ("c",), near.over_x)
    combine_pair[:tokens, :] = kept.T

    copies.arrived(og_pair.at[mine], ("og",), near.over_x)
    copies.remote(lambda: (og_pair.at[mine],) * 2, ("og2",), ("og2",), near.twin)
    for tile in range(tiles):
        rows = pl.ds(tile * ROWS, ROWS)
        if waits[tile % 2] is not None:
            waits[tile % 2]()
        turned[tile % 2] = x_own[rows, :].T
        waits[tile % 2] = copies.copy(
            lambda rows=rows, side=tile % 2: (turned.at[side], xt_hbm.at[:, rows]),
            ("xt", tile), False,
        )
    copies.arrived(columns_got, ("c",), near.over_x)
    combine_pair[tokens:, :] = columns_got[...].T
    copies.arrived(og_pair.at[theirs], ("og2",), near.twin)
    order = [(step + 2 * core) % tiles for step in range(2)]
    order += [(step + 2 * (1 - core)) % tiles for step in range(2)]

    def og_rows(step):
        return pl.ds(pl.multiple_of(tokens + order[step] * ROWS, ROWS), ROWS)

    def og_load(step):
        return copies.copy(
            lambda: (og_pair.at[og_rows(step)], stage.at[step % 2]), ("ogin", step), False
        )

    loaded = og_load(0)
    for step in range(tiles):
        loaded()
        if step + 1 < tiles:
            loaded = og_load(step + 1)
        side = step % 2
        waits[side]()
        turned[side] = stage[side].T
        waits[side] = copies.copy(
            lambda step=step, side=side: (turned.at[side], ogt_hbm.at[:, og_rows(step)]),
            ("ogt", step), False,
        )
    for step in range(tiles):
        rows = pl.ds(pl.multiple_of(order[step] * ROWS, ROWS), ROWS)
        there = pl.ds(pl.multiple_of(tokens + order[step] * ROWS, ROWS), ROWS)
        if step < 2:
            copies.arrived(x_got.at[rows], ("x", step), near.over_x)
            copies.remote(
                lambda rows=rows: (x_got.at[rows],) * 2, ("x2", step), ("x2", step), near.twin
            )
        else:
            copies.arrived(x_got.at[rows], ("x2", step - 2), near.twin)
        copies.copy(
            lambda rows=rows, there=there: (x_got.at[rows], x_hbm.at[there]), ("xg", step)
        )
        side = step % 2
        waits[side]()
        turned[side] = x_got[rows, :].T
        waits[side] = copies.copy(
            lambda there=there, side=side: (turned.at[side], xt_hbm.at[:, there]),
            ("xgt", step), False,
        )
    ring_two(1)
    for wait in waits + middle_out:
        wait()
    ring_got(1, 2)
    ring_got(1, 3)
    ring_got(2, 2)
    ring_got(2, 3)
    for k in range(SLOTS):
        copies.arrived(far_hbm.at[0, k], ("f", 0, k), near.over_y)
    for k in (2, 3):
        copies.arrived(far_hbm.at[1, k], ("f", 1, k), near.along[k])
    copies.arrived(far_hbm.at[2, 0], ("f", 2, 0), near.over_y)
    copies.finish()


def forward_pass(weights, frequency, segments, routes, gateup, down, hidden, og):
    tokens, width = hidden.shape
    experts, hid = down.shape[0], down.shape[2]
    block, q_width = weights[0].shape
    kv_width = weights[1].shape[2]
    q_columns = q_width + 2 * kv_width + LANES
    slabs, kv_heads = q_width // LANES, kv_width // HEAD_DIM
    chunks = experts // (2 * CHUNK)
    columns = 3 * CHUNK * hid
    anywhere, vmem = pl.BlockSpec(memory_space=pl.ANY), vmem_spec()
    shape = jax.ShapeDtypeStruct
    inner = lax.axis_size("dp") // 16
    dma = pltpu.SemaphoreType.DMA
    kept = [
        shape((16, block, q_columns), BF16),
        shape((16, block, q_width), BF16),
        shape((width, tokens), BF16),
        shape((tokens, q_width), BF16),
        shape((tokens, kv_width), BF16),
        shape((tokens, kv_width), BF16),
        shape((tokens, q_width), BF16),
        shape((slabs, 8, tokens), F32),
        shape((tokens, LANES), F32),
        shape((tokens, LANES), F32),
    ]
    return pl.pallas_call(
        functools.partial(forward_kernel, inner),
        in_specs=[vmem] * 8 + [anywhere] * 4,
        out_specs=[vmem] * 4 + [anywhere] * 18,
        out_shape=[
            shape((24, width), F32),
            shape((tokens, LANES), F32),
            shape((2 * tokens, experts // 2), F32),
            shape((tokens, 1), F32),
            *kept,
            shape((tokens, width), F32),
            shape((2 * tokens, width), BF16),
            shape((width, 2 * tokens), BF16),
            shape((2 * tokens, width), BF16),
            shape((width, 2 * tokens), BF16),
            shape((chunks, 2 * block, columns), BF16),
            shape((chunks - 1, SLOTS - 1, 2 * block, columns), BF16),
            shape((LATE + 1, SLOTS, 2 * block, columns), BF16),
        ],
        scratch_shapes=[
            pltpu.VMEM((tokens, width), BF16),
            pltpu.VMEM(gateup.shape, gateup.dtype),
            pltpu.VMEM(down.shape, down.dtype),
            pltpu.VMEM((chunks, block, columns), BF16),
            pltpu.VMEM((chunks, 2 * block, columns), BF16),
            pltpu.VMEM((tokens, tokens), F32),
        ]
        + [pltpu.VMEM((kv_heads, tokens, LANES), BF16)] * 4
        + [pltpu.VMEM((tokens, width), BF16)] * 4
        + [
            pltpu.VMEM((2, ROWS, width), F32),
            pltpu.VMEM((2, ROWS, width), BF16),
            pltpu.VMEM((2, width, ROWS), BF16),
            pltpu.VMEM((experts // 2, tokens), F32),
            pltpu.VMEM((experts // 2, tokens), F32),
            pltpu.VMEM((block, q_columns), BF16),
            pltpu.VMEM((block, q_width), BF16),
            *[pltpu.VMEM(one.shape, one.dtype) for one in kept],
            dma((80,)), dma((80,)), dma((64,)),
        ],
        compiler_params=pltpu.CompilerParams(
            vmem_limit_bytes=EXPERT_VMEM, collective_id=1, has_side_effects=True
        ),
        name="forward_pass",
    )(*weights, frequency, segments[None, :], routes.T, gateup, down, hidden, og)


class Scatter:
    def __init__(self, copies, near, grad, one, two, got_y, got_x, got_z, share, tag):
        self.copies, self.near, self.grad, self.share, self.tag = copies, near, grad, share, tag
        self.one, self.two, self.got_y, self.got_x, self.got_z = one, two, got_y, got_x, got_z
        self.split = one.shape[2]

    def begin(self, k):
        near = self.near
        self.copies.remote(
            lambda: (self.grad.at[near.block(k, 1, 1), :, : self.split], self.one.at[k]),
            (self.tag, "one", k), (self.tag, "one", k), near.over_x,
        )
        self.copies.remote(
            lambda: (self.grad.at[near.block(k, 1, 1), :, self.split :], self.two.at[k]),
            (self.tag, "two", k), (self.tag, "two", k), near.over_y,
        )

    def cross(self, k):
        near, grad, split = self.near, self.grad, self.split
        self.copies.arrived(self.one.at[k], (self.tag, "one", k), near.over_x)
        at = near.block(k, 1, 0)
        for here in few_rows(grad.shape[1]):
            grad[at, here, :split] = (
                grad[at, here, :split].astype(F32) + self.one[k, here, :].astype(F32)
            ).astype(BF16)
        self.copies.remote(
            lambda: (grad.at[near.block(k, 1, 0)], self.got_y.at[k]),
            (self.tag, "y", k), (self.tag, "y", k), near.over_y,
        )
        self.copies.arrived(self.two.at[k], (self.tag, "two", k), near.over_y)
        at = near.block(k, 0, 1)
        for here in few_rows(grad.shape[1]):
            grad[at, here, split:] = (
                grad[at, here, split:].astype(F32) + self.two[k, here, :].astype(F32)
            ).astype(BF16)
        self.copies.remote(
            lambda: (grad.at[near.block(k, 0, 1)], self.got_x.at[k]),
            (self.tag, "x", k), (self.tag, "x", k), near.over_x,
        )

    def plane(self, k):
        near, grad = self.near, self.grad
        self.copies.arrived(self.got_y.at[k], (self.tag, "y", k), near.over_y)
        self.copies.arrived(self.got_x.at[k], (self.tag, "x", k), near.over_x)
        at = near.block(k, 0, 0)
        for here in few_rows(grad.shape[1]):
            total = grad[at, here, :].astype(F32) + self.got_y[k, here, :].astype(F32)
            total = total + self.got_x[k, here, :].astype(F32)
            if k == 0:
                self.share[here, :] = total
            else:
                grad[at, here, :] = total.astype(BF16)
        if k == 0:
            return
        self.copies.remote(
            lambda: (grad.at[near.block(k, 0, 0)], self.got_z.at[BACK[k] - 1]),
            (self.tag, "z", k), (self.tag, "z", BACK[k]), near.along[k],
        )

    def end(self):
        for k in range(1, SLOTS):
            self.copies.arrived(self.got_z.at[k - 1], (self.tag, "z", k), self.near.along[k])
            for here in few_rows(self.share.shape[0]):
                self.share[here, :] = self.share[here, :] + self.got_z[k - 1, here, :].astype(F32)


STRIP = 128


def backward_kernel(
    inner,
    seg_col, seg_row, small, combine, gate_turned,
    o_full_hbm, attended_hbm, q_ref_hbm, k_ref_hbm, v_ref_hbm, lse_hbm, cos_hbm, sin_hbm, q_hbm, normed_hbm, hidden_hbm, og_hbm, middle_hbm, dx_own, dx_twin, dx_other,
    mix_pair, *refs,
):
    keeps, refs = refs[:SENT], refs[SENT:]
    parts, refs = refs[:SENT], refs[SENT:]
    near_two, near_three, late_got, far_first, far_three = refs[:5]
    q_share, o_share, input_grad, block_out, kept_out, given_got, mid_grad = refs[5:12]
    far_got, first_got, z_two, z_three, mix_twin, mix_other = refs[12:18]
    (
        attended_grad, lin_grad, o_grad, q_grad, o_one, o_two, o_y, o_x, o_z,
        q_one, q_two, q_y, q_x, q_z, part_got, pieces, z_send, z_keep, given, kept,
        strips, wide_in, wide_out, strip_out, router_rows, gate_columns, small_sum,
        o_full, attended, q_ref, k_ref, v_ref, lse_ref, cos, sin,
        send, recv, local, strip_sem, wide_sem, out_sem,
    ) = refs[18:]
    near = Neighbours(inner)
    copies = Copies(send, recv, local)
    tokens, width = hidden_hbm.shape
    block = width // 16
    x, core = near.x, near.core
    half = tokens // 2
    q_width = q_ref.shape[1]
    kv_width = k_ref.shape[1]
    kv_slabs, slabs = kv_width // LANES, q_width // LANES
    qkv_width = q_width + 2 * kv_width
    experts = gate_turned.shape[0]
    each = 2 + experts
    strip_count = tokens // STRIP
    ours = pl.ds(0, tokens)
    half_mine = pl.ds(pl.multiple_of(tokens + core * half, half), half)
    there = pl.ds(pl.multiple_of(core * half, half), half)
    not_there = pl.ds(pl.multiple_of((1 - core) * half, half), half)
    scatter_o = Scatter(copies, near, o_grad, o_one, o_two, o_y, o_x, o_z, o_share, "o")
    scatter_q = Scatter(copies, near, q_grad, q_one, q_two, q_y, q_x, q_z, q_share, "q")
    z_gots = [*parts, z_two, z_three]

    def y_ends(c, k):
        if c == SENT:
            return near_two.at[k], first_got if k == 0 else late_got.at[k - 1]
        return near_three.at[k], far_got.at[k]

    def y_load(c, k, i, which):
        if 0 in which:
            copies.copy(lambda: (y_ends(c, k)[0], pieces.at[2 * i]), ("own", c, k), False)
        if 1 in which:
            copies.copy(lambda: (y_ends(c, k)[1], pieces.at[2 * i + 1]), ("got", c, k), False)

    def y_sum(c, k, i):
        copies.wait_copy(lambda: (y_ends(c, k)[0], pieces.at[2 * i]), ("own", c, k))
        copies.wait_copy(lambda: (y_ends(c, k)[1], pieces.at[2 * i + 1]), ("got", c, k))
        if k > 0 and c > SENT:
            copies.sent(
                lambda: (z_send.at[k - 1], z_two.at[BACK[k] - 1]), (SENT, "z", k), near.along[k]
            )
        target = z_keep.at[c - SENT] if k == 0 else z_send.at[k - 1]
        for here in few_rows(target.shape[0]):
            target[here, :] = (
                pieces[2 * i, here, :].astype(F32) + pieces[2 * i + 1, here, :].astype(F32)
            ).astype(BF16)
        if k == 0:
            return
        copies.remote(
            lambda: (z_send.at[k - 1], z_gots[c].at[BACK[k] - 1]),
            (c, "z", k), (c, "z", BACK[k]), near.along[k], last=c > SENT,
        )

    def far_arrived(k):
        copies.arrived(far_got.at[k], ("far", k), near.over_y)

    def chunk_ends(c, k):
        return keeps[c] if k == 0 else z_gots[c].at[k - 1], pieces.at[k]

    def load_chunk(c):
        for k in range(1 if c >= SENT else 0, SLOTS):
            if c >= SENT:
                copies.arrived(z_gots[c].at[k - 1], (c, "z", k), near.along[k])
            copies.copy(lambda k=k: chunk_ends(c, k), (c, "sum", k), False)

    def sum_chunk(c):
        for k in range(1 if c >= SENT else 0, SLOTS):
            copies.wait_copy(lambda: chunk_ends(c, k), (c, "sum", k))
        if c >= 2:
            copies.wait_copy(lambda: (kept.at[c % 2], kept_out.at[c - 2]), ("kept", c - 2))
        for base, mine in ((x * block, True), ((1 - x) * block, False)):
            for here, rows in zip(few_rows(block), few_rows(block, base)):
                total = (pieces[0, rows, :] if c < SENT else z_keep[c - SENT, rows, :]).astype(F32)
                for k in range(1, SLOTS):
                    total = total + pieces[k, rows, :].astype(F32)
                if mine:
                    kept[c % 2, here, :] = total
                else:
                    given[c, here, :] = total.astype(BF16)
        copies.copy(lambda: (kept.at[c % 2], kept_out.at[c]), ("kept", c), c >= 2)
        copies.remote(
            lambda: (given.at[c], given_got.at[c]), ("given", c), ("given", c), near.over_x
        )

    def strip_rows(t):
        return pl.ds(pl.multiple_of(t * STRIP, STRIP), STRIP)

    def strip_loads(t, sources, wide):
        side = t % 2
        rows = strip_rows(t)
        loads = [
            pltpu.make_async_copy(source.at[rows], strips.at[i, side], strip_sem.at[i, side])
            for i, source in enumerate(sources)
        ]
        if wide is not None:
            loads.append(
                pltpu.make_async_copy(wide.at[rows], wide_in.at[side], wide_sem.at[side])
            )
        return loads

    def strip_store(t, source, target):
        side = t % 2
        return pltpu.make_async_copy(
            source.at[side], target.at[strip_rows(t)], out_sem.at[side]
        )

    def over_strips(sources, wide, source, target, compute):
        for load in strip_loads(0, sources, wide):
            load.start()

        def one(t, carry):
            side = t % 2

            @pl.when(t + 1 < strip_count)
            def _():
                for load in strip_loads(t + 1, sources, wide):
                    load.start()

            for load in strip_loads(t, sources, wide):
                load.wait()

            @pl.when(t >= 2)
            def _():
                strip_store(t - 2, source, target).wait()

            compute(t, side)
            strip_store(t, source, target).start()
            return carry

        lax.fori_loop(0, strip_count, one, 0)
        for t in (strip_count - 2, strip_count - 1):
            strip_store(t, source, target).wait()

    for i, k in enumerate((1, 2)):
        y_load(SENT, k, i, (0, 1))
    weights_in = copies.copy(lambda: (o_full_hbm, o_full), "o full", False)
    attended_in = copies.copy(lambda: (attended_hbm, attended), "attended", False)
    operands_in = [
        copies.copy(lambda one=one, to=to: (one, to), ("operand", i), False)
        for i, (one, to) in enumerate(
            (
                (q_ref_hbm, q_ref), (k_ref_hbm, k_ref), (v_ref_hbm, v_ref), (lse_hbm, lse_ref),
                (cos_hbm, cos), (sin_hbm, sin),
            )
        )
    ]
    near.greet()
    for k in (1, 2, 3, 0):
        copies.remote(
            lambda k=k: (far_three.at[k], far_got.at[k]), ("far", k), ("far", k), near.over_y
        )
    copies.remote(lambda: (far_first, first_got), ("first",), ("first",), near.over_y)
    copies.remote(
        lambda: (mix_pair.at[half_mine], mix_other.at[there]), ("mo",), ("mo",), near.over_x
    )
    copies.remote(lambda: (mix_pair.at[ours], mix_twin), ("mt",), ("mt",), near.twin)
    y_sum(SENT, 1, 0)
    y_load(SENT, 3, 0, (0, 1))
    y_sum(SENT, 2, 1)
    y_sum(SENT, 3, 0)
    load_chunk(0)

    router = small[2 : 2 + experts, :]
    high = router.astype(BF16).astype(F32)
    mid = (router - high).astype(BF16).astype(F32)
    low = router - high - mid
    router_rows[...] = jnp.concatenate(
        [high, mid, low, high, mid, high, jnp.zeros((LANES - 6 * experts, width), F32)]
    ).astype(BF16)
    gate_columns[...] = jnp.concatenate(
        [gate_turned[...], jnp.zeros((LANES - experts, tokens), F32)]
    ).T
    small_sum[...] = jnp.zeros_like(small_sum)

    def middle_part(turned_back):
        def compute(t, side):
            rows = strip_rows(t)
            gates, grads = combine[rows, :], gate_columns[rows, :]
            logit = gates * (grads - jnp.sum(gates * grads, axis=1, keepdims=True))
            one = logit.astype(BF16).astype(F32)
            two = (logit - one).astype(BF16).astype(F32)
            three = (logit - one - two).astype(BF16).astype(F32)

            def moved(piece, by):
                return pltpu.roll(piece, by * experts, 1)

            row = one + moved(one, 1) + moved(one, 2) + moved(two, 3) + moved(two, 4)
            row = (row + moved(three, 5)).astype(BF16)
            wide_out[side] = dot(row, router_rows[...])
            gain = small[1:2, :]
            gain_part = None
            back, n_one, n_two, n_three = (
                strip_out.at[0], strip_out.at[1], z_keep.at[0], z_keep.at[1]
            )
            for here in few_rows(STRIP):
                upstream = strips[0, side, here, :].astype(F32) + strips[1, side, here, :].astype(F32)
                upstream = upstream + strips[2, side, here, :].astype(F32)
                upstream = upstream + wide_out[side, here, :]
                middle = wide_in[side, here, :]
                inverse = lax.rsqrt(jnp.mean(middle * middle, axis=1, keepdims=True) + NORM_EPSILON)
                scaled = middle * inverse
                weighted = upstream * gain
                mean_term = jnp.mean(weighted * scaled, axis=1, keepdims=True)
                grad = strips[3, side, here, :].astype(F32) + inverse * (
                    weighted - scaled * mean_term
                )
                wide_out[side, here, :] = grad
                back[here, :] = (RESIDUAL_SCALE * grad).astype(BF16)
                gained = jnp.sum(upstream * scaled, axis=0, keepdims=True)
                gain_part = gained if gain_part is None else gain_part + gained
                normed = scaled * gain
                piece = normed.astype(BF16)
                n_one[here, :] = piece
                rest = normed - piece.astype(F32)
                piece = rest.astype(BF16)
                n_two[here, :] = piece
                n_three[here, :] = (rest - piece.astype(F32)).astype(BF16)
            small_sum[0:1, :] += gain_part
            strip = pl.ds(0, STRIP)
            turned_back[:, rows] = back[...].T
            attended_grad[rows, :] = dot(back[...], o_full[...].reshape(width, q_width)).astype(BF16)
            columns = (one + moved(two, 1) + moved(three, 2)).T[: 3 * experts, :].astype(BF16)
            a, b, c = (
                dot(columns, n_one[...]), dot(columns, n_two[strip, :]), dot(columns, n_three[strip, :])
            )
            e = experts
            small_sum[8 : 8 + e, :] += (
                a[:e] + a[e : 2 * e] + a[2 * e :] + b[:e] + b[e : 2 * e] + c[:e]
            )

        weights_in()
        over_strips([dx_own, dx_twin, dx_other, og_hbm], middle_hbm, wide_out, mid_grad, compute)
        attended_in()
        for group in range(SLOTS):
            rows = slice(4 * block * group, 4 * block * (group + 1))
            o_grad[4 * group : 4 * (group + 1)] = (
                dot(turned_back[rows, :], attended[...]).astype(BF16).reshape(4, block, q_width)
            )

    pl.run_scoped(middle_part, pltpu.VMEM((width, tokens), BF16))
    for k in (1, 2, 3, 0):
        scatter_o.begin(k)

    def attention_part(bias0, bias1, bias2, bias3, k_low, k_high, v_low, v_high, dk, dv, dq):
        biases = (bias0, bias1, bias2, bias3)
        for wait in operands_in:
            wait()
        for at, bias in enumerate(biases):
            upto = bias.shape[0]
            keys_at = lax.broadcasted_iota(jnp.int32, bias.shape, 0)
            rows_at = at * ROWS + lax.broadcasted_iota(jnp.int32, bias.shape, 1)
            same = seg_col[:upto, :] == seg_row[:, at * ROWS : (at + 1) * ROWS].astype(F32)
            bias[...] = jnp.where((rows_at >= keys_at) & same, 0.0, MASK_VALUE).astype(F32)
        for j in range(kv_slabs):
            lanes = slice(j * LANES, (j + 1) * LANES)
            spread_heads(k_ref[:, lanes], k_low, k_high, 2 * j)
            spread_heads(v_ref[:, lanes], v_low, v_high, 2 * j)
        dk[...] = jnp.zeros_like(dk)
        dv[...] = jnp.zeros_like(dv)

        def slab(g, carry):
            lanes = pl.ds(pl.multiple_of(g * LANES, LANES), LANES)
            kv_even, kv_odd = (2 * g) // 3, (2 * g + 1) // 3
            for at, bias in enumerate(biases):
                rows = slice(at * ROWS, (at + 1) * ROWS)
                upto = (at + 1) * ROWS
                queries, grads = q_ref[rows, lanes], attended_grad[rows, lanes]
                turned = (grads.astype(F32) * attended[rows, lanes].astype(F32)).T
                zero = jnp.zeros_like(queries)
                dq_part = None
                for upper, keys, values, kv_at in (
                    (False, k_low, v_low, kv_even), (True, k_high, v_high, kv_odd)
                ):
                    first = HEAD_DIM if upper else 0
                    delta = jnp.sum(turned[first : first + HEAD_DIM, :], axis=0, keepdims=True)
                    head = 1 if upper else 0
                    total = lse_ref[g, head : head + 1, rows]
                    keys_here = keys[kv_at, :upto, :]
                    scores = dot(keys_here, queries, NT) * SCORE_SCALE + bias[...]
                    probability = jnp.exp(scores - total)
                    prob_grad = dot(values[kv_at, :upto, :], grads, NT)
                    score_grad = (probability * (prob_grad - delta)).astype(BF16)
                    mask = half_mask(ROWS, upper)
                    dv[kv_at, :upto, :] += dot(
                        probability.astype(BF16), jnp.where(mask, grads, zero)
                    )
                    dk[kv_at, :upto, :] += dot(score_grad, jnp.where(mask, queries, zero))
                    one = dot(score_grad, keys_here, TN)
                    dq_part = one if dq_part is None else dq_part + one
                dq[rows, :] = dq_part * SCORE_SCALE
            whole = dq[...]
            lin_grad[:, lanes] = (
                whole * cos[...] - rotate_halves(whole) * sin[...]
            ).astype(BF16)

            @pl.when(g == 1)
            def _():
                for k in (1, 2, 3, 0):
                    scatter_o.cross(k)

            @pl.when(g == 2)
            def _():
                sum_chunk(0)
                y_load(SENT + 1, 1, 0, (0,))
                y_load(SENT + 1, 2, 1, (0,))

            @pl.when(g == 3)
            def _():
                far_arrived(1)
                y_load(SENT + 1, 1, 0, (1,))
                far_arrived(2)
                y_load(SENT + 1, 2, 1, (1,))
                far_arrived(3)
                y_sum(SENT + 1, 1, 0)
                y_load(SENT + 1, 3, 0, (0, 1))
                y_sum(SENT + 1, 2, 1)
                y_sum(SENT + 1, 3, 0)
                load_chunk(1)

            @pl.when(g == 4)
            def _():
                for k in (1, 2, 3, 0):
                    scatter_o.plane(k)
                sum_chunk(1)
                far_arrived(0)
                y_load(SENT + 1, 0, 0, (0, 1))
                copies.arrived(first_got, ("first",), near.over_y)
                y_load(SENT, 0, 1, (0, 1))

            return carry

        lax.fori_loop(0, slabs, slab, 0)
        low = half_mask(tokens, False)

        def joined(sums, j):
            one, two = sums[2 * j], sums[2 * j + 1]
            one = one + pltpu.roll(one, HEAD_DIM, 1)
            two = two + pltpu.roll(two, HEAD_DIM, 1)
            return jnp.where(low, one, two)

        for j in range(kv_slabs):
            at = q_width + j * LANES
            whole = joined(dk, j) * SCORE_SCALE
            lin_grad[:, at : at + LANES] = (
                whole * cos[...] - rotate_halves(whole) * sin[...]
            ).astype(BF16)
            at = at + kv_width
            lin_grad[:, at : at + LANES] = joined(dv, j).astype(BF16)

    kv_shape = (2 * kv_slabs, tokens, LANES)
    pl.run_scoped(
        attention_part,
        *[pltpu.VMEM(((at + 1) * ROWS, ROWS), F32) for at in range(tokens // ROWS)],
        *[pltpu.VMEM(kv_shape, BF16)] * 4,
        *[pltpu.VMEM(kv_shape, F32)] * 2,
        pltpu.VMEM((tokens, LANES), F32),
    )

    def last_part(normed_turned, q_full, part):
        normed_in = copies.copy(lambda: (normed_hbm, normed_turned), "normed", False)
        weights_in = copies.copy(lambda: (q_hbm, q_full), "q weights", False)
        columns = jnp.concatenate(
            [
                small_sum[0:1, :], small_sum[8 : 8 + experts, :],
                jnp.zeros((LANES - 1 - experts, width), F32),
            ]
        ).T
        q_grad[:, :, qkv_width:] = columns.astype(BF16).reshape(16, block, LANES)
        normed_in()
        for k in (1, 2, 3, 0):
            spot = near.spots[k]
            rows = pl.ds(pl.multiple_of(spot * 4 * block, 4 * block), 4 * block)
            q_grad[pl.ds(spot * 4, 4), :, :qkv_width] = (
                dot(normed_turned[rows, :], lin_grad[...])
                .astype(BF16)
                .reshape(4, block, qkv_width)
            )
            scatter_q.begin(k)
        weights_in()

        def project(tile):
            rows = pl.ds(tile * ROWS, ROWS)
            for group in range(SLOTS):
                cols = slice(4 * block * group, 4 * block * (group + 1))
                weight = q_full[4 * group : 4 * (group + 1), :, :qkv_width]
                part[rows, cols] = dot(
                    lin_grad[rows, :], weight.reshape(4 * block, qkv_width), NT
                ).astype(BF16)
            copies.remote(
                lambda: (part.at[rows], part_got.at[rows]), ("n", tile), ("n", tile), near.twin,
                last=False,
            )

        project(0)
        project(1)
        for k in (1, 2, 3, 0):
            scatter_q.cross(k)
        y_sum(SENT + 1, 0, 0)
        y_sum(SENT, 0, 1)
        load_chunk(2)
        project(2)
        project(3)
        scatter_o.end()
        copies.arrived(mix_other.at[there], ("mo",), near.over_x)
        copies.remote(lambda: (mix_other.at[there],) * 2, ("m2",), ("m2",), near.twin)
        sum_chunk(2)
        for tile in range(tokens // ROWS):
            rows = pl.ds(tile * ROWS, ROWS)
            copies.arrived(part_got.at[rows], ("n", tile), near.twin)

        def finish_rows(t, side):
            for here in few_rows(STRIP):
                at = pl.ds(pl.multiple_of(t * STRIP + here.start, 16), 16)
                value = strips[0, side, here, :].astype(F32)
                inverse = lax.rsqrt(jnp.mean(value * value, axis=1, keepdims=True) + NORM_EPSILON)
                upstream = part[at, :].astype(F32) + part_got[at, :].astype(F32)
                scaled = value * inverse
                weighted = upstream * small[0:1, :]
                mean_term = jnp.mean(weighted * scaled, axis=1, keepdims=True)
                wide_out[side, here, :] = wide_in[side, here, :] + inverse * (
                    weighted - scaled * mean_term
                )

        over_strips([hidden_hbm], mid_grad, wide_out, input_grad, finish_rows)
        for k in (1, 2, 3, 0):
            scatter_q.plane(k)
        load_chunk(3)
        for tile in range(tokens // ROWS):
            rows = pl.ds(tile * ROWS, ROWS)
            copies.sent(lambda: (part.at[rows], part_got.at[rows]), ("n", tile), near.twin)

    pl.run_scoped(
        last_part,
        pltpu.VMEM((width, tokens), BF16), pltpu.VMEM(q_hbm.shape, BF16),
        pltpu.VMEM((tokens, width), BF16),
    )
    sum_chunk(3)
    copies.arrived(mix_twin, ("mt",), near.twin)
    copies.arrived(mix_other.at[not_there], ("m2",), near.twin)

    def mix_rows(t, side):
        for here in few_rows(STRIP):
            mix = strips[0, side, here, :].astype(F32) + strips[1, side, here, :].astype(F32)
            mix = mix + strips[2, side, here, :].astype(F32)
            strip_out[side, here, :] = (wide_in[side, here, :] + RESIDUAL_SCALE * mix).astype(BF16)

    over_strips([mix_pair, mix_twin, mix_other], middle_hbm, strip_out, block_out, mix_rows)
    scatter_q.end()
    for c in range(2 * SENT):
        copies.arrived(given_got.at[c], ("given", c), near.over_x)
    copies.finish()


def backward_pass(
    o_full, q, k, v, attended, lse, cosine, sine, seg_col, segments, small, combine, gate_turned,
    q_full, normed, hidden, og, middle, dx, mix, keep, parts, near_grads, far_grads,
):
    tokens, width = hidden.shape
    q_width, kv_width = q.shape[1], k.shape[1]
    block, q_columns = q_full.shape[1:]
    qkv_width = q_width + 2 * kv_width
    pair, columns = keep[0].shape
    chunks = 2 * SENT
    experts = gate_turned.shape[0]
    anywhere, vmem = pl.BlockSpec(memory_space=pl.ANY), vmem_spec()
    shape = jax.ShapeDtypeStruct
    dma = pltpu.SemaphoreType.DMA
    inner = lax.axis_size("dp") // 16

    def scatter_scratch(total):
        split = total // (2 * LANES) * LANES
        return [
            pltpu.VMEM((SLOTS, block, split), BF16),
            pltpu.VMEM((SLOTS, block, total - split), BF16),
            pltpu.VMEM((SLOTS, block, total), BF16),
            pltpu.VMEM((SLOTS, block, total), BF16),
            pltpu.VMEM((SLOTS - 1, block, total), BF16),
        ]

    values = (seg_col, segments[None, :], small, combine, gate_turned)
    read = (o_full, attended, q, k, v, lse, cosine, sine)
    far_values = (
        *read, q_full, normed, hidden, og, middle, *dx, mix, *keep, *parts, *near_grads, *far_grads,
    )
    return pl.pallas_call(
        functools.partial(backward_kernel, inner),
        in_specs=[vmem] * len(values) + [anywhere] * len(far_values),
        out_specs=[vmem] * 2 + [anywhere] * 11,
        out_shape=[
            shape((block, q_columns), F32),
            shape((block, q_width), F32),
            shape((tokens, width), F32),
            shape((tokens, width), BF16),
            shape((chunks, block, columns), F32),
            shape((chunks, block, columns), BF16),
            shape((tokens, width), F32),
            shape((SLOTS, pair, columns), BF16),
            shape((pair, columns), BF16),
            shape((SLOTS - 1, pair, columns), BF16),
            shape((SLOTS - 1, pair, columns), BF16),
            shape((tokens, width), BF16),
            shape((tokens, width), BF16),
        ],
        scratch_shapes=[
            pltpu.VMEM((tokens, q_width), BF16),
            pltpu.VMEM((tokens, qkv_width), BF16),
            pltpu.VMEM((16, block, q_width), BF16),
            pltpu.VMEM((16, block, q_columns), BF16),
        ]
        + scatter_scratch(q_width)
        + scatter_scratch(q_columns)
        + [
            pltpu.VMEM((tokens, width), BF16),
            pltpu.VMEM((SLOTS, pair, columns), BF16),
            pltpu.VMEM((SLOTS - 1, pair, columns), BF16),
            pltpu.VMEM((2, pair, columns), BF16),
            pltpu.VMEM((chunks, block, columns), BF16),
            pltpu.VMEM((2, block, columns), F32),
            pltpu.VMEM((4, 2, STRIP, width), BF16),
            pltpu.VMEM((2, STRIP, width), F32),
            pltpu.VMEM((2, STRIP, width), F32),
            pltpu.VMEM((2, STRIP, width), BF16),
            pltpu.VMEM((LANES, width), BF16),
            pltpu.VMEM((tokens, LANES), F32),
            pltpu.VMEM((8 + experts, width), F32),
            *[pltpu.VMEM(one.shape, one.dtype) for one in read],
            dma((80,)), dma((80,)), dma((64,)), dma((4, 2)), dma((2,)), dma((2,)),
        ],
        compiler_params=pltpu.CompilerParams(
            vmem_limit_bytes=EXPERT_VMEM, collective_id=2, has_side_effects=True
        ),
        name="backward_pass",
    )(*values, *far_values)


def whole_call(kernel, values, outs, earlier=(), name=None):
    return pl.pallas_call(
        with_earlier(kernel, len(values), len(earlier)),
        in_specs=[vmem_spec()] * len(values) + any_specs(earlier),
        out_specs=[vmem_spec()] * len(outs),
        out_shape=[jax.ShapeDtypeStruct(shape, dtype) for shape, dtype in outs],
        compiler_params=pltpu.CompilerParams(vmem_limit_bytes=VMEM_BYTES),
        name=name,
    )(*values, *earlier)


def fence_kernel(*refs):
    count = len(refs) // 2
    for value, out in zip(refs[:count], refs[count:]):
        out[...] = value[...]


def fence_all(values, *earlier):
    return whole_call(fence_kernel, values, [(v.shape, v.dtype) for v in values], earlier, "fence")


def fence(value, *earlier):
    return fence_all([value], *earlier)[0]


def sum_y_kernel(near, got, *outs):
    for k, out in enumerate(outs):
        out[...] = (near[k].astype(F32) + got[k].astype(F32)).astype(BF16)


def sum_y(near, got, *earlier):
    outs = [(near.shape[1:], BF16)] * SLOTS
    return whole_call(sum_y_kernel, [near, got], outs, earlier, "sum_y")


def sum_z_kernel(x_at, *refs):
    kept, given = refs[-2:]
    half = kept.shape[1]
    for c in range(kept.shape[0]):
        parts = refs[SLOTS * c : SLOTS * (c + 1)]
        for rows, out in ((x_at[0], kept), (1 - x_at[0], given)):
            rows = pl.ds(pl.multiple_of(rows * half, half), half)
            total = parts[0][rows, :].astype(F32)
            for part in parts[1:]:
                total = total + part[rows, :].astype(F32)
            out[c] = total.astype(out.dtype)


def sum_z(x_at, chunks, *earlier):
    count = len(chunks)
    pair, columns = chunks[0][0].shape
    flat = [part for parts in chunks for part in parts]
    return pl.pallas_call(
        with_earlier(sum_z_kernel, 1 + len(flat), len(earlier)),
        in_specs=[smem_spec()] + [vmem_spec()] * len(flat) + any_specs(earlier),
        out_specs=[vmem_spec()] * 2,
        out_shape=[
            jax.ShapeDtypeStruct((count, pair // 2, columns), F32),
            jax.ShapeDtypeStruct((count, pair // 2, columns), BF16),
        ],
        compiler_params=pltpu.CompilerParams(vmem_limit_bytes=VMEM_BYTES),
        name="sum_z",
    )(x_at, *flat, *earlier)


def sum_parts_kernel(parts, out):
    total = parts[0].astype(F32)
    for c in range(1, parts.shape[0]):
        total = total + parts[c].astype(F32)
    out[...] = total.astype(BF16)


def sum_parts(parts, *earlier):
    chunks, tokens, width = parts.shape
    return pl.pallas_call(
        with_earlier(sum_parts_kernel, 1, len(earlier)),
        grid=(tokens // EXPERT_ROWS,),
        in_specs=[pl.BlockSpec((chunks, EXPERT_ROWS, width), lambda s: (0, s, 0))]
        + any_specs(earlier),
        out_specs=pl.BlockSpec((EXPERT_ROWS, width), lambda s: (s, 0)),
        out_shape=jax.ShapeDtypeStruct((tokens, width), BF16),
        compiler_params=pltpu.CompilerParams(vmem_limit_bytes=VMEM_BYTES),
        name="sum_parts",
    )(parts, *earlier)


def adam_attention_kernel(q_share, o_share, *refs):
    states, outs = refs[:9], refs[9:18]
    gain_part = refs[18]
    q_width, kv_width = states[0].shape[1], states[3].shape[2]
    rate = (MODEL_DIM // 12) ** (-0.5)
    grad = q_share[:, :q_width]
    total = jnp.sum(states[0][...].astype(BF16).astype(F32) * grad, axis=1, keepdims=True)
    results = [
        adam_update(states[0][...], grad, states[1][...], states[2][...], rate, WEIGHT_DECAY)
    ]
    for out, result in zip(outs[:3], results[0]):
        out[...] = result
    for c in range(2):
        first = q_width + c * kv_width
        grad = q_share[:, first : first + kv_width]
        value = states[3][c]
        total = total + jnp.sum(value.astype(BF16).astype(F32) * grad, axis=1, keepdims=True)
        results = adam_update(value, grad, states[4][c], states[5][c], rate, WEIGHT_DECAY)
        for out, result in zip(outs[3:6], results):
            out[c] = result
    gain_part[...] = total
    results = adam_update(
        states[6][...], o_share[...], states[7][...], states[8][...],
        max(1, QUERY_HEADS * HEAD_DIM // 96) ** (-0.5), WEIGHT_DECAY,
    )
    for out, result in zip(outs[6:], results):
        out[...] = result


def adam_attention(q_share, o_share, states):
    outs = [(one.shape, F32) for one in states] + [((q_share.shape[0], 1), F32)]
    return whole_call(adam_attention_kernel, [q_share, o_share, *states], outs, (), "adam_attention")


def adam_experts_kernel(x_at, kept, got, *refs):
    states, outs = refs[:6], refs[6:]
    own = kept.shape[1]
    hidden = states[0].shape[3]
    mine = pl.program_id(0) // (pl.num_programs(0) // 2) == x_at[0]
    grad = jnp.where(mine, kept[0], got[0].astype(F32))
    for e in range(CHUNK):
        for part in range(2):
            first = hidden * (2 * e + part)
            results = adam_update(
                states[0][e, part], grad[:, first : first + hidden],
                states[1][e, part], states[2][e, part], MODEL_DIM ** (-0.5), WEIGHT_DECAY,
            )
            for out, result in zip(outs[:3], results):
                out[e, part] = result
        first = hidden * (2 * CHUNK + e)
        results = adam_update(
            states[3][e], grad[:, first : first + hidden], states[4][e], states[5][e],
            max(1, F // 256) ** (-0.5), WEIGHT_DECAY,
        )
        for out, result in zip(outs[3:], results):
            out[e] = result


def adam_experts(x_at, kept, got, gateup, down):
    chunks, own, columns = kept.shape
    experts, hidden = down[0].shape[0], down[0].shape[2]
    share = pl.BlockSpec((1, own, columns), lambda j: (j % chunks, 0, 0))
    big = pl.BlockSpec((CHUNK, 2, own, hidden), lambda j: (j, 0, 0, 0))
    small = pl.BlockSpec((CHUNK, own, hidden), lambda j: (j, 0, 0))
    return pl.pallas_call(
        adam_experts_kernel,
        grid=(experts // CHUNK,),
        in_specs=[smem_spec(), share, share] + [big] * 3 + [small] * 3,
        out_specs=[big] * 3 + [small] * 3,
        out_shape=[jax.ShapeDtypeStruct(gateup[0].shape, F32)] * 3
        + [jax.ShapeDtypeStruct(down[0].shape, F32)] * 3,
        compiler_params=pltpu.CompilerParams(vmem_limit_bytes=VMEM_BYTES),
        name="adam_experts",
    )(x_at, kept, got, *gateup, *down)


def join_tokens_kernel(own, first, second, out, turned):
    half = own.shape[0] // 2
    for at, part in ((0, own[:half, :]), (half, own[half:, :]), (2 * half, first[...]), (3 * half, second[...])):
        out[at : at + half, :] = part
        turned[:, at : at + half] = part.T


def join_tokens(own, first, second, *earlier):
    tokens, width = own.shape
    return pl.pallas_call(
        with_earlier(join_tokens_kernel, 3, len(earlier)),
        in_specs=[vmem_spec()] * 3 + any_specs(earlier),
        out_specs=[vmem_spec()] * 2,
        out_shape=[
            jax.ShapeDtypeStruct((2 * tokens, width), own.dtype),
            jax.ShapeDtypeStruct((width, 2 * tokens), own.dtype),
        ],
        compiler_params=pltpu.CompilerParams(vmem_limit_bytes=VMEM_BYTES),
        name="join_tokens",
    )(own, first, second, *earlier)


def move(array, dz=0, dy=0, dx=0):
    total = lax.axis_size("dp")
    inner = total // 16
    pairs = []
    for at in range(16):
        z, y, x = at // 4, at // 2 % 2, at % 2
        to = ((z + dz) % 4) * 4 + (y ^ dy) * 2 + (x ^ dx)
        pairs += [(at * inner + i, to * inner + i) for i in range(inner)]
    return lax.ppermute(array, "dp", pairs)


def place():
    at = lax.axis_index("dp") // (lax.axis_size("dp") // 16)
    return at // 4, at // 2 % 2, at % 2


def inner_groups(total):
    inner = total // 16
    return [[at * inner + i for i in range(inner)] for at in range(16)]


def inner_gather(shard, axis):
    total = lax.axis_size("dp")
    if total == 16:
        return shard
    return lax.all_gather(
        shard, "dp", axis=axis, tiled=True, axis_index_groups=inner_groups(total)
    )


def inner_scatter(share, axis):
    total = lax.axis_size("dp")
    if total == 16:
        return share
    return lax.psum_scatter(
        share, "dp", scatter_dimension=axis, tiled=True, axis_index_groups=inner_groups(total)
    )


def block_rows(parts, rows):
    z, y, x = place()
    starts = []
    for dz, dy, dx in parts:
        starts.append((((z + dz + 4) % 4) * 4 + (y ^ dy) * 2 + (x ^ dx)) * rows)
    return jnp.stack(starts).astype(jnp.int32)


def gather_z(shard):
    return jnp.stack([shard] + [move(shard, dz=-dz) for dz in Z_FROM[1:]])


def gather_ring(shard):
    below, above = move(shard, dz=1), move(shard, dz=-1)
    return [shard, below, above, move(below, dz=1)]


def send_z(parts):
    return [move(parts[k].astype(BF16), dz=Z_FROM[k]) for k in range(1, SLOTS)]


def scatter_z(parts, moved=None):
    result = parts[0]
    for one in moved or send_z(parts):
        result = result + one.astype(F32)
    return result


def gather_plane(own):
    half = own.shape[-1] // 2
    along_y, along_x = move(own, dy=1), move(own, dx=1)
    both = (move(along_y[..., :half], dx=1), move(along_x[..., half:], dy=1))
    return own, along_y, along_x, *both


def scatter_plane(pieces):
    own, along_y, along_x, both_one, both_two = pieces
    half = both_one.shape[-1]
    got_one, got_two = move(both_one, dx=1), move(both_two, dy=1)
    pass_y = jnp.concatenate(
        [(along_y[..., :half].astype(F32) + got_one.astype(F32)).astype(BF16), along_y[..., half:]],
        axis=-1,
    )
    pass_x = jnp.concatenate(
        [along_x[..., :half], (along_x[..., half:].astype(F32) + got_two.astype(F32)).astype(BF16)],
        axis=-1,
    )
    got_y, got_x = move(pass_y, dy=1), move(pass_x, dx=1)
    return scatter_z(
        [
            own[k].astype(F32) + got_y[k].astype(F32) + got_x[k].astype(F32)
            for k in range(SLOTS)
        ]
    )


PLANE = [(dz, dy, dx) for dy, dx in ((0, 0), (1, 0), (0, 1), (1, 1)) for dz in Z_FROM]


def join_kernel(rows_at, *refs):
    pieces, out = refs[:-1], refs[-1]
    slots, own, width = pieces[0].shape
    half = width // 2
    for at in range(4 * slots):
        rows = pl.ds(pl.multiple_of(rows_at[at], own), own)
        group, slot = at // slots, at % slots
        if group < 3:
            out[rows, :] = pieces[group][slot]
        else:
            out[rows, :half] = pieces[3][slot]
            out[rows, half:] = pieces[4][slot]


def part_kernel(rows_at, whole, *pieces):
    slots, own, width = pieces[0].shape
    half = width // 2
    for at in range(4 * slots):
        rows = pl.ds(pl.multiple_of(rows_at[at], own), own)
        group, slot = at // slots, at % slots
        if group < 3:
            pieces[group][slot] = whole[rows, :]
        else:
            pieces[3][slot] = whole[rows, :half]
            pieces[4][slot] = whole[rows, half:]


def smem_spec():
    return pl.BlockSpec(memory_space=pltpu.SMEM)


def vmem_spec():
    return pl.BlockSpec(memory_space=pltpu.VMEM)


def join_blocks(rows_at, pieces, earlier=()):
    slots, own, width = pieces[0].shape
    return pl.pallas_call(
        with_earlier(join_kernel, 6, len(earlier)),
        in_specs=[smem_spec()] + [vmem_spec()] * 5 + any_specs(earlier),
        out_specs=vmem_spec(),
        out_shape=jax.ShapeDtypeStruct((4 * slots * own, width), BF16),
        compiler_params=pltpu.CompilerParams(vmem_limit_bytes=VMEM_BYTES),
        name="join_blocks",
    )(rows_at, *pieces, *earlier)


def part_blocks(rows_at, whole, earlier=()):
    own, width = whole.shape[0] // (4 * SLOTS), whole.shape[1]
    full = jax.ShapeDtypeStruct((SLOTS, own, width), BF16)
    half = jax.ShapeDtypeStruct((SLOTS, own, width // 2), BF16)
    return pl.pallas_call(
        with_earlier(part_kernel, 2, len(earlier)),
        in_specs=[smem_spec(), vmem_spec()] + any_specs(earlier),
        out_specs=[vmem_spec()] * 5,
        out_shape=[full] * 3 + [half] * 2,
        compiler_params=pltpu.CompilerParams(vmem_limit_bytes=VMEM_BYTES),
        name="part_blocks",
    )(rows_at, whole, *earlier)


def after(value, *earlier):
    marks = []
    for one in earlier:
        slots = one.shape[0] if one.shape[0] == SLOTS else 1
        lead, rest = (slots > 1) * 1, one.ndim - 1
        marks.append(lax.slice(one, (lead,) + (0,) * rest, (slots,) + (1,) * rest))
    return lax.optimization_barrier((value, *marks))[0]


def split_three(values):
    high = values.astype(BF16)
    rest = values - high.astype(F32)
    middle = rest.astype(BF16)
    low = (rest - middle.astype(F32)).astype(BF16)
    return [high, middle, low]


def swap_cores(part):
    return lax.ppermute(part, "tensor", [(0, 1), (1, 0)])


def pair_sum(part):
    return part.astype(F32) + swap_cores(part).astype(F32)


def norm_backward(values, inverse, gain_row, upstream):
    scaled = values * inverse
    weighted = upstream * gain_row
    mean_term = jnp.mean(weighted * scaled, axis=-1, keepdims=True)
    return (inverse * (weighted - scaled * mean_term), jnp.sum(upstream * scaled, axis=0))


def adam_update(value, gradient, mean_old, square_old, rate, decay):
    mean_new = FIRST_DECAY * mean_old + (1.0 - FIRST_DECAY) * gradient
    square_new = SECOND_DECAY * square_old + (1.0 - SECOND_DECAY) * gradient * gradient
    mean_hat = mean_new / (1.0 - FIRST_DECAY**STEP)
    square_hat = square_new / (1.0 - SECOND_DECAY**STEP)
    updated = value - rate * (mean_hat / (jnp.sqrt(square_hat) + ADAM_EPSILON) + decay * value)
    return (mean_new, square_new, updated)


def shards(
    hidden_in,
    out_grad,
    routes,
    segments,
    norm_gains,
    gains_mean,
    gains_square,
    w_query,
    query_mean,
    query_square,
    key_value_weight,
    key_value_first_moment,
    key_value_second_moment,
    w_out,
    out_mean,
    out_square,
    w_router,
    router_mean,
    router_square,
    w_gateup,
    gateup_mean,
    gateup_square,
    w_down,
    down_mean,
    down_square,
):
    tokens, width = hidden_in.shape
    own = w_query.shape[0]
    experts, hidden = w_down.shape[0], w_down.shape[1]
    q_width, kv_width = w_query.shape[1], key_value_weight.shape[2]
    qkv_width = q_width + 2 * kv_width
    each = 2 + experts
    half_experts = experts // 2
    block = width // 16
    z_at, y_at, x_at = place()
    core = lax.axis_index("tensor")
    plane_rows = block_rows(PLANE, block)
    turned_down = [one.transpose(0, 2, 1) for one in (w_down, down_mean, down_square)]
    gateup_rows, down_rows = w_gateup, turned_down[0]
    if lax.axis_size("dp") > 16:
        gateup_rows = inner_gather(w_gateup.astype(BF16), 2)
        down_rows = inner_gather(down_rows.astype(BF16), 1)
    chunks = experts // (2 * CHUNK)
    first = x_at == 0
    half_width = HEAD_DIM // 2
    frequency = ROPE_BASE ** (-2.0 * jnp.arange(half_width, dtype=F32) / HEAD_DIM)
    frequency = jnp.concatenate([frequency] * 4)[None, :]
    turned_out = [one.T for one in (w_out, out_mean, out_square)]
    weights = (
        inner_gather(w_query, 0), inner_gather(key_value_weight, 1),
        inner_gather(turned_out[0], 0), inner_gather(w_router, 0), inner_gather(norm_gains, 1),
    )
    (
        small, combine, combine_pair, seg_col,
        qkv_blocks, out_blocks, normed_low, queries, keys, values, attended, lse, cosine, sine,
        middle, x_pair, x_turned, og_pair, og_turned, pairs, near, far,
    ) = forward_pass(
        weights, frequency, segments, routes, gateup_rows, down_rows, hidden_in, out_grad
    )
    dx, mix_pair, gate_turned, keep, z_got, near_grads, far_grads = experts_pass(
        x_pair, og_pair, x_turned, og_turned, combine_pair, pairs, near, far
    )
    qkv_share, output_share, input_grad, block_out, kept_share, got_share = backward_pass(
        out_blocks, queries, keys, values, attended, lse, cosine, sine, seg_col, segments, small,
        combine, gate_turned, qkv_blocks, normed_low, hidden_in, out_grad, middle, dx, mix_pair, keep,
        z_got, near_grads, far_grads,
    )[:6]
    kept_share, got_share = inner_scatter(kept_share, 1), inner_scatter(got_share, 1)
    x_here = x_at.astype(jnp.int32)[None]
    output_share = inner_scatter(output_share, 0)
    qkv_share = inner_scatter(qkv_share, 0)
    *attention_results, gain_one_part = adam_attention(
        qkv_share, output_share,
        [
            w_query, query_mean, query_square, key_value_weight, key_value_first_moment,
            key_value_second_moment, *turned_out,
        ],
    )
    gain_one_share = pair_sum(gain_one_part.T) / norm_gains[:1]
    gains_share = jnp.concatenate([gain_one_share, qkv_share[:, qkv_width][None, :]])
    router_share = qkv_share[:, qkv_width + 1 : qkv_width + 1 + experts]

    gains_result = adam_update(norm_gains, gains_share, gains_mean, gains_square, GAIN_RATE, 0.0)
    router_result = adam_update(
        w_router, router_share, router_mean, router_square, (4 * MODEL_DIM) ** (-0.5), WEIGHT_DECAY
    )
    expert_results = adam_experts(
        x_here, kept_share, got_share,
        (w_gateup, gateup_mean, gateup_square), turned_down,
    )
    expert_results = [*expert_results[:3], *(one.transpose(0, 2, 1) for one in expert_results[3:])]
    return (
        (block_out, input_grad)
        + gains_result
        + tuple(attention_results[:6])
        + tuple(one.T for one in attention_results[6:])
        + router_result
        + tuple(expert_results)
    )


def solution(mesh):
    tokens, gains = P("dp", None), P(None, "dp")
    query, keyval, out = P("dp", "tensor"), P(None, "dp", "tensor"), P("tensor", "dp")
    router, gateup, down = P("dp", None), P(None, None, "dp", "tensor"), P(None, "tensor", "dp")
    states = tuple(
        spec for one in (gains, query, keyval, out, router, gateup, down) for spec in (one,) * 3
    )
    return jax.shard_map(
        shards,
        mesh=mesh,
        in_specs=(tokens, tokens, tokens, P("dp")) + states,
        out_specs=(tokens, tokens) + states,
        check_vma=False,
    )
```

```python
import functools

import jax
import jax.numpy as jnp
from jax import lax
from jax.experimental import pallas as pl
from jax.experimental.pallas import tpu as pltpu
from jax.sharding import PartitionSpec as P

MODEL_DIM = 1536
QUERY_HEADS = 24
HEAD_DIM = 64
F = 512
SEQUENCE_LENGTH = 1024
STEP = 10

NORM_EPSILON = 1e-06
SCORE_SCALE = 0.015625
RESIDUAL_SCALE = 0.22
ROPE_BASE = 10000.0
FIRST_DECAY = 0.9
SECOND_DECAY = 0.95
ADAM_EPSILON = 1e-08
WEIGHT_DECAY = 0.1
GAIN_RATE = 0.6
MASK_VALUE = -1e30
HIGHEST_PRECISION = lax.Precision.HIGHEST

BF16 = jnp.bfloat16
F32 = jnp.float32
LANES = 128
ROWS = 256
VMEM_BYTES = 58 * 1024 * 1024

NN = (((1,), (0,)), ((), ()))
NT = (((1,), (1,)), ((), ()))
TN = (((0,), (0,)), ((), ()))


def dot(a, b, dims=NN):
    return lax.dot_general(a, b, dims, preferred_element_type=F32)


def seq_positions(segment_row):
    counter = jnp.arange(segment_row.shape[0], dtype=jnp.int32)
    earlier = jnp.concatenate([segment_row[:1] - 1, segment_row[:-1]])
    starts = lax.cummax(jnp.where(segment_row != earlier, counter, 0), axis=0)
    return counter - starts


def rope_tables(positions):
    half_width = HEAD_DIM // 2
    frequency = ROPE_BASE ** (-2.0 * jnp.arange(half_width, dtype=F32) / HEAD_DIM)
    angles = positions.astype(F32)[:, None] * frequency[None, :]
    cosine, sine = jnp.cos(angles), jnp.sin(angles)
    return (
        jnp.concatenate([cosine] * 4, axis=1),
        jnp.concatenate([-sine, sine] * 2, axis=1),
    )


def rotate_halves(slab):
    lane = lax.broadcasted_iota(jnp.int32, slab.shape, 1)
    ahead = pltpu.roll(slab, LANES - HEAD_DIM // 2, 1)
    behind = pltpu.roll(slab, HEAD_DIM // 2, 1)
    return jnp.where(lane % HEAD_DIM < HEAD_DIM // 2, ahead, behind)


def few_rows(count, base=None):
    for r in range(0, count, 16):
        yield pl.ds(r, 16) if base is None else pl.ds(pl.multiple_of(base + r, 16), 16)


def half_mask(rows, upper):
    lane = lax.broadcasted_iota(jnp.int32, (rows, LANES), 1)
    return (lane >= HEAD_DIM) if upper else (lane < HEAD_DIM)


def spread_heads(slab, lower_out, upper_out, index):
    rows = slab.shape[0]
    moved = pltpu.roll(slab.astype(F32), HEAD_DIM, 1).astype(BF16)
    zero = jnp.zeros_like(slab)
    low, high = half_mask(rows, False), half_mask(rows, True)
    lower_out[index] = jnp.where(low, slab, zero)
    upper_out[index] = jnp.where(high, moved, zero)
    lower_out[index + 1] = jnp.where(low, moved, zero)
    upper_out[index + 1] = jnp.where(high, slab, zero)


def fill_bias(bias, seg_col, seg_row):
    span = bias.shape[0]
    for at in range(0, span, ROWS):
        rows_at = at + lax.broadcasted_iota(jnp.int32, (ROWS, span), 0)
        cols_at = lax.broadcasted_iota(jnp.int32, (ROWS, span), 1)
        allowed = (rows_at >= cols_at) & (seg_col[at : at + ROWS, :] == seg_row[...])
        bias[at : at + ROWS, :] = jnp.where(allowed, 0.0, MASK_VALUE).astype(F32)


def with_earlier(kernel, inputs, count):
    def run(*refs):
        kernel(*refs[:inputs], *refs[inputs + count :])

    return run


def any_specs(arrays):
    return [pl.BlockSpec(memory_space=pl.ANY)] * len(arrays)


def attention_forward_kernel(
    lin_ref, kv_ref, cos_ref, sin_ref, seg_col, seg_row,
    out_ref, q_ref, k_ref, v_ref, lse_ref,
    bias, k_low, k_high, v_low, v_high,
):
    slab_at = pl.program_id(0)
    span = lin_ref.shape[0]
    kv_slabs = kv_ref.shape[1] // (2 * LANES)

    @pl.when(slab_at == 0)
    def _():
        fill_bias(bias, seg_col, seg_row)
        for j in range(kv_slabs):
            lanes = slice(j * LANES, (j + 1) * LANES)
            lin = kv_ref[:, lanes]
            keys = (lin * cos_ref[...] + rotate_halves(lin) * sin_ref[...]).astype(BF16)
            k_ref[:, lanes] = keys
            spread_heads(keys, k_low, k_high, 2 * j)
            lanes = slice((kv_slabs + j) * LANES, (kv_slabs + j + 1) * LANES)
            values = kv_ref[:, lanes].astype(BF16)
            v_ref[:, slice(j * LANES, (j + 1) * LANES)] = values
            spread_heads(values, v_low, v_high, 2 * j)

    lin = lin_ref[...]
    q_ref[...] = (lin * cos_ref[...] + rotate_halves(lin) * sin_ref[...]).astype(BF16)
    kv_even, kv_odd = (2 * slab_at) // 3, (2 * slab_at + 1) // 3
    for at in range(0, span, ROWS):
        rows = slice(at, at + ROWS)
        queries = q_ref[rows, :]
        total = None
        stats = []
        for keys, values, kv_at in ((k_low, v_low, kv_even), (k_high, v_high, kv_odd)):
            upto = at + ROWS
            scores = dot(queries, keys[kv_at, :upto, :], NT) * SCORE_SCALE + bias[rows, :upto]
            highest = jnp.max(scores, axis=1, keepdims=True)
            weights = jnp.exp(scores - highest)
            summed = jnp.sum(weights, axis=1, keepdims=True)
            probability = (weights * (1.0 / summed)).astype(BF16)
            part = dot(probability, values[kv_at, :upto, :])
            total = part if total is None else total + part
            stats.append(highest + jnp.log(summed))
        out_ref[rows, :] = total.astype(BF16)
        spread = jnp.where(half_mask(ROWS, False), stats[0], stats[1])
        turned = spread.T
        lse_ref[0, 0:1, rows] = turned[0:1, :]
        lse_ref[0, 1:2, rows] = turned[HEAD_DIM : HEAD_DIM + 1, :]


def attention_forward(qkv_lin, cosine, sine, segment_row, earlier=()):
    span = qkv_lin.shape[0]
    q_width = MODEL_DIM // 2
    kv_width = (qkv_lin.shape[1] - q_width) // 2
    slabs, kv_heads = q_width // LANES, kv_width // HEAD_DIM
    whole = lambda shape: pl.BlockSpec(shape, lambda g: (0,) * len(shape))
    slab = pl.BlockSpec((span, LANES), lambda g: (0, g))
    q_lin, kv_lin = qkv_lin[:, :q_width], qkv_lin[:, q_width:]
    return pl.pallas_call(
        with_earlier(attention_forward_kernel, 6, len(earlier)),
        grid=(slabs,),
        in_specs=[
            slab, whole((span, 2 * kv_width)), whole((span, LANES)), whole((span, LANES)),
            whole((span, 1)), whole((1, span)),
        ]
        + any_specs(earlier),
        out_specs=[
            slab, slab, whole((span, kv_width)), whole((span, kv_width)),
            pl.BlockSpec((1, 8, span), lambda g: (g, 0, 0)),
        ],
        out_shape=[
            jax.ShapeDtypeStruct((span, q_width), BF16),
            jax.ShapeDtypeStruct((span, q_width), BF16),
            jax.ShapeDtypeStruct((span, kv_width), BF16),
            jax.ShapeDtypeStruct((span, kv_width), BF16),
            jax.ShapeDtypeStruct((slabs, 8, span), F32),
        ],
        scratch_shapes=[pltpu.VMEM((span, span), F32)]
        + [pltpu.VMEM((kv_heads, span, LANES), BF16)] * 4,
        compiler_params=pltpu.CompilerParams(vmem_limit_bytes=VMEM_BYTES),
        cost_estimate=pl.CostEstimate(
            flops=32 * slabs * span * span * LANES, bytes_accessed=16 * span * q_width,
            transcendentals=slabs * span * span,
        ),
        name="attention_forward",
    )(q_lin, kv_lin, cosine, sine, segment_row[:, None], segment_row[None, :], *earlier)


def attention_backward_kernel(
    q_ref, k_ref, v_ref, out_ref, grad_ref, cos_ref, sin_ref, seg_col, seg_row, lse_ref,
    dq_ref, dkv_ref,
    bias, k_low, k_high, v_low, v_high, dk_low, dk_high, dv_low, dv_high, dq_sum,
):
    slab_at = pl.program_id(0)
    span = q_ref.shape[0]
    kv_slabs = k_ref.shape[1] // LANES

    @pl.when(slab_at == 0)
    def _():
        for at in range(0, span, ROWS):
            keys_at = at + lax.broadcasted_iota(jnp.int32, (ROWS, span), 0)
            rows_at = lax.broadcasted_iota(jnp.int32, (ROWS, span), 1)
            allowed = (rows_at >= keys_at) & (seg_col[at : at + ROWS, :] == seg_row[...])
            bias[at : at + ROWS, :] = jnp.where(allowed, 0.0, MASK_VALUE).astype(F32)
        for j in range(kv_slabs):
            lanes = slice(j * LANES, (j + 1) * LANES)
            spread_heads(k_ref[:, lanes], k_low, k_high, 2 * j)
            spread_heads(v_ref[:, lanes], v_low, v_high, 2 * j)
        for sums in (dk_low, dk_high, dv_low, dv_high):
            sums[...] = jnp.zeros_like(sums)

    kv_even, kv_odd = (2 * slab_at) // 3, (2 * slab_at + 1) // 3
    for at in range(0, span, ROWS):
        rows = slice(at, at + ROWS)
        upto = at + ROWS
        queries, grads = q_ref[rows, :], grad_ref[rows, :]
        turned = (grads.astype(F32) * out_ref[rows, :].astype(F32)).T
        zero = jnp.zeros_like(queries)
        dq_part = None
        for upper, keys, values, dk_sum, dv_sum, kv_at in (
            (False, k_low, v_low, dk_low, dv_low, kv_even),
            (True, k_high, v_high, dk_high, dv_high, kv_odd),
        ):
            first = HEAD_DIM if upper else 0
            delta = jnp.sum(turned[first : first + HEAD_DIM, :], axis=0, keepdims=True)
            head = 1 if upper else 0
            total = lse_ref[0, head : head + 1, rows]
            keys_here = keys[kv_at, :upto, :]
            scores = dot(keys_here, queries, NT) * SCORE_SCALE + bias[:upto, rows]
            probability = jnp.exp(scores - total)
            prob_grad = dot(values[kv_at, :upto, :], grads, NT)
            score_grad = (probability * (prob_grad - delta)).astype(BF16)
            mask = half_mask(ROWS, upper)
            dv_sum[kv_at, :upto, :] += dot(
                probability.astype(BF16), jnp.where(mask, grads, zero)
            )
            dk_sum[kv_at, :upto, :] += dot(score_grad, jnp.where(mask, queries, zero))
            part = dot(score_grad, keys_here, TN)
            dq_part = part if dq_part is None else dq_part + part
        dq_sum[rows, :] = dq_part * SCORE_SCALE
    slab = dq_sum[...]
    dq_ref[...] = (slab * cos_ref[...] - rotate_halves(slab) * sin_ref[...]).astype(BF16)

    @pl.when(slab_at == pl.num_programs(0) - 1)
    def _():
        low = half_mask(span, False)

        def joined(sums_low, sums_high, j):
            one = sums_low[2 * j] + pltpu.roll(sums_high[2 * j], HEAD_DIM, 1)
            two = pltpu.roll(sums_low[2 * j + 1], HEAD_DIM, 1) + sums_high[2 * j + 1]
            return jnp.where(low, one, two)

        for j in range(kv_slabs):
            slab = joined(dk_low, dk_high, j) * SCORE_SCALE
            dkv_ref[:, j * LANES : (j + 1) * LANES] = (
                slab * cos_ref[...] - rotate_halves(slab) * sin_ref[...]
            ).astype(BF16)
            at = (kv_slabs + j) * LANES
            dkv_ref[:, at : at + LANES] = joined(dv_low, dv_high, j).astype(BF16)


def attention_backward(
    queries, keys, values, attended, grad, cosine, sine, segment_row, lse, earlier=()
):
    span, q_width = queries.shape
    kv_width = keys.shape[1]
    slabs, kv_heads = q_width // LANES, kv_width // HEAD_DIM
    whole = lambda shape: pl.BlockSpec(shape, lambda g: (0,) * len(shape))
    slab = pl.BlockSpec((span, LANES), lambda g: (0, g))
    return pl.pallas_call(
        with_earlier(attention_backward_kernel, 10, len(earlier)),
        grid=(slabs,),
        in_specs=[
            slab, whole((span, kv_width)), whole((span, kv_width)), slab, slab,
            whole((span, LANES)), whole((span, LANES)), whole((span, 1)), whole((1, span)),
            pl.BlockSpec((1, 8, span), lambda g: (g, 0, 0)),
        ]
        + any_specs(earlier),
        out_specs=[slab, whole((span, 2 * kv_width))],
        out_shape=[
            jax.ShapeDtypeStruct((span, q_width), BF16),
            jax.ShapeDtypeStruct((span, 2 * kv_width), BF16),
        ],
        scratch_shapes=[pltpu.VMEM((span, span), F32)]
        + [pltpu.VMEM((kv_heads, span, LANES), BF16)] * 4
        + [pltpu.VMEM((kv_heads, span, LANES), F32)] * 4
        + [pltpu.VMEM((span, LANES), F32)],
        compiler_params=pltpu.CompilerParams(vmem_limit_bytes=VMEM_BYTES),
        cost_estimate=pl.CostEstimate(
            flops=40 * slabs * span * span * LANES, bytes_accessed=16 * span * q_width,
            transcendentals=slabs * span * span,
        ),
        name="attention_backward",
    )(
        queries, keys, values, attended, grad, cosine, sine,
        segment_row[:, None], segment_row[None, :], lse, *earlier,
    )


EXPERT_ROWS = 256
EXPERT_VMEM = 63 * 1024 * 1024
SLOTS = 4
Z_FROM = (0, -1, 1, 2)
CHUNK = 2
LATE = 2
SENT = 2
MESH_ID = pl.DeviceIdType.MESH


def experts_kernel(
    inner, chunks, row_steps, x_ref, og_ref, xt_ref, ogt_ref, combine_ref,
    pairs_ref, near_ref, far_ref,
    dx_own, dx_twin, dx_other, mix_out, gate_out, *refs,
):
    keep_outs, refs = refs[:SENT], refs[SENT:]
    part_outs, refs = refs[:SENT], refs[SENT:]
    near_outs, refs = refs[: chunks - SENT], refs[chunks - SENT :]
    late_out, first_out, far_out, refs = *refs[:3], refs[3:]
    slots, arrived, held_both, held_down, dx_sum, mix_sum, twin_rows, twin_mix = refs[:8]
    gates, gate_kept, gate_got, gate_full, gate_twin, send, recv, local = refs[8:]
    weights, grads = slots.at[pl.ds(1, chunks)], slots
    near = Neighbours(inner)
    copies = Copies(send, recv, local)
    z, y, x, core, spots = near.z, near.y, near.x, near.core, near.spots
    step = pl.program_id(0)
    steps = row_steps + SLOTS
    chunk, turn = step // steps, step % steps
    last = chunks - 1
    width = x_ref.shape[1]
    block = width // 16
    hidden = held_down.shape[1] // CHUNK
    both = 2 * hidden * CHUNK
    lane = lax.broadcasted_iota(jnp.int32, (EXPERT_ROWS, LANES), 1)
    tokens = dx_sum.shape[0] // 2
    tiles = tokens // EXPERT_ROWS
    tile = (turn + tiles) % row_steps
    rows = pl.ds(pl.multiple_of(tile * EXPERT_ROWS, EXPERT_ROWS), EXPERT_ROWS)

    def near_piece(c, k):
        return pairs_ref.at[c] if k == 0 else near_ref.at[c, k - 1]

    def near_copy(c, k):
        copies.copy(
            lambda c=c, k=k: (near_piece(c, k), weights.at[c, spots[k], y]), ("near", c, k), False
        )

    def near_wait(c, k):
        copies.wait_copy(
            lambda c=c, k=k: (near_piece(c, k), weights.at[c, spots[k], y]), ("near", c, k)
        )

    def far_ends(c, k):
        return far_ref.at[c, k], weights.at[c, spots[k], 1 - y]

    @pl.when(step == 0)
    def _():
        near.greet()
        gates[...] = jnp.zeros_like(gates)
        for k in range(SLOTS):
            near_copy(0, k)
            copies.copy(lambda k=k: far_ends(0, k), ("far", 0, k), False)
        copies.remote(
            lambda: (pairs_ref.at[last], weights.at[last, z, y]), ("y",), ("y",), near.over_y
        )
        for k in range(1, SLOTS):
            copies.remote(
                lambda: (pairs_ref.at[last], weights.at[last, z, y]),
                ("z", k), ("z", BACK[k]), near.along[k],
            )
        for c in range(LATE, last):
            for k in range(1, SLOTS):
                copies.remote(
                    lambda c=c, k=k: (near_piece(c, k), weights.at[c, spots[k], y]),
                    ("f", c, k), ("f", c, k), near.over_y,
                )
        for c in range(1, chunks):
            for k in range(SLOTS if c < last else 1):
                near_copy(c, k)
                if c < LATE or (c < last and k == 0):
                    copies.copy(lambda c=c, k=k: far_ends(c, k), ("far", c, k), False)

    @pl.when(step == steps)
    def _():
        copies.arrived(weights.at[last, z, 1 - y], ("y",), near.over_y)
        for k in range(1, SLOTS):
            copies.remote(
                lambda: (weights.at[last, z, 1 - y],) * 2,
                ("z2", k), ("z2", BACK[k]), near.along[k],
            )

    for c in range(chunks):

        @pl.when(step == c * steps)
        def _():
            for k in range(SLOTS):
                if c < last or k == 0:
                    near_wait(c, k)
                if c < LATE or (c < last and k == 0):
                    copies.wait_copy(lambda c=c, k=k: far_ends(c, k), ("far", c, k))
                elif c < last:
                    copies.arrived(weights.at[c, spots[k], 1 - y], ("f", c, k), near.over_y)
                elif k > 0:
                    copies.arrived(weights.at[c, spots[k], y], ("z", k), near.along[k])
                    copies.arrived(weights.at[c, spots[k], 1 - y], ("z2", k), near.along[k])

    def add_arrived(c):
        copies.arrived(arrived.at[c], ("sum", c), near.over_y)
        for k in range(SLOTS):
            own = grads.at[c, spots[k], y]
            for here in few_rows(own.shape[0]):
                own[here, :] = (
                    own[here, :].astype(F32) + arrived[c, spots[k], here, :].astype(F32)
                ).astype(BF16)
        copies.copy(lambda c=c: (grads.at[c, z, y], keep_outs[c]), ("keep", c))
        for k in range(1, SLOTS):
            copies.remote(
                lambda c=c, k=k: (grads.at[c, spots[k], y], part_outs[c].at[BACK[k] - 1]),
                ("part", c, k), ("part", c, BACK[k]), near.along[k],
            )

    @pl.when(step == 2 * steps + 1)
    def _():
        add_arrived(0)

    @pl.when(step == 3 * steps + 2)
    def _():
        add_arrived(1)

    @pl.when(turn < row_steps)
    def _():
        for e in range(CHUNK):
            first = 2 * hidden * e
            w_both = weights[chunk, :, :, :, first : first + 2 * hidden].reshape(width, 2 * hidden)
            start = both + hidden * e
            w_down = weights[chunk, :, :, :, start : start + hidden].reshape(width, hidden)
            gate_up = dot(x_ref[...], w_both)
            raw = dot(og_ref[...], w_down) * RESIDUAL_SCALE
            gate, up = gate_up[:, :hidden], gate_up[:, hidden:]
            gate_lane = lax.broadcasted_iota(
                jnp.int32, (EXPERT_ROWS, combine_ref.shape[1]), 1
            )
            column = jnp.sum(
                jnp.where(gate_lane == chunk * CHUNK + e, combine_ref[...], 0.0),
                axis=1, keepdims=True,
            )
            sigmoid = 1.0 / (1.0 + jnp.exp(-gate))
            active = gate * sigmoid
            inner_value = (active * up).astype(BF16).astype(F32)
            held_down[rows, hidden * e : hidden * (e + 1)] = (inner_value * column).astype(BF16)
            gates[rows, :] = jnp.where(
                lane == chunk * CHUNK + e,
                jnp.sum(inner_value * raw, axis=1, keepdims=True),
                gates[rows, :],
            )
            inner_grad = raw * column
            held_both[rows, first : first + hidden] = (
                inner_grad * up * sigmoid * (1.0 + gate * (1.0 - sigmoid))
            ).astype(BF16)
            held_both[rows, first + hidden : first + 2 * hidden] = (inner_grad * active).astype(BF16)

        def sums(add):
            for part in range(SLOTS):
                cols = slice(4 * block * part, 4 * block * (part + 1))
                w_both = weights[chunk, part, :, :, :both].reshape(4 * block, both)
                w_down = weights[chunk, part, :, :, both:].reshape(4 * block, hidden * CHUNK)
                mix = dot(held_down[rows, :], w_down, NT)
                dx = dot(held_both[rows, :], w_both, NT)
                if add:
                    mix = mix + mix_sum[rows, cols].astype(F32)
                    dx = dx + dx_sum[rows, cols].astype(F32)
                mix_sum[rows, cols] = mix.astype(BF16)
                dx_sum[rows, cols] = dx.astype(BF16)

        @pl.when(chunk == 0)
        def _():
            sums(False)

        @pl.when(chunk > 0)
        def _():
            sums(True)

    @pl.when(turn >= row_steps)
    def _():
        part = turn - row_steps
        grads[chunk, part, :, :, :both] = (
            dot(xt_ref[...], held_both[...]).astype(BF16).reshape(2, 2 * block, both)
        )
        grads[chunk, part, :, :, both:] = (
            (dot(ogt_ref[...], held_down[...]) * RESIDUAL_SCALE)
            .astype(BF16)
            .reshape(2, 2 * block, hidden * CHUNK)
        )

    begin = last * steps
    for i in range(2):
        for c in range(2):
            mine = pl.ds(tokens + (2 * c + i) * EXPERT_ROWS, EXPERT_ROWS)
            there = pl.ds((2 * c + i) * EXPERT_ROWS, EXPERT_ROWS)

            @pl.when((step == begin + 2 * c + i) & (core != c))
            def _():
                for name, total, got in (("t", dx_sum, twin_rows), ("mt", mix_sum, twin_mix)):
                    copies.remote(
                        lambda: (total.at[mine], got.at[i]), (name, i), (name, i), near.twin,
                        last=False,
                    )

            @pl.when((step == begin + 2 + 2 * c + i) & (core == c))
            def _():
                for name, total, got in (("t", dx_sum, twin_rows), ("mt", mix_sum, twin_mix)):
                    copies.arrived(got.at[i], (name, i), near.twin)
                    for here in few_rows(EXPERT_ROWS):
                        at = pl.ds(mine.start + here.start, 16)
                        total[at, :] = (
                            total[at, :].astype(F32) + got[i, here, :].astype(F32)
                        ).astype(BF16)
                copies.remote(
                    lambda: (dx_sum.at[mine], dx_other.at[there]), ("o", i), ("o", i), near.over_x,
                    last=False,
                )

            @pl.when((step == begin + steps - 2 + i) & (core == c))
            def _():
                copies.arrived(dx_other.at[there], ("o", i), near.over_x)
                copies.remote(
                    lambda: (dx_other.at[there],) * 2, ("o2", i), ("o2", i), near.twin, last=False
                )

    for i in range(tiles):

        @pl.when(step == begin + tiles + i)
        def _():
            own = pl.ds(i * EXPERT_ROWS, EXPERT_ROWS)
            copies.copy(lambda own=own: (dx_sum.at[own], dx_own.at[own]), ("own", i))
            copies.remote(
                lambda own=own: (dx_sum.at[own], dx_twin.at[own]), ("own", i), ("own", i), near.twin
            )

    shares = gate_kept.shape[0]

    @pl.when(step == begin + row_steps)
    def _():
        copies.copy(lambda: (mix_sum, mix_out), "mix")
        turned = gates[...].T[:shares, :]
        gate_kept[...] = turned
        copies.remote(
            lambda: (gate_kept.at[:, pl.ds(tokens, tokens)], gate_got), ("g",), ("g",), near.over_x
        )

    @pl.when(step == begin + steps - 2)
    def _():
        copies.arrived(gate_got, ("g",), near.over_x)
        gate_full[pl.ds(pl.multiple_of(x * shares, shares), shares), :] = gate_kept[:, :tokens]
        gate_full[pl.ds(pl.multiple_of((1 - x) * shares, shares), shares), :] = gate_got[...]
        copies.remote(lambda: (gate_full, gate_twin), ("g2",), ("g2",), near.twin)

    for c in range(chunks):

        @pl.when(step == (c + 1) * steps - 1)
        def _():
            if c < SENT:
                copies.remote(
                    lambda c=c: (grads.at[c, :, 1 - y], arrived.at[c]),
                    ("sum", c), ("sum", c), near.over_y,
                )
            else:
                for k in range(SLOTS):
                    copies.copy(
                        lambda c=c, k=k: (grads.at[c, spots[k], y], near_outs[c - SENT].at[k]),
                        ("near out", c, k),
                    )
                    if c < last and k == 0:
                        copies.copy(lambda c=c: (grads.at[c, z, 1 - y], first_out), "first out")
                    elif c < last:
                        copies.remote(
                            lambda c=c, k=k: (grads.at[c, spots[k], 1 - y], late_out.at[k - 1]),
                            ("late", k), ("late", k), near.over_y,
                        )
                    else:
                        copies.copy(
                            lambda c=c, k=k: (grads.at[c, spots[k], 1 - y], far_out.at[k]),
                            ("far out", k),
                        )

    @pl.when(step == chunks * steps - 1)
    def _():
        copies.arrived(gate_twin, ("g2",), near.twin)
        gate_out[...] = gate_full[...] + gate_twin[...]
        for i in range(tiles):
            copies.arrived(
                dx_twin.at[pl.ds(i * EXPERT_ROWS, EXPERT_ROWS)], ("own", i), near.twin
            )
        for i in range(2):
            for c in range(2):
                mine = pl.ds(tokens + (2 * c + i) * EXPERT_ROWS, EXPERT_ROWS)
                there = pl.ds((2 * c + i) * EXPERT_ROWS, EXPERT_ROWS)

                @pl.when(core != c)
                def _():
                    copies.sent(lambda: (dx_sum.at[mine], twin_rows.at[i]), ("t", i), near.twin)
                    copies.sent(lambda: (mix_sum.at[mine], twin_mix.at[i]), ("mt", i), near.twin)
                    copies.arrived(dx_other.at[there], ("o2", i), near.twin)

                @pl.when(core == c)
                def _():
                    copies.sent(
                        lambda: (dx_sum.at[mine], dx_other.at[there]), ("o", i), near.over_x
                    )
                    copies.sent(lambda: (dx_other.at[there],) * 2, ("o2", i), near.twin)

        for c in range(SENT):
            for k in range(1, SLOTS):
                copies.arrived(part_outs[c].at[k - 1], ("part", c, k), near.along[k])
        for k in range(1, SLOTS):
            copies.arrived(late_out.at[k - 1], ("late", k), near.over_y)
        copies.finish()


def experts_pass(x, og, xt, ogt, combine, pairs, near, far):
    tokens, width = x.shape
    chunks, pair, columns = pairs.shape
    hidden = columns // (3 * CHUNK)
    shares = chunks * CHUNK
    row_steps = tokens // EXPERT_ROWS
    steps = row_steps + SLOTS
    inner = lax.axis_size("dp") // 16
    row_at = lambda s: ((jnp.minimum(s % steps, row_steps - 1) + row_steps // 2) % row_steps, 0)
    width_at = lambda s: (jnp.maximum(s % steps - row_steps, 0), 0)
    row = pl.BlockSpec((EXPERT_ROWS, width), row_at)
    turned = pl.BlockSpec((width // SLOTS, tokens), width_at)
    anywhere = pl.BlockSpec(memory_space=pl.ANY)
    left = chunks - SENT
    dma = pltpu.SemaphoreType.DMA
    shape = jax.ShapeDtypeStruct
    outs = pl.pallas_call(
        functools.partial(experts_kernel, inner, chunks, row_steps),
        grid=(chunks * steps,),
        in_specs=[row, row, turned, turned, pl.BlockSpec((EXPERT_ROWS, combine.shape[1]), row_at)]
        + [anywhere] * 3,
        out_specs=[anywhere] * 4
        + [pl.BlockSpec((2 * shares, tokens // 2), lambda s: (0, 0))]
        + [anywhere] * (2 * SENT + left + 3),
        out_shape=[shape((tokens // 2, width), BF16)] * 3
        + [shape((tokens, width), BF16), shape((2 * shares, tokens // 2), F32)]
        + [shape((pair, columns), BF16)] * SENT
        + [shape((SLOTS - 1, pair, columns), BF16)] * SENT
        + [shape((SLOTS, pair, columns), BF16)] * left
        + [shape((SLOTS - 1, pair, columns), BF16), shape((pair, columns), BF16)]
        + [shape((SLOTS, pair, columns), BF16)],
        scratch_shapes=[
            pltpu.VMEM((chunks + 1, SLOTS, 2, pair, columns), BF16),
            pltpu.VMEM((SENT, SLOTS, pair, columns), BF16),
            pltpu.VMEM((tokens, 2 * hidden * CHUNK), BF16),
            pltpu.VMEM((tokens, hidden * CHUNK), BF16),
            pltpu.VMEM((tokens, width), BF16),
            pltpu.VMEM((tokens, width), BF16),
            pltpu.VMEM((2, EXPERT_ROWS, width), BF16),
            pltpu.VMEM((2, EXPERT_ROWS, width), BF16),
            pltpu.VMEM((tokens, LANES), F32),
            pltpu.VMEM((shares, tokens), F32),
            pltpu.VMEM((shares, tokens // 2), F32),
            pltpu.VMEM((2 * shares, tokens // 2), F32),
            pltpu.VMEM((2 * shares, tokens // 2), F32),
            dma((48,)), dma((48,)), dma((48,)),
        ],
        compiler_params=pltpu.CompilerParams(
            vmem_limit_bytes=EXPERT_VMEM, collective_id=0, has_side_effects=True
        ),
        cost_estimate=pl.CostEstimate(
            flops=8 * tokens * width * chunks * columns,
            bytes_accessed=2 * chunks * width * columns, transcendentals=0,
        ),
        name="experts_pass",
    )(x, og, xt, ogt, combine, pairs, near, far)
    dx, mix, gate = outs[:3], outs[3], outs[4]
    rest = outs[5:]
    keep, parts, rest = rest[:SENT], rest[SENT : 2 * SENT], rest[2 * SENT :]
    return dx, mix, gate, keep, parts, rest[:left], rest[left:]


class Copies:
    def __init__(self, send, recv, local):
        self.send, self.recv, self.local = send, recv, local
        self.sends, self.recvs, self.locals, self.started = {}, {}, {}, []

    def remote(self, ends, name, arrives, device, last=True):
        sent = self.sends.setdefault(name, len(self.sends))
        got = self.recvs.setdefault(arrives, len(self.recvs))

        def make():
            source, target = ends()
            return pltpu.make_async_remote_copy(
                source, target, self.send.at[sent], self.recv.at[got],
                device_id=device, device_id_type=MESH_ID,
            )

        make().start()
        if last:
            self.started.append(lambda: make().wait_send())

    def sent(self, ends, name, device):
        source, target = ends()
        pltpu.make_async_remote_copy(
            source, target, self.send.at[self.sends[name]], self.recv.at[0],
            device_id=device, device_id_type=MESH_ID,
        ).wait_send()

    def arrived(self, place, name, device):
        got = self.recvs.setdefault(name, len(self.recvs))
        pltpu.make_async_remote_copy(
            place, place, self.send.at[0], self.recv.at[got],
            device_id=device, device_id_type=MESH_ID,
        ).wait_recv()

    def copy(self, ends, name, wait_last=True):
        at = self.locals.setdefault(name, len(self.locals))

        def make():
            return pltpu.make_async_copy(*ends(), self.local.at[at])

        make().start()
        if wait_last:
            self.started.append(lambda: make().wait())
        return lambda: make().wait()

    def wait_copy(self, ends, name):
        pltpu.make_async_copy(*ends(), self.local.at[self.locals[name]]).wait()

    def finish(self):
        for wait in self.started:
            wait()


class Neighbours:
    def __init__(self, inner):
        me = lax.axis_index("dp")
        at = me // inner
        self.core = lax.axis_index("tensor")
        self.z, self.y, self.x = at // 4, at // 2 % 2, at % 2
        self.spots = [(self.z + dz + 4) % 4 for dz in Z_FROM]
        self.along = [{"dp": me + (spot - self.z) * 4 * inner} for spot in self.spots]
        self.over_y = {"dp": me + (1 - 2 * self.y) * 2 * inner}
        self.over_x = {"dp": me + (1 - 2 * self.x) * inner}
        self.twin = {"tensor": 1 - self.core}
        self.blocks = {
            (k, other_y, other_x): self.spots[k] * 4
            + (1 - self.y if other_y else self.y) * 2
            + (1 - self.x if other_x else self.x)
            for k in range(SLOTS)
            for other_y in (0, 1)
            for other_x in (0, 1)
        }

    def greet(self):
        barrier = pltpu.get_barrier_semaphore()
        devices = [*self.along[1:], self.over_y, self.over_x, self.twin]
        for device in devices:
            pl.semaphore_signal(barrier, inc=1, device_id=device, device_id_type=MESH_ID)
        pl.semaphore_wait(barrier, len(devices))

    def block(self, k, other_y, other_x):
        return self.blocks[k, other_y, other_x]


BACK = (0, 2, 1, 3)


class Gather:
    def __init__(self, copies, near, shard, full, tag):
        self.copies, self.near, self.shard, self.full, self.tag = copies, near, shard, full, tag
        self.split = full.shape[2] // (2 * LANES) * LANES

    def source(self, k):
        return self.shard if k == 0 else self.full.at[self.near.block(k, 0, 0)]

    def begin(self):
        for k in range(1, SLOTS):
            self.copies.remote(
                lambda: (self.shard, self.full.at[self.near.block(0, 0, 0)]),
                (self.tag, "z", k), (self.tag, "z", BACK[k]), self.near.along[k],
            )
        self.full[self.near.block(0, 0, 0)] = self.shard[...]

    def spread(self, k):
        near, place = self.near, self.full.at[self.near.block(k, 0, 0)]
        if k > 0:
            self.copies.arrived(place, (self.tag, "z", k), near.along[k])
        for way, device in (("y", near.over_y), ("x", near.over_x)):
            name = (self.tag, way, k)
            self.copies.remote(
                lambda: (self.source(k), self.full.at[near.block(k, 0, 0)]), name, name, device
            )

    def cross(self, k):
        near = self.near
        from_y = self.full.at[near.block(k, 1, 0)]
        from_x = self.full.at[near.block(k, 0, 1)]
        self.copies.arrived(from_y, (self.tag, "y", k), near.over_y)
        self.copies.remote(
            lambda: (self.full.at[near.block(k, 1, 0), :, : self.split],) * 2,
            (self.tag, "one", k), (self.tag, "one", k), near.over_x,
        )
        self.copies.arrived(from_x, (self.tag, "x", k), near.over_x)
        self.copies.remote(
            lambda: (self.full.at[near.block(k, 0, 1), :, self.split :],) * 2,
            (self.tag, "two", k), (self.tag, "two", k), near.over_y,
        )

    def end(self):
        near = self.near
        for k in range(SLOTS):
            place = self.full.at[near.block(k, 1, 1)]
            self.copies.arrived(place.at[:, : self.split], (self.tag, "one", k), near.over_x)
            self.copies.arrived(place.at[:, self.split :], (self.tag, "two", k), near.over_y)


def roll_left(slab, lanes):
    return pltpu.roll(slab, LANES - lanes, 1)


def forward_kernel(
    inner, w_query, w_keyval, w_out, w_router, gains, frequency, seg_row, routes,
    gateup_hbm, down_hbm, hidden_hbm, og_hbm,
    small, combine, combine_pair, seg_col,
    q_full_out, o_full_out, normed_out, q_out, k_out, v_out, attended_out, lse_out, cos_out, sin_out,
    middle_hbm, x_hbm, xt_hbm, og_pair, ogt_hbm, pairs_hbm, near_hbm, far_hbm,
    hidden, gateup, down, given, pairs, bias, k_low, k_high, v_low, v_high, part, part_got, x_own, x_got,
    middle, stage, turned, columns_out, columns_got, q_shard, o_shard,
    q_full, o_full, normed, q_ref, k_ref, v_ref, attended, lse_ref, cos, sin, send, recv, local,
):
    near = Neighbours(inner)
    copies = Copies(send, recv, local)
    tokens, width = hidden.shape
    block = width // 16
    chunks = pairs.shape[0]
    hid = down.shape[2]
    q_width = q_ref.shape[1]
    kv_slabs = k_ref.shape[1] // LANES
    slabs = q_width // LANES
    qkv_width = q_width + 2 * k_ref.shape[1]
    experts = down.shape[0]
    each = 2 + experts
    half = tokens // 2
    tiles = tokens // ROWS
    x, core = near.x, near.core
    own_half = pl.ds(pl.multiple_of(core * half, half), half)
    mine = pl.ds(pl.multiple_of(tokens + core * half, half), half)
    theirs = pl.ds(pl.multiple_of(tokens + (1 - core) * half, half), half)

    weights_in = [
        copies.copy(lambda: (gateup_hbm, gateup), "gateup", False),
        copies.copy(lambda: (down_hbm, down), "down", False),
    ]
    hidden_in = copies.copy(lambda: (hidden_hbm, hidden), "hidden", False)
    kv_width = k_ref.shape[1]
    q_shard[:, :q_width] = w_query[...].astype(BF16)
    q_shard[:, q_width : q_width + kv_width] = w_keyval[0].astype(BF16)
    q_shard[:, q_width + kv_width : qkv_width] = w_keyval[1].astype(BF16)
    o_shard[...] = w_out[...].astype(BF16)
    cos[:block, :] = jnp.zeros((block, LANES), F32)
    cos[:block, :experts] = w_router[...]
    value = jnp.concatenate([gains[...], jnp.zeros((LANES - 2, block), F32)]).T
    value = value + pltpu.roll(cos[:block, :], 2, 1)
    high = value.astype(BF16).astype(F32)
    mid = (value - high).astype(BF16).astype(F32)
    low = value - high - mid
    value = high + pltpu.roll(mid, each, 1) + pltpu.roll(low, 2 * each, 1)
    q_shard[:, qkv_width:] = value.astype(BF16)
    near.greet()
    gather_q = Gather(copies, near, q_shard, q_full, "q")
    gather_o = Gather(copies, near, o_shard, o_full, "o")
    gather_q.begin()
    gather_q.spread(0)
    copies.copy(lambda: (og_hbm, og_pair.at[pl.ds(0, tokens)]), "og")
    segment = seg_row[...].astype(F32)
    seg_col[...] = jnp.broadcast_to(segment, (8, tokens)).T[:, :1]

    def pack(c, mine):
        first = 2 * (chunks * (x if mine else 1 - x) + c)
        rows = pl.ds(pl.multiple_of(x * block, block), block)
        for e in range(CHUNK):
            for part_at in range(2):
                at = hid * (2 * e + part_at)
                value = gateup[first + e, part_at].astype(BF16)
                if mine:
                    pairs[c, rows, at : at + hid] = value
                else:
                    given[c, :, at : at + hid] = value
            at = hid * (2 * CHUNK + e)
            value = down[first + e].astype(BF16)
            if mine:
                pairs[c, rows, at : at + hid] = value
            else:
                given[c, :, at : at + hid] = value

    def swap(c):
        rows = pl.ds(pl.multiple_of(x * block, block), block)
        copies.remote(
            lambda: (given.at[c], pairs.at[c, rows]), ("s", c), ("s", c), near.over_x
        )

    def swapped(c):
        rows = pl.ds(pl.multiple_of((1 - x) * block, block), block)
        copies.arrived(pairs.at[c, rows], ("s", c), near.over_x)

    def ring_one(c):
        copies.remote(
            lambda: (pairs.at[c], near_hbm.at[c, 0]), ("up", c), ("r", c, 1), near.along[2]
        )
        copies.remote(
            lambda: (pairs.at[c], near_hbm.at[c, 1]), ("down", c), ("r", c, 2), near.along[1]
        )

    def ring_two(c):
        copies.arrived(near_hbm.at[c, 0], ("r", c, 1), near.along[1])
        copies.remote(
            lambda: (near_hbm.at[c, 0], near_hbm.at[c, 2]), ("two", c), ("r", c, 3), near.along[2]
        )

    def over_y(c, k):
        copies.remote(
            lambda: (pairs.at[c] if k == 0 else near_hbm.at[c, k - 1], far_hbm.at[c, k]),
            ("f", c, k), ("f", c, k), near.over_y,
        )

    def ring_got(c, k):
        copies.arrived(near_hbm.at[c, k - 1], ("r", c, k), near.along[k])

    def turn_tile(source, target, name, side):
        copies.copy(lambda: (source, stage.at[side]), (name, "in"), False)()
        turned[side] = stage[side].T
        return copies.copy(lambda: (turned.at[side], target), (name, "out"), False)

    waits = [None, None]

    def turn_next(source, target, name, side):
        if waits[side] is not None:
            waits[side]()
        waits[side] = turn_tile(source, target, name, side)

    for wait in weights_in:
        wait()
    pack(0, False)
    swap(0)
    pack(0, True)
    gather_q.spread(1)
    gather_q.spread(2)
    pack(1, False)
    pack(1, True)
    gather_q.cross(0)
    gather_q.spread(3)
    half_width = HEAD_DIM // 2
    lane = lax.broadcasted_iota(jnp.int32, (ROWS, LANES), 1)
    for at in range(0, tokens, ROWS):
        rows = slice(at, at + ROWS)
        earlier = jnp.where(segment < seg_col[rows, :], 1.0, 0.0)
        position = (at + lax.broadcasted_iota(jnp.int32, (ROWS, 1), 0)).astype(F32)
        position = position - jnp.sum(earlier, axis=1, keepdims=True)
        angle = position * frequency[...]
        cos[rows, :] = jnp.cos(angle)
        wave = jnp.sin(angle)
        sin[rows, :] = jnp.where(lane % HEAD_DIM < half_width, -wave, wave)
    gather_q.cross(1)
    gather_q.cross(2)
    gather_q.cross(3)
    gather_o.begin()
    gather_o.spread(0)
    swap(1)
    pack(2, False)
    pack(2, True)
    pack(3, False)
    pack(3, True)
    fill_bias(bias, seg_col, segment)
    for tile in range(tiles):
        rows = pl.ds(tile * ROWS, ROWS)
        turn_next(og_hbm.at[rows], ogt_hbm.at[:, rows], ("og", tile), tile % 2)
    hidden_in()
    gather_q.end()
    pieces = q_full[:, :, qkv_width:].reshape(width, LANES)
    wide = pieces.astype(F32)
    summed = wide + roll_left(wide, each) + roll_left(wide, 2 * each)
    small[...] = summed.T[: small.shape[0], :]
    copies.copy(lambda: (q_full, q_full_out), "q full")
    copies.copy(lambda: (cos, cos_out), "cos")
    copies.copy(lambda: (sin, sin_out), "sin")
    swapped(0)
    ring_one(0)
    over_y(0, 0)
    swap(2)
    swap(3)

    def project(tile, carry):
        rows = pl.ds(pl.multiple_of(tile * ROWS, ROWS), ROWS)
        for here in few_rows(ROWS):
            value = hidden[pl.ds(pl.multiple_of(tile * ROWS + here.start, 16), 16), :].astype(F32)
            inverse = lax.rsqrt(jnp.mean(value * value, axis=1, keepdims=True) + NORM_EPSILON)
            stage[0, here, :] = (value * inverse * small[0:1, :]).astype(BF16)
        low = stage[0]
        normed[:, rows] = low.T
        cosine, sine = cos[rows, :], sin[rows, :]
        for g in range(slabs + 2 * kv_slabs):
            lanes = slice(g * LANES, (g + 1) * LANES)
            if g % 2 == 0:
                two = slice(g * LANES, (g + 2) * LANES)
                lin_two = dot(low, q_full[:, :, two].reshape(width, 2 * LANES))
            lin = lin_two[:, (g % 2) * LANES : (g % 2 + 1) * LANES]
            if g < slabs + kv_slabs:
                lin = lin * cosine + rotate_halves(lin) * sine
            if g < slabs:
                q_ref[rows, lanes] = lin.astype(BF16)
            elif g < slabs + kv_slabs:
                at = (g - slabs) * LANES
                k_ref[rows, at : at + LANES] = lin.astype(BF16)
            else:
                at = (g - slabs - kv_slabs) * LANES
                v_ref[rows, at : at + LANES] = lin.astype(BF16)

        @pl.when(tile == 1)
        def _():
            gather_o.spread(1)

        @pl.when(tile == 2)
        def _():
            gather_o.spread(2)
            gather_o.cross(0)

        return carry

    lax.fori_loop(0, tiles, project, 0)
    copies.copy(lambda: (normed, normed_out), "normed")
    copies.copy(lambda: (q_ref, q_out), "q")
    copies.copy(lambda: (k_ref, k_out), "k")
    copies.copy(lambda: (v_ref, v_out), "v")
    for j in range(kv_slabs):
        lanes = slice(j * LANES, (j + 1) * LANES)
        spread_heads(k_ref[:, lanes], k_low, k_high, 2 * j)
        spread_heads(v_ref[:, lanes], v_low, v_high, 2 * j)

    def attend(g, carry):
        lanes = pl.ds(pl.multiple_of(g * LANES, LANES), LANES)
        kv_even, kv_odd = (2 * g) // 3, (2 * g + 1) // 3
        for at in range(0, tokens, ROWS):
            rows = slice(at, at + ROWS)
            upto = at + ROWS
            queries = q_ref[rows, lanes]
            total = None
            stats = []
            for keys, values, kv_at in ((k_low, v_low, kv_even), (k_high, v_high, kv_odd)):
                scores = dot(queries, keys[kv_at, :upto, :], NT) * SCORE_SCALE + bias[rows, :upto]
                highest = jnp.max(scores, axis=1, keepdims=True)
                weights = jnp.exp(scores - highest)
                whole = jnp.sum(weights, axis=1, keepdims=True)
                probability = (weights * (1.0 / whole)).astype(BF16)
                one = dot(probability, values[kv_at, :upto, :])
                total = one if total is None else total + one
                stats.append(highest + jnp.log(whole))
            attended[rows, lanes] = total.astype(BF16)
            across = jnp.where(half_mask(ROWS, False), stats[0], stats[1]).T
            lse_ref[g, 0:1, rows] = across[0:1, :]
            lse_ref[g, 1:2, rows] = across[HEAD_DIM : HEAD_DIM + 1, :]

        @pl.when(g == 0)
        def _():
            gather_o.spread(3)
            gather_o.cross(1)
            gather_o.cross(2)

        @pl.when(g == 1)
        def _():
            ring_two(0)
            over_y(0, 1)
            ring_got(0, 2)
            over_y(0, 2)
            swapped(1)
            ring_one(1)
            over_y(1, 0)
            copies.remote(
                lambda: (og_hbm.at[own_half], og_pair.at[mine]), ("og",), ("og",), near.over_x
            )

        @pl.when(g == 2)
        def _():
            gather_o.cross(3)

        @pl.when(g == 4)
        def _():
            gather_o.end()

        @pl.when(g == slabs - 1)
        def _():
            ring_got(0, 3)
            over_y(0, 3)
            swapped(2)
            ring_one(2)
            over_y(2, 0)

        return carry

    lax.fori_loop(0, slabs, attend, 0)
    copies.copy(lambda: (o_full, o_full_out), "o full")
    copies.copy(lambda: (attended, attended_out), "attended")
    copies.copy(lambda: (lse_ref, lse_out), "lse")

    def project_out(step, carry):
        tile = (step + 2 * (1 - core)) % tiles
        rows = pl.ds(pl.multiple_of(tile * ROWS, ROWS), ROWS)
        low = attended[rows, :]
        for group in range(SLOTS):
            cols = slice(4 * block * group, 4 * block * (group + 1))
            weight = o_full[4 * group : 4 * (group + 1)].reshape(4 * block, q_width)
            part[rows, cols] = dot(low, weight, NT).astype(BF16)
        return carry

    for step in range(tiles):
        project_out(step, 0)
        tile = (step + 2 * (1 - core)) % tiles
        rows = pl.ds(pl.multiple_of(tile * ROWS, ROWS), ROWS)
        copies.remote(
            lambda rows=rows: (part.at[rows], part_got.at[rows]),
            ("p", step), ("p", step), near.twin,
        )
    router = q_full[:, :, qkv_width:].reshape(width, LANES)
    for step in range(tiles):
        tile = (step + 2 * core) % tiles
        rows = pl.ds(pl.multiple_of(tile * ROWS, ROWS), ROWS)
        copies.arrived(part_got.at[rows], ("p", step), near.twin)
        side = step % 2
        if step >= 2:
            middle_out[side]()
        elif step == 0:
            middle_out = [None, None]
        for here in few_rows(ROWS):
            at = pl.ds(pl.multiple_of(tile * ROWS + here.start, 16), 16)
            total = hidden[at, :].astype(F32) + RESIDUAL_SCALE * (
                part[at, :].astype(F32) + part_got[at, :].astype(F32)
            )
            middle[side, here, :] = total
            inverse = lax.rsqrt(jnp.mean(total * total, axis=1, keepdims=True) + NORM_EPSILON)
            value = total * inverse * small[1:2, :]
            high = value.astype(BF16)
            x_own[at, :] = high
            rest = value - high.astype(F32)
            mid = rest.astype(BF16)
            stage[0, here, :] = mid
            stage[1, here, :] = (rest - mid.astype(F32)).astype(BF16)
        middle_out[side] = copies.copy(
            lambda rows=rows, side=side: (middle.at[side], middle_hbm.at[rows]), ("m", step), False
        )
        copies.copy(lambda rows=rows: (x_own.at[rows], x_hbm.at[rows]), ("x", step))
        if step < 2:
            copies.remote(
                lambda rows=rows: (x_own.at[rows], x_got.at[rows]),
                ("x", step), ("x", step), near.over_x,
            )
        one, two, three = dot(x_own[rows, :], router), dot(stage[0], router), dot(stage[1], router)
        logits = one + roll_left(one, each) + roll_left(one, 2 * each) + two + roll_left(two, each)
        logits = roll_left(logits + three, 2)
        lane = lax.broadcasted_iota(jnp.int32, (ROWS, LANES), 1)
        chosen = lane < 0
        route = routes[:, rows].astype(F32).T
        for k in range(routes.shape[0]):
            chosen = chosen | (route[:, k : k + 1] == lane.astype(F32))
        logits = jnp.where(chosen, logits, MASK_VALUE)
        powers = jnp.exp(logits - jnp.max(logits, axis=1, keepdims=True))
        powers = jnp.where(chosen, powers, 0.0)
        combine[rows, :] = powers * (1.0 / jnp.sum(powers, axis=1, keepdims=True))
        if step == 0:
            swapped(3)
            copies.copy(lambda: (pairs, pairs_hbm), "pairs")
        if step == 1:
            ring_two(1)
            over_y(1, 1)
            ring_got(1, 2)
            over_y(1, 2)

    shares = experts // 2
    flipped = combine[...].T
    kept = jnp.where(x == 0, flipped[:shares, :], flipped[shares : 2 * shares, :])
    gone = jnp.where(x == 0, flipped[shares : 2 * shares, :], flipped[:shares, :])
    columns_out[...] = gone
    copies.remote(lambda: (columns_out, columns_got), ("c",), ("c",), near.over_x)
    combine_pair[:tokens, :] = kept.T
    ring_two(2)
    ring_got(1, 3)
    over_y(1, 3)

    copies.arrived(og_pair.at[mine], ("og",), near.over_x)
    copies.remote(lambda: (og_pair.at[mine],) * 2, ("og2",), ("og2",), near.twin)
    for tile in range(tiles):
        rows = pl.ds(tile * ROWS, ROWS)
        if waits[tile % 2] is not None:
            waits[tile % 2]()
        turned[tile % 2] = x_own[rows, :].T
        waits[tile % 2] = copies.copy(
            lambda rows=rows, side=tile % 2: (turned.at[side], xt_hbm.at[:, rows]),
            ("xt", tile), False,
        )
    copies.arrived(columns_got, ("c",), near.over_x)
    combine_pair[tokens:, :] = columns_got[...].T
    copies.arrived(og_pair.at[theirs], ("og2",), near.twin)
    order = [(step + 2 * core) % tiles for step in range(2)]
    order += [(step + 2 * (1 - core)) % tiles for step in range(2)]

    def og_rows(step):
        return pl.ds(pl.multiple_of(tokens + order[step] * ROWS, ROWS), ROWS)

    def og_load(step):
        return copies.copy(
            lambda: (og_pair.at[og_rows(step)], stage.at[step % 2]), ("ogin", step), False
        )

    loaded = og_load(0)
    for step in range(tiles):
        loaded()
        if step + 1 < tiles:
            loaded = og_load(step + 1)
        side = step % 2
        waits[side]()
        turned[side] = stage[side].T
        waits[side] = copies.copy(
            lambda step=step, side=side: (turned.at[side], ogt_hbm.at[:, og_rows(step)]),
            ("ogt", step), False,
        )
    for step in range(tiles):
        rows = pl.ds(pl.multiple_of(order[step] * ROWS, ROWS), ROWS)
        there = pl.ds(pl.multiple_of(tokens + order[step] * ROWS, ROWS), ROWS)
        if step < 2:
            copies.arrived(x_got.at[rows], ("x", step), near.over_x)
            copies.remote(
                lambda rows=rows: (x_got.at[rows],) * 2, ("x2", step), ("x2", step), near.twin
            )
        else:
            copies.arrived(x_got.at[rows], ("x2", step - 2), near.twin)
        copies.copy(
            lambda rows=rows, there=there: (x_got.at[rows], x_hbm.at[there]), ("xg", step)
        )
        side = step % 2
        waits[side]()
        turned[side] = x_got[rows, :].T
        waits[side] = copies.copy(
            lambda there=there, side=side: (turned.at[side], xt_hbm.at[:, there]),
            ("xgt", step), False,
        )
    for wait in waits + middle_out:
        wait()
    ring_got(2, 2)
    ring_got(2, 3)
    for c in range(LATE + 1):
        for k in range(SLOTS if c < LATE else 1):
            copies.arrived(far_hbm.at[c, k], ("f", c, k), near.over_y)
    copies.finish()


def forward_pass(weights, frequency, segments, routes, gateup, down, hidden, og):
    tokens, width = hidden.shape
    experts, hid = down.shape[0], down.shape[2]
    block, q_width = weights[0].shape
    kv_width = weights[1].shape[2]
    q_columns = q_width + 2 * kv_width + LANES
    slabs, kv_heads = q_width // LANES, kv_width // HEAD_DIM
    chunks = experts // (2 * CHUNK)
    columns = 3 * CHUNK * hid
    anywhere, vmem = pl.BlockSpec(memory_space=pl.ANY), vmem_spec()
    shape = jax.ShapeDtypeStruct
    inner = lax.axis_size("dp") // 16
    dma = pltpu.SemaphoreType.DMA
    kept = [
        shape((16, block, q_columns), BF16),
        shape((16, block, q_width), BF16),
        shape((width, tokens), BF16),
        shape((tokens, q_width), BF16),
        shape((tokens, kv_width), BF16),
        shape((tokens, kv_width), BF16),
        shape((tokens, q_width), BF16),
        shape((slabs, 8, tokens), F32),
        shape((tokens, LANES), F32),
        shape((tokens, LANES), F32),
    ]
    return pl.pallas_call(
        functools.partial(forward_kernel, inner),
        in_specs=[vmem] * 8 + [anywhere] * 4,
        out_specs=[vmem] * 4 + [anywhere] * 18,
        out_shape=[
            shape((24, width), F32),
            shape((tokens, LANES), F32),
            shape((2 * tokens, experts // 2), F32),
            shape((tokens, 1), F32),
            *kept,
            shape((tokens, width), F32),
            shape((2 * tokens, width), BF16),
            shape((width, 2 * tokens), BF16),
            shape((2 * tokens, width), BF16),
            shape((width, 2 * tokens), BF16),
            shape((chunks, 2 * block, columns), BF16),
            shape((chunks - 1, SLOTS - 1, 2 * block, columns), BF16),
            shape((LATE + 1, SLOTS, 2 * block, columns), BF16),
        ],
        scratch_shapes=[
            pltpu.VMEM((tokens, width), BF16),
            pltpu.VMEM(gateup.shape, gateup.dtype),
            pltpu.VMEM(down.shape, down.dtype),
            pltpu.VMEM((chunks, block, columns), BF16),
            pltpu.VMEM((chunks, 2 * block, columns), BF16),
            pltpu.VMEM((tokens, tokens), F32),
        ]
        + [pltpu.VMEM((kv_heads, tokens, LANES), BF16)] * 4
        + [pltpu.VMEM((tokens, width), BF16)] * 4
        + [
            pltpu.VMEM((2, ROWS, width), F32),
            pltpu.VMEM((2, ROWS, width), BF16),
            pltpu.VMEM((2, width, ROWS), BF16),
            pltpu.VMEM((experts // 2, tokens), F32),
            pltpu.VMEM((experts // 2, tokens), F32),
            pltpu.VMEM((block, q_columns), BF16),
            pltpu.VMEM((block, q_width), BF16),
            *[pltpu.VMEM(one.shape, one.dtype) for one in kept],
            dma((80,)), dma((80,)), dma((64,)),
        ],
        compiler_params=pltpu.CompilerParams(
            vmem_limit_bytes=EXPERT_VMEM, collective_id=1, has_side_effects=True
        ),
        name="forward_pass",
    )(*weights, frequency, segments[None, :], routes.T, gateup, down, hidden, og)


class Scatter:
    def __init__(self, copies, near, grad, one, two, got_y, got_x, got_z, share, tag):
        self.copies, self.near, self.grad, self.share, self.tag = copies, near, grad, share, tag
        self.one, self.two, self.got_y, self.got_x, self.got_z = one, two, got_y, got_x, got_z
        self.split = one.shape[2]

    def begin(self, k):
        near = self.near
        self.copies.remote(
            lambda: (self.grad.at[near.block(k, 1, 1), :, : self.split], self.one.at[k]),
            (self.tag, "one", k), (self.tag, "one", k), near.over_x,
        )
        self.copies.remote(
            lambda: (self.grad.at[near.block(k, 1, 1), :, self.split :], self.two.at[k]),
            (self.tag, "two", k), (self.tag, "two", k), near.over_y,
        )

    def cross(self, k):
        near, grad, split = self.near, self.grad, self.split
        self.copies.arrived(self.one.at[k], (self.tag, "one", k), near.over_x)
        at = near.block(k, 1, 0)
        for here in few_rows(grad.shape[1]):
            grad[at, here, :split] = (
                grad[at, here, :split].astype(F32) + self.one[k, here, :].astype(F32)
            ).astype(BF16)
        self.copies.remote(
            lambda: (grad.at[near.block(k, 1, 0)], self.got_y.at[k]),
            (self.tag, "y", k), (self.tag, "y", k), near.over_y,
        )
        self.copies.arrived(self.two.at[k], (self.tag, "two", k), near.over_y)
        at = near.block(k, 0, 1)
        for here in few_rows(grad.shape[1]):
            grad[at, here, split:] = (
                grad[at, here, split:].astype(F32) + self.two[k, here, :].astype(F32)
            ).astype(BF16)
        self.copies.remote(
            lambda: (grad.at[near.block(k, 0, 1)], self.got_x.at[k]),
            (self.tag, "x", k), (self.tag, "x", k), near.over_x,
        )

    def plane(self, k):
        near, grad = self.near, self.grad
        self.copies.arrived(self.got_y.at[k], (self.tag, "y", k), near.over_y)
        self.copies.arrived(self.got_x.at[k], (self.tag, "x", k), near.over_x)
        at = near.block(k, 0, 0)
        for here in few_rows(grad.shape[1]):
            total = grad[at, here, :].astype(F32) + self.got_y[k, here, :].astype(F32)
            total = total + self.got_x[k, here, :].astype(F32)
            if k == 0:
                self.share[here, :] = total
            else:
                grad[at, here, :] = total.astype(BF16)
        if k == 0:
            return
        self.copies.remote(
            lambda: (grad.at[near.block(k, 0, 0)], self.got_z.at[BACK[k] - 1]),
            (self.tag, "z", k), (self.tag, "z", BACK[k]), near.along[k],
        )

    def end(self):
        for k in range(1, SLOTS):
            self.copies.arrived(self.got_z.at[k - 1], (self.tag, "z", k), self.near.along[k])
            for here in few_rows(self.share.shape[0]):
                self.share[here, :] = self.share[here, :] + self.got_z[k - 1, here, :].astype(F32)


STRIP = 128


def backward_kernel(
    inner,
    seg_col, seg_row, small, combine, gate_turned,
    o_full_hbm, attended_hbm, q_ref_hbm, k_ref_hbm, v_ref_hbm, lse_hbm, cos_hbm, sin_hbm, q_hbm, normed_hbm, hidden_hbm, og_hbm, middle_hbm, dx_own, dx_twin, dx_other,
    mix_pair, *refs,
):
    keeps, refs = refs[:SENT], refs[SENT:]
    parts, refs = refs[:SENT], refs[SENT:]
    near_two, near_three, late_got, far_first, far_three = refs[:5]
    q_share, o_share, input_grad, block_out, kept_out, given_got, mid_grad = refs[5:12]
    far_got, first_got, z_two, z_three, mix_twin, mix_other = refs[12:18]
    (
        attended_grad, lin_grad, o_grad, q_grad, o_one, o_two, o_y, o_x, o_z,
        q_one, q_two, q_y, q_x, q_z, part_got, pieces, z_send, z_keep, given, kept,
        strips, wide_in, wide_out, strip_out, router_rows, gate_columns, small_sum,
        o_full, attended, q_ref, k_ref, v_ref, lse_ref, cos, sin,
        send, recv, local, strip_sem, wide_sem, out_sem,
    ) = refs[18:]
    near = Neighbours(inner)
    copies = Copies(send, recv, local)
    tokens, width = hidden_hbm.shape
    block = width // 16
    x, core = near.x, near.core
    half = tokens // 2
    q_width = q_ref.shape[1]
    kv_width = k_ref.shape[1]
    kv_slabs, slabs = kv_width // LANES, q_width // LANES
    qkv_width = q_width + 2 * kv_width
    experts = gate_turned.shape[0]
    each = 2 + experts
    strip_count = tokens // STRIP
    ours = pl.ds(0, tokens)
    half_mine = pl.ds(pl.multiple_of(tokens + core * half, half), half)
    there = pl.ds(pl.multiple_of(core * half, half), half)
    not_there = pl.ds(pl.multiple_of((1 - core) * half, half), half)
    scatter_o = Scatter(copies, near, o_grad, o_one, o_two, o_y, o_x, o_z, o_share, "o")
    scatter_q = Scatter(copies, near, q_grad, q_one, q_two, q_y, q_x, q_z, q_share, "q")
    z_gots = [*parts, z_two, z_three]

    def y_ends(c, k):
        if c == SENT:
            return near_two.at[k], first_got if k == 0 else late_got.at[k - 1]
        return near_three.at[k], far_got.at[k]

    def y_load(c, k, i, which):
        if 0 in which:
            copies.copy(lambda: (y_ends(c, k)[0], pieces.at[2 * i]), ("own", c, k), False)
        if 1 in which:
            copies.copy(lambda: (y_ends(c, k)[1], pieces.at[2 * i + 1]), ("got", c, k), False)

    def y_sum(c, k, i):
        copies.wait_copy(lambda: (y_ends(c, k)[0], pieces.at[2 * i]), ("own", c, k))
        copies.wait_copy(lambda: (y_ends(c, k)[1], pieces.at[2 * i + 1]), ("got", c, k))
        if k > 0 and c > SENT:
            copies.sent(
                lambda: (z_send.at[k - 1], z_two.at[BACK[k] - 1]), (SENT, "z", k), near.along[k]
            )
        target = z_keep.at[c - SENT] if k == 0 else z_send.at[k - 1]
        for here in few_rows(target.shape[0]):
            target[here, :] = (
                pieces[2 * i, here, :].astype(F32) + pieces[2 * i + 1, here, :].astype(F32)
            ).astype(BF16)
        if k == 0:
            return
        copies.remote(
            lambda: (z_send.at[k - 1], z_gots[c].at[BACK[k] - 1]),
            (c, "z", k), (c, "z", BACK[k]), near.along[k], last=c > SENT,
        )

    def far_arrived(k):
        copies.arrived(far_got.at[k], ("far", k), near.over_y)

    def chunk_ends(c, k):
        return keeps[c] if k == 0 else z_gots[c].at[k - 1], pieces.at[k]

    def load_chunk(c):
        for k in range(1 if c >= SENT else 0, SLOTS):
            if c >= SENT:
                copies.arrived(z_gots[c].at[k - 1], (c, "z", k), near.along[k])
            copies.copy(lambda k=k: chunk_ends(c, k), (c, "sum", k), False)

    def sum_chunk(c):
        for k in range(1 if c >= SENT else 0, SLOTS):
            copies.wait_copy(lambda: chunk_ends(c, k), (c, "sum", k))
        if c >= 2:
            copies.wait_copy(lambda: (kept.at[c % 2], kept_out.at[c - 2]), ("kept", c - 2))
        for base, mine in ((x * block, True), ((1 - x) * block, False)):
            for here, rows in zip(few_rows(block), few_rows(block, base)):
                total = (pieces[0, rows, :] if c < SENT else z_keep[c - SENT, rows, :]).astype(F32)
                for k in range(1, SLOTS):
                    total = total + pieces[k, rows, :].astype(F32)
                if mine:
                    kept[c % 2, here, :] = total
                else:
                    given[c, here, :] = total.astype(BF16)
        copies.copy(lambda: (kept.at[c % 2], kept_out.at[c]), ("kept", c), c >= 2)
        copies.remote(
            lambda: (given.at[c], given_got.at[c]), ("given", c), ("given", c), near.over_x
        )

    def strip_rows(t):
        return pl.ds(pl.multiple_of(t * STRIP, STRIP), STRIP)

    def strip_loads(t, sources, wide):
        side = t % 2
        rows = strip_rows(t)
        loads = [
            pltpu.make_async_copy(source.at[rows], strips.at[i, side], strip_sem.at[i, side])
            for i, source in enumerate(sources)
        ]
        if wide is not None:
            loads.append(
                pltpu.make_async_copy(wide.at[rows], wide_in.at[side], wide_sem.at[side])
            )
        return loads

    def strip_store(t, source, target):
        side = t % 2
        return pltpu.make_async_copy(
            source.at[side], target.at[strip_rows(t)], out_sem.at[side]
        )

    def over_strips(sources, wide, source, target, compute):
        for load in strip_loads(0, sources, wide):
            load.start()

        def one(t, carry):
            side = t % 2

            @pl.when(t + 1 < strip_count)
            def _():
                for load in strip_loads(t + 1, sources, wide):
                    load.start()

            for load in strip_loads(t, sources, wide):
                load.wait()

            @pl.when(t >= 2)
            def _():
                strip_store(t - 2, source, target).wait()

            compute(t, side)
            strip_store(t, source, target).start()
            return carry

        lax.fori_loop(0, strip_count, one, 0)
        for t in (strip_count - 2, strip_count - 1):
            strip_store(t, source, target).wait()

    for i, k in enumerate((1, 2)):
        y_load(SENT, k, i, (0, 1))
    weights_in = copies.copy(lambda: (o_full_hbm, o_full), "o full", False)
    attended_in = copies.copy(lambda: (attended_hbm, attended), "attended", False)
    operands_in = [
        copies.copy(lambda one=one, to=to: (one, to), ("operand", i), False)
        for i, (one, to) in enumerate(
            (
                (q_ref_hbm, q_ref), (k_ref_hbm, k_ref), (v_ref_hbm, v_ref), (lse_hbm, lse_ref),
                (cos_hbm, cos), (sin_hbm, sin),
            )
        )
    ]
    near.greet()
    for k in (1, 2, 3, 0):
        copies.remote(
            lambda k=k: (far_three.at[k], far_got.at[k]), ("far", k), ("far", k), near.over_y
        )
    copies.remote(lambda: (far_first, first_got), ("first",), ("first",), near.over_y)
    copies.remote(
        lambda: (mix_pair.at[half_mine], mix_other.at[there]), ("mo",), ("mo",), near.over_x
    )
    copies.remote(lambda: (mix_pair.at[ours], mix_twin), ("mt",), ("mt",), near.twin)
    y_sum(SENT, 1, 0)
    y_load(SENT, 3, 0, (0, 1))
    y_sum(SENT, 2, 1)
    y_sum(SENT, 3, 0)
    load_chunk(0)

    router = small[2 : 2 + experts, :]
    high = router.astype(BF16).astype(F32)
    mid = (router - high).astype(BF16).astype(F32)
    low = router - high - mid
    router_rows[...] = jnp.concatenate(
        [high, mid, low, high, mid, high, jnp.zeros((LANES - 6 * experts, width), F32)]
    ).astype(BF16)
    gate_columns[...] = jnp.concatenate(
        [gate_turned[...], jnp.zeros((LANES - experts, tokens), F32)]
    ).T
    small_sum[...] = jnp.zeros_like(small_sum)

    def middle_part(turned_back):
        def compute(t, side):
            rows = strip_rows(t)
            gates, grads = combine[rows, :], gate_columns[rows, :]
            logit = gates * (grads - jnp.sum(gates * grads, axis=1, keepdims=True))
            one = logit.astype(BF16).astype(F32)
            two = (logit - one).astype(BF16).astype(F32)
            three = (logit - one - two).astype(BF16).astype(F32)

            def moved(piece, by):
                return pltpu.roll(piece, by * experts, 1)

            row = one + moved(one, 1) + moved(one, 2) + moved(two, 3) + moved(two, 4)
            row = (row + moved(three, 5)).astype(BF16)
            wide_out[side] = dot(row, router_rows[...])
            gain = small[1:2, :]
            gain_part = None
            back, n_one, n_two, n_three = (
                strip_out.at[0], strip_out.at[1], z_keep.at[0], z_keep.at[1]
            )
            for here in few_rows(STRIP):
                upstream = strips[0, side, here, :].astype(F32) + strips[1, side, here, :].astype(F32)
                upstream = upstream + strips[2, side, here, :].astype(F32)
                upstream = upstream + wide_out[side, here, :]
                middle = wide_in[side, here, :]
                inverse = lax.rsqrt(jnp.mean(middle * middle, axis=1, keepdims=True) + NORM_EPSILON)
                scaled = middle * inverse
                weighted = upstream * gain
                mean_term = jnp.mean(weighted * scaled, axis=1, keepdims=True)
                grad = strips[3, side, here, :].astype(F32) + inverse * (
                    weighted - scaled * mean_term
                )
                wide_out[side, here, :] = grad
                back[here, :] = (RESIDUAL_SCALE * grad).astype(BF16)
                gained = jnp.sum(upstream * scaled, axis=0, keepdims=True)
                gain_part = gained if gain_part is None else gain_part + gained
                normed = scaled * gain
                piece = normed.astype(BF16)
                n_one[here, :] = piece
                rest = normed - piece.astype(F32)
                piece = rest.astype(BF16)
                n_two[here, :] = piece
                n_three[here, :] = (rest - piece.astype(F32)).astype(BF16)
            small_sum[0:1, :] += gain_part
            strip = pl.ds(0, STRIP)
            turned_back[:, rows] = back[...].T
            attended_grad[rows, :] = dot(back[...], o_full[...].reshape(width, q_width)).astype(BF16)
            columns = (one + moved(two, 1) + moved(three, 2)).T[: 3 * experts, :].astype(BF16)
            a, b, c = (
                dot(columns, n_one[...]), dot(columns, n_two[strip, :]), dot(columns, n_three[strip, :])
            )
            e = experts
            small_sum[8 : 8 + e, :] += (
                a[:e] + a[e : 2 * e] + a[2 * e :] + b[:e] + b[e : 2 * e] + c[:e]
            )

        weights_in()
        over_strips([dx_own, dx_twin, dx_other, og_hbm], middle_hbm, wide_out, mid_grad, compute)
        attended_in()
        for group in range(SLOTS):
            rows = slice(4 * block * group, 4 * block * (group + 1))
            o_grad[4 * group : 4 * (group + 1)] = (
                dot(turned_back[rows, :], attended[...]).astype(BF16).reshape(4, block, q_width)
            )

    pl.run_scoped(middle_part, pltpu.VMEM((width, tokens), BF16))
    for k in (1, 2, 3, 0):
        scatter_o.begin(k)

    def attention_part(bias0, bias1, bias2, bias3, k_low, k_high, v_low, v_high, dk, dv, dq):
        biases = (bias0, bias1, bias2, bias3)
        for wait in operands_in:
            wait()
        for at, bias in enumerate(biases):
            upto = bias.shape[0]
            keys_at = lax.broadcasted_iota(jnp.int32, bias.shape, 0)
            rows_at = at * ROWS + lax.broadcasted_iota(jnp.int32, bias.shape, 1)
            same = seg_col[:upto, :] == seg_row[:, at * ROWS : (at + 1) * ROWS].astype(F32)
            bias[...] = jnp.where((rows_at >= keys_at) & same, 0.0, MASK_VALUE).astype(F32)
        for j in range(kv_slabs):
            lanes = slice(j * LANES, (j + 1) * LANES)
            spread_heads(k_ref[:, lanes], k_low, k_high, 2 * j)
            spread_heads(v_ref[:, lanes], v_low, v_high, 2 * j)
        dk[...] = jnp.zeros_like(dk)
        dv[...] = jnp.zeros_like(dv)

        def slab(g, carry):
            lanes = pl.ds(pl.multiple_of(g * LANES, LANES), LANES)
            kv_even, kv_odd = (2 * g) // 3, (2 * g + 1) // 3
            for at, bias in enumerate(biases):
                rows = slice(at * ROWS, (at + 1) * ROWS)
                upto = (at + 1) * ROWS
                queries, grads = q_ref[rows, lanes], attended_grad[rows, lanes]
                turned = (grads.astype(F32) * attended[rows, lanes].astype(F32)).T
                zero = jnp.zeros_like(queries)
                dq_part = None
                for upper, keys, values, kv_at in (
                    (False, k_low, v_low, kv_even), (True, k_high, v_high, kv_odd)
                ):
                    first = HEAD_DIM if upper else 0
                    delta = jnp.sum(turned[first : first + HEAD_DIM, :], axis=0, keepdims=True)
                    head = 1 if upper else 0
                    total = lse_ref[g, head : head + 1, rows]
                    keys_here = keys[kv_at, :upto, :]
                    scores = dot(keys_here, queries, NT) * SCORE_SCALE + bias[...]
                    probability = jnp.exp(scores - total)
                    prob_grad = dot(values[kv_at, :upto, :], grads, NT)
                    score_grad = (probability * (prob_grad - delta)).astype(BF16)
                    mask = half_mask(ROWS, upper)
                    dv[kv_at, :upto, :] += dot(
                        probability.astype(BF16), jnp.where(mask, grads, zero)
                    )
                    dk[kv_at, :upto, :] += dot(score_grad, jnp.where(mask, queries, zero))
                    one = dot(score_grad, keys_here, TN)
                    dq_part = one if dq_part is None else dq_part + one
                dq[rows, :] = dq_part * SCORE_SCALE
            whole = dq[...]
            lin_grad[:, lanes] = (
                whole * cos[...] - rotate_halves(whole) * sin[...]
            ).astype(BF16)

            @pl.when(g == 1)
            def _():
                for k in (1, 2, 3, 0):
                    scatter_o.cross(k)

            @pl.when(g == 2)
            def _():
                sum_chunk(0)
                y_load(SENT + 1, 1, 0, (0,))
                y_load(SENT + 1, 2, 1, (0,))

            @pl.when(g == 3)
            def _():
                far_arrived(1)
                y_load(SENT + 1, 1, 0, (1,))
                far_arrived(2)
                y_load(SENT + 1, 2, 1, (1,))
                far_arrived(3)
                y_sum(SENT + 1, 1, 0)
                y_load(SENT + 1, 3, 0, (0, 1))
                y_sum(SENT + 1, 2, 1)
                y_sum(SENT + 1, 3, 0)
                load_chunk(1)

            @pl.when(g == 4)
            def _():
                for k in (1, 2, 3, 0):
                    scatter_o.plane(k)
                sum_chunk(1)
                far_arrived(0)
                y_load(SENT + 1, 0, 0, (0, 1))
                copies.arrived(first_got, ("first",), near.over_y)
                y_load(SENT, 0, 1, (0, 1))

            return carry

        lax.fori_loop(0, slabs, slab, 0)
        low = half_mask(tokens, False)

        def joined(sums, j):
            one, two = sums[2 * j], sums[2 * j + 1]
            one = one + pltpu.roll(one, HEAD_DIM, 1)
            two = two + pltpu.roll(two, HEAD_DIM, 1)
            return jnp.where(low, one, two)

        for j in range(kv_slabs):
            at = q_width + j * LANES
            whole = joined(dk, j) * SCORE_SCALE
            lin_grad[:, at : at + LANES] = (
                whole * cos[...] - rotate_halves(whole) * sin[...]
            ).astype(BF16)
            at = at + kv_width
            lin_grad[:, at : at + LANES] = joined(dv, j).astype(BF16)

    kv_shape = (2 * kv_slabs, tokens, LANES)
    pl.run_scoped(
        attention_part,
        *[pltpu.VMEM(((at + 1) * ROWS, ROWS), F32) for at in range(tokens // ROWS)],
        *[pltpu.VMEM(kv_shape, BF16)] * 4,
        *[pltpu.VMEM(kv_shape, F32)] * 2,
        pltpu.VMEM((tokens, LANES), F32),
    )

    def last_part(normed_turned, q_full, part):
        normed_in = copies.copy(lambda: (normed_hbm, normed_turned), "normed", False)
        weights_in = copies.copy(lambda: (q_hbm, q_full), "q weights", False)
        columns = jnp.concatenate(
            [
                small_sum[0:1, :], small_sum[8 : 8 + experts, :],
                jnp.zeros((LANES - 1 - experts, width), F32),
            ]
        ).T
        q_grad[:, :, qkv_width:] = columns.astype(BF16).reshape(16, block, LANES)
        normed_in()
        for k in (1, 2, 3, 0):
            spot = near.spots[k]
            rows = pl.ds(pl.multiple_of(spot * 4 * block, 4 * block), 4 * block)
            q_grad[pl.ds(spot * 4, 4), :, :qkv_width] = (
                dot(normed_turned[rows, :], lin_grad[...])
                .astype(BF16)
                .reshape(4, block, qkv_width)
            )
            scatter_q.begin(k)
        weights_in()

        def project(tile):
            rows = pl.ds(tile * ROWS, ROWS)
            for group in range(SLOTS):
                cols = slice(4 * block * group, 4 * block * (group + 1))
                weight = q_full[4 * group : 4 * (group + 1), :, :qkv_width]
                part[rows, cols] = dot(
                    lin_grad[rows, :], weight.reshape(4 * block, qkv_width), NT
                ).astype(BF16)
            copies.remote(
                lambda: (part.at[rows], part_got.at[rows]), ("n", tile), ("n", tile), near.twin,
                last=False,
            )

        project(0)
        project(1)
        for k in (1, 2, 3, 0):
            scatter_q.cross(k)
        y_sum(SENT + 1, 0, 0)
        y_sum(SENT, 0, 1)
        load_chunk(2)
        project(2)
        project(3)
        scatter_o.end()
        copies.arrived(mix_other.at[there], ("mo",), near.over_x)
        copies.remote(lambda: (mix_other.at[there],) * 2, ("m2",), ("m2",), near.twin)
        sum_chunk(2)
        for tile in range(tokens // ROWS):
            rows = pl.ds(tile * ROWS, ROWS)
            copies.arrived(part_got.at[rows], ("n", tile), near.twin)

        def finish_rows(t, side):
            for here in few_rows(STRIP):
                at = pl.ds(pl.multiple_of(t * STRIP + here.start, 16), 16)
                value = strips[0, side, here, :].astype(F32)
                inverse = lax.rsqrt(jnp.mean(value * value, axis=1, keepdims=True) + NORM_EPSILON)
                upstream = part[at, :].astype(F32) + part_got[at, :].astype(F32)
                scaled = value * inverse
                weighted = upstream * small[0:1, :]
                mean_term = jnp.mean(weighted * scaled, axis=1, keepdims=True)
                wide_out[side, here, :] = wide_in[side, here, :] + inverse * (
                    weighted - scaled * mean_term
                )

        over_strips([hidden_hbm], mid_grad, wide_out, input_grad, finish_rows)
        for k in (1, 2, 3, 0):
            scatter_q.plane(k)
        load_chunk(3)
        for tile in range(tokens // ROWS):
            rows = pl.ds(tile * ROWS, ROWS)
            copies.sent(lambda: (part.at[rows], part_got.at[rows]), ("n", tile), near.twin)

    pl.run_scoped(
        last_part,
        pltpu.VMEM((width, tokens), BF16), pltpu.VMEM(q_hbm.shape, BF16),
        pltpu.VMEM((tokens, width), BF16),
    )
    sum_chunk(3)
    copies.arrived(mix_twin, ("mt",), near.twin)
    copies.arrived(mix_other.at[not_there], ("m2",), near.twin)

    def mix_rows(t, side):
        for here in few_rows(STRIP):
            mix = strips[0, side, here, :].astype(F32) + strips[1, side, here, :].astype(F32)
            mix = mix + strips[2, side, here, :].astype(F32)
            strip_out[side, here, :] = (wide_in[side, here, :] + RESIDUAL_SCALE * mix).astype(BF16)

    over_strips([mix_pair, mix_twin, mix_other], middle_hbm, strip_out, block_out, mix_rows)
    scatter_q.end()
    for c in range(2 * SENT):
        copies.arrived(given_got.at[c], ("given", c), near.over_x)
    copies.finish()


def backward_pass(
    o_full, q, k, v, attended, lse, cosine, sine, seg_col, segments, small, combine, gate_turned,
    q_full, normed, hidden, og, middle, dx, mix, keep, parts, near_grads, far_grads,
):
    tokens, width = hidden.shape
    q_width, kv_width = q.shape[1], k.shape[1]
    block, q_columns = q_full.shape[1:]
    qkv_width = q_width + 2 * kv_width
    pair, columns = keep[0].shape
    chunks = 2 * SENT
    experts = gate_turned.shape[0]
    anywhere, vmem = pl.BlockSpec(memory_space=pl.ANY), vmem_spec()
    shape = jax.ShapeDtypeStruct
    dma = pltpu.SemaphoreType.DMA
    inner = lax.axis_size("dp") // 16

    def scatter_scratch(total):
        split = total // (2 * LANES) * LANES
        return [
            pltpu.VMEM((SLOTS, block, split), BF16),
            pltpu.VMEM((SLOTS, block, total - split), BF16),
            pltpu.VMEM((SLOTS, block, total), BF16),
            pltpu.VMEM((SLOTS, block, total), BF16),
            pltpu.VMEM((SLOTS - 1, block, total), BF16),
        ]

    values = (seg_col, segments[None, :], small, combine, gate_turned)
    read = (o_full, attended, q, k, v, lse, cosine, sine)
    far_values = (
        *read, q_full, normed, hidden, og, middle, *dx, mix, *keep, *parts, *near_grads, *far_grads,
    )
    return pl.pallas_call(
        functools.partial(backward_kernel, inner),
        in_specs=[vmem] * len(values) + [anywhere] * len(far_values),
        out_specs=[vmem] * 2 + [anywhere] * 11,
        out_shape=[
            shape((block, q_columns), F32),
            shape((block, q_width), F32),
            shape((tokens, width), F32),
            shape((tokens, width), BF16),
            shape((chunks, block, columns), F32),
            shape((chunks, block, columns), BF16),
            shape((tokens, width), F32),
            shape((SLOTS, pair, columns), BF16),
            shape((pair, columns), BF16),
            shape((SLOTS - 1, pair, columns), BF16),
            shape((SLOTS - 1, pair, columns), BF16),
            shape((tokens, width), BF16),
            shape((tokens, width), BF16),
        ],
        scratch_shapes=[
            pltpu.VMEM((tokens, q_width), BF16),
            pltpu.VMEM((tokens, qkv_width), BF16),
            pltpu.VMEM((16, block, q_width), BF16),
            pltpu.VMEM((16, block, q_columns), BF16),
        ]
        + scatter_scratch(q_width)
        + scatter_scratch(q_columns)
        + [
            pltpu.VMEM((tokens, width), BF16),
            pltpu.VMEM((SLOTS, pair, columns), BF16),
            pltpu.VMEM((SLOTS - 1, pair, columns), BF16),
            pltpu.VMEM((2, pair, columns), BF16),
            pltpu.VMEM((chunks, block, columns), BF16),
            pltpu.VMEM((2, block, columns), F32),
            pltpu.VMEM((4, 2, STRIP, width), BF16),
            pltpu.VMEM((2, STRIP, width), F32),
            pltpu.VMEM((2, STRIP, width), F32),
            pltpu.VMEM((2, STRIP, width), BF16),
            pltpu.VMEM((LANES, width), BF16),
            pltpu.VMEM((tokens, LANES), F32),
            pltpu.VMEM((8 + experts, width), F32),
            *[pltpu.VMEM(one.shape, one.dtype) for one in read],
            dma((80,)), dma((80,)), dma((64,)), dma((4, 2)), dma((2,)), dma((2,)),
        ],
        compiler_params=pltpu.CompilerParams(
            vmem_limit_bytes=EXPERT_VMEM, collective_id=2, has_side_effects=True
        ),
        name="backward_pass",
    )(*values, *far_values)


def whole_call(kernel, values, outs, earlier=(), name=None):
    return pl.pallas_call(
        with_earlier(kernel, len(values), len(earlier)),
        in_specs=[vmem_spec()] * len(values) + any_specs(earlier),
        out_specs=[vmem_spec()] * len(outs),
        out_shape=[jax.ShapeDtypeStruct(shape, dtype) for shape, dtype in outs],
        compiler_params=pltpu.CompilerParams(vmem_limit_bytes=VMEM_BYTES),
        name=name,
    )(*values, *earlier)


def fence_kernel(*refs):
    count = len(refs) // 2
    for value, out in zip(refs[:count], refs[count:]):
        out[...] = value[...]


def fence_all(values, *earlier):
    return whole_call(fence_kernel, values, [(v.shape, v.dtype) for v in values], earlier, "fence")


def fence(value, *earlier):
    return fence_all([value], *earlier)[0]


def sum_y_kernel(near, got, *outs):
    for k, out in enumerate(outs):
        out[...] = (near[k].astype(F32) + got[k].astype(F32)).astype(BF16)


def sum_y(near, got, *earlier):
    outs = [(near.shape[1:], BF16)] * SLOTS
    return whole_call(sum_y_kernel, [near, got], outs, earlier, "sum_y")


def sum_z_kernel(x_at, *refs):
    kept, given = refs[-2:]
    half = kept.shape[1]
    for c in range(kept.shape[0]):
        parts = refs[SLOTS * c : SLOTS * (c + 1)]
        for rows, out in ((x_at[0], kept), (1 - x_at[0], given)):
            rows = pl.ds(pl.multiple_of(rows * half, half), half)
            total = parts[0][rows, :].astype(F32)
            for part in parts[1:]:
                total = total + part[rows, :].astype(F32)
            out[c] = total.astype(out.dtype)


def sum_z(x_at, chunks, *earlier):
    count = len(chunks)
    pair, columns = chunks[0][0].shape
    flat = [part for parts in chunks for part in parts]
    return pl.pallas_call(
        with_earlier(sum_z_kernel, 1 + len(flat), len(earlier)),
        in_specs=[smem_spec()] + [vmem_spec()] * len(flat) + any_specs(earlier),
        out_specs=[vmem_spec()] * 2,
        out_shape=[
            jax.ShapeDtypeStruct((count, pair // 2, columns), F32),
            jax.ShapeDtypeStruct((count, pair // 2, columns), BF16),
        ],
        compiler_params=pltpu.CompilerParams(vmem_limit_bytes=VMEM_BYTES),
        name="sum_z",
    )(x_at, *flat, *earlier)


def sum_parts_kernel(parts, out):
    total = parts[0].astype(F32)
    for c in range(1, parts.shape[0]):
        total = total + parts[c].astype(F32)
    out[...] = total.astype(BF16)


def sum_parts(parts, *earlier):
    chunks, tokens, width = parts.shape
    return pl.pallas_call(
        with_earlier(sum_parts_kernel, 1, len(earlier)),
        grid=(tokens // EXPERT_ROWS,),
        in_specs=[pl.BlockSpec((chunks, EXPERT_ROWS, width), lambda s: (0, s, 0))]
        + any_specs(earlier),
        out_specs=pl.BlockSpec((EXPERT_ROWS, width), lambda s: (s, 0)),
        out_shape=jax.ShapeDtypeStruct((tokens, width), BF16),
        compiler_params=pltpu.CompilerParams(vmem_limit_bytes=VMEM_BYTES),
        name="sum_parts",
    )(parts, *earlier)


def adam_attention_kernel(q_share, o_share, *refs):
    states, outs = refs[:9], refs[9:18]
    gain_part = refs[18]
    q_width, kv_width = states[0].shape[1], states[3].shape[2]
    rate = (MODEL_DIM // 12) ** (-0.5)
    grad = q_share[:, :q_width]
    total = jnp.sum(states[0][...].astype(BF16).astype(F32) * grad, axis=1, keepdims=True)
    results = [
        adam_update(states[0][...], grad, states[1][...], states[2][...], rate, WEIGHT_DECAY)
    ]
    for out, result in zip(outs[:3], results[0]):
        out[...] = result
    for c in range(2):
        first = q_width + c * kv_width
        grad = q_share[:, first : first + kv_width]
        value = states[3][c]
        total = total + jnp.sum(value.astype(BF16).astype(F32) * grad, axis=1, keepdims=True)
        results = adam_update(value, grad, states[4][c], states[5][c], rate, WEIGHT_DECAY)
        for out, result in zip(outs[3:6], results):
            out[c] = result
    gain_part[...] = total
    results = adam_update(
        states[6][...], o_share[...], states[7][...], states[8][...],
        max(1, QUERY_HEADS * HEAD_DIM // 96) ** (-0.5), WEIGHT_DECAY,
    )
    for out, result in zip(outs[6:], results):
        out[...] = result


def adam_attention(q_share, o_share, states):
    outs = [(one.shape, F32) for one in states] + [((q_share.shape[0], 1), F32)]
    return whole_call(adam_attention_kernel, [q_share, o_share, *states], outs, (), "adam_attention")


def adam_experts_kernel(x_at, kept, got, *refs):
    states, outs = refs[:6], refs[6:]
    own = kept.shape[1]
    hidden = states[0].shape[3]
    mine = pl.program_id(0) // (pl.num_programs(0) // 2) == x_at[0]
    grad = jnp.where(mine, kept[0], got[0].astype(F32))
    for e in range(CHUNK):
        for part in range(2):
            first = hidden * (2 * e + part)
            results = adam_update(
                states[0][e, part], grad[:, first : first + hidden],
                states[1][e, part], states[2][e, part], MODEL_DIM ** (-0.5), WEIGHT_DECAY,
            )
            for out, result in zip(outs[:3], results):
                out[e, part] = result
        first = hidden * (2 * CHUNK + e)
        results = adam_update(
            states[3][e], grad[:, first : first + hidden], states[4][e], states[5][e],
            max(1, F // 256) ** (-0.5), WEIGHT_DECAY,
        )
        for out, result in zip(outs[3:], results):
            out[e] = result


def adam_experts(x_at, kept, got, gateup, down):
    chunks, own, columns = kept.shape
    experts, hidden = down[0].shape[0], down[0].shape[2]
    share = pl.BlockSpec((1, own, columns), lambda j: (j % chunks, 0, 0))
    big = pl.BlockSpec((CHUNK, 2, own, hidden), lambda j: (j, 0, 0, 0))
    small = pl.BlockSpec((CHUNK, own, hidden), lambda j: (j, 0, 0))
    return pl.pallas_call(
        adam_experts_kernel,
        grid=(experts // CHUNK,),
        in_specs=[smem_spec(), share, share] + [big] * 3 + [small] * 3,
        out_specs=[big] * 3 + [small] * 3,
        out_shape=[jax.ShapeDtypeStruct(gateup[0].shape, F32)] * 3
        + [jax.ShapeDtypeStruct(down[0].shape, F32)] * 3,
        compiler_params=pltpu.CompilerParams(vmem_limit_bytes=VMEM_BYTES),
        name="adam_experts",
    )(x_at, kept, got, *gateup, *down)


def join_tokens_kernel(own, first, second, out, turned):
    half = own.shape[0] // 2
    for at, part in ((0, own[:half, :]), (half, own[half:, :]), (2 * half, first[...]), (3 * half, second[...])):
        out[at : at + half, :] = part
        turned[:, at : at + half] = part.T


def join_tokens(own, first, second, *earlier):
    tokens, width = own.shape
    return pl.pallas_call(
        with_earlier(join_tokens_kernel, 3, len(earlier)),
        in_specs=[vmem_spec()] * 3 + any_specs(earlier),
        out_specs=[vmem_spec()] * 2,
        out_shape=[
            jax.ShapeDtypeStruct((2 * tokens, width), own.dtype),
            jax.ShapeDtypeStruct((width, 2 * tokens), own.dtype),
        ],
        compiler_params=pltpu.CompilerParams(vmem_limit_bytes=VMEM_BYTES),
        name="join_tokens",
    )(own, first, second, *earlier)


def move(array, dz=0, dy=0, dx=0):
    total = lax.axis_size("dp")
    inner = total // 16
    pairs = []
    for at in range(16):
        z, y, x = at // 4, at // 2 % 2, at % 2
        to = ((z + dz) % 4) * 4 + (y ^ dy) * 2 + (x ^ dx)
        pairs += [(at * inner + i, to * inner + i) for i in range(inner)]
    return lax.ppermute(array, "dp", pairs)


def place():
    at = lax.axis_index("dp") // (lax.axis_size("dp") // 16)
    return at // 4, at // 2 % 2, at % 2


def inner_groups(total):
    inner = total // 16
    return [[at * inner + i for i in range(inner)] for at in range(16)]


def inner_gather(shard, axis):
    total = lax.axis_size("dp")
    if total == 16:
        return shard
    return lax.all_gather(
        shard, "dp", axis=axis, tiled=True, axis_index_groups=inner_groups(total)
    )


def inner_scatter(share, axis):
    total = lax.axis_size("dp")
    if total == 16:
        return share
    return lax.psum_scatter(
        share, "dp", scatter_dimension=axis, tiled=True, axis_index_groups=inner_groups(total)
    )


def block_rows(parts, rows):
    z, y, x = place()
    starts = []
    for dz, dy, dx in parts:
        starts.append((((z + dz + 4) % 4) * 4 + (y ^ dy) * 2 + (x ^ dx)) * rows)
    return jnp.stack(starts).astype(jnp.int32)


def gather_z(shard):
    return jnp.stack([shard] + [move(shard, dz=-dz) for dz in Z_FROM[1:]])


def gather_ring(shard):
    below, above = move(shard, dz=1), move(shard, dz=-1)
    return [shard, below, above, move(below, dz=1)]


def send_z(parts):
    return [move(parts[k].astype(BF16), dz=Z_FROM[k]) for k in range(1, SLOTS)]


def scatter_z(parts, moved=None):
    result = parts[0]
    for one in moved or send_z(parts):
        result = result + one.astype(F32)
    return result


def gather_plane(own):
    half = own.shape[-1] // 2
    along_y, along_x = move(own, dy=1), move(own, dx=1)
    both = (move(along_y[..., :half], dx=1), move(along_x[..., half:], dy=1))
    return own, along_y, along_x, *both


def scatter_plane(pieces):
    own, along_y, along_x, both_one, both_two = pieces
    half = both_one.shape[-1]
    got_one, got_two = move(both_one, dx=1), move(both_two, dy=1)
    pass_y = jnp.concatenate(
        [(along_y[..., :half].astype(F32) + got_one.astype(F32)).astype(BF16), along_y[..., half:]],
        axis=-1,
    )
    pass_x = jnp.concatenate(
        [along_x[..., :half], (along_x[..., half:].astype(F32) + got_two.astype(F32)).astype(BF16)],
        axis=-1,
    )
    got_y, got_x = move(pass_y, dy=1), move(pass_x, dx=1)
    return scatter_z(
        [
            own[k].astype(F32) + got_y[k].astype(F32) + got_x[k].astype(F32)
            for k in range(SLOTS)
        ]
    )


PLANE = [(dz, dy, dx) for dy, dx in ((0, 0), (1, 0), (0, 1), (1, 1)) for dz in Z_FROM]


def join_kernel(rows_at, *refs):
    pieces, out = refs[:-1], refs[-1]
    slots, own, width = pieces[0].shape
    half = width // 2
    for at in range(4 * slots):
        rows = pl.ds(pl.multiple_of(rows_at[at], own), own)
        group, slot = at // slots, at % slots
        if group < 3:
            out[rows, :] = pieces[group][slot]
        else:
            out[rows, :half] = pieces[3][slot]
            out[rows, half:] = pieces[4][slot]


def part_kernel(rows_at, whole, *pieces):
    slots, own, width = pieces[0].shape
    half = width // 2
    for at in range(4 * slots):
        rows = pl.ds(pl.multiple_of(rows_at[at], own), own)
        group, slot = at // slots, at % slots
        if group < 3:
            pieces[group][slot] = whole[rows, :]
        else:
            pieces[3][slot] = whole[rows, :half]
            pieces[4][slot] = whole[rows, half:]


def smem_spec():
    return pl.BlockSpec(memory_space=pltpu.SMEM)


def vmem_spec():
    return pl.BlockSpec(memory_space=pltpu.VMEM)


def join_blocks(rows_at, pieces, earlier=()):
    slots, own, width = pieces[0].shape
    return pl.pallas_call(
        with_earlier(join_kernel, 6, len(earlier)),
        in_specs=[smem_spec()] + [vmem_spec()] * 5 + any_specs(earlier),
        out_specs=vmem_spec(),
        out_shape=jax.ShapeDtypeStruct((4 * slots * own, width), BF16),
        compiler_params=pltpu.CompilerParams(vmem_limit_bytes=VMEM_BYTES),
        name="join_blocks",
    )(rows_at, *pieces, *earlier)


def part_blocks(rows_at, whole, earlier=()):
    own, width = whole.shape[0] // (4 * SLOTS), whole.shape[1]
    full = jax.ShapeDtypeStruct((SLOTS, own, width), BF16)
    half = jax.ShapeDtypeStruct((SLOTS, own, width // 2), BF16)
    return pl.pallas_call(
        with_earlier(part_kernel, 2, len(earlier)),
        in_specs=[smem_spec(), vmem_spec()] + any_specs(earlier),
        out_specs=[vmem_spec()] * 5,
        out_shape=[full] * 3 + [half] * 2,
        compiler_params=pltpu.CompilerParams(vmem_limit_bytes=VMEM_BYTES),
        name="part_blocks",
    )(rows_at, whole, *earlier)


def after(value, *earlier):
    marks = []
    for one in earlier:
        slots = one.shape[0] if one.shape[0] == SLOTS else 1
        lead, rest = (slots > 1) * 1, one.ndim - 1
        marks.append(lax.slice(one, (lead,) + (0,) * rest, (slots,) + (1,) * rest))
    return lax.optimization_barrier((value, *marks))[0]


def split_three(values):
    high = values.astype(BF16)
    rest = values - high.astype(F32)
    middle = rest.astype(BF16)
    low = (rest - middle.astype(F32)).astype(BF16)
    return [high, middle, low]


def swap_cores(part):
    return lax.ppermute(part, "tensor", [(0, 1), (1, 0)])


def pair_sum(part):
    return part.astype(F32) + swap_cores(part).astype(F32)


def norm_backward(values, inverse, gain_row, upstream):
    scaled = values * inverse
    weighted = upstream * gain_row
    mean_term = jnp.mean(weighted * scaled, axis=-1, keepdims=True)
    return (inverse * (weighted - scaled * mean_term), jnp.sum(upstream * scaled, axis=0))


def adam_update(value, gradient, mean_old, square_old, rate, decay):
    mean_new = FIRST_DECAY * mean_old + (1.0 - FIRST_DECAY) * gradient
    square_new = SECOND_DECAY * square_old + (1.0 - SECOND_DECAY) * gradient * gradient
    mean_hat = mean_new / (1.0 - FIRST_DECAY**STEP)
    square_hat = square_new / (1.0 - SECOND_DECAY**STEP)
    updated = value - rate * (mean_hat / (jnp.sqrt(square_hat) + ADAM_EPSILON) + decay * value)
    return (mean_new, square_new, updated)


def shards(
    hidden_in,
    out_grad,
    routes,
    segments,
    norm_gains,
    gains_mean,
    gains_square,
    w_query,
    query_mean,
    query_square,
    key_value_weight,
    key_value_first_moment,
    key_value_second_moment,
    w_out,
    out_mean,
    out_square,
    w_router,
    router_mean,
    router_square,
    w_gateup,
    gateup_mean,
    gateup_square,
    w_down,
    down_mean,
    down_square,
):
    tokens, width = hidden_in.shape
    own = w_query.shape[0]
    experts, hidden = w_down.shape[0], w_down.shape[1]
    q_width, kv_width = w_query.shape[1], key_value_weight.shape[2]
    qkv_width = q_width + 2 * kv_width
    each = 2 + experts
    half_experts = experts // 2
    block = width // 16
    z_at, y_at, x_at = place()
    core = lax.axis_index("tensor")
    plane_rows = block_rows(PLANE, block)
    turned_down = [one.transpose(0, 2, 1) for one in (w_down, down_mean, down_square)]
    gateup_rows, down_rows = w_gateup, turned_down[0]
    if lax.axis_size("dp") > 16:
        gateup_rows = inner_gather(w_gateup.astype(BF16), 2)
        down_rows = inner_gather(down_rows.astype(BF16), 1)
    chunks = experts // (2 * CHUNK)
    first = x_at == 0
    half_width = HEAD_DIM // 2
    frequency = ROPE_BASE ** (-2.0 * jnp.arange(half_width, dtype=F32) / HEAD_DIM)
    frequency = jnp.concatenate([frequency] * 4)[None, :]
    turned_out = [one.T for one in (w_out, out_mean, out_square)]
    weights = (
        inner_gather(w_query, 0), inner_gather(key_value_weight, 1),
        inner_gather(turned_out[0], 0), inner_gather(w_router, 0), inner_gather(norm_gains, 1),
    )
    (
        small, combine, combine_pair, seg_col,
        qkv_blocks, out_blocks, normed_low, queries, keys, values, attended, lse, cosine, sine,
        middle, x_pair, x_turned, og_pair, og_turned, pairs, near, far,
    ) = forward_pass(
        weights, frequency, segments, routes, gateup_rows, down_rows, hidden_in, out_grad
    )
    dx, mix_pair, gate_turned, keep, z_got, near_grads, far_grads = experts_pass(
        x_pair, og_pair, x_turned, og_turned, combine_pair, pairs, near, far
    )
    qkv_share, output_share, input_grad, block_out, kept_share, got_share = backward_pass(
        out_blocks, queries, keys, values, attended, lse, cosine, sine, seg_col, segments, small,
        combine, gate_turned, qkv_blocks, normed_low, hidden_in, out_grad, middle, dx, mix_pair, keep,
        z_got, near_grads, far_grads,
    )[:6]
    kept_share, got_share = inner_scatter(kept_share, 1), inner_scatter(got_share, 1)
    x_here = x_at.astype(jnp.int32)[None]
    output_share = inner_scatter(output_share, 0)
    qkv_share = inner_scatter(qkv_share, 0)
    *attention_results, gain_one_part = adam_attention(
        qkv_share, output_share,
        [
            w_query, query_mean, query_square, key_value_weight, key_value_first_moment,
            key_value_second_moment, *turned_out,
        ],
    )
    gain_one_share = pair_sum(gain_one_part.T) / norm_gains[:1]
    gains_share = jnp.concatenate([gain_one_share, qkv_share[:, qkv_width][None, :]])
    router_share = qkv_share[:, qkv_width + 1 : qkv_width + 1 + experts]

    gains_result = adam_update(norm_gains, gains_share, gains_mean, gains_square, GAIN_RATE, 0.0)
    router_result = adam_update(
        w_router, router_share, router_mean, router_square, (4 * MODEL_DIM) ** (-0.5), WEIGHT_DECAY
    )
    expert_results = adam_experts(
        x_here, kept_share, got_share,
        (w_gateup, gateup_mean, gateup_square), turned_down,
    )
    expert_results = [*expert_results[:3], *(one.transpose(0, 2, 1) for one in expert_results[3:])]
    return (
        (block_out, input_grad)
        + gains_result
        + tuple(attention_results[:6])
        + tuple(one.T for one in attention_results[6:])
        + router_result
        + tuple(expert_results)
    )


def solution(mesh):
    tokens, gains = P("dp", None), P(None, "dp")
    query, keyval, out = P("dp", "tensor"), P(None, "dp", "tensor"), P("tensor", "dp")
    router, gateup, down = P("dp", None), P(None, None, "dp", "tensor"), P(None, "tensor", "dp")
    states = tuple(
        spec for one in (gains, query, keyval, out, router, gateup, down) for spec in (one,) * 3
    )
    return jax.shard_map(
        shards,
        mesh=mesh,
        in_specs=(tokens, tokens, tokens, P("dp")) + states,
        out_specs=(tokens, tokens) + states,
        check_vma=False,
    )
```

```python
import functools

import jax
import jax.numpy as jnp
from jax import lax
from jax.experimental import pallas as pl
from jax.experimental.pallas import tpu as pltpu
from jax.sharding import PartitionSpec as P

MODEL_DIM = 1536
QUERY_HEADS = 24
HEAD_DIM = 64
F = 512
STEP = 10

NORM_EPSILON = 1e-06
SCORE_SCALE = 0.015625
RESIDUAL_SCALE = 0.22
ROPE_BASE = 10000.0
FIRST_DECAY = 0.9
SECOND_DECAY = 0.95
ADAM_EPSILON = 1e-08
WEIGHT_DECAY = 0.1
GAIN_RATE = 0.6
MASK_VALUE = -1e30

BF16 = jnp.bfloat16
F32 = jnp.float32
LANES = 128
ROWS = 256
VMEM_BYTES = 58 * 1024 * 1024

NN = (((1,), (0,)), ((), ()))
NT = (((1,), (1,)), ((), ()))
TN = (((0,), (0,)), ((), ()))


def dot(a, b, dims=NN):
    return lax.dot_general(a, b, dims, preferred_element_type=F32)


def rotate_halves(slab):
    lane = lax.broadcasted_iota(jnp.int32, slab.shape, 1)
    ahead = pltpu.roll(slab, LANES - HEAD_DIM // 2, 1)
    behind = pltpu.roll(slab, HEAD_DIM // 2, 1)
    return jnp.where(lane % HEAD_DIM < HEAD_DIM // 2, ahead, behind)


def few_rows(count, base=None):
    for r in range(0, count, 16):
        yield pl.ds(r, 16) if base is None else pl.ds(pl.multiple_of(base + r, 16), 16)


def half_mask(rows, upper):
    lane = lax.broadcasted_iota(jnp.int32, (rows, LANES), 1)
    return (lane >= HEAD_DIM) if upper else (lane < HEAD_DIM)


def spread_heads(slab, lower_out, upper_out, index):
    rows = slab.shape[0]
    moved = pltpu.roll(slab.astype(F32), HEAD_DIM, 1).astype(BF16)
    zero = jnp.zeros_like(slab)
    low, high = half_mask(rows, False), half_mask(rows, True)
    lower_out[index] = jnp.where(low, slab, zero)
    upper_out[index] = jnp.where(high, moved, zero)
    lower_out[index + 1] = jnp.where(low, moved, zero)
    upper_out[index + 1] = jnp.where(high, slab, zero)


def fill_bias(bias, seg_col, seg_row):
    span = bias.shape[0]
    for at in range(0, span, ROWS):
        rows_at = at + lax.broadcasted_iota(jnp.int32, (ROWS, span), 0)
        cols_at = lax.broadcasted_iota(jnp.int32, (ROWS, span), 1)
        allowed = (rows_at >= cols_at) & (seg_col[at : at + ROWS, :] == seg_row[...])
        bias[at : at + ROWS, :] = jnp.where(allowed, 0.0, MASK_VALUE).astype(F32)


def with_earlier(kernel, inputs, count):
    def run(*refs):
        kernel(*refs[:inputs], *refs[inputs + count :])

    return run


def any_specs(arrays):
    return [pl.BlockSpec(memory_space=pl.ANY)] * len(arrays)


EXPERT_ROWS = 256
EXPERT_VMEM = 63 * 1024 * 1024
SLOTS = 4
Z_FROM = (0, -1, 1, 2)
CHUNK = 2
LATE = 2
SENT = 2
MESH_ID = pl.DeviceIdType.MESH


def experts_kernel(
    inner, chunks, row_steps, x_ref, og_ref, xt_ref, ogt_ref, combine_ref,
    pairs_ref, near_ref, far_ref,
    dx_own, dx_twin, dx_other, mix_out, gate_out, *refs,
):
    keep_outs, refs = refs[:SENT], refs[SENT:]
    part_outs, refs = refs[:SENT], refs[SENT:]
    near_outs, refs = refs[: chunks - SENT], refs[chunks - SENT :]
    late_out, first_out, far_out, refs = *refs[:3], refs[3:]
    slots, arrived, held_both, held_down, dx_sum, mix_sum, twin_rows, twin_mix = refs[:8]
    gates, gate_kept, gate_got, gate_full, gate_twin, send, recv, local = refs[8:]
    weights, grads = slots.at[pl.ds(1, chunks)], slots
    near = Neighbours(inner)
    copies = Copies(send, recv, local)
    z, y, x, core, spots = near.z, near.y, near.x, near.core, near.spots
    step = pl.program_id(0)
    steps = row_steps + SLOTS
    chunk, turn = step // steps, step % steps
    last = chunks - 1
    width = x_ref.shape[1]
    block = width // 16
    hidden = held_down.shape[1] // CHUNK
    both = 2 * hidden * CHUNK
    lane = lax.broadcasted_iota(jnp.int32, (EXPERT_ROWS, LANES), 1)
    tokens = dx_sum.shape[0] // 2
    tiles = tokens // EXPERT_ROWS
    tile = (turn + tiles) % row_steps
    rows = pl.ds(pl.multiple_of(tile * EXPERT_ROWS, EXPERT_ROWS), EXPERT_ROWS)

    def near_piece(c, k):
        return pairs_ref.at[c] if k == 0 else near_ref.at[c, k - 1]

    def near_copy(c, k):
        copies.copy(
            lambda c=c, k=k: (near_piece(c, k), weights.at[c, spots[k], y]), ("near", c, k), False
        )

    def near_wait(c, k):
        copies.wait_copy(
            lambda c=c, k=k: (near_piece(c, k), weights.at[c, spots[k], y]), ("near", c, k)
        )

    def far_ends(c, k):
        return far_ref.at[c, k], weights.at[c, spots[k], 1 - y]

    @pl.when(step == 0)
    def _():
        near.greet()
        gates[...] = jnp.zeros_like(gates)
        for k in range(SLOTS):
            near_copy(0, k)
            copies.copy(lambda k=k: far_ends(0, k), ("far", 0, k), False)
        copies.remote(
            lambda: (pairs_ref.at[last], weights.at[last, z, y]), ("y",), ("y",), near.over_y
        )
        for k in range(1, SLOTS):
            copies.remote(
                lambda: (pairs_ref.at[last], weights.at[last, z, y]),
                ("z", k), ("z", BACK[k]), near.along[k],
            )
        for c in range(LATE, last):
            for k in range(1, SLOTS):
                copies.remote(
                    lambda c=c, k=k: (near_piece(c, k), weights.at[c, spots[k], y]),
                    ("f", c, k), ("f", c, k), near.over_y,
                )
        for c in range(1, chunks):
            for k in range(SLOTS if c < last else 1):
                near_copy(c, k)
                if c < LATE or (c < last and k == 0):
                    copies.copy(lambda c=c, k=k: far_ends(c, k), ("far", c, k), False)

    @pl.when(step == steps)
    def _():
        copies.arrived(weights.at[last, z, 1 - y], ("y",), near.over_y)
        for k in range(1, SLOTS):
            copies.remote(
                lambda: (weights.at[last, z, 1 - y],) * 2,
                ("z2", k), ("z2", BACK[k]), near.along[k],
            )

    for c in range(chunks):

        @pl.when(step == c * steps)
        def _():
            for k in range(SLOTS):
                if c < last or k == 0:
                    near_wait(c, k)
                if c < LATE or (c < last and k == 0):
                    copies.wait_copy(lambda c=c, k=k: far_ends(c, k), ("far", c, k))
                elif c < last:
                    copies.arrived(weights.at[c, spots[k], 1 - y], ("f", c, k), near.over_y)
                elif k > 0:
                    copies.arrived(weights.at[c, spots[k], y], ("z", k), near.along[k])
                    copies.arrived(weights.at[c, spots[k], 1 - y], ("z2", k), near.along[k])

    def add_arrived(c):
        copies.arrived(arrived.at[c], ("sum", c), near.over_y)
        for k in range(SLOTS):
            own = grads.at[c, spots[k], y]
            for here in few_rows(own.shape[0]):
                own[here, :] = (
                    own[here, :].astype(F32) + arrived[c, spots[k], here, :].astype(F32)
                ).astype(BF16)
        copies.copy(lambda c=c: (grads.at[c, z, y], keep_outs[c]), ("keep", c))
        for k in range(1, SLOTS):
            copies.remote(
                lambda c=c, k=k: (grads.at[c, spots[k], y], part_outs[c].at[BACK[k] - 1]),
                ("part", c, k), ("part", c, BACK[k]), near.along[k],
            )

    @pl.when(step == 2 * steps + 1)
    def _():
        add_arrived(0)

    @pl.when(step == 3 * steps + 2)
    def _():
        add_arrived(1)

    @pl.when(turn < row_steps)
    def _():
        for e in range(CHUNK):
            first = 2 * hidden * e
            w_both = weights[chunk, :, :, :, first : first + 2 * hidden].reshape(width, 2 * hidden)
            start = both + hidden * e
            w_down = weights[chunk, :, :, :, start : start + hidden].reshape(width, hidden)
            gate_up = dot(x_ref[...], w_both)
            raw = dot(og_ref[...], w_down) * RESIDUAL_SCALE
            gate, up = gate_up[:, :hidden], gate_up[:, hidden:]
            gate_lane = lax.broadcasted_iota(
                jnp.int32, (EXPERT_ROWS, combine_ref.shape[1]), 1
            )
            column = jnp.sum(
                jnp.where(gate_lane == chunk * CHUNK + e, combine_ref[...], 0.0),
                axis=1, keepdims=True,
            )
            sigmoid = 1.0 / (1.0 + jnp.exp(-gate))
            active = gate * sigmoid
            inner_value = (active * up).astype(BF16).astype(F32)
            held_down[rows, hidden * e : hidden * (e + 1)] = (inner_value * column).astype(BF16)
            gates[rows, :] = jnp.where(
                lane == chunk * CHUNK + e,
                jnp.sum(inner_value * raw, axis=1, keepdims=True),
                gates[rows, :],
            )
            inner_grad = raw * column
            held_both[rows, first : first + hidden] = (
                inner_grad * up * sigmoid * (1.0 + gate * (1.0 - sigmoid))
            ).astype(BF16)
            held_both[rows, first + hidden : first + 2 * hidden] = (inner_grad * active).astype(BF16)

        def sums(add):
            for part in range(SLOTS):
                cols = slice(4 * block * part, 4 * block * (part + 1))
                w_both = weights[chunk, part, :, :, :both].reshape(4 * block, both)
                w_down = weights[chunk, part, :, :, both:].reshape(4 * block, hidden * CHUNK)
                mix = dot(held_down[rows, :], w_down, NT)
                dx = dot(held_both[rows, :], w_both, NT)
                if add:
                    mix = mix + mix_sum[rows, cols].astype(F32)
                    dx = dx + dx_sum[rows, cols].astype(F32)
                mix_sum[rows, cols] = mix.astype(BF16)
                dx_sum[rows, cols] = dx.astype(BF16)

        @pl.when(chunk == 0)
        def _():
            sums(False)

        @pl.when(chunk > 0)
        def _():
            sums(True)

    @pl.when(turn >= row_steps)
    def _():
        part = turn - row_steps
        grads[chunk, part, :, :, :both] = (
            dot(xt_ref[...], held_both[...]).astype(BF16).reshape(2, 2 * block, both)
        )
        grads[chunk, part, :, :, both:] = (
            (dot(ogt_ref[...], held_down[...]) * RESIDUAL_SCALE)
            .astype(BF16)
            .reshape(2, 2 * block, hidden * CHUNK)
        )

    begin = last * steps
    for i in range(2):
        for c in range(2):
            mine = pl.ds(tokens + (2 * c + i) * EXPERT_ROWS, EXPERT_ROWS)
            there = pl.ds((2 * c + i) * EXPERT_ROWS, EXPERT_ROWS)

            @pl.when((step == begin + 2 * c + i) & (core != c))
            def _():
                for name, total, got in (("t", dx_sum, twin_rows), ("mt", mix_sum, twin_mix)):
                    copies.remote(
                        lambda: (total.at[mine], got.at[i]), (name, i), (name, i), near.twin,
                        last=False,
                    )

            @pl.when((step == begin + 2 + 2 * c + i) & (core == c))
            def _():
                for name, total, got in (("t", dx_sum, twin_rows), ("mt", mix_sum, twin_mix)):
                    copies.arrived(got.at[i], (name, i), near.twin)
                    for here in few_rows(EXPERT_ROWS):
                        at = pl.ds(mine.start + here.start, 16)
                        total[at, :] = (
                            total[at, :].astype(F32) + got[i, here, :].astype(F32)
                        ).astype(BF16)
                copies.remote(
                    lambda: (dx_sum.at[mine], dx_other.at[there]), ("o", i), ("o", i), near.over_x,
                    last=False,
                )

            @pl.when((step == begin + steps - 2 + i) & (core == c))
            def _():
                copies.arrived(dx_other.at[there], ("o", i), near.over_x)
                copies.remote(
                    lambda: (dx_other.at[there],) * 2, ("o2", i), ("o2", i), near.twin, last=False
                )

    for i in range(tiles):

        @pl.when(step == begin + tiles + i)
        def _():
            own = pl.ds(i * EXPERT_ROWS, EXPERT_ROWS)
            copies.copy(lambda own=own: (dx_sum.at[own], dx_own.at[own]), ("own", i))
            copies.remote(
                lambda own=own: (dx_sum.at[own], dx_twin.at[own]), ("own", i), ("own", i), near.twin
            )

    shares = gate_kept.shape[0]

    @pl.when(step == begin + row_steps)
    def _():
        copies.copy(lambda: (mix_sum, mix_out), "mix")
        turned = gates[...].T[:shares, :]
        gate_kept[...] = turned
        copies.remote(
            lambda: (gate_kept.at[:, pl.ds(tokens, tokens)], gate_got), ("g",), ("g",), near.over_x
        )

    @pl.when(step == begin + steps - 2)
    def _():
        copies.arrived(gate_got, ("g",), near.over_x)
        gate_full[pl.ds(pl.multiple_of(x * shares, shares), shares), :] = gate_kept[:, :tokens]
        gate_full[pl.ds(pl.multiple_of((1 - x) * shares, shares), shares), :] = gate_got[...]
        copies.remote(lambda: (gate_full, gate_twin), ("g2",), ("g2",), near.twin)

    for c in range(chunks):

        @pl.when(step == (c + 1) * steps - 1)
        def _():
            if c < SENT:
                copies.remote(
                    lambda c=c: (grads.at[c, :, 1 - y], arrived.at[c]),
                    ("sum", c), ("sum", c), near.over_y,
                )
            else:
                for k in range(SLOTS):
                    copies.copy(
                        lambda c=c, k=k: (grads.at[c, spots[k], y], near_outs[c - SENT].at[k]),
                        ("near out", c, k),
                    )
                    if c < last and k == 0:
                        copies.copy(lambda c=c: (grads.at[c, z, 1 - y], first_out), "first out")
                    elif c < last:
                        copies.remote(
                            lambda c=c, k=k: (grads.at[c, spots[k], 1 - y], late_out.at[k - 1]),
                            ("late", k), ("late", k), near.over_y,
                        )
                    else:
                        copies.copy(
                            lambda c=c, k=k: (grads.at[c, spots[k], 1 - y], far_out.at[k]),
                            ("far out", k),
                        )

    @pl.when(step == chunks * steps - 1)
    def _():
        copies.arrived(gate_twin, ("g2",), near.twin)
        gate_out[...] = gate_full[...] + gate_twin[...]
        for i in range(tiles):
            copies.arrived(
                dx_twin.at[pl.ds(i * EXPERT_ROWS, EXPERT_ROWS)], ("own", i), near.twin
            )
        for i in range(2):
            for c in range(2):
                mine = pl.ds(tokens + (2 * c + i) * EXPERT_ROWS, EXPERT_ROWS)
                there = pl.ds((2 * c + i) * EXPERT_ROWS, EXPERT_ROWS)

                @pl.when(core != c)
                def _():
                    copies.sent(lambda: (dx_sum.at[mine], twin_rows.at[i]), ("t", i), near.twin)
                    copies.sent(lambda: (mix_sum.at[mine], twin_mix.at[i]), ("mt", i), near.twin)
                    copies.arrived(dx_other.at[there], ("o2", i), near.twin)

                @pl.when(core == c)
                def _():
                    copies.sent(
                        lambda: (dx_sum.at[mine], dx_other.at[there]), ("o", i), near.over_x
                    )
                    copies.sent(lambda: (dx_other.at[there],) * 2, ("o2", i), near.twin)

        for c in range(SENT):
            for k in range(1, SLOTS):
                copies.arrived(part_outs[c].at[k - 1], ("part", c, k), near.along[k])
        for k in range(1, SLOTS):
            copies.arrived(late_out.at[k - 1], ("late", k), near.over_y)
        copies.finish()


def experts_pass(x, og, xt, ogt, combine, pairs, near, far):
    tokens, width = x.shape
    chunks, pair, columns = pairs.shape
    hidden = columns // (3 * CHUNK)
    shares = chunks * CHUNK
    row_steps = tokens // EXPERT_ROWS
    steps = row_steps + SLOTS
    inner = lax.axis_size("dp") // 16
    row_at = lambda s: ((jnp.minimum(s % steps, row_steps - 1) + row_steps // 2) % row_steps, 0)
    width_at = lambda s: (jnp.maximum(s % steps - row_steps, 0), 0)
    row = pl.BlockSpec((EXPERT_ROWS, width), row_at)
    turned = pl.BlockSpec((width // SLOTS, tokens), width_at)
    anywhere = pl.BlockSpec(memory_space=pl.ANY)
    left = chunks - SENT
    dma = pltpu.SemaphoreType.DMA
    shape = jax.ShapeDtypeStruct
    outs = pl.pallas_call(
        functools.partial(experts_kernel, inner, chunks, row_steps),
        grid=(chunks * steps,),
        in_specs=[row, row, turned, turned, pl.BlockSpec((EXPERT_ROWS, combine.shape[1]), row_at)]
        + [anywhere] * 3,
        out_specs=[anywhere] * 4
        + [pl.BlockSpec((2 * shares, tokens // 2), lambda s: (0, 0))]
        + [anywhere] * (2 * SENT + left + 3),
        out_shape=[shape((tokens // 2, width), BF16)] * 3
        + [shape((tokens, width), BF16), shape((2 * shares, tokens // 2), F32)]
        + [shape((pair, columns), BF16)] * SENT
        + [shape((SLOTS - 1, pair, columns), BF16)] * SENT
        + [shape((SLOTS, pair, columns), BF16)] * left
        + [shape((SLOTS - 1, pair, columns), BF16), shape((pair, columns), BF16)]
        + [shape((SLOTS, pair, columns), BF16)],
        scratch_shapes=[
            pltpu.VMEM((chunks + 1, SLOTS, 2, pair, columns), BF16),
            pltpu.VMEM((SENT, SLOTS, pair, columns), BF16),
            pltpu.VMEM((tokens, 2 * hidden * CHUNK), BF16),
            pltpu.VMEM((tokens, hidden * CHUNK), BF16),
            pltpu.VMEM((tokens, width), BF16),
            pltpu.VMEM((tokens, width), BF16),
            pltpu.VMEM((2, EXPERT_ROWS, width), BF16),
            pltpu.VMEM((2, EXPERT_ROWS, width), BF16),
            pltpu.VMEM((tokens, LANES), F32),
            pltpu.VMEM((shares, tokens), F32),
            pltpu.VMEM((shares, tokens // 2), F32),
            pltpu.VMEM((2 * shares, tokens // 2), F32),
            pltpu.VMEM((2 * shares, tokens // 2), F32),
            dma((48,)), dma((48,)), dma((48,)),
        ],
        compiler_params=pltpu.CompilerParams(
            vmem_limit_bytes=EXPERT_VMEM, collective_id=0, has_side_effects=True
        ),
        cost_estimate=pl.CostEstimate(
            flops=8 * tokens * width * chunks * columns,
            bytes_accessed=2 * chunks * width * columns, transcendentals=0,
        ),
        name="experts_pass",
    )(x, og, xt, ogt, combine, pairs, near, far)
    dx, mix, gate = outs[:3], outs[3], outs[4]
    rest = outs[5:]
    keep, parts, rest = rest[:SENT], rest[SENT : 2 * SENT], rest[2 * SENT :]
    return dx, mix, gate, keep, parts, rest[:left], rest[left:]


class Copies:
    def __init__(self, send, recv, local):
        self.send, self.recv, self.local = send, recv, local
        self.sends, self.recvs, self.locals, self.started = {}, {}, {}, []

    def remote(self, ends, name, arrives, device, last=True):
        sent = self.sends.setdefault(name, len(self.sends))
        got = self.recvs.setdefault(arrives, len(self.recvs))

        def make():
            source, target = ends()
            return pltpu.make_async_remote_copy(
                source, target, self.send.at[sent], self.recv.at[got],
                device_id=device, device_id_type=MESH_ID,
            )

        make().start()
        if last:
            self.started.append(lambda: make().wait_send())

    def sent(self, ends, name, device):
        source, target = ends()
        pltpu.make_async_remote_copy(
            source, target, self.send.at[self.sends[name]], self.recv.at[0],
            device_id=device, device_id_type=MESH_ID,
        ).wait_send()

    def arrived(self, place, name, device):
        got = self.recvs.setdefault(name, len(self.recvs))
        pltpu.make_async_remote_copy(
            place, place, self.send.at[0], self.recv.at[got],
            device_id=device, device_id_type=MESH_ID,
        ).wait_recv()

    def copy(self, ends, name, wait_last=True):
        at = self.locals.setdefault(name, len(self.locals))

        def make():
            return pltpu.make_async_copy(*ends(), self.local.at[at])

        make().start()
        if wait_last:
            self.started.append(lambda: make().wait())
        return lambda: make().wait()

    def wait_copy(self, ends, name):
        pltpu.make_async_copy(*ends(), self.local.at[self.locals[name]]).wait()

    def finish(self):
        for wait in self.started:
            wait()


class Neighbours:
    def __init__(self, inner):
        me = lax.axis_index("dp")
        at = me // inner
        self.core = lax.axis_index("tensor")
        self.z, self.y, self.x = at // 4, at // 2 % 2, at % 2
        self.spots = [(self.z + dz + 4) % 4 for dz in Z_FROM]
        self.along = [{"dp": me + (spot - self.z) * 4 * inner} for spot in self.spots]
        self.over_y = {"dp": me + (1 - 2 * self.y) * 2 * inner}
        self.over_x = {"dp": me + (1 - 2 * self.x) * inner}
        self.twin = {"tensor": 1 - self.core}
        self.blocks = {
            (k, other_y, other_x): self.spots[k] * 4
            + (1 - self.y if other_y else self.y) * 2
            + (1 - self.x if other_x else self.x)
            for k in range(SLOTS)
            for other_y in (0, 1)
            for other_x in (0, 1)
        }

    def greet(self):
        barrier = pltpu.get_barrier_semaphore()
        devices = [*self.along[1:], self.over_y, self.over_x, self.twin]
        for device in devices:
            pl.semaphore_signal(barrier, inc=1, device_id=device, device_id_type=MESH_ID)
        pl.semaphore_wait(barrier, len(devices))

    def block(self, k, other_y, other_x):
        return self.blocks[k, other_y, other_x]


BACK = (0, 2, 1, 3)


class Gather:
    def __init__(self, copies, near, shard, full, tag):
        self.copies, self.near, self.shard, self.full, self.tag = copies, near, shard, full, tag
        self.split = full.shape[2] // (2 * LANES) * LANES

    def source(self, k):
        return self.shard if k == 0 else self.full.at[self.near.block(k, 0, 0)]

    def begin(self):
        for k in range(1, SLOTS):
            self.copies.remote(
                lambda: (self.shard, self.full.at[self.near.block(0, 0, 0)]),
                (self.tag, "z", k), (self.tag, "z", BACK[k]), self.near.along[k],
            )
        self.full[self.near.block(0, 0, 0)] = self.shard[...]

    def spread(self, k):
        near, place = self.near, self.full.at[self.near.block(k, 0, 0)]
        if k > 0:
            self.copies.arrived(place, (self.tag, "z", k), near.along[k])
        for way, device in (("y", near.over_y), ("x", near.over_x)):
            name = (self.tag, way, k)
            self.copies.remote(
                lambda: (self.source(k), self.full.at[near.block(k, 0, 0)]), name, name, device
            )

    def cross(self, k):
        near = self.near
        from_y = self.full.at[near.block(k, 1, 0)]
        from_x = self.full.at[near.block(k, 0, 1)]
        self.copies.arrived(from_y, (self.tag, "y", k), near.over_y)
        self.copies.remote(
            lambda: (self.full.at[near.block(k, 1, 0), :, : self.split],) * 2,
            (self.tag, "one", k), (self.tag, "one", k), near.over_x,
        )
        self.copies.arrived(from_x, (self.tag, "x", k), near.over_x)
        self.copies.remote(
            lambda: (self.full.at[near.block(k, 0, 1), :, self.split :],) * 2,
            (self.tag, "two", k), (self.tag, "two", k), near.over_y,
        )

    def end(self):
        near = self.near
        for k in range(SLOTS):
            place = self.full.at[near.block(k, 1, 1)]
            self.copies.arrived(place.at[:, : self.split], (self.tag, "one", k), near.over_x)
            self.copies.arrived(place.at[:, self.split :], (self.tag, "two", k), near.over_y)


def roll_left(slab, lanes):
    return pltpu.roll(slab, LANES - lanes, 1)


def forward_kernel(
    inner, w_query, w_keyval, w_out, w_router, gains, frequency, seg_row, routes,
    gateup_hbm, down_hbm, hidden_hbm, og_hbm,
    small, combine, combine_pair, seg_col,
    q_full_out, o_full_out, normed_out, q_out, k_out, v_out, attended_out, lse_out, cos_out, sin_out,
    middle_hbm, x_hbm, xt_hbm, og_pair, ogt_hbm, pairs_hbm, near_hbm, far_hbm,
    hidden, gateup, down, given, pairs, bias, k_low, k_high, v_low, v_high, part, part_got, x_own, x_got,
    middle, stage, turned, columns_out, columns_got, q_shard, o_shard,
    q_full, o_full, normed, q_ref, k_ref, v_ref, attended, lse_ref, cos, sin, send, recv, local,
):
    near = Neighbours(inner)
    copies = Copies(send, recv, local)
    tokens, width = hidden.shape
    block = width // 16
    chunks = pairs.shape[0]
    hid = down.shape[2]
    q_width = q_ref.shape[1]
    kv_slabs = k_ref.shape[1] // LANES
    slabs = q_width // LANES
    qkv_width = q_width + 2 * k_ref.shape[1]
    experts = down.shape[0]
    each = 2 + experts
    half = tokens // 2
    tiles = tokens // ROWS
    x, core = near.x, near.core
    own_half = pl.ds(pl.multiple_of(core * half, half), half)
    mine = pl.ds(pl.multiple_of(tokens + core * half, half), half)
    theirs = pl.ds(pl.multiple_of(tokens + (1 - core) * half, half), half)

    weights_in = [
        copies.copy(lambda: (gateup_hbm, gateup), "gateup", False),
        copies.copy(lambda: (down_hbm, down), "down", False),
    ]
    hidden_in = copies.copy(lambda: (hidden_hbm, hidden), "hidden", False)
    kv_width = k_ref.shape[1]
    q_shard[:, :q_width] = w_query[...].astype(BF16)
    q_shard[:, q_width : q_width + kv_width] = w_keyval[0].astype(BF16)
    q_shard[:, q_width + kv_width : qkv_width] = w_keyval[1].astype(BF16)
    o_shard[...] = w_out[...].astype(BF16)
    value = jnp.concatenate(
        [gains[...], w_router[...], jnp.zeros((LANES - each, block), F32)]
    ).T
    high = value.astype(BF16).astype(F32)
    mid = (value - high).astype(BF16).astype(F32)
    low = value - high - mid
    value = high + pltpu.roll(mid, each, 1) + pltpu.roll(low, 2 * each, 1)
    q_shard[:, qkv_width:] = value.astype(BF16)
    near.greet()
    gather_q = Gather(copies, near, q_shard, q_full, "q")
    gather_o = Gather(copies, near, o_shard, o_full, "o")
    gather_q.begin()
    gather_q.spread(0)
    copies.copy(lambda: (og_hbm, og_pair.at[pl.ds(0, tokens)]), "og")
    segment = seg_row[...].astype(F32)
    seg_col[...] = jnp.broadcast_to(segment, (8, tokens)).T[:, :1]

    def pack(c, mine):
        first = 2 * (chunks * (x if mine else 1 - x) + c)
        rows = pl.ds(pl.multiple_of(x * block, block), block)
        for e in range(CHUNK):
            for part_at in range(2):
                at = hid * (2 * e + part_at)
                value = gateup[first + e, part_at].astype(BF16)
                if mine:
                    pairs[c, rows, at : at + hid] = value
                else:
                    given[c, :, at : at + hid] = value
            at = hid * (2 * CHUNK + e)
            value = down[first + e].astype(BF16)
            if mine:
                pairs[c, rows, at : at + hid] = value
            else:
                given[c, :, at : at + hid] = value

    def swap(c):
        rows = pl.ds(pl.multiple_of(x * block, block), block)
        copies.remote(
            lambda: (given.at[c], pairs.at[c, rows]), ("s", c), ("s", c), near.over_x
        )

    def swapped(c):
        rows = pl.ds(pl.multiple_of((1 - x) * block, block), block)
        copies.arrived(pairs.at[c, rows], ("s", c), near.over_x)

    def ring_one(c):
        copies.remote(
            lambda: (pairs.at[c], near_hbm.at[c, 0]), ("up", c), ("r", c, 1), near.along[2]
        )
        copies.remote(
            lambda: (pairs.at[c], near_hbm.at[c, 1]), ("down", c), ("r", c, 2), near.along[1]
        )

    def ring_two(c):
        copies.arrived(near_hbm.at[c, 0], ("r", c, 1), near.along[1])
        copies.remote(
            lambda: (near_hbm.at[c, 0], near_hbm.at[c, 2]), ("two", c), ("r", c, 3), near.along[2]
        )

    def over_y(c, k):
        copies.remote(
            lambda: (pairs.at[c] if k == 0 else near_hbm.at[c, k - 1], far_hbm.at[c, k]),
            ("f", c, k), ("f", c, k), near.over_y,
        )

    def ring_got(c, k):
        copies.arrived(near_hbm.at[c, k - 1], ("r", c, k), near.along[k])

    def turn_tile(source, target, name, side):
        copies.copy(lambda: (source, stage.at[side]), (name, "in"), False)()
        turned[side] = stage[side].T
        return copies.copy(lambda: (turned.at[side], target), (name, "out"), False)

    waits = [None, None]

    def turn_next(source, target, name, side):
        if waits[side] is not None:
            waits[side]()
        waits[side] = turn_tile(source, target, name, side)

    for wait in weights_in:
        wait()
    pack(0, False)
    swap(0)
    pack(0, True)
    gather_q.spread(1)
    gather_q.spread(2)
    pack(1, False)
    pack(1, True)
    gather_q.cross(0)
    gather_q.spread(3)
    half_width = HEAD_DIM // 2
    lane = lax.broadcasted_iota(jnp.int32, (ROWS, LANES), 1)
    for at in range(0, tokens, ROWS):
        rows = slice(at, at + ROWS)
        earlier = jnp.where(segment < seg_col[rows, :], 1.0, 0.0)
        position = (at + lax.broadcasted_iota(jnp.int32, (ROWS, 1), 0)).astype(F32)
        position = position - jnp.sum(earlier, axis=1, keepdims=True)
        angle = position * frequency[...]
        cos[rows, :] = jnp.cos(angle)
        wave = jnp.sin(angle)
        sin[rows, :] = jnp.where(lane % HEAD_DIM < half_width, -wave, wave)
    gather_q.cross(1)
    gather_q.cross(2)
    gather_q.cross(3)
    gather_o.begin()
    gather_o.spread(0)
    swap(1)
    pack(2, False)
    pack(2, True)
    pack(3, False)
    pack(3, True)
    fill_bias(bias, seg_col, segment)
    for tile in range(tiles):
        rows = pl.ds(tile * ROWS, ROWS)
        turn_next(og_hbm.at[rows], ogt_hbm.at[:, rows], ("og", tile), tile % 2)
    hidden_in()
    gather_q.end()
    pieces = q_full[:, :, qkv_width:].reshape(width, LANES)
    wide = pieces.astype(F32)
    summed = wide + roll_left(wide, each) + roll_left(wide, 2 * each)
    small[...] = summed.T[: small.shape[0], :]
    copies.copy(lambda: (q_full, q_full_out), "q full")
    copies.copy(lambda: (cos, cos_out), "cos")
    copies.copy(lambda: (sin, sin_out), "sin")
    swapped(0)
    ring_one(0)
    over_y(0, 0)
    swap(2)
    swap(3)

    def project(tile, carry):
        rows = pl.ds(pl.multiple_of(tile * ROWS, ROWS), ROWS)
        for here in few_rows(ROWS):
            value = hidden[pl.ds(pl.multiple_of(tile * ROWS + here.start, 16), 16), :].astype(F32)
            inverse = lax.rsqrt(jnp.mean(value * value, axis=1, keepdims=True) + NORM_EPSILON)
            stage[0, here, :] = (value * inverse * small[0:1, :]).astype(BF16)
        low = stage[0]
        normed[:, rows] = low.T
        cosine, sine = cos[rows, :], sin[rows, :]
        for g in range(slabs + 2 * kv_slabs):
            lanes = slice(g * LANES, (g + 1) * LANES)
            if g % 2 == 0:
                two = slice(g * LANES, (g + 2) * LANES)
                lin_two = dot(low, q_full[:, :, two].reshape(width, 2 * LANES))
            lin = lin_two[:, (g % 2) * LANES : (g % 2 + 1) * LANES]
            if g < slabs + kv_slabs:
                lin = lin * cosine + rotate_halves(lin) * sine
            if g < slabs:
                q_ref[rows, lanes] = lin.astype(BF16)
            elif g < slabs + kv_slabs:
                at = (g - slabs) * LANES
                k_ref[rows, at : at + LANES] = lin.astype(BF16)
            else:
                at = (g - slabs - kv_slabs) * LANES
                v_ref[rows, at : at + LANES] = lin.astype(BF16)

        @pl.when(tile == 1)
        def _():
            gather_o.spread(1)

        @pl.when(tile == 2)
        def _():
            gather_o.spread(2)
            gather_o.cross(0)

        return carry

    lax.fori_loop(0, tiles, project, 0)
    copies.copy(lambda: (normed, normed_out), "normed")
    copies.copy(lambda: (q_ref, q_out), "q")
    copies.copy(lambda: (k_ref, k_out), "k")
    copies.copy(lambda: (v_ref, v_out), "v")
    for j in range(kv_slabs):
        lanes = slice(j * LANES, (j + 1) * LANES)
        spread_heads(k_ref[:, lanes], k_low, k_high, 2 * j)
        spread_heads(v_ref[:, lanes], v_low, v_high, 2 * j)

    def attend(g, carry):
        lanes = pl.ds(pl.multiple_of(g * LANES, LANES), LANES)
        kv_even, kv_odd = (2 * g) // 3, (2 * g + 1) // 3
        for at in range(0, tokens, ROWS):
            rows = slice(at, at + ROWS)
            upto = at + ROWS
            queries = q_ref[rows, lanes]
            total = None
            stats = []
            for keys, values, kv_at in ((k_low, v_low, kv_even), (k_high, v_high, kv_odd)):
                scores = dot(queries, keys[kv_at, :upto, :], NT) * SCORE_SCALE + bias[rows, :upto]
                highest = jnp.max(scores, axis=1, keepdims=True)
                weights = jnp.exp(scores - highest)
                whole = jnp.sum(weights, axis=1, keepdims=True)
                probability = (weights * (1.0 / whole)).astype(BF16)
                one = dot(probability, values[kv_at, :upto, :])
                total = one if total is None else total + one
                stats.append(highest + jnp.log(whole))
            attended[rows, lanes] = total.astype(BF16)
            across = jnp.where(half_mask(ROWS, False), stats[0], stats[1]).T
            lse_ref[g, 0:1, rows] = across[0:1, :]
            lse_ref[g, 1:2, rows] = across[HEAD_DIM : HEAD_DIM + 1, :]

        @pl.when(g == 0)
        def _():
            gather_o.spread(3)
            gather_o.cross(1)
            gather_o.cross(2)

        @pl.when(g == 1)
        def _():
            ring_two(0)
            over_y(0, 1)
            ring_got(0, 2)
            over_y(0, 2)
            swapped(1)
            ring_one(1)
            over_y(1, 0)
            copies.remote(
                lambda: (og_hbm.at[own_half], og_pair.at[mine]), ("og",), ("og",), near.over_x
            )

        @pl.when(g == 2)
        def _():
            gather_o.cross(3)

        @pl.when(g == 4)
        def _():
            gather_o.end()

        @pl.when(g == slabs - 1)
        def _():
            ring_got(0, 3)
            over_y(0, 3)
            swapped(2)
            ring_one(2)
            over_y(2, 0)

        return carry

    lax.fori_loop(0, slabs, attend, 0)
    copies.copy(lambda: (o_full, o_full_out), "o full")
    copies.copy(lambda: (attended, attended_out), "attended")
    copies.copy(lambda: (lse_ref, lse_out), "lse")

    def project_out(step, carry):
        tile = (step + 2 * (1 - core)) % tiles
        rows = pl.ds(pl.multiple_of(tile * ROWS, ROWS), ROWS)
        low = attended[rows, :]
        for group in range(SLOTS):
            cols = slice(4 * block * group, 4 * block * (group + 1))
            weight = o_full[4 * group : 4 * (group + 1)].reshape(4 * block, q_width)
            part[rows, cols] = dot(low, weight, NT).astype(BF16)
        return carry

    for step in range(tiles):
        project_out(step, 0)
        tile = (step + 2 * (1 - core)) % tiles
        rows = pl.ds(pl.multiple_of(tile * ROWS, ROWS), ROWS)
        copies.remote(
            lambda rows=rows: (part.at[rows], part_got.at[rows]),
            ("p", step), ("p", step), near.twin,
        )
    router = q_full[:, :, qkv_width:].reshape(width, LANES)
    for step in range(tiles):
        tile = (step + 2 * core) % tiles
        rows = pl.ds(pl.multiple_of(tile * ROWS, ROWS), ROWS)
        copies.arrived(part_got.at[rows], ("p", step), near.twin)
        side = step % 2
        if step >= 2:
            middle_out[side]()
        elif step == 0:
            middle_out = [None, None]
        for here in few_rows(ROWS):
            at = pl.ds(pl.multiple_of(tile * ROWS + here.start, 16), 16)
            total = hidden[at, :].astype(F32) + RESIDUAL_SCALE * (
                part[at, :].astype(F32) + part_got[at, :].astype(F32)
            )
            middle[side, here, :] = total
            inverse = lax.rsqrt(jnp.mean(total * total, axis=1, keepdims=True) + NORM_EPSILON)
            value = total * inverse * small[1:2, :]
            high = value.astype(BF16)
            x_own[at, :] = high
            rest = value - high.astype(F32)
            mid = rest.astype(BF16)
            stage[0, here, :] = mid
            stage[1, here, :] = (rest - mid.astype(F32)).astype(BF16)
        middle_out[side] = copies.copy(
            lambda rows=rows, side=side: (middle.at[side], middle_hbm.at[rows]), ("m", step), False
        )
        copies.copy(lambda rows=rows: (x_own.at[rows], x_hbm.at[rows]), ("x", step))
        if step < 2:
            copies.remote(
                lambda rows=rows: (x_own.at[rows], x_got.at[rows]),
                ("x", step), ("x", step), near.over_x,
            )
        one, two, three = dot(x_own[rows, :], router), dot(stage[0], router), dot(stage[1], router)
        logits = one + roll_left(one, each) + roll_left(one, 2 * each) + two + roll_left(two, each)
        logits = roll_left(logits + three, 2)
        lane = lax.broadcasted_iota(jnp.int32, (ROWS, LANES), 1)
        chosen = lane < 0
        route = routes[:, rows].astype(F32).T
        for k in range(routes.shape[0]):
            chosen = chosen | (route[:, k : k + 1] == lane.astype(F32))
        logits = jnp.where(chosen, logits, MASK_VALUE)
        powers = jnp.exp(logits - jnp.max(logits, axis=1, keepdims=True))
        powers = jnp.where(chosen, powers, 0.0)
        combine[rows, :] = powers * (1.0 / jnp.sum(powers, axis=1, keepdims=True))
        if step == 0:
            swapped(3)
            copies.copy(lambda: (pairs, pairs_hbm), "pairs")
        if step == 1:
            ring_two(1)
            over_y(1, 1)
            ring_got(1, 2)
            over_y(1, 2)

    shares = experts // 2
    flipped = combine[...].T
    kept = jnp.where(x == 0, flipped[:shares, :], flipped[shares : 2 * shares, :])
    gone = jnp.where(x == 0, flipped[shares : 2 * shares, :], flipped[:shares, :])
    columns_out[...] = gone
    copies.remote(lambda: (columns_out, columns_got), ("c",), ("c",), near.over_x)
    combine_pair[:tokens, :] = kept.T
    ring_two(2)
    ring_got(1, 3)
    over_y(1, 3)

    copies.arrived(og_pair.at[mine], ("og",), near.over_x)
    copies.remote(lambda: (og_pair.at[mine],) * 2, ("og2",), ("og2",), near.twin)
    for tile in range(tiles):
        rows = pl.ds(tile * ROWS, ROWS)
        if waits[tile % 2] is not None:
            waits[tile % 2]()
        turned[tile % 2] = x_own[rows, :].T
        waits[tile % 2] = copies.copy(
            lambda rows=rows, side=tile % 2: (turned.at[side], xt_hbm.at[:, rows]),
            ("xt", tile), False,
        )
    copies.arrived(columns_got, ("c",), near.over_x)
    combine_pair[tokens:, :] = columns_got[...].T
    copies.arrived(og_pair.at[theirs], ("og2",), near.twin)
    order = [(step + 2 * core) % tiles for step in range(2)]
    order += [(step + 2 * (1 - core)) % tiles for step in range(2)]

    def og_rows(step):
        return pl.ds(pl.multiple_of(tokens + order[step] * ROWS, ROWS), ROWS)

    def og_load(step):
        return copies.copy(
            lambda: (og_pair.at[og_rows(step)], stage.at[step % 2]), ("ogin", step), False
        )

    loaded = og_load(0)
    for step in range(tiles):
        loaded()
        if step + 1 < tiles:
            loaded = og_load(step + 1)
        side = step % 2
        waits[side]()
        turned[side] = stage[side].T
        waits[side] = copies.copy(
            lambda step=step, side=side: (turned.at[side], ogt_hbm.at[:, og_rows(step)]),
            ("ogt", step), False,
        )
    for step in range(tiles):
        rows = pl.ds(pl.multiple_of(order[step] * ROWS, ROWS), ROWS)
        there = pl.ds(pl.multiple_of(tokens + order[step] * ROWS, ROWS), ROWS)
        if step < 2:
            copies.arrived(x_got.at[rows], ("x", step), near.over_x)
            copies.remote(
                lambda rows=rows: (x_got.at[rows],) * 2, ("x2", step), ("x2", step), near.twin
            )
        else:
            copies.arrived(x_got.at[rows], ("x2", step - 2), near.twin)
        copies.copy(
            lambda rows=rows, there=there: (x_got.at[rows], x_hbm.at[there]), ("xg", step)
        )
        side = step % 2
        waits[side]()
        turned[side] = x_got[rows, :].T
        waits[side] = copies.copy(
            lambda there=there, side=side: (turned.at[side], xt_hbm.at[:, there]),
            ("xgt", step), False,
        )
    for wait in waits + middle_out:
        wait()
    ring_got(2, 2)
    ring_got(2, 3)
    for c in range(LATE + 1):
        for k in range(SLOTS if c < LATE else 1):
            copies.arrived(far_hbm.at[c, k], ("f", c, k), near.over_y)
    copies.finish()


def forward_pass(weights, frequency, segments, routes, gateup, down, hidden, og):
    tokens, width = hidden.shape
    experts, hid = down.shape[0], down.shape[2]
    block, q_width = weights[0].shape
    kv_width = weights[1].shape[2]
    q_columns = q_width + 2 * kv_width + LANES
    slabs, kv_heads = q_width // LANES, kv_width // HEAD_DIM
    chunks = experts // (2 * CHUNK)
    columns = 3 * CHUNK * hid
    anywhere, vmem = pl.BlockSpec(memory_space=pl.ANY), vmem_spec()
    shape = jax.ShapeDtypeStruct
    inner = lax.axis_size("dp") // 16
    dma = pltpu.SemaphoreType.DMA
    kept = [
        shape((16, block, q_columns), BF16),
        shape((16, block, q_width), BF16),
        shape((width, tokens), BF16),
        shape((tokens, q_width), BF16),
        shape((tokens, kv_width), BF16),
        shape((tokens, kv_width), BF16),
        shape((tokens, q_width), BF16),
        shape((slabs, 8, tokens), F32),
        shape((tokens, LANES), F32),
        shape((tokens, LANES), F32),
    ]
    return pl.pallas_call(
        functools.partial(forward_kernel, inner),
        in_specs=[vmem] * 8 + [anywhere] * 4,
        out_specs=[vmem] * 4 + [anywhere] * 18,
        out_shape=[
            shape((24, width), F32),
            shape((tokens, LANES), F32),
            shape((2 * tokens, experts // 2), F32),
            shape((tokens, 1), F32),
            *kept,
            shape((tokens, width), F32),
            shape((2 * tokens, width), BF16),
            shape((width, 2 * tokens), BF16),
            shape((2 * tokens, width), BF16),
            shape((width, 2 * tokens), BF16),
            shape((chunks, 2 * block, columns), BF16),
            shape((chunks - 1, SLOTS - 1, 2 * block, columns), BF16),
            shape((LATE + 1, SLOTS, 2 * block, columns), BF16),
        ],
        scratch_shapes=[
            pltpu.VMEM((tokens, width), BF16),
            pltpu.VMEM(gateup.shape, gateup.dtype),
            pltpu.VMEM(down.shape, down.dtype),
            pltpu.VMEM((chunks, block, columns), BF16),
            pltpu.VMEM((chunks, 2 * block, columns), BF16),
            pltpu.VMEM((tokens, tokens), F32),
        ]
        + [pltpu.VMEM((kv_heads, tokens, LANES), BF16)] * 4
        + [pltpu.VMEM((tokens, width), BF16)] * 4
        + [
            pltpu.VMEM((2, ROWS, width), F32),
            pltpu.VMEM((2, ROWS, width), BF16),
            pltpu.VMEM((2, width, ROWS), BF16),
            pltpu.VMEM((experts // 2, tokens), F32),
            pltpu.VMEM((experts // 2, tokens), F32),
            pltpu.VMEM((block, q_columns), BF16),
            pltpu.VMEM((block, q_width), BF16),
            *[pltpu.VMEM(one.shape, one.dtype) for one in kept],
            dma((80,)), dma((80,)), dma((64,)),
        ],
        compiler_params=pltpu.CompilerParams(
            vmem_limit_bytes=EXPERT_VMEM, collective_id=1, has_side_effects=True
        ),
        name="forward_pass",
    )(*weights, frequency, segments[None, :], routes.T, gateup, down, hidden, og)


class Scatter:
    def __init__(self, copies, near, grad, one, two, got_y, got_x, got_z, share, tag):
        self.copies, self.near, self.grad, self.share, self.tag = copies, near, grad, share, tag
        self.one, self.two, self.got_y, self.got_x, self.got_z = one, two, got_y, got_x, got_z
        self.split = one.shape[2]

    def begin(self, k):
        near = self.near
        self.copies.remote(
            lambda: (self.grad.at[near.block(k, 1, 1), :, : self.split], self.one.at[k]),
            (self.tag, "one", k), (self.tag, "one", k), near.over_x,
        )
        self.copies.remote(
            lambda: (self.grad.at[near.block(k, 1, 1), :, self.split :], self.two.at[k]),
            (self.tag, "two", k), (self.tag, "two", k), near.over_y,
        )

    def cross(self, k):
        near, grad, split = self.near, self.grad, self.split
        self.copies.arrived(self.one.at[k], (self.tag, "one", k), near.over_x)
        at = near.block(k, 1, 0)
        for here in few_rows(grad.shape[1]):
            grad[at, here, :split] = (
                grad[at, here, :split].astype(F32) + self.one[k, here, :].astype(F32)
            ).astype(BF16)
        self.copies.remote(
            lambda: (grad.at[near.block(k, 1, 0)], self.got_y.at[k]),
            (self.tag, "y", k), (self.tag, "y", k), near.over_y,
        )
        self.copies.arrived(self.two.at[k], (self.tag, "two", k), near.over_y)
        at = near.block(k, 0, 1)
        for here in few_rows(grad.shape[1]):
            grad[at, here, split:] = (
                grad[at, here, split:].astype(F32) + self.two[k, here, :].astype(F32)
            ).astype(BF16)
        self.copies.remote(
            lambda: (grad.at[near.block(k, 0, 1)], self.got_x.at[k]),
            (self.tag, "x", k), (self.tag, "x", k), near.over_x,
        )

    def plane(self, k):
        near, grad = self.near, self.grad
        self.copies.arrived(self.got_y.at[k], (self.tag, "y", k), near.over_y)
        self.copies.arrived(self.got_x.at[k], (self.tag, "x", k), near.over_x)
        at = near.block(k, 0, 0)
        for here in few_rows(grad.shape[1]):
            total = grad[at, here, :].astype(F32) + self.got_y[k, here, :].astype(F32)
            total = total + self.got_x[k, here, :].astype(F32)
            if k == 0:
                self.share[here, :] = total
            else:
                grad[at, here, :] = total.astype(BF16)
        if k == 0:
            return
        self.copies.remote(
            lambda: (grad.at[near.block(k, 0, 0)], self.got_z.at[BACK[k] - 1]),
            (self.tag, "z", k), (self.tag, "z", BACK[k]), near.along[k],
        )

    def end(self):
        for k in range(1, SLOTS):
            self.copies.arrived(self.got_z.at[k - 1], (self.tag, "z", k), self.near.along[k])
            for here in few_rows(self.share.shape[0]):
                self.share[here, :] = self.share[here, :] + self.got_z[k - 1, here, :].astype(F32)


STRIP = 128


def backward_kernel(
    inner,
    seg_col, seg_row, small, combine, gate_turned,
    o_full_hbm, attended_hbm, q_ref_hbm, k_ref_hbm, v_ref_hbm, lse_hbm, cos_hbm, sin_hbm, q_hbm, normed_hbm, hidden_hbm, og_hbm, middle_hbm, dx_own, dx_twin, dx_other,
    mix_pair, *refs,
):
    keeps, refs = refs[:SENT], refs[SENT:]
    parts, refs = refs[:SENT], refs[SENT:]
    near_two, near_three, late_got, far_first, far_three = refs[:5]
    q_share, o_share, input_grad, block_out, kept_out, given_got, mid_grad = refs[5:12]
    far_got, first_got, z_two, z_three, mix_twin, mix_other = refs[12:18]
    (
        attended_grad, lin_grad, o_grad, q_grad, o_one, o_two, o_y, o_x, o_z,
        q_one, q_two, q_y, q_x, q_z, part_got, pieces, z_send, z_keep, given, kept,
        strips, wide_in, wide_out, strip_out, router_rows, gate_columns, small_sum,
        o_full, attended, q_ref, k_ref, v_ref, lse_ref, cos, sin,
        send, recv, local, strip_sem, wide_sem, out_sem,
    ) = refs[18:]
    near = Neighbours(inner)
    copies = Copies(send, recv, local)
    tokens, width = hidden_hbm.shape
    block = width // 16
    x, core = near.x, near.core
    half = tokens // 2
    q_width = q_ref.shape[1]
    kv_width = k_ref.shape[1]
    kv_slabs, slabs = kv_width // LANES, q_width // LANES
    qkv_width = q_width + 2 * kv_width
    experts = gate_turned.shape[0]
    each = 2 + experts
    strip_count = tokens // STRIP
    ours = pl.ds(0, tokens)
    half_mine = pl.ds(pl.multiple_of(tokens + core * half, half), half)
    there = pl.ds(pl.multiple_of(core * half, half), half)
    not_there = pl.ds(pl.multiple_of((1 - core) * half, half), half)
    scatter_o = Scatter(copies, near, o_grad, o_one, o_two, o_y, o_x, o_z, o_share, "o")
    scatter_q = Scatter(copies, near, q_grad, q_one, q_two, q_y, q_x, q_z, q_share, "q")
    z_gots = [*parts, z_two, z_three]

    def y_ends(c, k):
        if c == SENT:
            return near_two.at[k], first_got if k == 0 else late_got.at[k - 1]
        return near_three.at[k], far_got.at[k]

    def y_load(c, k, i, which):
        if 0 in which:
            copies.copy(lambda: (y_ends(c, k)[0], pieces.at[2 * i]), ("own", c, k), False)
        if 1 in which:
            copies.copy(lambda: (y_ends(c, k)[1], pieces.at[2 * i + 1]), ("got", c, k), False)

    def y_sum(c, k, i):
        copies.wait_copy(lambda: (y_ends(c, k)[0], pieces.at[2 * i]), ("own", c, k))
        copies.wait_copy(lambda: (y_ends(c, k)[1], pieces.at[2 * i + 1]), ("got", c, k))
        if k > 0 and c > SENT:
            copies.sent(
                lambda: (z_send.at[k - 1], z_two.at[BACK[k] - 1]), (SENT, "z", k), near.along[k]
            )
        target = z_keep.at[c - SENT] if k == 0 else z_send.at[k - 1]
        for here in few_rows(target.shape[0]):
            target[here, :] = (
                pieces[2 * i, here, :].astype(F32) + pieces[2 * i + 1, here, :].astype(F32)
            ).astype(BF16)
        if k == 0:
            return
        copies.remote(
            lambda: (z_send.at[k - 1], z_gots[c].at[BACK[k] - 1]),
            (c, "z", k), (c, "z", BACK[k]), near.along[k], last=c > SENT,
        )

    def far_arrived(k):
        copies.arrived(far_got.at[k], ("far", k), near.over_y)

    def chunk_ends(c, k):
        return keeps[c] if k == 0 else z_gots[c].at[k - 1], pieces.at[k]

    def load_chunk(c):
        for k in range(1 if c >= SENT else 0, SLOTS):
            if c >= SENT:
                copies.arrived(z_gots[c].at[k - 1], (c, "z", k), near.along[k])
            copies.copy(lambda k=k: chunk_ends(c, k), (c, "sum", k), False)

    def sum_chunk(c):
        for k in range(1 if c >= SENT else 0, SLOTS):
            copies.wait_copy(lambda: chunk_ends(c, k), (c, "sum", k))
        if c >= 2:
            copies.wait_copy(lambda: (kept.at[c % 2], kept_out.at[c - 2]), ("kept", c - 2))
        for base, mine in ((x * block, True), ((1 - x) * block, False)):
            for here, rows in zip(few_rows(block), few_rows(block, base)):
                total = (pieces[0, rows, :] if c < SENT else z_keep[c - SENT, rows, :]).astype(F32)
                for k in range(1, SLOTS):
                    total = total + pieces[k, rows, :].astype(F32)
                if mine:
                    kept[c % 2, here, :] = total
                else:
                    given[c, here, :] = total.astype(BF16)
        copies.copy(lambda: (kept.at[c % 2], kept_out.at[c]), ("kept", c), c >= 2)
        copies.remote(
            lambda: (given.at[c], given_got.at[c]), ("given", c), ("given", c), near.over_x
        )

    def strip_rows(t):
        return pl.ds(pl.multiple_of(t * STRIP, STRIP), STRIP)

    def strip_loads(t, sources, wide):
        side = t % 2
        rows = strip_rows(t)
        loads = [
            pltpu.make_async_copy(source.at[rows], strips.at[i, side], strip_sem.at[i, side])
            for i, source in enumerate(sources)
        ]
        if wide is not None:
            loads.append(
                pltpu.make_async_copy(wide.at[rows], wide_in.at[side], wide_sem.at[side])
            )
        return loads

    def strip_store(t, source, target):
        side = t % 2
        return pltpu.make_async_copy(
            source.at[side], target.at[strip_rows(t)], out_sem.at[side]
        )

    def over_strips(sources, wide, source, target, compute):
        for load in strip_loads(0, sources, wide):
            load.start()

        def one(t, carry):
            side = t % 2

            @pl.when(t + 1 < strip_count)
            def _():
                for load in strip_loads(t + 1, sources, wide):
                    load.start()

            for load in strip_loads(t, sources, wide):
                load.wait()

            @pl.when(t >= 2)
            def _():
                strip_store(t - 2, source, target).wait()

            compute(t, side)
            strip_store(t, source, target).start()
            return carry

        lax.fori_loop(0, strip_count, one, 0)
        for t in (strip_count - 2, strip_count - 1):
            strip_store(t, source, target).wait()

    for i, k in enumerate((1, 2)):
        y_load(SENT, k, i, (0, 1))
    weights_in = copies.copy(lambda: (o_full_hbm, o_full), "o full", False)
    attended_in = copies.copy(lambda: (attended_hbm, attended), "attended", False)
    operands_in = [
        copies.copy(lambda one=one, to=to: (one, to), ("operand", i), False)
        for i, (one, to) in enumerate(
            (
                (q_ref_hbm, q_ref), (k_ref_hbm, k_ref), (v_ref_hbm, v_ref), (lse_hbm, lse_ref),
                (cos_hbm, cos), (sin_hbm, sin),
            )
        )
    ]
    near.greet()
    for k in (1, 2, 3, 0):
        copies.remote(
            lambda k=k: (far_three.at[k], far_got.at[k]), ("far", k), ("far", k), near.over_y
        )
    copies.remote(lambda: (far_first, first_got), ("first",), ("first",), near.over_y)
    copies.remote(
        lambda: (mix_pair.at[half_mine], mix_other.at[there]), ("mo",), ("mo",), near.over_x
    )
    copies.remote(lambda: (mix_pair.at[ours], mix_twin), ("mt",), ("mt",), near.twin)
    y_sum(SENT, 1, 0)
    y_load(SENT, 3, 0, (0, 1))
    y_sum(SENT, 2, 1)
    y_sum(SENT, 3, 0)
    load_chunk(0)

    router = small[2 : 2 + experts, :]
    high = router.astype(BF16).astype(F32)
    mid = (router - high).astype(BF16).astype(F32)
    low = router - high - mid
    router_rows[...] = jnp.concatenate(
        [high, mid, low, high, mid, high, jnp.zeros((LANES - 6 * experts, width), F32)]
    ).astype(BF16)
    gate_columns[...] = jnp.concatenate(
        [gate_turned[...], jnp.zeros((LANES - experts, tokens), F32)]
    ).T
    small_sum[...] = jnp.zeros_like(small_sum)

    def middle_part(turned_back):
        def compute(t, side):
            rows = strip_rows(t)
            gates, grads = combine[rows, :], gate_columns[rows, :]
            logit = gates * (grads - jnp.sum(gates * grads, axis=1, keepdims=True))
            one = logit.astype(BF16).astype(F32)
            two = (logit - one).astype(BF16).astype(F32)
            three = (logit - one - two).astype(BF16).astype(F32)

            def moved(piece, by):
                return pltpu.roll(piece, by * experts, 1)

            row = one + moved(one, 1) + moved(one, 2) + moved(two, 3) + moved(two, 4)
            row = (row + moved(three, 5)).astype(BF16)
            wide_out[side] = dot(row, router_rows[...])
            gain = small[1:2, :]
            gain_part = None
            back, n_one, n_two, n_three = (
                strip_out.at[0], strip_out.at[1], z_keep.at[0], z_keep.at[1]
            )
            for here in few_rows(STRIP):
                upstream = strips[0, side, here, :].astype(F32) + strips[1, side, here, :].astype(F32)
                upstream = upstream + strips[2, side, here, :].astype(F32)
                upstream = upstream + wide_out[side, here, :]
                middle = wide_in[side, here, :]
                inverse = lax.rsqrt(jnp.mean(middle * middle, axis=1, keepdims=True) + NORM_EPSILON)
                scaled = middle * inverse
                weighted = upstream * gain
                mean_term = jnp.mean(weighted * scaled, axis=1, keepdims=True)
                grad = strips[3, side, here, :].astype(F32) + inverse * (
                    weighted - scaled * mean_term
                )
                wide_out[side, here, :] = grad
                back[here, :] = (RESIDUAL_SCALE * grad).astype(BF16)
                gained = jnp.sum(upstream * scaled, axis=0, keepdims=True)
                gain_part = gained if gain_part is None else gain_part + gained
                normed = scaled * gain
                piece = normed.astype(BF16)
                n_one[here, :] = piece
                rest = normed - piece.astype(F32)
                piece = rest.astype(BF16)
                n_two[here, :] = piece
                n_three[here, :] = (rest - piece.astype(F32)).astype(BF16)
            small_sum[0:1, :] += gain_part
            strip = pl.ds(0, STRIP)
            turned_back[:, rows] = back[...].T
            attended_grad[rows, :] = dot(back[...], o_full[...].reshape(width, q_width)).astype(BF16)
            columns = (one + moved(two, 1) + moved(three, 2)).T[: 3 * experts, :].astype(BF16)
            a, b, c = (
                dot(columns, n_one[...]), dot(columns, n_two[strip, :]), dot(columns, n_three[strip, :])
            )
            e = experts
            small_sum[8 : 8 + e, :] += (
                a[:e] + a[e : 2 * e] + a[2 * e :] + b[:e] + b[e : 2 * e] + c[:e]
            )

        weights_in()
        over_strips([dx_own, dx_twin, dx_other, og_hbm], middle_hbm, wide_out, mid_grad, compute)
        attended_in()
        for group in range(SLOTS):
            rows = slice(4 * block * group, 4 * block * (group + 1))
            o_grad[4 * group : 4 * (group + 1)] = (
                dot(turned_back[rows, :], attended[...]).astype(BF16).reshape(4, block, q_width)
            )

    pl.run_scoped(middle_part, pltpu.VMEM((width, tokens), BF16))
    for k in (1, 2, 3, 0):
        scatter_o.begin(k)

    def attention_part(bias0, bias1, bias2, bias3, k_low, k_high, v_low, v_high, dk, dv, dq):
        biases = (bias0, bias1, bias2, bias3)
        for wait in operands_in:
            wait()
        for at, bias in enumerate(biases):
            upto = bias.shape[0]
            keys_at = lax.broadcasted_iota(jnp.int32, bias.shape, 0)
            rows_at = at * ROWS + lax.broadcasted_iota(jnp.int32, bias.shape, 1)
            same = seg_col[:upto, :] == seg_row[:, at * ROWS : (at + 1) * ROWS].astype(F32)
            bias[...] = jnp.where((rows_at >= keys_at) & same, 0.0, MASK_VALUE).astype(F32)
        for j in range(kv_slabs):
            lanes = slice(j * LANES, (j + 1) * LANES)
            spread_heads(k_ref[:, lanes], k_low, k_high, 2 * j)
            spread_heads(v_ref[:, lanes], v_low, v_high, 2 * j)
        dk[...] = jnp.zeros_like(dk)
        dv[...] = jnp.zeros_like(dv)

        def slab(g, carry):
            lanes = pl.ds(pl.multiple_of(g * LANES, LANES), LANES)
            kv_even, kv_odd = (2 * g) // 3, (2 * g + 1) // 3
            for at, bias in enumerate(biases):
                rows = slice(at * ROWS, (at + 1) * ROWS)
                upto = (at + 1) * ROWS
                queries, grads = q_ref[rows, lanes], attended_grad[rows, lanes]
                turned = (grads.astype(F32) * attended[rows, lanes].astype(F32)).T
                zero = jnp.zeros_like(queries)
                dq_part = None
                for upper, keys, values, kv_at in (
                    (False, k_low, v_low, kv_even), (True, k_high, v_high, kv_odd)
                ):
                    first = HEAD_DIM if upper else 0
                    delta = jnp.sum(turned[first : first + HEAD_DIM, :], axis=0, keepdims=True)
                    head = 1 if upper else 0
                    total = lse_ref[g, head : head + 1, rows]
                    keys_here = keys[kv_at, :upto, :]
                    scores = dot(keys_here, queries, NT) * SCORE_SCALE + bias[...]
                    probability = jnp.exp(scores - total)
                    prob_grad = dot(values[kv_at, :upto, :], grads, NT)
                    score_grad = (probability * (prob_grad - delta)).astype(BF16)
                    mask = half_mask(ROWS, upper)
                    dv[kv_at, :upto, :] += dot(
                        probability.astype(BF16), jnp.where(mask, grads, zero)
                    )
                    dk[kv_at, :upto, :] += dot(score_grad, jnp.where(mask, queries, zero))
                    one = dot(score_grad, keys_here, TN)
                    dq_part = one if dq_part is None else dq_part + one
                dq[rows, :] = dq_part * SCORE_SCALE
            whole = dq[...]
            lin_grad[:, lanes] = (
                whole * cos[...] - rotate_halves(whole) * sin[...]
            ).astype(BF16)

            @pl.when(g == 1)
            def _():
                for k in (1, 2, 3, 0):
                    scatter_o.cross(k)

            @pl.when(g == 2)
            def _():
                sum_chunk(0)
                y_load(SENT + 1, 1, 0, (0,))
                y_load(SENT + 1, 2, 1, (0,))

            @pl.when(g == 3)
            def _():
                far_arrived(1)
                y_load(SENT + 1, 1, 0, (1,))
                far_arrived(2)
                y_load(SENT + 1, 2, 1, (1,))
                far_arrived(3)
                y_sum(SENT + 1, 1, 0)
                y_load(SENT + 1, 3, 0, (0, 1))
                y_sum(SENT + 1, 2, 1)
                y_sum(SENT + 1, 3, 0)
                load_chunk(1)

            @pl.when(g == 4)
            def _():
                for k in (1, 2, 3, 0):
                    scatter_o.plane(k)
                sum_chunk(1)
                far_arrived(0)
                y_load(SENT + 1, 0, 0, (0, 1))
                copies.arrived(first_got, ("first",), near.over_y)
                y_load(SENT, 0, 1, (0, 1))

            return carry

        lax.fori_loop(0, slabs, slab, 0)
        low = half_mask(tokens, False)

        def joined(sums, j):
            one, two = sums[2 * j], sums[2 * j + 1]
            one = one + pltpu.roll(one, HEAD_DIM, 1)
            two = two + pltpu.roll(two, HEAD_DIM, 1)
            return jnp.where(low, one, two)

        for j in range(kv_slabs):
            at = q_width + j * LANES
            whole = joined(dk, j) * SCORE_SCALE
            lin_grad[:, at : at + LANES] = (
                whole * cos[...] - rotate_halves(whole) * sin[...]
            ).astype(BF16)
            at = at + kv_width
            lin_grad[:, at : at + LANES] = joined(dv, j).astype(BF16)

    kv_shape = (2 * kv_slabs, tokens, LANES)
    pl.run_scoped(
        attention_part,
        *[pltpu.VMEM(((at + 1) * ROWS, ROWS), F32) for at in range(tokens // ROWS)],
        *[pltpu.VMEM(kv_shape, BF16)] * 4,
        *[pltpu.VMEM(kv_shape, F32)] * 2,
        pltpu.VMEM((tokens, LANES), F32),
    )

    def last_part(normed_turned, q_full, part):
        normed_in = copies.copy(lambda: (normed_hbm, normed_turned), "normed", False)
        weights_in = copies.copy(lambda: (q_hbm, q_full), "q weights", False)
        columns = jnp.concatenate(
            [
                small_sum[0:1, :], small_sum[8 : 8 + experts, :],
                jnp.zeros((LANES - 1 - experts, width), F32),
            ]
        ).T
        q_grad[:, :, qkv_width:] = columns.astype(BF16).reshape(16, block, LANES)
        normed_in()
        for k in (1, 2, 3, 0):
            spot = near.spots[k]
            rows = pl.ds(pl.multiple_of(spot * 4 * block, 4 * block), 4 * block)
            q_grad[pl.ds(spot * 4, 4), :, :qkv_width] = (
                dot(normed_turned[rows, :], lin_grad[...])
                .astype(BF16)
                .reshape(4, block, qkv_width)
            )
            scatter_q.begin(k)
        weights_in()

        def project(tile):
            rows = pl.ds(tile * ROWS, ROWS)
            for group in range(SLOTS):
                cols = slice(4 * block * group, 4 * block * (group + 1))
                weight = q_full[4 * group : 4 * (group + 1), :, :qkv_width]
                part[rows, cols] = dot(
                    lin_grad[rows, :], weight.reshape(4 * block, qkv_width), NT
                ).astype(BF16)
            copies.remote(
                lambda: (part.at[rows], part_got.at[rows]), ("n", tile), ("n", tile), near.twin,
                last=False,
            )

        project(0)
        project(1)
        for k in (1, 2, 3, 0):
            scatter_q.cross(k)
        y_sum(SENT + 1, 0, 0)
        y_sum(SENT, 0, 1)
        load_chunk(2)
        project(2)
        project(3)
        scatter_o.end()
        copies.arrived(mix_other.at[there], ("mo",), near.over_x)
        copies.remote(lambda: (mix_other.at[there],) * 2, ("m2",), ("m2",), near.twin)
        sum_chunk(2)
        for tile in range(tokens // ROWS):
            rows = pl.ds(tile * ROWS, ROWS)
            copies.arrived(part_got.at[rows], ("n", tile), near.twin)

        def finish_rows(t, side):
            for here in few_rows(STRIP):
                at = pl.ds(pl.multiple_of(t * STRIP + here.start, 16), 16)
                value = strips[0, side, here, :].astype(F32)
                inverse = lax.rsqrt(jnp.mean(value * value, axis=1, keepdims=True) + NORM_EPSILON)
                upstream = part[at, :].astype(F32) + part_got[at, :].astype(F32)
                scaled = value * inverse
                weighted = upstream * small[0:1, :]
                mean_term = jnp.mean(weighted * scaled, axis=1, keepdims=True)
                wide_out[side, here, :] = wide_in[side, here, :] + inverse * (
                    weighted - scaled * mean_term
                )

        over_strips([hidden_hbm], mid_grad, wide_out, input_grad, finish_rows)
        for k in (1, 2, 3, 0):
            scatter_q.plane(k)
        load_chunk(3)
        for tile in range(tokens // ROWS):
            rows = pl.ds(tile * ROWS, ROWS)
            copies.sent(lambda: (part.at[rows], part_got.at[rows]), ("n", tile), near.twin)

    pl.run_scoped(
        last_part,
        pltpu.VMEM((width, tokens), BF16), pltpu.VMEM(q_hbm.shape, BF16),
        pltpu.VMEM((tokens, width), BF16),
    )
    sum_chunk(3)
    copies.arrived(mix_twin, ("mt",), near.twin)
    copies.arrived(mix_other.at[not_there], ("m2",), near.twin)

    def mix_rows(t, side):
        for here in few_rows(STRIP):
            mix = strips[0, side, here, :].astype(F32) + strips[1, side, here, :].astype(F32)
            mix = mix + strips[2, side, here, :].astype(F32)
            strip_out[side, here, :] = (wide_in[side, here, :] + RESIDUAL_SCALE * mix).astype(BF16)

    over_strips([mix_pair, mix_twin, mix_other], middle_hbm, strip_out, block_out, mix_rows)
    scatter_q.end()
    for c in range(2 * SENT):
        copies.arrived(given_got.at[c], ("given", c), near.over_x)
    copies.finish()


def backward_pass(
    o_full, q, k, v, attended, lse, cosine, sine, seg_col, segments, small, combine, gate_turned,
    q_full, normed, hidden, og, middle, dx, mix, keep, parts, near_grads, far_grads,
):
    tokens, width = hidden.shape
    q_width, kv_width = q.shape[1], k.shape[1]
    block, q_columns = q_full.shape[1:]
    qkv_width = q_width + 2 * kv_width
    pair, columns = keep[0].shape
    chunks = 2 * SENT
    experts = gate_turned.shape[0]
    anywhere, vmem = pl.BlockSpec(memory_space=pl.ANY), vmem_spec()
    shape = jax.ShapeDtypeStruct
    dma = pltpu.SemaphoreType.DMA
    inner = lax.axis_size("dp") // 16

    def scatter_scratch(total):
        split = total // (2 * LANES) * LANES
        return [
            pltpu.VMEM((SLOTS, block, split), BF16),
            pltpu.VMEM((SLOTS, block, total - split), BF16),
            pltpu.VMEM((SLOTS, block, total), BF16),
            pltpu.VMEM((SLOTS, block, total), BF16),
            pltpu.VMEM((SLOTS - 1, block, total), BF16),
        ]

    values = (seg_col, segments[None, :], small, combine, gate_turned)
    read = (o_full, attended, q, k, v, lse, cosine, sine)
    far_values = (
        *read, q_full, normed, hidden, og, middle, *dx, mix, *keep, *parts, *near_grads, *far_grads,
    )
    return pl.pallas_call(
        functools.partial(backward_kernel, inner),
        in_specs=[vmem] * len(values) + [anywhere] * len(far_values),
        out_specs=[vmem] * 2 + [anywhere] * 11,
        out_shape=[
            shape((block, q_columns), F32),
            shape((block, q_width), F32),
            shape((tokens, width), F32),
            shape((tokens, width), BF16),
            shape((chunks, block, columns), F32),
            shape((chunks, block, columns), BF16),
            shape((tokens, width), F32),
            shape((SLOTS, pair, columns), BF16),
            shape((pair, columns), BF16),
            shape((SLOTS - 1, pair, columns), BF16),
            shape((SLOTS - 1, pair, columns), BF16),
            shape((tokens, width), BF16),
            shape((tokens, width), BF16),
        ],
        scratch_shapes=[
            pltpu.VMEM((tokens, q_width), BF16),
            pltpu.VMEM((tokens, qkv_width), BF16),
            pltpu.VMEM((16, block, q_width), BF16),
            pltpu.VMEM((16, block, q_columns), BF16),
        ]
        + scatter_scratch(q_width)
        + scatter_scratch(q_columns)
        + [
            pltpu.VMEM((tokens, width), BF16),
            pltpu.VMEM((SLOTS, pair, columns), BF16),
            pltpu.VMEM((SLOTS - 1, pair, columns), BF16),
            pltpu.VMEM((2, pair, columns), BF16),
            pltpu.VMEM((chunks, block, columns), BF16),
            pltpu.VMEM((2, block, columns), F32),
            pltpu.VMEM((4, 2, STRIP, width), BF16),
            pltpu.VMEM((2, STRIP, width), F32),
            pltpu.VMEM((2, STRIP, width), F32),
            pltpu.VMEM((2, STRIP, width), BF16),
            pltpu.VMEM((LANES, width), BF16),
            pltpu.VMEM((tokens, LANES), F32),
            pltpu.VMEM((8 + experts, width), F32),
            *[pltpu.VMEM(one.shape, one.dtype) for one in read],
            dma((80,)), dma((80,)), dma((64,)), dma((4, 2)), dma((2,)), dma((2,)),
        ],
        compiler_params=pltpu.CompilerParams(
            vmem_limit_bytes=EXPERT_VMEM, collective_id=2, has_side_effects=True
        ),
        name="backward_pass",
    )(*values, *far_values)


def whole_call(kernel, values, outs, earlier=(), name=None):
    return pl.pallas_call(
        with_earlier(kernel, len(values), len(earlier)),
        in_specs=[vmem_spec()] * len(values) + any_specs(earlier),
        out_specs=[vmem_spec()] * len(outs),
        out_shape=[jax.ShapeDtypeStruct(shape, dtype) for shape, dtype in outs],
        compiler_params=pltpu.CompilerParams(vmem_limit_bytes=VMEM_BYTES),
        name=name,
    )(*values, *earlier)


def adam_attention_kernel(q_share, o_share, *refs):
    states, outs = refs[:9], refs[9:18]
    gain_part = refs[18]
    q_width, kv_width = states[0].shape[1], states[3].shape[2]
    rate = (MODEL_DIM // 12) ** (-0.5)
    grad = q_share[:, :q_width]
    total = jnp.sum(states[0][...].astype(BF16).astype(F32) * grad, axis=1, keepdims=True)
    results = [
        adam_update(states[0][...], grad, states[1][...], states[2][...], rate, WEIGHT_DECAY)
    ]
    for out, result in zip(outs[:3], results[0]):
        out[...] = result
    for c in range(2):
        first = q_width + c * kv_width
        grad = q_share[:, first : first + kv_width]
        value = states[3][c]
        total = total + jnp.sum(value.astype(BF16).astype(F32) * grad, axis=1, keepdims=True)
        results = adam_update(value, grad, states[4][c], states[5][c], rate, WEIGHT_DECAY)
        for out, result in zip(outs[3:6], results):
            out[c] = result
    gain_part[...] = total
    results = adam_update(
        states[6][...], o_share[...], states[7][...], states[8][...],
        max(1, QUERY_HEADS * HEAD_DIM // 96) ** (-0.5), WEIGHT_DECAY,
    )
    for out, result in zip(outs[6:], results):
        out[...] = result


def adam_attention(q_share, o_share, states):
    outs = [(one.shape, F32) for one in states] + [((q_share.shape[0], 1), F32)]
    return whole_call(adam_attention_kernel, [q_share, o_share, *states], outs, (), "adam_attention")


def adam_experts_kernel(x_at, kept, got, *refs):
    states, outs = refs[:6], refs[6:]
    own = kept.shape[1]
    hidden = states[0].shape[3]
    mine = pl.program_id(0) // (pl.num_programs(0) // 2) == x_at[0]
    grad = jnp.where(mine, kept[0], got[0].astype(F32))
    for e in range(CHUNK):
        for part in range(2):
            first = hidden * (2 * e + part)
            results = adam_update(
                states[0][e, part], grad[:, first : first + hidden],
                states[1][e, part], states[2][e, part], MODEL_DIM ** (-0.5), WEIGHT_DECAY,
            )
            for out, result in zip(outs[:3], results):
                out[e, part] = result
        first = hidden * (2 * CHUNK + e)
        results = adam_update(
            states[3][e], grad[:, first : first + hidden], states[4][e], states[5][e],
            max(1, F // 256) ** (-0.5), WEIGHT_DECAY,
        )
        for out, result in zip(outs[3:], results):
            out[e] = result


def adam_experts(x_at, kept, got, gateup, down):
    chunks, own, columns = kept.shape
    experts, hidden = down[0].shape[0], down[0].shape[2]
    share = pl.BlockSpec((1, own, columns), lambda j: (j % chunks, 0, 0))
    big = pl.BlockSpec((CHUNK, 2, own, hidden), lambda j: (j, 0, 0, 0))
    small = pl.BlockSpec((CHUNK, own, hidden), lambda j: (j, 0, 0))
    return pl.pallas_call(
        adam_experts_kernel,
        grid=(experts // CHUNK,),
        in_specs=[smem_spec(), share, share] + [big] * 3 + [small] * 3,
        out_specs=[big] * 3 + [small] * 3,
        out_shape=[jax.ShapeDtypeStruct(gateup[0].shape, F32)] * 3
        + [jax.ShapeDtypeStruct(down[0].shape, F32)] * 3,
        compiler_params=pltpu.CompilerParams(vmem_limit_bytes=VMEM_BYTES),
        name="adam_experts",
    )(x_at, kept, got, *gateup, *down)


def place():
    at = lax.axis_index("dp") // (lax.axis_size("dp") // 16)
    return at // 4, at // 2 % 2, at % 2


def inner_groups(total):
    inner = total // 16
    return [[at * inner + i for i in range(inner)] for at in range(16)]


def inner_gather(shard, axis):
    total = lax.axis_size("dp")
    if total == 16:
        return shard
    return lax.all_gather(
        shard, "dp", axis=axis, tiled=True, axis_index_groups=inner_groups(total)
    )


def inner_scatter(share, axis):
    total = lax.axis_size("dp")
    if total == 16:
        return share
    return lax.psum_scatter(
        share, "dp", scatter_dimension=axis, tiled=True, axis_index_groups=inner_groups(total)
    )


def smem_spec():
    return pl.BlockSpec(memory_space=pltpu.SMEM)


def vmem_spec():
    return pl.BlockSpec(memory_space=pltpu.VMEM)


def swap_cores(part):
    return lax.ppermute(part, "tensor", [(0, 1), (1, 0)])


def pair_sum(part):
    return part.astype(F32) + swap_cores(part).astype(F32)


def adam_update(value, gradient, mean_old, square_old, rate, decay):
    mean_new = FIRST_DECAY * mean_old + (1.0 - FIRST_DECAY) * gradient
    square_new = SECOND_DECAY * square_old + (1.0 - SECOND_DECAY) * gradient * gradient
    mean_hat = mean_new / (1.0 - FIRST_DECAY**STEP)
    square_hat = square_new / (1.0 - SECOND_DECAY**STEP)
    updated = value - rate * (mean_hat / (jnp.sqrt(square_hat) + ADAM_EPSILON) + decay * value)
    return (mean_new, square_new, updated)


def shards(
    hidden_in,
    out_grad,
    routes,
    segments,
    norm_gains,
    gains_mean,
    gains_square,
    w_query,
    query_mean,
    query_square,
    key_value_weight,
    key_value_first_moment,
    key_value_second_moment,
    w_out,
    out_mean,
    out_square,
    w_router,
    router_mean,
    router_square,
    w_gateup,
    gateup_mean,
    gateup_square,
    w_down,
    down_mean,
    down_square,
):
    experts = w_down.shape[0]
    q_width, kv_width = w_query.shape[1], key_value_weight.shape[2]
    qkv_width = q_width + 2 * kv_width
    x_at = lax.axis_index("dp") // (lax.axis_size("dp") // 16) % 2
    turned_down = [one.transpose(0, 2, 1) for one in (w_down, down_mean, down_square)]
    gateup_rows, down_rows = w_gateup, turned_down[0]
    if lax.axis_size("dp") > 16:
        gateup_rows = inner_gather(w_gateup.astype(BF16), 2)
        down_rows = inner_gather(down_rows.astype(BF16), 1)
    half_width = HEAD_DIM // 2
    frequency = ROPE_BASE ** (-2.0 * jnp.arange(half_width, dtype=F32) / HEAD_DIM)
    frequency = jnp.concatenate([frequency] * 4)[None, :]
    turned_out = [one.T for one in (w_out, out_mean, out_square)]
    turned_router = [one.T for one in (w_router, router_mean, router_square)]
    weights = (
        inner_gather(w_query, 0), inner_gather(key_value_weight, 1),
        inner_gather(turned_out[0], 0), inner_gather(turned_router[0], 1), inner_gather(norm_gains, 1),
    )
    (
        small, combine, combine_pair, seg_col,
        qkv_blocks, out_blocks, normed_low, queries, keys, values, attended, lse, cosine, sine,
        middle, x_pair, x_turned, og_pair, og_turned, pairs, near, far,
    ) = forward_pass(
        weights, frequency, segments, routes, gateup_rows, down_rows, hidden_in, out_grad
    )
    dx, mix_pair, gate_turned, keep, z_got, near_grads, far_grads = experts_pass(
        x_pair, og_pair, x_turned, og_turned, combine_pair, pairs, near, far
    )
    qkv_share, output_share, input_grad, block_out, kept_share, got_share = backward_pass(
        out_blocks, queries, keys, values, attended, lse, cosine, sine, seg_col, segments, small,
        combine, gate_turned, qkv_blocks, normed_low, hidden_in, out_grad, middle, dx, mix_pair, keep,
        z_got, near_grads, far_grads,
    )[:6]
    kept_share, got_share = inner_scatter(kept_share, 1), inner_scatter(got_share, 1)
    x_here = x_at.astype(jnp.int32)[None]
    output_share = inner_scatter(output_share, 0)
    qkv_share = inner_scatter(qkv_share, 0)
    *attention_results, gain_one_part = adam_attention(
        qkv_share, output_share,
        [
            w_query, query_mean, query_square, key_value_weight, key_value_first_moment,
            key_value_second_moment, *turned_out,
        ],
    )
    gain_one_share = pair_sum(gain_one_part.T) / norm_gains[:1]
    gains_share = jnp.concatenate([gain_one_share, qkv_share[:, qkv_width][None, :]])
    router_share = qkv_share[:, qkv_width + 1 : qkv_width + 1 + experts].T

    gains_result = adam_update(norm_gains, gains_share, gains_mean, gains_square, GAIN_RATE, 0.0)
    router_result = adam_update(
        turned_router[0], router_share, turned_router[1], turned_router[2],
        (4 * MODEL_DIM) ** (-0.5), WEIGHT_DECAY,
    )
    expert_results = adam_experts(
        x_here, kept_share, got_share,
        (w_gateup, gateup_mean, gateup_square), turned_down,
    )
    expert_results = [*expert_results[:3], *(one.transpose(0, 2, 1) for one in expert_results[3:])]
    return (
        (block_out, input_grad)
        + gains_result
        + tuple(attention_results[:6])
        + tuple(one.T for one in attention_results[6:])
        + tuple(one.T for one in router_result)
        + tuple(expert_results)
    )


def solution(mesh):
    tokens, gains = P("dp", None), P(None, "dp")
    query, keyval, out = P("dp", "tensor"), P(None, "dp", "tensor"), P("tensor", "dp")
    router, gateup, down = P("dp", None), P(None, None, "dp", "tensor"), P(None, "tensor", "dp")
    states = tuple(
        spec for one in (gains, query, keyval, out, router, gateup, down) for spec in (one,) * 3
    )
    return jax.shard_map(
        shards,
        mesh=mesh,
        in_specs=(tokens, tokens, tokens, P("dp")) + states,
        out_specs=(tokens, tokens) + states,
        check_vma=False,
    )
```
